32 devices in a mesh: blk: 16 (over z, x, core), head: 2 (over y).
Axes of the slice: x: 2, y: 2, z: 4, core: 2. Of those that a mesh axis runs over, the one named last changes fastest.
Arguments:
- token_ids: int32 [4096], P('blk'), may hold values from 0 to 32127
- targets: int32 [4096], P('blk'), may hold values from 0 to 32127
- valid_mask: int32 [4096], replicated, may hold values from 0 to 1
- cont_lengths: int32 [16], replicated, may hold values from 1 to 256, 2048 in all
- routes: int32 [2, 4096], P(None, 'blk'), may hold values from 0 to 1
- vocab_table: float32 [32128, 768], P(('blk', 'head')), may hold values from -12 to 12
- vocab_first: float32 [32128, 768], P(('blk', 'head')), may hold values from -2.3841858e-06 to 2.3841858e-06
- vocab_second: float32 [32128, 768], P(('blk', 'head')), may hold values from 1.03575046e-13 to 4.1430019e-13
- attn_weights: float32 [2, 768, 3072], P(None, ('blk', 'head')), may hold values from -2.309401 to 2.309401
- attn_first: float32 [2, 768, 3072], P(None, ('blk', 'head')), may hold values from -2.3841858e-06 to 2.3841858e-06
- attn_second: float32 [2, 768, 3072], P(None, ('blk', 'head')), may hold values from 1.03575046e-13 to 4.1430019e-13
- router: float32 [2, 768, 2], P(None, ('blk', 'head')), may hold values from -0.375 to 0.375
- router_first: float32 [2, 768, 2], P(None, ('blk', 'head')), may hold values from -2.3841858e-06 to 2.3841858e-06
- router_second: float32 [2, 768, 2], P(None, ('blk', 'head')), may hold values from 1.03575046e-13 to 4.1430019e-13
- norm_gains: float32 [5, 768], P(None, ('blk', 'head')), may hold values from 0.25 to 2.2
- gains_first: float32 [5, 768], P(None, ('blk', 'head')), may hold values from -6.1035156e-05 to 6.1035156e-05
- gains_second: float32 [5, 768], P(None, ('blk', 'head')), may hold values from 9.3217545e-11 to 3.7287018e-10
- expert_up: float32 [2, 2, 768, 3072], P(None, None, 'blk', 'head'), may hold values from -0.21875 to 0.21875
- up_first: float32 [2, 2, 768, 3072], P(None, None, 'blk', 'head'), may hold values from -2.3841858e-06 to 2.3841858e-06
- up_second: float32 [2, 2, 768, 3072], P(None, None, 'blk', 'head'), may hold values from 1.03575046e-13 to 4.1430019e-13
- expert_down: float32 [2, 2, 768, 3072], P(None, None, 'blk', 'head'), may hold values from -0.21875 to 0.21875
- down_first: float32 [2, 2, 768, 3072], P(None, None, 'blk', 'head'), may hold values from -2.3841858e-06 to 2.3841858e-06
- down_second: float32 [2, 2, 768, 3072], P(None, None, 'blk', 'head'), may hold values from 1.03575046e-13 to 4.1430019e-13
Outputs:
- loss_sum: float32 [], replicated
- token_count: float32 [], replicated
- grad_norm: float32 [], replicated
- vocab_out: float32 [32128, 768], P(('blk', 'head'))
- vocab_first_out: float32 [32128, 768], P(('blk', 'head'))
- vocab_second_out: float32 [32128, 768], P(('blk', 'head'))
- attn_out: float32 [2, 768, 3072], P(None, ('blk', 'head'))
- attn_first_out: float32 [2, 768, 3072], P(None, ('blk', 'head'))
- attn_second_out: float32 [2, 768, 3072], P(None, ('blk', 'head'))
- router_out: float32 [2, 768, 2], P(None, ('blk', 'head'))
- router_first_out: float32 [2, 768, 2], P(None, ('blk', 'head'))
- router_second_out: float32 [2, 768, 2], P(None, ('blk', 'head'))
- gains_out: float32 [5, 768], P(None, ('blk', 'head'))
- gains_first_out: float32 [5, 768], P(None, ('blk', 'head'))
- gains_second_out: float32 [5, 768], P(None, ('blk', 'head'))
- up_out: float32 [2, 2, 768, 3072], P(None, None, 'blk', 'head')
- up_first_out: float32 [2, 2, 768, 3072], P(None, None, 'blk', 'head')
- up_second_out: float32 [2, 2, 768, 3072], P(None, None, 'blk', 'head')
- down_out: float32 [2, 2, 768, 3072], P(None, None, 'blk', 'head')
- down_first_out: float32 [2, 2, 768, 3072], P(None, None, 'blk', 'head')
- down_second_out: float32 [2, 2, 768, 3072], P(None, None, 'blk', 'head')
The draws below stay inside these ranges and needn't reach their ends.
Inputs may be any that keep to these rules, and one draw needn't show every extreme that they name: `cont_lengths`: continuation j covers the positions that follow the prompt and the continuations before it.
All inputs are finite; a program needn't handle non-finite values.
Results may differ from the reference program's by a relative error of at most 0.013.
Values may be sent and summed in bfloat16 or wider, within the bound.
A program may use at most 448 MiB of HBM per device.

```python
import math
import jax
import jax.numpy as jnp
import numpy as np
from jax import lax

D = 768
HEADS = 12
HEAD_DIM = 64
FF = 3072
V = 32128
EXPERTS = 2
LAYERS = 2
PROMPT = 2048
CLEN = 256
STEP = 10
TOKENS = 4096
CONTS = 16
PARAMS = 48274176
N_BLK = 16
N_HEAD = 2


def draw_valid_mask(key, part):
    key = jax.random.fold_in(key, 11)
    position = jnp.arange(TOKENS, dtype=jnp.int32)
    chance_level = 250 + 500 * position // TOKENS
    return (jax.random.randint(key, (TOKENS,), 0, 1000) < chance_level).astype(jnp.int32)


def draw_vocab_table(key, part):
    key = jax.random.fold_in(key, 12)
    shard_rows = V // (N_BLK * N_HEAD)
    row_block = jnp.arange(V, dtype=jnp.int32) // shard_rows
    rank_order = row_block % N_HEAD * N_BLK + row_block // N_HEAD
    row_frac = (rank_order.astype(jnp.float32) / (N_BLK * N_HEAD))[:, None]
    noise = jax.random.truncated_normal(key, -4.0, 4.0, (V, D), jnp.float32)
    row_scale = 1.0 + 2.0 * row_frac
    return noise * row_scale


def draw_attn_weights(key, part):
    key = jax.random.fold_in(key, 13)
    column = jnp.arange(4 * D, dtype=jnp.int32)
    col_scale = jnp.where(column >= 3 * D, 16.0, 1.0)[None, None, :] * D ** (-0.5)
    noise = jax.random.truncated_normal(key, -4.0, 4.0, (LAYERS, D, 4 * D), jnp.float32)
    return noise * col_scale


def draw_norm_gains(key, part):
    key = jax.random.fold_in(key, 14)
    col_frac = jnp.arange(D, dtype=jnp.float32)[None, :] / D
    noise = 0.1 * jax.random.truncated_normal(key, -4.0, 4.0, (2 * LAYERS + 1, D), jnp.float32)
    ramp = 0.5 + col_frac
    return ramp * (1.0 + noise)


def touch_ends(values, own_key, least, largest):
    shape = values.shape
    index_at = [jax.random.randint(jax.random.fold_in(own_key, axis), (), 0, shape[axis]) for axis in range(len(shape))]
    values = values.at[tuple(index_at)].set(least)
    longest = shape.index(max(shape))
    index_at[longest] = (index_at[longest] + 1) % shape[longest]
    return values.at[tuple(index_at)].set(largest)


def shard_levels(rng, extent, cuts, least, high):
    factor_of = 1.0
    for dim, shards_of in cuts:
        draws = jax.random.uniform(jax.random.fold_in(jax.random.fold_in(rng, 6), dim), (shards_of,), jnp.float32, least / len(cuts), high / len(cuts))
        factor_of = factor_of * jnp.repeat(jnp.exp(draws), extent[dim] // shards_of).reshape((-1,) + (1,) * (len(extent) - 1 - dim))
    return factor_of


def rank_table(number_of, slope):
    weights = [(1 << 20) // math.isqrt(grade ** slope) + 1 for grade in range(1, number_of + 1)]
    scale = 1 + sum(weights) // (1 << 30)
    return np.cumsum(np.array([max(1, weight // scale) for weight in weights]))


def ranked_ids(key, extent, number_of, lean):
    listing = rank_table(number_of, lean)
    pick = jax.random.randint(jax.random.fold_in(key, 1), extent, 0, int(listing[number_of - 1]))
    standing = jnp.searchsorted(jnp.asarray(listing, jnp.int32), pick, side="right")
    return jax.random.permutation(jax.random.fold_in(key, 2), number_of)[standing].astype(jnp.int32)


def length_profile(count, total, bound, lean):
    portions = [(1 << 20) // math.isqrt(standing ** lean) + 1 for standing in range(2, count + 1)]
    surplus, given = total - bound - (count - 1), [1] * (count - 1)
    while surplus > 0:
        candidates = [i for i in range(count - 1) if given[i] < bound]
        mass, remaining = sum([portions[i] for i in candidates]), surplus
        for i in candidates:
            more = min(bound - given[i], max(1, remaining * portions[i] // mass), surplus)
            given[i] = given[i] + more
            surplus = surplus - more
    return np.array([bound] + given)


def uneven_parts(key, count, total, reach, lean):
    if count == 2:
        one = jax.random.randint(key, (), max(1, total - reach), min(reach, total - 1) + 1)
        return jnp.stack([one, total - one])
    lengths = jnp.asarray(length_profile(count, total, reach, lean), jnp.int32)
    pairs = (count - 1) // 2
    donor, sink = lengths[1:1 + 2 * pairs:2], lengths[2:2 + 2 * pairs:2]
    slack = jnp.minimum(donor - 1, reach - sink)
    passed = jax.random.randint(jax.random.fold_in(key, 1), (pairs,), 0, 1 << 20) % (slack + 1)
    lengths = lengths.at[1:1 + 2 * pairs:2].set(donor - passed).at[2:2 + 2 * pairs:2].set(sink + passed)
    return lengths[jax.random.permutation(jax.random.fold_in(key, 2), count)]


def centred(rng, extent, scale, most, cuts=(), held_as=jnp.bfloat16):
    drawn = scale * jax.random.normal(rng, extent, jnp.float32)
    if cuts:
        drawn = drawn * shard_levels(rng, extent, cuts, -0.22, 0.18)
    return jnp.clip(drawn, -most, most).astype(held_as)


def setup_inputs(seed: int = 0) -> dict:
    arg_keys = jax.random.split(jax.random.key(seed), 24)
    token_ids = touch_ends(ranked_ids(arg_keys[0], (TOKENS,), V, 2), jax.random.fold_in(arg_keys[0], 3), 0, V - 1).astype(jnp.int32)
    targets = touch_ends(ranked_ids(arg_keys[1], (TOKENS,), V, 2), jax.random.fold_in(arg_keys[1], 3), 0, V - 1).astype(jnp.int32)
    valid_mask = draw_valid_mask(jax.random.fold_in(arg_keys[23], 71), 0)
    cont_lengths = uneven_parts(arg_keys[3], CONTS, TOKENS - PROMPT, CLEN, 2).astype(jnp.int32)
    routes = touch_ends(jax.random.randint(arg_keys[4], (LAYERS, TOKENS), 0, EXPERTS), jax.random.fold_in(arg_keys[4], 1), 0, EXPERTS - 1).astype(jnp.int32)
    vocab_table = draw_vocab_table(jax.random.fold_in(arg_keys[23], 71), 0)
    vocab_first = centred(arg_keys[6], (V, D), (0.0011 * PARAMS ** -0.5), 2.384185791015625e-06, ((0, 32),), jnp.float32)
    vocab_second = jnp.clip(jnp.exp(math.log(4.1430018595488283e-13) - 1.3862944 * jax.random.uniform(arg_keys[7], (V, D), jnp.float32) ** shard_levels(arg_keys[7], (V, D), ((0, 32),), -0.2, 0.2)), 1.0357504648872071e-13, 4.1430018595488283e-13)
    attn_weights = draw_attn_weights(jax.random.fold_in(arg_keys[23], 71), 0)
    attn_first = centred(arg_keys[9], (LAYERS, D, 4 * D), (0.0011 * PARAMS ** -0.5), 2.384185791015625e-06, ((1, 32),), jnp.float32)
    attn_second = jnp.clip(jnp.exp(math.log(4.1430018595488283e-13) - 1.3862944 * jax.random.uniform(arg_keys[10], (LAYERS, D, 4 * D), jnp.float32) ** shard_levels(arg_keys[10], (LAYERS, D, 4 * D), ((1, 32),), -0.2, 0.2)), 1.0357504648872071e-13, 4.1430018595488283e-13)
    router = centred(arg_keys[11], (LAYERS, D, EXPERTS), (0.7 * D ** -0.5), 0.375, ((1, 32),), jnp.float32)
    router_first = centred(arg_keys[12], (LAYERS, D, EXPERTS), (0.0011 * PARAMS ** -0.5), 2.384185791015625e-06, ((1, 32),), jnp.float32)
    router_second = jnp.clip(jnp.exp(math.log(4.1430018595488283e-13) - 1.3862944 * jax.random.uniform(arg_keys[13], (LAYERS, D, EXPERTS), jnp.float32) ** shard_levels(arg_keys[13], (LAYERS, D, EXPERTS), ((1, 32),), -0.2, 0.2)), 1.0357504648872071e-13, 4.1430018595488283e-13)
    norm_gains = draw_norm_gains(jax.random.fold_in(arg_keys[23], 71), 0)
    gains_first = centred(arg_keys[15], (2 * LAYERS + 1, D), (0.033 * PARAMS ** -0.5), 6.103515625e-05, ((1, 32),), jnp.float32)
    gains_second = jnp.clip(jnp.exp(math.log(3.728701791771982e-10) - 1.3862944 * jax.random.uniform(arg_keys[16], (2 * LAYERS + 1, D), jnp.float32) ** shard_levels(arg_keys[16], (2 * LAYERS + 1, D), ((1, 32),), -0.2, 0.2)), 9.321754479429956e-11, 3.728701791771982e-10)
    expert_up = centred(arg_keys[17], (LAYERS, EXPERTS, D, FF), D ** -0.5, 0.21875, ((2, 16), (3, 2)), jnp.float32)
    up_first = centred(arg_keys[18], (LAYERS, EXPERTS, D, FF), (0.0011 * PARAMS ** -0.5), 2.384185791015625e-06, ((2, 16), (3, 2)), jnp.float32)
    up_second = jnp.clip(jnp.exp(math.log(4.1430018595488283e-13) - 1.3862944 * jax.random.uniform(arg_keys[19], (LAYERS, EXPERTS, D, FF), jnp.float32) ** shard_levels(arg_keys[19], (LAYERS, EXPERTS, D, FF), ((2, 16), (3, 2)), -0.2, 0.2)), 1.0357504648872071e-13, 4.1430018595488283e-13)
    expert_down = centred(arg_keys[20], (LAYERS, EXPERTS, D, FF), (FF // 4) ** -0.5, 0.21875, ((2, 16), (3, 2)), jnp.float32)
    down_first = centred(arg_keys[21], (LAYERS, EXPERTS, D, FF), (0.0011 * PARAMS ** -0.5), 2.384185791015625e-06, ((2, 16), (3, 2)), jnp.float32)
    down_second = jnp.clip(jnp.exp(math.log(4.1430018595488283e-13) - 1.3862944 * jax.random.uniform(arg_keys[22], (LAYERS, EXPERTS, D, FF), jnp.float32) ** shard_levels(arg_keys[22], (LAYERS, EXPERTS, D, FF), ((2, 16), (3, 2)), -0.2, 0.2)), 1.0357504648872071e-13, 4.1430018595488283e-13)
    return dict(token_ids=token_ids, targets=targets, valid_mask=valid_mask, cont_lengths=cont_lengths, routes=routes, vocab_table=vocab_table, vocab_first=vocab_first, vocab_second=vocab_second, attn_weights=attn_weights, attn_first=attn_first, attn_second=attn_second, router=router, router_first=router_first, router_second=router_second, norm_gains=norm_gains, gains_first=gains_first, gains_second=gains_second, expert_up=expert_up, up_first=up_first, up_second=up_second, expert_down=expert_down, down_first=down_first, down_second=down_second)


NORM_EPS = 1e-06
BETA_ONE = 0.9
BETA_TWO = 0.95
ADAM_EPS = 1e-08
CLIP_AT = 0.01
MASKED = -1e+30
STEP_RATES = (2.0, 0.25, 0.04, 0.4, 0.04, 0.04)
DECAY_RATES = (0.01, 0.01, 0.01, 0.0, 0.01, 0.01)
HIGHEST = lax.Precision.HIGHEST

@jax.custom_vjp
def low(v):
    return lax.optimization_barrier(v.astype(jnp.bfloat16)).astype(jnp.float32)

@jax.custom_vjp
def low_back(v):
    return v

def low_keep(v):
    return (low(v), None)

def low_pass(kept, grad):
    return (grad,)

def back_keep(v):
    return (v, None)

def back_low(kept, grad):
    return (low(grad),)
low.defvjp(low_keep, low_pass)
low_back.defvjp(back_keep, back_low)

def rms_norm(stream, gain):
    return stream * lax.rsqrt(lax.optimization_barrier(jnp.mean(stream * stream, axis=-1, keepdims=True)) + NORM_EPS) * gain

def segment_of(position, cont_ends):
    later = lax.optimization_barrier(jnp.sum((cont_ends[None, :] <= (position - PROMPT)[:, None]).astype(jnp.int32), axis=1))
    return jnp.where(position < PROMPT, 0, 1 + later).astype(jnp.int32)

def matmul(left, right):
    return jnp.dot(left, right, precision=HIGHEST)

def attention(qkv_rows, segment):
    queries = qkv_rows[:, :D].reshape(TOKENS, HEADS, HEAD_DIM)
    key_rows = qkv_rows[:, D:2 * D].reshape(TOKENS, HEADS, HEAD_DIM)
    value_rows = qkv_rows[:, 2 * D:].reshape(TOKENS, HEADS, HEAD_DIM)
    position = jnp.arange(TOKENS, dtype=jnp.int32)
    query_block = min(512, TOKENS)
    blocks = TOKENS // query_block

    def one_block(element):
        block_queries, query_pos, query_seg = element
        scores = low_back(jnp.einsum('qhd,khd->hqk', block_queries, key_rows, precision=HIGHEST) * HEAD_DIM ** (-0.5))
        shown_mask = ((position[None, :] <= query_pos[:, None]) & ((segment[None, :] == 0) | (segment[None, :] == query_seg[:, None])))[None]
        scores = jnp.where(shown_mask, scores, MASKED)
        row_max = lax.optimization_barrier(jnp.max(scores, axis=-1, keepdims=True))
        chance = jnp.where(shown_mask, jnp.exp(scores - row_max), 0.0)
        row_sum = lax.optimization_barrier(jnp.sum(chance, axis=-1))
        weighted = jnp.einsum('hqk,khd->qhd', low(chance), value_rows, precision=HIGHEST)
        return (weighted / row_sum.T[:, :, None]).reshape(query_block, D)
    result = lax.map(jax.checkpoint(one_block), (queries.reshape(blocks, query_block, HEADS, HEAD_DIM), position.reshape(blocks, query_block), segment.reshape(blocks, query_block)))
    return result.reshape(TOKENS, D)

def forward(params, token_ids, targets, valid_mask, routes, segment):
    vocab_table, attn_weights, router, norm_gains, expert_up, expert_down = params
    table_low = low(vocab_table)
    gains_low = low(norm_gains)
    stream = low_back(table_low[token_ids])
    expert_ids = jnp.arange(EXPERTS, dtype=jnp.int32)
    for layer_index in range(LAYERS):
        weight = low(attn_weights[layer_index])
        normed = low(rms_norm(stream, gains_low[2 * layer_index]))
        qkv_rows = low_back(low(matmul(normed, weight[:, :3 * D])))
        mixed_rows = low_back(low(attention(qkv_rows, segment)))
        stream = stream + low_back(matmul(mixed_rows, weight[:, 3 * D:]))
        normed = low(rms_norm(stream, gains_low[2 * layer_index + 1]))
        chance = jax.nn.softmax(matmul(normed, low(router[layer_index])), axis=-1)
        picked = (routes[layer_index][:, None] == expert_ids[None, :]).astype(jnp.float32)
        gate_value = lax.optimization_barrier(jnp.sum(chance * picked, axis=1))
        before = low_back(jnp.einsum('td,edf->tef', normed, low(expert_up[layer_index]), precision=HIGHEST))
        hidden = low(jax.nn.gelu(before, approximate=False) * picked[:, :, None])
        output = low_back(jnp.einsum('tef,edf->td', hidden, low(expert_down[layer_index]), precision=HIGHEST))
        stream = stream + gate_value[:, None] * output
    final = low(rms_norm(stream, gains_low[2 * LAYERS]))
    loss_rows = min(512, TOKENS)
    loss_blocks = TOKENS // loss_rows

    def loss_block(element):
        block_rows, block_targets, block_valid = element
        logits = low_back(matmul(block_rows, table_low.T) * D ** (-0.5))
        row_max = lax.optimization_barrier(jnp.max(logits, axis=-1, keepdims=True))
        log_total = row_max[:, 0] + jnp.log(lax.optimization_barrier(jnp.sum(jnp.exp(logits - row_max), axis=-1)))
        target_logit = jnp.take_along_axis(logits, block_targets[:, None], axis=1)[:, 0]
        return jnp.sum(block_valid * (log_total - target_logit))
    totals = lax.map(jax.checkpoint(loss_block), (final.reshape(loss_blocks, loss_rows, D), targets.reshape(loss_blocks, loss_rows), valid_mask.astype(jnp.float32).reshape(loss_blocks, loss_rows)))
    return jnp.sum(totals)

def adam_update(weight, moment_one, moment_two, gradient, step_rate, decay_rate):
    first_new = BETA_ONE * moment_one + (1.0 - BETA_ONE) * gradient
    second_new = BETA_TWO * moment_two + (1.0 - BETA_TWO) * gradient * gradient
    normalized = first_new / (1.0 - BETA_ONE ** STEP) / (jnp.sqrt(second_new / (1.0 - BETA_TWO ** STEP)) + ADAM_EPS)
    return (weight - step_rate * (normalized + decay_rate * weight), first_new, second_new)

def reference(token_ids, targets, valid_mask, cont_lengths, routes, vocab_table, vocab_first, vocab_second, attn_weights, attn_first, attn_second, router, router_first, router_second, norm_gains, gains_first, gains_second, expert_up, up_first, up_second, expert_down, down_first, down_second):
    position = jnp.arange(TOKENS, dtype=jnp.int32)
    segment = segment_of(position, jnp.cumsum(cont_lengths).astype(jnp.int32))
    token_count = jnp.sum(valid_mask).astype(jnp.float32)
    params = (vocab_table, attn_weights, router, norm_gains, expert_up, expert_down)
    loss_sum, pullback = jax.vjp(lambda *weights: forward(weights, token_ids, targets, valid_mask, routes, segment), *params)
    gradients = pullback((jnp.ones_like(loss_sum) / token_count).astype(loss_sum.dtype))
    grad_norm = jnp.sqrt(sum((jnp.sum(gradient * gradient) for gradient in gradients)))
    factor = CLIP_AT / jnp.maximum(grad_norm, CLIP_AT)
    firsts = (vocab_first, attn_first, router_first, gains_first, up_first, down_first)
    seconds = (vocab_second, attn_second, router_second, gains_second, up_second, down_second)
    results = [loss_sum, token_count, grad_norm]
    for number in range(6):
        results.extend(adam_update(params[number], firsts[number], seconds[number], factor * gradients[number], STEP_RATES[number], DECAY_RATES[number]))
    return tuple(results)
```

```python
import functools

import jax
import jax.numpy as jnp
from jax import lax
from jax.experimental import pallas as pl
from jax.experimental.pallas import tpu as pltpu
from jax.sharding import Mesh, PartitionSpec as P

D = 768
HEADS = 12
HEAD_DIM = 64
EXPERTS = 2
LAYERS = 2
PROMPT = 2048
STEP = 10

NORM_EPS = 1e-06
BETA_ONE = 0.9
BETA_TWO = 0.95
ADAM_EPS = 1e-08
CLIP_AT = 0.01
MASKED = -1e30
STEP_RATES = (2.0, 0.25, 0.04, 0.4, 0.04, 0.04)
DECAY_RATES = (0.01, 0.01, 0.01, 0.0, 0.01, 0.01)

ALL = ("z", "x", "core", "head")
BLK = ("z", "x", "core")
PLANE = ("x", "head")
LINE = ("z", "core")
MIB = 2**20


def rms_norm(stream, gain):
    return stream * lax.rsqrt(jnp.mean(stream * stream, axis=-1, keepdims=True) + NORM_EPS) * gain


def segment_of(position, cont_ends):
    later = jnp.sum((cont_ends[None, :] <= (position - PROMPT)[:, None]).astype(jnp.int32), axis=1)
    return jnp.where(position < PROMPT, 0, 1 + later)


def matmul(left, right):
    return jnp.dot(left, right, preferred_element_type=jnp.float32)


def inner(left, right):
    return lax.dot_general(
        left, right, (((0,), (0,)), ((), ())), preferred_element_type=jnp.float32
    )


def outer(left, right):
    return lax.dot_general(
        left, right, (((1,), (1,)), ((), ())), preferred_element_type=jnp.float32
    )


def gather_plane(rows):
    return lax.all_gather(rows, PLANE, axis=0, tiled=True)


def scatter_plane(partial_rows):
    return lax.psum_scatter(
        partial_rows.astype(jnp.bfloat16), PLANE, scatter_dimension=0, tiled=True
    ).astype(jnp.float32)


def gather_all(rows):
    return lax.all_gather(rows, ALL, axis=0, tiled=True)


def scatter_all(partial_rows):
    return lax.psum_scatter(
        partial_rows.astype(jnp.bfloat16), ALL, scatter_dimension=0, tiled=True
    ).astype(jnp.float32)


def key_position(index, part, chunk):
    lane = 2 * chunk
    start = (part // 2) * (2 * lane) + (part % 2) * chunk
    return start + index + jnp.where(index >= chunk, chunk, 0)


def attend_kernel(
    chunk, query, keys, values, near_keys, near_values, query_pos, query_seg, near_pos, near_seg,
    out, log_total, scores, values_t,
):
    lane, feature = query.shape
    group = feature // HEAD_DIM
    prompt_rows = keys.shape[0]
    parts = prompt_rows // lane
    query_t = (query[...].astype(jnp.float32) * HEAD_DIM ** (-0.5)).T.astype(jnp.bfloat16)
    values_t[:, :prompt_rows] = values[...].astype(jnp.float32).T.astype(jnp.bfloat16)
    values_t[:, prompt_rows:] = near_values[...].astype(jnp.float32).T.astype(jnp.bfloat16)
    row_of = lax.broadcasted_iota(jnp.int32, (feature, lane), 0)
    q_pos = query_pos[...]

    for head in range(group):
        low, high = head * HEAD_DIM, (head + 1) * HEAD_DIM
        query_h = jnp.where((row_of >= low) & (row_of < high), query_t, 0)

        def score_part(part, peak):
            block = keys[pl.ds(pl.multiple_of(part * lane, lane), lane), :]
            value = matmul(block, query_h)
            index = lax.broadcasted_iota(jnp.int32, (lane, lane), 0)
            value = jnp.where(key_position(index, part, chunk) <= q_pos, value, MASKED)
            scores[pl.ds(pl.multiple_of(part * lane, lane), lane), :] = value
            return jnp.maximum(peak, jnp.max(value, axis=0, keepdims=True))

        peak = lax.fori_loop(0, parts, score_part, jnp.full((1, lane), MASKED, jnp.float32))
        near_peaks = []
        for side in range(2):
            columns = slice(side * chunk, (side + 1) * chunk)
            rows = slice(side * lane, (side + 1) * lane)
            value = matmul(near_keys[rows, :], query_h[:, columns])
            shown = (
                (near_seg[rows, :] == query_seg[:, columns])
                & (near_pos[rows, :] <= q_pos[:, columns])
                & (near_pos[rows, :] >= PROMPT)
            )
            value = jnp.where(shown, value, MASKED)
            scores[prompt_rows : prompt_rows + lane, columns] = value
            near_peaks.append(jnp.max(value, axis=0, keepdims=True))
        peak = jnp.maximum(peak, jnp.concatenate(near_peaks, axis=1))

        def weigh_part(part, state):
            total, mixed = state
            start = pl.multiple_of(part * lane, lane)
            chance = jnp.exp(scores[pl.ds(start, lane), :] - peak)
            total = total + jnp.sum(chance, axis=0, keepdims=True)
            mixed = mixed + matmul(
                values_t[low:high, pl.ds(start, lane)], chance.astype(jnp.bfloat16)
            )
            return total, mixed

        total, mixed = lax.fori_loop(
            0,
            parts,
            weigh_part,
            (jnp.zeros((1, lane), jnp.float32), jnp.zeros((HEAD_DIM, lane), jnp.float32)),
        )
        near_total, near_mixed = [], []
        for side in range(2):
            columns = slice(side * chunk, (side + 1) * chunk)
            rows = slice(prompt_rows + side * lane, prompt_rows + (side + 1) * lane)
            chance = jnp.exp(scores[prompt_rows : prompt_rows + lane, columns] - peak[:, columns])
            near_total.append(jnp.sum(chance, axis=0, keepdims=True))
            near_mixed.append(matmul(values_t[low:high, rows], chance.astype(jnp.bfloat16)))
        total = total + jnp.concatenate(near_total, axis=1)
        mixed = mixed + jnp.concatenate(near_mixed, axis=1)
        out[low:high, :] = mixed / total
        log_total[head : head + 1, :] = peak + jnp.log(total)


def attend(queries, keys, values, near_keys, near_values, places, chunk):
    lane, feature = queries.shape
    prompt_rows = keys.shape[0]
    group = feature // HEAD_DIM
    total_rows = prompt_rows + lane
    return pl.pallas_call(
        functools.partial(attend_kernel, chunk),
        out_shape=(
            jax.ShapeDtypeStruct((feature, lane), jnp.float32),
            jax.ShapeDtypeStruct((group, lane), jnp.float32),
        ),
        in_specs=[pl.BlockSpec(memory_space=pltpu.VMEM)] * 9,
        out_specs=(pl.BlockSpec(memory_space=pltpu.VMEM),) * 2,
        scratch_shapes=[
            pltpu.VMEM((total_rows, lane), jnp.float32),
            pltpu.VMEM((feature, prompt_rows + 2 * lane), jnp.bfloat16),
        ],
        compiler_params=pltpu.CompilerParams(vmem_limit_bytes=48 * MIB),
        cost_estimate=pl.CostEstimate(
            flops=8 * group * lane * total_rows * 128,
            bytes_accessed=8 * MIB,
            transcendentals=group * lane * total_rows,
        ),
    )(queries, keys, values, near_keys, near_values, *places)


def attend_back_kernel(
    chunk, query, keys, values, near_keys, near_values, query_pos, query_seg, near_pos, near_seg,
    log_total, delta, answer, query_grad, far_grad, near_grad, keys_t,
):
    lane, feature = query.shape
    group = feature // HEAD_DIM
    prompt_rows = keys.shape[0]
    parts = prompt_rows // lane
    scaled = (query[...].astype(jnp.float32) * HEAD_DIM ** (-0.5)).astype(jnp.bfloat16)
    query_t = scaled.astype(jnp.float32).T.astype(jnp.bfloat16)
    answers = answer[...]
    answer_t = answers.astype(jnp.float32).T.astype(jnp.bfloat16)
    keys_t[:, :prompt_rows] = keys[...].astype(jnp.float32).T.astype(jnp.bfloat16)
    keys_t[:, prompt_rows:] = near_keys[...].astype(jnp.float32).T.astype(jnp.bfloat16)
    row_of = lax.broadcasted_iota(jnp.int32, (feature, lane), 0)
    column_of = lax.broadcasted_iota(jnp.int32, (lane, feature), 1)
    q_pos = query_pos[...]

    for head in range(group):
        low, high = head * HEAD_DIM, (head + 1) * HEAD_DIM
        in_rows = (row_of >= low) & (row_of < high)
        in_columns = (column_of >= low) & (column_of < high)
        query_ht = jnp.where(in_rows, query_t, 0)
        answer_ht = jnp.where(in_rows, answer_t, 0)
        query_h = jnp.where(in_columns, scaled, 0)
        answer_h = jnp.where(in_columns, answers, 0)
        log_h = log_total[head : head + 1, :]
        delta_h = delta[head : head + 1, :]

        def slopes(key_block, value_block, shown, columns):
            value = matmul(key_block, query_ht[:, columns])
            chance = jnp.exp(jnp.where(shown, value - log_h[:, columns], MASKED))
            slope = matmul(value_block, answer_ht[:, columns])
            change = (chance * (slope - delta_h[:, columns])).astype(jnp.bfloat16)
            chance = chance.astype(jnp.bfloat16)
            return change, matmul(change, query_h[columns]), matmul(chance, answer_h[columns])

        def back_part(part, total):
            start = pl.multiple_of(part * lane, lane)
            rows = pl.ds(start, lane)
            index = lax.broadcasted_iota(jnp.int32, (lane, lane), 0)
            shown = key_position(index, part, chunk) <= q_pos
            change, key_part, value_part = slopes(
                keys[rows, :], values[rows, :], shown, slice(0, lane)
            )
            if head == 0:
                far_grad[0, rows, :] = key_part
                far_grad[1, rows, :] = value_part
            else:
                far_grad[0, rows, :] += key_part
                far_grad[1, rows, :] += value_part
            return total + matmul(keys_t[low:high, rows], change)

        total = lax.fori_loop(0, parts, back_part, jnp.zeros((HEAD_DIM, lane), jnp.float32))
        near_total = []
        for side in range(2):
            columns = slice(side * chunk, (side + 1) * chunk)
            rows = slice(side * lane, (side + 1) * lane)
            shown = (
                (near_seg[rows, :] == query_seg[:, columns])
                & (near_pos[rows, :] <= q_pos[:, columns])
                & (near_pos[rows, :] >= PROMPT)
            )
            change, key_part, value_part = slopes(
                near_keys[rows, :], near_values[rows, :], shown, columns
            )
            if head == 0:
                near_grad[0, rows, :] = key_part
                near_grad[1, rows, :] = value_part
            else:
                near_grad[0, rows, :] += key_part
                near_grad[1, rows, :] += value_part
            near_rows = slice(prompt_rows + side * lane, prompt_rows + (side + 1) * lane)
            near_total.append(matmul(keys_t[low:high, near_rows], change))
        query_grad[low:high, :] = (total + jnp.concatenate(near_total, axis=1)) * HEAD_DIM ** (-0.5)


def attend_back(queries, keys, values, near_keys, near_values, places, log_total, delta, answer, chunk):
    lane, feature = queries.shape
    prompt_rows = keys.shape[0]
    group = feature // HEAD_DIM
    total_rows = prompt_rows + lane
    return pl.pallas_call(
        functools.partial(attend_back_kernel, chunk),
        out_shape=(
            jax.ShapeDtypeStruct((feature, lane), jnp.float32),
            jax.ShapeDtypeStruct((2, prompt_rows, feature), jnp.float32),
            jax.ShapeDtypeStruct((2, 2 * lane, feature), jnp.float32),
        ),
        in_specs=[pl.BlockSpec(memory_space=pltpu.VMEM)] * 12,
        out_specs=(pl.BlockSpec(memory_space=pltpu.VMEM),) * 3,
        scratch_shapes=[pltpu.VMEM((feature, prompt_rows + 2 * lane), jnp.bfloat16)],
        compiler_params=pltpu.CompilerParams(vmem_limit_bytes=48 * MIB),
        cost_estimate=pl.CostEstimate(
            flops=20 * group * lane * total_rows * 128,
            bytes_accessed=12 * MIB,
            transcendentals=group * lane * total_rows,
        ),
    )(queries, keys, values, near_keys, near_values, *places, log_total, delta, answer)


def adam_update(weight, moment_one, moment_two, gradient, step_rate, decay_rate):
    first_new = BETA_ONE * moment_one + (1.0 - BETA_ONE) * gradient
    second_new = BETA_TWO * moment_two + (1.0 - BETA_TWO) * gradient * gradient
    normalized = (
        first_new
        / (1.0 - BETA_ONE**STEP)
        / (jnp.sqrt(second_new / (1.0 - BETA_TWO**STEP)) + ADAM_EPS)
    )
    return (weight - step_rate * (normalized + decay_rate * weight), first_new, second_new)


def per_device(
    token_ids,
    targets,
    valid_mask,
    cont_lengths,
    routes,
    vocab_table,
    vocab_first,
    vocab_second,
    attn_weights,
    attn_first,
    attn_second,
    router,
    router_first,
    router_second,
    norm_gains,
    gains_first,
    gains_second,
    expert_up,
    up_first,
    up_second,
    expert_down,
    down_first,
    down_second,
):
    slabs = lax.axis_size("z")
    planes = lax.axis_size("x")
    cores = lax.axis_size("core")
    sides = lax.axis_size("head")
    groups = planes * sides
    z_at, x_at, core_at, side_at = (lax.axis_index(name) for name in ALL)
    blk_at = (z_at * planes + x_at) * cores + core_at
    device_at = blk_at * sides + side_at
    group_at = x_at * sides + side_at
    tokens = valid_mask.shape[0]
    chunk = token_ids.shape[0]
    own = chunk // sides
    lane = planes * chunk
    feature = D // groups
    wide = expert_up.shape[3] // planes
    shard_rows = vocab_table.shape[0]
    logit_scale = D ** (-0.5)

    cont_ends = jnp.cumsum(cont_lengths)
    valid_f = valid_mask.astype(jnp.float32)
    token_count = jnp.sum(valid_mask).astype(jnp.float32)
    expert_ids = jnp.arange(EXPERTS, dtype=jnp.int32)

    whole = lax.all_gather(
        jnp.concatenate([token_ids[None], targets[None], routes], axis=0), BLK, axis=0
    )
    ids_all = whole[:, 0].reshape(tokens)
    targets_all = whole[:, 1].reshape(tokens)
    routes_lane = (
        lax.dynamic_index_in_dim(
            whole.reshape(slabs, planes, cores, 2 + LAYERS, chunk), z_at, 0, False
        )
    )
    routes_lane = lax.dynamic_index_in_dim(routes_lane, core_at, 1, False)[:, 2:]
    routes_lane = routes_lane.transpose(1, 0, 2).reshape(LAYERS, lane)
    routes_own = lax.dynamic_slice_in_dim(routes, side_at * own, own, axis=1)

    table = vocab_table.astype(jnp.bfloat16)
    small_all = lax.all_gather(
        jnp.concatenate(
            [router.transpose(1, 0, 2).reshape(-1, LAYERS * EXPERTS), norm_gains.T], axis=1
        ).astype(jnp.bfloat16),
        ALL,
        axis=0,
        tiled=True,
    )
    router_all = small_all[:, : LAYERS * EXPERTS].reshape(D, LAYERS, EXPERTS).transpose(1, 0, 2)
    gains_f = small_all[:, LAYERS * EXPERTS :].T.astype(jnp.float32)

    attn_low = attn_weights.astype(jnp.bfloat16)
    rows_of = attn_low.shape[1]
    qkv_send = attn_low[:, :, : 3 * D].reshape(LAYERS, rows_of, 3, groups, feature)
    qkv_send = qkv_send.transpose(3, 0, 1, 2, 4).reshape(groups, LAYERS, rows_of, 3 * feature)
    qkv_got = lax.all_to_all(qkv_send, PLANE, split_axis=0, concat_axis=0, tiled=True)
    out_all = lax.all_gather(attn_low[:, :, 3 * D :], ALL, axis=1, tiled=True)
    out_mine = lax.dynamic_slice_in_dim(out_all, group_at * feature, feature, axis=1)
    expert_send = jnp.stack([expert_up, expert_down], axis=1).astype(jnp.bfloat16)
    depth = expert_send.shape[3]
    expert_send = expert_send.reshape(LAYERS, 2 * EXPERTS, depth, planes, wide)
    expert_send = expert_send.transpose(3, 0, 1, 2, 4)
    expert_got = lax.all_to_all(expert_send, ("x",), split_axis=0, concat_axis=0, tiled=True)
    qkv_weights, expert_weights = [], []
    for layer_index in range(LAYERS):
        block = lax.all_gather(qkv_got[:, layer_index], LINE, axis=0)
        block = block.reshape(slabs, cores, planes, sides, rows_of, 3 * feature)
        qkv_weights.append(block.transpose(0, 2, 1, 3, 4, 5).reshape(D, 3 * feature))
        block = lax.all_gather(expert_got[:, layer_index], LINE, axis=0)
        block = block.reshape(slabs, cores, planes, 2, EXPERTS, depth, wide)
        block = block.transpose(3, 4, 0, 2, 1, 5, 6).reshape(2, EXPERTS, D, wide)
        expert_weights.append(block)

    offsets = jnp.arange(chunk, dtype=jnp.int32)
    first_blk = z_at * planes * cores + core_at
    query_pos = jnp.concatenate([(first_blk + cores * part) * chunk + offsets for part in range(planes)])
    near_blks = [first_blk - 1 + part for part in range(2 * planes)]
    near_pos = jnp.concatenate([blk * chunk + offsets for blk in near_blks])
    query_seg = segment_of(query_pos, cont_ends)
    near_seg = segment_of(near_pos, cont_ends)
    places = (query_pos[None, :], query_seg[None, :], near_pos[:, None], near_seg[:, None])

    def near_index(blk):
        blk = jnp.maximum(blk, 0)
        slab, rest = blk // (planes * cores), blk % (planes * cores)
        return slab * (planes * cores) + (rest % cores) * planes + rest // cores

    def spread_keys(key_values):
        return lax.all_gather(key_values, LINE, axis=0, tiled=True)

    def near_rows(spread):
        return jnp.concatenate(
            [
                lax.dynamic_slice_in_dim(spread, near_index(blk) * chunk, chunk, axis=0)
                for blk in near_blks
            ],
            axis=0,
        )

    vocab_ids = device_at * shard_rows + jnp.arange(shard_rows, dtype=jnp.int32)
    token_hot = (ids_all[:, None] == vocab_ids[None, :]).astype(jnp.bfloat16)
    stream = scatter_all(matmul(token_hot, table))

    kept = []
    for layer_index in range(LAYERS):
        up, down = expert_weights[layer_index][0], expert_weights[layer_index][1]
        normed_lane = gather_plane(
            rms_norm(stream, gains_f[2 * layer_index]).astype(jnp.bfloat16)
        )
        qkv = matmul(normed_lane, qkv_weights[layer_index]).astype(jnp.bfloat16)
        queries = qkv[:, :feature]
        spread = spread_keys(qkv[:, feature:])
        far = spread[:PROMPT]
        near = near_rows(spread)
        key_args = (far[:, :feature], far[:, feature:], near[:, :feature], near[:, feature:])
        mixed_t, log_total = attend(queries, *key_args, places, chunk)
        mixed = mixed_t.T
        mixed_low = mixed.astype(jnp.bfloat16)
        middle = stream + scatter_plane(matmul(mixed_low, out_mine[layer_index]))
        normed_two = rms_norm(middle, gains_f[2 * layer_index + 1]).astype(jnp.bfloat16)
        chance = jax.nn.softmax(matmul(normed_two, router_all[layer_index]), axis=-1)
        wide_rows = gather_plane(normed_two)
        picked = routes_lane[layer_index][:, None] == expert_ids[None, :]
        before = jnp.where(picked[:, :1], matmul(wide_rows, up[0]), matmul(wide_rows, up[1]))
        active = jax.nn.gelu(before, approximate=False)
        hidden = [
            jnp.where(picked[:, e : e + 1], active, 0.0).astype(jnp.bfloat16)
            for e in range(EXPERTS)
        ]
        output = scatter_plane(outer(hidden[0], down[0]) + outer(hidden[1], down[1]))
        own_pick = (routes_own[layer_index][:, None] == expert_ids[None, :]).astype(jnp.float32)
        gate = jnp.sum(chance * own_pick, axis=1, keepdims=True)
        kept.append(
            (
                stream, normed_lane, queries, key_args, mixed, mixed_low, log_total, middle,
                normed_two, chance, wide_rows, picked, before, hidden, output, own_pick, gate,
            )
        )
        stream = middle + gate * output

    final_gain = gains_f[2 * LAYERS]
    final_all = gather_all(rms_norm(stream, final_gain).astype(jnp.bfloat16))
    logits = outer(final_all, table) * logit_scale
    row_max = jnp.max(logits, axis=1, keepdims=True)
    row_log = row_max[:, 0] + jnp.log(jnp.sum(jnp.exp(logits - row_max), axis=1))
    target_hot = targets_all[:, None] == vocab_ids[None, :]
    hit_loss = jnp.sum(jnp.where(target_hot, logits, 0.0) * valid_f[:, None])
    row_logs = lax.all_gather(row_log, ALL, axis=0)
    log_sum = jax.nn.logsumexp(row_logs, axis=0)
    own_log = lax.dynamic_slice_in_dim(log_sum * valid_f, device_at * own, own)
    own_loss = jnp.sum(own_log) - hit_loss
    logit_grad = (
        (jnp.exp(logits - log_sum[:, None]) - target_hot.astype(jnp.float32))
        * (valid_f / token_count)[:, None]
    ).astype(jnp.bfloat16)
    final_grad = scatter_all(matmul(logit_grad, table) * logit_scale)
    table_grad = inner(logit_grad, final_all) * logit_scale
    stream_grad, final_gain_grad = jax.vjp(rms_norm, stream, final_gain)[1](final_grad)

    qkv_shares = [None] * LAYERS
    out_shares = [None] * LAYERS
    router_list = [None] * LAYERS
    expert_shares = [None] * LAYERS
    gain_list = [None] * (2 * LAYERS + 1)
    gain_list[2 * LAYERS] = final_gain_grad
    for layer_index in reversed(range(LAYERS)):
        (
            stream, normed_lane, queries, key_args, mixed, mixed_low, log_total, middle,
            normed_two, chance, wide_rows, picked, before, hidden, output, own_pick, gate,
        ) = kept[layer_index]
        up, down = expert_weights[layer_index][0], expert_weights[layer_index][1]
        out_grad = (gate * stream_grad).astype(jnp.bfloat16)
        wide_grad = gather_plane(out_grad)
        chance_grad = jnp.sum(stream_grad * output, axis=1)[:, None] * own_pick
        choice_grad = chance * (chance_grad - jnp.sum(chance * chance_grad, axis=1, keepdims=True))
        router_list[layer_index] = jnp.dot(
            normed_two.astype(jnp.float32).T, choice_grad, precision=lax.Precision.HIGHEST
        )
        normed_grad = jnp.dot(
            choice_grad,
            router_all[layer_index].astype(jnp.float32).T,
            precision=lax.Precision.HIGHEST,
        )
        hidden_grad = jnp.where(
            picked[:, :1], matmul(wide_grad, down[0]), matmul(wide_grad, down[1])
        )
        _, gelu_back = jax.vjp(lambda v: jax.nn.gelu(v, approximate=False), before)
        before_grad = gelu_back(hidden_grad)[0]
        before_grads = [
            jnp.where(picked[:, e : e + 1], before_grad, 0.0).astype(jnp.bfloat16)
            for e in range(EXPERTS)
        ]
        normed_grad = normed_grad + scatter_plane(
            outer(before_grads[0], up[0]) + outer(before_grads[1], up[1])
        )
        expert_grad = jnp.stack(
            [inner(wide_rows, before_grads[e]) for e in range(EXPERTS)]
            + [inner(wide_grad, hidden[e]) for e in range(EXPERTS)]
        ).astype(jnp.bfloat16)
        expert_grad = expert_grad.reshape(2 * EXPERTS, slabs, planes, cores, depth, wide)
        expert_grad = expert_grad.transpose(1, 3, 2, 0, 4, 5).reshape(
            slabs * cores, planes, 2 * EXPERTS, depth, wide
        )
        expert_grad = lax.psum_scatter(expert_grad, LINE, scatter_dimension=0, tiled=True)[0]
        expert_grad = lax.all_to_all(
            expert_grad, ("x",), split_axis=0, concat_axis=0, tiled=True
        )
        expert_shares[layer_index] = (
            expert_grad.transpose(1, 2, 0, 3)
            .reshape(2, EXPERTS, depth, planes * wide)
            .astype(jnp.float32)
        )
        middle_part, gain_list[2 * layer_index + 1] = jax.vjp(
            rms_norm, middle, gains_f[2 * layer_index + 1]
        )[1](normed_grad)
        middle_grad = stream_grad + middle_part
        branch_lane = gather_plane(middle_grad.astype(jnp.bfloat16))
        answer_f = outer(branch_lane, out_mine[layer_index])
        answer = answer_f.astype(jnp.bfloat16)
        out_proj_grad = inner(mixed_low, branch_lane).astype(jnp.bfloat16)
        out_full = jnp.zeros((D, D), jnp.bfloat16)
        out_full = lax.dynamic_update_slice_in_dim(out_full, out_proj_grad, group_at * feature, 0)
        out_shares[layer_index] = lax.psum_scatter(
            out_full, ALL, scatter_dimension=0, tiled=True
        ).astype(jnp.float32)
        delta = jnp.sum(
            (answer.astype(jnp.float32) * mixed).reshape(lane, feature // HEAD_DIM, HEAD_DIM),
            axis=-1,
        ).T
        query_grad_t, far_grad, near_grad = attend_back(
            queries, *key_args, places, log_total, delta, answer, chunk
        )
        spread_grad = jnp.zeros((tokens, 2 * feature), jnp.float32)
        spread_grad = spread_grad.at[:PROMPT].set(
            far_grad.transpose(1, 0, 2).reshape(PROMPT, 2 * feature)
        )
        near_grad = near_grad.transpose(1, 0, 2).reshape(2 * lane, 2 * feature)
        for part, blk in enumerate(near_blks):
            start = near_index(blk) * chunk
            piece = lax.dynamic_slice_in_dim(spread_grad, start, chunk, axis=0)
            piece = piece + near_grad[part * chunk : (part + 1) * chunk]
            spread_grad = lax.dynamic_update_slice_in_dim(spread_grad, piece, start, axis=0)
        key_value_grad = lax.psum_scatter(
            spread_grad.astype(jnp.bfloat16), LINE, scatter_dimension=0, tiled=True
        )
        qkv_grad = jnp.concatenate([query_grad_t.T.astype(jnp.bfloat16), key_value_grad], axis=1)
        qkv_proj = inner(normed_lane, qkv_grad).astype(jnp.bfloat16)
        qkv_proj = qkv_proj.reshape(slabs, planes, cores, sides, rows_of, 3 * feature)
        qkv_proj = qkv_proj.transpose(0, 2, 1, 3, 4, 5).reshape(
            slabs * cores, groups, rows_of, 3 * feature
        )
        qkv_proj = lax.psum_scatter(qkv_proj, LINE, scatter_dimension=0, tiled=True)[0]
        qkv_proj = lax.all_to_all(qkv_proj, PLANE, split_axis=0, concat_axis=0, tiled=True)
        qkv_shares[layer_index] = (
            qkv_proj.reshape(groups, rows_of, 3, feature)
            .transpose(1, 2, 0, 3)
            .reshape(rows_of, 3 * D)
            .astype(jnp.float32)
        )
        normed_att_grad = scatter_plane(outer(qkv_grad, qkv_weights[layer_index]))
        stream_part, gain_list[2 * layer_index] = jax.vjp(
            rms_norm, stream, gains_f[2 * layer_index]
        )[1](normed_att_grad)
        stream_grad = middle_grad + stream_part

    embed_grad = gather_all(stream_grad.astype(jnp.bfloat16))
    table_share = table_grad + inner(token_hot, embed_grad)
    small = jnp.concatenate(
        [jnp.stack(router_list).transpose(1, 0, 2).reshape(D, -1), jnp.stack(gain_list).T], axis=1
    )
    small = lax.psum_scatter(small, ALL, scatter_dimension=0, tiled=True)
    router_share = (
        small[:, : LAYERS * EXPERTS].reshape(rows_of, LAYERS, EXPERTS).transpose(1, 0, 2)
    )
    gain_share = small[:, LAYERS * EXPERTS :].T
    attn_share = jnp.stack(
        [
            jnp.concatenate([qkv_shares[index], out_shares[index]], axis=1)
            for index in range(LAYERS)
        ]
    )
    up_share = jnp.stack([share[0] for share in expert_shares])
    down_share = jnp.stack([share[1] for share in expert_shares])
    shares = (table_share, attn_share, router_share, gain_share, up_share, down_share)
    squares = jnp.sum(table_share * table_share)
    for share_part in shares[1:]:
        squares = squares + jnp.sum(share_part * share_part)
    square_total, loss_sum = lax.psum((squares, own_loss), ALL)
    grad_norm = jnp.sqrt(square_total)
    factor = CLIP_AT / jnp.maximum(grad_norm, CLIP_AT)
    weights = (vocab_table, attn_weights, router, norm_gains, expert_up, expert_down)
    firsts = (vocab_first, attn_first, router_first, gains_first, up_first, down_first)
    seconds = (vocab_second, attn_second, router_second, gains_second, up_second, down_second)
    results = [loss_sum, token_count, grad_norm]
    for number in range(6):
        results.extend(
            adam_update(
                weights[number],
                firsts[number],
                seconds[number],
                factor * shares[number],
                STEP_RATES[number],
                DECAY_RATES[number],
            )
        )
    return tuple(results)


def solution(mesh):
    blocks, sides = mesh.shape["blk"], mesh.shape["head"]
    fine = Mesh(mesh.devices.reshape(blocks // 4, 2, 2, sides), ALL)
    weight_specs = (
        (P(ALL, None),) * 3
        + (P(None, ALL, None),) * 3
        + (P(None, ALL, None),) * 3
        + (P(None, ALL),) * 3
        + (P(None, None, BLK, "head"),) * 6
    )
    return jax.shard_map(
        per_device,
        mesh=fine,
        in_specs=(P(BLK), P(BLK), P(), P(), P(None, BLK)) + weight_specs,
        out_specs=(P(), P(), P()) + weight_specs,
        check_vma=False,
    )
```

```python
import functools

import jax
import jax.numpy as jnp
from jax import lax
from jax.experimental import pallas as pl
from jax.experimental.pallas import tpu as pltpu
from jax.sharding import Mesh, PartitionSpec as P

D = 768
HEADS = 12
HEAD_DIM = 64
EXPERTS = 2
LAYERS = 2
PROMPT = 2048
STEP = 10

NORM_EPS = 1e-06
BETA_ONE = 0.9
BETA_TWO = 0.95
ADAM_EPS = 1e-08
CLIP_AT = 0.01
MASKED = -1e30
STEP_RATES = (2.0, 0.25, 0.04, 0.4, 0.04, 0.04)
DECAY_RATES = (0.01, 0.01, 0.01, 0.0, 0.01, 0.01)

ALL = ("z", "x", "core", "head")
BLK = ("z", "x", "core")
PLANE = ("x", "head")
LINE = ("z", "core")
MIB = 2**20
MESH = pl.DeviceIdType.MESH
ANY = pl.BlockSpec(memory_space=pl.ANY)
VMEM = pl.BlockSpec(memory_space=pltpu.VMEM)


def rms_norm(stream, gain):
    return stream * lax.rsqrt(jnp.mean(stream * stream, axis=-1, keepdims=True) + NORM_EPS) * gain


def segment_of(position, cont_ends):
    later = jnp.sum((cont_ends[None, :] <= (position - PROMPT)[:, None]).astype(jnp.int32), axis=1)
    return jnp.where(position < PROMPT, 0, 1 + later)


def matmul(left, right):
    return jnp.dot(left, right, preferred_element_type=jnp.float32)


def inner(left, right):
    return lax.dot_general(
        left, right, (((0,), (0,)), ((), ())), preferred_element_type=jnp.float32
    )


def outer(left, right):
    return lax.dot_general(
        left, right, (((1,), (1,)), ((), ())), preferred_element_type=jnp.float32
    )


def gather_plane(rows):
    return lax.all_gather(rows, PLANE, axis=0, tiled=True)


def scatter_plane(partial_rows):
    return lax.psum_scatter(
        partial_rows.astype(jnp.bfloat16), PLANE, scatter_dimension=0, tiled=True
    ).astype(jnp.float32)


def place():
    return tuple(lax.axis_index(name) for name in ALL)


def sizes():
    return tuple(lax.axis_size(name) for name in ALL)


def remote(source, target, send, receive, device):
    return pltpu.make_async_remote_copy(
        src_ref=source, dst_ref=target, send_sem=send, recv_sem=receive,
        device_id=device, device_id_type=MESH,
    )


def greet(devices):
    barrier = pltpu.get_barrier_semaphore()
    for device in devices:
        pl.semaphore_signal(barrier, inc=1, device_id=device, device_id_type=MESH)
    pl.semaphore_wait(barrier, len(devices))


def around():
    z, x, c, y = place()
    return (z, x, c, y), (z, 1 - x, c, y), (z, x, c, 1 - y), (z, x, 1 - c, y)


def swap_kernel(broadcast, source, out, send_sem, receive_sem, own_sem):
    n_z, n_x, n_c, n_y = sizes()
    count = n_z * n_x * n_c * n_y
    z, x, c, y = place()
    me = ((z * n_x + x) * n_c + c) * n_y + y

    def device_of(index):
        return (
            index // (n_x * n_c * n_y), index // (n_c * n_y) % n_x, index // n_y % n_c, index % n_y
        )

    def taken(index):
        return source.at[0] if broadcast else source.at[index]

    barrier = pltpu.get_barrier_semaphore()

    def call(step, unused):
        other = lax.rem(me + step, count)
        pl.semaphore_signal(barrier, inc=1, device_id=device_of(other), device_id_type=MESH)
        return unused

    lax.fori_loop(1, count, call, 0)
    own = pltpu.make_async_copy(taken(me), out.at[me], own_sem)
    own.start()
    pl.semaphore_wait(barrier, count - 1)

    def copy(step):
        other = lax.rem(me + step, count)
        return remote(
            taken(other), out.at[me], send_sem.at[step], receive_sem.at[step], device_of(other)
        )

    def start(step, unused):
        copy(step).start()
        return unused

    def finish(step, unused):
        copy(step).wait()
        return unused

    lax.fori_loop(1, count, start, 0)
    lax.fori_loop(1, count, finish, 0)
    own.wait()


def swap(blocks, broadcast, collective_id):
    count = 1
    for size in sizes():
        count *= size
    return pl.pallas_call(
        functools.partial(swap_kernel, broadcast),
        out_shape=jax.ShapeDtypeStruct((count,) + blocks.shape[1:], blocks.dtype),
        in_specs=[VMEM],
        out_specs=VMEM,
        scratch_shapes=[
            pltpu.SemaphoreType.DMA((count,)),
            pltpu.SemaphoreType.DMA((count,)),
            pltpu.SemaphoreType.DMA,
        ],
        compiler_params=pltpu.CompilerParams(collective_id=collective_id, has_side_effects=True),
    )(blocks)


def gather_all_kernel(rows_in, out, z_send, z_recv, x_send, x_recv, y_send, y_recv, c_send, c_recv, own_sem):
    n_z = lax.axis_size("z")
    half = rows_in.shape[0] // 2
    (z, x, c, y), x_near, y_near, c_near = around()
    low, high = pl.ds(0, half), pl.ds(half, half)
    everything = pl.ds(0, 2 * half)

    barrier = pltpu.get_barrier_semaphore()
    for device in (x_near, y_near, c_near):
        pl.semaphore_signal(barrier, inc=1, device_id=device, device_id_type=MESH)

    @pl.when(z > 0)
    def _():
        pl.semaphore_signal(barrier, inc=1, device_id=(z - 1, x, c, y), device_id_type=MESH)

    @pl.when(z < n_z - 1)
    def _():
        pl.semaphore_signal(barrier, inc=1, device_id=(z + 1, x, c, y), device_id_type=MESH)

    own = pltpu.make_async_copy(rows_in, out.at[z, x, c, y], own_sem)
    own.start()
    pl.semaphore_wait(
        barrier, 3 + jnp.where(z > 0, 1, 0) + jnp.where(z < n_z - 1, 1, 0)
    )

    def block(origin, px, py, rows):
        return out.at[origin, px, c, py, rows]

    def z_copy(source, origin, up):
        other = (z + 1, x, c, y) if up else (z - 1, x, c, y)
        return remote(
            source, out.at[origin, x, c, y], z_send.at[origin, 1 if up else 0], z_recv.at[origin], other
        )

    def x_copy(source, origin):
        return remote(source, out.at[origin, x, c, y], x_send.at[origin, 0], x_recv.at[origin, 0], x_near)

    def y_copy(source, origin):
        return remote(source, out.at[origin, x, c, y], y_send.at[origin, 0], y_recv.at[origin, 0], y_near)

    def x_relay(origin):
        part = block(origin, x, 1 - y, high)
        return remote(part, part, x_send.at[origin, 1], x_recv.at[origin, 1], x_near)

    def y_relay(origin):
        part = block(origin, 1 - x, y, low)
        return remote(part, part, y_send.at[origin, 1], y_recv.at[origin, 1], y_near)

    def c_copy(source, origin, px, py):
        slot = px * 2 + py
        return remote(
            source, out.at[origin, px, c, py], c_send.at[origin, slot], c_recv.at[origin, slot], c_near
        )

    def spread(source, origin):
        x_copy(source, origin).start()
        y_copy(source, origin).start()
        c_copy(source, origin, x, y).start()

    def column(origin):
        return out.at[origin, x, c, y]

    def relay(origin):
        x_copy(column(origin), origin).wait_recv()
        y_relay(origin).start()
        y_copy(column(origin), origin).wait_recv()
        x_relay(origin).start()
        c_copy(block(origin, 1 - x, y, everything), origin, 1 - x, y).start()
        c_copy(block(origin, x, 1 - y, everything), origin, x, 1 - y).start()

    def finish(origin):
        x_relay(origin).wait_recv()
        y_relay(origin).wait_recv()
        c_copy(block(origin, 1 - x, 1 - y, everything), origin, 1 - x, 1 - y).start()

    def when_origin(origin, action):
        @pl.when((origin >= 0) & (origin < n_z))
        def _():
            action(origin)

    def arrive(step):
        below, above = z - step, z + step

        @pl.when(below >= 0)
        def _():
            z_copy(rows_in, below, True).wait_recv()

            @pl.when(z < n_z - 1)
            def _():
                z_copy(column(below), below, True).start()

            spread(column(below), below)

        @pl.when(above < n_z)
        def _():
            z_copy(rows_in, above, False).wait_recv()

            @pl.when(z > 0)
            def _():
                z_copy(column(above), above, False).start()

            spread(column(above), above)

    @pl.when(z < n_z - 1)
    def _():
        z_copy(rows_in, z, True).start()

    @pl.when(z > 0)
    def _():
        z_copy(rows_in, z, False).start()

    spread(rows_in, z)
    for step in range(1, n_z + 2):
        if step < n_z:
            arrive(step)
        for action, back in ((relay, 1), (finish, 2)):
            late = step - back
            if late == 0:
                action(z)
            elif 0 < late < n_z:
                when_origin(z - late, action)
                when_origin(z + late, action)
    own.wait()

    def close(origin, unused):
        x_copy(rows_in, origin).wait_send()
        y_copy(rows_in, origin).wait_send()
        x_relay(origin).wait_send()
        y_relay(origin).wait_send()
        for px in range(2):
            for py in range(2):
                copy = c_copy(out.at[origin, px, c, py], origin, px, py)
                copy.wait_send()
                copy.wait_recv()

        @pl.when((z < n_z - 1) & (origin <= z))
        def _():
            z_copy(rows_in, origin, True).wait_send()

        @pl.when((z > 0) & (origin >= z))
        def _():
            z_copy(rows_in, origin, False).wait_send()

        return unused

    lax.fori_loop(0, n_z, close, 0)


def gather_all(rows, collective_id):
    n_z = lax.axis_size("z")
    shape = sizes() + rows.shape
    dma = pltpu.SemaphoreType.DMA
    out = pl.pallas_call(
        gather_all_kernel,
        out_shape=jax.ShapeDtypeStruct(shape, rows.dtype),
        in_specs=[ANY],
        out_specs=ANY,
        scratch_shapes=[
            dma((n_z, 2)), dma((n_z,)), dma((n_z, 2)), dma((n_z, 2)), dma((n_z, 2)), dma((n_z, 2)),
            dma((n_z, 4)), dma((n_z, 4)), dma,
        ],
        compiler_params=pltpu.CompilerParams(collective_id=collective_id, has_side_effects=True),
    )(rows)
    return out.reshape(-1, rows.shape[1])


def total_of(*parts):
    total = parts[0].astype(jnp.float32)
    for part in parts[1:]:
        total = total + part.astype(jnp.float32)
    return total


def scatter_all_kernel(
    source, out, lanes, c_got, x_got, y_got, x_last, y_last, below, above,
    own_sem, c_send, c_recv, x_send, x_recv, y_send, y_recv, z_send, z_recv,
):
    n_z = lax.axis_size("z")
    rows = source.shape[4]
    half = rows // 2
    (z, x, c, y), x_near, y_near, c_near = around()
    low, high = pl.ds(0, half), pl.ds(half, half)
    up, down = n_z - 1 - z, z
    longer, shorter = jnp.maximum(up, down), jnp.minimum(up, down)
    far_side = jnp.where(up >= down, 1, -1)

    def target(step):
        late = step - (longer - shorter)
        near_side = jnp.where(late % 2 == 0, far_side, -far_side)
        return jnp.where(
            late < 0, z + far_side * (longer - step), z + near_side * (shorter - late // 2)
        )

    barrier = pltpu.get_barrier_semaphore()
    for device in (x_near, y_near, c_near):
        pl.semaphore_signal(barrier, inc=1, device_id=device, device_id_type=MESH)

    @pl.when(z > 0)
    def _():
        pl.semaphore_signal(barrier, inc=1, device_id=(z - 1, x, c, y), device_id_type=MESH)

    @pl.when(z < n_z - 1)
    def _():
        pl.semaphore_signal(barrier, inc=1, device_id=(z + 1, x, c, y), device_id_type=MESH)

    def own_copy(slab, px):
        return pltpu.make_async_copy(source.at[slab, px, c], lanes.at[slab, px], own_sem.at[slab, px])

    def c_copy(slab, px):
        return remote(
            source.at[slab, px, 1 - c], c_got.at[slab, px], c_send.at[slab, px], c_recv.at[slab, px], c_near
        )

    def load(step, unused):
        for px in range(2):
            own_copy(target(step), px).start()
        return unused

    lax.fori_loop(0, n_z, load, 0)
    pl.semaphore_wait(barrier, 3 + jnp.where(z > 0, 1, 0) + jnp.where(z < n_z - 1, 1, 0))

    def hand(step, unused):
        for px in range(2):
            c_copy(target(step), px).start()
        return unused

    lax.fori_loop(0, n_z, hand, 0)

    def x_first(slab, part):
        block = lanes.at[slab, 1 - x, jnp.where(part == 0, y, 1 - y), low]
        return remote(block, x_got.at[slab, part], x_send.at[slab, part], x_recv.at[slab, part], x_near)

    def y_first(slab, part):
        block = lanes.at[slab, jnp.where(part == 0, x, 1 - x), 1 - y, high]
        return remote(block, y_got.at[slab, part], y_send.at[slab, part], y_recv.at[slab, part], y_near)

    def y_second(slab):
        block = lanes.at[slab, x, 1 - y, low]
        return remote(block, y_last.at[slab], y_send.at[slab, 2], y_recv.at[slab, 2], y_near)

    def x_second(slab):
        block = lanes.at[slab, 1 - x, y, high]
        return remote(block, x_last.at[slab], x_send.at[slab, 2], x_recv.at[slab, 2], x_near)

    def z_up(slab):
        return remote(
            lanes.at[slab, x, y], below.at[slab], z_send.at[slab], z_recv.at[slab, 0], (z + 1, x, c, y)
        )

    def z_down(slab):
        return remote(
            lanes.at[slab, x, y], above.at[slab], z_send.at[slab], z_recv.at[slab, 1], (z - 1, x, c, y)
        )

    def begin(step):
        slab = target(step)
        for px in range(2):
            own_copy(slab, px).wait()
            c_copy(slab, px).wait_recv()

        def merge(px, py):
            lanes[slab, px, py] = total_of(lanes[slab, px, py], c_got[slab, px, py]).astype(jnp.bfloat16)

        merge(1 - x, 1 - y)
        x_first(slab, 1).start()
        y_first(slab, 1).start()
        merge(1 - x, y)
        x_first(slab, 0).start()
        merge(x, 1 - y)
        y_first(slab, 0).start()
        merge(x, y)

    def middle(step):
        slab = target(step)
        x_first(slab, 1).wait_recv()
        x_first(slab, 0).wait_send()
        y_first(slab, 0).wait_send()
        lanes[slab, x, 1 - y, low] = total_of(
            lanes[slab, x, 1 - y, low], x_got[slab, 1]
        ).astype(jnp.bfloat16)
        y_second(slab).start()
        y_first(slab, 1).wait_recv()
        lanes[slab, 1 - x, y, high] = total_of(
            lanes[slab, 1 - x, y, high], y_got[slab, 1]
        ).astype(jnp.bfloat16)
        x_second(slab).start()

    def finish(step):
        slab = target(step)
        x_first(slab, 0).wait_recv()
        y_second(slab).wait_recv()
        first = total_of(lanes[slab, x, y, low], x_got[slab, 0], y_last[slab])
        y_first(slab, 0).wait_recv()
        x_second(slab).wait_recv()
        second = total_of(lanes[slab, x, y, high], y_got[slab, 0], x_last[slab])

        @pl.when(slab > z)
        def _():
            @pl.when(z == 0)
            def _():
                lanes[slab, x, y, low] = first.astype(jnp.bfloat16)
                lanes[slab, x, y, high] = second.astype(jnp.bfloat16)

            @pl.when(z > 0)
            def _():
                z_up(slab).wait_recv()
                lanes[slab, x, y, low] = total_of(first, below[slab, low]).astype(jnp.bfloat16)
                lanes[slab, x, y, high] = total_of(second, below[slab, high]).astype(jnp.bfloat16)

            z_up(slab).start()

        @pl.when(slab < z)
        def _():
            @pl.when(z == n_z - 1)
            def _():
                lanes[slab, x, y, low] = first.astype(jnp.bfloat16)
                lanes[slab, x, y, high] = second.astype(jnp.bfloat16)

            @pl.when(z < n_z - 1)
            def _():
                z_down(slab).wait_recv()
                lanes[slab, x, y, low] = total_of(first, above[slab, low]).astype(jnp.bfloat16)
                lanes[slab, x, y, high] = total_of(second, above[slab, high]).astype(jnp.bfloat16)

            z_down(slab).start()

        @pl.when(slab == z)
        def _():
            out[low, :] = first
            out[high, :] = second

            @pl.when(z > 0)
            def _():
                z_up(slab).wait_recv()
                out[...] += below[slab].astype(jnp.float32)

            @pl.when(z < n_z - 1)
            def _():
                z_down(slab).wait_recv()
                out[...] += above[slab].astype(jnp.float32)

    def turn(step, unused):
        @pl.when(step < n_z)
        def _():
            begin(step)

        @pl.when((step >= 1) & (step < n_z + 1))
        def _():
            middle(step - 1)

        @pl.when(step >= 2)
        def _():
            finish(step - 2)

        return unused

    lax.fori_loop(0, n_z + 2, turn, 0)

    def close(slab, unused):
        for px in range(2):
            c_copy(slab, px).wait_send()
        x_first(slab, 1).wait_send()
        y_first(slab, 1).wait_send()
        x_second(slab).wait_send()
        y_second(slab).wait_send()

        @pl.when(slab > z)
        def _():
            z_up(slab).wait_send()

        @pl.when(slab < z)
        def _():
            z_down(slab).wait_send()

        return unused

    lax.fori_loop(0, n_z, close, 0)


def scatter_all(partial_rows, collective_id):
    n_z, n_x, n_c, n_y = sizes()
    rows = partial_rows.shape[0] // (n_z * n_x * n_c * n_y)
    width = partial_rows.shape[1]
    half = rows // 2
    low = jnp.bfloat16
    dma = pltpu.SemaphoreType.DMA
    return pl.pallas_call(
        scatter_all_kernel,
        out_shape=jax.ShapeDtypeStruct((rows, width), jnp.float32),
        in_specs=[ANY],
        out_specs=VMEM,
        scratch_shapes=[
            pltpu.VMEM((n_z, n_x, n_y, rows, width), low),
            pltpu.VMEM((n_z, n_x, n_y, rows, width), low),
            pltpu.VMEM((n_z, 2, half, width), low),
            pltpu.VMEM((n_z, 2, half, width), low),
            pltpu.VMEM((n_z, half, width), low),
            pltpu.VMEM((n_z, half, width), low),
            pltpu.VMEM((n_z, rows, width), low),
            pltpu.VMEM((n_z, rows, width), low),
            dma((n_z, 2)), dma((n_z, 2)), dma((n_z, 2)), dma((n_z, 3)), dma((n_z, 3)), dma((n_z, 3)),
            dma((n_z, 3)), dma((n_z,)), dma((n_z, 2)),
        ],
        compiler_params=pltpu.CompilerParams(
            collective_id=collective_id, has_side_effects=True, vmem_limit_bytes=56 * MIB
        ),
    )(partial_rows.astype(low).reshape(n_z, n_x, n_c, n_y, rows, width))


def trade_kernel(source, out, send_sem, recv_sem, own_sem):
    (z, x, c, y), x_near, y_near, _ = around()
    diagonal = (z, 1 - x, c, 1 - y)
    own = pltpu.make_async_copy(source.at[x, y], out.at[x, y], own_sem)
    own.start()
    greet((x_near, y_near, diagonal))
    copies = [
        remote(source.at[device[1], device[3]], out.at[x, y], send_sem.at[slot], recv_sem.at[slot], device)
        for slot, device in enumerate((diagonal, x_near, y_near))
    ]
    for copy in copies:
        copy.start()
    for copy in copies:
        copy.wait()
    own.wait()


def trade(blocks, collective_id):
    return pl.pallas_call(
        trade_kernel,
        out_shape=jax.ShapeDtypeStruct(blocks.shape, blocks.dtype),
        in_specs=[VMEM],
        out_specs=VMEM,
        scratch_shapes=[
            pltpu.SemaphoreType.DMA((3,)), pltpu.SemaphoreType.DMA((3,)), pltpu.SemaphoreType.DMA
        ],
        compiler_params=pltpu.CompilerParams(collective_id=collective_id, has_side_effects=True),
    )(blocks)


def key_position(index, part, chunk):
    lane = 2 * chunk
    start = (part // 2) * (2 * lane) + (part % 2) * chunk
    return start + index + jnp.where(index >= chunk, chunk, 0)


def attend_kernel(
    chunk, query, keys, values, near_keys, near_values, query_pos, query_seg, near_pos, near_seg,
    out, log_total, scores, values_t,
):
    lane, feature = query.shape
    group = feature // HEAD_DIM
    prompt_rows = keys.shape[0]
    parts = prompt_rows // lane
    query_t = (query[...].astype(jnp.float32) * HEAD_DIM ** (-0.5)).T.astype(jnp.bfloat16)
    values_t[:, :prompt_rows] = values[...].astype(jnp.float32).T.astype(jnp.bfloat16)
    values_t[:, prompt_rows:] = near_values[...].astype(jnp.float32).T.astype(jnp.bfloat16)
    row_of = lax.broadcasted_iota(jnp.int32, (feature, lane), 0)
    q_pos = query_pos[...]

    for head in range(group):
        low, high = head * HEAD_DIM, (head + 1) * HEAD_DIM
        query_h = jnp.where((row_of >= low) & (row_of < high), query_t, 0)

        def score_part(part, peak):
            block = keys[pl.ds(pl.multiple_of(part * lane, lane), lane), :]
            value = matmul(block, query_h)
            index = lax.broadcasted_iota(jnp.int32, (lane, lane), 0)
            value = jnp.where(key_position(index, part, chunk) <= q_pos, value, MASKED)
            scores[pl.ds(pl.multiple_of(part * lane, lane), lane), :] = value
            return jnp.maximum(peak, jnp.max(value, axis=0, keepdims=True))

        peak = lax.fori_loop(0, parts, score_part, jnp.full((1, lane), MASKED, jnp.float32))
        near_peaks = []
        for side in range(2):
            columns = slice(side * chunk, (side + 1) * chunk)
            rows = slice(side * lane, (side + 1) * lane)
            value = matmul(near_keys[rows, :], query_h[:, columns])
            shown = (
                (near_seg[rows, :] == query_seg[:, columns])
                & (near_pos[rows, :] <= q_pos[:, columns])
                & (near_pos[rows, :] >= PROMPT)
            )
            value = jnp.where(shown, value, MASKED)
            scores[prompt_rows : prompt_rows + lane, columns] = value
            near_peaks.append(jnp.max(value, axis=0, keepdims=True))
        peak = jnp.maximum(peak, jnp.concatenate(near_peaks, axis=1))

        def weigh_part(part, state):
            total, mixed = state
            start = pl.multiple_of(part * lane, lane)
            chance = jnp.exp(scores[pl.ds(start, lane), :] - peak)
            total = total + jnp.sum(chance, axis=0, keepdims=True)
            mixed = mixed + matmul(
                values_t[low:high, pl.ds(start, lane)], chance.astype(jnp.bfloat16)
            )
            return total, mixed

        total, mixed = lax.fori_loop(
            0,
            parts,
            weigh_part,
            (jnp.zeros((1, lane), jnp.float32), jnp.zeros((HEAD_DIM, lane), jnp.float32)),
        )
        near_total, near_mixed = [], []
        for side in range(2):
            columns = slice(side * chunk, (side + 1) * chunk)
            rows = slice(prompt_rows + side * lane, prompt_rows + (side + 1) * lane)
            chance = jnp.exp(scores[prompt_rows : prompt_rows + lane, columns] - peak[:, columns])
            near_total.append(jnp.sum(chance, axis=0, keepdims=True))
            near_mixed.append(matmul(values_t[low:high, rows], chance.astype(jnp.bfloat16)))
        total = total + jnp.concatenate(near_total, axis=1)
        mixed = mixed + jnp.concatenate(near_mixed, axis=1)
        out[low:high, :] = mixed / total
        log_total[head : head + 1, :] = peak + jnp.log(total)


def attend(queries, keys, values, near_keys, near_values, places, chunk):
    lane, feature = queries.shape
    prompt_rows = keys.shape[0]
    group = feature // HEAD_DIM
    total_rows = prompt_rows + lane
    return pl.pallas_call(
        functools.partial(attend_kernel, chunk),
        out_shape=(
            jax.ShapeDtypeStruct((feature, lane), jnp.float32),
            jax.ShapeDtypeStruct((group, lane), jnp.float32),
        ),
        in_specs=[pl.BlockSpec(memory_space=pltpu.VMEM)] * 9,
        out_specs=(pl.BlockSpec(memory_space=pltpu.VMEM),) * 2,
        scratch_shapes=[
            pltpu.VMEM((total_rows, lane), jnp.float32),
            pltpu.VMEM((feature, prompt_rows + 2 * lane), jnp.bfloat16),
        ],
        compiler_params=pltpu.CompilerParams(vmem_limit_bytes=48 * MIB),
        cost_estimate=pl.CostEstimate(
            flops=8 * group * lane * total_rows * 128,
            bytes_accessed=8 * MIB,
            transcendentals=group * lane * total_rows,
        ),
    )(queries, keys, values, near_keys, near_values, *places)


def attend_back_kernel(
    chunk, query, keys, values, near_keys, near_values, query_pos, query_seg, near_pos, near_seg,
    log_total, mixed, answer, query_grad, far_grad, near_grad, keys_t,
):
    lane, feature = query.shape
    group = feature // HEAD_DIM
    prompt_rows = keys.shape[0]
    parts = prompt_rows // lane
    scaled = (query[...].astype(jnp.float32) * HEAD_DIM ** (-0.5)).astype(jnp.bfloat16)
    query_t = scaled.astype(jnp.float32).T.astype(jnp.bfloat16)
    answers = answer[...]
    answer_t = answers.astype(jnp.float32).T.astype(jnp.bfloat16)
    keys_t[:, :prompt_rows] = keys[...].astype(jnp.float32).T.astype(jnp.bfloat16)
    keys_t[:, prompt_rows:] = near_keys[...].astype(jnp.float32).T.astype(jnp.bfloat16)
    row_of = lax.broadcasted_iota(jnp.int32, (feature, lane), 0)
    column_of = lax.broadcasted_iota(jnp.int32, (lane, feature), 1)
    q_pos = query_pos[...]

    for head in range(group):
        low, high = head * HEAD_DIM, (head + 1) * HEAD_DIM
        in_rows = (row_of >= low) & (row_of < high)
        in_columns = (column_of >= low) & (column_of < high)
        query_ht = jnp.where(in_rows, query_t, 0)
        answer_ht = jnp.where(in_rows, answer_t, 0)
        query_h = jnp.where(in_columns, scaled, 0)
        answer_h = jnp.where(in_columns, answers, 0)
        log_h = log_total[head : head + 1, :]
        delta_h = jnp.sum(
            answer_t[low:high, :].astype(jnp.float32) * mixed[low:high, :], axis=0, keepdims=True
        )

        def slopes(key_block, value_block, shown, columns):
            value = matmul(key_block, query_ht[:, columns])
            chance = jnp.exp(jnp.where(shown, value - log_h[:, columns], MASKED))
            slope = matmul(value_block, answer_ht[:, columns])
            change = (chance * (slope - delta_h[:, columns])).astype(jnp.bfloat16)
            chance = chance.astype(jnp.bfloat16)
            return change, matmul(change, query_h[columns]), matmul(chance, answer_h[columns])

        def back_part(part, total):
            start = pl.multiple_of(part * lane, lane)
            rows = pl.ds(start, lane)
            index = lax.broadcasted_iota(jnp.int32, (lane, lane), 0)
            shown = key_position(index, part, chunk) <= q_pos
            change, key_part, value_part = slopes(
                keys[rows, :], values[rows, :], shown, slice(0, lane)
            )
            if head == 0:
                far_grad[0, rows, :] = key_part
                far_grad[1, rows, :] = value_part
            else:
                far_grad[0, rows, :] += key_part
                far_grad[1, rows, :] += value_part
            return total + matmul(keys_t[low:high, rows], change)

        total = lax.fori_loop(0, parts, back_part, jnp.zeros((HEAD_DIM, lane), jnp.float32))
        near_total = []
        for side in range(2):
            columns = slice(side * chunk, (side + 1) * chunk)
            rows = slice(side * lane, (side + 1) * lane)
            shown = (
                (near_seg[rows, :] == query_seg[:, columns])
                & (near_pos[rows, :] <= q_pos[:, columns])
                & (near_pos[rows, :] >= PROMPT)
            )
            change, key_part, value_part = slopes(
                near_keys[rows, :], near_values[rows, :], shown, columns
            )
            if head == 0:
                near_grad[0, rows, :] = key_part
                near_grad[1, rows, :] = value_part
            else:
                near_grad[0, rows, :] += key_part
                near_grad[1, rows, :] += value_part
            near_rows = slice(prompt_rows + side * lane, prompt_rows + (side + 1) * lane)
            near_total.append(matmul(keys_t[low:high, near_rows], change))
        query_grad[low:high, :] = (total + jnp.concatenate(near_total, axis=1)) * HEAD_DIM ** (-0.5)


def attend_back(queries, keys, values, near_keys, near_values, places, log_total, mixed, answer, chunk):
    lane, feature = queries.shape
    prompt_rows = keys.shape[0]
    group = feature // HEAD_DIM
    total_rows = prompt_rows + lane
    return pl.pallas_call(
        functools.partial(attend_back_kernel, chunk),
        out_shape=(
            jax.ShapeDtypeStruct((feature, lane), jnp.float32),
            jax.ShapeDtypeStruct((2, prompt_rows, feature), jnp.float32),
            jax.ShapeDtypeStruct((2, 2 * lane, feature), jnp.float32),
        ),
        in_specs=[pl.BlockSpec(memory_space=pltpu.VMEM)] * 12,
        out_specs=(pl.BlockSpec(memory_space=pltpu.VMEM),) * 3,
        scratch_shapes=[pltpu.VMEM((feature, prompt_rows + 2 * lane), jnp.bfloat16)],
        compiler_params=pltpu.CompilerParams(vmem_limit_bytes=48 * MIB),
        cost_estimate=pl.CostEstimate(
            flops=20 * group * lane * total_rows * 128,
            bytes_accessed=12 * MIB,
            transcendentals=group * lane * total_rows,
        ),
    )(queries, keys, values, near_keys, near_values, *places, log_total, mixed, answer)


def pad_rows(block):
    return jnp.pad(block, ((0, 8 - block.shape[0]), (0, 0)))


def adam_update(weight, moment_one, moment_two, gradient, step_rate, decay_rate):
    first_new = BETA_ONE * moment_one + (1.0 - BETA_ONE) * gradient
    second_new = BETA_TWO * moment_two + (1.0 - BETA_TWO) * gradient * gradient
    normalized = (
        first_new
        / (1.0 - BETA_ONE**STEP)
        / (jnp.sqrt(second_new / (1.0 - BETA_TWO**STEP)) + ADAM_EPS)
    )
    return (weight - step_rate * (normalized + decay_rate * weight), first_new, second_new)


def per_device(
    token_ids,
    targets,
    valid_mask,
    cont_lengths,
    routes,
    vocab_table,
    vocab_first,
    vocab_second,
    attn_weights,
    attn_first,
    attn_second,
    router,
    router_first,
    router_second,
    norm_gains,
    gains_first,
    gains_second,
    expert_up,
    up_first,
    up_second,
    expert_down,
    down_first,
    down_second,
):
    slabs = lax.axis_size("z")
    planes = lax.axis_size("x")
    cores = lax.axis_size("core")
    sides = lax.axis_size("head")
    groups = planes * sides
    z_at, x_at, core_at, side_at = (lax.axis_index(name) for name in ALL)
    blk_at = (z_at * planes + x_at) * cores + core_at
    device_at = blk_at * sides + side_at
    group_at = x_at * sides + side_at
    tokens = valid_mask.shape[0]
    chunk = token_ids.shape[0]
    own = chunk // sides
    lane = planes * chunk
    feature = D // groups
    wide = expert_up.shape[3] // planes
    shard_rows = vocab_table.shape[0]
    logit_scale = D ** (-0.5)

    cont_ends = jnp.cumsum(cont_lengths)
    valid_f = valid_mask.astype(jnp.float32)
    token_count = jnp.sum(valid_mask).astype(jnp.float32)
    expert_ids = jnp.arange(EXPERTS, dtype=jnp.int32)

    own_ints = jnp.concatenate([token_ids[None], targets[None], routes], axis=0)
    own_ints = lax.dynamic_slice_in_dim(own_ints, side_at * own, own, axis=1)
    whole = swap(pad_rows(own_ints)[None], True, 1)[:, : 2 + LAYERS]
    ids_all = whole[:, 0].reshape(tokens)
    targets_all = whole[:, 1].reshape(tokens)
    routes_lane = lax.dynamic_index_in_dim(
        whole.reshape(slabs, planes, cores, sides, 2 + LAYERS, own), z_at, 0, False
    )
    routes_lane = lax.dynamic_index_in_dim(routes_lane, core_at, 1, False)[:, :, 2:]
    routes_lane = routes_lane.transpose(2, 0, 1, 3).reshape(LAYERS, lane)
    routes_own = lax.dynamic_slice_in_dim(routes, side_at * own, own, axis=1)

    table = vocab_table.astype(jnp.bfloat16)
    small_all = lax.all_gather(
        jnp.concatenate(
            [router.transpose(1, 0, 2).reshape(-1, LAYERS * EXPERTS), norm_gains.T], axis=1
        ).astype(jnp.bfloat16),
        ALL,
        axis=0,
        tiled=True,
    )
    router_all = small_all[:, : LAYERS * EXPERTS].reshape(D, LAYERS, EXPERTS).transpose(1, 0, 2)
    gains_f = small_all[:, LAYERS * EXPERTS :].T.astype(jnp.float32)

    attn_low = attn_weights.astype(jnp.bfloat16)
    rows_of = attn_low.shape[1]
    qkv_send = attn_low[:, :, : 3 * D].reshape(LAYERS, rows_of, 3, groups, feature)
    qkv_send = qkv_send.transpose(3, 0, 1, 2, 4).reshape(groups, LAYERS, rows_of, 3 * feature)
    qkv_got = lax.all_to_all(qkv_send, PLANE, split_axis=0, concat_axis=0, tiled=True)
    out_all = lax.all_gather(attn_low[:, :, 3 * D :], ALL, axis=1, tiled=True)
    expert_send = jnp.stack([expert_up, expert_down], axis=1).astype(jnp.bfloat16)
    depth = expert_send.shape[3]
    expert_send = expert_send.reshape(LAYERS, 2 * EXPERTS, depth, planes, wide)
    expert_send = expert_send.transpose(3, 0, 1, 2, 4)
    expert_got = lax.all_to_all(expert_send, ("x",), split_axis=0, concat_axis=0, tiled=True)
    qkv_weights, expert_weights = [], []
    for layer_index in range(LAYERS):
        block = lax.all_gather(qkv_got[:, layer_index], LINE, axis=0)
        block = block.reshape(slabs, cores, planes, sides, rows_of, 3 * feature)
        qkv_weights.append(block.transpose(0, 2, 1, 3, 4, 5).reshape(D, 3 * feature))
        block = lax.all_gather(expert_got[:, layer_index], LINE, axis=0)
        block = block.reshape(slabs, cores, planes, 2, EXPERTS, depth, wide)
        block = block.transpose(3, 4, 0, 2, 1, 5, 6).reshape(2, EXPERTS, D, wide)
        expert_weights.append(block)

    offsets = jnp.arange(chunk, dtype=jnp.int32)
    first_blk = z_at * planes * cores + core_at
    query_pos = jnp.concatenate([(first_blk + cores * part) * chunk + offsets for part in range(planes)])
    near_blks = [first_blk - 1 + part for part in range(2 * planes)]
    near_pos = jnp.concatenate([blk * chunk + offsets for blk in near_blks])
    query_seg = segment_of(query_pos, cont_ends)
    near_seg = segment_of(near_pos, cont_ends)
    places = (query_pos[None, :], query_seg[None, :], near_pos[:, None], near_seg[:, None])

    def near_index(blk):
        blk = jnp.maximum(blk, 0)
        slab, rest = blk // (planes * cores), blk % (planes * cores)
        return slab * (planes * cores) + (rest % cores) * planes + rest // cores

    def spread_keys(key_values):
        return lax.all_gather(key_values, LINE, axis=0, tiled=True)

    def near_rows(spread):
        return jnp.concatenate(
            [
                lax.dynamic_slice_in_dim(spread, near_index(blk) * chunk, chunk, axis=0)
                for blk in near_blks
            ],
            axis=0,
        )

    vocab_ids = device_at * shard_rows + jnp.arange(shard_rows, dtype=jnp.int32)
    token_hot = (ids_all[:, None] == vocab_ids[None, :]).astype(jnp.bfloat16)
    stream = scatter_all(matmul(token_hot, table), 2)

    kept = []
    for layer_index in range(LAYERS):
        up, down = expert_weights[layer_index][0], expert_weights[layer_index][1]
        normed_lane = gather_plane(
            rms_norm(stream, gains_f[2 * layer_index]).astype(jnp.bfloat16)
        )
        qkv = matmul(normed_lane, qkv_weights[layer_index]).astype(jnp.bfloat16)
        queries = qkv[:, :feature]
        spread = spread_keys(qkv[:, feature:])
        far = spread[:PROMPT]
        near = near_rows(spread)
        key_args = (far[:, :feature], far[:, feature:], near[:, :feature], near[:, feature:])
        mixed_t, log_total = attend(queries, *key_args, places, chunk)
        mixed_own = trade(
            mixed_t.T.astype(jnp.bfloat16).reshape(planes, sides, own, feature), 3
        )
        mixed_own = mixed_own.transpose(2, 0, 1, 3).reshape(own, D)
        middle = stream + matmul(mixed_own, out_all[layer_index])
        normed_two = rms_norm(middle, gains_f[2 * layer_index + 1]).astype(jnp.bfloat16)
        chance = jax.nn.softmax(matmul(normed_two, router_all[layer_index]), axis=-1)
        wide_rows = gather_plane(normed_two)
        picked = routes_lane[layer_index][:, None] == expert_ids[None, :]
        before = jnp.where(picked[:, :1], matmul(wide_rows, up[0]), matmul(wide_rows, up[1]))
        active = jax.nn.gelu(before, approximate=False)
        hidden = [
            jnp.where(picked[:, e : e + 1], active, 0.0).astype(jnp.bfloat16)
            for e in range(EXPERTS)
        ]
        output = scatter_plane(outer(hidden[0], down[0]) + outer(hidden[1], down[1]))
        own_pick = (routes_own[layer_index][:, None] == expert_ids[None, :]).astype(jnp.float32)
        gate = jnp.sum(chance * own_pick, axis=1, keepdims=True)
        kept.append(
            (
                stream, normed_lane, queries, key_args, mixed_t, mixed_own, log_total, middle,
                normed_two, chance, wide_rows, picked, before, hidden, output, own_pick, gate,
            )
        )
        stream = middle + gate * output

    final_gain = gains_f[2 * LAYERS]
    final_all = gather_all(rms_norm(stream, final_gain).astype(jnp.bfloat16), 4)
    logits = outer(final_all, table) * logit_scale
    row_max = jnp.max(logits, axis=1, keepdims=True)
    row_log = row_max[:, 0] + jnp.log(jnp.sum(jnp.exp(logits - row_max), axis=1))
    target_hot = targets_all[:, None] == vocab_ids[None, :]
    hit_loss = jnp.sum(jnp.where(target_hot, logits, 0.0) * valid_f[:, None])
    devices = tokens // own
    row_logs = jnp.broadcast_to(row_log.reshape(devices, 1, own), (devices, 8, own))
    own_log = jax.nn.logsumexp(swap(row_logs, False, 5), axis=0)
    log_sum = swap(own_log[None], True, 6)[:, 0].reshape(tokens)
    own_valid = lax.dynamic_slice_in_dim(valid_f, device_at * own, own)
    own_loss = jnp.sum(own_log[0] * own_valid) - hit_loss
    logit_grad = (
        (jnp.exp(logits - log_sum[:, None]) - target_hot.astype(jnp.float32))
        * (valid_f / token_count)[:, None]
    ).astype(jnp.bfloat16)
    final_grad = scatter_all(matmul(logit_grad, table) * logit_scale, 2)
    table_grad = inner(logit_grad, final_all) * logit_scale
    stream_grad, final_gain_grad = jax.vjp(rms_norm, stream, final_gain)[1](final_grad)

    qkv_shares = [None] * LAYERS
    out_shares = [None] * LAYERS
    router_list = [None] * LAYERS
    expert_shares = [None] * LAYERS
    gain_list = [None] * (2 * LAYERS + 1)
    gain_list[2 * LAYERS] = final_gain_grad
    for layer_index in reversed(range(LAYERS)):
        (
            stream, normed_lane, queries, key_args, mixed_t, mixed_own, log_total, middle,
            normed_two, chance, wide_rows, picked, before, hidden, output, own_pick, gate,
        ) = kept[layer_index]
        up, down = expert_weights[layer_index][0], expert_weights[layer_index][1]
        out_grad = (gate * stream_grad).astype(jnp.bfloat16)
        wide_grad = gather_plane(out_grad)
        chance_grad = jnp.sum(stream_grad * output, axis=1)[:, None] * own_pick
        choice_grad = chance * (chance_grad - jnp.sum(chance * chance_grad, axis=1, keepdims=True))
        router_list[layer_index] = jnp.dot(
            normed_two.astype(jnp.float32).T, choice_grad, precision=lax.Precision.HIGHEST
        )
        normed_grad = jnp.dot(
            choice_grad,
            router_all[layer_index].astype(jnp.float32).T,
            precision=lax.Precision.HIGHEST,
        )
        hidden_grad = jnp.where(
            picked[:, :1], matmul(wide_grad, down[0]), matmul(wide_grad, down[1])
        )
        _, gelu_back = jax.vjp(lambda v: jax.nn.gelu(v, approximate=False), before)
        before_grad = gelu_back(hidden_grad)[0]
        before_grads = [
            jnp.where(picked[:, e : e + 1], before_grad, 0.0).astype(jnp.bfloat16)
            for e in range(EXPERTS)
        ]
        normed_grad = normed_grad + scatter_plane(
            outer(before_grads[0], up[0]) + outer(before_grads[1], up[1])
        )
        expert_grad = jnp.stack(
            [inner(wide_rows, before_grads[e]) for e in range(EXPERTS)]
            + [inner(wide_grad, hidden[e]) for e in range(EXPERTS)]
        ).astype(jnp.bfloat16)
        expert_grad = expert_grad.reshape(2 * EXPERTS, slabs, planes, cores, depth, wide)
        expert_grad = expert_grad.transpose(1, 3, 2, 0, 4, 5).reshape(
            slabs * cores, planes, 2 * EXPERTS, depth, wide
        )
        expert_grad = lax.psum_scatter(expert_grad, LINE, scatter_dimension=0, tiled=True)[0]
        expert_grad = lax.all_to_all(
            expert_grad, ("x",), split_axis=0, concat_axis=0, tiled=True
        )
        expert_shares[layer_index] = (
            expert_grad.transpose(1, 2, 0, 3)
            .reshape(2, EXPERTS, depth, planes * wide)
            .astype(jnp.float32)
        )
        middle_part, gain_list[2 * layer_index + 1] = jax.vjp(
            rms_norm, middle, gains_f[2 * layer_index + 1]
        )[1](normed_grad)
        middle_grad = stream_grad + middle_part
        branch_grad = middle_grad.astype(jnp.bfloat16)
        answer_own = outer(branch_grad, out_all[layer_index]).astype(jnp.bfloat16)
        answer = trade(
            answer_own.reshape(own, planes, sides, feature).transpose(1, 2, 0, 3), 3
        ).reshape(lane, feature)
        out_shares[layer_index] = inner(mixed_own, branch_grad).astype(jnp.bfloat16)
        query_grad_t, far_grad, near_grad = attend_back(
            queries, *key_args, places, log_total, mixed_t, answer, chunk
        )
        spread_grad = jnp.zeros((tokens, 2 * feature), jnp.float32)
        spread_grad = spread_grad.at[:PROMPT].set(
            far_grad.transpose(1, 0, 2).reshape(PROMPT, 2 * feature)
        )
        near_grad = near_grad.transpose(1, 0, 2).reshape(2 * lane, 2 * feature)
        for part, blk in enumerate(near_blks):
            start = near_index(blk) * chunk
            piece = lax.dynamic_slice_in_dim(spread_grad, start, chunk, axis=0)
            piece = piece + near_grad[part * chunk : (part + 1) * chunk]
            spread_grad = lax.dynamic_update_slice_in_dim(spread_grad, piece, start, axis=0)
        key_value_grad = lax.psum_scatter(
            spread_grad.astype(jnp.bfloat16), LINE, scatter_dimension=0, tiled=True
        )
        qkv_grad = jnp.concatenate([query_grad_t.T.astype(jnp.bfloat16), key_value_grad], axis=1)
        qkv_proj = inner(normed_lane, qkv_grad).astype(jnp.bfloat16)
        qkv_proj = qkv_proj.reshape(slabs, planes, cores, sides, rows_of, 3 * feature)
        qkv_proj = qkv_proj.transpose(0, 2, 1, 3, 4, 5).reshape(
            slabs * cores, groups, rows_of, 3 * feature
        )
        qkv_proj = lax.psum_scatter(qkv_proj, LINE, scatter_dimension=0, tiled=True)[0]
        qkv_proj = lax.all_to_all(qkv_proj, PLANE, split_axis=0, concat_axis=0, tiled=True)
        qkv_shares[layer_index] = (
            qkv_proj.reshape(groups, rows_of, 3, feature)
            .transpose(1, 2, 0, 3)
            .reshape(rows_of, 3 * D)
            .astype(jnp.float32)
        )
        normed_att_grad = scatter_plane(outer(qkv_grad, qkv_weights[layer_index]))
        stream_part, gain_list[2 * layer_index] = jax.vjp(
            rms_norm, stream, gains_f[2 * layer_index]
        )[1](normed_att_grad)
        stream_grad = middle_grad + stream_part

    embed_grad = gather_all(stream_grad.astype(jnp.bfloat16), 4)
    table_share = table_grad + inner(token_hot, embed_grad)
    small = jnp.concatenate(
        [jnp.stack(router_list).transpose(1, 0, 2).reshape(D, -1), jnp.stack(gain_list).T], axis=1
    )
    small = small.reshape(devices, rows_of, -1).transpose(0, 2, 1)
    small = jnp.pad(small, ((0, 0), (0, 16 - small.shape[1]), (0, 128 - rows_of)))
    small = jnp.sum(swap(small, False, 7), axis=0)[:, :rows_of]
    router_share = (
        small[: LAYERS * EXPERTS].reshape(LAYERS, EXPERTS, rows_of).transpose(0, 2, 1)
    )
    gain_share = small[LAYERS * EXPERTS : LAYERS * EXPERTS + 2 * LAYERS + 1]
    out_share = jnp.stack(out_shares).reshape(LAYERS, devices, rows_of, D).transpose(1, 0, 2, 3)
    out_share = scatter_all(out_share.reshape(devices * 32, -1), 8)
    out_shares = out_share.reshape(LAYERS, rows_of, D)
    attn_share = jnp.stack(
        [
            jnp.concatenate([qkv_shares[index], out_shares[index]], axis=1)
            for index in range(LAYERS)
        ]
    )
    up_share = jnp.stack([share[0] for share in expert_shares])
    down_share = jnp.stack([share[1] for share in expert_shares])
    shares = (table_share, attn_share, router_share, gain_share, up_share, down_share)
    squares = jnp.sum(table_share * table_share)
    for share_part in shares[1:]:
        squares = squares + jnp.sum(share_part * share_part)
    sums = jnp.pad(jnp.stack([squares, own_loss])[:, None], ((0, 6), (0, 127)))
    sums = jnp.sum(swap(sums[None], True, 9)[:, :2, 0], axis=0)
    square_total, loss_sum = sums[0], sums[1]
    grad_norm = jnp.sqrt(square_total)
    factor = CLIP_AT / jnp.maximum(grad_norm, CLIP_AT)
    weights = (vocab_table, attn_weights, router, norm_gains, expert_up, expert_down)
    firsts = (vocab_first, attn_first, router_first, gains_first, up_first, down_first)
    seconds = (vocab_second, attn_second, router_second, gains_second, up_second, down_second)
    results = [loss_sum, token_count, grad_norm]
    for number in range(6):
        results.extend(
            adam_update(
                weights[number],
                firsts[number],
                seconds[number],
                factor * shares[number],
                STEP_RATES[number],
                DECAY_RATES[number],
            )
        )
    return tuple(results)


def solution(mesh):
    blocks, sides = mesh.shape["blk"], mesh.shape["head"]
    fine = Mesh(mesh.devices.reshape(blocks // 4, 2, 2, sides), ALL)
    weight_specs = (
        (P(ALL, None),) * 3
        + (P(None, ALL, None),) * 3
        + (P(None, ALL, None),) * 3
        + (P(None, ALL),) * 3
        + (P(None, None, BLK, "head"),) * 6
    )
    return jax.shard_map(
        per_device,
        mesh=fine,
        in_specs=(P(BLK), P(BLK), P(), P(), P(None, BLK)) + weight_specs,
        out_specs=(P(), P(), P()) + weight_specs,
        check_vma=False,
    )
```

```python
import functools

import jax
import jax.numpy as jnp
from jax import lax
from jax.experimental import pallas as pl
from jax.experimental.pallas import tpu as pltpu
from jax.sharding import Mesh, PartitionSpec as P

D = 768
HEADS = 12
HEAD_DIM = 64
EXPERTS = 2
LAYERS = 2
PROMPT = 2048
STEP = 10

NORM_EPS = 1e-06
BETA_ONE = 0.9
BETA_TWO = 0.95
ADAM_EPS = 1e-08
CLIP_AT = 0.01
MASKED = -1e30
STEP_RATES = (2.0, 0.25, 0.04, 0.4, 0.04, 0.04)
DECAY_RATES = (0.01, 0.01, 0.01, 0.0, 0.01, 0.01)

ALL = ("z", "x", "core", "head")
BLK = ("z", "x", "core")
PLANE = ("x", "head")
LINE = ("z", "core")
MIB = 2**20
MESH = pl.DeviceIdType.MESH
ANY = pl.BlockSpec(memory_space=pl.ANY)
VMEM = pl.BlockSpec(memory_space=pltpu.VMEM)


def rms_norm(stream, gain):
    return stream * lax.rsqrt(jnp.mean(stream * stream, axis=-1, keepdims=True) + NORM_EPS) * gain


def segment_of(position, cont_ends):
    later = jnp.sum((cont_ends[None, :] <= (position - PROMPT)[:, None]).astype(jnp.int32), axis=1)
    return jnp.where(position < PROMPT, 0, 1 + later)


def place():
    return tuple(lax.axis_index(name) for name in ALL)


def sizes():
    return tuple(lax.axis_size(name) for name in ALL)


def remote(source, target, send, receive, device):
    return pltpu.make_async_remote_copy(
        src_ref=source, dst_ref=target, send_sem=send, recv_sem=receive,
        device_id=device, device_id_type=MESH,
    )


def greet(devices):
    barrier = pltpu.get_barrier_semaphore()
    for device in devices:
        pl.semaphore_signal(barrier, inc=1, device_id=device, device_id_type=MESH)
    pl.semaphore_wait(barrier, len(devices))


def around():
    z, x, c, y = place()
    return (z, x, c, y), (z, 1 - x, c, y), (z, x, c, 1 - y), (z, x, 1 - c, y)


def swap_kernel(broadcast, source, out, send_sem, receive_sem, own_sem):
    n_z, n_x, n_c, n_y = sizes()
    count = n_z * n_x * n_c * n_y
    z, x, c, y = place()
    me = ((z * n_x + x) * n_c + c) * n_y + y

    def device_of(index):
        return (
            index // (n_x * n_c * n_y), index // (n_c * n_y) % n_x, index // n_y % n_c, index % n_y
        )

    def taken(index):
        return source.at[0] if broadcast else source.at[index]

    barrier = pltpu.get_barrier_semaphore()

    def call(step, unused):
        other = lax.rem(me + step, count)
        pl.semaphore_signal(barrier, inc=1, device_id=device_of(other), device_id_type=MESH)
        return unused

    lax.fori_loop(1, count, call, 0)
    own = pltpu.make_async_copy(taken(me), out.at[me], own_sem)
    own.start()
    pl.semaphore_wait(barrier, count - 1)

    def copy(step):
        other = lax.rem(me + step, count)
        return remote(
            taken(other), out.at[me], send_sem.at[step], receive_sem.at[step], device_of(other)
        )

    def start(step, unused):
        copy(step).start()
        return unused

    def finish(step, unused):
        copy(step).wait()
        return unused

    lax.fori_loop(1, count, start, 0)
    lax.fori_loop(1, count, finish, 0)
    own.wait()


def swap(blocks, broadcast, collective_id):
    count = 1
    for size in sizes():
        count *= size
    return pl.pallas_call(
        functools.partial(swap_kernel, broadcast),
        out_shape=jax.ShapeDtypeStruct((count,) + blocks.shape[1:], blocks.dtype),
        in_specs=[VMEM],
        out_specs=VMEM,
        scratch_shapes=[
            pltpu.SemaphoreType.DMA((count,)),
            pltpu.SemaphoreType.DMA((count,)),
            pltpu.SemaphoreType.DMA,
        ],
        compiler_params=pltpu.CompilerParams(collective_id=collective_id, has_side_effects=True),
    )(blocks)


def gather_all_kernel(rows_in, out, z_send, z_recv, x_send, x_recv, y_send, y_recv, c_send, c_recv, own_sem):
    n_z = lax.axis_size("z")
    half = rows_in.shape[0] // 2
    (z, x, c, y), x_near, y_near, c_near = around()
    low, high = pl.ds(0, half), pl.ds(half, half)
    everything = pl.ds(0, 2 * half)

    barrier = pltpu.get_barrier_semaphore()
    for device in (x_near, y_near, c_near):
        pl.semaphore_signal(barrier, inc=1, device_id=device, device_id_type=MESH)

    @pl.when(z > 0)
    def _():
        pl.semaphore_signal(barrier, inc=1, device_id=(z - 1, x, c, y), device_id_type=MESH)

    @pl.when(z < n_z - 1)
    def _():
        pl.semaphore_signal(barrier, inc=1, device_id=(z + 1, x, c, y), device_id_type=MESH)

    own = pltpu.make_async_copy(rows_in, out.at[z, x, c, y], own_sem)
    own.start()
    pl.semaphore_wait(
        barrier, 3 + jnp.where(z > 0, 1, 0) + jnp.where(z < n_z - 1, 1, 0)
    )

    def block(origin, px, py, rows):
        return out.at[origin, px, c, py, rows]

    def z_copy(source, origin, up):
        other = (z + 1, x, c, y) if up else (z - 1, x, c, y)
        return remote(
            source, out.at[origin, x, c, y], z_send.at[origin, 1 if up else 0], z_recv.at[origin], other
        )

    def x_copy(source, origin):
        return remote(source, out.at[origin, x, c, y], x_send.at[origin, 0], x_recv.at[origin, 0], x_near)

    def y_copy(source, origin):
        return remote(source, out.at[origin, x, c, y], y_send.at[origin, 0], y_recv.at[origin, 0], y_near)

    def x_relay(origin):
        part = block(origin, x, 1 - y, high)
        return remote(part, part, x_send.at[origin, 1], x_recv.at[origin, 1], x_near)

    def y_relay(origin):
        part = block(origin, 1 - x, y, low)
        return remote(part, part, y_send.at[origin, 1], y_recv.at[origin, 1], y_near)

    def c_copy(source, origin, px, py):
        slot = px * 2 + py
        return remote(
            source, out.at[origin, px, c, py], c_send.at[origin, slot], c_recv.at[origin, slot], c_near
        )

    def spread(source, origin):
        x_copy(source, origin).start()
        y_copy(source, origin).start()
        c_copy(source, origin, x, y).start()

    def column(origin):
        return out.at[origin, x, c, y]

    def relay(origin):
        x_copy(column(origin), origin).wait_recv()
        y_relay(origin).start()
        y_copy(column(origin), origin).wait_recv()
        x_relay(origin).start()
        c_copy(block(origin, 1 - x, y, everything), origin, 1 - x, y).start()
        c_copy(block(origin, x, 1 - y, everything), origin, x, 1 - y).start()

    def finish(origin):
        x_relay(origin).wait_recv()
        y_relay(origin).wait_recv()
        c_copy(block(origin, 1 - x, 1 - y, everything), origin, 1 - x, 1 - y).start()

    def when_origin(origin, action):
        @pl.when((origin >= 0) & (origin < n_z))
        def _():
            action(origin)

    def arrive(step):
        below, above = z - step, z + step

        @pl.when(below >= 0)
        def _():
            z_copy(rows_in, below, True).wait_recv()

            @pl.when(z < n_z - 1)
            def _():
                z_copy(column(below), below, True).start()

            spread(column(below), below)

        @pl.when(above < n_z)
        def _():
            z_copy(rows_in, above, False).wait_recv()

            @pl.when(z > 0)
            def _():
                z_copy(column(above), above, False).start()

            spread(column(above), above)

    @pl.when(z < n_z - 1)
    def _():
        z_copy(rows_in, z, True).start()

    @pl.when(z > 0)
    def _():
        z_copy(rows_in, z, False).start()

    spread(rows_in, z)
    for step in range(1, n_z + 2):
        if step < n_z:
            arrive(step)
        for action, back in ((relay, 1), (finish, 2)):
            late = step - back
            if late == 0:
                action(z)
            elif 0 < late < n_z:
                when_origin(z - late, action)
                when_origin(z + late, action)
    own.wait()

    def close(origin, unused):
        x_copy(rows_in, origin).wait_send()
        y_copy(rows_in, origin).wait_send()
        x_relay(origin).wait_send()
        y_relay(origin).wait_send()
        for px in range(2):
            for py in range(2):
                copy = c_copy(out.at[origin, px, c, py], origin, px, py)
                copy.wait_send()
                copy.wait_recv()

        @pl.when((z < n_z - 1) & (origin <= z))
        def _():
            z_copy(rows_in, origin, True).wait_send()

        @pl.when((z > 0) & (origin >= z))
        def _():
            z_copy(rows_in, origin, False).wait_send()

        return unused

    lax.fori_loop(0, n_z, close, 0)


def gather_all(rows, collective_id):
    n_z = lax.axis_size("z")
    shape = sizes() + rows.shape
    dma = pltpu.SemaphoreType.DMA
    out = pl.pallas_call(
        gather_all_kernel,
        out_shape=jax.ShapeDtypeStruct(shape, rows.dtype),
        in_specs=[ANY],
        out_specs=ANY,
        scratch_shapes=[
            dma((n_z, 2)), dma((n_z,)), dma((n_z, 2)), dma((n_z, 2)), dma((n_z, 2)), dma((n_z, 2)),
            dma((n_z, 4)), dma((n_z, 4)), dma,
        ],
        compiler_params=pltpu.CompilerParams(collective_id=collective_id, has_side_effects=True),
    )(rows)
    return out.reshape(-1, rows.shape[1])


def total_of(*parts):
    total = parts[0].astype(jnp.float32)
    for part in parts[1:]:
        total = total + part.astype(jnp.float32)
    return total


def scatter_all_kernel(
    source, out, lanes, c_got, x_got, y_got, x_last, y_last, below, above,
    own_sem, c_send, c_recv, x_send, x_recv, y_send, y_recv, z_send, z_recv,
):
    n_z = lax.axis_size("z")
    rows = source.shape[4]
    half = rows // 2
    (z, x, c, y), x_near, y_near, c_near = around()
    low, high = pl.ds(0, half), pl.ds(half, half)
    up, down = n_z - 1 - z, z
    longer, shorter = jnp.maximum(up, down), jnp.minimum(up, down)
    far_side = jnp.where(up >= down, 1, -1)

    def target(step):
        late = step - (longer - shorter)
        near_side = jnp.where(late % 2 == 0, far_side, -far_side)
        return jnp.where(
            late < 0, z + far_side * (longer - step), z + near_side * (shorter - late // 2)
        )

    barrier = pltpu.get_barrier_semaphore()
    for device in (x_near, y_near, c_near):
        pl.semaphore_signal(barrier, inc=1, device_id=device, device_id_type=MESH)

    @pl.when(z > 0)
    def _():
        pl.semaphore_signal(barrier, inc=1, device_id=(z - 1, x, c, y), device_id_type=MESH)

    @pl.when(z < n_z - 1)
    def _():
        pl.semaphore_signal(barrier, inc=1, device_id=(z + 1, x, c, y), device_id_type=MESH)

    def own_copy(slab, px):
        return pltpu.make_async_copy(source.at[slab, px, c], lanes.at[slab, px], own_sem.at[slab, px])

    def c_copy(slab, px):
        return remote(
            source.at[slab, px, 1 - c], c_got.at[slab, px], c_send.at[slab, px], c_recv.at[slab, px], c_near
        )

    def load(step, unused):
        for px in range(2):
            own_copy(target(step), px).start()
        return unused

    lax.fori_loop(0, n_z, load, 0)
    pl.semaphore_wait(barrier, 3 + jnp.where(z > 0, 1, 0) + jnp.where(z < n_z - 1, 1, 0))

    def hand(step, unused):
        for px in range(2):
            c_copy(target(step), px).start()
        return unused

    lax.fori_loop(0, n_z, hand, 0)

    def x_first(slab, part):
        block = lanes.at[slab, 1 - x, jnp.where(part == 0, y, 1 - y), low]
        return remote(block, x_got.at[slab, part], x_send.at[slab, part], x_recv.at[slab, part], x_near)

    def y_first(slab, part):
        block = lanes.at[slab, jnp.where(part == 0, x, 1 - x), 1 - y, high]
        return remote(block, y_got.at[slab, part], y_send.at[slab, part], y_recv.at[slab, part], y_near)

    def y_second(slab):
        block = lanes.at[slab, x, 1 - y, low]
        return remote(block, y_last.at[slab], y_send.at[slab, 2], y_recv.at[slab, 2], y_near)

    def x_second(slab):
        block = lanes.at[slab, 1 - x, y, high]
        return remote(block, x_last.at[slab], x_send.at[slab, 2], x_recv.at[slab, 2], x_near)

    def z_up(slab):
        return remote(
            lanes.at[slab, x, y], below.at[slab], z_send.at[slab], z_recv.at[slab, 0], (z + 1, x, c, y)
        )

    def z_down(slab):
        return remote(
            lanes.at[slab, x, y], above.at[slab], z_send.at[slab], z_recv.at[slab, 1], (z - 1, x, c, y)
        )

    def begin(step):
        slab = target(step)
        for px in range(2):
            own_copy(slab, px).wait()
            c_copy(slab, px).wait_recv()

        def merge(px, py):
            lanes[slab, px, py] = total_of(lanes[slab, px, py], c_got[slab, px, py]).astype(jnp.bfloat16)

        merge(1 - x, 1 - y)
        x_first(slab, 1).start()
        y_first(slab, 1).start()
        merge(1 - x, y)
        x_first(slab, 0).start()
        merge(x, 1 - y)
        y_first(slab, 0).start()
        merge(x, y)

    def middle(step):
        slab = target(step)
        x_first(slab, 1).wait_recv()
        x_first(slab, 0).wait_send()
        y_first(slab, 0).wait_send()
        lanes[slab, x, 1 - y, low] = total_of(
            lanes[slab, x, 1 - y, low], x_got[slab, 1]
        ).astype(jnp.bfloat16)
        y_second(slab).start()
        y_first(slab, 1).wait_recv()
        lanes[slab, 1 - x, y, high] = total_of(
            lanes[slab, 1 - x, y, high], y_got[slab, 1]
        ).astype(jnp.bfloat16)
        x_second(slab).start()

    def finish(step):
        slab = target(step)
        x_first(slab, 0).wait_recv()
        y_second(slab).wait_recv()
        first = total_of(lanes[slab, x, y, low], x_got[slab, 0], y_last[slab])
        y_first(slab, 0).wait_recv()
        x_second(slab).wait_recv()
        second = total_of(lanes[slab, x, y, high], y_got[slab, 0], x_last[slab])

        @pl.when(slab > z)
        def _():
            @pl.when(z == 0)
            def _():
                lanes[slab, x, y, low] = first.astype(jnp.bfloat16)
                lanes[slab, x, y, high] = second.astype(jnp.bfloat16)

            @pl.when(z > 0)
            def _():
                z_up(slab).wait_recv()
                lanes[slab, x, y, low] = total_of(first, below[slab, low]).astype(jnp.bfloat16)
                lanes[slab, x, y, high] = total_of(second, below[slab, high]).astype(jnp.bfloat16)

            z_up(slab).start()

        @pl.when(slab < z)
        def _():
            @pl.when(z == n_z - 1)
            def _():
                lanes[slab, x, y, low] = first.astype(jnp.bfloat16)
                lanes[slab, x, y, high] = second.astype(jnp.bfloat16)

            @pl.when(z < n_z - 1)
            def _():
                z_down(slab).wait_recv()
                lanes[slab, x, y, low] = total_of(first, above[slab, low]).astype(jnp.bfloat16)
                lanes[slab, x, y, high] = total_of(second, above[slab, high]).astype(jnp.bfloat16)

            z_down(slab).start()

        @pl.when(slab == z)
        def _():
            out[low, :] = first
            out[high, :] = second

            @pl.when(z > 0)
            def _():
                z_up(slab).wait_recv()
                out[...] += below[slab].astype(jnp.float32)

            @pl.when(z < n_z - 1)
            def _():
                z_down(slab).wait_recv()
                out[...] += above[slab].astype(jnp.float32)

    def turn(step, unused):
        @pl.when(step < n_z)
        def _():
            begin(step)

        @pl.when((step >= 1) & (step < n_z + 1))
        def _():
            middle(step - 1)

        @pl.when(step >= 2)
        def _():
            finish(step - 2)

        return unused

    lax.fori_loop(0, n_z + 2, turn, 0)

    def close(slab, unused):
        for px in range(2):
            c_copy(slab, px).wait_send()
        x_first(slab, 1).wait_send()
        y_first(slab, 1).wait_send()
        x_second(slab).wait_send()
        y_second(slab).wait_send()

        @pl.when(slab > z)
        def _():
            z_up(slab).wait_send()

        @pl.when(slab < z)
        def _():
            z_down(slab).wait_send()

        return unused

    lax.fori_loop(0, n_z, close, 0)


def scatter_all(partial_rows, collective_id):
    n_z, n_x, n_c, n_y = sizes()
    rows = partial_rows.shape[0] // (n_z * n_x * n_c * n_y)
    width = partial_rows.shape[1]
    half = rows // 2
    low = jnp.bfloat16
    dma = pltpu.SemaphoreType.DMA
    return pl.pallas_call(
        scatter_all_kernel,
        out_shape=jax.ShapeDtypeStruct((rows, width), jnp.float32),
        in_specs=[ANY],
        out_specs=VMEM,
        scratch_shapes=[
            pltpu.VMEM((n_z, n_x, n_y, rows, width), low),
            pltpu.VMEM((n_z, n_x, n_y, rows, width), low),
            pltpu.VMEM((n_z, 2, half, width), low),
            pltpu.VMEM((n_z, 2, half, width), low),
            pltpu.VMEM((n_z, half, width), low),
            pltpu.VMEM((n_z, half, width), low),
            pltpu.VMEM((n_z, rows, width), low),
            pltpu.VMEM((n_z, rows, width), low),
            dma((n_z, 2)), dma((n_z, 2)), dma((n_z, 2)), dma((n_z, 3)), dma((n_z, 3)), dma((n_z, 3)),
            dma((n_z, 3)), dma((n_z,)), dma((n_z, 2)),
        ],
        compiler_params=pltpu.CompilerParams(
            collective_id=collective_id, has_side_effects=True, vmem_limit_bytes=56 * MIB
        ),
    )(partial_rows.astype(low).reshape(n_z, n_x, n_c, n_y, rows, width))


def trade_kernel(source, out, send_sem, recv_sem, own_sem):
    (z, x, c, y), x_near, y_near, _ = around()
    diagonal = (z, 1 - x, c, 1 - y)
    own = pltpu.make_async_copy(source.at[x, y], out.at[x, y], own_sem)
    own.start()
    greet((x_near, y_near, diagonal))
    copies = [
        remote(source.at[device[1], device[3]], out.at[x, y], send_sem.at[slot], recv_sem.at[slot], device)
        for slot, device in enumerate((diagonal, x_near, y_near))
    ]
    for copy in copies:
        copy.start()
    for copy in copies:
        copy.wait()
    own.wait()


def trade(blocks, collective_id):
    return pl.pallas_call(
        trade_kernel,
        out_shape=jax.ShapeDtypeStruct(blocks.shape, blocks.dtype),
        in_specs=[VMEM],
        out_specs=VMEM,
        scratch_shapes=[
            pltpu.SemaphoreType.DMA((3,)), pltpu.SemaphoreType.DMA((3,)), pltpu.SemaphoreType.DMA
        ],
        compiler_params=pltpu.CompilerParams(collective_id=collective_id, has_side_effects=True),
    )(blocks)


PIECES = 4


def spread_kernel(
    prompt_slabs, own_rows, far, near, tail, z_send, z_recv, c_send, c_recv, n_send, n_recv, own_sem
):
    n_z = lax.axis_size("z")
    lane = own_rows.shape[0]
    chunk = lane // 2
    size = lane // PIECES
    (z, x, c, y), _, _, c_near = around()
    above, below = (z + 1, x, c, y), (z - 1, x, c, y)
    in_prompt = z < prompt_slabs
    takes_down = z < prompt_slabs - 1
    gives_down = (z > 0) & (z < prompt_slabs)

    barrier = pltpu.get_barrier_semaphore()
    pl.semaphore_signal(barrier, inc=1, device_id=c_near, device_id_type=MESH)

    @pl.when(z > 0)
    def _():
        pl.semaphore_signal(barrier, inc=1, device_id=below, device_id_type=MESH)

    @pl.when(takes_down)
    def _():
        pl.semaphore_signal(barrier, inc=1, device_id=above, device_id_type=MESH)

    first, second = pl.ds(0, chunk), pl.ds(chunk, chunk)
    own = [
        pltpu.make_async_copy(own_rows.at[first], near.at[1], own_sem.at[0]),
        pltpu.make_async_copy(own_rows.at[second], near.at[3], own_sem.at[1]),
    ]
    own_far = pltpu.make_async_copy(own_rows, far.at[jnp.minimum(z, prompt_slabs - 1), c], own_sem.at[2])
    own_edge = pltpu.make_async_copy(own_rows.at[first], near.at[0], own_sem.at[3])
    edge = (z == 0) & (c == 0)
    for copy in own:
        copy.start()

    @pl.when(in_prompt)
    def _():
        own_far.start()

    @pl.when(edge)
    def _():
        own_edge.start()

    pl.semaphore_wait(
        barrier, 1 + jnp.where(z < n_z - 1, 1, 0) + jnp.where(gives_down, 1, 0)
    )

    def part(index):
        return pl.ds(index * size, size)

    def z_copy(source, slab, index, up):
        return remote(
            source, far.at[slab, c, part(index)], z_send.at[slab, index, 1 if up else 0],
            z_recv.at[slab, index], above if up else below,
        )

    def c_copy(source, slab, index):
        return remote(
            source, far.at[slab, c, part(index)], c_send.at[slab, index], c_recv.at[slab, index], c_near
        )

    def t_copy():
        return remote(own_rows.at[second], tail, n_send.at[0], n_recv.at[0], above)

    def t_hand():
        return remote(tail, near.at[0], n_send.at[1], n_recv.at[1], c_near)

    def n_copy(half):
        slot = jnp.where(c == 0, 2 * half, 2)
        return remote(
            own_rows.at[pl.ds(half * chunk, chunk)], near.at[slot], n_send.at[2 + half], n_recv.at[2 + half],
            c_near,
        )

    @pl.when(in_prompt)
    def _():
        for index in range(PIECES):
            source = own_rows.at[part(index)]

            @pl.when(z < n_z - 1)
            def _():
                z_copy(source, z, index, True).start()

            @pl.when(z > 0)
            def _():
                z_copy(source, z, index, False).start()

            c_copy(source, z, index).start()

    @pl.when((c == 1) & (z < n_z - 1))
    def _():
        t_copy().start()

    n_copy(0).start()

    @pl.when(c == 0)
    def _():
        n_copy(1).start()

    for distance in range(1, n_z):
        low_slab, high_slab = z - distance, z + distance
        for index in range(PIECES):

            @pl.when((low_slab >= 0) & (low_slab < prompt_slabs))
            def _():
                source = far.at[low_slab, c, part(index)]
                z_copy(source, low_slab, index, True).wait_recv()

                @pl.when(z < n_z - 1)
                def _():
                    z_copy(source, low_slab, index, True).start()

                c_copy(source, low_slab, index).start()

            if distance < prompt_slabs:

                @pl.when(high_slab < prompt_slabs)
                def _():
                    source = far.at[high_slab, c, part(index)]
                    z_copy(source, high_slab, index, False).wait_recv()

                    @pl.when(z > 0)
                    def _():
                        z_copy(source, high_slab, index, False).start()

                    c_copy(source, high_slab, index).start()

    @pl.when((c == 1) & (z > 0))
    def _():
        t_copy().wait_recv()
        t_hand().start()
        t_hand().wait_send()

    @pl.when((c == 1) & (z < n_z - 1))
    def _():
        t_copy().wait_send()

    @pl.when((c == 0) & (z > 0))
    def _():
        t_hand().wait_recv()

    n_copy(0).wait_send()
    n_copy(0).wait_recv()

    @pl.when(c == 0)
    def _():
        n_copy(1).wait_send()

    @pl.when(c == 1)
    def _():
        n_copy(1).wait_recv()

    for slab in range(prompt_slabs):
        for index in range(PIECES):
            copy = c_copy(own_rows.at[part(index)], slab, index)
            copy.wait_send()
            copy.wait_recv()

            @pl.when((z < n_z - 1) & (slab <= z))
            def _():
                z_copy(own_rows.at[part(index)], slab, index, True).wait_send()

            @pl.when((z > 0) & (slab >= z))
            def _():
                z_copy(own_rows.at[part(index)], slab, index, False).wait_send()

    for copy in own:
        copy.wait()

    @pl.when(in_prompt)
    def _():
        own_far.wait()

    @pl.when(edge)
    def _():
        own_edge.wait()


def spread_keys(own_rows, prompt_rows, collective_id):
    lane, width = own_rows.shape
    slabs = prompt_rows // (2 * lane)
    dma = pltpu.SemaphoreType.DMA
    far, near, _ = pl.pallas_call(
        functools.partial(spread_kernel, slabs),
        out_shape=(
            jax.ShapeDtypeStruct((slabs, 2, lane, width), own_rows.dtype),
            jax.ShapeDtypeStruct((4, lane // 2, width), own_rows.dtype),
            jax.ShapeDtypeStruct((lane // 2, width), own_rows.dtype),
        ),
        in_specs=[VMEM],
        out_specs=(VMEM,) * 3,
        scratch_shapes=[
            dma((slabs, PIECES, 2)), dma((slabs, PIECES)), dma((slabs, PIECES)), dma((slabs, PIECES)),
            dma((4,)), dma((4,)), dma((4,)),
        ],
        compiler_params=pltpu.CompilerParams(collective_id=collective_id, has_side_effects=True),
    )(own_rows)
    return far.reshape(prompt_rows, width), near.reshape(2 * lane, width)


def collect_kernel(
    prompt_slabs, far, near, out, own, c_got, z_got, n_got, tail_pass, tail_got,
    c_send, c_recv, z_send, z_recv, n_send, n_recv,
):
    n_z = lax.axis_size("z")
    lane = out.shape[0]
    chunk = lane // 2
    size = lane // PIECES
    (z, x, c, y), _, _, c_near = around()
    above, below = (z + 1, x, c, y), (z - 1, x, c, y)

    barrier = pltpu.get_barrier_semaphore()
    pl.semaphore_signal(barrier, inc=1, device_id=c_near, device_id_type=MESH)

    @pl.when(z < n_z - 1)
    def _():
        pl.semaphore_signal(barrier, inc=1, device_id=above, device_id_type=MESH)

    pl.semaphore_wait(barrier, 1 + jnp.where(z > 0, 1, 0))

    def part(index):
        return pl.ds(index * size, size)

    def c_copy(slab, index):
        return remote(
            far.at[slab, 1 - c, part(index)], c_got.at[slab, part(index)], c_send.at[slab, index],
            c_recv.at[slab, index], c_near,
        )

    def z_copy(slab, index):
        return remote(
            own.at[slab, part(index)], z_got.at[slab, part(index)], z_send.at[slab, index],
            z_recv.at[slab, index], below,
        )

    def n_copy(half):
        slot = jnp.where(c == 0, 2, 2 * half)
        return remote(near.at[slot], n_got.at[half], n_send.at[half], n_recv.at[half], c_near)

    def t_hand():
        return remote(near.at[0], tail_pass, n_send.at[2], n_recv.at[2], c_near)

    def t_copy():
        return remote(tail_pass, tail_got, n_send.at[3], n_recv.at[3], below)

    for slab in range(prompt_slabs):
        for index in range(PIECES):
            c_copy(slab, index).start()
    n_copy(0).start()

    @pl.when(c == 1)
    def _():
        n_copy(1).start()

    @pl.when((c == 0) & (z > 0))
    def _():
        t_hand().start()

    for slab in range(prompt_slabs):
        for index in range(PIECES):
            c_copy(slab, index).wait_recv()
            rows = part(index)
            mine = total_of(far[slab, c, rows, :], c_got[slab, rows, :])

            @pl.when((z == n_z - 1) & (z > slab))
            def _():
                own[slab, rows, :] = mine.astype(jnp.bfloat16)
                z_copy(slab, index).start()

            @pl.when((z < n_z - 1) & (z > slab))
            def _():
                z_copy(slab, index).wait_recv()
                own[slab, rows, :] = total_of(mine, z_got[slab, rows, :]).astype(jnp.bfloat16)
                z_copy(slab, index).start()

            @pl.when((z < n_z - 1) & (z == slab))
            def _():
                z_copy(slab, index).wait_recv()
                out[rows, :] = total_of(mine, z_got[slab, rows, :])

            @pl.when((z == n_z - 1) & (z == slab))
            def _():
                out[rows, :] = mine

    @pl.when((c == 1) & (z > 0))
    def _():
        t_hand().wait_recv()
        t_copy().start()

    @pl.when(z >= prompt_slabs)
    def _():
        out[...] = jnp.zeros_like(out)

    n_copy(0).wait_recv()
    first, second = pl.ds(0, chunk), pl.ds(chunk, chunk)
    out[first, :] += total_of(near[1], n_got[0])
    out[second, :] += near[3].astype(jnp.float32)

    @pl.when(c == 0)
    def _():
        n_copy(1).wait_recv()
        out[second, :] += n_got[1].astype(jnp.float32)

    @pl.when((c == 1) & (z < n_z - 1))
    def _():
        t_copy().wait_recv()
        out[second, :] += tail_got[...].astype(jnp.float32)

    @pl.when((c == 1) & (z > 0))
    def _():
        t_copy().wait_send()

    @pl.when((c == 0) & (z > 0))
    def _():
        t_hand().wait_send()

    n_copy(0).wait_send()

    @pl.when(c == 1)
    def _():
        n_copy(1).wait_send()

    for slab in range(prompt_slabs):
        for index in range(PIECES):
            c_copy(slab, index).wait_send()

            @pl.when(z > slab)
            def _():
                z_copy(slab, index).wait_send()


def collect_keys(far, near, collective_id):
    prompt_rows, width = far.shape
    lane = near.shape[0] // 2
    slabs = prompt_rows // (2 * lane)
    dma = pltpu.SemaphoreType.DMA
    low = jnp.bfloat16
    return pl.pallas_call(
        functools.partial(collect_kernel, slabs),
        out_shape=jax.ShapeDtypeStruct((lane, width), jnp.float32),
        in_specs=[VMEM] * 2,
        out_specs=VMEM,
        scratch_shapes=[
            pltpu.VMEM((slabs, lane, width), low),
            pltpu.VMEM((slabs, lane, width), low),
            pltpu.VMEM((slabs, lane, width), low),
            pltpu.VMEM((2, lane // 2, width), low),
            pltpu.VMEM((lane // 2, width), low),
            pltpu.VMEM((lane // 2, width), low),
            dma((slabs, PIECES)), dma((slabs, PIECES)), dma((slabs, PIECES)), dma((slabs, PIECES)),
            dma((4,)), dma((4,)),
        ],
        compiler_params=pltpu.CompilerParams(
            collective_id=collective_id, has_side_effects=True, vmem_limit_bytes=40 * MIB
        ),
    )(far.astype(low).reshape(slabs, 2, lane, width), near.astype(low).reshape(4, lane // 2, width))


SQRT_HALF = 0.5**0.5
DENSITY = 0.3989422804014327


def matmul(left, right):
    return jnp.dot(left, right, preferred_element_type=jnp.float32)


def inner(left, right):
    return lax.dot_general(
        left, right, (((0,), (0,)), ((), ())), preferred_element_type=jnp.float32
    )


def outer(left, right):
    return lax.dot_general(
        left, right, (((1,), (1,)), ((), ())), preferred_element_type=jnp.float32
    )


def plane_gather(own_rows, blocks, send_sem, recv_sem):
    half = own_rows.shape[0] // 2
    (z, x, c, y), x_near, y_near, _ = around()
    low, high = pl.ds(0, half), pl.ds(half, half)

    def copy(slot, px, py, rows, source, device):
        target = blocks.at[px, py, rows]
        return remote(target if source is None else source.at[rows], target, send_sem.at[slot], recv_sem.at[slot], device)

    first = [
        copy(0, x, y, low, own_rows, x_near),
        copy(1, x, y, high, own_rows, y_near),
        copy(2, x, y, high, own_rows, x_near),
        copy(3, x, y, low, own_rows, y_near),
    ]
    relays = [copy(4, 1 - x, y, low, None, y_near), copy(5, x, 1 - y, high, None, x_near)]
    for each in first:
        each.start()

    def wait_near():
        first[0].wait_recv()
        relays[0].start()
        first[1].wait_recv()
        relays[1].start()

    def wait_x():
        first[2].wait_recv()

    def wait_y():
        first[3].wait_recv()

    def wait_diagonal():
        for each in relays:
            each.wait_recv()

    def close():
        for each in first + relays:
            each.wait_send()

    return wait_near, wait_x, wait_y, wait_diagonal, close


def plane_sum(parts, got, out, send_sem, recv_sem):
    (z, x, c, y), x_near, y_near, _ = around()
    diagonal = (z, 1 - x, c, 1 - y)
    copies = [
        remote(parts.at[device[1], device[3]], got.at[slot], send_sem.at[slot], recv_sem.at[slot], device)
        for slot, device in enumerate((x_near, y_near, diagonal))
    ]

    def close():
        for each in copies:
            each.wait_recv()
        out[...] = total_of(parts[x, y], got[0], got[1], got[2])
        for each in copies:
            each.wait_send()

    return copies, close


def experts_kernel(
    own_rows, route, up, down, out, wide, before, hidden, parts, got, g_send, g_recv, s_send, s_recv
):
    (z, x, c, y), x_near, y_near, _ = around()
    diagonal = (z, 1 - x, c, 1 - y)
    greet((x_near, y_near, diagonal))
    wait_near, wait_x, wait_y, wait_diagonal, close = plane_gather(own_rows, wide, g_send, g_recv)
    copies, finish = plane_sum(parts, got, out, s_send, s_recv)
    wide[x, y] = own_rows[...]

    def work(px, py):
        rows = wide[px, py]
        first = route[px, py] == 0
        value = jnp.where(first, matmul(rows, up[0]), matmul(rows, up[1]))
        before[px, py] = value
        active = 0.5 * value * (1.0 + lax.erf(value * SQRT_HALF))
        hidden_first = jnp.where(first, active, 0.0).astype(jnp.bfloat16)
        hidden_second = jnp.where(first, 0.0, active).astype(jnp.bfloat16)
        hidden[px, py] = active.astype(jnp.bfloat16)
        total = outer(hidden_first, down[0]) + outer(hidden_second, down[1])
        parts[px, py] = total.astype(jnp.bfloat16)

    work(x, y)
    wait_near()
    wait_x()
    work(1 - x, y)
    copies[0].start()
    wait_y()
    work(x, 1 - y)
    copies[1].start()
    wait_diagonal()
    work(1 - x, 1 - y)
    copies[2].start()
    finish()
    close()


def experts(own_rows, route, up, down, collective_id):
    _, n_x, _, n_y = sizes()
    own, width = own_rows.shape
    wide = up.shape[2]
    dma = pltpu.SemaphoreType.DMA
    low = jnp.bfloat16
    return pl.pallas_call(
        experts_kernel,
        out_shape=(
            jax.ShapeDtypeStruct((own, width), jnp.float32),
            jax.ShapeDtypeStruct((n_x, n_y, own, width), low),
            jax.ShapeDtypeStruct((n_x, n_y, own, wide), jnp.float32),
            jax.ShapeDtypeStruct((n_x, n_y, own, wide), low),
        ),
        in_specs=[VMEM] * 4,
        out_specs=(VMEM,) * 4,
        scratch_shapes=[
            pltpu.VMEM((n_x, n_y, own, width), low),
            pltpu.VMEM((3, own, width), low),
            dma((6,)), dma((6,)), dma((3,)), dma((3,)),
        ],
        compiler_params=pltpu.CompilerParams(
            collective_id=collective_id, has_side_effects=True, vmem_limit_bytes=40 * MIB
        ),
        cost_estimate=pl.CostEstimate(
            flops=8 * own * 4 * width * wide, bytes_accessed=8 * MIB, transcendentals=4 * own * wide
        ),
    )(own_rows, route, up, down)


def experts_back_kernel(
    own_rows, route, up, down, wide, before, hidden, out, grads,
    wide_grad, before_grad, parts, got, g_send, g_recv, s_send, s_recv,
):
    (z, x, c, y), x_near, y_near, _ = around()
    diagonal = (z, 1 - x, c, 1 - y)
    greet((x_near, y_near, diagonal))
    wait_near, wait_x, wait_y, wait_diagonal, close = plane_gather(own_rows, wide_grad, g_send, g_recv)
    copies, finish = plane_sum(parts, got, out, s_send, s_recv)
    wide_grad[x, y] = own_rows[...]

    def work(px, py):
        rows = wide_grad[px, py]
        first = route[px, py] == 0
        hidden_grad = jnp.where(first, matmul(rows, down[0]), matmul(rows, down[1]))
        value = before[px, py]
        slope = 0.5 * (1.0 + lax.erf(value * SQRT_HALF)) + value * (
            DENSITY * jnp.exp(-0.5 * value * value)
        )
        change = (hidden_grad * slope).astype(jnp.bfloat16)
        before_grad[px, py] = change
        change_first = jnp.where(first, change, 0)
        change_second = jnp.where(first, 0, change)
        total = outer(change_first, up[0]) + outer(change_second, up[1])
        parts[px, py] = total.astype(jnp.bfloat16)

    work(x, y)
    wait_near()
    wait_x()
    work(1 - x, y)
    copies[0].start()
    wait_y()
    work(x, 1 - y)
    copies[1].start()
    wait_diagonal()
    work(1 - x, 1 - y)
    copies[2].start()
    close()

    lane = 4 * own_rows.shape[0]
    rows = wide[...].reshape(lane, -1)
    grad_rows = wide_grad[...].reshape(lane, -1)
    first = route[...].reshape(lane, 1) == 0
    change = before_grad[...].reshape(lane, -1)
    active = hidden[...].reshape(lane, -1)
    low = jnp.bfloat16
    grads[0] = inner(rows, jnp.where(first, change, 0)).astype(low)
    grads[1] = inner(rows, jnp.where(first, 0, change)).astype(low)
    grads[2] = inner(grad_rows, jnp.where(first, active, 0)).astype(low)
    grads[3] = inner(grad_rows, jnp.where(first, 0, active)).astype(low)
    finish()


def experts_back(own_rows, route, up, down, wide, before, hidden, collective_id):
    _, n_x, _, n_y = sizes()
    own, width = own_rows.shape
    units = up.shape[2]
    dma = pltpu.SemaphoreType.DMA
    low = jnp.bfloat16
    return pl.pallas_call(
        experts_back_kernel,
        out_shape=(
            jax.ShapeDtypeStruct((own, width), jnp.float32),
            jax.ShapeDtypeStruct((4, width, units), low),
        ),
        in_specs=[VMEM] * 7,
        out_specs=(VMEM,) * 2,
        scratch_shapes=[
            pltpu.VMEM((n_x, n_y, own, width), low),
            pltpu.VMEM((n_x, n_y, own, units), low),
            pltpu.VMEM((n_x, n_y, own, width), low),
            pltpu.VMEM((3, own, width), low),
            dma((6,)), dma((6,)), dma((3,)), dma((3,)),
        ],
        compiler_params=pltpu.CompilerParams(
            collective_id=collective_id, has_side_effects=True, vmem_limit_bytes=48 * MIB
        ),
        cost_estimate=pl.CostEstimate(
            flops=16 * own * 4 * width * units, bytes_accessed=12 * MIB, transcendentals=8 * own * units
        ),
    )(own_rows, route, up, down, wide, before, hidden)


def project_kernel(rows, weight, out, parts, got, s_send, s_recv):
    (z, x, c, y), x_near, y_near, _ = around()
    diagonal = (z, 1 - x, c, 1 - y)
    barrier = pltpu.get_barrier_semaphore()
    for device in (x_near, y_near, diagonal):
        pl.semaphore_signal(barrier, inc=1, device_id=device, device_id_type=MESH)
    copies, finish = plane_sum(parts, got, out, s_send, s_recv)

    def work(px, py):
        parts[px, py] = outer(rows[px, py], weight[...]).astype(jnp.bfloat16)

    work(1 - x, 1 - y)
    pl.semaphore_wait(barrier, 3)
    copies[2].start()
    work(1 - x, y)
    copies[0].start()
    work(x, 1 - y)
    copies[1].start()
    work(x, y)
    finish()


def project(rows, weight, collective_id):
    n_x, n_y, own, depth = rows.shape
    width = weight.shape[0]
    low = jnp.bfloat16
    dma = pltpu.SemaphoreType.DMA
    return pl.pallas_call(
        project_kernel,
        out_shape=jax.ShapeDtypeStruct((own, width), jnp.float32),
        in_specs=[VMEM] * 2,
        out_specs=VMEM,
        scratch_shapes=[
            pltpu.VMEM((n_x, n_y, own, width), low), pltpu.VMEM((3, own, width), low), dma((3,)), dma((3,)),
        ],
        compiler_params=pltpu.CompilerParams(
            collective_id=collective_id, has_side_effects=True, vmem_limit_bytes=32 * MIB
        ),
        cost_estimate=pl.CostEstimate(
            flops=8 * own * width * depth, bytes_accessed=4 * MIB, transcendentals=0
        ),
    )(rows, weight)


def key_position(index, part, chunk):
    lane = 2 * chunk
    start = (part // 2) * (2 * lane) + (part % 2) * chunk
    return start + index + jnp.where(index >= chunk, chunk, 0)


def near_shown(side, chunk, query_pos, query_seg, near_pos, near_seg):
    columns = slice(side * chunk, (side + 1) * chunk)
    rows = slice(2 * side * chunk, 2 * (side + 1) * chunk)
    shown = (
        (near_seg[rows, :] == query_seg[:, columns])
        & (near_pos[rows, :] <= query_pos[:, columns])
        & (near_pos[rows, :] >= PROMPT)
    )
    return columns, rows, shown


def attend_kernel(
    chunk, query, far, near, query_pos, query_seg, near_pos, near_seg,
    out, out_low, log_total, scores, far_t, near_t,
):
    lane, feature = query.shape
    group = feature // HEAD_DIM
    prompt_rows = far.shape[0]
    parts = prompt_rows // lane
    query_t = (query[...].astype(jnp.float32) * HEAD_DIM ** (-0.5)).T.astype(jnp.bfloat16)
    far_t[...] = far[...].astype(jnp.float32).T.astype(jnp.bfloat16)
    near_t[...] = near[...].astype(jnp.float32).T.astype(jnp.bfloat16)
    row_of = lax.broadcasted_iota(jnp.int32, (feature, lane), 0)
    q_pos = query_pos[...]

    for head in range(group):
        low, high = head * HEAD_DIM, (head + 1) * HEAD_DIM
        query_h = jnp.where((row_of >= low) & (row_of < high), query_t, 0)

        def score_part(part, peak):
            block = far[pl.ds(pl.multiple_of(part * lane, lane), lane), :feature]
            value = matmul(block, query_h)
            index = lax.broadcasted_iota(jnp.int32, (lane, lane), 0)
            value = jnp.where(key_position(index, part, chunk) <= q_pos, value, MASKED)
            scores[pl.ds(pl.multiple_of(part * lane, lane), lane), :] = value
            return jnp.maximum(peak, jnp.max(value, axis=0, keepdims=True))

        peak = lax.fori_loop(0, parts, score_part, jnp.full((1, lane), MASKED, jnp.float32))
        near_peaks = []
        for side in range(2):
            columns, rows, shown = near_shown(side, chunk, query_pos, query_seg, near_pos, near_seg)
            value = matmul(near[rows, :feature], query_h[:, columns])
            value = jnp.where(shown, value, MASKED)
            scores[prompt_rows : prompt_rows + lane, columns] = value
            near_peaks.append(jnp.max(value, axis=0, keepdims=True))
        peak = jnp.maximum(peak, jnp.concatenate(near_peaks, axis=1))

        def weigh_part(part, state):
            total, mixed = state
            start = pl.multiple_of(part * lane, lane)
            chance = jnp.exp(scores[pl.ds(start, lane), :] - peak)
            total = total + jnp.sum(chance, axis=0, keepdims=True)
            mixed = mixed + matmul(
                far_t[feature + low : feature + high, pl.ds(start, lane)],
                chance.astype(jnp.bfloat16),
            )
            return total, mixed

        total, mixed = lax.fori_loop(
            0,
            parts,
            weigh_part,
            (jnp.zeros((1, lane), jnp.float32), jnp.zeros((HEAD_DIM, lane), jnp.float32)),
        )
        near_total, near_mixed = [], []
        for side in range(2):
            columns = slice(side * chunk, (side + 1) * chunk)
            rows = slice(side * lane, (side + 1) * lane)
            chance = jnp.exp(scores[prompt_rows : prompt_rows + lane, columns] - peak[:, columns])
            near_total.append(jnp.sum(chance, axis=0, keepdims=True))
            near_mixed.append(
                matmul(near_t[feature + low : feature + high, rows], chance.astype(jnp.bfloat16))
            )
        total = total + jnp.concatenate(near_total, axis=1)
        mixed = mixed + jnp.concatenate(near_mixed, axis=1)
        out[low:high, :] = mixed / total
        log_total[head : head + 1, :] = peak + jnp.log(total)
    out_low[...] = out[...].T.astype(jnp.bfloat16)


def attend(queries, far, near, places, chunk):
    lane, feature = queries.shape
    prompt_rows = far.shape[0]
    group = feature // HEAD_DIM
    total_rows = prompt_rows + lane
    return pl.pallas_call(
        functools.partial(attend_kernel, chunk),
        out_shape=(
            jax.ShapeDtypeStruct((feature, lane), jnp.float32),
            jax.ShapeDtypeStruct((lane, feature), jnp.bfloat16),
            jax.ShapeDtypeStruct((group, lane), jnp.float32),
        ),
        in_specs=[VMEM] * 7,
        out_specs=(VMEM,) * 3,
        scratch_shapes=[
            pltpu.VMEM((total_rows, lane), jnp.float32),
            pltpu.VMEM((2 * feature, prompt_rows), jnp.bfloat16),
            pltpu.VMEM((2 * feature, 2 * lane), jnp.bfloat16),
        ],
        compiler_params=pltpu.CompilerParams(vmem_limit_bytes=48 * MIB),
        cost_estimate=pl.CostEstimate(
            flops=8 * group * lane * total_rows * 128,
            bytes_accessed=8 * MIB,
            transcendentals=group * lane * total_rows,
        ),
    )(queries, far, near, *places)


def attend_back_kernel(
    chunk, query, far, near, query_pos, query_seg, near_pos, near_seg,
    log_total, mixed, answer, query_grad, far_grad, near_grad,
    far_t, near_t, far_values, near_values, far_sum, near_sum, query_sum,
):
    lane, feature = query.shape
    group = feature // HEAD_DIM
    prompt_rows = far.shape[0]
    parts = prompt_rows // lane
    scaled = (query[...].astype(jnp.float32) * HEAD_DIM ** (-0.5)).astype(jnp.bfloat16)
    query_t = scaled.astype(jnp.float32).T.astype(jnp.bfloat16)
    answers = answer[...]
    answer_t = answers.astype(jnp.float32).T.astype(jnp.bfloat16)
    far_t[...] = far[:, :feature].astype(jnp.float32).T.astype(jnp.bfloat16)
    near_t[...] = near[:, :feature].astype(jnp.float32).T.astype(jnp.bfloat16)
    far_values[...] = far[:, feature:]
    near_values[...] = near[:, feature:]
    row_of = lax.broadcasted_iota(jnp.int32, (feature, lane), 0)
    column_of = lax.broadcasted_iota(jnp.int32, (lane, feature), 1)
    q_pos = query_pos[...]

    for head in range(group):
        low, high = head * HEAD_DIM, (head + 1) * HEAD_DIM
        in_rows = (row_of >= low) & (row_of < high)
        in_columns = (column_of >= low) & (column_of < high)
        query_ht = jnp.where(in_rows, query_t, 0)
        answer_ht = jnp.where(in_rows, answer_t, 0)
        query_h = jnp.where(in_columns, scaled, 0)
        answer_h = jnp.where(in_columns, answers, 0)
        log_h = log_total[head : head + 1, :]
        delta_h = jnp.sum(
            answer_t[low:high, :].astype(jnp.float32) * mixed[low:high, :], axis=0, keepdims=True
        )

        def slopes(key_block, value_block, shown, columns):
            value = matmul(key_block, query_ht[:, columns])
            chance = jnp.exp(jnp.where(shown, value - log_h[:, columns], MASKED))
            slope = matmul(value_block, answer_ht[:, columns])
            change = (chance * (slope - delta_h[:, columns])).astype(jnp.bfloat16)
            chance = chance.astype(jnp.bfloat16)
            return change, matmul(change, query_h[columns]), matmul(chance, answer_h[columns])

        def add(sums, rows, key_part, value_part):
            if head == 0:
                sums[0, rows, :] = key_part
                sums[1, rows, :] = value_part
            else:
                sums[0, rows, :] += key_part
                sums[1, rows, :] += value_part

        def back_part(part, total):
            rows = pl.ds(pl.multiple_of(part * lane, lane), lane)
            index = lax.broadcasted_iota(jnp.int32, (lane, lane), 0)
            shown = key_position(index, part, chunk) <= q_pos
            change, key_part, value_part = slopes(
                far[rows, :feature], far_values[rows, :], shown, slice(0, lane)
            )
            add(far_sum, rows, key_part, value_part)
            return total + matmul(far_t[low:high, rows], change)

        total = lax.fori_loop(0, parts, back_part, jnp.zeros((HEAD_DIM, lane), jnp.float32))
        near_total = []
        for side in range(2):
            columns, rows, shown = near_shown(side, chunk, query_pos, query_seg, near_pos, near_seg)
            change, key_part, value_part = slopes(
                near[rows, :feature], near_values[rows, :], shown, columns
            )
            add(near_sum, rows, key_part, value_part)
            near_total.append(matmul(near_t[low:high, rows], change))
        query_sum[low:high, :] = (total + jnp.concatenate(near_total, axis=1)) * HEAD_DIM ** (-0.5)
    query_grad[...] = query_sum[...].T.astype(jnp.bfloat16)
    for sums, grad in ((far_sum, far_grad), (near_sum, near_grad)):
        grad[...] = jnp.concatenate(
            [sums[0].astype(jnp.bfloat16), sums[1].astype(jnp.bfloat16)], axis=1
        )


def attend_back(queries, far, near, places, log_total, mixed, answer, chunk):
    lane, feature = queries.shape
    prompt_rows = far.shape[0]
    group = feature // HEAD_DIM
    total_rows = prompt_rows + lane
    low = jnp.bfloat16
    return pl.pallas_call(
        functools.partial(attend_back_kernel, chunk),
        out_shape=(
            jax.ShapeDtypeStruct((lane, feature), low),
            jax.ShapeDtypeStruct((prompt_rows, 2 * feature), low),
            jax.ShapeDtypeStruct((2 * lane, 2 * feature), low),
        ),
        in_specs=[VMEM] * 10,
        out_specs=(VMEM,) * 3,
        scratch_shapes=[
            pltpu.VMEM((feature, prompt_rows), low),
            pltpu.VMEM((feature, 2 * lane), low),
            pltpu.VMEM((prompt_rows, feature), low),
            pltpu.VMEM((2 * lane, feature), low),
            pltpu.VMEM((2, prompt_rows, feature), jnp.float32),
            pltpu.VMEM((2, 2 * lane, feature), jnp.float32),
            pltpu.VMEM((feature, lane), jnp.float32),
        ],
        compiler_params=pltpu.CompilerParams(vmem_limit_bytes=48 * MIB),
        cost_estimate=pl.CostEstimate(
            flops=20 * group * lane * total_rows * 128,
            bytes_accessed=12 * MIB,
            transcendentals=group * lane * total_rows,
        ),
    )(queries, far, near, *places, log_total, mixed, answer)


def pad_rows(block):
    return jnp.pad(block, ((0, 8 - block.shape[0]), (0, 0)))


def adam_update(weight, moment_one, moment_two, gradient, step_rate, decay_rate):
    first_new = BETA_ONE * moment_one + (1.0 - BETA_ONE) * gradient
    second_new = BETA_TWO * moment_two + (1.0 - BETA_TWO) * gradient * gradient
    normalized = (
        first_new
        / (1.0 - BETA_ONE**STEP)
        / (jnp.sqrt(second_new / (1.0 - BETA_TWO**STEP)) + ADAM_EPS)
    )
    return (weight - step_rate * (normalized + decay_rate * weight), first_new, second_new)


def per_device(
    token_ids,
    targets,
    valid_mask,
    cont_lengths,
    routes,
    vocab_table,
    vocab_first,
    vocab_second,
    attn_weights,
    attn_first,
    attn_second,
    router,
    router_first,
    router_second,
    norm_gains,
    gains_first,
    gains_second,
    expert_up,
    up_first,
    up_second,
    expert_down,
    down_first,
    down_second,
):
    slabs = lax.axis_size("z")
    planes = lax.axis_size("x")
    cores = lax.axis_size("core")
    sides = lax.axis_size("head")
    groups = planes * sides
    z_at, x_at, core_at, side_at = (lax.axis_index(name) for name in ALL)
    blk_at = (z_at * planes + x_at) * cores + core_at
    device_at = blk_at * sides + side_at
    group_at = x_at * sides + side_at
    tokens = valid_mask.shape[0]
    chunk = token_ids.shape[0]
    own = chunk // sides
    lane = planes * chunk
    feature = D // groups
    wide = expert_up.shape[3] // planes
    shard_rows = vocab_table.shape[0]
    logit_scale = D ** (-0.5)

    cont_ends = jnp.cumsum(cont_lengths)
    valid_f = valid_mask.astype(jnp.float32)
    token_count = jnp.sum(valid_mask).astype(jnp.float32)
    expert_ids = jnp.arange(EXPERTS, dtype=jnp.int32)

    own_ints = jnp.concatenate([token_ids[None], targets[None], routes], axis=0)
    own_ints = lax.dynamic_slice_in_dim(own_ints, side_at * own, own, axis=1).astype(jnp.float32)
    rows_of = attn_weights.shape[1]
    smalls = jnp.concatenate(
        [router.transpose(0, 2, 1).reshape(LAYERS * EXPERTS, rows_of), norm_gains], axis=0
    )
    smalls = smalls.astype(jnp.bfloat16).astype(jnp.float32)
    smalls = jnp.pad(smalls, ((0, 16 - smalls.shape[0]), (0, own - rows_of)))
    whole_f = swap(jnp.concatenate([pad_rows(own_ints), smalls], axis=0)[None], True, 1)
    whole = whole_f[:, : 2 + LAYERS].astype(jnp.int32)
    smalls = whole_f[:, 8:, :rows_of].transpose(1, 0, 2).reshape(16, D)
    router_all = smalls[: LAYERS * EXPERTS].reshape(LAYERS, EXPERTS, D).transpose(0, 2, 1)
    router_all = router_all.astype(jnp.bfloat16)
    gains_f = smalls[LAYERS * EXPERTS :]
    ids_all = whole[:, 0].reshape(tokens)
    targets_all = whole[:, 1].reshape(tokens)
    routes_lane = lax.dynamic_index_in_dim(
        whole.reshape(slabs, planes, cores, sides, 2 + LAYERS, own), z_at, 0, False
    )
    routes_lane = lax.dynamic_index_in_dim(routes_lane, core_at, 1, False)[:, :, 2:]
    routes_lane = routes_lane.transpose(2, 0, 1, 3)[..., None]
    routes_own = lax.dynamic_slice_in_dim(routes, side_at * own, own, axis=1)

    table = vocab_table.astype(jnp.bfloat16)
    attn_low = attn_weights.astype(jnp.bfloat16)
    qkv_send = attn_low[:, :, : 3 * D].reshape(LAYERS, rows_of, 3, groups, feature)
    qkv_send = jnp.concatenate([qkv_send[:, :, 1:], qkv_send[:, :, :1]], axis=2)
    qkv_send = qkv_send.transpose(3, 0, 1, 2, 4).reshape(groups, LAYERS, rows_of, 3 * feature)
    qkv_got = lax.all_to_all(qkv_send, PLANE, split_axis=0, concat_axis=0, tiled=True)
    out_all = lax.all_gather(attn_low[:, :, 3 * D :], ALL, axis=1, tiled=True)
    expert_send = jnp.stack([expert_up, expert_down], axis=1).astype(jnp.bfloat16)
    depth = expert_send.shape[3]
    expert_send = expert_send.reshape(LAYERS, 2 * EXPERTS, depth, planes, wide)
    expert_send = expert_send.transpose(3, 0, 1, 2, 4)
    expert_got = lax.all_to_all(expert_send, ("x",), split_axis=0, concat_axis=0, tiled=True)
    qkv_weights, expert_weights = [], []
    for layer_index in range(LAYERS):
        block = lax.all_gather(qkv_got[:, layer_index], LINE, axis=0)
        block = block.reshape(slabs, cores, planes, sides, rows_of, 3 * feature)
        qkv_weights.append(block.transpose(0, 2, 1, 3, 4, 5).reshape(D, 3 * feature))
        block = lax.all_gather(expert_got[:, layer_index], LINE, axis=0)
        block = block.reshape(slabs, cores, planes, 2, EXPERTS, depth, wide)
        block = block.transpose(3, 4, 0, 2, 1, 5, 6).reshape(2, EXPERTS, D, wide)
        expert_weights.append(block)

    offsets = jnp.arange(chunk, dtype=jnp.int32)
    first_blk = z_at * planes * cores + core_at
    query_pos = jnp.concatenate([(first_blk + cores * part) * chunk + offsets for part in range(planes)])
    near_blks = [first_blk - 1 + part for part in range(2 * planes)]
    near_pos = jnp.concatenate([blk * chunk + offsets for blk in near_blks])
    query_seg = segment_of(query_pos, cont_ends)
    near_seg = segment_of(near_pos, cont_ends)
    places = (query_pos[None, :], query_seg[None, :], near_pos[:, None], near_seg[:, None])

    vocab_ids = device_at * shard_rows + jnp.arange(shard_rows, dtype=jnp.int32)
    token_hot = (ids_all[:, None] == vocab_ids[None, :]).astype(jnp.bfloat16)
    stream = scatter_all(matmul(token_hot, table), 2)

    kept = []
    for layer_index in range(LAYERS):
        up, down = expert_weights[layer_index][0], expert_weights[layer_index][1]
        normed_lane = lax.all_gather(
            rms_norm(stream, gains_f[2 * layer_index]).astype(jnp.bfloat16),
            PLANE, axis=0, tiled=True,
        )
        qkv = matmul(normed_lane, qkv_weights[layer_index]).astype(jnp.bfloat16)
        queries = qkv[:, 2 * feature :]
        far, near = spread_keys(qkv[:, : 2 * feature], PROMPT, 10)
        mixed_t, mixed_low, log_total = attend(queries, far, near, places, chunk)
        mixed_own = trade(mixed_low.reshape(planes, sides, own, feature), 3)
        mixed_own = mixed_own.transpose(2, 0, 1, 3).reshape(own, D)
        middle = stream + matmul(mixed_own, out_all[layer_index])
        normed_two = rms_norm(middle, gains_f[2 * layer_index + 1]).astype(jnp.bfloat16)
        chance = jax.nn.softmax(matmul(normed_two, router_all[layer_index]), axis=-1)
        output, wide_rows, before, hidden = experts(
            normed_two, routes_lane[layer_index], up, down, 11
        )
        own_pick = (routes_own[layer_index][:, None] == expert_ids[None, :]).astype(jnp.float32)
        gate = jnp.sum(chance * own_pick, axis=1, keepdims=True)
        kept.append(
            (
                stream, normed_lane, queries, far, near, mixed_t, mixed_own, log_total, middle,
                normed_two, chance, wide_rows, before, hidden, output, own_pick, gate,
            )
        )
        stream = middle + gate * output

    final_gain = gains_f[2 * LAYERS]
    final_all = gather_all(rms_norm(stream, final_gain).astype(jnp.bfloat16), 4)
    logits = outer(final_all, table) * logit_scale
    row_max = jnp.max(logits, axis=1, keepdims=True)
    row_log = row_max[:, 0] + jnp.log(jnp.sum(jnp.exp(logits - row_max), axis=1))
    target_hot = targets_all[:, None] == vocab_ids[None, :]
    hit_loss = jnp.sum(jnp.where(target_hot, logits, 0.0) * valid_f[:, None])
    devices = tokens // own
    row_logs = jnp.broadcast_to(row_log.reshape(devices, 1, own), (devices, 8, own))
    own_log = jax.nn.logsumexp(swap(row_logs, False, 5), axis=0)
    log_sum = swap(own_log[None], True, 6)[:, 0].reshape(tokens)
    own_valid = lax.dynamic_slice_in_dim(valid_f, device_at * own, own)
    own_loss = jnp.sum(own_log[0] * own_valid) - hit_loss
    logit_grad = (
        (jnp.exp(logits - log_sum[:, None]) - target_hot.astype(jnp.float32))
        * (valid_f / token_count)[:, None]
    ).astype(jnp.bfloat16)
    final_grad = scatter_all(matmul(logit_grad, table) * logit_scale, 2)
    table_grad = inner(logit_grad, final_all) * logit_scale
    stream_grad, final_gain_grad = jax.vjp(rms_norm, stream, final_gain)[1](final_grad)

    qkv_shares = [None] * LAYERS
    out_shares = [None] * LAYERS
    router_list = [None] * LAYERS
    expert_shares = [None] * LAYERS
    gain_list = [None] * (2 * LAYERS + 1)
    gain_list[2 * LAYERS] = final_gain_grad
    for layer_index in reversed(range(LAYERS)):
        (
            stream, normed_lane, queries, far, near, mixed_t, mixed_own, log_total, middle,
            normed_two, chance, wide_rows, before, hidden, output, own_pick, gate,
        ) = kept[layer_index]
        up, down = expert_weights[layer_index][0], expert_weights[layer_index][1]
        out_grad = (gate * stream_grad).astype(jnp.bfloat16)
        chance_grad = jnp.sum(stream_grad * output, axis=1)[:, None] * own_pick
        choice_grad = chance * (chance_grad - jnp.sum(chance * chance_grad, axis=1, keepdims=True))
        router_list[layer_index] = jnp.dot(
            normed_two.astype(jnp.float32).T, choice_grad, precision=lax.Precision.HIGHEST
        )
        normed_grad = jnp.dot(
            choice_grad,
            router_all[layer_index].astype(jnp.float32).T,
            precision=lax.Precision.HIGHEST,
        )
        rows_grad, expert_grad = experts_back(
            out_grad, routes_lane[layer_index], up, down, wide_rows, before, hidden, 12
        )
        normed_grad = normed_grad + rows_grad
        expert_grad = expert_grad.reshape(2 * EXPERTS, slabs, planes, cores, depth, wide)
        expert_grad = expert_grad.transpose(1, 3, 2, 0, 4, 5).reshape(
            slabs * cores, planes, 2 * EXPERTS, depth, wide
        )
        expert_grad = lax.psum_scatter(expert_grad, LINE, scatter_dimension=0, tiled=True)[0]
        expert_grad = lax.all_to_all(
            expert_grad, ("x",), split_axis=0, concat_axis=0, tiled=True
        )
        expert_shares[layer_index] = (
            expert_grad.transpose(1, 2, 0, 3)
            .reshape(2, EXPERTS, depth, planes * wide)
            .astype(jnp.float32)
        )
        middle_part, gain_list[2 * layer_index + 1] = jax.vjp(
            rms_norm, middle, gains_f[2 * layer_index + 1]
        )[1](normed_grad)
        middle_grad = stream_grad + middle_part
        branch_grad = middle_grad.astype(jnp.bfloat16)
        answer_own = outer(branch_grad, out_all[layer_index]).astype(jnp.bfloat16)
        answer = trade(
            answer_own.reshape(own, planes, sides, feature).transpose(1, 2, 0, 3), 3
        ).reshape(lane, feature)
        out_shares[layer_index] = inner(mixed_own, branch_grad).astype(jnp.bfloat16)
        query_grad, far_grad, near_grad = attend_back(
            queries, far, near, places, log_total, mixed_t, answer, chunk
        )
        key_grad = collect_keys(far_grad, near_grad, 13).astype(jnp.bfloat16)
        qkv_grad = jnp.concatenate([key_grad, query_grad], axis=1)
        qkv_proj = inner(normed_lane, qkv_grad).astype(jnp.bfloat16)
        qkv_proj = qkv_proj.reshape(slabs, planes, cores, sides, rows_of, 3 * feature)
        qkv_proj = qkv_proj.transpose(0, 2, 1, 3, 4, 5).reshape(
            slabs * cores, groups, rows_of, 3 * feature
        )
        qkv_proj = lax.psum_scatter(qkv_proj, LINE, scatter_dimension=0, tiled=True)[0]
        qkv_proj = lax.all_to_all(qkv_proj, PLANE, split_axis=0, concat_axis=0, tiled=True)
        qkv_proj = qkv_proj.reshape(groups, rows_of, 3, feature)
        qkv_proj = jnp.concatenate([qkv_proj[:, :, 2:], qkv_proj[:, :, :2]], axis=2)
        qkv_shares[layer_index] = (
            qkv_proj.transpose(1, 2, 0, 3)
            .reshape(rows_of, 3 * D)
            .astype(jnp.float32)
        )
        normed_att_grad = project(
            qkv_grad.reshape(planes, sides, own, 3 * feature), qkv_weights[layer_index], 14
        )
        stream_part, gain_list[2 * layer_index] = jax.vjp(
            rms_norm, stream, gains_f[2 * layer_index]
        )[1](normed_att_grad)
        stream_grad = middle_grad + stream_part

    embed_grad = gather_all(stream_grad.astype(jnp.bfloat16), 4)
    table_share = table_grad + inner(token_hot, embed_grad)
    small = jnp.concatenate(
        [jnp.stack(router_list).transpose(1, 0, 2).reshape(D, -1), jnp.stack(gain_list).T], axis=1
    )
    small = small.reshape(devices, rows_of, -1).transpose(0, 2, 1)
    small = jnp.pad(small, ((0, 0), (0, 16 - small.shape[1]), (0, 128 - rows_of)))
    small = jnp.sum(swap(small, False, 7), axis=0)[:, :rows_of]
    router_share = (
        small[: LAYERS * EXPERTS].reshape(LAYERS, EXPERTS, rows_of).transpose(0, 2, 1)
    )
    gain_share = small[LAYERS * EXPERTS : LAYERS * EXPERTS + 2 * LAYERS + 1]
    out_share = jnp.stack(out_shares).reshape(LAYERS, devices, rows_of, D).transpose(1, 0, 2, 3)
    out_share = scatter_all(out_share.reshape(devices * 32, -1), 8)
    out_shares = out_share.reshape(LAYERS, rows_of, D)
    attn_share = jnp.stack(
        [
            jnp.concatenate([qkv_shares[index], out_shares[index]], axis=1)
            for index in range(LAYERS)
        ]
    )
    up_share = jnp.stack([share[0] for share in expert_shares])
    down_share = jnp.stack([share[1] for share in expert_shares])
    shares = (table_share, attn_share, router_share, gain_share, up_share, down_share)
    squares = jnp.sum(table_share * table_share)
    for share_part in shares[1:]:
        squares = squares + jnp.sum(share_part * share_part)
    sums = jnp.pad(jnp.stack([squares, own_loss])[:, None], ((0, 6), (0, 127)))
    sums = jnp.sum(swap(sums[None], True, 9)[:, :2, 0], axis=0)
    square_total, loss_sum = sums[0], sums[1]
    grad_norm = jnp.sqrt(square_total)
    factor = CLIP_AT / jnp.maximum(grad_norm, CLIP_AT)
    weights = (vocab_table, attn_weights, router, norm_gains, expert_up, expert_down)
    firsts = (vocab_first, attn_first, router_first, gains_first, up_first, down_first)
    seconds = (vocab_second, attn_second, router_second, gains_second, up_second, down_second)
    results = [loss_sum, token_count, grad_norm]
    for number in range(6):
        results.extend(
            adam_update(
                weights[number],
                firsts[number],
                seconds[number],
                factor * shares[number],
                STEP_RATES[number],
                DECAY_RATES[number],
            )
        )
    return tuple(results)


def solution(mesh):
    blocks, sides = mesh.shape["blk"], mesh.shape["head"]
    fine = Mesh(mesh.devices.reshape(blocks // 4, 2, 2, sides), ALL)
    weight_specs = (
        (P(ALL, None),) * 3
        + (P(None, ALL, None),) * 3
        + (P(None, ALL, None),) * 3
        + (P(None, ALL),) * 3
        + (P(None, None, BLK, "head"),) * 6
    )
    return jax.shard_map(
        per_device,
        mesh=fine,
        in_specs=(P(BLK), P(BLK), P(), P(), P(None, BLK)) + weight_specs,
        out_specs=(P(), P(), P()) + weight_specs,
        check_vma=False,
    )
```

```python
import functools

import jax
import jax.numpy as jnp
from jax import lax
from jax.experimental import pallas as pl
from jax.experimental.pallas import tpu as pltpu
from jax.sharding import Mesh, PartitionSpec as P

D = 768
HEADS = 12
HEAD_DIM = 64
EXPERTS = 2
LAYERS = 2
PROMPT = 2048
STEP = 10

NORM_EPS = 1e-06
BETA_ONE = 0.9
BETA_TWO = 0.95
ADAM_EPS = 1e-08
CLIP_AT = 0.01
MASKED = -1e30
STEP_RATES = (2.0, 0.25, 0.04, 0.4, 0.04, 0.04)
DECAY_RATES = (0.01, 0.01, 0.01, 0.0, 0.01, 0.01)

ALL = ("z", "x", "core", "head")
BLK = ("z", "x", "core")
PLANE = ("x", "head")
LINE = ("z", "core")
MIB = 2**20
MESH = pl.DeviceIdType.MESH
ANY = pl.BlockSpec(memory_space=pl.ANY)
VMEM = pl.BlockSpec(memory_space=pltpu.VMEM)


def rms_norm(stream, gain):
    return stream * lax.rsqrt(jnp.mean(stream * stream, axis=-1, keepdims=True) + NORM_EPS) * gain


def segment_of(position, cont_ends):
    later = jnp.sum((cont_ends[None, :] <= (position - PROMPT)[:, None]).astype(jnp.int32), axis=1)
    return jnp.where(position < PROMPT, 0, 1 + later)


def place():
    return tuple(lax.axis_index(name) for name in ALL)


def sizes():
    return tuple(lax.axis_size(name) for name in ALL)


def remote(source, target, send, receive, device):
    return pltpu.make_async_remote_copy(
        src_ref=source, dst_ref=target, send_sem=send, recv_sem=receive,
        device_id=device, device_id_type=MESH,
    )


def greet(devices):
    barrier = pltpu.get_barrier_semaphore()
    for device in devices:
        pl.semaphore_signal(barrier, inc=1, device_id=device, device_id_type=MESH)
    pl.semaphore_wait(barrier, len(devices))


def around():
    z, x, c, y = place()
    return (z, x, c, y), (z, 1 - x, c, y), (z, x, c, 1 - y), (z, x, 1 - c, y)


def swap_kernel(broadcast, source, out, send_sem, receive_sem, own_sem):
    n_z, n_x, n_c, n_y = sizes()
    count = n_z * n_x * n_c * n_y
    z, x, c, y = place()
    me = ((z * n_x + x) * n_c + c) * n_y + y

    def device_of(index):
        return (
            index // (n_x * n_c * n_y), index // (n_c * n_y) % n_x, index // n_y % n_c, index % n_y
        )

    def taken(index):
        return source.at[0] if broadcast else source.at[index]

    barrier = pltpu.get_barrier_semaphore()

    def call(step, unused):
        other = lax.rem(me + step, count)
        pl.semaphore_signal(barrier, inc=1, device_id=device_of(other), device_id_type=MESH)
        return unused

    lax.fori_loop(1, count, call, 0)
    own = pltpu.make_async_copy(taken(me), out.at[me], own_sem)
    own.start()
    pl.semaphore_wait(barrier, count - 1)

    def copy(step):
        other = lax.rem(me + step, count)
        return remote(
            taken(other), out.at[me], send_sem.at[step], receive_sem.at[step], device_of(other)
        )

    def start(step, unused):
        copy(step).start()
        return unused

    def finish(step, unused):
        copy(step).wait()
        return unused

    lax.fori_loop(1, count, start, 0)
    lax.fori_loop(1, count, finish, 0)
    own.wait()


def swap(blocks, broadcast, collective_id):
    count = 1
    for size in sizes():
        count *= size
    return pl.pallas_call(
        functools.partial(swap_kernel, broadcast),
        out_shape=jax.ShapeDtypeStruct((count,) + blocks.shape[1:], blocks.dtype),
        in_specs=[VMEM],
        out_specs=VMEM,
        scratch_shapes=[
            pltpu.SemaphoreType.DMA((count,)),
            pltpu.SemaphoreType.DMA((count,)),
            pltpu.SemaphoreType.DMA,
        ],
        compiler_params=pltpu.CompilerParams(collective_id=collective_id, has_side_effects=True),
    )(blocks)


def gather_all_kernel(rows_in, out, z_send, z_recv, x_send, x_recv, y_send, y_recv, c_send, c_recv, own_sem):
    n_z = lax.axis_size("z")
    half = rows_in.shape[0] // 2
    (z, x, c, y), x_near, y_near, c_near = around()
    low, high = pl.ds(0, half), pl.ds(half, half)
    everything = pl.ds(0, 2 * half)

    barrier = pltpu.get_barrier_semaphore()
    for device in (x_near, y_near, c_near):
        pl.semaphore_signal(barrier, inc=1, device_id=device, device_id_type=MESH)

    @pl.when(z > 0)
    def _():
        pl.semaphore_signal(barrier, inc=1, device_id=(z - 1, x, c, y), device_id_type=MESH)

    @pl.when(z < n_z - 1)
    def _():
        pl.semaphore_signal(barrier, inc=1, device_id=(z + 1, x, c, y), device_id_type=MESH)

    own = pltpu.make_async_copy(rows_in, out.at[z, x, c, y], own_sem)
    own.start()
    pl.semaphore_wait(
        barrier, 3 + jnp.where(z > 0, 1, 0) + jnp.where(z < n_z - 1, 1, 0)
    )

    def block(origin, px, py, rows):
        return out.at[origin, px, c, py, rows]

    def z_copy(source, origin, up):
        other = (z + 1, x, c, y) if up else (z - 1, x, c, y)
        return remote(
            source, out.at[origin, x, c, y], z_send.at[origin, 1 if up else 0], z_recv.at[origin], other
        )

    def x_copy(source, origin):
        return remote(source, out.at[origin, x, c, y], x_send.at[origin, 0], x_recv.at[origin, 0], x_near)

    def y_copy(source, origin):
        return remote(source, out.at[origin, x, c, y], y_send.at[origin, 0], y_recv.at[origin, 0], y_near)

    def x_relay(origin):
        part = block(origin, x, 1 - y, high)
        return remote(part, part, x_send.at[origin, 1], x_recv.at[origin, 1], x_near)

    def y_relay(origin):
        part = block(origin, 1 - x, y, low)
        return remote(part, part, y_send.at[origin, 1], y_recv.at[origin, 1], y_near)

    def c_copy(source, origin, px, py):
        slot = px * 2 + py
        return remote(
            source, out.at[origin, px, c, py], c_send.at[origin, slot], c_recv.at[origin, slot], c_near
        )

    def spread(source, origin):
        x_copy(source, origin).start()
        y_copy(source, origin).start()
        c_copy(source, origin, x, y).start()

    def column(origin):
        return out.at[origin, x, c, y]

    def relay(origin):
        x_copy(column(origin), origin).wait_recv()
        y_relay(origin).start()
        y_copy(column(origin), origin).wait_recv()
        x_relay(origin).start()
        c_copy(block(origin, 1 - x, y, everything), origin, 1 - x, y).start()
        c_copy(block(origin, x, 1 - y, everything), origin, x, 1 - y).start()

    def finish(origin):
        x_relay(origin).wait_recv()
        y_relay(origin).wait_recv()
        c_copy(block(origin, 1 - x, 1 - y, everything), origin, 1 - x, 1 - y).start()

    def when_origin(origin, action):
        @pl.when((origin >= 0) & (origin < n_z))
        def _():
            action(origin)

    def arrive(step):
        below, above = z - step, z + step

        @pl.when(below >= 0)
        def _():
            z_copy(rows_in, below, True).wait_recv()

            @pl.when(z < n_z - 1)
            def _():
                z_copy(column(below), below, True).start()

            spread(column(below), below)

        @pl.when(above < n_z)
        def _():
            z_copy(rows_in, above, False).wait_recv()

            @pl.when(z > 0)
            def _():
                z_copy(column(above), above, False).start()

            spread(column(above), above)

    @pl.when(z < n_z - 1)
    def _():
        z_copy(rows_in, z, True).start()

    @pl.when(z > 0)
    def _():
        z_copy(rows_in, z, False).start()

    spread(rows_in, z)
    for step in range(1, n_z + 2):
        if step < n_z:
            arrive(step)
        for action, back in ((relay, 1), (finish, 2)):
            late = step - back
            if late == 0:
                action(z)
            elif 0 < late < n_z:
                when_origin(z - late, action)
                when_origin(z + late, action)
    own.wait()

    def close(origin, unused):
        x_copy(rows_in, origin).wait_send()
        y_copy(rows_in, origin).wait_send()
        x_relay(origin).wait_send()
        y_relay(origin).wait_send()
        for px in range(2):
            for py in range(2):
                copy = c_copy(out.at[origin, px, c, py], origin, px, py)
                copy.wait_send()
                copy.wait_recv()

        @pl.when((z < n_z - 1) & (origin <= z))
        def _():
            z_copy(rows_in, origin, True).wait_send()

        @pl.when((z > 0) & (origin >= z))
        def _():
            z_copy(rows_in, origin, False).wait_send()

        return unused

    lax.fori_loop(0, n_z, close, 0)


def gather_all(rows, collective_id):
    n_z = lax.axis_size("z")
    shape = sizes() + rows.shape
    dma = pltpu.SemaphoreType.DMA
    out = pl.pallas_call(
        gather_all_kernel,
        out_shape=jax.ShapeDtypeStruct(shape, rows.dtype),
        in_specs=[ANY],
        out_specs=ANY,
        scratch_shapes=[
            dma((n_z, 2)), dma((n_z,)), dma((n_z, 2)), dma((n_z, 2)), dma((n_z, 2)), dma((n_z, 2)),
            dma((n_z, 4)), dma((n_z, 4)), dma,
        ],
        compiler_params=pltpu.CompilerParams(collective_id=collective_id, has_side_effects=True),
    )(rows)
    return out.reshape(-1, rows.shape[1])


def total_of(*parts):
    total = parts[0].astype(jnp.float32)
    for part in parts[1:]:
        total = total + part.astype(jnp.float32)
    return total


def scatter_all_kernel(
    source, out, lanes, c_got, x_got, y_got, x_last, y_last, below, above,
    own_sem, c_send, c_recv, x_send, x_recv, y_send, y_recv, z_send, z_recv,
):
    n_z = lax.axis_size("z")
    rows = source.shape[4]
    half = rows // 2
    (z, x, c, y), x_near, y_near, c_near = around()
    low, high = pl.ds(0, half), pl.ds(half, half)
    up, down = n_z - 1 - z, z
    longer, shorter = jnp.maximum(up, down), jnp.minimum(up, down)
    far_side = jnp.where(up >= down, 1, -1)

    def target(step):
        late = step - (longer - shorter)
        near_side = jnp.where(late % 2 == 0, far_side, -far_side)
        return jnp.where(
            late < 0, z + far_side * (longer - step), z + near_side * (shorter - late // 2)
        )

    barrier = pltpu.get_barrier_semaphore()
    for device in (x_near, y_near, c_near):
        pl.semaphore_signal(barrier, inc=1, device_id=device, device_id_type=MESH)

    @pl.when(z > 0)
    def _():
        pl.semaphore_signal(barrier, inc=1, device_id=(z - 1, x, c, y), device_id_type=MESH)

    @pl.when(z < n_z - 1)
    def _():
        pl.semaphore_signal(barrier, inc=1, device_id=(z + 1, x, c, y), device_id_type=MESH)

    def own_copy(slab, px):
        return pltpu.make_async_copy(source.at[slab, px, c], lanes.at[slab, px], own_sem.at[slab, px])

    def c_copy(slab, px):
        return remote(
            source.at[slab, px, 1 - c], c_got.at[slab, px], c_send.at[slab, px], c_recv.at[slab, px], c_near
        )

    def load(step, unused):
        for px in range(2):
            own_copy(target(step), px).start()
        return unused

    lax.fori_loop(0, n_z, load, 0)
    pl.semaphore_wait(barrier, 3 + jnp.where(z > 0, 1, 0) + jnp.where(z < n_z - 1, 1, 0))

    def hand(step, unused):
        for px in range(2):
            c_copy(target(step), px).start()
        return unused

    lax.fori_loop(0, n_z, hand, 0)

    def x_first(slab, part):
        block = lanes.at[slab, 1 - x, jnp.where(part == 0, y, 1 - y), low]
        return remote(block, x_got.at[slab, part], x_send.at[slab, part], x_recv.at[slab, part], x_near)

    def y_first(slab, part):
        block = lanes.at[slab, jnp.where(part == 0, x, 1 - x), 1 - y, high]
        return remote(block, y_got.at[slab, part], y_send.at[slab, part], y_recv.at[slab, part], y_near)

    def y_second(slab):
        block = lanes.at[slab, x, 1 - y, low]
        return remote(block, y_last.at[slab], y_send.at[slab, 2], y_recv.at[slab, 2], y_near)

    def x_second(slab):
        block = lanes.at[slab, 1 - x, y, high]
        return remote(block, x_last.at[slab], x_send.at[slab, 2], x_recv.at[slab, 2], x_near)

    def z_up(slab):
        return remote(
            lanes.at[slab, x, y], below.at[slab], z_send.at[slab], z_recv.at[slab, 0], (z + 1, x, c, y)
        )

    def z_down(slab):
        return remote(
            lanes.at[slab, x, y], above.at[slab], z_send.at[slab], z_recv.at[slab, 1], (z - 1, x, c, y)
        )

    def begin(step):
        slab = target(step)
        for px in range(2):
            own_copy(slab, px).wait()
            c_copy(slab, px).wait_recv()

        def merge(px, py):
            lanes[slab, px, py] = total_of(lanes[slab, px, py], c_got[slab, px, py]).astype(jnp.bfloat16)

        merge(1 - x, 1 - y)
        x_first(slab, 1).start()
        y_first(slab, 1).start()
        merge(1 - x, y)
        x_first(slab, 0).start()
        merge(x, 1 - y)
        y_first(slab, 0).start()
        merge(x, y)

    def middle(step):
        slab = target(step)
        x_first(slab, 1).wait_recv()
        x_first(slab, 0).wait_send()
        y_first(slab, 0).wait_send()
        lanes[slab, x, 1 - y, low] = total_of(
            lanes[slab, x, 1 - y, low], x_got[slab, 1]
        ).astype(jnp.bfloat16)
        y_second(slab).start()
        y_first(slab, 1).wait_recv()
        lanes[slab, 1 - x, y, high] = total_of(
            lanes[slab, 1 - x, y, high], y_got[slab, 1]
        ).astype(jnp.bfloat16)
        x_second(slab).start()

    def finish(step):
        slab = target(step)
        x_first(slab, 0).wait_recv()
        y_second(slab).wait_recv()
        first = total_of(lanes[slab, x, y, low], x_got[slab, 0], y_last[slab])
        y_first(slab, 0).wait_recv()
        x_second(slab).wait_recv()
        second = total_of(lanes[slab, x, y, high], y_got[slab, 0], x_last[slab])

        @pl.when(slab > z)
        def _():
            @pl.when(z == 0)
            def _():
                lanes[slab, x, y, low] = first.astype(jnp.bfloat16)
                lanes[slab, x, y, high] = second.astype(jnp.bfloat16)

            @pl.when(z > 0)
            def _():
                z_up(slab).wait_recv()
                lanes[slab, x, y, low] = total_of(first, below[slab, low]).astype(jnp.bfloat16)
                lanes[slab, x, y, high] = total_of(second, below[slab, high]).astype(jnp.bfloat16)

            z_up(slab).start()

        @pl.when(slab < z)
        def _():
            @pl.when(z == n_z - 1)
            def _():
                lanes[slab, x, y, low] = first.astype(jnp.bfloat16)
                lanes[slab, x, y, high] = second.astype(jnp.bfloat16)

            @pl.when(z < n_z - 1)
            def _():
                z_down(slab).wait_recv()
                lanes[slab, x, y, low] = total_of(first, above[slab, low]).astype(jnp.bfloat16)
                lanes[slab, x, y, high] = total_of(second, above[slab, high]).astype(jnp.bfloat16)

            z_down(slab).start()

        @pl.when(slab == z)
        def _():
            out[low, :] = first
            out[high, :] = second

            @pl.when(z > 0)
            def _():
                z_up(slab).wait_recv()
                out[...] += below[slab].astype(jnp.float32)

            @pl.when(z < n_z - 1)
            def _():
                z_down(slab).wait_recv()
                out[...] += above[slab].astype(jnp.float32)

    def turn(step, unused):
        @pl.when(step < n_z)
        def _():
            begin(step)

        @pl.when((step >= 1) & (step < n_z + 1))
        def _():
            middle(step - 1)

        @pl.when(step >= 2)
        def _():
            finish(step - 2)

        return unused

    lax.fori_loop(0, n_z + 2, turn, 0)

    def close(slab, unused):
        for px in range(2):
            c_copy(slab, px).wait_send()
        x_first(slab, 1).wait_send()
        y_first(slab, 1).wait_send()
        x_second(slab).wait_send()
        y_second(slab).wait_send()

        @pl.when(slab > z)
        def _():
            z_up(slab).wait_send()

        @pl.when(slab < z)
        def _():
            z_down(slab).wait_send()

        return unused

    lax.fori_loop(0, n_z, close, 0)


def scatter_all(partial_rows, collective_id):
    n_z, n_x, n_c, n_y = sizes()
    rows = partial_rows.shape[0] // (n_z * n_x * n_c * n_y)
    width = partial_rows.shape[1]
    half = rows // 2
    low = jnp.bfloat16
    dma = pltpu.SemaphoreType.DMA
    return pl.pallas_call(
        scatter_all_kernel,
        out_shape=jax.ShapeDtypeStruct((rows, width), jnp.float32),
        in_specs=[ANY],
        out_specs=VMEM,
        scratch_shapes=[
            pltpu.VMEM((n_z, n_x, n_y, rows, width), low),
            pltpu.VMEM((n_z, n_x, n_y, rows, width), low),
            pltpu.VMEM((n_z, 2, half, width), low),
            pltpu.VMEM((n_z, 2, half, width), low),
            pltpu.VMEM((n_z, half, width), low),
            pltpu.VMEM((n_z, half, width), low),
            pltpu.VMEM((n_z, rows, width), low),
            pltpu.VMEM((n_z, rows, width), low),
            dma((n_z, 2)), dma((n_z, 2)), dma((n_z, 2)), dma((n_z, 3)), dma((n_z, 3)), dma((n_z, 3)),
            dma((n_z, 3)), dma((n_z,)), dma((n_z, 2)),
        ],
        compiler_params=pltpu.CompilerParams(
            collective_id=collective_id, has_side_effects=True,
            vmem_limit_bytes=n_z * 3 * MIB + 4 * MIB,
        ),
    )(partial_rows.astype(low).reshape(n_z, n_x, n_c, n_y, rows, width))


PIECES = 4


def spread_kernel(
    prompt_slabs, own_rows, far, near, tail, z_send, z_recv, c_send, c_recv, n_send, n_recv, own_sem
):
    n_z = lax.axis_size("z")
    lane = own_rows.shape[0]
    chunk = lane // 2
    size = lane // PIECES
    (z, x, c, y), _, _, c_near = around()
    above, below = (z + 1, x, c, y), (z - 1, x, c, y)
    in_prompt = z < prompt_slabs
    takes_down = z < prompt_slabs - 1
    gives_down = (z > 0) & (z < prompt_slabs)

    barrier = pltpu.get_barrier_semaphore()
    pl.semaphore_signal(barrier, inc=1, device_id=c_near, device_id_type=MESH)

    @pl.when(z > 0)
    def _():
        pl.semaphore_signal(barrier, inc=1, device_id=below, device_id_type=MESH)

    @pl.when(takes_down)
    def _():
        pl.semaphore_signal(barrier, inc=1, device_id=above, device_id_type=MESH)

    first, second = pl.ds(0, chunk), pl.ds(chunk, chunk)
    own = [
        pltpu.make_async_copy(own_rows.at[first], near.at[1], own_sem.at[0]),
        pltpu.make_async_copy(own_rows.at[second], near.at[3], own_sem.at[1]),
    ]
    own_far = pltpu.make_async_copy(own_rows, far.at[jnp.minimum(z, prompt_slabs - 1), c], own_sem.at[2])
    own_edge = pltpu.make_async_copy(own_rows.at[first], near.at[0], own_sem.at[3])
    edge = (z == 0) & (c == 0)
    for copy in own:
        copy.start()

    @pl.when(in_prompt)
    def _():
        own_far.start()

    @pl.when(edge)
    def _():
        own_edge.start()

    pl.semaphore_wait(
        barrier, 1 + jnp.where(z < n_z - 1, 1, 0) + jnp.where(gives_down, 1, 0)
    )

    def part(index):
        return pl.ds(index * size, size)

    def z_copy(source, slab, index, up):
        return remote(
            source, far.at[slab, c, part(index)], z_send.at[slab, index, 1 if up else 0],
            z_recv.at[slab, index], above if up else below,
        )

    def c_copy(source, slab, index):
        return remote(
            source, far.at[slab, c, part(index)], c_send.at[slab, index], c_recv.at[slab, index], c_near
        )

    def t_copy():
        return remote(own_rows.at[second], tail, n_send.at[0], n_recv.at[0], above)

    def t_hand():
        return remote(tail, near.at[0], n_send.at[1], n_recv.at[1], c_near)

    def n_copy(half):
        slot = jnp.where(c == 0, 2 * half, 2)
        return remote(
            own_rows.at[pl.ds(half * chunk, chunk)], near.at[slot], n_send.at[2 + half], n_recv.at[2 + half],
            c_near,
        )

    @pl.when(in_prompt)
    def _():
        for index in range(PIECES):
            source = own_rows.at[part(index)]

            @pl.when(z < n_z - 1)
            def _():
                z_copy(source, z, index, True).start()

            @pl.when(z > 0)
            def _():
                z_copy(source, z, index, False).start()

            c_copy(source, z, index).start()

    @pl.when((c == 1) & (z < n_z - 1))
    def _():
        t_copy().start()

    n_copy(0).start()

    @pl.when(c == 0)
    def _():
        n_copy(1).start()

    for distance in range(1, n_z):
        low_slab, high_slab = z - distance, z + distance
        for index in range(PIECES):

            @pl.when((low_slab >= 0) & (low_slab < prompt_slabs))
            def _():
                source = far.at[low_slab, c, part(index)]
                z_copy(source, low_slab, index, True).wait_recv()

                @pl.when(z < n_z - 1)
                def _():
                    z_copy(source, low_slab, index, True).start()

                c_copy(source, low_slab, index).start()

            if distance < prompt_slabs:

                @pl.when(high_slab < prompt_slabs)
                def _():
                    source = far.at[high_slab, c, part(index)]
                    z_copy(source, high_slab, index, False).wait_recv()

                    @pl.when(z > 0)
                    def _():
                        z_copy(source, high_slab, index, False).start()

                    c_copy(source, high_slab, index).start()

    @pl.when((c == 1) & (z > 0))
    def _():
        t_copy().wait_recv()
        t_hand().start()
        t_hand().wait_send()

    @pl.when((c == 1) & (z < n_z - 1))
    def _():
        t_copy().wait_send()

    @pl.when((c == 0) & (z > 0))
    def _():
        t_hand().wait_recv()

    n_copy(0).wait_send()
    n_copy(0).wait_recv()

    @pl.when(c == 0)
    def _():
        n_copy(1).wait_send()

    @pl.when(c == 1)
    def _():
        n_copy(1).wait_recv()

    for slab in range(prompt_slabs):
        for index in range(PIECES):
            copy = c_copy(own_rows.at[part(index)], slab, index)
            copy.wait_send()
            copy.wait_recv()

            @pl.when((z < n_z - 1) & (slab <= z))
            def _():
                z_copy(own_rows.at[part(index)], slab, index, True).wait_send()

            @pl.when((z > 0) & (slab >= z))
            def _():
                z_copy(own_rows.at[part(index)], slab, index, False).wait_send()

    for copy in own:
        copy.wait()

    @pl.when(in_prompt)
    def _():
        own_far.wait()

    @pl.when(edge)
    def _():
        own_edge.wait()


def spread_keys(own_rows, prompt_rows, collective_id):
    lane, width = own_rows.shape
    slabs = prompt_rows // (2 * lane)
    dma = pltpu.SemaphoreType.DMA
    far, near, _ = pl.pallas_call(
        functools.partial(spread_kernel, slabs),
        out_shape=(
            jax.ShapeDtypeStruct((slabs, 2, lane, width), own_rows.dtype),
            jax.ShapeDtypeStruct((4, lane // 2, width), own_rows.dtype),
            jax.ShapeDtypeStruct((lane // 2, width), own_rows.dtype),
        ),
        in_specs=[VMEM],
        out_specs=(VMEM,) * 3,
        scratch_shapes=[
            dma((slabs, PIECES, 2)), dma((slabs, PIECES)), dma((slabs, PIECES)), dma((slabs, PIECES)),
            dma((4,)), dma((4,)), dma((4,)),
        ],
        compiler_params=pltpu.CompilerParams(collective_id=collective_id, has_side_effects=True),
    )(own_rows)
    return far.reshape(prompt_rows, width), near.reshape(2 * lane, width)


def collect_kernel(
    prompt_slabs, far, near, out, own, c_got, z_got, n_got, tail_pass, tail_got,
    c_send, c_recv, z_send, z_recv, n_send, n_recv,
):
    n_z = lax.axis_size("z")
    lane = out.shape[0]
    chunk = lane // 2
    size = lane // PIECES
    (z, x, c, y), _, _, c_near = around()
    above, below = (z + 1, x, c, y), (z - 1, x, c, y)

    barrier = pltpu.get_barrier_semaphore()
    pl.semaphore_signal(barrier, inc=1, device_id=c_near, device_id_type=MESH)

    @pl.when(z < n_z - 1)
    def _():
        pl.semaphore_signal(barrier, inc=1, device_id=above, device_id_type=MESH)

    pl.semaphore_wait(barrier, 1 + jnp.where(z > 0, 1, 0))

    def part(index):
        return pl.ds(index * size, size)

    def c_copy(slab, index):
        return remote(
            far.at[slab, 1 - c, part(index)], c_got.at[slab, part(index)], c_send.at[slab, index],
            c_recv.at[slab, index], c_near,
        )

    def z_copy(slab, index):
        return remote(
            own.at[slab, part(index)], z_got.at[slab, part(index)], z_send.at[slab, index],
            z_recv.at[slab, index], below,
        )

    def n_copy(half):
        slot = jnp.where(c == 0, 2, 2 * half)
        return remote(near.at[slot], n_got.at[half], n_send.at[half], n_recv.at[half], c_near)

    def t_hand():
        return remote(near.at[0], tail_pass, n_send.at[2], n_recv.at[2], c_near)

    def t_copy():
        return remote(tail_pass, tail_got, n_send.at[3], n_recv.at[3], below)

    for slab in range(prompt_slabs):
        for index in range(PIECES):
            c_copy(slab, index).start()
    n_copy(0).start()

    @pl.when(c == 1)
    def _():
        n_copy(1).start()

    @pl.when((c == 0) & (z > 0))
    def _():
        t_hand().start()

    for slab in range(prompt_slabs):
        for index in range(PIECES):
            c_copy(slab, index).wait_recv()
            rows = part(index)
            mine = total_of(far[slab, c, rows, :], c_got[slab, rows, :])

            @pl.when((z == n_z - 1) & (z > slab))
            def _():
                own[slab, rows, :] = mine.astype(jnp.bfloat16)
                z_copy(slab, index).start()

            @pl.when((z < n_z - 1) & (z > slab))
            def _():
                z_copy(slab, index).wait_recv()
                own[slab, rows, :] = total_of(mine, z_got[slab, rows, :]).astype(jnp.bfloat16)
                z_copy(slab, index).start()

            @pl.when((z < n_z - 1) & (z == slab))
            def _():
                z_copy(slab, index).wait_recv()
                out[rows, :] = total_of(mine, z_got[slab, rows, :])

            @pl.when((z == n_z - 1) & (z == slab))
            def _():
                out[rows, :] = mine

    @pl.when((c == 1) & (z > 0))
    def _():
        t_hand().wait_recv()
        t_copy().start()

    @pl.when(z >= prompt_slabs)
    def _():
        out[...] = jnp.zeros_like(out)

    n_copy(0).wait_recv()
    first, second = pl.ds(0, chunk), pl.ds(chunk, chunk)
    out[first, :] += total_of(near[1], n_got[0])
    out[second, :] += near[3].astype(jnp.float32)

    @pl.when(c == 0)
    def _():
        n_copy(1).wait_recv()
        out[second, :] += n_got[1].astype(jnp.float32)

    @pl.when((c == 1) & (z < n_z - 1))
    def _():
        t_copy().wait_recv()
        out[second, :] += tail_got[...].astype(jnp.float32)

    @pl.when((c == 1) & (z > 0))
    def _():
        t_copy().wait_send()

    @pl.when((c == 0) & (z > 0))
    def _():
        t_hand().wait_send()

    n_copy(0).wait_send()

    @pl.when(c == 1)
    def _():
        n_copy(1).wait_send()

    for slab in range(prompt_slabs):
        for index in range(PIECES):
            c_copy(slab, index).wait_send()

            @pl.when(z > slab)
            def _():
                z_copy(slab, index).wait_send()


def collect_keys(far, near, collective_id):
    prompt_rows, width = far.shape
    lane = near.shape[0] // 2
    slabs = prompt_rows // (2 * lane)
    dma = pltpu.SemaphoreType.DMA
    low = jnp.bfloat16
    return pl.pallas_call(
        functools.partial(collect_kernel, slabs),
        out_shape=jax.ShapeDtypeStruct((lane, width), jnp.float32),
        in_specs=[VMEM] * 2,
        out_specs=VMEM,
        scratch_shapes=[
            pltpu.VMEM((slabs, lane, width), low),
            pltpu.VMEM((slabs, lane, width), low),
            pltpu.VMEM((slabs, lane, width), low),
            pltpu.VMEM((2, lane // 2, width), low),
            pltpu.VMEM((lane // 2, width), low),
            pltpu.VMEM((lane // 2, width), low),
            dma((slabs, PIECES)), dma((slabs, PIECES)), dma((slabs, PIECES)), dma((slabs, PIECES)),
            dma((4,)), dma((4,)),
        ],
        compiler_params=pltpu.CompilerParams(
            collective_id=collective_id, has_side_effects=True, vmem_limit_bytes=20 * MIB
        ),
    )(far.astype(low).reshape(slabs, 2, lane, width), near.astype(low).reshape(4, lane // 2, width))


SQRT_HALF = 0.5**0.5
DENSITY = 0.3989422804014327


def matmul(left, right):
    return jnp.dot(left, right, preferred_element_type=jnp.float32)


def inner(left, right):
    return lax.dot_general(
        left, right, (((0,), (0,)), ((), ())), preferred_element_type=jnp.float32
    )


def outer(left, right):
    return lax.dot_general(
        left, right, (((1,), (1,)), ((), ())), preferred_element_type=jnp.float32
    )


def plane_gather(own_rows, blocks, send_sem, recv_sem):
    half = own_rows.shape[0] // 2
    (z, x, c, y), x_near, y_near, _ = around()
    low, high = pl.ds(0, half), pl.ds(half, half)

    def copy(slot, px, py, rows, source, device):
        target = blocks.at[px, py, rows]
        return remote(target if source is None else source.at[rows], target, send_sem.at[slot], recv_sem.at[slot], device)

    first = [
        copy(0, x, y, low, own_rows, x_near),
        copy(1, x, y, high, own_rows, y_near),
        copy(2, x, y, high, own_rows, x_near),
        copy(3, x, y, low, own_rows, y_near),
    ]
    relays = [copy(4, 1 - x, y, low, None, y_near), copy(5, x, 1 - y, high, None, x_near)]
    for each in first:
        each.start()

    def wait_near():
        first[0].wait_recv()
        relays[0].start()
        first[1].wait_recv()
        relays[1].start()

    def wait_x():
        first[2].wait_recv()

    def wait_y():
        first[3].wait_recv()

    def wait_diagonal():
        for each in relays:
            each.wait_recv()

    def close():
        for each in first + relays:
            each.wait_send()

    return wait_near, wait_x, wait_y, wait_diagonal, close


def plane_sum(parts, got, out, send_sem, recv_sem):
    (z, x, c, y), x_near, y_near, _ = around()
    diagonal = (z, 1 - x, c, 1 - y)
    copies = [
        remote(parts.at[device[1], device[3]], got.at[slot], send_sem.at[slot], recv_sem.at[slot], device)
        for slot, device in enumerate((x_near, y_near, diagonal))
    ]

    def close():
        for each in copies:
            each.wait_recv()
        out[...] = total_of(parts[x, y], got[0], got[1], got[2])
        for each in copies:
            each.wait_send()

    return copies, close


def experts_kernel(
    own_rows, route, up, down, out, wide, before, hidden, parts, got, g_send, g_recv, s_send, s_recv
):
    (z, x, c, y), x_near, y_near, _ = around()
    diagonal = (z, 1 - x, c, 1 - y)
    greet((x_near, y_near, diagonal))
    wait_near, wait_x, wait_y, wait_diagonal, close = plane_gather(own_rows, wide, g_send, g_recv)
    copies, finish = plane_sum(parts, got, out, s_send, s_recv)
    wide[x, y] = own_rows[...]

    def work(px, py):
        rows = wide[px, py]
        first = route[px, py] == 0
        value = jnp.where(first, matmul(rows, up[0]), matmul(rows, up[1]))
        before[px, py] = value
        active = 0.5 * value * (1.0 + lax.erf(value * SQRT_HALF))
        hidden_first = jnp.where(first, active, 0.0).astype(jnp.bfloat16)
        hidden_second = jnp.where(first, 0.0, active).astype(jnp.bfloat16)
        hidden[px, py] = active.astype(jnp.bfloat16)
        total = outer(hidden_first, down[0]) + outer(hidden_second, down[1])
        parts[px, py] = total.astype(jnp.bfloat16)

    work(x, y)
    wait_near()
    wait_x()
    work(1 - x, y)
    copies[0].start()
    wait_y()
    work(x, 1 - y)
    copies[1].start()
    wait_diagonal()
    work(1 - x, 1 - y)
    copies[2].start()
    finish()
    close()


def experts(own_rows, route, up, down, collective_id):
    _, n_x, _, n_y = sizes()
    own, width = own_rows.shape
    wide = up.shape[2]
    dma = pltpu.SemaphoreType.DMA
    low = jnp.bfloat16
    return pl.pallas_call(
        experts_kernel,
        out_shape=(
            jax.ShapeDtypeStruct((own, width), jnp.float32),
            jax.ShapeDtypeStruct((n_x, n_y, own, width), low),
            jax.ShapeDtypeStruct((n_x, n_y, own, wide), jnp.float32),
            jax.ShapeDtypeStruct((n_x, n_y, own, wide), low),
        ),
        in_specs=[VMEM] * 4,
        out_specs=(VMEM,) * 4,
        scratch_shapes=[
            pltpu.VMEM((n_x, n_y, own, width), low),
            pltpu.VMEM((3, own, width), low),
            dma((6,)), dma((6,)), dma((3,)), dma((3,)),
        ],
        compiler_params=pltpu.CompilerParams(
            collective_id=collective_id, has_side_effects=True, vmem_limit_bytes=20 * MIB
        ),
        cost_estimate=pl.CostEstimate(
            flops=8 * own * 4 * width * wide, bytes_accessed=8 * MIB, transcendentals=4 * own * wide
        ),
    )(own_rows, route, up, down)


def experts_back_kernel(
    own_rows, route, up, down, wide, before, hidden, out, grads,
    wide_grad, before_grad, parts, got, g_send, g_recv, s_send, s_recv,
):
    (z, x, c, y), x_near, y_near, _ = around()
    diagonal = (z, 1 - x, c, 1 - y)
    greet((x_near, y_near, diagonal))
    wait_near, wait_x, wait_y, wait_diagonal, close = plane_gather(own_rows, wide_grad, g_send, g_recv)
    copies, finish = plane_sum(parts, got, out, s_send, s_recv)
    wide_grad[x, y] = own_rows[...]

    def work(px, py):
        rows = wide_grad[px, py]
        first = route[px, py] == 0
        hidden_grad = jnp.where(first, matmul(rows, down[0]), matmul(rows, down[1]))
        value = before[px, py]
        slope = 0.5 * (1.0 + lax.erf(value * SQRT_HALF)) + value * (
            DENSITY * jnp.exp(-0.5 * value * value)
        )
        change = (hidden_grad * slope).astype(jnp.bfloat16)
        before_grad[px, py] = change
        change_first = jnp.where(first, change, 0)
        change_second = jnp.where(first, 0, change)
        total = outer(change_first, up[0]) + outer(change_second, up[1])
        parts[px, py] = total.astype(jnp.bfloat16)

    work(x, y)
    wait_near()
    wait_x()
    work(1 - x, y)
    copies[0].start()
    wait_y()
    work(x, 1 - y)
    copies[1].start()
    wait_diagonal()
    work(1 - x, 1 - y)
    copies[2].start()
    close()

    lane = 4 * own_rows.shape[0]
    rows = wide[...].reshape(lane, -1)
    grad_rows = wide_grad[...].reshape(lane, -1)
    first = route[...].reshape(lane, 1) == 0
    change = before_grad[...].reshape(lane, -1)
    active = hidden[...].reshape(lane, -1)
    low = jnp.bfloat16
    grads[0] = inner(rows, jnp.where(first, change, 0)).astype(low)
    grads[1] = inner(rows, jnp.where(first, 0, change)).astype(low)
    grads[2] = inner(grad_rows, jnp.where(first, active, 0)).astype(low)
    grads[3] = inner(grad_rows, jnp.where(first, 0, active)).astype(low)
    finish()


def experts_back(own_rows, route, up, down, wide, before, hidden, collective_id):
    _, n_x, _, n_y = sizes()
    own, width = own_rows.shape
    units = up.shape[2]
    dma = pltpu.SemaphoreType.DMA
    low = jnp.bfloat16
    return pl.pallas_call(
        experts_back_kernel,
        out_shape=(
            jax.ShapeDtypeStruct((own, width), jnp.float32),
            jax.ShapeDtypeStruct((4, width, units), low),
        ),
        in_specs=[VMEM] * 7,
        out_specs=(VMEM,) * 2,
        scratch_shapes=[
            pltpu.VMEM((n_x, n_y, own, width), low),
            pltpu.VMEM((n_x, n_y, own, units), low),
            pltpu.VMEM((n_x, n_y, own, width), low),
            pltpu.VMEM((3, own, width), low),
            dma((6,)), dma((6,)), dma((3,)), dma((3,)),
        ],
        compiler_params=pltpu.CompilerParams(
            collective_id=collective_id, has_side_effects=True, vmem_limit_bytes=28 * MIB
        ),
        cost_estimate=pl.CostEstimate(
            flops=16 * own * 4 * width * units, bytes_accessed=12 * MIB, transcendentals=8 * own * units
        ),
    )(own_rows, route, up, down, wide, before, hidden)


def project_kernel(transposed, rows, weight, out, parts, got, s_send, s_recv):
    (z, x, c, y), x_near, y_near, _ = around()
    diagonal = (z, 1 - x, c, 1 - y)
    barrier = pltpu.get_barrier_semaphore()
    for device in (x_near, y_near, diagonal):
        pl.semaphore_signal(barrier, inc=1, device_id=device, device_id_type=MESH)
    copies, finish = plane_sum(parts, got, out, s_send, s_recv)

    def work(px, py):
        times = outer if transposed else matmul
        parts[px, py] = times(rows[px, py], weight[...]).astype(jnp.bfloat16)

    work(1 - x, 1 - y)
    pl.semaphore_wait(barrier, 3)
    copies[2].start()
    work(1 - x, y)
    copies[0].start()
    work(x, 1 - y)
    copies[1].start()
    work(x, y)
    finish()


def project(rows, weight, transposed, collective_id):
    n_x, n_y, own, depth = rows.shape
    width = weight.shape[0] if transposed else weight.shape[1]
    low = jnp.bfloat16
    dma = pltpu.SemaphoreType.DMA
    return pl.pallas_call(
        functools.partial(project_kernel, transposed),
        out_shape=jax.ShapeDtypeStruct((own, width), jnp.float32),
        in_specs=[VMEM] * 2,
        out_specs=VMEM,
        scratch_shapes=[
            pltpu.VMEM((n_x, n_y, own, width), low), pltpu.VMEM((3, own, width), low), dma((3,)), dma((3,)),
        ],
        compiler_params=pltpu.CompilerParams(
            collective_id=collective_id, has_side_effects=True, vmem_limit_bytes=10 * MIB
        ),
        cost_estimate=pl.CostEstimate(
            flops=8 * own * width * depth, bytes_accessed=4 * MIB, transcendentals=0
        ),
    )(rows, weight)


def gather_project_kernel(transposed, own_rows, weight, wide, out, g_send, g_recv):
    (z, x, c, y), x_near, y_near, _ = around()
    greet((x_near, y_near))
    wait_near, wait_x, wait_y, wait_diagonal, close = plane_gather(own_rows, wide, g_send, g_recv)
    wide[x, y] = own_rows[...]

    def work(px, py):
        times = outer if transposed else matmul
        out[px, py] = times(wide[px, py], weight[...]).astype(jnp.bfloat16)

    work(x, y)
    wait_near()
    wait_x()
    work(1 - x, y)
    wait_y()
    work(x, 1 - y)
    wait_diagonal()
    work(1 - x, 1 - y)
    close()


def gather_project(own_rows, weight, transposed, collective_id):
    _, n_x, _, n_y = sizes()
    own, width = own_rows.shape
    depth = weight.shape[0] if transposed else weight.shape[1]
    dma = pltpu.SemaphoreType.DMA
    low = jnp.bfloat16
    return pl.pallas_call(
        functools.partial(gather_project_kernel, transposed),
        out_shape=(
            jax.ShapeDtypeStruct((n_x, n_y, own, width), low),
            jax.ShapeDtypeStruct((n_x, n_y, own, depth), low),
        ),
        in_specs=[VMEM] * 2,
        out_specs=(VMEM,) * 2,
        scratch_shapes=[dma((6,)), dma((6,))],
        compiler_params=pltpu.CompilerParams(
            collective_id=collective_id, has_side_effects=True, vmem_limit_bytes=12 * MIB
        ),
        cost_estimate=pl.CostEstimate(
            flops=8 * own * width * depth, bytes_accessed=4 * MIB, transcendentals=0
        ),
    )(own_rows, weight)


def merge_logs_kernel(source, out, got, mine, send_one, recv_one, send_two, recv_two):
    n_z, n_x, n_c, n_y = sizes()
    count = n_z * n_x * n_c * n_y
    z, x, c, y = place()
    me = ((z * n_x + x) * n_c + c) * n_y + y

    def device_of(index):
        return (
            index // (n_x * n_c * n_y), index // (n_c * n_y) % n_x, index // n_y % n_c, index % n_y
        )

    barrier = pltpu.get_barrier_semaphore()

    def call(step, unused):
        other = lax.rem(me + step, count)
        pl.semaphore_signal(barrier, inc=1, device_id=device_of(other), device_id_type=MESH)
        return unused

    lax.fori_loop(1, count, call, 0)
    got[me] = source[me]
    pl.semaphore_wait(barrier, count - 1)

    def first(step):
        other = lax.rem(me + step, count)
        return remote(
            source.at[other], got.at[me], send_one.at[step], recv_one.at[step], device_of(other)
        )

    def second(step):
        other = lax.rem(me + step, count)
        return remote(mine, out.at[me], send_two.at[step], recv_two.at[step], device_of(other))

    def each(action):
        def body(step, unused):
            action(step)
            return unused

        lax.fori_loop(1, count, body, 0)

    each(lambda step: first(step).start())
    each(lambda step: first(step).wait())
    values = got[...]
    peak = jnp.max(values, axis=0)
    mine[...] = peak + jnp.log(jnp.sum(jnp.exp(values - peak[None]), axis=0))
    out[me] = mine[...]
    each(lambda step: second(step).start())
    each(lambda step: second(step).wait())


def merge_logs(blocks, collective_id):
    count = blocks.shape[0]
    dma = pltpu.SemaphoreType.DMA
    return pl.pallas_call(
        merge_logs_kernel,
        out_shape=jax.ShapeDtypeStruct(blocks.shape, blocks.dtype),
        in_specs=[VMEM],
        out_specs=VMEM,
        scratch_shapes=[
            pltpu.VMEM(blocks.shape, blocks.dtype), pltpu.VMEM(blocks.shape[1:], blocks.dtype),
            dma((count,)), dma((count,)), dma((count,)), dma((count,)),
        ],
        compiler_params=pltpu.CompilerParams(collective_id=collective_id, has_side_effects=True),
    )(blocks)


def key_position(index, part, chunk):
    lane = 2 * chunk
    start = (part // 2) * (2 * lane) + (part % 2) * chunk
    return start + index + jnp.where(index >= chunk, chunk, 0)


def near_shown(side, chunk, query_pos, query_seg, near_pos, near_seg):
    columns = slice(side * chunk, (side + 1) * chunk)
    rows = slice(2 * side * chunk, 2 * (side + 1) * chunk)
    shown = (
        (near_seg[rows, :] == query_seg[:, columns])
        & (near_pos[rows, :] <= query_pos[:, columns])
        & (near_pos[rows, :] >= PROMPT)
    )
    return columns, rows, shown


def attend_kernel(
    chunk, query, far, near, query_pos, query_seg, near_pos, near_seg,
    out, out_low, log_total, scores, far_t, near_t,
):
    lane, feature = query.shape
    group = feature // HEAD_DIM
    prompt_rows = far.shape[0]
    parts = prompt_rows // lane
    query_t = (query[...].astype(jnp.float32) * HEAD_DIM ** (-0.5)).T.astype(jnp.bfloat16)
    far_t[...] = far[...].astype(jnp.float32).T.astype(jnp.bfloat16)
    near_t[...] = near[...].astype(jnp.float32).T.astype(jnp.bfloat16)
    row_of = lax.broadcasted_iota(jnp.int32, (feature, lane), 0)
    q_pos = query_pos[...]

    for head in range(group):
        low, high = head * HEAD_DIM, (head + 1) * HEAD_DIM
        query_h = jnp.where((row_of >= low) & (row_of < high), query_t, 0)

        def score_part(part, peak):
            block = far[pl.ds(pl.multiple_of(part * lane, lane), lane), :feature]
            value = matmul(block, query_h)
            index = lax.broadcasted_iota(jnp.int32, (lane, lane), 0)
            value = jnp.where(key_position(index, part, chunk) <= q_pos, value, MASKED)
            scores[pl.ds(pl.multiple_of(part * lane, lane), lane), :] = value
            return jnp.maximum(peak, jnp.max(value, axis=0, keepdims=True))

        peak = lax.fori_loop(0, parts, score_part, jnp.full((1, lane), MASKED, jnp.float32))
        near_peaks = []
        for side in range(2):
            columns, rows, shown = near_shown(side, chunk, query_pos, query_seg, near_pos, near_seg)
            value = matmul(near[rows, :feature], query_h[:, columns])
            value = jnp.where(shown, value, MASKED)
            scores[prompt_rows : prompt_rows + lane, columns] = value
            near_peaks.append(jnp.max(value, axis=0, keepdims=True))
        peak = jnp.maximum(peak, jnp.concatenate(near_peaks, axis=1))

        def weigh_part(part, state):
            total, mixed = state
            start = pl.multiple_of(part * lane, lane)
            chance = jnp.exp(scores[pl.ds(start, lane), :] - peak)
            total = total + jnp.sum(chance, axis=0, keepdims=True)
            mixed = mixed + matmul(
                far_t[feature + low : feature + high, pl.ds(start, lane)],
                chance.astype(jnp.bfloat16),
            )
            return total, mixed

        total, mixed = lax.fori_loop(
            0,
            parts,
            weigh_part,
            (jnp.zeros((1, lane), jnp.float32), jnp.zeros((HEAD_DIM, lane), jnp.float32)),
        )
        near_total, near_mixed = [], []
        for side in range(2):
            columns = slice(side * chunk, (side + 1) * chunk)
            rows = slice(side * lane, (side + 1) * lane)
            chance = jnp.exp(scores[prompt_rows : prompt_rows + lane, columns] - peak[:, columns])
            near_total.append(jnp.sum(chance, axis=0, keepdims=True))
            near_mixed.append(
                matmul(near_t[feature + low : feature + high, rows], chance.astype(jnp.bfloat16))
            )
        total = total + jnp.concatenate(near_total, axis=1)
        mixed = mixed + jnp.concatenate(near_mixed, axis=1)
        out[low:high, :] = mixed / total
        log_total[head : head + 1, :] = peak + jnp.log(total)
    out_low[...] = out[...].T.astype(jnp.bfloat16)


def attend(queries, far, near, places, chunk):
    lane, feature = queries.shape
    prompt_rows = far.shape[0]
    group = feature // HEAD_DIM
    total_rows = prompt_rows + lane
    return pl.pallas_call(
        functools.partial(attend_kernel, chunk),
        out_shape=(
            jax.ShapeDtypeStruct((feature, lane), jnp.float32),
            jax.ShapeDtypeStruct((lane, feature), jnp.bfloat16),
            jax.ShapeDtypeStruct((group, lane), jnp.float32),
        ),
        in_specs=[VMEM] * 7,
        out_specs=(VMEM,) * 3,
        scratch_shapes=[
            pltpu.VMEM((total_rows, lane), jnp.float32),
            pltpu.VMEM((2 * feature, prompt_rows), jnp.bfloat16),
            pltpu.VMEM((2 * feature, 2 * lane), jnp.bfloat16),
        ],
        compiler_params=pltpu.CompilerParams(vmem_limit_bytes=20 * MIB),
        cost_estimate=pl.CostEstimate(
            flops=8 * group * lane * total_rows * 128,
            bytes_accessed=8 * MIB,
            transcendentals=group * lane * total_rows,
        ),
    )(queries, far, near, *places)


def attend_back_kernel(
    chunk, query, far, near, query_pos, query_seg, near_pos, near_seg,
    log_total, mixed, answer, query_grad, far_grad, near_grad,
    far_t, near_t, far_values, near_values, far_sum, near_sum, query_sum,
):
    lane, feature = query.shape
    group = feature // HEAD_DIM
    prompt_rows = far.shape[0]
    parts = prompt_rows // lane
    scaled = (query[...].astype(jnp.float32) * HEAD_DIM ** (-0.5)).astype(jnp.bfloat16)
    query_t = scaled.astype(jnp.float32).T.astype(jnp.bfloat16)
    answers = answer[...]
    answer_t = answers.astype(jnp.float32).T.astype(jnp.bfloat16)
    far_t[...] = far[:, :feature].astype(jnp.float32).T.astype(jnp.bfloat16)
    near_t[...] = near[:, :feature].astype(jnp.float32).T.astype(jnp.bfloat16)
    far_values[...] = far[:, feature:]
    near_values[...] = near[:, feature:]
    row_of = lax.broadcasted_iota(jnp.int32, (feature, lane), 0)
    column_of = lax.broadcasted_iota(jnp.int32, (lane, feature), 1)
    q_pos = query_pos[...]

    for head in range(group):
        low, high = head * HEAD_DIM, (head + 1) * HEAD_DIM
        in_rows = (row_of >= low) & (row_of < high)
        in_columns = (column_of >= low) & (column_of < high)
        query_ht = jnp.where(in_rows, query_t, 0)
        answer_ht = jnp.where(in_rows, answer_t, 0)
        query_h = jnp.where(in_columns, scaled, 0)
        answer_h = jnp.where(in_columns, answers, 0)
        log_h = log_total[head : head + 1, :]
        delta_h = jnp.sum(
            answer_t[low:high, :].astype(jnp.float32) * mixed[low:high, :], axis=0, keepdims=True
        )

        def slopes(key_block, value_block, shown, columns):
            value = matmul(key_block, query_ht[:, columns])
            chance = jnp.exp(jnp.where(shown, value - log_h[:, columns], MASKED))
            slope = matmul(value_block, answer_ht[:, columns])
            change = (chance * (slope - delta_h[:, columns])).astype(jnp.bfloat16)
            chance = chance.astype(jnp.bfloat16)
            return change, matmul(change, query_h[columns]), matmul(chance, answer_h[columns])

        def add(sums, rows, key_part, value_part):
            if head == 0:
                sums[0, rows, :] = key_part
                sums[1, rows, :] = value_part
            else:
                sums[0, rows, :] += key_part
                sums[1, rows, :] += value_part

        def back_part(part, total):
            rows = pl.ds(pl.multiple_of(part * lane, lane), lane)
            index = lax.broadcasted_iota(jnp.int32, (lane, lane), 0)
            shown = key_position(index, part, chunk) <= q_pos
            change, key_part, value_part = slopes(
                far[rows, :feature], far_values[rows, :], shown, slice(0, lane)
            )
            add(far_sum, rows, key_part, value_part)
            return total + matmul(far_t[low:high, rows], change)

        total = lax.fori_loop(0, parts, back_part, jnp.zeros((HEAD_DIM, lane), jnp.float32))
        near_total = []
        for side in range(2):
            columns, rows, shown = near_shown(side, chunk, query_pos, query_seg, near_pos, near_seg)
            change, key_part, value_part = slopes(
                near[rows, :feature], near_values[rows, :], shown, columns
            )
            add(near_sum, rows, key_part, value_part)
            near_total.append(matmul(near_t[low:high, rows], change))
        query_sum[low:high, :] = (total + jnp.concatenate(near_total, axis=1)) * HEAD_DIM ** (-0.5)
    query_grad[...] = query_sum[...].T.astype(jnp.bfloat16)
    for sums, grad in ((far_sum, far_grad), (near_sum, near_grad)):
        grad[...] = jnp.concatenate(
            [sums[0].astype(jnp.bfloat16), sums[1].astype(jnp.bfloat16)], axis=1
        )


def attend_back(queries, far, near, places, log_total, mixed, answer, chunk):
    lane, feature = queries.shape
    prompt_rows = far.shape[0]
    group = feature // HEAD_DIM
    total_rows = prompt_rows + lane
    low = jnp.bfloat16
    return pl.pallas_call(
        functools.partial(attend_back_kernel, chunk),
        out_shape=(
            jax.ShapeDtypeStruct((lane, feature), low),
            jax.ShapeDtypeStruct((prompt_rows, 2 * feature), low),
            jax.ShapeDtypeStruct((2 * lane, 2 * feature), low),
        ),
        in_specs=[VMEM] * 10,
        out_specs=(VMEM,) * 3,
        scratch_shapes=[
            pltpu.VMEM((feature, prompt_rows), low),
            pltpu.VMEM((feature, 2 * lane), low),
            pltpu.VMEM((prompt_rows, feature), low),
            pltpu.VMEM((2 * lane, feature), low),
            pltpu.VMEM((2, prompt_rows, feature), jnp.float32),
            pltpu.VMEM((2, 2 * lane, feature), jnp.float32),
            pltpu.VMEM((feature, lane), jnp.float32),
        ],
        compiler_params=pltpu.CompilerParams(vmem_limit_bytes=28 * MIB),
        cost_estimate=pl.CostEstimate(
            flops=20 * group * lane * total_rows * 128,
            bytes_accessed=12 * MIB,
            transcendentals=group * lane * total_rows,
        ),
    )(queries, far, near, *places, log_total, mixed, answer)


def head_places(back):
    n_z, n_x, n_c, n_y = sizes()
    line = n_z * n_c
    pairs = []
    for device in range(line * n_x * n_y):
        group, at = device // line, device % line
        place_of = ((at // n_c * n_x + group // n_y) * n_c + at % n_c) * n_y + group % n_y
        pairs.append((place_of, device) if back else (device, place_of))
    return tuple(pairs)


def pad_rows(block):
    return jnp.pad(block, ((0, 8 - block.shape[0]), (0, 0)))


def adam_update(weight, moment_one, moment_two, gradient, step_rate, decay_rate):
    first_new = BETA_ONE * moment_one + (1.0 - BETA_ONE) * gradient
    second_new = BETA_TWO * moment_two + (1.0 - BETA_TWO) * gradient * gradient
    normalized = (
        first_new
        / (1.0 - BETA_ONE**STEP)
        / (jnp.sqrt(second_new / (1.0 - BETA_TWO**STEP)) + ADAM_EPS)
    )
    return (weight - step_rate * (normalized + decay_rate * weight), first_new, second_new)


def per_device(
    token_ids,
    targets,
    valid_mask,
    cont_lengths,
    routes,
    vocab_table,
    vocab_first,
    vocab_second,
    attn_weights,
    attn_first,
    attn_second,
    router,
    router_first,
    router_second,
    norm_gains,
    gains_first,
    gains_second,
    expert_up,
    up_first,
    up_second,
    expert_down,
    down_first,
    down_second,
):
    slabs = lax.axis_size("z")
    planes = lax.axis_size("x")
    cores = lax.axis_size("core")
    sides = lax.axis_size("head")
    groups = planes * sides
    z_at, x_at, core_at, side_at = (lax.axis_index(name) for name in ALL)
    blk_at = (z_at * planes + x_at) * cores + core_at
    device_at = blk_at * sides + side_at
    group_at = x_at * sides + side_at
    tokens = valid_mask.shape[0]
    chunk = token_ids.shape[0]
    own = chunk // sides
    lane = planes * chunk
    feature = D // groups
    wide = expert_up.shape[3] // planes
    shard_rows = vocab_table.shape[0]
    logit_scale = D ** (-0.5)

    cont_ends = jnp.cumsum(cont_lengths)
    valid_f = valid_mask.astype(jnp.float32)
    token_count = jnp.sum(valid_mask).astype(jnp.float32)
    expert_ids = jnp.arange(EXPERTS, dtype=jnp.int32)

    own_ints = jnp.concatenate([token_ids[None], targets[None], routes], axis=0)
    own_ints = lax.dynamic_slice_in_dim(own_ints, side_at * own, own, axis=1).astype(jnp.float32)
    rows_of = attn_weights.shape[1]
    smalls = jnp.concatenate(
        [router.transpose(0, 2, 1).reshape(LAYERS * EXPERTS, rows_of), norm_gains], axis=0
    )
    smalls = smalls.astype(jnp.bfloat16).astype(jnp.float32)
    smalls = jnp.pad(smalls, ((0, 16 - smalls.shape[0]), (0, own - rows_of)))
    whole_f = swap(jnp.concatenate([pad_rows(own_ints), smalls], axis=0)[None], True, 1)
    whole = whole_f[:, : 2 + LAYERS].astype(jnp.int32)
    smalls = whole_f[:, 8:, :rows_of].transpose(1, 0, 2).reshape(16, D)
    router_all = smalls[: LAYERS * EXPERTS].reshape(LAYERS, EXPERTS, D).transpose(0, 2, 1)
    router_all = router_all.astype(jnp.bfloat16)
    gains_f = smalls[LAYERS * EXPERTS :]
    ids_all = whole[:, 0].reshape(tokens)
    targets_all = whole[:, 1].reshape(tokens)
    routes_lane = lax.dynamic_index_in_dim(
        whole.reshape(slabs, planes, cores, sides, 2 + LAYERS, own), z_at, 0, False
    )
    routes_lane = lax.dynamic_index_in_dim(routes_lane, core_at, 1, False)[:, :, 2:]
    routes_lane = routes_lane.transpose(2, 0, 1, 3)[..., None]
    routes_own = lax.dynamic_slice_in_dim(routes, side_at * own, own, axis=1)

    table = vocab_table.astype(jnp.bfloat16)
    attn_low = attn_weights.astype(jnp.bfloat16)
    qkv_send = attn_low[:, :, : 3 * D].reshape(LAYERS, rows_of, 3, groups, feature)
    qkv_send = jnp.concatenate([qkv_send[:, :, 1:], qkv_send[:, :, :1]], axis=2)
    qkv_send = qkv_send.transpose(3, 0, 1, 2, 4).reshape(groups, LAYERS, rows_of, 3 * feature)
    qkv_got = lax.all_to_all(qkv_send, PLANE, split_axis=0, concat_axis=0, tiled=True)
    out_rows = attn_low[:, :, 3 * D :]
    out_rows = lax.ppermute(out_rows, ALL, head_places(False))
    out_rows = out_rows.reshape(LAYERS, rows_of, groups, feature).transpose(2, 0, 1, 3)
    attn_pack = jnp.concatenate([qkv_got, out_rows], axis=3)
    attn_pack = lax.all_gather(attn_pack, LINE, axis=0)
    qkv_weights, out_weights = [], []
    for layer_index in range(LAYERS):
        block = attn_pack[:, :, layer_index]
        part = block[..., : 3 * feature].reshape(slabs, cores, planes, sides, rows_of, 3 * feature)
        qkv_weights.append(part.transpose(0, 2, 1, 3, 4, 5).reshape(D, 3 * feature))
        part = block[..., 3 * feature :]
        out_weights.append(part.transpose(0, 2, 1, 3).reshape(feature, D))
    expert_send = jnp.stack([expert_up, expert_down], axis=1).astype(jnp.bfloat16)
    depth = expert_send.shape[3]
    expert_send = expert_send.reshape(LAYERS, 2 * EXPERTS, depth, planes, wide)
    expert_send = expert_send.transpose(3, 0, 1, 2, 4)
    expert_weights = []
    for layer_index in range(LAYERS):
        kept_half = lax.dynamic_index_in_dim(expert_send[:, layer_index], x_at, 0, False)
        sent_half = lax.dynamic_index_in_dim(expert_send[:, layer_index], 1 - x_at, 0, False)
        got_half = lax.ppermute(sent_half, "x", ((0, 1), (1, 0)))
        halves = jnp.stack(
            [jnp.where(x_at == 0, kept_half, got_half), jnp.where(x_at == 0, got_half, kept_half)]
        )
        block = lax.all_gather(halves, LINE, axis=0)
        block = block.reshape(slabs, cores, planes, 2, EXPERTS, depth, wide)
        block = block.transpose(3, 4, 0, 2, 1, 5, 6).reshape(2, EXPERTS, D, wide)
        expert_weights.append(block)

    offsets = jnp.arange(chunk, dtype=jnp.int32)
    first_blk = z_at * planes * cores + core_at
    query_pos = jnp.concatenate([(first_blk + cores * part) * chunk + offsets for part in range(planes)])
    near_blks = [first_blk - 1 + part for part in range(2 * planes)]
    near_pos = jnp.concatenate([blk * chunk + offsets for blk in near_blks])
    query_seg = segment_of(query_pos, cont_ends)
    near_seg = segment_of(near_pos, cont_ends)
    places = (query_pos[None, :], query_seg[None, :], near_pos[:, None], near_seg[:, None])

    vocab_ids = device_at * shard_rows + jnp.arange(shard_rows, dtype=jnp.int32)
    token_hot = (ids_all[:, None] == vocab_ids[None, :]).astype(jnp.bfloat16)
    stream = scatter_all(matmul(token_hot, table), 2)

    kept = []
    for layer_index in range(LAYERS):
        up, down = expert_weights[layer_index][0], expert_weights[layer_index][1]
        normed_lane, qkv = gather_project(
            rms_norm(stream, gains_f[2 * layer_index]).astype(jnp.bfloat16),
            qkv_weights[layer_index], False, 3,
        )
        qkv = qkv.reshape(lane, 3 * feature)
        queries = qkv[:, 2 * feature :]
        far, near = spread_keys(qkv[:, : 2 * feature], PROMPT, 10)
        mixed_t, mixed_low, log_total = attend(queries, far, near, places, chunk)
        middle = stream + project(
            mixed_low.reshape(planes, sides, own, feature), out_weights[layer_index], False, 15
        )
        normed_two = rms_norm(middle, gains_f[2 * layer_index + 1]).astype(jnp.bfloat16)
        chance = jax.nn.softmax(matmul(normed_two, router_all[layer_index]), axis=-1)
        output, wide_rows, before, hidden = experts(
            normed_two, routes_lane[layer_index], up, down, 11
        )
        own_pick = (routes_own[layer_index][:, None] == expert_ids[None, :]).astype(jnp.float32)
        gate = jnp.sum(chance * own_pick, axis=1, keepdims=True)
        kept.append(
            (
                stream, normed_lane, queries, far, near, mixed_t, mixed_low, log_total, middle,
                normed_two, chance, wide_rows, before, hidden, output, own_pick, gate,
            )
        )
        stream = middle + gate * output

    final_gain = gains_f[2 * LAYERS]
    final_all = gather_all(rms_norm(stream, final_gain).astype(jnp.bfloat16), 4)
    logits = outer(final_all, table) * logit_scale
    row_max = jnp.max(logits, axis=1, keepdims=True)
    row_log = row_max[:, 0] + jnp.log(jnp.sum(jnp.exp(logits - row_max), axis=1))
    target_hot = targets_all[:, None] == vocab_ids[None, :]
    hit_loss = jnp.sum(jnp.where(target_hot, logits, 0.0) * valid_f[:, None])
    devices = tokens // own
    row_logs = jnp.broadcast_to(row_log.reshape(devices, 1, own), (devices, 8, own))
    log_sum = merge_logs(row_logs, 5)[:, 0].reshape(tokens)
    own_log = lax.dynamic_slice_in_dim(log_sum, device_at * own, own)
    own_valid = lax.dynamic_slice_in_dim(valid_f, device_at * own, own)
    own_loss = jnp.sum(own_log * own_valid) - hit_loss
    logit_grad = (
        (jnp.exp(logits - log_sum[:, None]) - target_hot.astype(jnp.float32))
        * (valid_f / token_count)[:, None]
    ).astype(jnp.bfloat16)
    final_grad = scatter_all(matmul(logit_grad, table) * logit_scale, 2)
    table_grad = inner(logit_grad, final_all) * logit_scale
    stream_grad, final_gain_grad = jax.vjp(rms_norm, stream, final_gain)[1](final_grad)

    attn_packs = [None] * LAYERS
    router_list = [None] * LAYERS
    expert_shares = [None] * LAYERS
    gain_list = [None] * (2 * LAYERS + 1)
    gain_list[2 * LAYERS] = final_gain_grad
    for layer_index in reversed(range(LAYERS)):
        (
            stream, normed_lane, queries, far, near, mixed_t, mixed_low, log_total, middle,
            normed_two, chance, wide_rows, before, hidden, output, own_pick, gate,
        ) = kept[layer_index]
        up, down = expert_weights[layer_index][0], expert_weights[layer_index][1]
        out_grad = (gate * stream_grad).astype(jnp.bfloat16)
        chance_grad = jnp.sum(stream_grad * output, axis=1)[:, None] * own_pick
        choice_grad = chance * (chance_grad - jnp.sum(chance * chance_grad, axis=1, keepdims=True))
        router_list[layer_index] = jnp.dot(
            normed_two.astype(jnp.float32).T, choice_grad, precision=lax.Precision.HIGHEST
        )
        normed_grad = jnp.dot(
            choice_grad,
            router_all[layer_index].astype(jnp.float32).T,
            precision=lax.Precision.HIGHEST,
        )
        rows_grad, expert_grad = experts_back(
            out_grad, routes_lane[layer_index], up, down, wide_rows, before, hidden, 12
        )
        normed_grad = normed_grad + rows_grad
        expert_grad = expert_grad.reshape(2 * EXPERTS, slabs, planes, cores, depth, wide)
        expert_grad = expert_grad.transpose(1, 3, 2, 0, 4, 5).reshape(
            slabs * cores, planes, 2 * EXPERTS, depth, wide
        )
        expert_grad = lax.psum_scatter(expert_grad, LINE, scatter_dimension=0, tiled=True)[0]
        kept_half = lax.dynamic_index_in_dim(expert_grad, x_at, 0, False)
        sent_half = lax.dynamic_index_in_dim(expert_grad, 1 - x_at, 0, False)
        got_half = lax.ppermute(sent_half, "x", ((0, 1), (1, 0)))
        expert_grad = jnp.concatenate(
            [jnp.where(x_at == 0, kept_half, got_half), jnp.where(x_at == 0, got_half, kept_half)],
            axis=-1,
        )
        expert_shares[layer_index] = expert_grad.reshape(
            2, EXPERTS, depth, planes * wide
        ).astype(jnp.float32)
        middle_part, gain_list[2 * layer_index + 1] = jax.vjp(
            rms_norm, middle, gains_f[2 * layer_index + 1]
        )[1](normed_grad)
        middle_grad = stream_grad + middle_part
        branch_lane, answer = gather_project(
            middle_grad.astype(jnp.bfloat16), out_weights[layer_index], True, 16
        )
        answer = answer.reshape(lane, feature)
        out_proj = inner(mixed_low, branch_lane.reshape(lane, D)).astype(jnp.bfloat16)
        query_grad, far_grad, near_grad = attend_back(
            queries, far, near, places, log_total, mixed_t, answer, chunk
        )
        key_grad = collect_keys(far_grad, near_grad, 13).astype(jnp.bfloat16)
        qkv_grad = jnp.concatenate([key_grad, query_grad], axis=1)
        qkv_proj = inner(normed_lane.reshape(lane, D), qkv_grad).astype(jnp.bfloat16)
        qkv_proj = qkv_proj.reshape(slabs, planes, cores, sides, rows_of, 3 * feature)
        qkv_proj = qkv_proj.transpose(0, 2, 1, 3, 4, 5).reshape(
            slabs * cores, groups, rows_of, 3 * feature
        )
        out_proj = out_proj.reshape(slabs * cores, rows_of, groups, feature).transpose(0, 2, 1, 3)
        attn_pack = jnp.concatenate([qkv_proj, out_proj], axis=3)
        attn_packs[layer_index] = lax.psum_scatter(
            attn_pack, LINE, scatter_dimension=0, tiled=True
        )[0]
        normed_att_grad = project(
            qkv_grad.reshape(planes, sides, own, 3 * feature), qkv_weights[layer_index], True, 14
        )
        stream_part, gain_list[2 * layer_index] = jax.vjp(
            rms_norm, stream, gains_f[2 * layer_index]
        )[1](normed_att_grad)
        stream_grad = middle_grad + stream_part

    embed_grad = gather_all(stream_grad.astype(jnp.bfloat16), 4)
    table_share = table_grad + inner(token_hot, embed_grad)
    small = jnp.concatenate(
        [jnp.stack(router_list).transpose(1, 0, 2).reshape(D, -1), jnp.stack(gain_list).T], axis=1
    )
    small = small.reshape(devices, rows_of, -1).transpose(0, 2, 1)
    small = jnp.pad(small, ((0, 0), (0, 16 - small.shape[1]), (0, 128 - rows_of)))
    small = jnp.sum(swap(small, False, 7), axis=0)[:, :rows_of]
    router_share = (
        small[: LAYERS * EXPERTS].reshape(LAYERS, EXPERTS, rows_of).transpose(0, 2, 1)
    )
    gain_share = small[LAYERS * EXPERTS : LAYERS * EXPERTS + 2 * LAYERS + 1]
    attn_pack = jnp.stack(attn_packs, axis=1)
    qkv_share = lax.all_to_all(
        attn_pack[..., : 3 * feature], PLANE, split_axis=0, concat_axis=0, tiled=True
    )
    qkv_share = qkv_share.reshape(groups, LAYERS, rows_of, 3, feature)
    qkv_share = jnp.concatenate([qkv_share[:, :, :, 2:], qkv_share[:, :, :, :2]], axis=3)
    qkv_share = qkv_share.transpose(1, 2, 3, 0, 4).reshape(LAYERS, rows_of, 3 * D)
    out_share = attn_pack[..., 3 * feature :].transpose(1, 2, 0, 3).reshape(LAYERS, rows_of, D)
    out_share = lax.ppermute(out_share, ALL, head_places(True))
    attn_share = jnp.concatenate([qkv_share, out_share], axis=2).astype(jnp.float32)
    up_share = jnp.stack([share[0] for share in expert_shares])
    down_share = jnp.stack([share[1] for share in expert_shares])
    shares = (table_share, attn_share, router_share, gain_share, up_share, down_share)
    squares = jnp.sum(table_share * table_share)
    for share_part in shares[1:]:
        squares = squares + jnp.sum(share_part * share_part)
    sums = jnp.pad(jnp.stack([squares, own_loss])[:, None], ((0, 6), (0, 127)))
    sums = jnp.sum(swap(sums[None], True, 9)[:, :2, 0], axis=0)
    square_total, loss_sum = sums[0], sums[1]
    grad_norm = jnp.sqrt(square_total)
    factor = CLIP_AT / jnp.maximum(grad_norm, CLIP_AT)
    weights = (vocab_table, attn_weights, router, norm_gains, expert_up, expert_down)
    firsts = (vocab_first, attn_first, router_first, gains_first, up_first, down_first)
    seconds = (vocab_second, attn_second, router_second, gains_second, up_second, down_second)
    results = [loss_sum, token_count, grad_norm]
    for number in range(6):
        results.extend(
            adam_update(
                weights[number],
                firsts[number],
                seconds[number],
                factor * shares[number],
                STEP_RATES[number],
                DECAY_RATES[number],
            )
        )
    return tuple(results)


def solution(mesh):
    blocks, sides = mesh.shape["blk"], mesh.shape["head"]
    fine = Mesh(mesh.devices.reshape(blocks // 4, 2, 2, sides), ALL)
    weight_specs = (
        (P(ALL, None),) * 3
        + (P(None, ALL, None),) * 3
        + (P(None, ALL, None),) * 3
        + (P(None, ALL),) * 3
        + (P(None, None, BLK, "head"),) * 6
    )
    return jax.shard_map(
        per_device,
        mesh=fine,
        in_specs=(P(BLK), P(BLK), P(), P(), P(None, BLK)) + weight_specs,
        out_specs=(P(), P(), P()) + weight_specs,
        check_vma=False,
    )
```

```python
import functools

import jax
import jax.numpy as jnp
from jax import lax
from jax.experimental import pallas as pl
from jax.experimental.pallas import tpu as pltpu
from jax.sharding import Mesh, PartitionSpec as P

D = 768
HEADS = 12
HEAD_DIM = 64
EXPERTS = 2
LAYERS = 2
PROMPT = 2048
STEP = 10

NORM_EPS = 1e-06
BETA_ONE = 0.9
BETA_TWO = 0.95
ADAM_EPS = 1e-08
CLIP_AT = 0.01
MASKED = -1e30
STEP_RATES = (2.0, 0.25, 0.04, 0.4, 0.04, 0.04)
DECAY_RATES = (0.01, 0.01, 0.01, 0.0, 0.01, 0.01)

ALL = ("z", "x", "core", "head")
BLK = ("z", "x", "core")
PLANE = ("x", "head")
LINE = ("z", "core")
MIB = 2**20
MESH = pl.DeviceIdType.MESH
ANY = pl.BlockSpec(memory_space=pl.ANY)
VMEM = pl.BlockSpec(memory_space=pltpu.VMEM)


def rms_norm(stream, gain):
    return stream * lax.rsqrt(jnp.mean(stream * stream, axis=-1, keepdims=True) + NORM_EPS) * gain


def segment_of(position, cont_ends):
    later = jnp.sum((cont_ends[None, :] <= (position - PROMPT)[:, None]).astype(jnp.int32), axis=1)
    return jnp.where(position < PROMPT, 0, 1 + later)


def place():
    return tuple(lax.axis_index(name) for name in ALL)


def sizes():
    return tuple(lax.axis_size(name) for name in ALL)


def remote(source, target, send, receive, device):
    return pltpu.make_async_remote_copy(
        src_ref=source, dst_ref=target, send_sem=send, recv_sem=receive,
        device_id=device, device_id_type=MESH,
    )


def greet(devices):
    barrier = pltpu.get_barrier_semaphore()
    for device in devices:
        pl.semaphore_signal(barrier, inc=1, device_id=device, device_id_type=MESH)
    pl.semaphore_wait(barrier, len(devices))


def around():
    z, x, c, y = place()
    return (z, x, c, y), (z, 1 - x, c, y), (z, x, c, 1 - y), (z, x, 1 - c, y)


def swap_kernel(broadcast, source, out, send_sem, receive_sem, own_sem):
    n_z, n_x, n_c, n_y = sizes()
    count = n_z * n_x * n_c * n_y
    z, x, c, y = place()
    me = ((z * n_x + x) * n_c + c) * n_y + y

    def device_of(index):
        return (
            index // (n_x * n_c * n_y), index // (n_c * n_y) % n_x, index // n_y % n_c, index % n_y
        )

    def taken(index):
        return source.at[0] if broadcast else source.at[index]

    barrier = pltpu.get_barrier_semaphore()

    def call(step, unused):
        other = lax.rem(me + step, count)
        pl.semaphore_signal(barrier, inc=1, device_id=device_of(other), device_id_type=MESH)
        return unused

    lax.fori_loop(1, count, call, 0)
    own = pltpu.make_async_copy(taken(me), out.at[me], own_sem)
    own.start()
    pl.semaphore_wait(barrier, count - 1)

    def copy(step):
        other = lax.rem(me + step, count)
        return remote(
            taken(other), out.at[me], send_sem.at[step], receive_sem.at[step], device_of(other)
        )

    def start(step, unused):
        copy(step).start()
        return unused

    def finish(step, unused):
        copy(step).wait()
        return unused

    lax.fori_loop(1, count, start, 0)
    lax.fori_loop(1, count, finish, 0)
    own.wait()


def swap(blocks, broadcast, collective_id):
    count = 1
    for size in sizes():
        count *= size
    return pl.pallas_call(
        functools.partial(swap_kernel, broadcast),
        out_shape=jax.ShapeDtypeStruct((count,) + blocks.shape[1:], blocks.dtype),
        in_specs=[VMEM],
        out_specs=VMEM,
        scratch_shapes=[
            pltpu.SemaphoreType.DMA((count,)),
            pltpu.SemaphoreType.DMA((count,)),
            pltpu.SemaphoreType.DMA,
        ],
        compiler_params=pltpu.CompilerParams(collective_id=collective_id, has_side_effects=True),
    )(blocks)


def total_of(*parts):
    total = parts[0].astype(jnp.float32)
    for part in parts[1:]:
        total = total + part.astype(jnp.float32)
    return total


PIECES = 4


def spread_kernel(
    prompt_slabs, own_rows, far, near, tail, z_send, z_recv, c_send, c_recv, n_send, n_recv, own_sem
):
    n_z = lax.axis_size("z")
    lane = own_rows.shape[0]
    chunk = lane // 2
    size = lane // PIECES
    (z, x, c, y), _, _, c_near = around()
    above, below = (z + 1, x, c, y), (z - 1, x, c, y)
    in_prompt = z < prompt_slabs
    takes_down = z < prompt_slabs - 1
    gives_down = (z > 0) & (z < prompt_slabs)

    barrier = pltpu.get_barrier_semaphore()
    pl.semaphore_signal(barrier, inc=1, device_id=c_near, device_id_type=MESH)

    @pl.when(z > 0)
    def _():
        pl.semaphore_signal(barrier, inc=1, device_id=below, device_id_type=MESH)

    @pl.when(takes_down)
    def _():
        pl.semaphore_signal(barrier, inc=1, device_id=above, device_id_type=MESH)

    first, second = pl.ds(0, chunk), pl.ds(chunk, chunk)
    own = [
        pltpu.make_async_copy(own_rows.at[first], near.at[1], own_sem.at[0]),
        pltpu.make_async_copy(own_rows.at[second], near.at[3], own_sem.at[1]),
    ]
    own_far = pltpu.make_async_copy(own_rows, far.at[jnp.minimum(z, prompt_slabs - 1), c], own_sem.at[2])
    own_edge = pltpu.make_async_copy(own_rows.at[first], near.at[0], own_sem.at[3])
    edge = (z == 0) & (c == 0)
    for copy in own:
        copy.start()

    @pl.when(in_prompt)
    def _():
        own_far.start()

    @pl.when(edge)
    def _():
        own_edge.start()

    pl.semaphore_wait(
        barrier, 1 + jnp.where(z < n_z - 1, 1, 0) + jnp.where(gives_down, 1, 0)
    )

    def part(index):
        return pl.ds(index * size, size)

    def z_copy(source, slab, index, up):
        return remote(
            source, far.at[slab, c, part(index)], z_send.at[slab, index, 1 if up else 0],
            z_recv.at[slab, index], above if up else below,
        )

    def c_copy(source, slab, index):
        return remote(
            source, far.at[slab, c, part(index)], c_send.at[slab, index], c_recv.at[slab, index], c_near
        )

    def t_copy():
        return remote(own_rows.at[second], tail, n_send.at[0], n_recv.at[0], above)

    def t_hand():
        return remote(tail, near.at[0], n_send.at[1], n_recv.at[1], c_near)

    def n_copy(half):
        slot = jnp.where(c == 0, 2 * half, 2)
        return remote(
            own_rows.at[pl.ds(half * chunk, chunk)], near.at[slot], n_send.at[2 + half], n_recv.at[2 + half],
            c_near,
        )

    @pl.when(in_prompt)
    def _():
        for index in range(PIECES):
            source = own_rows.at[part(index)]

            @pl.when(z < n_z - 1)
            def _():
                z_copy(source, z, index, True).start()

            @pl.when(z > 0)
            def _():
                z_copy(source, z, index, False).start()

            c_copy(source, z, index).start()

    @pl.when((c == 1) & (z < n_z - 1))
    def _():
        t_copy().start()

    n_copy(0).start()

    @pl.when(c == 0)
    def _():
        n_copy(1).start()

    for distance in range(1, n_z):
        low_slab, high_slab = z - distance, z + distance
        for index in range(PIECES):

            @pl.when((low_slab >= 0) & (low_slab < prompt_slabs))
            def _():
                source = far.at[low_slab, c, part(index)]
                z_copy(source, low_slab, index, True).wait_recv()

                @pl.when(z < n_z - 1)
                def _():
                    z_copy(source, low_slab, index, True).start()

                c_copy(source, low_slab, index).start()

            if distance < prompt_slabs:

                @pl.when(high_slab < prompt_slabs)
                def _():
                    source = far.at[high_slab, c, part(index)]
                    z_copy(source, high_slab, index, False).wait_recv()

                    @pl.when(z > 0)
                    def _():
                        z_copy(source, high_slab, index, False).start()

                    c_copy(source, high_slab, index).start()

    @pl.when((c == 1) & (z > 0))
    def _():
        t_copy().wait_recv()
        t_hand().start()
        t_hand().wait_send()

    @pl.when((c == 1) & (z < n_z - 1))
    def _():
        t_copy().wait_send()

    @pl.when((c == 0) & (z > 0))
    def _():
        t_hand().wait_recv()

    n_copy(0).wait_send()
    n_copy(0).wait_recv()

    @pl.when(c == 0)
    def _():
        n_copy(1).wait_send()

    @pl.when(c == 1)
    def _():
        n_copy(1).wait_recv()

    for slab in range(prompt_slabs):
        for index in range(PIECES):
            copy = c_copy(own_rows.at[part(index)], slab, index)
            copy.wait_send()
            copy.wait_recv()

            @pl.when((z < n_z - 1) & (slab <= z))
            def _():
                z_copy(own_rows.at[part(index)], slab, index, True).wait_send()

            @pl.when((z > 0) & (slab >= z))
            def _():
                z_copy(own_rows.at[part(index)], slab, index, False).wait_send()

    for copy in own:
        copy.wait()

    @pl.when(in_prompt)
    def _():
        own_far.wait()

    @pl.when(edge)
    def _():
        own_edge.wait()


def spread_keys(own_rows, prompt_rows, collective_id):
    lane, width = own_rows.shape
    slabs = prompt_rows // (2 * lane)
    dma = pltpu.SemaphoreType.DMA
    far, near, _ = pl.pallas_call(
        functools.partial(spread_kernel, slabs),
        out_shape=(
            jax.ShapeDtypeStruct((slabs, 2, lane, width), own_rows.dtype),
            jax.ShapeDtypeStruct((4, lane // 2, width), own_rows.dtype),
            jax.ShapeDtypeStruct((lane // 2, width), own_rows.dtype),
        ),
        in_specs=[VMEM],
        out_specs=(VMEM,) * 3,
        scratch_shapes=[
            dma((slabs, PIECES, 2)), dma((slabs, PIECES)), dma((slabs, PIECES)), dma((slabs, PIECES)),
            dma((4,)), dma((4,)), dma((4,)),
        ],
        compiler_params=pltpu.CompilerParams(collective_id=collective_id, has_side_effects=True),
    )(own_rows)
    return far.reshape(prompt_rows, width), near.reshape(2 * lane, width)


def collect_kernel(
    prompt_slabs, far, near, out, own, c_got, z_got, n_got, tail_pass, tail_got,
    c_send, c_recv, z_send, z_recv, n_send, n_recv,
):
    n_z = lax.axis_size("z")
    lane = out.shape[0]
    chunk = lane // 2
    size = lane // PIECES
    (z, x, c, y), _, _, c_near = around()
    above, below = (z + 1, x, c, y), (z - 1, x, c, y)

    barrier = pltpu.get_barrier_semaphore()
    pl.semaphore_signal(barrier, inc=1, device_id=c_near, device_id_type=MESH)

    @pl.when(z < n_z - 1)
    def _():
        pl.semaphore_signal(barrier, inc=1, device_id=above, device_id_type=MESH)

    pl.semaphore_wait(barrier, 1 + jnp.where(z > 0, 1, 0))

    def part(index):
        return pl.ds(index * size, size)

    def c_copy(slab, index):
        return remote(
            far.at[slab, 1 - c, part(index)], c_got.at[slab, part(index)], c_send.at[slab, index],
            c_recv.at[slab, index], c_near,
        )

    def z_copy(slab, index):
        return remote(
            own.at[slab, part(index)], z_got.at[slab, part(index)], z_send.at[slab, index],
            z_recv.at[slab, index], below,
        )

    def n_copy(half):
        slot = jnp.where(c == 0, 2, 2 * half)
        return remote(near.at[slot], n_got.at[half], n_send.at[half], n_recv.at[half], c_near)

    def t_hand():
        return remote(near.at[0], tail_pass, n_send.at[2], n_recv.at[2], c_near)

    def t_copy():
        return remote(tail_pass, tail_got, n_send.at[3], n_recv.at[3], below)

    for slab in range(prompt_slabs):
        for index in range(PIECES):
            c_copy(slab, index).start()
    n_copy(0).start()

    @pl.when(c == 1)
    def _():
        n_copy(1).start()

    @pl.when((c == 0) & (z > 0))
    def _():
        t_hand().start()

    for slab in range(prompt_slabs):
        for index in range(PIECES):
            c_copy(slab, index).wait_recv()
            rows = part(index)
            mine = total_of(far[slab, c, rows, :], c_got[slab, rows, :])

            @pl.when((z == n_z - 1) & (z > slab))
            def _():
                own[slab, rows, :] = mine.astype(jnp.bfloat16)
                z_copy(slab, index).start()

            @pl.when((z < n_z - 1) & (z > slab))
            def _():
                z_copy(slab, index).wait_recv()
                own[slab, rows, :] = total_of(mine, z_got[slab, rows, :]).astype(jnp.bfloat16)
                z_copy(slab, index).start()

            @pl.when((z < n_z - 1) & (z == slab))
            def _():
                z_copy(slab, index).wait_recv()
                out[rows, :] = total_of(mine, z_got[slab, rows, :])

            @pl.when((z == n_z - 1) & (z == slab))
            def _():
                out[rows, :] = mine

    @pl.when((c == 1) & (z > 0))
    def _():
        t_hand().wait_recv()
        t_copy().start()

    @pl.when(z >= prompt_slabs)
    def _():
        out[...] = jnp.zeros_like(out)

    n_copy(0).wait_recv()
    first, second = pl.ds(0, chunk), pl.ds(chunk, chunk)
    out[first, :] += total_of(near[1], n_got[0])
    out[second, :] += near[3].astype(jnp.float32)

    @pl.when(c == 0)
    def _():
        n_copy(1).wait_recv()
        out[second, :] += n_got[1].astype(jnp.float32)

    @pl.when((c == 1) & (z < n_z - 1))
    def _():
        t_copy().wait_recv()
        out[second, :] += tail_got[...].astype(jnp.float32)

    @pl.when((c == 1) & (z > 0))
    def _():
        t_copy().wait_send()

    @pl.when((c == 0) & (z > 0))
    def _():
        t_hand().wait_send()

    n_copy(0).wait_send()

    @pl.when(c == 1)
    def _():
        n_copy(1).wait_send()

    for slab in range(prompt_slabs):
        for index in range(PIECES):
            c_copy(slab, index).wait_send()

            @pl.when(z > slab)
            def _():
                z_copy(slab, index).wait_send()


def collect_keys(far, near, collective_id):
    prompt_rows, width = far.shape
    lane = near.shape[0] // 2
    slabs = prompt_rows // (2 * lane)
    dma = pltpu.SemaphoreType.DMA
    low = jnp.bfloat16
    return pl.pallas_call(
        functools.partial(collect_kernel, slabs),
        out_shape=jax.ShapeDtypeStruct((lane, width), jnp.float32),
        in_specs=[VMEM] * 2,
        out_specs=VMEM,
        scratch_shapes=[
            pltpu.VMEM((slabs, lane, width), low),
            pltpu.VMEM((slabs, lane, width), low),
            pltpu.VMEM((slabs, lane, width), low),
            pltpu.VMEM((2, lane // 2, width), low),
            pltpu.VMEM((lane // 2, width), low),
            pltpu.VMEM((lane // 2, width), low),
            dma((slabs, PIECES)), dma((slabs, PIECES)), dma((slabs, PIECES)), dma((slabs, PIECES)),
            dma((4,)), dma((4,)),
        ],
        compiler_params=pltpu.CompilerParams(
            collective_id=collective_id, has_side_effects=True, vmem_limit_bytes=20 * MIB
        ),
    )(far.astype(low).reshape(slabs, 2, lane, width), near.astype(low).reshape(4, lane // 2, width))


def greet_all():
    n_z, n_x, n_c, n_y = sizes()
    count = n_z * n_x * n_c * n_y
    barrier = pltpu.get_barrier_semaphore()

    def call(step, unused):
        pl.semaphore_signal(barrier, inc=1, device_id=device_after(step), device_id_type=MESH)
        return unused

    lax.fori_loop(1, count, call, 0)
    pl.semaphore_wait(barrier, count - 1)


def index_after(step):
    n_z, n_x, n_c, n_y = sizes()
    z, x, c, y = place()
    me = ((z * n_x + x) * n_c + c) * n_y + y
    return lax.rem(me + step, n_z * n_x * n_c * n_y)


def device_after(step):
    _, n_x, n_c, n_y = sizes()
    index = index_after(step)
    return (
        index // (n_x * n_c * n_y), index // (n_c * n_y) % n_x, index // n_y % n_c, index % n_y
    )


def greet_near():
    n_z = lax.axis_size("z")
    (z, x, c, y), x_near, y_near, c_near = around()
    barrier = pltpu.get_barrier_semaphore()
    for device in (x_near, y_near, c_near):
        pl.semaphore_signal(barrier, inc=1, device_id=device, device_id_type=MESH)

    @pl.when(z > 0)
    def _():
        pl.semaphore_signal(barrier, inc=1, device_id=(z - 1, x, c, y), device_id_type=MESH)

    @pl.when(z < n_z - 1)
    def _():
        pl.semaphore_signal(barrier, inc=1, device_id=(z + 1, x, c, y), device_id_type=MESH)

    pl.semaphore_wait(barrier, 3 + jnp.where(z > 0, 1, 0) + jnp.where(z < n_z - 1, 1, 0))


Z_PIECES = 4


def gather_sems():
    n_z = lax.axis_size("z")
    dma = pltpu.SemaphoreType.DMA
    return [
        dma((n_z, Z_PIECES, 2)), dma((n_z, Z_PIECES)), dma((n_z, 2)), dma((n_z, 2)), dma((n_z, 2)),
        dma((n_z, 2)), dma((n_z, 4)), dma((n_z, 4)), dma,
    ]


def gather_slabs(rows_in, out, sems, work):
    z_send, z_recv, x_send, x_recv, y_send, y_recv, c_send, c_recv, own_sem = sems
    n_z = lax.axis_size("z")
    half = rows_in.shape[0] // 2
    size = rows_in.shape[0] // Z_PIECES
    (z, x, c, y), x_near, y_near, c_near = around()
    low, high = pl.ds(0, half), pl.ds(half, half)
    everything = pl.ds(0, 2 * half)
    own = pltpu.make_async_copy(rows_in, out.at[z, x, c, y], own_sem)
    own.start()

    def block(origin, px, py, rows):
        return out.at[origin, px, c, py, rows]

    def z_copy(source, origin, index, up):
        rows = pl.ds(index * size, size)
        other = (z + 1, x, c, y) if up else (z - 1, x, c, y)
        return remote(
            source.at[rows], block(origin, x, y, rows), z_send.at[origin, index, 1 if up else 0],
            z_recv.at[origin, index], other,
        )

    def x_copy(source, origin):
        return remote(source, out.at[origin, x, c, y], x_send.at[origin, 0], x_recv.at[origin, 0], x_near)

    def y_copy(source, origin):
        return remote(source, out.at[origin, x, c, y], y_send.at[origin, 0], y_recv.at[origin, 0], y_near)

    def x_relay(origin):
        part = block(origin, x, 1 - y, high)
        return remote(part, part, x_send.at[origin, 1], x_recv.at[origin, 1], x_near)

    def y_relay(origin):
        part = block(origin, 1 - x, y, low)
        return remote(part, part, y_send.at[origin, 1], y_recv.at[origin, 1], y_near)

    def c_copy(source, origin, px, py):
        slot = px * 2 + py
        return remote(
            source, out.at[origin, px, c, py], c_send.at[origin, slot], c_recv.at[origin, slot], c_near
        )

    def column(origin):
        return out.at[origin, x, c, y]

    def spread(source, origin):
        x_copy(source, origin).start()
        y_copy(source, origin).start()
        c_copy(source, origin, x, y).start()

    def relay(origin):
        x_copy(column(origin), origin).wait_recv()
        y_relay(origin).start()
        y_copy(column(origin), origin).wait_recv()
        x_relay(origin).start()
        c_copy(block(origin, 1 - x, y, everything), origin, 1 - x, y).start()
        c_copy(block(origin, x, 1 - y, everything), origin, x, 1 - y).start()

    def finish(origin):
        x_relay(origin).wait_recv()
        y_relay(origin).wait_recv()
        c_copy(block(origin, 1 - x, 1 - y, everything), origin, 1 - x, 1 - y).start()

    def use(origin):
        for px in range(2):
            for py in range(2):
                c_copy(out.at[origin, px, c, py], origin, px, py).wait_recv()
        work(origin)

    def arrive(step):
        below, above = z - step, z + step

        @pl.when(below >= 0)
        def _():
            for index in range(Z_PIECES):
                z_copy(rows_in, below, index, True).wait_recv()

                @pl.when(z < n_z - 1)
                def _():
                    z_copy(column(below), below, index, True).start()

            spread(column(below), below)

        @pl.when(above < n_z)
        def _():
            for index in range(Z_PIECES):
                z_copy(rows_in, above, index, False).wait_recv()

                @pl.when(z > 0)
                def _():
                    z_copy(column(above), above, index, False).start()

            spread(column(above), above)

    for index in range(Z_PIECES):

        @pl.when(z < n_z - 1)
        def _():
            z_copy(rows_in, z, index, True).start()

        @pl.when(z > 0)
        def _():
            z_copy(rows_in, z, index, False).start()

    spread(rows_in, z)
    for step in range(1, n_z + 3):
        if step < n_z:
            arrive(step)
        for action, back in ((relay, 1), (finish, 2), (use, 3)):
            late = step - back
            if late == 0:
                if action is use:
                    own.wait()
                action(z)
            elif 0 < late < n_z:
                for origin in (z - late, z + late):

                    @pl.when((origin >= 0) & (origin < n_z))
                    def _():
                        action(origin)

    def close(origin, unused):
        x_copy(rows_in, origin).wait_send()
        y_copy(rows_in, origin).wait_send()
        x_relay(origin).wait_send()
        y_relay(origin).wait_send()
        for px in range(2):
            for py in range(2):
                c_copy(out.at[origin, px, c, py], origin, px, py).wait_send()
        for index in range(Z_PIECES):

            @pl.when((z < n_z - 1) & (origin <= z))
            def _():
                z_copy(rows_in, origin, index, True).wait_send()

            @pl.when((z > 0) & (origin >= z))
            def _():
                z_copy(rows_in, origin, index, False).wait_send()

        return unused

    lax.fori_loop(0, n_z, close, 0)


def in_pairs(values, slab, px, pc, row):
    return jnp.concatenate([values[slab, px, pc, py, row : row + 1, :] for py in range(2)], axis=1)


def vocab_ids(extent, chunk, shard_rows):
    n_z, n_x, n_c, n_y = sizes()
    z, x, c, y = place()
    me = ((z * n_x + x) * n_c + c) * n_y + y
    rows = lax.broadcasted_iota(jnp.int32, (extent, chunk), 0)
    return rows + me * shard_rows


def logits_kernel(shard_rows, rows_in, table, ints, valid, out, logs, hits, *sems):
    extent = table.shape[0]
    chunk = 2 * rows_in.shape[0]
    scale = table.shape[1] ** (-0.5)
    greet_near()
    hits[...] = jnp.zeros_like(hits)

    def work(slab):
        def one(index, unused):
            px, pc = index // 2, index % 2
            rows = out[slab, px, pc].reshape(chunk, -1)
            value = outer(table[...], rows) * scale
            ids = vocab_ids(extent, chunk, shard_rows)
            inside = lax.broadcasted_iota(jnp.int32, (extent, chunk), 0) < shard_rows
            target = in_pairs(ints, slab, px, pc, 1).astype(jnp.int32)
            shown = in_pairs(valid, slab, px, pc, 0)
            hit = jnp.where((ids == target) & inside, value, 0.0)
            hits[...] += jnp.sum(hit, axis=0, keepdims=True) * shown
            value = jnp.where(inside, value, MASKED)
            peak = jnp.max(value, axis=0, keepdims=True)
            log = peak + jnp.log(jnp.sum(jnp.exp(value - peak), axis=0, keepdims=True))
            half = chunk // 2
            logs[slab, px, pc, 0] = log[:, :half]
            logs[slab, px, pc, 1] = log[:, half:]
            return unused

        lax.fori_loop(0, 4, one, 0)

    gather_slabs(rows_in, out, sems, work)


def gather_logits(rows, table, ints, valid, shard_rows, collective_id):
    own, width = rows.shape
    shape = sizes() + (own, width)
    return pl.pallas_call(
        functools.partial(logits_kernel, shard_rows),
        out_shape=(
            jax.ShapeDtypeStruct(shape, rows.dtype),
            jax.ShapeDtypeStruct(sizes() + (1, own), jnp.float32),
            jax.ShapeDtypeStruct((1, 2 * own), jnp.float32),
        ),
        in_specs=[VMEM] * 4,
        out_specs=(VMEM,) * 3,
        scratch_shapes=gather_sems(),
        compiler_params=pltpu.CompilerParams(
            collective_id=collective_id, has_side_effects=True,
            vmem_limit_bytes=lax.axis_size("z") * 2 * MIB + 20 * MIB,
        ),
    )(rows, table, ints, valid)


def embed_back_kernel(shard_rows, rows_in, ints, table_grad, smalls, out, small_sum, slabs, small_got, *sems):
    extent = out.shape[0]
    chunk = 2 * rows_in.shape[0]
    small_send, small_recv = sems[-2:]
    n_z, n_x, n_c, n_y = sizes()
    count = n_z * n_x * n_c * n_y
    me = index_after(0)
    greet_all()

    def small(step):
        return remote(
            smalls.at[index_after(step)], small_got.at[me], small_send.at[step], small_recv.at[step],
            device_after(step),
        )

    def each(action):
        def body(step, unused):
            action(step)
            return unused

        lax.fori_loop(1, count, body, 0)

    each(lambda step: small(step).start())
    small_got[me] = smalls[me]
    out[...] = table_grad[...]

    def work(slab):
        def one(index, unused):
            px, pc = index // 2, index % 2
            token = in_pairs(ints, slab, px, pc, 0).astype(jnp.int32)
            inside = lax.broadcasted_iota(jnp.int32, (extent, chunk), 0) < shard_rows
            hot = (vocab_ids(extent, chunk, shard_rows) == token) & inside
            hot = jnp.where(hot, 1.0, 0.0).astype(jnp.bfloat16)
            out[...] += matmul(hot, slabs[slab, px, pc].reshape(chunk, -1))
            return unused

        lax.fori_loop(0, 4, one, 0)

    gather_slabs(rows_in, slabs, sems[:-2], work)
    each(lambda step: small(step).wait())
    small_sum[...] = jnp.sum(small_got[...], axis=0)


def embed_back(rows, ints, table_grad, smalls, shard_rows, collective_id):
    own, width = rows.shape
    count = smalls.shape[0]
    dma = pltpu.SemaphoreType.DMA
    return pl.pallas_call(
        functools.partial(embed_back_kernel, shard_rows),
        out_shape=(
            jax.ShapeDtypeStruct(table_grad.shape, jnp.float32),
            jax.ShapeDtypeStruct(smalls.shape[1:], jnp.float32),
        ),
        in_specs=[VMEM] * 4,
        out_specs=(VMEM,) * 2,
        scratch_shapes=[
            pltpu.VMEM(sizes() + (own, width), rows.dtype), pltpu.VMEM(smalls.shape, jnp.float32),
        ] + gather_sems() + [dma((count,)), dma((count,))],
        compiler_params=pltpu.CompilerParams(
            collective_id=collective_id, has_side_effects=True,
            vmem_limit_bytes=lax.axis_size("z") * 2 * MIB + 20 * MIB,
        ),
    )(rows, ints, table_grad, smalls)


def slab_order():
    n_z = lax.axis_size("z")
    z = lax.axis_index("z")
    up, down = n_z - 1 - z, z
    longer, shorter = jnp.maximum(up, down), jnp.minimum(up, down)
    far_side = jnp.where(up >= down, 1, -1)

    def target(step):
        late = step - (longer - shorter)
        near_side = jnp.where(late % 2 == 0, far_side, -far_side)
        return jnp.where(
            late < 0, z + far_side * (longer - step), z + near_side * (shorter - late // 2)
        )

    return target


def scatter_scratch(rows, width):
    n_z, n_x, n_c, n_y = sizes()
    half = rows // 2
    low = jnp.bfloat16
    dma = pltpu.SemaphoreType.DMA
    return [
        pltpu.VMEM((n_z, n_x, n_y, rows, width), low),
        pltpu.VMEM((n_z, n_x, n_y, rows, width), low),
        pltpu.VMEM((n_z, n_x, n_y, rows, width), low),
        pltpu.VMEM((n_z, 2, half, width), low),
        pltpu.VMEM((n_z, 2, half, width), low),
        pltpu.VMEM((n_z, half, width), low),
        pltpu.VMEM((n_z, half, width), low),
        pltpu.VMEM((n_z, rows, width), low),
        pltpu.VMEM((n_z, rows, width), low),
        dma((n_z, 2)), dma((n_z, 2)), dma((n_z, 3)), dma((n_z, 3)), dma((n_z, 3)),
        dma((n_z, 3)), dma((n_z, 2)), dma((n_z, 2, 2)),
    ]


def scatter_slabs(out, scratch, before, make, after):
    (
        lanes, handed, c_got, x_got, y_got, x_last, y_last, below, above,
        c_send, c_recv, x_send, x_recv, y_send, y_recv, z_send, z_recv,
    ) = scratch
    n_z = lax.axis_size("z")
    rows = out.shape[0]
    half = rows // 2
    (z, x, c, y), x_near, y_near, c_near = around()
    halves = (pl.ds(0, half), pl.ds(half, half))
    low, high = halves
    target = slab_order()

    def c_copy(slab, px):
        return remote(
            handed.at[slab, px], c_got.at[slab, px], c_send.at[slab, px], c_recv.at[slab, px], c_near
        )

    def x_first(slab, part):
        block = lanes.at[slab, 1 - x, y if part == 0 else 1 - y, low]
        return remote(block, x_got.at[slab, part], x_send.at[slab, part], x_recv.at[slab, part], x_near)

    def y_first(slab, part):
        block = lanes.at[slab, x if part == 0 else 1 - x, 1 - y, high]
        return remote(block, y_got.at[slab, part], y_send.at[slab, part], y_recv.at[slab, part], y_near)

    def y_second(slab):
        block = lanes.at[slab, x, 1 - y, low]
        return remote(block, y_last.at[slab], y_send.at[slab, 2], y_recv.at[slab, 2], y_near)

    def x_second(slab):
        block = lanes.at[slab, 1 - x, y, high]
        return remote(block, x_last.at[slab], x_send.at[slab, 2], x_recv.at[slab, 2], x_near)

    def z_up(slab, part):
        return remote(
            lanes.at[slab, x, y, halves[part]], below.at[slab, halves[part]], z_send.at[slab, part],
            z_recv.at[slab, 0, part], (z + 1, x, c, y),
        )

    def z_down(slab, part):
        return remote(
            lanes.at[slab, x, y, halves[part]], above.at[slab, halves[part]], z_send.at[slab, part],
            z_recv.at[slab, 1, part], (z - 1, x, c, y),
        )

    def produce(step):
        slab = target(step)
        before(step)

        def hand(px, unused):
            handed[slab, px] = make(step, slab, px, 1 - c).reshape(2, rows, -1)
            c_copy(slab, px).start()
            return unused

        def keep(px, unused):
            lanes[slab, px] = make(step, slab, px, c).reshape(2, rows, -1)
            return unused

        lax.fori_loop(0, 2, hand, 0)
        lax.fori_loop(0, 2, keep, 0)

    def begin(step):
        slab = target(step)
        for px in range(2):
            c_copy(slab, px).wait_recv()

        def merge(px, py):
            lanes[slab, px, py] = total_of(lanes[slab, px, py], c_got[slab, px, py]).astype(jnp.bfloat16)

        merge(1 - x, 1 - y)
        x_first(slab, 1).start()
        y_first(slab, 1).start()
        merge(1 - x, y)
        x_first(slab, 0).start()
        merge(x, 1 - y)
        y_first(slab, 0).start()
        merge(x, y)
        after(step)

    def middle(step):
        slab = target(step)
        x_first(slab, 1).wait_recv()
        x_first(slab, 0).wait_send()
        y_first(slab, 0).wait_send()
        lanes[slab, x, 1 - y, low] = total_of(
            lanes[slab, x, 1 - y, low], x_got[slab, 1]
        ).astype(jnp.bfloat16)
        y_second(slab).start()
        y_first(slab, 1).wait_recv()
        lanes[slab, 1 - x, y, high] = total_of(
            lanes[slab, 1 - x, y, high], y_got[slab, 1]
        ).astype(jnp.bfloat16)
        x_second(slab).start()

    def finish(step):
        slab = target(step)
        for part in range(2):
            if part == 0:
                x_first(slab, 0).wait_recv()
                y_second(slab).wait_recv()
                value = total_of(lanes[slab, x, y, low], x_got[slab, 0], y_last[slab])
            else:
                y_first(slab, 0).wait_recv()
                x_second(slab).wait_recv()
                value = total_of(lanes[slab, x, y, high], y_got[slab, 0], x_last[slab])
            rows_of = halves[part]

            @pl.when(slab > z)
            def _():
                @pl.when(z == 0)
                def _():
                    lanes[slab, x, y, rows_of] = value.astype(jnp.bfloat16)

                @pl.when(z > 0)
                def _():
                    z_up(slab, part).wait_recv()
                    lanes[slab, x, y, rows_of] = total_of(value, below[slab, rows_of]).astype(jnp.bfloat16)

                z_up(slab, part).start()

            @pl.when(slab < z)
            def _():
                @pl.when(z == n_z - 1)
                def _():
                    lanes[slab, x, y, rows_of] = value.astype(jnp.bfloat16)

                @pl.when(z < n_z - 1)
                def _():
                    z_down(slab, part).wait_recv()
                    lanes[slab, x, y, rows_of] = total_of(value, above[slab, rows_of]).astype(jnp.bfloat16)

                z_down(slab, part).start()

            @pl.when(slab == z)
            def _():
                out[rows_of, :] = value

                @pl.when(z > 0)
                def _():
                    z_up(slab, part).wait_recv()
                    out[rows_of, :] += below[slab, rows_of].astype(jnp.float32)

                @pl.when(z < n_z - 1)
                def _():
                    z_down(slab, part).wait_recv()
                    out[rows_of, :] += above[slab, rows_of].astype(jnp.float32)

    def turn(step, unused):
        for action, back in ((produce, 0), (begin, 0), (middle, 1), (finish, 2)):

            @pl.when((step >= back) & (step < n_z + back))
            def _():
                action(step - back)

        return unused

    lax.fori_loop(0, n_z + 2, turn, 0)

    def close(slab, unused):
        for px in range(2):
            c_copy(slab, px).wait_send()
        x_first(slab, 1).wait_send()
        y_first(slab, 1).wait_send()
        x_second(slab).wait_send()
        y_second(slab).wait_send()
        for part in range(2):

            @pl.when(slab > z)
            def _():
                z_up(slab, part).wait_send()

            @pl.when(slab < z)
            def _():
                z_down(slab, part).wait_send()

        return unused

    lax.fori_loop(0, n_z, close, 0)


def embed_kernel(shard_rows, table, ints, out, *scratch):
    extent = table.shape[0]
    chunk = 2 * out.shape[0]
    greet_near()

    def make(step, slab, px, pc):
        token = in_pairs(ints, slab, px, pc, 0).astype(jnp.int32)
        inside = lax.broadcasted_iota(jnp.int32, (extent, chunk), 0) < shard_rows
        hot = (vocab_ids(extent, chunk, shard_rows) == token) & inside
        hot = jnp.where(hot, 1.0, 0.0).astype(jnp.bfloat16)
        return inner(hot, table[...]).astype(jnp.bfloat16)

    scatter_slabs(out, scratch, lambda step: None, make, lambda step: None)


def embed(table, ints, own, shard_rows, collective_id):
    width = table.shape[1]
    return pl.pallas_call(
        functools.partial(embed_kernel, shard_rows),
        out_shape=jax.ShapeDtypeStruct((own, width), jnp.float32),
        in_specs=[VMEM] * 2,
        out_specs=VMEM,
        scratch_shapes=scatter_scratch(own, width),
        compiler_params=pltpu.CompilerParams(
            collective_id=collective_id, has_side_effects=True,
            vmem_limit_bytes=lax.axis_size("z") * 3 * MIB + 12 * MIB,
        ),
    )(table, ints)


def vocab_back_kernel(
    shard_rows, rows_all, table, ints, logs, weights, out, table_grad, slab_rows, changes, slab_sem, *scratch
):
    extent, width = table.shape
    chunk = 2 * out.shape[0]
    scale = width ** (-0.5)
    n_z = lax.axis_size("z")
    target = slab_order()

    def load(step):
        return pltpu.make_async_copy(
            rows_all.at[target(step)], slab_rows.at[step % 2], slab_sem.at[step % 2]
        )

    load(0).start()
    greet_near()
    table_grad[...] = jnp.zeros_like(table_grad)

    def before(step):
        load(step).wait()

        @pl.when(step + 1 < n_z)
        def _():
            load(step + 1).start()

    def make(step, slab, px, pc):
        rows = slab_rows[step % 2, px, pc].reshape(chunk, width)
        value = outer(table[...], rows) * scale
        inside = lax.broadcasted_iota(jnp.int32, (extent, chunk), 0) < shard_rows
        aim = in_pairs(ints, slab, px, pc, 1).astype(jnp.int32)
        hot = jnp.where(vocab_ids(extent, chunk, shard_rows) == aim, 1.0, 0.0)
        change = jnp.exp(value - in_pairs(logs, slab, px, pc, 0)) - hot
        change = jnp.where(inside, change * in_pairs(weights, slab, px, pc, 0), 0.0)
        change = change.astype(jnp.bfloat16)
        changes[px, pc] = change
        return (inner(change, table[...]) * scale).astype(jnp.bfloat16)

    def after(step):
        def one(index, unused):
            px, pc = index // 2, index % 2
            rows = slab_rows[step % 2, px, pc].reshape(chunk, width)
            table_grad[...] += matmul(changes[px, pc], rows)
            return unused

        lax.fori_loop(0, 4, one, 0)

    scatter_slabs(out, scratch, before, make, after)
    table_grad[...] = table_grad[...] * scale


def vocab_back(rows_all, table, ints, logs, weights, shard_rows, collective_id):
    own, width = rows_all.shape[4:]
    extent = table.shape[0]
    n_z, n_x, n_c, n_y = sizes()
    return pl.pallas_call(
        functools.partial(vocab_back_kernel, shard_rows),
        out_shape=(
            jax.ShapeDtypeStruct((own, width), jnp.float32),
            jax.ShapeDtypeStruct((extent, width), jnp.float32),
        ),
        in_specs=[ANY] + [VMEM] * 4,
        out_specs=(VMEM,) * 2,
        scratch_shapes=[
            pltpu.VMEM((2, n_x, n_c, n_y, own, width), rows_all.dtype),
            pltpu.VMEM((n_x, n_c, extent, 2 * own), jnp.bfloat16),
            pltpu.SemaphoreType.DMA((2,)),
        ] + scatter_scratch(own, width),
        compiler_params=pltpu.CompilerParams(
            collective_id=collective_id, has_side_effects=True,
            vmem_limit_bytes=n_z * 3 * MIB + 24 * MIB if n_z <= 8 else 62 * MIB,
        ),
    )(rows_all, table, ints, logs, weights)


SQRT_HALF = 0.5**0.5
DENSITY = 0.3989422804014327


def matmul(left, right):
    return jnp.dot(left, right, preferred_element_type=jnp.float32)


def inner(left, right):
    return lax.dot_general(
        left, right, (((0,), (0,)), ((), ())), preferred_element_type=jnp.float32
    )


def outer(left, right):
    return lax.dot_general(
        left, right, (((1,), (1,)), ((), ())), preferred_element_type=jnp.float32
    )


def plane_gather(own_rows, blocks, send_sem, recv_sem):
    half = own_rows.shape[0] // 2
    (z, x, c, y), x_near, y_near, _ = around()
    low, high = pl.ds(0, half), pl.ds(half, half)

    def copy(slot, px, py, rows, source, device):
        target = blocks.at[px, py, rows]
        return remote(target if source is None else source.at[rows], target, send_sem.at[slot], recv_sem.at[slot], device)

    first = [
        copy(0, x, y, low, own_rows, x_near),
        copy(1, x, y, high, own_rows, y_near),
        copy(2, x, y, high, own_rows, x_near),
        copy(3, x, y, low, own_rows, y_near),
    ]
    relays = [copy(4, 1 - x, y, low, None, y_near), copy(5, x, 1 - y, high, None, x_near)]
    for each in first:
        each.start()

    def wait_near():
        first[0].wait_recv()
        relays[0].start()
        first[1].wait_recv()
        relays[1].start()

    def wait_x():
        first[2].wait_recv()

    def wait_y():
        first[3].wait_recv()

    def wait_diagonal():
        for each in relays:
            each.wait_recv()

    def close():
        for each in first + relays:
            each.wait_send()

    return wait_near, wait_x, wait_y, wait_diagonal, close


def plane_sum(parts, got, out, send_sem, recv_sem):
    (z, x, c, y), x_near, y_near, _ = around()
    diagonal = (z, 1 - x, c, 1 - y)
    copies = [
        remote(parts.at[device[1], device[3]], got.at[slot], send_sem.at[slot], recv_sem.at[slot], device)
        for slot, device in enumerate((x_near, y_near, diagonal))
    ]

    def close():
        for each in copies:
            each.wait_recv()
        out[...] = total_of(parts[x, y], got[0], got[1], got[2])
        for each in copies:
            each.wait_send()

    return copies, close


def experts_kernel(
    own_rows, route, up, down, out, wide, before, hidden, parts, got, g_send, g_recv, s_send, s_recv
):
    (z, x, c, y), x_near, y_near, _ = around()
    diagonal = (z, 1 - x, c, 1 - y)
    greet((x_near, y_near, diagonal))
    wait_near, wait_x, wait_y, wait_diagonal, close = plane_gather(own_rows, wide, g_send, g_recv)
    copies, finish = plane_sum(parts, got, out, s_send, s_recv)
    wide[x, y] = own_rows[...]

    def work(px, py):
        rows = wide[px, py]
        first = route[px, py] == 0
        value = jnp.where(first, matmul(rows, up[0]), matmul(rows, up[1]))
        before[px, py] = value
        active = 0.5 * value * (1.0 + lax.erf(value * SQRT_HALF))
        hidden_first = jnp.where(first, active, 0.0).astype(jnp.bfloat16)
        hidden_second = jnp.where(first, 0.0, active).astype(jnp.bfloat16)
        hidden[px, py] = active.astype(jnp.bfloat16)
        total = outer(hidden_first, down[0]) + outer(hidden_second, down[1])
        parts[px, py] = total.astype(jnp.bfloat16)

    work(x, y)
    wait_near()
    wait_x()
    work(1 - x, y)
    copies[0].start()
    wait_y()
    work(x, 1 - y)
    copies[1].start()
    wait_diagonal()
    work(1 - x, 1 - y)
    copies[2].start()
    finish()
    close()


def experts(own_rows, route, up, down, collective_id):
    _, n_x, _, n_y = sizes()
    own, width = own_rows.shape
    wide = up.shape[2]
    dma = pltpu.SemaphoreType.DMA
    low = jnp.bfloat16
    return pl.pallas_call(
        experts_kernel,
        out_shape=(
            jax.ShapeDtypeStruct((own, width), jnp.float32),
            jax.ShapeDtypeStruct((n_x, n_y, own, width), low),
            jax.ShapeDtypeStruct((n_x, n_y, own, wide), jnp.float32),
            jax.ShapeDtypeStruct((n_x, n_y, own, wide), low),
        ),
        in_specs=[VMEM] * 4,
        out_specs=(VMEM,) * 4,
        scratch_shapes=[
            pltpu.VMEM((n_x, n_y, own, width), low),
            pltpu.VMEM((3, own, width), low),
            dma((6,)), dma((6,)), dma((3,)), dma((3,)),
        ],
        compiler_params=pltpu.CompilerParams(
            collective_id=collective_id, has_side_effects=True, vmem_limit_bytes=20 * MIB
        ),
        cost_estimate=pl.CostEstimate(
            flops=8 * own * 4 * width * wide, bytes_accessed=8 * MIB, transcendentals=4 * own * wide
        ),
    )(own_rows, route, up, down)


def experts_back_kernel(
    own_rows, route, up, down, wide, before, hidden, out, grads,
    wide_grad, before_grad, parts, got, g_send, g_recv, s_send, s_recv,
):
    (z, x, c, y), x_near, y_near, _ = around()
    diagonal = (z, 1 - x, c, 1 - y)
    greet((x_near, y_near, diagonal))
    wait_near, wait_x, wait_y, wait_diagonal, close = plane_gather(own_rows, wide_grad, g_send, g_recv)
    copies, finish = plane_sum(parts, got, out, s_send, s_recv)
    wide_grad[x, y] = own_rows[...]

    def work(px, py):
        rows = wide_grad[px, py]
        first = route[px, py] == 0
        hidden_grad = jnp.where(first, matmul(rows, down[0]), matmul(rows, down[1]))
        value = before[px, py]
        slope = 0.5 * (1.0 + lax.erf(value * SQRT_HALF)) + value * (
            DENSITY * jnp.exp(-0.5 * value * value)
        )
        change = (hidden_grad * slope).astype(jnp.bfloat16)
        before_grad[px, py] = change
        change_first = jnp.where(first, change, 0)
        change_second = jnp.where(first, 0, change)
        total = outer(change_first, up[0]) + outer(change_second, up[1])
        parts[px, py] = total.astype(jnp.bfloat16)

    work(x, y)
    wait_near()
    wait_x()
    work(1 - x, y)
    copies[0].start()
    wait_y()
    work(x, 1 - y)
    copies[1].start()
    wait_diagonal()
    work(1 - x, 1 - y)
    copies[2].start()
    close()

    lane = 4 * own_rows.shape[0]
    rows = wide[...].reshape(lane, -1)
    grad_rows = wide_grad[...].reshape(lane, -1)
    first = route[...].reshape(lane, 1) == 0
    change = before_grad[...].reshape(lane, -1)
    active = hidden[...].reshape(lane, -1)
    low = jnp.bfloat16
    grads[0] = inner(rows, jnp.where(first, change, 0)).astype(low)
    grads[1] = inner(rows, jnp.where(first, 0, change)).astype(low)
    grads[2] = inner(grad_rows, jnp.where(first, active, 0)).astype(low)
    grads[3] = inner(grad_rows, jnp.where(first, 0, active)).astype(low)
    finish()


def experts_back(own_rows, route, up, down, wide, before, hidden, collective_id):
    _, n_x, _, n_y = sizes()
    own, width = own_rows.shape
    units = up.shape[2]
    dma = pltpu.SemaphoreType.DMA
    low = jnp.bfloat16
    return pl.pallas_call(
        experts_back_kernel,
        out_shape=(
            jax.ShapeDtypeStruct((own, width), jnp.float32),
            jax.ShapeDtypeStruct((4, width, units), low),
        ),
        in_specs=[VMEM] * 7,
        out_specs=(VMEM,) * 2,
        scratch_shapes=[
            pltpu.VMEM((n_x, n_y, own, width), low),
            pltpu.VMEM((n_x, n_y, own, units), low),
            pltpu.VMEM((n_x, n_y, own, width), low),
            pltpu.VMEM((3, own, width), low),
            dma((6,)), dma((6,)), dma((3,)), dma((3,)),
        ],
        compiler_params=pltpu.CompilerParams(
            collective_id=collective_id, has_side_effects=True, vmem_limit_bytes=28 * MIB
        ),
        cost_estimate=pl.CostEstimate(
            flops=16 * own * 4 * width * units, bytes_accessed=12 * MIB, transcendentals=8 * own * units
        ),
    )(own_rows, route, up, down, wide, before, hidden)


def project_kernel(transposed, rows, weight, out, parts, got, s_send, s_recv):
    (z, x, c, y), x_near, y_near, _ = around()
    diagonal = (z, 1 - x, c, 1 - y)
    barrier = pltpu.get_barrier_semaphore()
    for device in (x_near, y_near, diagonal):
        pl.semaphore_signal(barrier, inc=1, device_id=device, device_id_type=MESH)
    copies, finish = plane_sum(parts, got, out, s_send, s_recv)

    def work(px, py):
        times = outer if transposed else matmul
        parts[px, py] = times(rows[px, py], weight[...]).astype(jnp.bfloat16)

    work(1 - x, 1 - y)
    pl.semaphore_wait(barrier, 3)
    copies[2].start()
    work(1 - x, y)
    copies[0].start()
    work(x, 1 - y)
    copies[1].start()
    work(x, y)
    finish()


def project(rows, weight, transposed, collective_id):
    n_x, n_y, own, depth = rows.shape
    width = weight.shape[0] if transposed else weight.shape[1]
    low = jnp.bfloat16
    dma = pltpu.SemaphoreType.DMA
    return pl.pallas_call(
        functools.partial(project_kernel, transposed),
        out_shape=jax.ShapeDtypeStruct((own, width), jnp.float32),
        in_specs=[VMEM] * 2,
        out_specs=VMEM,
        scratch_shapes=[
            pltpu.VMEM((n_x, n_y, own, width), low), pltpu.VMEM((3, own, width), low), dma((3,)), dma((3,)),
        ],
        compiler_params=pltpu.CompilerParams(
            collective_id=collective_id, has_side_effects=True, vmem_limit_bytes=10 * MIB
        ),
        cost_estimate=pl.CostEstimate(
            flops=8 * own * width * depth, bytes_accessed=4 * MIB, transcendentals=0
        ),
    )(rows, weight)


def gather_project_kernel(transposed, own_rows, weight, wide, out, g_send, g_recv):
    (z, x, c, y), x_near, y_near, _ = around()
    greet((x_near, y_near))
    wait_near, wait_x, wait_y, wait_diagonal, close = plane_gather(own_rows, wide, g_send, g_recv)
    wide[x, y] = own_rows[...]

    def work(px, py):
        times = outer if transposed else matmul
        out[px, py] = times(wide[px, py], weight[...]).astype(jnp.bfloat16)

    work(x, y)
    wait_near()
    wait_x()
    work(1 - x, y)
    wait_y()
    work(x, 1 - y)
    wait_diagonal()
    work(1 - x, 1 - y)
    close()


def gather_project(own_rows, weight, transposed, collective_id):
    _, n_x, _, n_y = sizes()
    own, width = own_rows.shape
    depth = weight.shape[0] if transposed else weight.shape[1]
    dma = pltpu.SemaphoreType.DMA
    low = jnp.bfloat16
    return pl.pallas_call(
        functools.partial(gather_project_kernel, transposed),
        out_shape=(
            jax.ShapeDtypeStruct((n_x, n_y, own, width), low),
            jax.ShapeDtypeStruct((n_x, n_y, own, depth), low),
        ),
        in_specs=[VMEM] * 2,
        out_specs=(VMEM,) * 2,
        scratch_shapes=[dma((6,)), dma((6,))],
        compiler_params=pltpu.CompilerParams(
            collective_id=collective_id, has_side_effects=True, vmem_limit_bytes=12 * MIB
        ),
        cost_estimate=pl.CostEstimate(
            flops=8 * own * width * depth, bytes_accessed=4 * MIB, transcendentals=0
        ),
    )(own_rows, weight)


def merge_logs_kernel(source, out, got, mine, send_one, recv_one, send_two, recv_two):
    n_z, n_x, n_c, n_y = sizes()
    count = n_z * n_x * n_c * n_y
    z, x, c, y = place()
    me = ((z * n_x + x) * n_c + c) * n_y + y

    def device_of(index):
        return (
            index // (n_x * n_c * n_y), index // (n_c * n_y) % n_x, index // n_y % n_c, index % n_y
        )

    barrier = pltpu.get_barrier_semaphore()

    def call(step, unused):
        other = lax.rem(me + step, count)
        pl.semaphore_signal(barrier, inc=1, device_id=device_of(other), device_id_type=MESH)
        return unused

    lax.fori_loop(1, count, call, 0)
    got[me] = source[me]
    pl.semaphore_wait(barrier, count - 1)

    def first(step):
        other = lax.rem(me + step, count)
        return remote(
            source.at[other], got.at[me], send_one.at[step], recv_one.at[step], device_of(other)
        )

    def second(step):
        other = lax.rem(me + step, count)
        return remote(mine, out.at[me], send_two.at[step], recv_two.at[step], device_of(other))

    def each(action):
        def body(step, unused):
            action(step)
            return unused

        lax.fori_loop(1, count, body, 0)

    each(lambda step: first(step).start())
    each(lambda step: first(step).wait())
    values = got[...]
    peak = jnp.max(values, axis=0)
    mine[...] = peak + jnp.log(jnp.sum(jnp.exp(values - peak[None]), axis=0))
    out[me] = mine[...]
    each(lambda step: second(step).start())
    each(lambda step: second(step).wait())


def merge_logs(blocks, collective_id):
    count = blocks.shape[0]
    dma = pltpu.SemaphoreType.DMA
    return pl.pallas_call(
        merge_logs_kernel,
        out_shape=jax.ShapeDtypeStruct(blocks.shape, blocks.dtype),
        in_specs=[VMEM],
        out_specs=VMEM,
        scratch_shapes=[
            pltpu.VMEM(blocks.shape, blocks.dtype), pltpu.VMEM(blocks.shape[1:], blocks.dtype),
            dma((count,)), dma((count,)), dma((count,)), dma((count,)),
        ],
        compiler_params=pltpu.CompilerParams(collective_id=collective_id, has_side_effects=True),
    )(blocks)


def key_position(index, part, chunk):
    lane = 2 * chunk
    start = (part // 2) * (2 * lane) + (part % 2) * chunk
    return start + index + jnp.where(index >= chunk, chunk, 0)


def near_shown(side, chunk, query_pos, query_seg, near_pos, near_seg):
    columns = slice(side * chunk, (side + 1) * chunk)
    rows = slice(2 * side * chunk, 2 * (side + 1) * chunk)
    shown = (
        (near_seg[rows, :] == query_seg[:, columns])
        & (near_pos[rows, :] <= query_pos[:, columns])
        & (near_pos[rows, :] >= PROMPT)
    )
    return columns, rows, shown


def attend_kernel(
    chunk, query, far, near, query_pos, query_seg, near_pos, near_seg,
    out, out_low, log_total, scores, far_t, near_t,
):
    lane, feature = query.shape
    group = feature // HEAD_DIM
    prompt_rows = far.shape[0]
    parts = prompt_rows // lane
    query_t = (query[...].astype(jnp.float32) * HEAD_DIM ** (-0.5)).T.astype(jnp.bfloat16)
    far_t[...] = far[...].astype(jnp.float32).T.astype(jnp.bfloat16)
    near_t[...] = near[...].astype(jnp.float32).T.astype(jnp.bfloat16)
    row_of = lax.broadcasted_iota(jnp.int32, (feature, lane), 0)
    q_pos = query_pos[...]

    for head in range(group):
        low, high = head * HEAD_DIM, (head + 1) * HEAD_DIM
        query_h = jnp.where((row_of >= low) & (row_of < high), query_t, 0)

        def score_part(part, peak):
            block = far[pl.ds(pl.multiple_of(part * lane, lane), lane), :feature]
            value = matmul(block, query_h)
            index = lax.broadcasted_iota(jnp.int32, (lane, lane), 0)
            value = jnp.where(key_position(index, part, chunk) <= q_pos, value, MASKED)
            scores[pl.ds(pl.multiple_of(part * lane, lane), lane), :] = value
            return jnp.maximum(peak, jnp.max(value, axis=0, keepdims=True))

        peak = lax.fori_loop(0, parts, score_part, jnp.full((1, lane), MASKED, jnp.float32))
        near_peaks = []
        for side in range(2):
            columns, rows, shown = near_shown(side, chunk, query_pos, query_seg, near_pos, near_seg)
            value = matmul(near[rows, :feature], query_h[:, columns])
            value = jnp.where(shown, value, MASKED)
            scores[prompt_rows : prompt_rows + lane, columns] = value
            near_peaks.append(jnp.max(value, axis=0, keepdims=True))
        peak = jnp.maximum(peak, jnp.concatenate(near_peaks, axis=1))

        def weigh_part(part, state):
            total, mixed = state
            start = pl.multiple_of(part * lane, lane)
            chance = jnp.exp(scores[pl.ds(start, lane), :] - peak)
            total = total + jnp.sum(chance, axis=0, keepdims=True)
            mixed = mixed + matmul(
                far_t[feature + low : feature + high, pl.ds(start, lane)],
                chance.astype(jnp.bfloat16),
            )
            return total, mixed

        total, mixed = lax.fori_loop(
            0,
            parts,
            weigh_part,
            (jnp.zeros((1, lane), jnp.float32), jnp.zeros((HEAD_DIM, lane), jnp.float32)),
        )
        near_total, near_mixed = [], []
        for side in range(2):
            columns = slice(side * chunk, (side + 1) * chunk)
            rows = slice(side * lane, (side + 1) * lane)
            chance = jnp.exp(scores[prompt_rows : prompt_rows + lane, columns] - peak[:, columns])
            near_total.append(jnp.sum(chance, axis=0, keepdims=True))
            near_mixed.append(
                matmul(near_t[feature + low : feature + high, rows], chance.astype(jnp.bfloat16))
            )
        total = total + jnp.concatenate(near_total, axis=1)
        mixed = mixed + jnp.concatenate(near_mixed, axis=1)
        out[low:high, :] = mixed / total
        log_total[head : head + 1, :] = peak + jnp.log(total)
    out_low[...] = out[...].T.astype(jnp.bfloat16)


def attend(queries, far, near, places, chunk):
    lane, feature = queries.shape
    prompt_rows = far.shape[0]
    group = feature // HEAD_DIM
    total_rows = prompt_rows + lane
    return pl.pallas_call(
        functools.partial(attend_kernel, chunk),
        out_shape=(
            jax.ShapeDtypeStruct((feature, lane), jnp.float32),
            jax.ShapeDtypeStruct((lane, feature), jnp.bfloat16),
            jax.ShapeDtypeStruct((group, lane), jnp.float32),
        ),
        in_specs=[VMEM] * 7,
        out_specs=(VMEM,) * 3,
        scratch_shapes=[
            pltpu.VMEM((total_rows, lane), jnp.float32),
            pltpu.VMEM((2 * feature, prompt_rows), jnp.bfloat16),
            pltpu.VMEM((2 * feature, 2 * lane), jnp.bfloat16),
        ],
        compiler_params=pltpu.CompilerParams(vmem_limit_bytes=20 * MIB),
        cost_estimate=pl.CostEstimate(
            flops=8 * group * lane * total_rows * 128,
            bytes_accessed=8 * MIB,
            transcendentals=group * lane * total_rows,
        ),
    )(queries, far, near, *places)


def attend_back_kernel(
    chunk, query, far, near, query_pos, query_seg, near_pos, near_seg,
    log_total, mixed, answer, query_grad, far_grad, near_grad,
    far_t, near_t, far_values, near_values, far_sum, near_sum, query_sum,
):
    lane, feature = query.shape
    group = feature // HEAD_DIM
    prompt_rows = far.shape[0]
    parts = prompt_rows // lane
    scaled = (query[...].astype(jnp.float32) * HEAD_DIM ** (-0.5)).astype(jnp.bfloat16)
    query_t = scaled.astype(jnp.float32).T.astype(jnp.bfloat16)
    answers = answer[...]
    answer_t = answers.astype(jnp.float32).T.astype(jnp.bfloat16)
    far_t[...] = far[:, :feature].astype(jnp.float32).T.astype(jnp.bfloat16)
    near_t[...] = near[:, :feature].astype(jnp.float32).T.astype(jnp.bfloat16)
    far_values[...] = far[:, feature:]
    near_values[...] = near[:, feature:]
    row_of = lax.broadcasted_iota(jnp.int32, (feature, lane), 0)
    column_of = lax.broadcasted_iota(jnp.int32, (lane, feature), 1)
    q_pos = query_pos[...]

    for head in range(group):
        low, high = head * HEAD_DIM, (head + 1) * HEAD_DIM
        in_rows = (row_of >= low) & (row_of < high)
        in_columns = (column_of >= low) & (column_of < high)
        query_ht = jnp.where(in_rows, query_t, 0)
        answer_ht = jnp.where(in_rows, answer_t, 0)
        query_h = jnp.where(in_columns, scaled, 0)
        answer_h = jnp.where(in_columns, answers, 0)
        log_h = log_total[head : head + 1, :]
        delta_h = jnp.sum(
            answer_t[low:high, :].astype(jnp.float32) * mixed[low:high, :], axis=0, keepdims=True
        )

        def slopes(key_block, value_block, shown, columns):
            value = matmul(key_block, query_ht[:, columns])
            chance = jnp.exp(jnp.where(shown, value - log_h[:, columns], MASKED))
            slope = matmul(value_block, answer_ht[:, columns])
            change = (chance * (slope - delta_h[:, columns])).astype(jnp.bfloat16)
            chance = chance.astype(jnp.bfloat16)
            return change, matmul(change, query_h[columns]), matmul(chance, answer_h[columns])

        def add(sums, rows, key_part, value_part):
            if head == 0:
                sums[0, rows, :] = key_part
                sums[1, rows, :] = value_part
            else:
                sums[0, rows, :] += key_part
                sums[1, rows, :] += value_part

        def back_part(part, total):
            rows = pl.ds(pl.multiple_of(part * lane, lane), lane)
            index = lax.broadcasted_iota(jnp.int32, (lane, lane), 0)
            shown = key_position(index, part, chunk) <= q_pos
            change, key_part, value_part = slopes(
                far[rows, :feature], far_values[rows, :], shown, slice(0, lane)
            )
            add(far_sum, rows, key_part, value_part)
            return total + matmul(far_t[low:high, rows], change)

        total = lax.fori_loop(0, parts, back_part, jnp.zeros((HEAD_DIM, lane), jnp.float32))
        near_total = []
        for side in range(2):
            columns, rows, shown = near_shown(side, chunk, query_pos, query_seg, near_pos, near_seg)
            change, key_part, value_part = slopes(
                near[rows, :feature], near_values[rows, :], shown, columns
            )
            add(near_sum, rows, key_part, value_part)
            near_total.append(matmul(near_t[low:high, rows], change))
        query_sum[low:high, :] = (total + jnp.concatenate(near_total, axis=1)) * HEAD_DIM ** (-0.5)
    query_grad[...] = query_sum[...].T.astype(jnp.bfloat16)
    for sums, grad in ((far_sum, far_grad), (near_sum, near_grad)):
        grad[...] = jnp.concatenate(
            [sums[0].astype(jnp.bfloat16), sums[1].astype(jnp.bfloat16)], axis=1
        )


def attend_back(queries, far, near, places, log_total, mixed, answer, chunk):
    lane, feature = queries.shape
    prompt_rows = far.shape[0]
    group = feature // HEAD_DIM
    total_rows = prompt_rows + lane
    low = jnp.bfloat16
    return pl.pallas_call(
        functools.partial(attend_back_kernel, chunk),
        out_shape=(
            jax.ShapeDtypeStruct((lane, feature), low),
            jax.ShapeDtypeStruct((prompt_rows, 2 * feature), low),
            jax.ShapeDtypeStruct((2 * lane, 2 * feature), low),
        ),
        in_specs=[VMEM] * 10,
        out_specs=(VMEM,) * 3,
        scratch_shapes=[
            pltpu.VMEM((feature, prompt_rows), low),
            pltpu.VMEM((feature, 2 * lane), low),
            pltpu.VMEM((prompt_rows, feature), low),
            pltpu.VMEM((2 * lane, feature), low),
            pltpu.VMEM((2, prompt_rows, feature), jnp.float32),
            pltpu.VMEM((2, 2 * lane, feature), jnp.float32),
            pltpu.VMEM((feature, lane), jnp.float32),
        ],
        compiler_params=pltpu.CompilerParams(vmem_limit_bytes=28 * MIB),
        cost_estimate=pl.CostEstimate(
            flops=20 * group * lane * total_rows * 128,
            bytes_accessed=12 * MIB,
            transcendentals=group * lane * total_rows,
        ),
    )(queries, far, near, *places, log_total, mixed, answer)


def head_places(back):
    n_z, n_x, n_c, n_y = sizes()
    line = n_z * n_c
    pairs = []
    for device in range(line * n_x * n_y):
        group, at = device // line, device % line
        place_of = ((at // n_c * n_x + group // n_y) * n_c + at % n_c) * n_y + group % n_y
        pairs.append((place_of, device) if back else (device, place_of))
    return tuple(pairs)


def pad_rows(block):
    return jnp.pad(block, ((0, 8 - block.shape[0]), (0, 0)))


def adam_update(weight, moment_one, moment_two, gradient, step_rate, decay_rate):
    first_new = BETA_ONE * moment_one + (1.0 - BETA_ONE) * gradient
    second_new = BETA_TWO * moment_two + (1.0 - BETA_TWO) * gradient * gradient
    normalized = (
        first_new
        / (1.0 - BETA_ONE**STEP)
        / (jnp.sqrt(second_new / (1.0 - BETA_TWO**STEP)) + ADAM_EPS)
    )
    return (weight - step_rate * (normalized + decay_rate * weight), first_new, second_new)


def per_device(
    token_ids,
    targets,
    valid_mask,
    cont_lengths,
    routes,
    vocab_table,
    vocab_first,
    vocab_second,
    attn_weights,
    attn_first,
    attn_second,
    router,
    router_first,
    router_second,
    norm_gains,
    gains_first,
    gains_second,
    expert_up,
    up_first,
    up_second,
    expert_down,
    down_first,
    down_second,
):
    slabs = lax.axis_size("z")
    planes = lax.axis_size("x")
    cores = lax.axis_size("core")
    sides = lax.axis_size("head")
    groups = planes * sides
    z_at, x_at, core_at, side_at = (lax.axis_index(name) for name in ALL)
    blk_at = (z_at * planes + x_at) * cores + core_at
    device_at = blk_at * sides + side_at
    group_at = x_at * sides + side_at
    tokens = valid_mask.shape[0]
    chunk = token_ids.shape[0]
    own = chunk // sides
    lane = planes * chunk
    feature = D // groups
    wide = expert_up.shape[3] // planes
    shard_rows = vocab_table.shape[0]
    logit_scale = D ** (-0.5)

    cont_ends = jnp.cumsum(cont_lengths)
    valid_f = valid_mask.astype(jnp.float32)
    token_count = jnp.sum(valid_mask).astype(jnp.float32)
    expert_ids = jnp.arange(EXPERTS, dtype=jnp.int32)

    own_ints = jnp.concatenate([token_ids[None], targets[None], routes], axis=0)
    own_ints = lax.dynamic_slice_in_dim(own_ints, side_at * own, own, axis=1).astype(jnp.float32)
    rows_of = attn_weights.shape[1]
    smalls = jnp.concatenate(
        [router.transpose(0, 2, 1).reshape(LAYERS * EXPERTS, rows_of), norm_gains], axis=0
    )
    smalls = smalls.astype(jnp.bfloat16).astype(jnp.float32)
    smalls = jnp.pad(smalls, ((0, 16 - smalls.shape[0]), (0, own - rows_of)))
    whole_f = swap(jnp.concatenate([pad_rows(own_ints), smalls], axis=0)[None], True, 1)
    attn_low = attn_weights.astype(jnp.bfloat16)
    qkv_send = attn_low[:, :, : 3 * D].reshape(LAYERS, rows_of, 3, groups, feature)
    qkv_send = jnp.concatenate([qkv_send[:, :, 1:], qkv_send[:, :, :1]], axis=2)
    qkv_send = qkv_send.transpose(3, 0, 1, 2, 4).reshape(groups, LAYERS, rows_of, 3 * feature)
    qkv_got = lax.all_to_all(qkv_send, PLANE, split_axis=0, concat_axis=0, tiled=True)
    out_rows = attn_low[:, :, 3 * D :]
    out_rows = lax.ppermute(out_rows, ALL, head_places(False))
    out_rows = out_rows.reshape(LAYERS, rows_of, groups, feature).transpose(2, 0, 1, 3)
    expert_send = jnp.stack([expert_up, expert_down], axis=1).astype(jnp.bfloat16)
    depth = expert_send.shape[3]
    expert_send = expert_send.reshape(LAYERS, 2 * EXPERTS, depth, planes, wide)
    expert_send = expert_send.transpose(3, 0, 1, 2, 4)
    expert_halves = []
    for layer_index in range(LAYERS):
        kept_half = lax.dynamic_index_in_dim(expert_send[:, layer_index], x_at, 0, False)
        sent_half = lax.dynamic_index_in_dim(expert_send[:, layer_index], 1 - x_at, 0, False)
        got_half = lax.ppermute(sent_half, "x", ((0, 1), (1, 0)))
        expert_halves.append((kept_half, got_half))
    whole_f, qkv_got, out_rows, expert_halves = lax.optimization_barrier(
        (whole_f, qkv_got, out_rows, expert_halves)
    )
    attn_pack = jnp.concatenate([qkv_got, out_rows], axis=3)
    expert_packs = []
    for kept_half, got_half in expert_halves:
        expert_packs.append(
            jnp.stack(
                [
                    jnp.where(x_at == 0, kept_half, got_half),
                    jnp.where(x_at == 0, got_half, kept_half),
                ]
            )
        )
    whole_f, attn_pack, expert_packs = lax.optimization_barrier((whole_f, attn_pack, expert_packs))
    attn_pack = lax.all_gather(attn_pack, LINE, axis=0)
    qkv_weights, out_weights = [], []
    for layer_index in range(LAYERS):
        block = attn_pack[:, :, layer_index]
        part = block[..., : 3 * feature].reshape(slabs, cores, planes, sides, rows_of, 3 * feature)
        qkv_weights.append(part.transpose(0, 2, 1, 3, 4, 5).reshape(D, 3 * feature))
        part = block[..., 3 * feature :]
        out_weights.append(part.transpose(0, 2, 1, 3).reshape(feature, D))
    expert_weights = []
    for halves in expert_packs:
        block = lax.all_gather(halves, LINE, axis=0)
        block = block.reshape(slabs, cores, planes, 2, EXPERTS, depth, wide)
        block = block.transpose(3, 4, 0, 2, 1, 5, 6).reshape(2, EXPERTS, D, wide)
        expert_weights.append(block)

    ints = whole_f.reshape(sizes() + whole_f.shape[1:])
    whole = whole_f[:, : 2 + LAYERS].astype(jnp.int32)
    smalls = whole_f[:, 8:, :rows_of].transpose(1, 0, 2).reshape(16, D)
    router_all = smalls[: LAYERS * EXPERTS].reshape(LAYERS, EXPERTS, D).transpose(0, 2, 1)
    router_all = router_all.astype(jnp.bfloat16)
    gains_f = smalls[LAYERS * EXPERTS :]
    routes_lane = lax.dynamic_index_in_dim(
        whole.reshape(slabs, planes, cores, sides, 2 + LAYERS, own), z_at, 0, False
    )
    routes_lane = lax.dynamic_index_in_dim(routes_lane, core_at, 1, False)[:, :, 2:]
    routes_lane = routes_lane.transpose(2, 0, 1, 3)[..., None]
    routes_own = lax.dynamic_slice_in_dim(routes, side_at * own, own, axis=1)

    extent = -(-shard_rows // 256) * 256
    table = jnp.pad(vocab_table.astype(jnp.bfloat16), ((0, extent - shard_rows), (0, 0)))
    offsets = jnp.arange(chunk, dtype=jnp.int32)
    first_blk = z_at * planes * cores + core_at
    query_pos = jnp.concatenate([(first_blk + cores * part) * chunk + offsets for part in range(planes)])
    near_blks = [first_blk - 1 + part for part in range(2 * planes)]
    near_pos = jnp.concatenate([blk * chunk + offsets for blk in near_blks])
    query_seg = segment_of(query_pos, cont_ends)
    near_seg = segment_of(near_pos, cont_ends)
    places = (query_pos[None, :], query_seg[None, :], near_pos[:, None], near_seg[:, None])

    stream = embed(table, ints, own, shard_rows, 2)

    kept = []
    for layer_index in range(LAYERS):
        up, down = expert_weights[layer_index][0], expert_weights[layer_index][1]
        normed_lane, qkv = gather_project(
            rms_norm(stream, gains_f[2 * layer_index]).astype(jnp.bfloat16),
            qkv_weights[layer_index], False, 3,
        )
        qkv = qkv.reshape(lane, 3 * feature)
        queries = qkv[:, 2 * feature :]
        far, near = spread_keys(qkv[:, : 2 * feature], PROMPT, 10)
        mixed_t, mixed_low, log_total = attend(queries, far, near, places, chunk)
        middle = stream + project(
            mixed_low.reshape(planes, sides, own, feature), out_weights[layer_index], False, 15
        )
        normed_two = rms_norm(middle, gains_f[2 * layer_index + 1]).astype(jnp.bfloat16)
        chance = jax.nn.softmax(matmul(normed_two, router_all[layer_index]), axis=-1)
        output, wide_rows, before, hidden = experts(
            normed_two, routes_lane[layer_index], up, down, 11
        )
        own_pick = (routes_own[layer_index][:, None] == expert_ids[None, :]).astype(jnp.float32)
        gate = jnp.sum(chance * own_pick, axis=1, keepdims=True)
        kept.append(
            (
                stream, normed_lane, queries, far, near, mixed_t, mixed_low, log_total, middle,
                normed_two, chance, wide_rows, before, hidden, output, own_pick, gate,
            )
        )
        stream = middle + gate * output

    final_gain = gains_f[2 * LAYERS]
    devices = tokens // own
    valid_rows = valid_f.reshape(sizes() + (1, own))
    final_all, row_logs, hits = gather_logits(
        rms_norm(stream, final_gain).astype(jnp.bfloat16), table, ints, valid_rows, shard_rows, 4
    )
    log_sums = merge_logs(row_logs.reshape(devices, 1, own), 5)
    log_sum = log_sums.reshape(tokens)
    own_log = lax.dynamic_slice_in_dim(log_sum, device_at * own, own)
    own_valid = lax.dynamic_slice_in_dim(valid_f, device_at * own, own)
    own_loss = jnp.sum(own_log * own_valid) - jnp.sum(hits)
    final_grad, table_grad = vocab_back(
        final_all, table, ints, log_sums.reshape(sizes() + (1, own)), valid_rows / token_count,
        shard_rows, 6,
    )
    stream_grad, final_gain_grad = jax.vjp(rms_norm, stream, final_gain)[1](final_grad)

    attn_packs = [None] * LAYERS
    router_list = [None] * LAYERS
    expert_shares = [None] * LAYERS
    gain_list = [None] * (2 * LAYERS + 1)
    gain_list[2 * LAYERS] = final_gain_grad
    for layer_index in reversed(range(LAYERS)):
        (
            stream, normed_lane, queries, far, near, mixed_t, mixed_low, log_total, middle,
            normed_two, chance, wide_rows, before, hidden, output, own_pick, gate,
        ) = kept[layer_index]
        up, down = expert_weights[layer_index][0], expert_weights[layer_index][1]
        out_grad = (gate * stream_grad).astype(jnp.bfloat16)
        chance_grad = jnp.sum(stream_grad * output, axis=1)[:, None] * own_pick
        choice_grad = chance * (chance_grad - jnp.sum(chance * chance_grad, axis=1, keepdims=True))
        router_list[layer_index] = jnp.dot(
            normed_two.astype(jnp.float32).T, choice_grad, precision=lax.Precision.HIGHEST
        )
        normed_grad = jnp.dot(
            choice_grad,
            router_all[layer_index].astype(jnp.float32).T,
            precision=lax.Precision.HIGHEST,
        )
        rows_grad, expert_grad = experts_back(
            out_grad, routes_lane[layer_index], up, down, wide_rows, before, hidden, 12
        )
        normed_grad = normed_grad + rows_grad
        expert_grad = expert_grad.reshape(2 * EXPERTS, slabs, planes, cores, depth, wide)
        expert_grad = expert_grad.transpose(1, 3, 2, 0, 4, 5).reshape(
            slabs * cores, planes, 2 * EXPERTS, depth, wide
        )
        expert_grad = lax.psum_scatter(expert_grad, LINE, scatter_dimension=0, tiled=True)[0]
        kept_half = lax.dynamic_index_in_dim(expert_grad, x_at, 0, False)
        sent_half = lax.dynamic_index_in_dim(expert_grad, 1 - x_at, 0, False)
        got_half = lax.ppermute(sent_half, "x", ((0, 1), (1, 0)))
        expert_grad = jnp.concatenate(
            [jnp.where(x_at == 0, kept_half, got_half), jnp.where(x_at == 0, got_half, kept_half)],
            axis=-1,
        )
        expert_shares[layer_index] = expert_grad.reshape(
            2, EXPERTS, depth, planes * wide
        ).astype(jnp.float32)
        middle_part, gain_list[2 * layer_index + 1] = jax.vjp(
            rms_norm, middle, gains_f[2 * layer_index + 1]
        )[1](normed_grad)
        middle_grad = stream_grad + middle_part
        branch_lane, answer = gather_project(
            middle_grad.astype(jnp.bfloat16), out_weights[layer_index], True, 16
        )
        answer = answer.reshape(lane, feature)
        out_proj = inner(mixed_low, branch_lane.reshape(lane, D)).astype(jnp.bfloat16)
        query_grad, far_grad, near_grad = attend_back(
            queries, far, near, places, log_total, mixed_t, answer, chunk
        )
        key_grad = collect_keys(far_grad, near_grad, 13).astype(jnp.bfloat16)
        qkv_grad = jnp.concatenate([key_grad, query_grad], axis=1)
        qkv_proj = inner(normed_lane.reshape(lane, D), qkv_grad).astype(jnp.bfloat16)
        qkv_proj = qkv_proj.reshape(slabs, planes, cores, sides, rows_of, 3 * feature)
        qkv_proj = qkv_proj.transpose(0, 2, 1, 3, 4, 5).reshape(
            slabs * cores, groups, rows_of, 3 * feature
        )
        out_proj = out_proj.reshape(slabs * cores, rows_of, groups, feature).transpose(0, 2, 1, 3)
        attn_pack = jnp.concatenate([qkv_proj, out_proj], axis=3)
        attn_packs[layer_index] = lax.psum_scatter(
            attn_pack, LINE, scatter_dimension=0, tiled=True
        )[0]
        normed_att_grad = project(
            qkv_grad.reshape(planes, sides, own, 3 * feature), qkv_weights[layer_index], True, 14
        )
        stream_part, gain_list[2 * layer_index] = jax.vjp(
            rms_norm, stream, gains_f[2 * layer_index]
        )[1](normed_att_grad)
        stream_grad = middle_grad + stream_part

    small = jnp.concatenate(
        [jnp.stack(router_list).transpose(1, 0, 2).reshape(D, -1), jnp.stack(gain_list).T], axis=1
    )
    small = small.reshape(devices, rows_of, -1).transpose(0, 2, 1)
    small = jnp.pad(small, ((0, 0), (0, 16 - small.shape[1]), (0, 128 - rows_of)))
    table_share, small = embed_back(
        stream_grad.astype(jnp.bfloat16), ints, table_grad, small, shard_rows, 7
    )
    table_share, small = table_share[:shard_rows], small[:, :rows_of]
    router_share = (
        small[: LAYERS * EXPERTS].reshape(LAYERS, EXPERTS, rows_of).transpose(0, 2, 1)
    )
    gain_share = small[LAYERS * EXPERTS : LAYERS * EXPERTS + 2 * LAYERS + 1]
    attn_pack = jnp.stack(attn_packs, axis=1)
    qkv_share = lax.all_to_all(
        attn_pack[..., : 3 * feature], PLANE, split_axis=0, concat_axis=0, tiled=True
    )
    qkv_share = qkv_share.reshape(groups, LAYERS, rows_of, 3, feature)
    qkv_share = jnp.concatenate([qkv_share[:, :, :, 2:], qkv_share[:, :, :, :2]], axis=3)
    qkv_share = qkv_share.transpose(1, 2, 3, 0, 4).reshape(LAYERS, rows_of, 3 * D)
    out_share = attn_pack[..., 3 * feature :].transpose(1, 2, 0, 3).reshape(LAYERS, rows_of, D)
    out_share = lax.ppermute(out_share, ALL, head_places(True))
    attn_share = jnp.concatenate([qkv_share, out_share], axis=2).astype(jnp.float32)
    up_share = jnp.stack([share[0] for share in expert_shares])
    down_share = jnp.stack([share[1] for share in expert_shares])
    shares = (table_share, attn_share, router_share, gain_share, up_share, down_share)
    squares = jnp.sum(table_share * table_share)
    for share_part in shares[1:]:
        squares = squares + jnp.sum(share_part * share_part)
    sums = jnp.pad(jnp.stack([squares, own_loss])[:, None], ((0, 6), (0, 127)))
    sums = jnp.sum(swap(sums[None], True, 9)[:, :2, 0], axis=0)
    square_total, loss_sum = sums[0], sums[1]
    grad_norm = jnp.sqrt(square_total)
    factor = CLIP_AT / jnp.maximum(grad_norm, CLIP_AT)
    weights = (vocab_table, attn_weights, router, norm_gains, expert_up, expert_down)
    firsts = (vocab_first, attn_first, router_first, gains_first, up_first, down_first)
    seconds = (vocab_second, attn_second, router_second, gains_second, up_second, down_second)
    results = [loss_sum, token_count, grad_norm]
    for number in range(6):
        results.extend(
            adam_update(
                weights[number],
                firsts[number],
                seconds[number],
                factor * shares[number],
                STEP_RATES[number],
                DECAY_RATES[number],
            )
        )
    return tuple(results)


def solution(mesh):
    blocks, sides = mesh.shape["blk"], mesh.shape["head"]
    fine = Mesh(mesh.devices.reshape(blocks // 4, 2, 2, sides), ALL)
    weight_specs = (
        (P(ALL, None),) * 3
        + (P(None, ALL, None),) * 3
        + (P(None, ALL, None),) * 3
        + (P(None, ALL),) * 3
        + (P(None, None, BLK, "head"),) * 6
    )
    return jax.shard_map(
        per_device,
        mesh=fine,
        in_specs=(P(BLK), P(BLK), P(), P(), P(None, BLK)) + weight_specs,
        out_specs=(P(), P(), P()) + weight_specs,
        check_vma=False,
    )
```

```python
import functools

import jax
import jax.numpy as jnp
from jax import lax
from jax.experimental import pallas as pl
from jax.experimental.pallas import tpu as pltpu
from jax.sharding import Mesh, PartitionSpec as P

D = 768
HEADS = 12
HEAD_DIM = 64
EXPERTS = 2
LAYERS = 2
PROMPT = 2048
STEP = 10

NORM_EPS = 1e-06
BETA_ONE = 0.9
BETA_TWO = 0.95
ADAM_EPS = 1e-08
CLIP_AT = 0.01
MASKED = -1e30
STEP_RATES = (2.0, 0.25, 0.04, 0.4, 0.04, 0.04)
DECAY_RATES = (0.01, 0.01, 0.01, 0.0, 0.01, 0.01)

ALL = ("z", "x", "core", "head")
BLK = ("z", "x", "core")
PLANE = ("x", "head")
LINE = ("z", "core")
MIB = 2**20
MESH = pl.DeviceIdType.MESH
ANY = pl.BlockSpec(memory_space=pl.ANY)
VMEM = pl.BlockSpec(memory_space=pltpu.VMEM)


def rms_norm(stream, gain):
    return stream * lax.rsqrt(jnp.mean(stream * stream, axis=-1, keepdims=True) + NORM_EPS) * gain


def segment_of(position, cont_ends):
    later = jnp.sum((cont_ends[None, :] <= (position - PROMPT)[:, None]).astype(jnp.int32), axis=1)
    return jnp.where(position < PROMPT, 0, 1 + later)


def place():
    return tuple(lax.axis_index(name) for name in ALL)


def sizes():
    return tuple(lax.axis_size(name) for name in ALL)


def remote(source, target, send, receive, device):
    return pltpu.make_async_remote_copy(
        src_ref=source, dst_ref=target, send_sem=send, recv_sem=receive,
        device_id=device, device_id_type=MESH,
    )


def greet(devices):
    barrier = pltpu.get_barrier_semaphore()
    for device in devices:
        pl.semaphore_signal(barrier, inc=1, device_id=device, device_id_type=MESH)
    pl.semaphore_wait(barrier, len(devices))


def around():
    z, x, c, y = place()
    return (z, x, c, y), (z, 1 - x, c, y), (z, x, c, 1 - y), (z, x, 1 - c, y)


def swap_kernel(broadcast, source, out, send_sem, receive_sem, own_sem):
    n_z, n_x, n_c, n_y = sizes()
    count = n_z * n_x * n_c * n_y
    z, x, c, y = place()
    me = ((z * n_x + x) * n_c + c) * n_y + y

    def device_of(index):
        return (
            index // (n_x * n_c * n_y), index // (n_c * n_y) % n_x, index // n_y % n_c, index % n_y
        )

    def taken(index):
        return source.at[0] if broadcast else source.at[index]

    barrier = pltpu.get_barrier_semaphore()

    def call(step, unused):
        other = lax.rem(me + step, count)
        pl.semaphore_signal(barrier, inc=1, device_id=device_of(other), device_id_type=MESH)
        return unused

    lax.fori_loop(1, count, call, 0)
    own = pltpu.make_async_copy(taken(me), out.at[me], own_sem)
    own.start()
    pl.semaphore_wait(barrier, count - 1)

    def copy(step):
        other = lax.rem(me + step, count)
        return remote(
            taken(other), out.at[me], send_sem.at[step], receive_sem.at[step], device_of(other)
        )

    def start(step, unused):
        copy(step).start()
        return unused

    def finish(step, unused):
        copy(step).wait()
        return unused

    lax.fori_loop(1, count, start, 0)
    lax.fori_loop(1, count, finish, 0)
    own.wait()


def swap(blocks, broadcast, collective_id):
    count = 1
    for size in sizes():
        count *= size
    return pl.pallas_call(
        functools.partial(swap_kernel, broadcast),
        out_shape=jax.ShapeDtypeStruct((count,) + blocks.shape[1:], blocks.dtype),
        in_specs=[VMEM],
        out_specs=VMEM,
        scratch_shapes=[
            pltpu.SemaphoreType.DMA((count,)),
            pltpu.SemaphoreType.DMA((count,)),
            pltpu.SemaphoreType.DMA,
        ],
        compiler_params=pltpu.CompilerParams(collective_id=collective_id, has_side_effects=True),
    )(blocks)


def total_of(*parts):
    total = parts[0].astype(jnp.float32)
    for part in parts[1:]:
        total = total + part.astype(jnp.float32)
    return total


PIECES = 4


def spread_kernel(
    prompt_slabs, own_rows, far, near, tail, z_send, z_recv, c_send, c_recv, n_send, n_recv, own_sem
):
    n_z = lax.axis_size("z")
    lane = own_rows.shape[0]
    chunk = lane // 2
    size = lane // PIECES
    (z, x, c, y), _, _, c_near = around()
    above, below = (z + 1, x, c, y), (z - 1, x, c, y)
    in_prompt = z < prompt_slabs
    takes_down = z < prompt_slabs - 1
    gives_down = (z > 0) & (z < prompt_slabs)

    barrier = pltpu.get_barrier_semaphore()
    pl.semaphore_signal(barrier, inc=1, device_id=c_near, device_id_type=MESH)

    @pl.when(z > 0)
    def _():
        pl.semaphore_signal(barrier, inc=1, device_id=below, device_id_type=MESH)

    @pl.when(takes_down)
    def _():
        pl.semaphore_signal(barrier, inc=1, device_id=above, device_id_type=MESH)

    first, second = pl.ds(0, chunk), pl.ds(chunk, chunk)
    own = [
        pltpu.make_async_copy(own_rows.at[first], near.at[1], own_sem.at[0]),
        pltpu.make_async_copy(own_rows.at[second], near.at[3], own_sem.at[1]),
    ]
    own_far = pltpu.make_async_copy(own_rows, far.at[jnp.minimum(z, prompt_slabs - 1), c], own_sem.at[2])
    own_edge = pltpu.make_async_copy(own_rows.at[first], near.at[0], own_sem.at[3])
    edge = (z == 0) & (c == 0)
    for copy in own:
        copy.start()

    @pl.when(in_prompt)
    def _():
        own_far.start()

    @pl.when(edge)
    def _():
        own_edge.start()

    pl.semaphore_wait(
        barrier, 1 + jnp.where(z < n_z - 1, 1, 0) + jnp.where(gives_down, 1, 0)
    )

    def part(index):
        return pl.ds(index * size, size)

    def z_copy(source, slab, index, up):
        return remote(
            source, far.at[slab, c, part(index)], z_send.at[slab, index, 1 if up else 0],
            z_recv.at[slab, index], above if up else below,
        )

    def c_copy(source, slab, index):
        return remote(
            source, far.at[slab, c, part(index)], c_send.at[slab, index], c_recv.at[slab, index], c_near
        )

    def t_copy():
        return remote(own_rows.at[second], tail, n_send.at[0], n_recv.at[0], above)

    def t_hand():
        return remote(tail, near.at[0], n_send.at[1], n_recv.at[1], c_near)

    def n_copy(half):
        slot = jnp.where(c == 0, 2 * half, 2)
        return remote(
            own_rows.at[pl.ds(half * chunk, chunk)], near.at[slot], n_send.at[2 + half], n_recv.at[2 + half],
            c_near,
        )

    @pl.when(in_prompt)
    def _():
        for index in range(PIECES):
            source = own_rows.at[part(index)]

            @pl.when(z < n_z - 1)
            def _():
                z_copy(source, z, index, True).start()

            @pl.when(z > 0)
            def _():
                z_copy(source, z, index, False).start()

            c_copy(source, z, index).start()

    @pl.when((c == 1) & (z < n_z - 1))
    def _():
        t_copy().start()

    n_copy(0).start()

    @pl.when(c == 0)
    def _():
        n_copy(1).start()

    for distance in range(1, n_z):
        low_slab, high_slab = z - distance, z + distance
        for index in range(PIECES):

            @pl.when((low_slab >= 0) & (low_slab < prompt_slabs))
            def _():
                source = far.at[low_slab, c, part(index)]
                z_copy(source, low_slab, index, True).wait_recv()

                @pl.when(z < n_z - 1)
                def _():
                    z_copy(source, low_slab, index, True).start()

                c_copy(source, low_slab, index).start()

            if distance < prompt_slabs:

                @pl.when(high_slab < prompt_slabs)
                def _():
                    source = far.at[high_slab, c, part(index)]
                    z_copy(source, high_slab, index, False).wait_recv()

                    @pl.when(z > 0)
                    def _():
                        z_copy(source, high_slab, index, False).start()

                    c_copy(source, high_slab, index).start()

    @pl.when((c == 1) & (z > 0))
    def _():
        t_copy().wait_recv()
        t_hand().start()
        t_hand().wait_send()

    @pl.when((c == 1) & (z < n_z - 1))
    def _():
        t_copy().wait_send()

    @pl.when((c == 0) & (z > 0))
    def _():
        t_hand().wait_recv()

    n_copy(0).wait_send()
    n_copy(0).wait_recv()

    @pl.when(c == 0)
    def _():
        n_copy(1).wait_send()

    @pl.when(c == 1)
    def _():
        n_copy(1).wait_recv()

    for slab in range(prompt_slabs):
        for index in range(PIECES):
            copy = c_copy(own_rows.at[part(index)], slab, index)
            copy.wait_send()
            copy.wait_recv()

            @pl.when((z < n_z - 1) & (slab <= z))
            def _():
                z_copy(own_rows.at[part(index)], slab, index, True).wait_send()

            @pl.when((z > 0) & (slab >= z))
            def _():
                z_copy(own_rows.at[part(index)], slab, index, False).wait_send()

    for copy in own:
        copy.wait()

    @pl.when(in_prompt)
    def _():
        own_far.wait()

    @pl.when(edge)
    def _():
        own_edge.wait()


def spread_keys(own_rows, prompt_rows, collective_id):
    lane, width = own_rows.shape
    slabs = prompt_rows // (2 * lane)
    dma = pltpu.SemaphoreType.DMA
    far, near, _ = pl.pallas_call(
        functools.partial(spread_kernel, slabs),
        out_shape=(
            jax.ShapeDtypeStruct((slabs, 2, lane, width), own_rows.dtype),
            jax.ShapeDtypeStruct((4, lane // 2, width), own_rows.dtype),
            jax.ShapeDtypeStruct((lane // 2, width), own_rows.dtype),
        ),
        in_specs=[VMEM],
        out_specs=(VMEM,) * 3,
        scratch_shapes=[
            dma((slabs, PIECES, 2)), dma((slabs, PIECES)), dma((slabs, PIECES)), dma((slabs, PIECES)),
            dma((4,)), dma((4,)), dma((4,)),
        ],
        compiler_params=pltpu.CompilerParams(collective_id=collective_id, has_side_effects=True),
    )(own_rows)
    return far.reshape(prompt_rows, width), near.reshape(2 * lane, width)


def collect_kernel(
    prompt_slabs, far, near, out, own, c_got, z_got, n_got, tail_pass, tail_got,
    c_send, c_recv, z_send, z_recv, n_send, n_recv,
):
    n_z = lax.axis_size("z")
    lane = out.shape[0]
    chunk = lane // 2
    size = lane // PIECES
    (z, x, c, y), _, _, c_near = around()
    above, below = (z + 1, x, c, y), (z - 1, x, c, y)

    barrier = pltpu.get_barrier_semaphore()
    pl.semaphore_signal(barrier, inc=1, device_id=c_near, device_id_type=MESH)

    @pl.when(z < n_z - 1)
    def _():
        pl.semaphore_signal(barrier, inc=1, device_id=above, device_id_type=MESH)

    pl.semaphore_wait(barrier, 1 + jnp.where(z > 0, 1, 0))

    def part(index):
        return pl.ds(index * size, size)

    def c_copy(slab, index):
        return remote(
            far.at[slab, 1 - c, part(index)], c_got.at[slab, part(index)], c_send.at[slab, index],
            c_recv.at[slab, index], c_near,
        )

    def z_copy(slab, index):
        return remote(
            own.at[slab, part(index)], z_got.at[slab, part(index)], z_send.at[slab, index],
            z_recv.at[slab, index], below,
        )

    def n_copy(half):
        slot = jnp.where(c == 0, 2, 2 * half)
        return remote(near.at[slot], n_got.at[half], n_send.at[half], n_recv.at[half], c_near)

    def t_hand():
        return remote(near.at[0], tail_pass, n_send.at[2], n_recv.at[2], c_near)

    def t_copy():
        return remote(tail_pass, tail_got, n_send.at[3], n_recv.at[3], below)

    for slab in range(prompt_slabs):
        for index in range(PIECES):
            c_copy(slab, index).start()
    n_copy(0).start()

    @pl.when(c == 1)
    def _():
        n_copy(1).start()

    @pl.when((c == 0) & (z > 0))
    def _():
        t_hand().start()

    for slab in range(prompt_slabs):
        for index in range(PIECES):
            c_copy(slab, index).wait_recv()
            rows = part(index)
            mine = total_of(far[slab, c, rows, :], c_got[slab, rows, :])

            @pl.when((z == n_z - 1) & (z > slab))
            def _():
                own[slab, rows, :] = mine.astype(jnp.bfloat16)
                z_copy(slab, index).start()

            @pl.when((z < n_z - 1) & (z > slab))
            def _():
                z_copy(slab, index).wait_recv()
                own[slab, rows, :] = total_of(mine, z_got[slab, rows, :]).astype(jnp.bfloat16)
                z_copy(slab, index).start()

            @pl.when((z < n_z - 1) & (z == slab))
            def _():
                z_copy(slab, index).wait_recv()
                out[rows, :] = total_of(mine, z_got[slab, rows, :])

            @pl.when((z == n_z - 1) & (z == slab))
            def _():
                out[rows, :] = mine

    @pl.when((c == 1) & (z > 0))
    def _():
        t_hand().wait_recv()
        t_copy().start()

    @pl.when(z >= prompt_slabs)
    def _():
        out[...] = jnp.zeros_like(out)

    n_copy(0).wait_recv()
    first, second = pl.ds(0, chunk), pl.ds(chunk, chunk)
    out[first, :] += total_of(near[1], n_got[0])
    out[second, :] += near[3].astype(jnp.float32)

    @pl.when(c == 0)
    def _():
        n_copy(1).wait_recv()
        out[second, :] += n_got[1].astype(jnp.float32)

    @pl.when((c == 1) & (z < n_z - 1))
    def _():
        t_copy().wait_recv()
        out[second, :] += tail_got[...].astype(jnp.float32)

    @pl.when((c == 1) & (z > 0))
    def _():
        t_copy().wait_send()

    @pl.when((c == 0) & (z > 0))
    def _():
        t_hand().wait_send()

    n_copy(0).wait_send()

    @pl.when(c == 1)
    def _():
        n_copy(1).wait_send()

    for slab in range(prompt_slabs):
        for index in range(PIECES):
            c_copy(slab, index).wait_send()

            @pl.when(z > slab)
            def _():
                z_copy(slab, index).wait_send()


def collect_keys(far, near, collective_id):
    prompt_rows, width = far.shape
    lane = near.shape[0] // 2
    slabs = prompt_rows // (2 * lane)
    dma = pltpu.SemaphoreType.DMA
    low = jnp.bfloat16
    return pl.pallas_call(
        functools.partial(collect_kernel, slabs),
        out_shape=jax.ShapeDtypeStruct((lane, width), jnp.float32),
        in_specs=[VMEM] * 2,
        out_specs=VMEM,
        scratch_shapes=[
            pltpu.VMEM((slabs, lane, width), low),
            pltpu.VMEM((slabs, lane, width), low),
            pltpu.VMEM((slabs, lane, width), low),
            pltpu.VMEM((2, lane // 2, width), low),
            pltpu.VMEM((lane // 2, width), low),
            pltpu.VMEM((lane // 2, width), low),
            dma((slabs, PIECES)), dma((slabs, PIECES)), dma((slabs, PIECES)), dma((slabs, PIECES)),
            dma((4,)), dma((4,)),
        ],
        compiler_params=pltpu.CompilerParams(
            collective_id=collective_id, has_side_effects=True, vmem_limit_bytes=20 * MIB
        ),
    )(far.astype(low).reshape(slabs, 2, lane, width), near.astype(low).reshape(4, lane // 2, width))


def greet_all():
    n_z, n_x, n_c, n_y = sizes()
    count = n_z * n_x * n_c * n_y
    barrier = pltpu.get_barrier_semaphore()

    def call(step, unused):
        pl.semaphore_signal(barrier, inc=1, device_id=device_after(step), device_id_type=MESH)
        return unused

    lax.fori_loop(1, count, call, 0)
    pl.semaphore_wait(barrier, count - 1)


def index_after(step):
    n_z, n_x, n_c, n_y = sizes()
    z, x, c, y = place()
    me = ((z * n_x + x) * n_c + c) * n_y + y
    return lax.rem(me + step, n_z * n_x * n_c * n_y)


def device_after(step):
    _, n_x, n_c, n_y = sizes()
    index = index_after(step)
    return (
        index // (n_x * n_c * n_y), index // (n_c * n_y) % n_x, index // n_y % n_c, index % n_y
    )


def greet_near():
    n_z = lax.axis_size("z")
    (z, x, c, y), x_near, y_near, c_near = around()
    barrier = pltpu.get_barrier_semaphore()
    for device in (x_near, y_near, c_near):
        pl.semaphore_signal(barrier, inc=1, device_id=device, device_id_type=MESH)

    @pl.when(z > 0)
    def _():
        pl.semaphore_signal(barrier, inc=1, device_id=(z - 1, x, c, y), device_id_type=MESH)

    @pl.when(z < n_z - 1)
    def _():
        pl.semaphore_signal(barrier, inc=1, device_id=(z + 1, x, c, y), device_id_type=MESH)

    pl.semaphore_wait(barrier, 3 + jnp.where(z > 0, 1, 0) + jnp.where(z < n_z - 1, 1, 0))


Z_PIECES = 4


def gather_sems():
    n_z = lax.axis_size("z")
    dma = pltpu.SemaphoreType.DMA
    return [
        dma((n_z, Z_PIECES, 2)), dma((n_z, Z_PIECES)), dma((n_z, 2)), dma((n_z, 2)), dma((n_z, 2)),
        dma((n_z, 2)), dma((n_z, 4)), dma((n_z, 4)), dma,
    ]


def gather_slabs(rows_in, out, sems, work, beside=lambda step: None):
    z_send, z_recv, x_send, x_recv, y_send, y_recv, c_send, c_recv, own_sem = sems
    n_z = lax.axis_size("z")
    half = rows_in.shape[0] // 2
    size = rows_in.shape[0] // Z_PIECES
    (z, x, c, y), x_near, y_near, c_near = around()
    low, high = pl.ds(0, half), pl.ds(half, half)
    everything = pl.ds(0, 2 * half)
    own = pltpu.make_async_copy(rows_in, out.at[z, x, c, y], own_sem)
    own.start()

    def block(origin, px, py, rows):
        return out.at[origin, px, c, py, rows]

    def z_copy(source, origin, index, up):
        rows = pl.ds(index * size, size)
        other = (z + 1, x, c, y) if up else (z - 1, x, c, y)
        return remote(
            source.at[rows], block(origin, x, y, rows), z_send.at[origin, index, 1 if up else 0],
            z_recv.at[origin, index], other,
        )

    def x_copy(source, origin):
        return remote(source, out.at[origin, x, c, y], x_send.at[origin, 0], x_recv.at[origin, 0], x_near)

    def y_copy(source, origin):
        return remote(source, out.at[origin, x, c, y], y_send.at[origin, 0], y_recv.at[origin, 0], y_near)

    def x_relay(origin):
        part = block(origin, x, 1 - y, high)
        return remote(part, part, x_send.at[origin, 1], x_recv.at[origin, 1], x_near)

    def y_relay(origin):
        part = block(origin, 1 - x, y, low)
        return remote(part, part, y_send.at[origin, 1], y_recv.at[origin, 1], y_near)

    def c_copy(source, origin, px, py):
        slot = px * 2 + py
        return remote(
            source, out.at[origin, px, c, py], c_send.at[origin, slot], c_recv.at[origin, slot], c_near
        )

    def column(origin):
        return out.at[origin, x, c, y]

    def spread(source, origin):
        x_copy(source, origin).start()
        y_copy(source, origin).start()
        c_copy(source, origin, x, y).start()

    def relay(origin):
        x_copy(column(origin), origin).wait_recv()
        y_relay(origin).start()
        y_copy(column(origin), origin).wait_recv()
        x_relay(origin).start()
        c_copy(block(origin, 1 - x, y, everything), origin, 1 - x, y).start()
        c_copy(block(origin, x, 1 - y, everything), origin, x, 1 - y).start()

    def finish(origin):
        x_relay(origin).wait_recv()
        y_relay(origin).wait_recv()
        c_copy(block(origin, 1 - x, 1 - y, everything), origin, 1 - x, 1 - y).start()

    def use(origin):
        for px in range(2):
            for py in range(2):
                c_copy(out.at[origin, px, c, py], origin, px, py).wait_recv()
        work(origin)

    def arrive(step):
        below, above = z - step, z + step

        @pl.when(below >= 0)
        def _():
            for index in range(Z_PIECES):
                z_copy(rows_in, below, index, True).wait_recv()

                @pl.when(z < n_z - 1)
                def _():
                    z_copy(column(below), below, index, True).start()

            spread(column(below), below)

        @pl.when(above < n_z)
        def _():
            for index in range(Z_PIECES):
                z_copy(rows_in, above, index, False).wait_recv()

                @pl.when(z > 0)
                def _():
                    z_copy(column(above), above, index, False).start()

            spread(column(above), above)

    for index in range(Z_PIECES):

        @pl.when(z < n_z - 1)
        def _():
            z_copy(rows_in, z, index, True).start()

        @pl.when(z > 0)
        def _():
            z_copy(rows_in, z, index, False).start()

    spread(rows_in, z)
    for step in range(1, n_z + 3):
        if step < n_z:
            arrive(step)
        for action, back in ((relay, 1), (finish, 2), (use, 3)):
            late = step - back
            if late == 0:
                if action is use:
                    own.wait()
                action(z)
            elif 0 < late < n_z:
                for origin in (z - late, z + late):

                    @pl.when((origin >= 0) & (origin < n_z))
                    def _():
                        action(origin)

        beside(step)

    def close(origin, unused):
        x_copy(rows_in, origin).wait_send()
        y_copy(rows_in, origin).wait_send()
        x_relay(origin).wait_send()
        y_relay(origin).wait_send()
        for px in range(2):
            for py in range(2):
                c_copy(out.at[origin, px, c, py], origin, px, py).wait_send()
        for index in range(Z_PIECES):

            @pl.when((z < n_z - 1) & (origin <= z))
            def _():
                z_copy(rows_in, origin, index, True).wait_send()

            @pl.when((z > 0) & (origin >= z))
            def _():
                z_copy(rows_in, origin, index, False).wait_send()

        return unused

    lax.fori_loop(0, n_z, close, 0)


def line_sems():
    n_z = lax.axis_size("z")
    dma = pltpu.SemaphoreType.DMA
    return [dma, dma, dma((n_z, 2)), dma((n_z, 2))]


def line_sum(pack, out, lanes, got, below, above, sems):
    c_send, c_recv, z_send, z_recv = sems
    n_z = lax.axis_size("z")
    (z, x, c, y), _, _, c_near = around()
    handed = remote(pack.at[1 - c], got, c_send, c_recv, c_near)

    def z_copy(slab, up):
        return remote(
            lanes.at[slab], below.at[slab] if up else above.at[slab], z_send.at[slab, 1 if up else 0],
            z_recv.at[slab, 1 if up else 0], (z + 1, x, c, y) if up else (z - 1, x, c, y),
        )

    handed.start()

    def merge():
        handed.wait()
        lanes[...] = total_of(pack[c], got[...]).astype(jnp.bfloat16)

    def hop(turn, step):
        high, low = n_z - 1 - turn, turn

        @pl.when((z == step - 1 - turn) & (z < high))
        def _():
            @pl.when(z > 0)
            def _():
                z_copy(high, True).wait_recv()
                lanes[high] = total_of(lanes[high], below[high]).astype(jnp.bfloat16)

            z_copy(high, True).start()

        @pl.when((n_z - 1 - z == step - 1 - turn) & (z > low))
        def _():
            @pl.when(z < n_z - 1)
            def _():
                z_copy(low, False).wait_recv()
                lanes[low] = total_of(lanes[low], above[low]).astype(jnp.bfloat16)

            z_copy(low, False).start()

    def beside(step):
        if step == 1:
            merge()
        if step < n_z:

            def body(turn, unused):
                hop(turn, step)
                return unused

            lax.fori_loop(0, n_z - 1, body, 0)

    def close():
        out[...] = lanes[z].astype(jnp.float32)

        @pl.when(z > 0)
        def _():
            z_copy(z, True).wait_recv()
            out[...] += below[z].astype(jnp.float32)

        @pl.when(z < n_z - 1)
        def _():
            z_copy(z, False).wait_recv()
            out[...] += above[z].astype(jnp.float32)

        def sent(slab, unused):
            @pl.when(slab > z)
            def _():
                z_copy(slab, True).wait_send()

            @pl.when(slab < z)
            def _():
                z_copy(slab, False).wait_send()

            return unused

        lax.fori_loop(0, n_z, sent, 0)

    return beside, close


def in_pairs(values, slab, px, pc, row):
    return jnp.concatenate([values[slab, px, pc, py, row : row + 1, :] for py in range(2)], axis=1)


def vocab_ids(extent, chunk, shard_rows):
    n_z, n_x, n_c, n_y = sizes()
    z, x, c, y = place()
    me = ((z * n_x + x) * n_c + c) * n_y + y
    rows = lax.broadcasted_iota(jnp.int32, (extent, chunk), 0)
    return rows + me * shard_rows


def logits_kernel(shard_rows, rows_in, table, ints, valid, out, logs, hits, *sems):
    extent = table.shape[0]
    chunk = 2 * rows_in.shape[0]
    scale = table.shape[1] ** (-0.5)
    greet_near()
    hits[...] = jnp.zeros_like(hits)

    def work(slab):
        def one(index, unused):
            px, pc = index // 2, index % 2
            rows = out[slab, px, pc].reshape(chunk, -1)
            value = outer(table[...], rows) * scale
            ids = vocab_ids(extent, chunk, shard_rows)
            inside = lax.broadcasted_iota(jnp.int32, (extent, chunk), 0) < shard_rows
            target = in_pairs(ints, slab, px, pc, 1).astype(jnp.int32)
            shown = in_pairs(valid, slab, px, pc, 0)
            hit = jnp.where((ids == target) & inside, value, 0.0)
            hits[...] += jnp.sum(hit, axis=0, keepdims=True) * shown
            value = jnp.where(inside, value, MASKED)
            peak = jnp.max(value, axis=0, keepdims=True)
            log = peak + jnp.log(jnp.sum(jnp.exp(value - peak), axis=0, keepdims=True))
            half = chunk // 2
            logs[slab, px, pc, 0] = log[:, :half]
            logs[slab, px, pc, 1] = log[:, half:]
            return unused

        lax.fori_loop(0, 4, one, 0)

    gather_slabs(rows_in, out, sems, work)


def gather_logits(rows, table, ints, valid, shard_rows, collective_id):
    own, width = rows.shape
    shape = sizes() + (own, width)
    return pl.pallas_call(
        functools.partial(logits_kernel, shard_rows),
        out_shape=(
            jax.ShapeDtypeStruct(shape, rows.dtype),
            jax.ShapeDtypeStruct(sizes() + (1, own), jnp.float32),
            jax.ShapeDtypeStruct((1, 2 * own), jnp.float32),
        ),
        in_specs=[VMEM] * 4,
        out_specs=(VMEM,) * 3,
        scratch_shapes=gather_sems(),
        compiler_params=pltpu.CompilerParams(
            collective_id=collective_id, has_side_effects=True,
            vmem_limit_bytes=lax.axis_size("z") * 2 * MIB + 20 * MIB,
        ),
    )(rows, table, ints, valid)


def embed_back_kernel(
    shard_rows, rows_in, ints, table_grad, smalls, pack, out, small_sum, pack_sum,
    slabs, small_got, lanes, got, below, above, *sems
):
    extent = out.shape[0]
    chunk = 2 * rows_in.shape[0]
    small_send, small_recv = sems[-6:-4]
    n_z, n_x, n_c, n_y = sizes()
    count = n_z * n_x * n_c * n_y
    me = index_after(0)
    greet_all()

    def small(step):
        return remote(
            smalls.at[index_after(step)], small_got.at[me], small_send.at[step], small_recv.at[step],
            device_after(step),
        )

    def each(action):
        def body(step, unused):
            action(step)
            return unused

        lax.fori_loop(1, count, body, 0)

    each(lambda step: small(step).start())
    beside, close_line = line_sum(pack, pack_sum, lanes, got, below, above, sems[-4:])
    small_got[me] = smalls[me]
    out[...] = table_grad[...]

    def work(slab):
        def one(index, unused):
            px, pc = index // 2, index % 2
            token = in_pairs(ints, slab, px, pc, 0).astype(jnp.int32)
            inside = lax.broadcasted_iota(jnp.int32, (extent, chunk), 0) < shard_rows
            hot = (vocab_ids(extent, chunk, shard_rows) == token) & inside
            hot = jnp.where(hot, 1.0, 0.0).astype(jnp.bfloat16)
            out[...] += matmul(hot, slabs[slab, px, pc].reshape(chunk, -1))
            return unused

        lax.fori_loop(0, 4, one, 0)

    gather_slabs(rows_in, slabs, sems[:-6], work, beside)
    close_line()
    each(lambda step: small(step).wait())
    small_sum[...] = jnp.sum(small_got[...], axis=0)


def embed_back(rows, ints, table_grad, smalls, pack, shard_rows, collective_id):
    own, width = rows.shape
    line = pack.shape[1:]
    count = smalls.shape[0]
    dma = pltpu.SemaphoreType.DMA
    return pl.pallas_call(
        functools.partial(embed_back_kernel, shard_rows),
        out_shape=(
            jax.ShapeDtypeStruct(table_grad.shape, jnp.float32),
            jax.ShapeDtypeStruct(smalls.shape[1:], jnp.float32),
            jax.ShapeDtypeStruct(line[1:], jnp.float32),
        ),
        in_specs=[VMEM] * 5,
        out_specs=(VMEM,) * 3,
        scratch_shapes=[
            pltpu.VMEM(sizes() + (own, width), rows.dtype), pltpu.VMEM(smalls.shape, jnp.float32),
            pltpu.VMEM(line, pack.dtype), pltpu.VMEM(line, pack.dtype),
            pltpu.VMEM(line, pack.dtype), pltpu.VMEM(line, pack.dtype),
        ] + gather_sems() + [dma((count,)), dma((count,))] + line_sems(),
        compiler_params=pltpu.CompilerParams(
            collective_id=collective_id, has_side_effects=True,
            vmem_limit_bytes=lax.axis_size("z") * 2 * MIB + 28 * MIB,
        ),
    )(rows, ints, table_grad, smalls, pack)


def slab_order():
    n_z = lax.axis_size("z")
    z = lax.axis_index("z")
    up, down = n_z - 1 - z, z
    longer, shorter = jnp.maximum(up, down), jnp.minimum(up, down)
    far_side = jnp.where(up >= down, 1, -1)

    def target(step):
        late = step - (longer - shorter)
        near_side = jnp.where(late % 2 == 0, far_side, -far_side)
        return jnp.where(
            late < 0, z + far_side * (longer - step), z + near_side * (shorter - late // 2)
        )

    return target


def scatter_scratch(rows, width):
    n_z, n_x, n_c, n_y = sizes()
    half = rows // 2
    low = jnp.bfloat16
    dma = pltpu.SemaphoreType.DMA
    return [
        pltpu.VMEM((n_z, n_x, n_y, rows, width), low),
        pltpu.VMEM((n_z, n_x, n_y, rows, width), low),
        pltpu.VMEM((n_z, n_x, n_y, rows, width), low),
        pltpu.VMEM((n_z, 2, half, width), low),
        pltpu.VMEM((n_z, 2, half, width), low),
        pltpu.VMEM((n_z, half, width), low),
        pltpu.VMEM((n_z, half, width), low),
        pltpu.VMEM((n_z, rows, width), low),
        pltpu.VMEM((n_z, rows, width), low),
        dma((n_z, 2)), dma((n_z, 2)), dma((n_z, 3)), dma((n_z, 3)), dma((n_z, 3)),
        dma((n_z, 3)), dma((n_z, 2)), dma((n_z, 2, 2)),
    ]


def scatter_slabs(out, scratch, before, make, after):
    (
        lanes, handed, c_got, x_got, y_got, x_last, y_last, below, above,
        c_send, c_recv, x_send, x_recv, y_send, y_recv, z_send, z_recv,
    ) = scratch
    n_z = lax.axis_size("z")
    rows = out.shape[0]
    half = rows // 2
    (z, x, c, y), x_near, y_near, c_near = around()
    halves = (pl.ds(0, half), pl.ds(half, half))
    low, high = halves
    target = slab_order()

    def c_copy(slab, px):
        return remote(
            handed.at[slab, px], c_got.at[slab, px], c_send.at[slab, px], c_recv.at[slab, px], c_near
        )

    def x_first(slab, part):
        block = lanes.at[slab, 1 - x, y if part == 0 else 1 - y, low]
        return remote(block, x_got.at[slab, part], x_send.at[slab, part], x_recv.at[slab, part], x_near)

    def y_first(slab, part):
        block = lanes.at[slab, x if part == 0 else 1 - x, 1 - y, high]
        return remote(block, y_got.at[slab, part], y_send.at[slab, part], y_recv.at[slab, part], y_near)

    def y_second(slab):
        block = lanes.at[slab, x, 1 - y, low]
        return remote(block, y_last.at[slab], y_send.at[slab, 2], y_recv.at[slab, 2], y_near)

    def x_second(slab):
        block = lanes.at[slab, 1 - x, y, high]
        return remote(block, x_last.at[slab], x_send.at[slab, 2], x_recv.at[slab, 2], x_near)

    def z_up(slab, part):
        return remote(
            lanes.at[slab, x, y, halves[part]], below.at[slab, halves[part]], z_send.at[slab, part],
            z_recv.at[slab, 0, part], (z + 1, x, c, y),
        )

    def z_down(slab, part):
        return remote(
            lanes.at[slab, x, y, halves[part]], above.at[slab, halves[part]], z_send.at[slab, part],
            z_recv.at[slab, 1, part], (z - 1, x, c, y),
        )

    def produce(step):
        slab = target(step)
        before(step)

        def hand(px, unused):
            handed[slab, px] = make(step, slab, px, 1 - c).reshape(2, rows, -1)
            c_copy(slab, px).start()
            return unused

        def keep(px, unused):
            lanes[slab, px] = make(step, slab, px, c).reshape(2, rows, -1)
            return unused

        lax.fori_loop(0, 2, hand, 0)
        lax.fori_loop(0, 2, keep, 0)

    def begin(step):
        slab = target(step)
        for px in range(2):
            c_copy(slab, px).wait_recv()

        def merge(px, py):
            lanes[slab, px, py] = total_of(lanes[slab, px, py], c_got[slab, px, py]).astype(jnp.bfloat16)

        merge(1 - x, 1 - y)
        x_first(slab, 1).start()
        y_first(slab, 1).start()
        merge(1 - x, y)
        x_first(slab, 0).start()
        merge(x, 1 - y)
        y_first(slab, 0).start()
        merge(x, y)
        after(step)

    def middle(step):
        slab = target(step)
        x_first(slab, 1).wait_recv()
        x_first(slab, 0).wait_send()
        y_first(slab, 0).wait_send()
        lanes[slab, x, 1 - y, low] = total_of(
            lanes[slab, x, 1 - y, low], x_got[slab, 1]
        ).astype(jnp.bfloat16)
        y_second(slab).start()
        y_first(slab, 1).wait_recv()
        lanes[slab, 1 - x, y, high] = total_of(
            lanes[slab, 1 - x, y, high], y_got[slab, 1]
        ).astype(jnp.bfloat16)
        x_second(slab).start()

    def finish(step):
        slab = target(step)
        for part in range(2):
            if part == 0:
                x_first(slab, 0).wait_recv()
                y_second(slab).wait_recv()
                value = total_of(lanes[slab, x, y, low], x_got[slab, 0], y_last[slab])
            else:
                y_first(slab, 0).wait_recv()
                x_second(slab).wait_recv()
                value = total_of(lanes[slab, x, y, high], y_got[slab, 0], x_last[slab])
            rows_of = halves[part]

            @pl.when(slab > z)
            def _():
                @pl.when(z == 0)
                def _():
                    lanes[slab, x, y, rows_of] = value.astype(jnp.bfloat16)

                @pl.when(z > 0)
                def _():
                    z_up(slab, part).wait_recv()
                    lanes[slab, x, y, rows_of] = total_of(value, below[slab, rows_of]).astype(jnp.bfloat16)

                z_up(slab, part).start()

            @pl.when(slab < z)
            def _():
                @pl.when(z == n_z - 1)
                def _():
                    lanes[slab, x, y, rows_of] = value.astype(jnp.bfloat16)

                @pl.when(z < n_z - 1)
                def _():
                    z_down(slab, part).wait_recv()
                    lanes[slab, x, y, rows_of] = total_of(value, above[slab, rows_of]).astype(jnp.bfloat16)

                z_down(slab, part).start()

            @pl.when(slab == z)
            def _():
                out[rows_of, :] = value

                @pl.when(z > 0)
                def _():
                    z_up(slab, part).wait_recv()
                    out[rows_of, :] += below[slab, rows_of].astype(jnp.float32)

                @pl.when(z < n_z - 1)
                def _():
                    z_down(slab, part).wait_recv()
                    out[rows_of, :] += above[slab, rows_of].astype(jnp.float32)

    def turn(step, unused):
        for action, back in ((produce, 0), (begin, 0), (middle, 1), (finish, 2)):

            @pl.when((step >= back) & (step < n_z + back))
            def _():
                action(step - back)

        return unused

    lax.fori_loop(0, n_z + 2, turn, 0)

    def close(slab, unused):
        for px in range(2):
            c_copy(slab, px).wait_send()
        x_first(slab, 1).wait_send()
        y_first(slab, 1).wait_send()
        x_second(slab).wait_send()
        y_second(slab).wait_send()
        for part in range(2):

            @pl.when(slab > z)
            def _():
                z_up(slab, part).wait_send()

            @pl.when(slab < z)
            def _():
                z_down(slab, part).wait_send()

        return unused

    lax.fori_loop(0, n_z, close, 0)


def embed_kernel(shard_rows, table, ints, out, *scratch):
    extent = table.shape[0]
    chunk = 2 * out.shape[0]
    greet_near()

    def make(step, slab, px, pc):
        token = in_pairs(ints, slab, px, pc, 0).astype(jnp.int32)
        inside = lax.broadcasted_iota(jnp.int32, (extent, chunk), 0) < shard_rows
        hot = (vocab_ids(extent, chunk, shard_rows) == token) & inside
        hot = jnp.where(hot, 1.0, 0.0).astype(jnp.bfloat16)
        return inner(hot, table[...]).astype(jnp.bfloat16)

    scatter_slabs(out, scratch, lambda step: None, make, lambda step: None)


def embed(table, ints, own, shard_rows, collective_id):
    width = table.shape[1]
    return pl.pallas_call(
        functools.partial(embed_kernel, shard_rows),
        out_shape=jax.ShapeDtypeStruct((own, width), jnp.float32),
        in_specs=[VMEM] * 2,
        out_specs=VMEM,
        scratch_shapes=scatter_scratch(own, width),
        compiler_params=pltpu.CompilerParams(
            collective_id=collective_id, has_side_effects=True,
            vmem_limit_bytes=lax.axis_size("z") * 3 * MIB + 12 * MIB,
        ),
    )(table, ints)


def vocab_back_kernel(
    shard_rows, rows_all, table, ints, logs, weights, out, table_grad, slab_rows, changes, slab_sem, *scratch
):
    extent, width = table.shape
    chunk = 2 * out.shape[0]
    scale = width ** (-0.5)
    n_z = lax.axis_size("z")
    target = slab_order()

    def load(step):
        return pltpu.make_async_copy(
            rows_all.at[target(step)], slab_rows.at[step % 2], slab_sem.at[step % 2]
        )

    load(0).start()
    greet_near()
    table_grad[...] = jnp.zeros_like(table_grad)

    def before(step):
        load(step).wait()

        @pl.when(step + 1 < n_z)
        def _():
            load(step + 1).start()

    def make(step, slab, px, pc):
        rows = slab_rows[step % 2, px, pc].reshape(chunk, width)
        value = outer(table[...], rows) * scale
        inside = lax.broadcasted_iota(jnp.int32, (extent, chunk), 0) < shard_rows
        aim = in_pairs(ints, slab, px, pc, 1).astype(jnp.int32)
        hot = jnp.where(vocab_ids(extent, chunk, shard_rows) == aim, 1.0, 0.0)
        change = jnp.exp(value - in_pairs(logs, slab, px, pc, 0)) - hot
        change = jnp.where(inside, change * in_pairs(weights, slab, px, pc, 0), 0.0)
        change = change.astype(jnp.bfloat16)
        changes[px, pc] = change
        return (inner(change, table[...]) * scale).astype(jnp.bfloat16)

    def after(step):
        def one(index, unused):
            px, pc = index // 2, index % 2
            rows = slab_rows[step % 2, px, pc].reshape(chunk, width)
            table_grad[...] += matmul(changes[px, pc], rows)
            return unused

        lax.fori_loop(0, 4, one, 0)

    scatter_slabs(out, scratch, before, make, after)
    table_grad[...] = table_grad[...] * scale


def vocab_back(rows_all, table, ints, logs, weights, shard_rows, collective_id):
    own, width = rows_all.shape[4:]
    extent = table.shape[0]
    n_z, n_x, n_c, n_y = sizes()
    return pl.pallas_call(
        functools.partial(vocab_back_kernel, shard_rows),
        out_shape=(
            jax.ShapeDtypeStruct((own, width), jnp.float32),
            jax.ShapeDtypeStruct((extent, width), jnp.float32),
        ),
        in_specs=[ANY] + [VMEM] * 4,
        out_specs=(VMEM,) * 2,
        scratch_shapes=[
            pltpu.VMEM((2, n_x, n_c, n_y, own, width), rows_all.dtype),
            pltpu.VMEM((n_x, n_c, extent, 2 * own), jnp.bfloat16),
            pltpu.SemaphoreType.DMA((2,)),
        ] + scatter_scratch(own, width),
        compiler_params=pltpu.CompilerParams(
            collective_id=collective_id, has_side_effects=True,
            vmem_limit_bytes=n_z * 3 * MIB + 24 * MIB if n_z <= 8 else 62 * MIB,
        ),
    )(rows_all, table, ints, logs, weights)


SQRT_HALF = 0.5**0.5
DENSITY = 0.3989422804014327


def matmul(left, right):
    return jnp.dot(left, right, preferred_element_type=jnp.float32)


def inner(left, right):
    return lax.dot_general(
        left, right, (((0,), (0,)), ((), ())), preferred_element_type=jnp.float32
    )


def outer(left, right):
    return lax.dot_general(
        left, right, (((1,), (1,)), ((), ())), preferred_element_type=jnp.float32
    )


def plane_gather(own_rows, blocks, send_sem, recv_sem):
    half = own_rows.shape[0] // 2
    (z, x, c, y), x_near, y_near, _ = around()
    low, high = pl.ds(0, half), pl.ds(half, half)

    def copy(slot, px, py, rows, source, device):
        target = blocks.at[px, py, rows]
        return remote(target if source is None else source.at[rows], target, send_sem.at[slot], recv_sem.at[slot], device)

    first = [
        copy(0, x, y, low, own_rows, x_near),
        copy(1, x, y, high, own_rows, y_near),
        copy(2, x, y, high, own_rows, x_near),
        copy(3, x, y, low, own_rows, y_near),
    ]
    relays = [copy(4, 1 - x, y, low, None, y_near), copy(5, x, 1 - y, high, None, x_near)]
    for each in first:
        each.start()

    def wait_near():
        first[0].wait_recv()
        relays[0].start()
        first[1].wait_recv()
        relays[1].start()

    def wait_x():
        first[2].wait_recv()

    def wait_y():
        first[3].wait_recv()

    def wait_diagonal():
        for each in relays:
            each.wait_recv()

    def close():
        for each in first + relays:
            each.wait_send()

    return wait_near, wait_x, wait_y, wait_diagonal, close


def plane_sum(parts, got, out, send_sem, recv_sem):
    (z, x, c, y), x_near, y_near, _ = around()
    diagonal = (z, 1 - x, c, 1 - y)
    copies = [
        remote(parts.at[device[1], device[3]], got.at[slot], send_sem.at[slot], recv_sem.at[slot], device)
        for slot, device in enumerate((x_near, y_near, diagonal))
    ]

    def close():
        for each in copies:
            each.wait_recv()
        out[...] = total_of(parts[x, y], got[0], got[1], got[2])
        for each in copies:
            each.wait_send()

    return copies, close


def experts_kernel(
    own_rows, route, up, down, out, wide, before, hidden, parts, got, g_send, g_recv, s_send, s_recv
):
    (z, x, c, y), x_near, y_near, _ = around()
    diagonal = (z, 1 - x, c, 1 - y)
    greet((x_near, y_near, diagonal))
    wait_near, wait_x, wait_y, wait_diagonal, close = plane_gather(own_rows, wide, g_send, g_recv)
    copies, finish = plane_sum(parts, got, out, s_send, s_recv)
    wide[x, y] = own_rows[...]

    def work(px, py):
        rows = wide[px, py]
        first = route[px, py] == 0
        value = jnp.where(first, matmul(rows, up[0]), matmul(rows, up[1]))
        before[px, py] = value
        active = 0.5 * value * (1.0 + lax.erf(value * SQRT_HALF))
        hidden_first = jnp.where(first, active, 0.0).astype(jnp.bfloat16)
        hidden_second = jnp.where(first, 0.0, active).astype(jnp.bfloat16)
        hidden[px, py] = active.astype(jnp.bfloat16)
        total = outer(hidden_first, down[0]) + outer(hidden_second, down[1])
        parts[px, py] = total.astype(jnp.bfloat16)

    work(x, y)
    wait_near()
    wait_x()
    work(1 - x, y)
    copies[0].start()
    wait_y()
    work(x, 1 - y)
    copies[1].start()
    wait_diagonal()
    work(1 - x, 1 - y)
    copies[2].start()
    finish()
    close()


def experts(own_rows, route, up, down, collective_id):
    _, n_x, _, n_y = sizes()
    own, width = own_rows.shape
    wide = up.shape[2]
    dma = pltpu.SemaphoreType.DMA
    low = jnp.bfloat16
    return pl.pallas_call(
        experts_kernel,
        out_shape=(
            jax.ShapeDtypeStruct((own, width), jnp.float32),
            jax.ShapeDtypeStruct((n_x, n_y, own, width), low),
            jax.ShapeDtypeStruct((n_x, n_y, own, wide), jnp.float32),
            jax.ShapeDtypeStruct((n_x, n_y, own, wide), low),
        ),
        in_specs=[VMEM] * 4,
        out_specs=(VMEM,) * 4,
        scratch_shapes=[
            pltpu.VMEM((n_x, n_y, own, width), low),
            pltpu.VMEM((3, own, width), low),
            dma((6,)), dma((6,)), dma((3,)), dma((3,)),
        ],
        compiler_params=pltpu.CompilerParams(
            collective_id=collective_id, has_side_effects=True, vmem_limit_bytes=20 * MIB
        ),
        cost_estimate=pl.CostEstimate(
            flops=8 * own * 4 * width * wide, bytes_accessed=8 * MIB, transcendentals=4 * own * wide
        ),
    )(own_rows, route, up, down)


def experts_back_kernel(
    own_rows, route, up, down, wide, before, hidden, out, grads,
    wide_grad, before_grad, parts, got, g_send, g_recv, s_send, s_recv,
):
    (z, x, c, y), x_near, y_near, _ = around()
    diagonal = (z, 1 - x, c, 1 - y)
    greet((x_near, y_near, diagonal))
    wait_near, wait_x, wait_y, wait_diagonal, close = plane_gather(own_rows, wide_grad, g_send, g_recv)
    copies, finish = plane_sum(parts, got, out, s_send, s_recv)
    wide_grad[x, y] = own_rows[...]

    def work(px, py):
        rows = wide_grad[px, py]
        first = route[px, py] == 0
        hidden_grad = jnp.where(first, matmul(rows, down[0]), matmul(rows, down[1]))
        value = before[px, py]
        slope = 0.5 * (1.0 + lax.erf(value * SQRT_HALF)) + value * (
            DENSITY * jnp.exp(-0.5 * value * value)
        )
        change = (hidden_grad * slope).astype(jnp.bfloat16)
        before_grad[px, py] = change
        change_first = jnp.where(first, change, 0)
        change_second = jnp.where(first, 0, change)
        total = outer(change_first, up[0]) + outer(change_second, up[1])
        parts[px, py] = total.astype(jnp.bfloat16)

    work(x, y)
    wait_near()
    wait_x()
    work(1 - x, y)
    copies[0].start()
    wait_y()
    work(x, 1 - y)
    copies[1].start()
    wait_diagonal()
    work(1 - x, 1 - y)
    copies[2].start()
    close()

    lane = 4 * own_rows.shape[0]
    rows = wide[...].reshape(lane, -1)
    grad_rows = wide_grad[...].reshape(lane, -1)
    first = route[...].reshape(lane, 1) == 0
    change = before_grad[...].reshape(lane, -1)
    active = hidden[...].reshape(lane, -1)
    low = jnp.bfloat16
    n_z, n_x, n_c, _ = sizes()
    depth = grads.shape[3]

    def keep(slot, value):
        value = value.astype(low)
        for pz in range(n_z):
            for px in range(n_x):
                for pc in range(n_c):
                    start = ((pz * n_x + px) * n_c + pc) * depth
                    grads[pz * n_c + pc, px, slot] = value[start : start + depth]

    keep(0, inner(rows, jnp.where(first, change, 0)))
    keep(1, inner(rows, jnp.where(first, 0, change)))
    keep(2, inner(grad_rows, jnp.where(first, active, 0)))
    keep(3, inner(grad_rows, jnp.where(first, 0, active)))
    finish()


def experts_back(own_rows, route, up, down, wide, before, hidden, collective_id):
    n_z, n_x, n_c, n_y = sizes()
    own, width = own_rows.shape
    units = up.shape[2]
    dma = pltpu.SemaphoreType.DMA
    low = jnp.bfloat16
    return pl.pallas_call(
        experts_back_kernel,
        out_shape=(
            jax.ShapeDtypeStruct((own, width), jnp.float32),
            jax.ShapeDtypeStruct((n_z * n_c, n_x, 4, width // (n_z * n_x * n_c), units), low),
        ),
        in_specs=[VMEM] * 7,
        out_specs=(VMEM,) * 2,
        scratch_shapes=[
            pltpu.VMEM((n_x, n_y, own, width), low),
            pltpu.VMEM((n_x, n_y, own, units), low),
            pltpu.VMEM((n_x, n_y, own, width), low),
            pltpu.VMEM((3, own, width), low),
            dma((6,)), dma((6,)), dma((3,)), dma((3,)),
        ],
        compiler_params=pltpu.CompilerParams(
            collective_id=collective_id, has_side_effects=True, vmem_limit_bytes=28 * MIB
        ),
        cost_estimate=pl.CostEstimate(
            flops=16 * own * 4 * width * units, bytes_accessed=12 * MIB, transcendentals=8 * own * units
        ),
    )(own_rows, route, up, down, wide, before, hidden)


def project_kernel(transposed, rows, weight, out, parts, got, s_send, s_recv):
    (z, x, c, y), x_near, y_near, _ = around()
    diagonal = (z, 1 - x, c, 1 - y)
    barrier = pltpu.get_barrier_semaphore()
    for device in (x_near, y_near, diagonal):
        pl.semaphore_signal(barrier, inc=1, device_id=device, device_id_type=MESH)
    copies, finish = plane_sum(parts, got, out, s_send, s_recv)

    def work(px, py):
        times = outer if transposed else matmul
        parts[px, py] = times(rows[px, py], weight[...]).astype(jnp.bfloat16)

    work(1 - x, 1 - y)
    pl.semaphore_wait(barrier, 3)
    copies[2].start()
    work(1 - x, y)
    copies[0].start()
    work(x, 1 - y)
    copies[1].start()
    work(x, y)
    finish()


def project(rows, weight, transposed, collective_id):
    n_x, n_y, own, depth = rows.shape
    width = weight.shape[0] if transposed else weight.shape[1]
    low = jnp.bfloat16
    dma = pltpu.SemaphoreType.DMA
    return pl.pallas_call(
        functools.partial(project_kernel, transposed),
        out_shape=jax.ShapeDtypeStruct((own, width), jnp.float32),
        in_specs=[VMEM] * 2,
        out_specs=VMEM,
        scratch_shapes=[
            pltpu.VMEM((n_x, n_y, own, width), low), pltpu.VMEM((3, own, width), low), dma((3,)), dma((3,)),
        ],
        compiler_params=pltpu.CompilerParams(
            collective_id=collective_id, has_side_effects=True, vmem_limit_bytes=10 * MIB
        ),
        cost_estimate=pl.CostEstimate(
            flops=8 * own * width * depth, bytes_accessed=4 * MIB, transcendentals=0
        ),
    )(rows, weight)


def gather_project_kernel(transposed, own_rows, weight, wide, out, g_send, g_recv):
    (z, x, c, y), x_near, y_near, _ = around()
    greet((x_near, y_near))
    wait_near, wait_x, wait_y, wait_diagonal, close = plane_gather(own_rows, wide, g_send, g_recv)
    wide[x, y] = own_rows[...]

    def work(px, py):
        times = outer if transposed else matmul
        out[px, py] = times(wide[px, py], weight[...]).astype(jnp.bfloat16)

    work(x, y)
    wait_near()
    wait_x()
    work(1 - x, y)
    wait_y()
    work(x, 1 - y)
    wait_diagonal()
    work(1 - x, 1 - y)
    close()


def gather_project(own_rows, weight, transposed, collective_id):
    _, n_x, _, n_y = sizes()
    own, width = own_rows.shape
    depth = weight.shape[0] if transposed else weight.shape[1]
    dma = pltpu.SemaphoreType.DMA
    low = jnp.bfloat16
    return pl.pallas_call(
        functools.partial(gather_project_kernel, transposed),
        out_shape=(
            jax.ShapeDtypeStruct((n_x, n_y, own, width), low),
            jax.ShapeDtypeStruct((n_x, n_y, own, depth), low),
        ),
        in_specs=[VMEM] * 2,
        out_specs=(VMEM,) * 2,
        scratch_shapes=[dma((6,)), dma((6,))],
        compiler_params=pltpu.CompilerParams(
            collective_id=collective_id, has_side_effects=True, vmem_limit_bytes=12 * MIB
        ),
        cost_estimate=pl.CostEstimate(
            flops=8 * own * width * depth, bytes_accessed=4 * MIB, transcendentals=0
        ),
    )(own_rows, weight)


def merge_logs_kernel(source, out, got, mine, send_one, recv_one, send_two, recv_two):
    n_z, n_x, n_c, n_y = sizes()
    count = n_z * n_x * n_c * n_y
    z, x, c, y = place()
    me = ((z * n_x + x) * n_c + c) * n_y + y

    def device_of(index):
        return (
            index // (n_x * n_c * n_y), index // (n_c * n_y) % n_x, index // n_y % n_c, index % n_y
        )

    barrier = pltpu.get_barrier_semaphore()

    def call(step, unused):
        other = lax.rem(me + step, count)
        pl.semaphore_signal(barrier, inc=1, device_id=device_of(other), device_id_type=MESH)
        return unused

    lax.fori_loop(1, count, call, 0)
    got[me] = source[me]
    pl.semaphore_wait(barrier, count - 1)

    def first(step):
        other = lax.rem(me + step, count)
        return remote(
            source.at[other], got.at[me], send_one.at[step], recv_one.at[step], device_of(other)
        )

    def second(step):
        other = lax.rem(me + step, count)
        return remote(mine, out.at[me], send_two.at[step], recv_two.at[step], device_of(other))

    def each(action):
        def body(step, unused):
            action(step)
            return unused

        lax.fori_loop(1, count, body, 0)

    each(lambda step: first(step).start())
    each(lambda step: first(step).wait())
    values = got[...]
    peak = jnp.max(values, axis=0)
    mine[...] = peak + jnp.log(jnp.sum(jnp.exp(values - peak[None]), axis=0))
    out[me] = mine[...]
    each(lambda step: second(step).start())
    each(lambda step: second(step).wait())


def merge_logs(blocks, collective_id):
    count = blocks.shape[0]
    dma = pltpu.SemaphoreType.DMA
    return pl.pallas_call(
        merge_logs_kernel,
        out_shape=jax.ShapeDtypeStruct(blocks.shape, blocks.dtype),
        in_specs=[VMEM],
        out_specs=VMEM,
        scratch_shapes=[
            pltpu.VMEM(blocks.shape, blocks.dtype), pltpu.VMEM(blocks.shape[1:], blocks.dtype),
            dma((count,)), dma((count,)), dma((count,)), dma((count,)),
        ],
        compiler_params=pltpu.CompilerParams(collective_id=collective_id, has_side_effects=True),
    )(blocks)


def key_position(index, part, chunk):
    lane = 2 * chunk
    start = (part // 2) * (2 * lane) + (part % 2) * chunk
    return start + index + jnp.where(index >= chunk, chunk, 0)


def near_shown(side, chunk, query_pos, query_seg, near_pos, near_seg):
    columns = slice(side * chunk, (side + 1) * chunk)
    rows = slice(2 * side * chunk, 2 * (side + 1) * chunk)
    shown = (
        (near_seg[rows, :] == query_seg[:, columns])
        & (near_pos[rows, :] <= query_pos[:, columns])
        & (near_pos[rows, :] >= PROMPT)
    )
    return columns, rows, shown


def attend_kernel(
    chunk, query, far, near, query_pos, query_seg, near_pos, near_seg,
    out, out_low, log_total, scores, far_t, near_t,
):
    lane, feature = query.shape
    group = feature // HEAD_DIM
    prompt_rows = far.shape[0]
    parts = prompt_rows // lane
    query_t = (query[...].astype(jnp.float32) * HEAD_DIM ** (-0.5)).T.astype(jnp.bfloat16)
    far_t[...] = far[...].astype(jnp.float32).T.astype(jnp.bfloat16)
    near_t[...] = near[...].astype(jnp.float32).T.astype(jnp.bfloat16)
    row_of = lax.broadcasted_iota(jnp.int32, (feature, lane), 0)
    q_pos = query_pos[...]

    for head in range(group):
        low, high = head * HEAD_DIM, (head + 1) * HEAD_DIM
        query_h = jnp.where((row_of >= low) & (row_of < high), query_t, 0)

        def score_part(part, peak):
            block = far[pl.ds(pl.multiple_of(part * lane, lane), lane), :feature]
            value = matmul(block, query_h)
            index = lax.broadcasted_iota(jnp.int32, (lane, lane), 0)
            value = jnp.where(key_position(index, part, chunk) <= q_pos, value, MASKED)
            scores[pl.ds(pl.multiple_of(part * lane, lane), lane), :] = value
            return jnp.maximum(peak, jnp.max(value, axis=0, keepdims=True))

        peak = lax.fori_loop(0, parts, score_part, jnp.full((1, lane), MASKED, jnp.float32))
        near_peaks = []
        for side in range(2):
            columns, rows, shown = near_shown(side, chunk, query_pos, query_seg, near_pos, near_seg)
            value = matmul(near[rows, :feature], query_h[:, columns])
            value = jnp.where(shown, value, MASKED)
            scores[prompt_rows : prompt_rows + lane, columns] = value
            near_peaks.append(jnp.max(value, axis=0, keepdims=True))
        peak = jnp.maximum(peak, jnp.concatenate(near_peaks, axis=1))

        def weigh_part(part, state):
            total, mixed = state
            start = pl.multiple_of(part * lane, lane)
            chance = jnp.exp(scores[pl.ds(start, lane), :] - peak)
            total = total + jnp.sum(chance, axis=0, keepdims=True)
            mixed = mixed + matmul(
                far_t[feature + low : feature + high, pl.ds(start, lane)],
                chance.astype(jnp.bfloat16),
            )
            return total, mixed

        total, mixed = lax.fori_loop(
            0,
            parts,
            weigh_part,
            (jnp.zeros((1, lane), jnp.float32), jnp.zeros((HEAD_DIM, lane), jnp.float32)),
        )
        near_total, near_mixed = [], []
        for side in range(2):
            columns = slice(side * chunk, (side + 1) * chunk)
            rows = slice(side * lane, (side + 1) * lane)
            chance = jnp.exp(scores[prompt_rows : prompt_rows + lane, columns] - peak[:, columns])
            near_total.append(jnp.sum(chance, axis=0, keepdims=True))
            near_mixed.append(
                matmul(near_t[feature + low : feature + high, rows], chance.astype(jnp.bfloat16))
            )
        total = total + jnp.concatenate(near_total, axis=1)
        mixed = mixed + jnp.concatenate(near_mixed, axis=1)
        out[low:high, :] = mixed / total
        log_total[head : head + 1, :] = peak + jnp.log(total)
    out_low[...] = out[...].T.astype(jnp.bfloat16)


def attend(queries, far, near, places, chunk):
    lane, feature = queries.shape
    prompt_rows = far.shape[0]
    group = feature // HEAD_DIM
    total_rows = prompt_rows + lane
    return pl.pallas_call(
        functools.partial(attend_kernel, chunk),
        out_shape=(
            jax.ShapeDtypeStruct((feature, lane), jnp.float32),
            jax.ShapeDtypeStruct((lane, feature), jnp.bfloat16),
            jax.ShapeDtypeStruct((group, lane), jnp.float32),
        ),
        in_specs=[VMEM] * 7,
        out_specs=(VMEM,) * 3,
        scratch_shapes=[
            pltpu.VMEM((total_rows, lane), jnp.float32),
            pltpu.VMEM((2 * feature, prompt_rows), jnp.bfloat16),
            pltpu.VMEM((2 * feature, 2 * lane), jnp.bfloat16),
        ],
        compiler_params=pltpu.CompilerParams(vmem_limit_bytes=20 * MIB),
        cost_estimate=pl.CostEstimate(
            flops=8 * group * lane * total_rows * 128,
            bytes_accessed=8 * MIB,
            transcendentals=group * lane * total_rows,
        ),
    )(queries, far, near, *places)


def attend_back_kernel(
    chunk, query, far, near, query_pos, query_seg, near_pos, near_seg,
    log_total, mixed, answer, query_grad, far_grad, near_grad,
    far_t, near_t, far_values, near_values, far_sum, near_sum, query_sum,
):
    lane, feature = query.shape
    group = feature // HEAD_DIM
    prompt_rows = far.shape[0]
    parts = prompt_rows // lane
    scaled = (query[...].astype(jnp.float32) * HEAD_DIM ** (-0.5)).astype(jnp.bfloat16)
    query_t = scaled.astype(jnp.float32).T.astype(jnp.bfloat16)
    answers = answer[...]
    answer_t = answers.astype(jnp.float32).T.astype(jnp.bfloat16)
    far_t[...] = far[:, :feature].astype(jnp.float32).T.astype(jnp.bfloat16)
    near_t[...] = near[:, :feature].astype(jnp.float32).T.astype(jnp.bfloat16)
    far_values[...] = far[:, feature:]
    near_values[...] = near[:, feature:]
    row_of = lax.broadcasted_iota(jnp.int32, (feature, lane), 0)
    column_of = lax.broadcasted_iota(jnp.int32, (lane, feature), 1)
    q_pos = query_pos[...]

    for head in range(group):
        low, high = head * HEAD_DIM, (head + 1) * HEAD_DIM
        in_rows = (row_of >= low) & (row_of < high)
        in_columns = (column_of >= low) & (column_of < high)
        query_ht = jnp.where(in_rows, query_t, 0)
        answer_ht = jnp.where(in_rows, answer_t, 0)
        query_h = jnp.where(in_columns, scaled, 0)
        answer_h = jnp.where(in_columns, answers, 0)
        log_h = log_total[head : head + 1, :]
        delta_h = jnp.sum(
            answer_t[low:high, :].astype(jnp.float32) * mixed[low:high, :], axis=0, keepdims=True
        )

        def slopes(key_block, value_block, shown, columns):
            value = matmul(key_block, query_ht[:, columns])
            chance = jnp.exp(jnp.where(shown, value - log_h[:, columns], MASKED))
            slope = matmul(value_block, answer_ht[:, columns])
            change = (chance * (slope - delta_h[:, columns])).astype(jnp.bfloat16)
            chance = chance.astype(jnp.bfloat16)
            return change, matmul(change, query_h[columns]), matmul(chance, answer_h[columns])

        def add(sums, rows, key_part, value_part):
            if head == 0:
                sums[0, rows, :] = key_part
                sums[1, rows, :] = value_part
            else:
                sums[0, rows, :] += key_part
                sums[1, rows, :] += value_part

        def back_part(part, total):
            rows = pl.ds(pl.multiple_of(part * lane, lane), lane)
            index = lax.broadcasted_iota(jnp.int32, (lane, lane), 0)
            shown = key_position(index, part, chunk) <= q_pos
            change, key_part, value_part = slopes(
                far[rows, :feature], far_values[rows, :], shown, slice(0, lane)
            )
            add(far_sum, rows, key_part, value_part)
            return total + matmul(far_t[low:high, rows], change)

        total = lax.fori_loop(0, parts, back_part, jnp.zeros((HEAD_DIM, lane), jnp.float32))
        near_total = []
        for side in range(2):
            columns, rows, shown = near_shown(side, chunk, query_pos, query_seg, near_pos, near_seg)
            change, key_part, value_part = slopes(
                near[rows, :feature], near_values[rows, :], shown, columns
            )
            add(near_sum, rows, key_part, value_part)
            near_total.append(matmul(near_t[low:high, rows], change))
        query_sum[low:high, :] = (total + jnp.concatenate(near_total, axis=1)) * HEAD_DIM ** (-0.5)
    query_grad[...] = query_sum[...].T.astype(jnp.bfloat16)
    for sums, grad in ((far_sum, far_grad), (near_sum, near_grad)):
        grad[...] = jnp.concatenate(
            [sums[0].astype(jnp.bfloat16), sums[1].astype(jnp.bfloat16)], axis=1
        )


def attend_back(queries, far, near, places, log_total, mixed, answer, chunk):
    lane, feature = queries.shape
    prompt_rows = far.shape[0]
    group = feature // HEAD_DIM
    total_rows = prompt_rows + lane
    low = jnp.bfloat16
    return pl.pallas_call(
        functools.partial(attend_back_kernel, chunk),
        out_shape=(
            jax.ShapeDtypeStruct((lane, feature), low),
            jax.ShapeDtypeStruct((prompt_rows, 2 * feature), low),
            jax.ShapeDtypeStruct((2 * lane, 2 * feature), low),
        ),
        in_specs=[VMEM] * 10,
        out_specs=(VMEM,) * 3,
        scratch_shapes=[
            pltpu.VMEM((feature, prompt_rows), low),
            pltpu.VMEM((feature, 2 * lane), low),
            pltpu.VMEM((prompt_rows, feature), low),
            pltpu.VMEM((2 * lane, feature), low),
            pltpu.VMEM((2, prompt_rows, feature), jnp.float32),
            pltpu.VMEM((2, 2 * lane, feature), jnp.float32),
            pltpu.VMEM((feature, lane), jnp.float32),
        ],
        compiler_params=pltpu.CompilerParams(vmem_limit_bytes=28 * MIB),
        cost_estimate=pl.CostEstimate(
            flops=20 * group * lane * total_rows * 128,
            bytes_accessed=12 * MIB,
            transcendentals=group * lane * total_rows,
        ),
    )(queries, far, near, *places, log_total, mixed, answer)


def head_places(back):
    n_z, n_x, n_c, n_y = sizes()
    line = n_z * n_c
    pairs = []
    for device in range(line * n_x * n_y):
        group, at = device // line, device % line
        place_of = ((at // n_c * n_x + group // n_y) * n_c + at % n_c) * n_y + group % n_y
        pairs.append((place_of, device) if back else (device, place_of))
    return tuple(pairs)


def pad_rows(block):
    return jnp.pad(block, ((0, 8 - block.shape[0]), (0, 0)))


def adam_update(weight, moment_one, moment_two, gradient, step_rate, decay_rate):
    first_new = BETA_ONE * moment_one + (1.0 - BETA_ONE) * gradient
    second_new = BETA_TWO * moment_two + (1.0 - BETA_TWO) * gradient * gradient
    normalized = (
        first_new
        / (1.0 - BETA_ONE**STEP)
        / (jnp.sqrt(second_new / (1.0 - BETA_TWO**STEP)) + ADAM_EPS)
    )
    return (weight - step_rate * (normalized + decay_rate * weight), first_new, second_new)


def per_device(
    token_ids,
    targets,
    valid_mask,
    cont_lengths,
    routes,
    vocab_table,
    vocab_first,
    vocab_second,
    attn_weights,
    attn_first,
    attn_second,
    router,
    router_first,
    router_second,
    norm_gains,
    gains_first,
    gains_second,
    expert_up,
    up_first,
    up_second,
    expert_down,
    down_first,
    down_second,
):
    slabs = lax.axis_size("z")
    planes = lax.axis_size("x")
    cores = lax.axis_size("core")
    sides = lax.axis_size("head")
    groups = planes * sides
    z_at, x_at, core_at, side_at = (lax.axis_index(name) for name in ALL)
    blk_at = (z_at * planes + x_at) * cores + core_at
    device_at = blk_at * sides + side_at
    group_at = x_at * sides + side_at
    tokens = valid_mask.shape[0]
    chunk = token_ids.shape[0]
    own = chunk // sides
    lane = planes * chunk
    feature = D // groups
    wide = expert_up.shape[3] // planes
    shard_rows = vocab_table.shape[0]
    logit_scale = D ** (-0.5)

    cont_ends = jnp.cumsum(cont_lengths)
    valid_f = valid_mask.astype(jnp.float32)
    token_count = jnp.sum(valid_mask).astype(jnp.float32)
    expert_ids = jnp.arange(EXPERTS, dtype=jnp.int32)

    own_ints = jnp.concatenate([token_ids[None], targets[None], routes], axis=0)
    own_ints = lax.dynamic_slice_in_dim(own_ints, side_at * own, own, axis=1).astype(jnp.float32)
    rows_of = attn_weights.shape[1]
    smalls = jnp.concatenate(
        [router.transpose(0, 2, 1).reshape(LAYERS * EXPERTS, rows_of), norm_gains], axis=0
    )
    smalls = smalls.astype(jnp.bfloat16).astype(jnp.float32)
    smalls = jnp.pad(smalls, ((0, 16 - smalls.shape[0]), (0, own - rows_of)))
    whole_f = swap(jnp.concatenate([pad_rows(own_ints), smalls], axis=0)[None], True, 1)
    attn_low = attn_weights.astype(jnp.bfloat16)
    qkv_send = attn_low[:, :, : 3 * D].reshape(LAYERS, rows_of, 3, groups, feature)
    qkv_send = jnp.concatenate([qkv_send[:, :, 1:], qkv_send[:, :, :1]], axis=2)
    qkv_send = qkv_send.transpose(3, 0, 1, 2, 4).reshape(groups, LAYERS, rows_of, 3 * feature)
    qkv_got = lax.all_to_all(qkv_send, PLANE, split_axis=0, concat_axis=0, tiled=True)
    out_rows = attn_low[:, :, 3 * D :]
    out_rows = lax.ppermute(out_rows, ALL, head_places(False))
    out_rows = out_rows.reshape(LAYERS, rows_of, groups, feature).transpose(2, 0, 1, 3)
    expert_send = jnp.stack([expert_up, expert_down], axis=1).astype(jnp.bfloat16)
    depth = expert_send.shape[3]
    expert_send = expert_send.reshape(LAYERS, 2 * EXPERTS, depth, planes, wide)
    expert_send = expert_send.transpose(3, 0, 1, 2, 4)
    expert_halves = []
    for layer_index in range(LAYERS):
        kept_half = lax.dynamic_index_in_dim(expert_send[:, layer_index], x_at, 0, False)
        sent_half = lax.dynamic_index_in_dim(expert_send[:, layer_index], 1 - x_at, 0, False)
        got_half = lax.ppermute(sent_half, "x", ((0, 1), (1, 0)))
        expert_halves.append((kept_half, got_half))
    whole_f, qkv_got, out_rows, expert_halves = lax.optimization_barrier(
        (whole_f, qkv_got, out_rows, expert_halves)
    )
    attn_pack = jnp.concatenate([qkv_got, out_rows], axis=3)
    expert_packs = []
    for kept_half, got_half in expert_halves:
        expert_packs.append(
            jnp.stack(
                [
                    jnp.where(x_at == 0, kept_half, got_half),
                    jnp.where(x_at == 0, got_half, kept_half),
                ]
            )
        )
    whole_f, attn_pack, expert_packs = lax.optimization_barrier((whole_f, attn_pack, expert_packs))
    attn_pack = lax.all_gather(attn_pack, LINE, axis=0)
    qkv_weights, out_weights = [], []
    for layer_index in range(LAYERS):
        block = attn_pack[:, :, layer_index]
        part = block[..., : 3 * feature].reshape(slabs, cores, planes, sides, rows_of, 3 * feature)
        qkv_weights.append(part.transpose(0, 2, 1, 3, 4, 5).reshape(D, 3 * feature))
        part = block[..., 3 * feature :]
        out_weights.append(part.transpose(0, 2, 1, 3).reshape(feature, D))

    def gather_experts(halves):
        block = lax.all_gather(halves, LINE, axis=0)
        block = block.reshape(slabs, cores, planes, 2, EXPERTS, depth, wide)
        return block.transpose(3, 4, 0, 2, 1, 5, 6).reshape(2, EXPERTS, D, wide)

    expert_weights = [gather_experts(expert_packs[0])]
    ints = whole_f.reshape(sizes() + whole_f.shape[1:])
    whole = whole_f[:, : 2 + LAYERS].astype(jnp.int32)
    smalls = whole_f[:, 8:, :rows_of].transpose(1, 0, 2).reshape(16, D)
    router_all = smalls[: LAYERS * EXPERTS].reshape(LAYERS, EXPERTS, D).transpose(0, 2, 1)
    router_all = router_all.astype(jnp.bfloat16)
    gains_f = smalls[LAYERS * EXPERTS :]
    routes_lane = lax.dynamic_index_in_dim(
        whole.reshape(slabs, planes, cores, sides, 2 + LAYERS, own), z_at, 0, False
    )
    routes_lane = lax.dynamic_index_in_dim(routes_lane, core_at, 1, False)[:, :, 2:]
    routes_lane = routes_lane.transpose(2, 0, 1, 3)[..., None]
    routes_own = lax.dynamic_slice_in_dim(routes, side_at * own, own, axis=1)

    extent = -(-shard_rows // 256) * 256
    table = jnp.pad(vocab_table.astype(jnp.bfloat16), ((0, extent - shard_rows), (0, 0)))
    offsets = jnp.arange(chunk, dtype=jnp.int32)
    first_blk = z_at * planes * cores + core_at
    query_pos = jnp.concatenate([(first_blk + cores * part) * chunk + offsets for part in range(planes)])
    near_blks = [first_blk - 1 + part for part in range(2 * planes)]
    near_pos = jnp.concatenate([blk * chunk + offsets for blk in near_blks])
    query_seg = segment_of(query_pos, cont_ends)
    near_seg = segment_of(near_pos, cont_ends)
    places = (query_pos[None, :], query_seg[None, :], near_pos[:, None], near_seg[:, None])

    stream = embed(table, ints, own, shard_rows, 2)

    kept = []
    for layer_index in range(LAYERS):
        up, down = expert_weights[layer_index][0], expert_weights[layer_index][1]
        normed_lane, qkv = gather_project(
            rms_norm(stream, gains_f[2 * layer_index]).astype(jnp.bfloat16),
            qkv_weights[layer_index], False, 3,
        )
        qkv = qkv.reshape(lane, 3 * feature)
        queries = qkv[:, 2 * feature :]
        far, near = spread_keys(qkv[:, : 2 * feature], PROMPT, 10)
        if layer_index + 1 < LAYERS:
            far, halves = lax.optimization_barrier((far, expert_packs[layer_index + 1]))
            expert_weights.append(gather_experts(halves))
        mixed_t, mixed_low, log_total = attend(queries, far, near, places, chunk)
        middle = stream + project(
            mixed_low.reshape(planes, sides, own, feature), out_weights[layer_index], False, 15
        )
        normed_two = rms_norm(middle, gains_f[2 * layer_index + 1]).astype(jnp.bfloat16)
        chance = jax.nn.softmax(matmul(normed_two, router_all[layer_index]), axis=-1)
        output, wide_rows, before, hidden = experts(
            normed_two, routes_lane[layer_index], up, down, 11
        )
        own_pick = (routes_own[layer_index][:, None] == expert_ids[None, :]).astype(jnp.float32)
        gate = jnp.sum(chance * own_pick, axis=1, keepdims=True)
        kept.append(
            (
                stream, normed_lane, queries, far, near, mixed_t, mixed_low, log_total, middle,
                normed_two, chance, wide_rows, before, hidden, output, own_pick, gate,
            )
        )
        stream = middle + gate * output

    final_gain = gains_f[2 * LAYERS]
    devices = tokens // own
    valid_rows = valid_f.reshape(sizes() + (1, own))
    final_all, row_logs, hits = gather_logits(
        rms_norm(stream, final_gain).astype(jnp.bfloat16), table, ints, valid_rows, shard_rows, 4
    )
    log_sums = merge_logs(row_logs.reshape(devices, 1, own), 5)
    log_sum = log_sums.reshape(tokens)
    own_log = lax.dynamic_slice_in_dim(log_sum, device_at * own, own)
    own_valid = lax.dynamic_slice_in_dim(valid_f, device_at * own, own)
    own_loss = jnp.sum(own_log * own_valid) - jnp.sum(hits)
    final_grad, table_grad = vocab_back(
        final_all, table, ints, log_sums.reshape(sizes() + (1, own)), valid_rows / token_count,
        shard_rows, 6,
    )
    stream_grad, final_gain_grad = jax.vjp(rms_norm, stream, final_gain)[1](final_grad)

    attn_packs = [None] * LAYERS
    router_list = [None] * LAYERS
    expert_shares = [None] * LAYERS
    gain_list = [None] * (2 * LAYERS + 1)
    gain_list[2 * LAYERS] = final_gain_grad
    for layer_index in reversed(range(LAYERS)):
        (
            stream, normed_lane, queries, far, near, mixed_t, mixed_low, log_total, middle,
            normed_two, chance, wide_rows, before, hidden, output, own_pick, gate,
        ) = kept[layer_index]
        up, down = expert_weights[layer_index][0], expert_weights[layer_index][1]
        out_grad = (gate * stream_grad).astype(jnp.bfloat16)
        chance_grad = jnp.sum(stream_grad * output, axis=1)[:, None] * own_pick
        choice_grad = chance * (chance_grad - jnp.sum(chance * chance_grad, axis=1, keepdims=True))
        router_list[layer_index] = jnp.dot(
            normed_two.astype(jnp.float32).T, choice_grad, precision=lax.Precision.HIGHEST
        )
        normed_grad = jnp.dot(
            choice_grad,
            router_all[layer_index].astype(jnp.float32).T,
            precision=lax.Precision.HIGHEST,
        )
        rows_grad, expert_grad = experts_back(
            out_grad, routes_lane[layer_index], up, down, wide_rows, before, hidden, 12
        )
        normed_grad = normed_grad + rows_grad
        expert_grad = lax.psum_scatter(expert_grad, LINE, scatter_dimension=0, tiled=True)[0]
        kept_half = lax.dynamic_index_in_dim(expert_grad, x_at, 0, False)
        sent_half = lax.dynamic_index_in_dim(expert_grad, 1 - x_at, 0, False)
        got_half = lax.ppermute(sent_half, "x", ((0, 1), (1, 0)))
        expert_grad = jnp.concatenate(
            [jnp.where(x_at == 0, kept_half, got_half), jnp.where(x_at == 0, got_half, kept_half)],
            axis=-1,
        )
        expert_shares[layer_index] = expert_grad.reshape(
            2, EXPERTS, depth, planes * wide
        ).astype(jnp.float32)
        middle_part, gain_list[2 * layer_index + 1] = jax.vjp(
            rms_norm, middle, gains_f[2 * layer_index + 1]
        )[1](normed_grad)
        middle_grad = stream_grad + middle_part
        branch_lane, answer = gather_project(
            middle_grad.astype(jnp.bfloat16), out_weights[layer_index], True, 16
        )
        answer = answer.reshape(lane, feature)
        out_proj = inner(mixed_low, branch_lane.reshape(lane, D)).astype(jnp.bfloat16)
        query_grad, far_grad, near_grad = attend_back(
            queries, far, near, places, log_total, mixed_t, answer, chunk
        )
        key_grad = collect_keys(far_grad, near_grad, 13).astype(jnp.bfloat16)
        qkv_grad = jnp.concatenate([key_grad, query_grad], axis=1)
        qkv_proj = inner(normed_lane.reshape(lane, D), qkv_grad).astype(jnp.bfloat16)
        qkv_proj = qkv_proj.reshape(slabs, planes, cores, sides, rows_of, 3 * feature)
        qkv_proj = qkv_proj.transpose(0, 2, 1, 3, 4, 5).reshape(
            slabs * cores, groups, rows_of, 3 * feature
        )
        out_proj = out_proj.reshape(slabs * cores, rows_of, groups, feature).transpose(0, 2, 1, 3)
        attn_packs[layer_index] = jnp.concatenate([qkv_proj, out_proj], axis=3)
        normed_att_grad = project(
            qkv_grad.reshape(planes, sides, own, 3 * feature), qkv_weights[layer_index], True, 14
        )
        stream_part, gain_list[2 * layer_index] = jax.vjp(
            rms_norm, stream, gains_f[2 * layer_index]
        )[1](normed_att_grad)
        stream_grad = middle_grad + stream_part

    small = jnp.concatenate(
        [jnp.stack(router_list).transpose(1, 0, 2).reshape(D, -1), jnp.stack(gain_list).T], axis=1
    )
    small = small.reshape(devices, rows_of, -1).transpose(0, 2, 1)
    small = jnp.pad(small, ((0, 0), (0, 16 - small.shape[1]), (0, 128 - rows_of)))
    attn_pack = jnp.stack(attn_packs, axis=2).reshape(slabs, cores, -1, D).transpose(1, 0, 2, 3)
    table_share, small, attn_pack = embed_back(
        stream_grad.astype(jnp.bfloat16), ints, table_grad, small, attn_pack, shard_rows, 7
    )
    attn_pack = attn_pack.reshape(groups, LAYERS, rows_of, D)
    table_share, small = table_share[:shard_rows], small[:, :rows_of]
    router_share = (
        small[: LAYERS * EXPERTS].reshape(LAYERS, EXPERTS, rows_of).transpose(0, 2, 1)
    )
    gain_share = small[LAYERS * EXPERTS : LAYERS * EXPERTS + 2 * LAYERS + 1]
    qkv_share = lax.all_to_all(
        attn_pack[..., : 3 * feature], PLANE, split_axis=0, concat_axis=0, tiled=True
    )
    qkv_share = qkv_share.reshape(groups, LAYERS, rows_of, 3, feature)
    qkv_share = jnp.concatenate([qkv_share[:, :, :, 2:], qkv_share[:, :, :, :2]], axis=3)
    qkv_share = qkv_share.transpose(1, 2, 3, 0, 4).reshape(LAYERS, rows_of, 3 * D)
    out_share = attn_pack[..., 3 * feature :].transpose(1, 2, 0, 3).reshape(LAYERS, rows_of, D)
    out_share = lax.ppermute(out_share, ALL, head_places(True))
    attn_share = jnp.concatenate([qkv_share, out_share], axis=2).astype(jnp.float32)
    up_share = jnp.stack([share[0] for share in expert_shares])
    down_share = jnp.stack([share[1] for share in expert_shares])
    shares = (table_share, attn_share, router_share, gain_share, up_share, down_share)
    squares = jnp.sum(table_share * table_share)
    for share_part in shares[1:]:
        squares = squares + jnp.sum(share_part * share_part)
    sums = jnp.pad(jnp.stack([squares, own_loss])[:, None], ((0, 6), (0, 127)))
    sums = jnp.sum(swap(sums[None], True, 9)[:, :2, 0], axis=0)
    square_total, loss_sum = sums[0], sums[1]
    grad_norm = jnp.sqrt(square_total)
    factor = CLIP_AT / jnp.maximum(grad_norm, CLIP_AT)
    weights = (vocab_table, attn_weights, router, norm_gains, expert_up, expert_down)
    firsts = (vocab_first, attn_first, router_first, gains_first, up_first, down_first)
    seconds = (vocab_second, attn_second, router_second, gains_second, up_second, down_second)
    results = [loss_sum, token_count, grad_norm]
    for number in range(6):
        results.extend(
            adam_update(
                weights[number],
                firsts[number],
                seconds[number],
                factor * shares[number],
                STEP_RATES[number],
                DECAY_RATES[number],
            )
        )
    return tuple(results)


def solution(mesh):
    blocks, sides = mesh.shape["blk"], mesh.shape["head"]
    fine = Mesh(mesh.devices.reshape(blocks // 4, 2, 2, sides), ALL)
    weight_specs = (
        (P(ALL, None),) * 3
        + (P(None, ALL, None),) * 3
        + (P(None, ALL, None),) * 3
        + (P(None, ALL),) * 3
        + (P(None, None, BLK, "head"),) * 6
    )
    return jax.shard_map(
        per_device,
        mesh=fine,
        in_specs=(P(BLK), P(BLK), P(), P(), P(None, BLK)) + weight_specs,
        out_specs=(P(), P(), P()) + weight_specs,
        check_vma=False,
    )
```

```python
import functools

import jax
import jax.numpy as jnp
from jax import lax
from jax.experimental import pallas as pl
from jax.experimental.pallas import tpu as pltpu
from jax.sharding import Mesh, PartitionSpec as P

D = 768
HEADS = 12
HEAD_DIM = 64
EXPERTS = 2
LAYERS = 2
PROMPT = 2048
STEP = 10

NORM_EPS = 1e-06
BETA_ONE = 0.9
BETA_TWO = 0.95
ADAM_EPS = 1e-08
CLIP_AT = 0.01
MASKED = -1e30
STEP_RATES = (2.0, 0.25, 0.04, 0.4, 0.04, 0.04)
DECAY_RATES = (0.01, 0.01, 0.01, 0.0, 0.01, 0.01)

ALL = ("z", "x", "core", "head")
BLK = ("z", "x", "core")
PLANE = ("x", "head")
LINE = ("z", "core")
MIB = 2**20
MESH = pl.DeviceIdType.MESH
ANY = pl.BlockSpec(memory_space=pl.ANY)
VMEM = pl.BlockSpec(memory_space=pltpu.VMEM)


def rms_norm(stream, gain):
    return stream * lax.rsqrt(jnp.mean(stream * stream, axis=-1, keepdims=True) + NORM_EPS) * gain


def segment_of(position, cont_ends):
    later = jnp.sum((cont_ends[None, :] <= (position - PROMPT)[:, None]).astype(jnp.int32), axis=1)
    return jnp.where(position < PROMPT, 0, 1 + later)


def place():
    return tuple(lax.axis_index(name) for name in ALL)


def sizes():
    return tuple(lax.axis_size(name) for name in ALL)


def remote(source, target, send, receive, device):
    return pltpu.make_async_remote_copy(
        src_ref=source, dst_ref=target, send_sem=send, recv_sem=receive,
        device_id=device, device_id_type=MESH,
    )


def greet(devices):
    barrier = pltpu.get_barrier_semaphore()
    for device in devices:
        pl.semaphore_signal(barrier, inc=1, device_id=device, device_id_type=MESH)
    pl.semaphore_wait(barrier, len(devices))


def around():
    z, x, c, y = place()
    return (z, x, c, y), (z, 1 - x, c, y), (z, x, c, 1 - y), (z, x, 1 - c, y)


def swap_kernel(broadcast, source, out, send_sem, receive_sem, own_sem):
    n_z, n_x, n_c, n_y = sizes()
    count = n_z * n_x * n_c * n_y
    z, x, c, y = place()
    me = ((z * n_x + x) * n_c + c) * n_y + y

    def device_of(index):
        return (
            index // (n_x * n_c * n_y), index // (n_c * n_y) % n_x, index // n_y % n_c, index % n_y
        )

    def taken(index):
        return source.at[0] if broadcast else source.at[index]

    barrier = pltpu.get_barrier_semaphore()

    def call(step, unused):
        other = lax.rem(me + step, count)
        pl.semaphore_signal(barrier, inc=1, device_id=device_of(other), device_id_type=MESH)
        return unused

    lax.fori_loop(1, count, call, 0)
    own = pltpu.make_async_copy(taken(me), out.at[me], own_sem)
    own.start()
    pl.semaphore_wait(barrier, count - 1)

    def copy(step):
        other = lax.rem(me + step, count)
        return remote(
            taken(other), out.at[me], send_sem.at[step], receive_sem.at[step], device_of(other)
        )

    def start(step, unused):
        copy(step).start()
        return unused

    def finish(step, unused):
        copy(step).wait()
        return unused

    lax.fori_loop(1, count, start, 0)
    lax.fori_loop(1, count, finish, 0)
    own.wait()


def swap(blocks, broadcast, collective_id):
    count = 1
    for size in sizes():
        count *= size
    return pl.pallas_call(
        functools.partial(swap_kernel, broadcast),
        out_shape=jax.ShapeDtypeStruct((count,) + blocks.shape[1:], blocks.dtype),
        in_specs=[VMEM],
        out_specs=VMEM,
        scratch_shapes=[
            pltpu.SemaphoreType.DMA((count,)),
            pltpu.SemaphoreType.DMA((count,)),
            pltpu.SemaphoreType.DMA,
        ],
        compiler_params=pltpu.CompilerParams(collective_id=collective_id, has_side_effects=True),
    )(blocks)


def total_of(*parts):
    total = parts[0].astype(jnp.float32)
    for part in parts[1:]:
        total = total + part.astype(jnp.float32)
    return total


PIECES = 4


def spread_kernel(
    prompt_slabs, own_rows, far, near, tail, z_send, z_recv, c_send, c_recv, n_send, n_recv, own_sem
):
    n_z = lax.axis_size("z")
    lane = own_rows.shape[0]
    chunk = lane // 2
    size = lane // PIECES
    (z, x, c, y), _, _, c_near = around()
    above, below = (z + 1, x, c, y), (z - 1, x, c, y)
    in_prompt = z < prompt_slabs
    takes_down = z < prompt_slabs - 1
    gives_down = (z > 0) & (z < prompt_slabs)

    barrier = pltpu.get_barrier_semaphore()
    pl.semaphore_signal(barrier, inc=1, device_id=c_near, device_id_type=MESH)

    @pl.when(z > 0)
    def _():
        pl.semaphore_signal(barrier, inc=1, device_id=below, device_id_type=MESH)

    @pl.when(takes_down)
    def _():
        pl.semaphore_signal(barrier, inc=1, device_id=above, device_id_type=MESH)

    first, second = pl.ds(0, chunk), pl.ds(chunk, chunk)
    own = [
        pltpu.make_async_copy(own_rows.at[first], near.at[1], own_sem.at[0]),
        pltpu.make_async_copy(own_rows.at[second], near.at[3], own_sem.at[1]),
    ]
    own_far = pltpu.make_async_copy(own_rows, far.at[jnp.minimum(z, prompt_slabs - 1), c], own_sem.at[2])
    own_edge = pltpu.make_async_copy(own_rows.at[first], near.at[0], own_sem.at[3])
    edge = (z == 0) & (c == 0)
    for copy in own:
        copy.start()

    @pl.when(in_prompt)
    def _():
        own_far.start()

    @pl.when(edge)
    def _():
        own_edge.start()

    pl.semaphore_wait(
        barrier, 1 + jnp.where(z < n_z - 1, 1, 0) + jnp.where(gives_down, 1, 0)
    )

    def part(index):
        return pl.ds(index * size, size)

    def z_copy(source, slab, index, up):
        return remote(
            source, far.at[slab, c, part(index)], z_send.at[slab, index, 1 if up else 0],
            z_recv.at[slab, index], above if up else below,
        )

    def c_copy(source, slab, index):
        return remote(
            source, far.at[slab, c, part(index)], c_send.at[slab, index], c_recv.at[slab, index], c_near
        )

    def t_copy():
        return remote(own_rows.at[second], tail, n_send.at[0], n_recv.at[0], above)

    def t_hand():
        return remote(tail, near.at[0], n_send.at[1], n_recv.at[1], c_near)

    def n_copy(half):
        slot = jnp.where(c == 0, 2 * half, 2)
        return remote(
            own_rows.at[pl.ds(half * chunk, chunk)], near.at[slot], n_send.at[2 + half], n_recv.at[2 + half],
            c_near,
        )

    @pl.when(in_prompt)
    def _():
        for index in range(PIECES):
            source = own_rows.at[part(index)]

            @pl.when(z < n_z - 1)
            def _():
                z_copy(source, z, index, True).start()

            @pl.when(z > 0)
            def _():
                z_copy(source, z, index, False).start()

            c_copy(source, z, index).start()

    @pl.when((c == 1) & (z < n_z - 1))
    def _():
        t_copy().start()

    n_copy(0).start()

    @pl.when(c == 0)
    def _():
        n_copy(1).start()

    for distance in range(1, n_z):
        low_slab, high_slab = z - distance, z + distance
        for index in range(PIECES):

            @pl.when((low_slab >= 0) & (low_slab < prompt_slabs))
            def _():
                source = far.at[low_slab, c, part(index)]
                z_copy(source, low_slab, index, True).wait_recv()

                @pl.when(z < n_z - 1)
                def _():
                    z_copy(source, low_slab, index, True).start()

                c_copy(source, low_slab, index).start()

            if distance < prompt_slabs:

                @pl.when(high_slab < prompt_slabs)
                def _():
                    source = far.at[high_slab, c, part(index)]
                    z_copy(source, high_slab, index, False).wait_recv()

                    @pl.when(z > 0)
                    def _():
                        z_copy(source, high_slab, index, False).start()

                    c_copy(source, high_slab, index).start()

    @pl.when((c == 1) & (z > 0))
    def _():
        t_copy().wait_recv()
        t_hand().start()
        t_hand().wait_send()

    @pl.when((c == 1) & (z < n_z - 1))
    def _():
        t_copy().wait_send()

    @pl.when((c == 0) & (z > 0))
    def _():
        t_hand().wait_recv()

    n_copy(0).wait_send()
    n_copy(0).wait_recv()

    @pl.when(c == 0)
    def _():
        n_copy(1).wait_send()

    @pl.when(c == 1)
    def _():
        n_copy(1).wait_recv()

    for slab in range(prompt_slabs):
        for index in range(PIECES):
            copy = c_copy(own_rows.at[part(index)], slab, index)
            copy.wait_send()
            copy.wait_recv()

            @pl.when((z < n_z - 1) & (slab <= z))
            def _():
                z_copy(own_rows.at[part(index)], slab, index, True).wait_send()

            @pl.when((z > 0) & (slab >= z))
            def _():
                z_copy(own_rows.at[part(index)], slab, index, False).wait_send()

    for copy in own:
        copy.wait()

    @pl.when(in_prompt)
    def _():
        own_far.wait()

    @pl.when(edge)
    def _():
        own_edge.wait()


def spread_keys(own_rows, prompt_rows, collective_id):
    lane, width = own_rows.shape
    slabs = prompt_rows // (2 * lane)
    dma = pltpu.SemaphoreType.DMA
    far, near, _ = pl.pallas_call(
        functools.partial(spread_kernel, slabs),
        out_shape=(
            jax.ShapeDtypeStruct((slabs, 2, lane, width), own_rows.dtype),
            jax.ShapeDtypeStruct((4, lane // 2, width), own_rows.dtype),
            jax.ShapeDtypeStruct((lane // 2, width), own_rows.dtype),
        ),
        in_specs=[VMEM],
        out_specs=(VMEM,) * 3,
        scratch_shapes=[
            dma((slabs, PIECES, 2)), dma((slabs, PIECES)), dma((slabs, PIECES)), dma((slabs, PIECES)),
            dma((4,)), dma((4,)), dma((4,)),
        ],
        compiler_params=pltpu.CompilerParams(collective_id=collective_id, has_side_effects=True),
    )(own_rows)
    return far.reshape(prompt_rows, width), near.reshape(2 * lane, width)


def collect_kernel(
    prompt_slabs, far, near, out, own, c_got, z_got, n_got, tail_pass, tail_got,
    c_send, c_recv, z_send, z_recv, n_send, n_recv,
):
    n_z = lax.axis_size("z")
    lane = out.shape[0]
    chunk = lane // 2
    size = lane // PIECES
    (z, x, c, y), _, _, c_near = around()
    above, below = (z + 1, x, c, y), (z - 1, x, c, y)

    barrier = pltpu.get_barrier_semaphore()
    pl.semaphore_signal(barrier, inc=1, device_id=c_near, device_id_type=MESH)

    @pl.when(z < n_z - 1)
    def _():
        pl.semaphore_signal(barrier, inc=1, device_id=above, device_id_type=MESH)

    pl.semaphore_wait(barrier, 1 + jnp.where(z > 0, 1, 0))

    def part(index):
        return pl.ds(index * size, size)

    def c_copy(slab, index):
        return remote(
            far.at[slab, 1 - c, part(index)], c_got.at[slab, part(index)], c_send.at[slab, index],
            c_recv.at[slab, index], c_near,
        )

    def z_copy(slab, index):
        return remote(
            own.at[slab, part(index)], z_got.at[slab, part(index)], z_send.at[slab, index],
            z_recv.at[slab, index], below,
        )

    def n_copy(half):
        slot = jnp.where(c == 0, 2, 2 * half)
        return remote(near.at[slot], n_got.at[half], n_send.at[half], n_recv.at[half], c_near)

    def t_hand():
        return remote(near.at[0], tail_pass, n_send.at[2], n_recv.at[2], c_near)

    def t_copy():
        return remote(tail_pass, tail_got, n_send.at[3], n_recv.at[3], below)

    for slab in range(prompt_slabs):
        for index in range(PIECES):
            c_copy(slab, index).start()
    n_copy(0).start()

    @pl.when(c == 1)
    def _():
        n_copy(1).start()

    @pl.when((c == 0) & (z > 0))
    def _():
        t_hand().start()

    for slab in range(prompt_slabs):
        for index in range(PIECES):
            c_copy(slab, index).wait_recv()
            rows = part(index)
            mine = total_of(far[slab, c, rows, :], c_got[slab, rows, :])

            @pl.when((z == n_z - 1) & (z > slab))
            def _():
                own[slab, rows, :] = mine.astype(jnp.bfloat16)
                z_copy(slab, index).start()

            @pl.when((z < n_z - 1) & (z > slab))
            def _():
                z_copy(slab, index).wait_recv()
                own[slab, rows, :] = total_of(mine, z_got[slab, rows, :]).astype(jnp.bfloat16)
                z_copy(slab, index).start()

            @pl.when((z < n_z - 1) & (z == slab))
            def _():
                z_copy(slab, index).wait_recv()
                out[rows, :] = total_of(mine, z_got[slab, rows, :])

            @pl.when((z == n_z - 1) & (z == slab))
            def _():
                out[rows, :] = mine

    @pl.when((c == 1) & (z > 0))
    def _():
        t_hand().wait_recv()
        t_copy().start()

    @pl.when(z >= prompt_slabs)
    def _():
        out[...] = jnp.zeros_like(out)

    n_copy(0).wait_recv()
    first, second = pl.ds(0, chunk), pl.ds(chunk, chunk)
    out[first, :] += total_of(near[1], n_got[0])
    out[second, :] += near[3].astype(jnp.float32)

    @pl.when(c == 0)
    def _():
        n_copy(1).wait_recv()
        out[second, :] += n_got[1].astype(jnp.float32)

    @pl.when((c == 1) & (z < n_z - 1))
    def _():
        t_copy().wait_recv()
        out[second, :] += tail_got[...].astype(jnp.float32)

    @pl.when((c == 1) & (z > 0))
    def _():
        t_copy().wait_send()

    @pl.when((c == 0) & (z > 0))
    def _():
        t_hand().wait_send()

    n_copy(0).wait_send()

    @pl.when(c == 1)
    def _():
        n_copy(1).wait_send()

    for slab in range(prompt_slabs):
        for index in range(PIECES):
            c_copy(slab, index).wait_send()

            @pl.when(z > slab)
            def _():
                z_copy(slab, index).wait_send()


def collect_keys(far, near, collective_id):
    prompt_rows, width = far.shape
    lane = near.shape[0] // 2
    slabs = prompt_rows // (2 * lane)
    dma = pltpu.SemaphoreType.DMA
    low = jnp.bfloat16
    return pl.pallas_call(
        functools.partial(collect_kernel, slabs),
        out_shape=jax.ShapeDtypeStruct((lane, width), jnp.float32),
        in_specs=[VMEM] * 2,
        out_specs=VMEM,
        scratch_shapes=[
            pltpu.VMEM((slabs, lane, width), low),
            pltpu.VMEM((slabs, lane, width), low),
            pltpu.VMEM((slabs, lane, width), low),
            pltpu.VMEM((2, lane // 2, width), low),
            pltpu.VMEM((lane // 2, width), low),
            pltpu.VMEM((lane // 2, width), low),
            dma((slabs, PIECES)), dma((slabs, PIECES)), dma((slabs, PIECES)), dma((slabs, PIECES)),
            dma((4,)), dma((4,)),
        ],
        compiler_params=pltpu.CompilerParams(
            collective_id=collective_id, has_side_effects=True, vmem_limit_bytes=20 * MIB
        ),
    )(far.astype(low).reshape(slabs, 2, lane, width), near.astype(low).reshape(4, lane // 2, width))


def greet_all():
    n_z, n_x, n_c, n_y = sizes()
    count = n_z * n_x * n_c * n_y
    barrier = pltpu.get_barrier_semaphore()

    def call(step, unused):
        pl.semaphore_signal(barrier, inc=1, device_id=device_after(step), device_id_type=MESH)
        return unused

    lax.fori_loop(1, count, call, 0)
    pl.semaphore_wait(barrier, count - 1)


def index_after(step):
    n_z, n_x, n_c, n_y = sizes()
    z, x, c, y = place()
    me = ((z * n_x + x) * n_c + c) * n_y + y
    return lax.rem(me + step, n_z * n_x * n_c * n_y)


def device_after(step):
    _, n_x, n_c, n_y = sizes()
    index = index_after(step)
    return (
        index // (n_x * n_c * n_y), index // (n_c * n_y) % n_x, index // n_y % n_c, index % n_y
    )


def greet_near():
    n_z = lax.axis_size("z")
    (z, x, c, y), x_near, y_near, c_near = around()
    barrier = pltpu.get_barrier_semaphore()
    for device in (x_near, y_near, c_near):
        pl.semaphore_signal(barrier, inc=1, device_id=device, device_id_type=MESH)

    @pl.when(z > 0)
    def _():
        pl.semaphore_signal(barrier, inc=1, device_id=(z - 1, x, c, y), device_id_type=MESH)

    @pl.when(z < n_z - 1)
    def _():
        pl.semaphore_signal(barrier, inc=1, device_id=(z + 1, x, c, y), device_id_type=MESH)

    pl.semaphore_wait(barrier, 3 + jnp.where(z > 0, 1, 0) + jnp.where(z < n_z - 1, 1, 0))


Z_PIECES = 4


def gather_sems():
    n_z = lax.axis_size("z")
    dma = pltpu.SemaphoreType.DMA
    return [
        dma((n_z, Z_PIECES, 2)), dma((n_z, Z_PIECES)), dma((n_z, 2)), dma((n_z, 2)), dma((n_z, 2)),
        dma((n_z, 2)), dma((n_z, 4)), dma((n_z, 4)), dma,
    ]


def gather_slabs(rows_in, out, sems, work, beside=lambda step: None):
    z_send, z_recv, x_send, x_recv, y_send, y_recv, c_send, c_recv, own_sem = sems
    n_z = lax.axis_size("z")
    half = rows_in.shape[0] // 2
    size = rows_in.shape[0] // Z_PIECES
    (z, x, c, y), x_near, y_near, c_near = around()
    low, high = pl.ds(0, half), pl.ds(half, half)
    everything = pl.ds(0, 2 * half)
    own = pltpu.make_async_copy(rows_in, out.at[z, x, c, y], own_sem)
    own.start()

    def block(origin, px, py, rows):
        return out.at[origin, px, c, py, rows]

    def z_copy(source, origin, index, up):
        rows = pl.ds(index * size, size)
        other = (z + 1, x, c, y) if up else (z - 1, x, c, y)
        return remote(
            source.at[rows], block(origin, x, y, rows), z_send.at[origin, index, 1 if up else 0],
            z_recv.at[origin, index], other,
        )

    def x_copy(source, origin):
        return remote(source, out.at[origin, x, c, y], x_send.at[origin, 0], x_recv.at[origin, 0], x_near)

    def y_copy(source, origin):
        return remote(source, out.at[origin, x, c, y], y_send.at[origin, 0], y_recv.at[origin, 0], y_near)

    def x_relay(origin):
        part = block(origin, x, 1 - y, high)
        return remote(part, part, x_send.at[origin, 1], x_recv.at[origin, 1], x_near)

    def y_relay(origin):
        part = block(origin, 1 - x, y, low)
        return remote(part, part, y_send.at[origin, 1], y_recv.at[origin, 1], y_near)

    def c_copy(source, origin, px, py):
        slot = px * 2 + py
        return remote(
            source, out.at[origin, px, c, py], c_send.at[origin, slot], c_recv.at[origin, slot], c_near
        )

    def column(origin):
        return out.at[origin, x, c, y]

    def spread(source, origin):
        x_copy(source, origin).start()
        y_copy(source, origin).start()
        c_copy(source, origin, x, y).start()

    def relay(origin):
        x_copy(column(origin), origin).wait_recv()
        y_relay(origin).start()
        y_copy(column(origin), origin).wait_recv()
        x_relay(origin).start()
        c_copy(block(origin, 1 - x, y, everything), origin, 1 - x, y).start()
        c_copy(block(origin, x, 1 - y, everything), origin, x, 1 - y).start()

    def finish(origin):
        x_relay(origin).wait_recv()
        y_relay(origin).wait_recv()
        c_copy(block(origin, 1 - x, 1 - y, everything), origin, 1 - x, 1 - y).start()

    def use(origin):
        for px in range(2):
            for py in range(2):
                c_copy(out.at[origin, px, c, py], origin, px, py).wait_recv()
        work(origin)

    def arrive(step):
        below, above = z - step, z + step

        @pl.when(below >= 0)
        def _():
            for index in range(Z_PIECES):
                z_copy(rows_in, below, index, True).wait_recv()

                @pl.when(z < n_z - 1)
                def _():
                    z_copy(column(below), below, index, True).start()

            spread(column(below), below)

        @pl.when(above < n_z)
        def _():
            for index in range(Z_PIECES):
                z_copy(rows_in, above, index, False).wait_recv()

                @pl.when(z > 0)
                def _():
                    z_copy(column(above), above, index, False).start()

            spread(column(above), above)

    for index in range(Z_PIECES):

        @pl.when(z < n_z - 1)
        def _():
            z_copy(rows_in, z, index, True).start()

        @pl.when(z > 0)
        def _():
            z_copy(rows_in, z, index, False).start()

    spread(rows_in, z)
    for step in range(1, n_z + 3):
        if step < n_z:
            arrive(step)
        for action, back in ((relay, 1), (finish, 2), (use, 3)):
            late = step - back
            if late == 0:
                if action is use:
                    own.wait()
                action(z)
            elif 0 < late < n_z:
                for origin in (z - late, z + late):

                    @pl.when((origin >= 0) & (origin < n_z))
                    def _():
                        action(origin)

        beside(step)

    def close(origin, unused):
        x_copy(rows_in, origin).wait_send()
        y_copy(rows_in, origin).wait_send()
        x_relay(origin).wait_send()
        y_relay(origin).wait_send()
        for px in range(2):
            for py in range(2):
                c_copy(out.at[origin, px, c, py], origin, px, py).wait_send()
        for index in range(Z_PIECES):

            @pl.when((z < n_z - 1) & (origin <= z))
            def _():
                z_copy(rows_in, origin, index, True).wait_send()

            @pl.when((z > 0) & (origin >= z))
            def _():
                z_copy(rows_in, origin, index, False).wait_send()

        return unused

    lax.fori_loop(0, n_z, close, 0)


def line_sems():
    n_z = lax.axis_size("z")
    dma = pltpu.SemaphoreType.DMA
    return [dma, dma, dma((n_z, 2)), dma((n_z, 2))]


def line_sum(pack, out, lanes, got, below, above, sems):
    c_send, c_recv, z_send, z_recv = sems
    n_z = lax.axis_size("z")
    (z, x, c, y), _, _, c_near = around()
    handed = remote(pack.at[1 - c], got, c_send, c_recv, c_near)

    def z_copy(slab, up):
        return remote(
            lanes.at[slab], below.at[slab] if up else above.at[slab], z_send.at[slab, 1 if up else 0],
            z_recv.at[slab, 1 if up else 0], (z + 1, x, c, y) if up else (z - 1, x, c, y),
        )

    handed.start()

    def merge():
        handed.wait()
        lanes[...] = total_of(pack[c], got[...]).astype(jnp.bfloat16)

    def hop(turn, step):
        high, low = n_z - 1 - turn, turn

        @pl.when((z == step - 1 - turn) & (z < high))
        def _():
            @pl.when(z > 0)
            def _():
                z_copy(high, True).wait_recv()
                lanes[high] = total_of(lanes[high], below[high]).astype(jnp.bfloat16)

            z_copy(high, True).start()

        @pl.when((n_z - 1 - z == step - 1 - turn) & (z > low))
        def _():
            @pl.when(z < n_z - 1)
            def _():
                z_copy(low, False).wait_recv()
                lanes[low] = total_of(lanes[low], above[low]).astype(jnp.bfloat16)

            z_copy(low, False).start()

    def beside(step):
        if step == 1:
            merge()
        if step < n_z:

            def body(turn, unused):
                hop(turn, step)
                return unused

            lax.fori_loop(0, n_z - 1, body, 0)

    def close():
        out[...] = lanes[z].astype(jnp.float32)

        @pl.when(z > 0)
        def _():
            z_copy(z, True).wait_recv()
            out[...] += below[z].astype(jnp.float32)

        @pl.when(z < n_z - 1)
        def _():
            z_copy(z, False).wait_recv()
            out[...] += above[z].astype(jnp.float32)

        def sent(slab, unused):
            @pl.when(slab > z)
            def _():
                z_copy(slab, True).wait_send()

            @pl.when(slab < z)
            def _():
                z_copy(slab, False).wait_send()

            return unused

        lax.fori_loop(0, n_z, sent, 0)

    return beside, close


def in_pairs(values, slab, px, pc, row):
    return jnp.concatenate([values[slab, px, pc, py, row : row + 1, :] for py in range(2)], axis=1)


def vocab_ids(extent, chunk, shard_rows):
    n_z, n_x, n_c, n_y = sizes()
    z, x, c, y = place()
    me = ((z * n_x + x) * n_c + c) * n_y + y
    rows = lax.broadcasted_iota(jnp.int32, (extent, chunk), 0)
    return rows + me * shard_rows


def logits_kernel(shard_rows, rows_in, table, ints, valid, out, logs, hits, *sems):
    extent = table.shape[0]
    chunk = 2 * rows_in.shape[0]
    scale = table.shape[1] ** (-0.5)
    greet_near()
    hits[...] = jnp.zeros_like(hits)

    def work(slab):
        def one(index, unused):
            px, pc = index // 2, index % 2
            rows = out[slab, px, pc].reshape(chunk, -1)
            value = outer(table[...], rows) * scale
            ids = vocab_ids(extent, chunk, shard_rows)
            inside = lax.broadcasted_iota(jnp.int32, (extent, chunk), 0) < shard_rows
            target = in_pairs(ints, slab, px, pc, 1).astype(jnp.int32)
            shown = in_pairs(valid, slab, px, pc, 0)
            hit = jnp.where(ids == target, value, 0.0)
            hits[...] += jnp.sum(hit, axis=0, keepdims=True) * shown
            value = jnp.where(inside, value, MASKED)
            peak = jnp.max(value, axis=0, keepdims=True)
            log = peak + jnp.log(jnp.sum(jnp.exp(value - peak), axis=0, keepdims=True))
            half = chunk // 2
            logs[slab, px, pc, 0] = log[:, :half]
            logs[slab, px, pc, 1] = log[:, half:]
            return unused

        lax.fori_loop(0, 4, one, 0)

    gather_slabs(rows_in, out, sems, work)


def gather_logits(rows, table, ints, valid, shard_rows, collective_id):
    own, width = rows.shape
    shape = sizes() + (own, width)
    return pl.pallas_call(
        functools.partial(logits_kernel, shard_rows),
        out_shape=(
            jax.ShapeDtypeStruct(shape, rows.dtype),
            jax.ShapeDtypeStruct(sizes() + (1, own), jnp.float32),
            jax.ShapeDtypeStruct((1, 2 * own), jnp.float32),
        ),
        in_specs=[VMEM] * 4,
        out_specs=(VMEM,) * 3,
        scratch_shapes=gather_sems(),
        compiler_params=pltpu.CompilerParams(
            collective_id=collective_id, has_side_effects=True,
            vmem_limit_bytes=lax.axis_size("z") * 2 * MIB + 20 * MIB,
        ),
    )(rows, table, ints, valid)


def embed_back_kernel(
    shard_rows, rows_in, ints, table_grad, smalls, pack, out, small_sum, pack_sum,
    slabs, small_got, lanes, got, below, above, *sems
):
    extent = out.shape[0]
    chunk = 2 * rows_in.shape[0]
    small_send, small_recv = sems[-6:-4]
    n_z, n_x, n_c, n_y = sizes()
    count = n_z * n_x * n_c * n_y
    me = index_after(0)
    greet_all()

    def small(step):
        return remote(
            smalls.at[index_after(step)], small_got.at[me], small_send.at[step], small_recv.at[step],
            device_after(step),
        )

    def each(action):
        def body(step, unused):
            action(step)
            return unused

        lax.fori_loop(1, count, body, 0)

    each(lambda step: small(step).start())
    beside, close_line = line_sum(pack, pack_sum, lanes, got, below, above, sems[-4:])
    small_got[me] = smalls[me]
    out[...] = table_grad[...]

    def work(slab):
        def one(index, unused):
            px, pc = index // 2, index % 2
            token = in_pairs(ints, slab, px, pc, 0).astype(jnp.int32)
            hot = vocab_ids(extent, chunk, shard_rows) == token
            hot = jnp.where(hot, 1.0, 0.0).astype(jnp.bfloat16)
            out[...] += matmul(hot, slabs[slab, px, pc].reshape(chunk, -1))
            return unused

        lax.fori_loop(0, 4, one, 0)

    gather_slabs(rows_in, slabs, sems[:-6], work, beside)
    close_line()
    each(lambda step: small(step).wait())
    small_sum[...] = jnp.sum(small_got[...], axis=0)


def embed_back(rows, ints, table_grad, smalls, pack, shard_rows, collective_id):
    own, width = rows.shape
    line = pack.shape[1:]
    count = smalls.shape[0]
    dma = pltpu.SemaphoreType.DMA
    return pl.pallas_call(
        functools.partial(embed_back_kernel, shard_rows),
        out_shape=(
            jax.ShapeDtypeStruct(table_grad.shape, jnp.float32),
            jax.ShapeDtypeStruct(smalls.shape[1:], jnp.float32),
            jax.ShapeDtypeStruct(line[1:], jnp.float32),
        ),
        in_specs=[VMEM] * 5,
        out_specs=(VMEM,) * 3,
        scratch_shapes=[
            pltpu.VMEM(sizes() + (own, width), rows.dtype), pltpu.VMEM(smalls.shape, jnp.float32),
            pltpu.VMEM(line, pack.dtype), pltpu.VMEM(line, pack.dtype),
            pltpu.VMEM(line, pack.dtype), pltpu.VMEM(line, pack.dtype),
        ] + gather_sems() + [dma((count,)), dma((count,))] + line_sems(),
        compiler_params=pltpu.CompilerParams(
            collective_id=collective_id, has_side_effects=True,
            vmem_limit_bytes=lax.axis_size("z") * 2 * MIB + 28 * MIB,
        ),
    )(rows, ints, table_grad, smalls, pack)


def slab_order():
    n_z = lax.axis_size("z")
    z = lax.axis_index("z")
    up, down = n_z - 1 - z, z
    longer, shorter = jnp.maximum(up, down), jnp.minimum(up, down)
    far_side = jnp.where(up >= down, 1, -1)

    def target(step):
        late = step - (longer - shorter)
        near_side = jnp.where(late % 2 == 0, far_side, -far_side)
        return jnp.where(
            late < 0, z + far_side * (longer - step), z + near_side * (shorter - late // 2)
        )

    return target


def scatter_scratch(rows, width):
    n_z, n_x, n_c, n_y = sizes()
    half = rows // 2
    low = jnp.bfloat16
    dma = pltpu.SemaphoreType.DMA
    return [
        pltpu.VMEM((n_z, n_x, n_y, rows, width), low),
        pltpu.VMEM((n_z, n_x, n_y, rows, width), low),
        pltpu.VMEM((n_z, n_x, n_y, rows, width), low),
        pltpu.VMEM((n_z, 2, half, width), low),
        pltpu.VMEM((n_z, 2, half, width), low),
        pltpu.VMEM((n_z, half, width), low),
        pltpu.VMEM((n_z, half, width), low),
        pltpu.VMEM((n_z, rows, width), low),
        pltpu.VMEM((n_z, rows, width), low),
        dma((n_z, 2)), dma((n_z, 2)), dma((n_z, 3)), dma((n_z, 3)), dma((n_z, 3)),
        dma((n_z, 3)), dma((n_z, 2)), dma((n_z, 2, 2)),
    ]


def scatter_slabs(out, scratch, before, make, after):
    (
        lanes, handed, c_got, x_got, y_got, x_last, y_last, below, above,
        c_send, c_recv, x_send, x_recv, y_send, y_recv, z_send, z_recv,
    ) = scratch
    n_z = lax.axis_size("z")
    rows = out.shape[0]
    half = rows // 2
    (z, x, c, y), x_near, y_near, c_near = around()
    halves = (pl.ds(0, half), pl.ds(half, half))
    low, high = halves
    target = slab_order()

    def c_copy(slab, px):
        return remote(
            handed.at[slab, px], c_got.at[slab, px], c_send.at[slab, px], c_recv.at[slab, px], c_near
        )

    def x_first(slab, part):
        block = lanes.at[slab, 1 - x, y if part == 0 else 1 - y, low]
        return remote(block, x_got.at[slab, part], x_send.at[slab, part], x_recv.at[slab, part], x_near)

    def y_first(slab, part):
        block = lanes.at[slab, x if part == 0 else 1 - x, 1 - y, high]
        return remote(block, y_got.at[slab, part], y_send.at[slab, part], y_recv.at[slab, part], y_near)

    def y_second(slab):
        block = lanes.at[slab, x, 1 - y, low]
        return remote(block, y_last.at[slab], y_send.at[slab, 2], y_recv.at[slab, 2], y_near)

    def x_second(slab):
        block = lanes.at[slab, 1 - x, y, high]
        return remote(block, x_last.at[slab], x_send.at[slab, 2], x_recv.at[slab, 2], x_near)

    def z_up(slab, part):
        return remote(
            lanes.at[slab, x, y, halves[part]], below.at[slab, halves[part]], z_send.at[slab, part],
            z_recv.at[slab, 0, part], (z + 1, x, c, y),
        )

    def z_down(slab, part):
        return remote(
            lanes.at[slab, x, y, halves[part]], above.at[slab, halves[part]], z_send.at[slab, part],
            z_recv.at[slab, 1, part], (z - 1, x, c, y),
        )

    def produce(step):
        slab = target(step)
        before(step)

        def hand(px, unused):
            handed[slab, px] = make(step, slab, px, 1 - c).reshape(2, rows, -1)
            c_copy(slab, px).start()
            return unused

        def keep(px, unused):
            lanes[slab, px] = make(step, slab, px, c).reshape(2, rows, -1)
            return unused

        lax.fori_loop(0, 2, hand, 0)
        lax.fori_loop(0, 2, keep, 0)

    def begin(step):
        slab = target(step)
        for px in range(2):
            c_copy(slab, px).wait_recv()

        def merge(px, py):
            lanes[slab, px, py] = total_of(lanes[slab, px, py], c_got[slab, px, py]).astype(jnp.bfloat16)

        merge(1 - x, 1 - y)
        x_first(slab, 1).start()
        y_first(slab, 1).start()
        merge(1 - x, y)
        x_first(slab, 0).start()
        merge(x, 1 - y)
        y_first(slab, 0).start()
        merge(x, y)
        after(step)

    def middle(step):
        slab = target(step)
        x_first(slab, 1).wait_recv()
        x_first(slab, 0).wait_send()
        y_first(slab, 0).wait_send()
        lanes[slab, x, 1 - y, low] = total_of(
            lanes[slab, x, 1 - y, low], x_got[slab, 1]
        ).astype(jnp.bfloat16)
        y_second(slab).start()
        y_first(slab, 1).wait_recv()
        lanes[slab, 1 - x, y, high] = total_of(
            lanes[slab, 1 - x, y, high], y_got[slab, 1]
        ).astype(jnp.bfloat16)
        x_second(slab).start()

    def finish(step):
        slab = target(step)
        for part in range(2):
            if part == 0:
                x_first(slab, 0).wait_recv()
                y_second(slab).wait_recv()
                value = total_of(lanes[slab, x, y, low], x_got[slab, 0], y_last[slab])
            else:
                y_first(slab, 0).wait_recv()
                x_second(slab).wait_recv()
                value = total_of(lanes[slab, x, y, high], y_got[slab, 0], x_last[slab])
            rows_of = halves[part]

            @pl.when(slab > z)
            def _():
                @pl.when(z == 0)
                def _():
                    lanes[slab, x, y, rows_of] = value.astype(jnp.bfloat16)

                @pl.when(z > 0)
                def _():
                    z_up(slab, part).wait_recv()
                    lanes[slab, x, y, rows_of] = total_of(value, below[slab, rows_of]).astype(jnp.bfloat16)

                z_up(slab, part).start()

            @pl.when(slab < z)
            def _():
                @pl.when(z == n_z - 1)
                def _():
                    lanes[slab, x, y, rows_of] = value.astype(jnp.bfloat16)

                @pl.when(z < n_z - 1)
                def _():
                    z_down(slab, part).wait_recv()
                    lanes[slab, x, y, rows_of] = total_of(value, above[slab, rows_of]).astype(jnp.bfloat16)

                z_down(slab, part).start()

            @pl.when(slab == z)
            def _():
                out[rows_of, :] = value

                @pl.when(z > 0)
                def _():
                    z_up(slab, part).wait_recv()
                    out[rows_of, :] += below[slab, rows_of].astype(jnp.float32)

                @pl.when(z < n_z - 1)
                def _():
                    z_down(slab, part).wait_recv()
                    out[rows_of, :] += above[slab, rows_of].astype(jnp.float32)

    def turn(step, unused):
        for action, back in ((produce, 0), (begin, 0), (middle, 1), (finish, 2)):

            @pl.when((step >= back) & (step < n_z + back))
            def _():
                action(step - back)

        return unused

    lax.fori_loop(0, n_z + 2, turn, 0)

    def close(slab, unused):
        for px in range(2):
            c_copy(slab, px).wait_send()
        x_first(slab, 1).wait_send()
        y_first(slab, 1).wait_send()
        x_second(slab).wait_send()
        y_second(slab).wait_send()
        for part in range(2):

            @pl.when(slab > z)
            def _():
                z_up(slab, part).wait_send()

            @pl.when(slab < z)
            def _():
                z_down(slab, part).wait_send()

        return unused

    lax.fori_loop(0, n_z, close, 0)


def embed_kernel(shard_rows, table, ints, out, *scratch):
    extent = table.shape[0]
    chunk = 2 * out.shape[0]
    greet_near()

    def make(step, slab, px, pc):
        token = in_pairs(ints, slab, px, pc, 0).astype(jnp.int32)
        hot = vocab_ids(extent, chunk, shard_rows) == token
        hot = jnp.where(hot, 1.0, 0.0).astype(jnp.bfloat16)
        return inner(hot, table[...]).astype(jnp.bfloat16)

    scatter_slabs(out, scratch, lambda step: None, make, lambda step: None)


def embed(table, ints, own, shard_rows, collective_id):
    width = table.shape[1]
    return pl.pallas_call(
        functools.partial(embed_kernel, shard_rows),
        out_shape=jax.ShapeDtypeStruct((own, width), jnp.float32),
        in_specs=[VMEM] * 2,
        out_specs=VMEM,
        scratch_shapes=scatter_scratch(own, width),
        compiler_params=pltpu.CompilerParams(
            collective_id=collective_id, has_side_effects=True,
            vmem_limit_bytes=lax.axis_size("z") * 3 * MIB + 12 * MIB,
        ),
    )(table, ints)


def vocab_back_kernel(
    shard_rows, held, rows_all, table, ints, logs, weights, out, table_grad, slab_rows, changes, slab_sem, *scratch
):
    extent, width = table.shape
    chunk = 2 * out.shape[0]
    scale = width ** (-0.5)
    n_z = lax.axis_size("z")
    target = slab_order()

    def load(step):
        return pltpu.make_async_copy(
            rows_all.at[target(step)], slab_rows.at[step % 2], slab_sem.at[step % 2]
        )

    if not held:
        load(0).start()
    greet_near()
    table_grad[...] = jnp.zeros_like(table_grad)

    def rows_of(step, px, pc):
        if held:
            return rows_all[target(step), px, pc].reshape(chunk, width)
        return slab_rows[step % 2, px, pc].reshape(chunk, width)

    def before(step):
        if held:
            return
        load(step).wait()

        @pl.when(step + 1 < n_z)
        def _():
            load(step + 1).start()

    def make(step, slab, px, pc):
        value = outer(table[...], rows_of(step, px, pc)) * scale
        aim = in_pairs(ints, slab, px, pc, 1).astype(jnp.int32)
        hot = jnp.where(vocab_ids(extent, chunk, shard_rows) == aim, 1.0, 0.0)
        change = jnp.exp(value - in_pairs(logs, slab, px, pc, 0)) - hot
        change = (change * in_pairs(weights, slab, px, pc, 0)).astype(jnp.bfloat16)
        changes[px, pc] = change
        return (inner(change, table[...]) * scale).astype(jnp.bfloat16)

    def after(step):
        def one(index, unused):
            px, pc = index // 2, index % 2
            table_grad[...] += matmul(changes[px, pc], rows_of(step, px, pc))
            return unused

        lax.fori_loop(0, 4, one, 0)

    scatter_slabs(out, scratch, before, make, after)
    table_grad[...] = table_grad[...] * scale


def vocab_back(rows_all, table, ints, logs, weights, shard_rows, collective_id):
    own, width = rows_all.shape[4:]
    extent = table.shape[0]
    n_z, n_x, n_c, n_y = sizes()
    held = n_z <= 4
    return pl.pallas_call(
        functools.partial(vocab_back_kernel, shard_rows, held),
        out_shape=(
            jax.ShapeDtypeStruct((own, width), jnp.float32),
            jax.ShapeDtypeStruct((extent, width), jnp.float32),
        ),
        in_specs=[VMEM if held else ANY] + [VMEM] * 4,
        out_specs=(VMEM,) * 2,
        scratch_shapes=[
            pltpu.VMEM((1,) * 6 if held else (2, n_x, n_c, n_y, own, width), rows_all.dtype),
            pltpu.VMEM((n_x, n_c, extent, 2 * own), jnp.bfloat16),
            pltpu.SemaphoreType.DMA((2,)),
        ] + scatter_scratch(own, width),
        compiler_params=pltpu.CompilerParams(
            collective_id=collective_id, has_side_effects=True,
            vmem_limit_bytes=n_z * 3 * MIB + 20 * MIB if n_z <= 8 else 62 * MIB,
        ),
    )(rows_all, table, ints, logs, weights)


SQRT_HALF = 0.5**0.5
DENSITY = 0.3989422804014327


def matmul(left, right):
    return jnp.dot(left, right, preferred_element_type=jnp.float32)


def inner(left, right):
    return lax.dot_general(
        left, right, (((0,), (0,)), ((), ())), preferred_element_type=jnp.float32
    )


def outer(left, right):
    return lax.dot_general(
        left, right, (((1,), (1,)), ((), ())), preferred_element_type=jnp.float32
    )


def plane_gather(own_rows, blocks, send_sem, recv_sem):
    half = own_rows.shape[0] // 2
    (z, x, c, y), x_near, y_near, _ = around()
    low, high = pl.ds(0, half), pl.ds(half, half)

    def copy(slot, px, py, rows, source, device):
        target = blocks.at[px, py, rows]
        return remote(target if source is None else source.at[rows], target, send_sem.at[slot], recv_sem.at[slot], device)

    first = [
        copy(0, x, y, low, own_rows, x_near),
        copy(1, x, y, high, own_rows, y_near),
        copy(2, x, y, high, own_rows, x_near),
        copy(3, x, y, low, own_rows, y_near),
    ]
    relays = [copy(4, 1 - x, y, low, None, y_near), copy(5, x, 1 - y, high, None, x_near)]
    for each in first:
        each.start()

    def wait_near():
        first[0].wait_recv()
        relays[0].start()
        first[1].wait_recv()
        relays[1].start()

    def wait_x():
        first[2].wait_recv()

    def wait_y():
        first[3].wait_recv()

    def wait_diagonal():
        for each in relays:
            each.wait_recv()

    def close():
        for each in first + relays:
            each.wait_send()

    return wait_near, wait_x, wait_y, wait_diagonal, close


def plane_sum(parts, got, out, send_sem, recv_sem):
    (z, x, c, y), x_near, y_near, _ = around()
    diagonal = (z, 1 - x, c, 1 - y)
    copies = [
        remote(parts.at[device[1], device[3]], got.at[slot], send_sem.at[slot], recv_sem.at[slot], device)
        for slot, device in enumerate((x_near, y_near, diagonal))
    ]

    def close():
        for each in copies:
            each.wait_recv()
        out[...] = total_of(parts[x, y], got[0], got[1], got[2])
        for each in copies:
            each.wait_send()

    return copies, close


def order_experts(weights, ordered, sems):
    n_z, n_c, n_x, _, depth, _ = weights.shape
    copies = []
    for pz in range(n_z):
        for pc in range(n_c):
            for px in range(n_x):
                at = (pz * n_x + px) * n_c + pc
                copies.append(
                    pltpu.make_async_copy(
                        weights.at[pz, pc, px], ordered.at[:, pl.ds(at * depth, depth)], sems.at[at]
                    )
                )
    for copy in copies:
        copy.start()
    return copies


def experts_kernel(
    own_rows, route, weights, out, wide, before, hidden, ordered, parts, got, w_sem, g_send, g_recv, s_send, s_recv
):
    (z, x, c, y), x_near, y_near, _ = around()
    diagonal = (z, 1 - x, c, 1 - y)
    loads = order_experts(weights, ordered, w_sem)
    up, down = ordered.at[pl.ds(0, 2)], ordered.at[pl.ds(2, 2)]
    greet((x_near, y_near, diagonal))
    wait_near, wait_x, wait_y, wait_diagonal, close = plane_gather(own_rows, wide, g_send, g_recv)
    copies, finish = plane_sum(parts, got, out, s_send, s_recv)
    wide[x, y] = own_rows[...]

    def work(px, py):
        rows = wide[px, py]
        first = route[px, py] == 0
        value = jnp.where(first, matmul(rows, up[0]), matmul(rows, up[1]))
        before[px, py] = value
        active = 0.5 * value * (1.0 + lax.erf(value * SQRT_HALF))
        hidden_first = jnp.where(first, active, 0.0).astype(jnp.bfloat16)
        hidden_second = jnp.where(first, 0.0, active).astype(jnp.bfloat16)
        hidden[px, py] = active.astype(jnp.bfloat16)
        total = outer(hidden_first, down[0]) + outer(hidden_second, down[1])
        parts[px, py] = total.astype(jnp.bfloat16)

    for load in loads:
        load.wait()
    work(x, y)
    wait_near()
    wait_x()
    work(1 - x, y)
    copies[0].start()
    wait_y()
    work(x, 1 - y)
    copies[1].start()
    wait_diagonal()
    work(1 - x, 1 - y)
    copies[2].start()
    finish()
    close()


def experts(own_rows, route, weights, collective_id):
    _, n_x, _, n_y = sizes()
    own, width = own_rows.shape
    wide = weights.shape[5]
    dma = pltpu.SemaphoreType.DMA
    low = jnp.bfloat16
    return pl.pallas_call(
        experts_kernel,
        out_shape=(
            jax.ShapeDtypeStruct((own, width), jnp.float32),
            jax.ShapeDtypeStruct((n_x, n_y, own, width), low),
            jax.ShapeDtypeStruct((n_x, n_y, own, wide), jnp.float32),
            jax.ShapeDtypeStruct((n_x, n_y, own, wide), low),
        ),
        in_specs=[VMEM, VMEM, ANY],
        out_specs=(VMEM,) * 4,
        scratch_shapes=[
            pltpu.VMEM((4, width, wide), low),
            pltpu.VMEM((n_x, n_y, own, width), low),
            pltpu.VMEM((3, own, width), low),
            dma((width // weights.shape[4],)), dma((6,)), dma((6,)), dma((3,)), dma((3,)),
        ],
        compiler_params=pltpu.CompilerParams(
            collective_id=collective_id, has_side_effects=True, vmem_limit_bytes=20 * MIB
        ),
        cost_estimate=pl.CostEstimate(
            flops=8 * own * 4 * width * wide, bytes_accessed=8 * MIB, transcendentals=4 * own * wide
        ),
    )(own_rows, route, weights)


def experts_back_kernel(
    own_rows, route, weights, wide, before, hidden, out, grads,
    ordered, wide_grad, before_grad, parts, got, w_sem, g_send, g_recv, s_send, s_recv,
):
    (z, x, c, y), x_near, y_near, _ = around()
    diagonal = (z, 1 - x, c, 1 - y)
    loads = order_experts(weights, ordered, w_sem)
    up, down = ordered.at[pl.ds(0, 2)], ordered.at[pl.ds(2, 2)]
    greet((x_near, y_near, diagonal))
    wait_near, wait_x, wait_y, wait_diagonal, close = plane_gather(own_rows, wide_grad, g_send, g_recv)
    copies, finish = plane_sum(parts, got, out, s_send, s_recv)
    wide_grad[x, y] = own_rows[...]

    def work(px, py):
        rows = wide_grad[px, py]
        first = route[px, py] == 0
        hidden_grad = jnp.where(first, matmul(rows, down[0]), matmul(rows, down[1]))
        value = before[px, py]
        slope = 0.5 * (1.0 + lax.erf(value * SQRT_HALF)) + value * (
            DENSITY * jnp.exp(-0.5 * value * value)
        )
        change = (hidden_grad * slope).astype(jnp.bfloat16)
        before_grad[px, py] = change
        change_first = jnp.where(first, change, 0)
        change_second = jnp.where(first, 0, change)
        total = outer(change_first, up[0]) + outer(change_second, up[1])
        parts[px, py] = total.astype(jnp.bfloat16)

    for load in loads:
        load.wait()
    work(x, y)
    wait_near()
    wait_x()
    work(1 - x, y)
    copies[0].start()
    wait_y()
    work(x, 1 - y)
    copies[1].start()
    wait_diagonal()
    work(1 - x, 1 - y)
    copies[2].start()
    close()

    lane = 4 * own_rows.shape[0]
    rows = wide[...].reshape(lane, -1)
    grad_rows = wide_grad[...].reshape(lane, -1)
    first = route[...].reshape(lane, 1) == 0
    change = before_grad[...].reshape(lane, -1)
    active = hidden[...].reshape(lane, -1)
    low = jnp.bfloat16
    n_z, n_x, n_c, _ = sizes()
    depth = grads.shape[3]

    def keep(slot, value):
        value = value.astype(low)
        for pz in range(n_z):
            for px in range(n_x):
                for pc in range(n_c):
                    start = ((pz * n_x + px) * n_c + pc) * depth
                    grads[pz * n_c + pc, px, slot] = value[start : start + depth]

    keep(0, inner(rows, jnp.where(first, change, 0)))
    keep(1, inner(rows, jnp.where(first, 0, change)))
    keep(2, inner(grad_rows, jnp.where(first, active, 0)))
    keep(3, inner(grad_rows, jnp.where(first, 0, active)))
    finish()


def experts_back(own_rows, route, weights, wide, before, hidden, collective_id):
    n_z, n_x, n_c, n_y = sizes()
    own, width = own_rows.shape
    units = weights.shape[5]
    dma = pltpu.SemaphoreType.DMA
    low = jnp.bfloat16
    return pl.pallas_call(
        experts_back_kernel,
        out_shape=(
            jax.ShapeDtypeStruct((own, width), jnp.float32),
            jax.ShapeDtypeStruct((n_z * n_c, n_x, 4, width // (n_z * n_x * n_c), units), low),
        ),
        in_specs=[VMEM, VMEM, ANY] + [VMEM] * 3,
        out_specs=(VMEM,) * 2,
        scratch_shapes=[
            pltpu.VMEM((4, width, units), low),
            pltpu.VMEM((n_x, n_y, own, width), low),
            pltpu.VMEM((n_x, n_y, own, units), low),
            pltpu.VMEM((n_x, n_y, own, width), low),
            pltpu.VMEM((3, own, width), low),
            dma((width // weights.shape[4],)), dma((6,)), dma((6,)), dma((3,)), dma((3,)),
        ],
        compiler_params=pltpu.CompilerParams(
            collective_id=collective_id, has_side_effects=True, vmem_limit_bytes=28 * MIB
        ),
        cost_estimate=pl.CostEstimate(
            flops=16 * own * 4 * width * units, bytes_accessed=12 * MIB, transcendentals=8 * own * units
        ),
    )(own_rows, route, weights, wide, before, hidden)


def project_kernel(transposed, rows, weight, out, parts, got, s_send, s_recv):
    (z, x, c, y), x_near, y_near, _ = around()
    diagonal = (z, 1 - x, c, 1 - y)
    barrier = pltpu.get_barrier_semaphore()
    for device in (x_near, y_near, diagonal):
        pl.semaphore_signal(barrier, inc=1, device_id=device, device_id_type=MESH)
    copies, finish = plane_sum(parts, got, out, s_send, s_recv)

    def work(px, py):
        times = outer if transposed else matmul
        parts[px, py] = times(rows[px, py], weight[...]).astype(jnp.bfloat16)

    work(1 - x, 1 - y)
    pl.semaphore_wait(barrier, 3)
    copies[2].start()
    work(1 - x, y)
    copies[0].start()
    work(x, 1 - y)
    copies[1].start()
    work(x, y)
    finish()


def project(rows, weight, transposed, collective_id):
    n_x, n_y, own, depth = rows.shape
    width = weight.shape[0] if transposed else weight.shape[1]
    low = jnp.bfloat16
    dma = pltpu.SemaphoreType.DMA
    return pl.pallas_call(
        functools.partial(project_kernel, transposed),
        out_shape=jax.ShapeDtypeStruct((own, width), jnp.float32),
        in_specs=[VMEM] * 2,
        out_specs=VMEM,
        scratch_shapes=[
            pltpu.VMEM((n_x, n_y, own, width), low), pltpu.VMEM((3, own, width), low), dma((3,)), dma((3,)),
        ],
        compiler_params=pltpu.CompilerParams(
            collective_id=collective_id, has_side_effects=True, vmem_limit_bytes=10 * MIB
        ),
        cost_estimate=pl.CostEstimate(
            flops=8 * own * width * depth, bytes_accessed=4 * MIB, transcendentals=0
        ),
    )(rows, weight)


def gather_project_kernel(transposed, own_rows, weight, wide, out, g_send, g_recv):
    (z, x, c, y), x_near, y_near, _ = around()
    greet((x_near, y_near))
    wait_near, wait_x, wait_y, wait_diagonal, close = plane_gather(own_rows, wide, g_send, g_recv)
    wide[x, y] = own_rows[...]

    def work(px, py):
        times = outer if transposed else matmul
        out[px, py] = times(wide[px, py], weight[...]).astype(jnp.bfloat16)

    work(x, y)
    wait_near()
    wait_x()
    work(1 - x, y)
    wait_y()
    work(x, 1 - y)
    wait_diagonal()
    work(1 - x, 1 - y)
    close()


def gather_project(own_rows, weight, transposed, collective_id):
    _, n_x, _, n_y = sizes()
    own, width = own_rows.shape
    depth = weight.shape[0] if transposed else weight.shape[1]
    dma = pltpu.SemaphoreType.DMA
    low = jnp.bfloat16
    return pl.pallas_call(
        functools.partial(gather_project_kernel, transposed),
        out_shape=(
            jax.ShapeDtypeStruct((n_x, n_y, own, width), low),
            jax.ShapeDtypeStruct((n_x, n_y, own, depth), low),
        ),
        in_specs=[VMEM] * 2,
        out_specs=(VMEM,) * 2,
        scratch_shapes=[dma((6,)), dma((6,))],
        compiler_params=pltpu.CompilerParams(
            collective_id=collective_id, has_side_effects=True, vmem_limit_bytes=12 * MIB
        ),
        cost_estimate=pl.CostEstimate(
            flops=8 * own * width * depth, bytes_accessed=4 * MIB, transcendentals=0
        ),
    )(own_rows, weight)


def merge_logs_kernel(source, out, got, mine, send_one, recv_one, send_two, recv_two):
    n_z, n_x, n_c, n_y = sizes()
    count = n_z * n_x * n_c * n_y
    z, x, c, y = place()
    me = ((z * n_x + x) * n_c + c) * n_y + y

    def device_of(index):
        return (
            index // (n_x * n_c * n_y), index // (n_c * n_y) % n_x, index // n_y % n_c, index % n_y
        )

    barrier = pltpu.get_barrier_semaphore()

    def call(step, unused):
        other = lax.rem(me + step, count)
        pl.semaphore_signal(barrier, inc=1, device_id=device_of(other), device_id_type=MESH)
        return unused

    lax.fori_loop(1, count, call, 0)
    got[me] = source[me]
    pl.semaphore_wait(barrier, count - 1)

    def first(step):
        other = lax.rem(me + step, count)
        return remote(
            source.at[other], got.at[me], send_one.at[step], recv_one.at[step], device_of(other)
        )

    def second(step):
        other = lax.rem(me + step, count)
        return remote(mine, out.at[me], send_two.at[step], recv_two.at[step], device_of(other))

    def each(action):
        def body(step, unused):
            action(step)
            return unused

        lax.fori_loop(1, count, body, 0)

    each(lambda step: first(step).start())
    each(lambda step: first(step).wait())
    values = got[...]
    peak = jnp.max(values, axis=0)
    mine[...] = peak + jnp.log(jnp.sum(jnp.exp(values - peak[None]), axis=0))
    out[me] = mine[...]
    each(lambda step: second(step).start())
    each(lambda step: second(step).wait())


def merge_logs(blocks, collective_id):
    count = blocks.shape[0]
    dma = pltpu.SemaphoreType.DMA
    return pl.pallas_call(
        merge_logs_kernel,
        out_shape=jax.ShapeDtypeStruct(blocks.shape, blocks.dtype),
        in_specs=[VMEM],
        out_specs=VMEM,
        scratch_shapes=[
            pltpu.VMEM(blocks.shape, blocks.dtype), pltpu.VMEM(blocks.shape[1:], blocks.dtype),
            dma((count,)), dma((count,)), dma((count,)), dma((count,)),
        ],
        compiler_params=pltpu.CompilerParams(collective_id=collective_id, has_side_effects=True),
    )(blocks)


def key_position(index, part, chunk):
    lane = 2 * chunk
    start = (part // 2) * (2 * lane) + (part % 2) * chunk
    return start + index + jnp.where(index >= chunk, chunk, 0)


def near_shown(side, chunk, query_pos, query_seg, near_pos, near_seg):
    columns = slice(side * chunk, (side + 1) * chunk)
    rows = slice(2 * side * chunk, 2 * (side + 1) * chunk)
    shown = (
        (near_seg[rows, :] == query_seg[:, columns])
        & (near_pos[rows, :] <= query_pos[:, columns])
        & (near_pos[rows, :] >= PROMPT)
    )
    return columns, rows, shown


def attend_kernel(
    chunk, query, far, near, query_pos, query_seg, near_pos, near_seg,
    out, out_low, log_total, scores, far_t, near_t,
):
    lane, feature = query.shape
    group = feature // HEAD_DIM
    prompt_rows = far.shape[0]
    parts = prompt_rows // lane
    query_t = (query[...].astype(jnp.float32) * HEAD_DIM ** (-0.5)).T.astype(jnp.bfloat16)
    far_t[...] = far[...].astype(jnp.float32).T.astype(jnp.bfloat16)
    near_t[...] = near[...].astype(jnp.float32).T.astype(jnp.bfloat16)
    row_of = lax.broadcasted_iota(jnp.int32, (feature, lane), 0)
    q_pos = query_pos[...]

    for head in range(group):
        low, high = head * HEAD_DIM, (head + 1) * HEAD_DIM
        query_h = jnp.where((row_of >= low) & (row_of < high), query_t, 0)

        def score_part(part, peak):
            block = far[pl.ds(pl.multiple_of(part * lane, lane), lane), :feature]
            value = matmul(block, query_h)
            index = lax.broadcasted_iota(jnp.int32, (lane, lane), 0)
            value = jnp.where(key_position(index, part, chunk) <= q_pos, value, MASKED)
            scores[pl.ds(pl.multiple_of(part * lane, lane), lane), :] = value
            return jnp.maximum(peak, jnp.max(value, axis=0, keepdims=True))

        peak = lax.fori_loop(0, parts, score_part, jnp.full((1, lane), MASKED, jnp.float32))
        near_peaks = []
        for side in range(2):
            columns, rows, shown = near_shown(side, chunk, query_pos, query_seg, near_pos, near_seg)
            value = matmul(near[rows, :feature], query_h[:, columns])
            value = jnp.where(shown, value, MASKED)
            scores[prompt_rows : prompt_rows + lane, columns] = value
            near_peaks.append(jnp.max(value, axis=0, keepdims=True))
        peak = jnp.maximum(peak, jnp.concatenate(near_peaks, axis=1))

        def weigh_part(part, state):
            total, mixed = state
            start = pl.multiple_of(part * lane, lane)
            chance = jnp.exp(scores[pl.ds(start, lane), :] - peak)
            total = total + jnp.sum(chance, axis=0, keepdims=True)
            mixed = mixed + matmul(
                far_t[feature + low : feature + high, pl.ds(start, lane)],
                chance.astype(jnp.bfloat16),
            )
            return total, mixed

        total, mixed = lax.fori_loop(
            0,
            parts,
            weigh_part,
            (jnp.zeros((1, lane), jnp.float32), jnp.zeros((HEAD_DIM, lane), jnp.float32)),
        )
        near_total, near_mixed = [], []
        for side in range(2):
            columns = slice(side * chunk, (side + 1) * chunk)
            rows = slice(side * lane, (side + 1) * lane)
            chance = jnp.exp(scores[prompt_rows : prompt_rows + lane, columns] - peak[:, columns])
            near_total.append(jnp.sum(chance, axis=0, keepdims=True))
            near_mixed.append(
                matmul(near_t[feature + low : feature + high, rows], chance.astype(jnp.bfloat16))
            )
        total = total + jnp.concatenate(near_total, axis=1)
        mixed = mixed + jnp.concatenate(near_mixed, axis=1)
        out[low:high, :] = mixed / total
        log_total[head : head + 1, :] = peak + jnp.log(total)
    out_low[...] = out[...].T.astype(jnp.bfloat16)


def attend(queries, far, near, places, chunk):
    lane, feature = queries.shape
    prompt_rows = far.shape[0]
    group = feature // HEAD_DIM
    total_rows = prompt_rows + lane
    return pl.pallas_call(
        functools.partial(attend_kernel, chunk),
        out_shape=(
            jax.ShapeDtypeStruct((feature, lane), jnp.float32),
            jax.ShapeDtypeStruct((lane, feature), jnp.bfloat16),
            jax.ShapeDtypeStruct((group, lane), jnp.float32),
        ),
        in_specs=[VMEM] * 7,
        out_specs=(VMEM,) * 3,
        scratch_shapes=[
            pltpu.VMEM((total_rows, lane), jnp.float32),
            pltpu.VMEM((2 * feature, prompt_rows), jnp.bfloat16),
            pltpu.VMEM((2 * feature, 2 * lane), jnp.bfloat16),
        ],
        compiler_params=pltpu.CompilerParams(vmem_limit_bytes=20 * MIB),
        cost_estimate=pl.CostEstimate(
            flops=8 * group * lane * total_rows * 128,
            bytes_accessed=8 * MIB,
            transcendentals=group * lane * total_rows,
        ),
    )(queries, far, near, *places)


def attend_back_kernel(
    chunk, query, far, near, query_pos, query_seg, near_pos, near_seg,
    log_total, mixed, answer, query_grad, far_grad, near_grad,
    far_t, near_t, far_values, near_values, far_sum, near_sum, query_sum,
):
    lane, feature = query.shape
    group = feature // HEAD_DIM
    prompt_rows = far.shape[0]
    parts = prompt_rows // lane
    scaled = (query[...].astype(jnp.float32) * HEAD_DIM ** (-0.5)).astype(jnp.bfloat16)
    query_t = scaled.astype(jnp.float32).T.astype(jnp.bfloat16)
    answers = answer[...]
    answer_t = answers.astype(jnp.float32).T.astype(jnp.bfloat16)
    far_t[...] = far[:, :feature].astype(jnp.float32).T.astype(jnp.bfloat16)
    near_t[...] = near[:, :feature].astype(jnp.float32).T.astype(jnp.bfloat16)
    far_values[...] = far[:, feature:]
    near_values[...] = near[:, feature:]
    row_of = lax.broadcasted_iota(jnp.int32, (feature, lane), 0)
    column_of = lax.broadcasted_iota(jnp.int32, (lane, feature), 1)
    q_pos = query_pos[...]

    for head in range(group):
        low, high = head * HEAD_DIM, (head + 1) * HEAD_DIM
        in_rows = (row_of >= low) & (row_of < high)
        in_columns = (column_of >= low) & (column_of < high)
        query_ht = jnp.where(in_rows, query_t, 0)
        answer_ht = jnp.where(in_rows, answer_t, 0)
        query_h = jnp.where(in_columns, scaled, 0)
        answer_h = jnp.where(in_columns, answers, 0)
        log_h = log_total[head : head + 1, :]
        delta_h = jnp.sum(
            answer_t[low:high, :].astype(jnp.float32) * mixed[low:high, :], axis=0, keepdims=True
        )

        def slopes(key_block, value_block, shown, columns):
            value = matmul(key_block, query_ht[:, columns])
            chance = jnp.exp(jnp.where(shown, value - log_h[:, columns], MASKED))
            slope = matmul(value_block, answer_ht[:, columns])
            change = (chance * (slope - delta_h[:, columns])).astype(jnp.bfloat16)
            chance = chance.astype(jnp.bfloat16)
            return change, matmul(change, query_h[columns]), matmul(chance, answer_h[columns])

        def add(sums, rows, key_part, value_part):
            if head == 0:
                sums[0, rows, :] = key_part
                sums[1, rows, :] = value_part
            else:
                sums[0, rows, :] += key_part
                sums[1, rows, :] += value_part

        def back_part(part, total):
            rows = pl.ds(pl.multiple_of(part * lane, lane), lane)
            index = lax.broadcasted_iota(jnp.int32, (lane, lane), 0)
            shown = key_position(index, part, chunk) <= q_pos
            change, key_part, value_part = slopes(
                far[rows, :feature], far_values[rows, :], shown, slice(0, lane)
            )
            add(far_sum, rows, key_part, value_part)
            return total + matmul(far_t[low:high, rows], change)

        total = lax.fori_loop(0, parts, back_part, jnp.zeros((HEAD_DIM, lane), jnp.float32))
        near_total = []
        for side in range(2):
            columns, rows, shown = near_shown(side, chunk, query_pos, query_seg, near_pos, near_seg)
            change, key_part, value_part = slopes(
                near[rows, :feature], near_values[rows, :], shown, columns
            )
            add(near_sum, rows, key_part, value_part)
            near_total.append(matmul(near_t[low:high, rows], change))
        query_sum[low:high, :] = (total + jnp.concatenate(near_total, axis=1)) * HEAD_DIM ** (-0.5)
    query_grad[...] = query_sum[...].T.astype(jnp.bfloat16)
    for sums, grad in ((far_sum, far_grad), (near_sum, near_grad)):
        grad[...] = jnp.concatenate(
            [sums[0].astype(jnp.bfloat16), sums[1].astype(jnp.bfloat16)], axis=1
        )


def attend_back(queries, far, near, places, log_total, mixed, answer, chunk):
    lane, feature = queries.shape
    prompt_rows = far.shape[0]
    group = feature // HEAD_DIM
    total_rows = prompt_rows + lane
    low = jnp.bfloat16
    return pl.pallas_call(
        functools.partial(attend_back_kernel, chunk),
        out_shape=(
            jax.ShapeDtypeStruct((lane, feature), low),
            jax.ShapeDtypeStruct((prompt_rows, 2 * feature), low),
            jax.ShapeDtypeStruct((2 * lane, 2 * feature), low),
        ),
        in_specs=[VMEM] * 10,
        out_specs=(VMEM,) * 3,
        scratch_shapes=[
            pltpu.VMEM((feature, prompt_rows), low),
            pltpu.VMEM((feature, 2 * lane), low),
            pltpu.VMEM((prompt_rows, feature), low),
            pltpu.VMEM((2 * lane, feature), low),
            pltpu.VMEM((2, prompt_rows, feature), jnp.float32),
            pltpu.VMEM((2, 2 * lane, feature), jnp.float32),
            pltpu.VMEM((feature, lane), jnp.float32),
        ],
        compiler_params=pltpu.CompilerParams(vmem_limit_bytes=28 * MIB),
        cost_estimate=pl.CostEstimate(
            flops=20 * group * lane * total_rows * 128,
            bytes_accessed=12 * MIB,
            transcendentals=group * lane * total_rows,
        ),
    )(queries, far, near, *places, log_total, mixed, answer)


def head_places(back):
    n_z, n_x, n_c, n_y = sizes()
    line = n_z * n_c
    pairs = []
    for device in range(line * n_x * n_y):
        group, at = device // line, device % line
        place_of = ((at // n_c * n_x + group // n_y) * n_c + at % n_c) * n_y + group % n_y
        pairs.append((place_of, device) if back else (device, place_of))
    return tuple(pairs)


def pad_rows(block):
    return jnp.pad(block, ((0, 8 - block.shape[0]), (0, 0)))


def adam_update(weight, moment_one, moment_two, gradient, step_rate, decay_rate):
    first_new = BETA_ONE * moment_one + (1.0 - BETA_ONE) * gradient
    second_new = BETA_TWO * moment_two + (1.0 - BETA_TWO) * gradient * gradient
    normalized = (
        first_new
        / (1.0 - BETA_ONE**STEP)
        / (jnp.sqrt(second_new / (1.0 - BETA_TWO**STEP)) + ADAM_EPS)
    )
    return (weight - step_rate * (normalized + decay_rate * weight), first_new, second_new)


def per_device(
    token_ids,
    targets,
    valid_mask,
    cont_lengths,
    routes,
    vocab_table,
    vocab_first,
    vocab_second,
    attn_weights,
    attn_first,
    attn_second,
    router,
    router_first,
    router_second,
    norm_gains,
    gains_first,
    gains_second,
    expert_up,
    up_first,
    up_second,
    expert_down,
    down_first,
    down_second,
):
    slabs = lax.axis_size("z")
    planes = lax.axis_size("x")
    cores = lax.axis_size("core")
    sides = lax.axis_size("head")
    groups = planes * sides
    z_at, x_at, core_at, side_at = (lax.axis_index(name) for name in ALL)
    blk_at = (z_at * planes + x_at) * cores + core_at
    device_at = blk_at * sides + side_at
    group_at = x_at * sides + side_at
    tokens = valid_mask.shape[0]
    chunk = token_ids.shape[0]
    own = chunk // sides
    lane = planes * chunk
    feature = D // groups
    wide = expert_up.shape[3] // planes
    shard_rows = vocab_table.shape[0]
    logit_scale = D ** (-0.5)

    cont_ends = jnp.cumsum(cont_lengths)
    valid_f = valid_mask.astype(jnp.float32)
    token_count = jnp.sum(valid_mask).astype(jnp.float32)
    expert_ids = jnp.arange(EXPERTS, dtype=jnp.int32)

    own_ints = jnp.concatenate([token_ids[None], targets[None], routes], axis=0)
    own_ints = lax.dynamic_slice_in_dim(own_ints, side_at * own, own, axis=1).astype(jnp.float32)
    rows_of = attn_weights.shape[1]
    smalls = jnp.concatenate(
        [router.transpose(0, 2, 1).reshape(LAYERS * EXPERTS, rows_of), norm_gains], axis=0
    )
    smalls = smalls.astype(jnp.bfloat16).astype(jnp.float32)
    smalls = jnp.pad(smalls, ((0, 16 - smalls.shape[0]), (0, own - rows_of)))
    whole_f = swap(jnp.concatenate([pad_rows(own_ints), smalls], axis=0)[None], True, 1)
    attn_low = attn_weights.astype(jnp.bfloat16)
    qkv_send = attn_low[:, :, : 3 * D].reshape(LAYERS, rows_of, 3, groups, feature)
    qkv_send = jnp.concatenate([qkv_send[:, :, 1:], qkv_send[:, :, :1]], axis=2)
    qkv_send = qkv_send.transpose(3, 0, 1, 2, 4).reshape(groups, LAYERS, rows_of, 3 * feature)
    qkv_got = lax.all_to_all(qkv_send, PLANE, split_axis=0, concat_axis=0, tiled=True)
    out_rows = attn_low[:, :, 3 * D :]
    out_rows = lax.ppermute(out_rows, ALL, head_places(False))
    out_rows = out_rows.reshape(LAYERS, rows_of, groups, feature).transpose(2, 0, 1, 3)
    expert_send = jnp.stack([expert_up, expert_down], axis=1).astype(jnp.bfloat16)
    depth = expert_send.shape[3]
    expert_send = expert_send.reshape(LAYERS, 2 * EXPERTS, depth, planes, wide)
    expert_send = expert_send.transpose(3, 0, 1, 2, 4)
    expert_halves = []
    for layer_index in range(LAYERS):
        kept_half = lax.dynamic_index_in_dim(expert_send[:, layer_index], x_at, 0, False)
        sent_half = lax.dynamic_index_in_dim(expert_send[:, layer_index], 1 - x_at, 0, False)
        got_half = lax.ppermute(sent_half, "x", ((0, 1), (1, 0)))
        expert_halves.append((kept_half, got_half))
    whole_f, qkv_got, out_rows, expert_halves = lax.optimization_barrier(
        (whole_f, qkv_got, out_rows, expert_halves)
    )
    attn_pack = jnp.concatenate([qkv_got, out_rows], axis=3)
    expert_packs = []
    for kept_half, got_half in expert_halves:
        expert_packs.append(
            jnp.stack(
                [
                    jnp.where(x_at == 0, kept_half, got_half),
                    jnp.where(x_at == 0, got_half, kept_half),
                ]
            )
        )
    whole_f, attn_pack, expert_packs = lax.optimization_barrier((whole_f, attn_pack, expert_packs))
    attn_pack = lax.all_gather(attn_pack, LINE, axis=0)
    qkv_weights, out_weights = [], []
    for layer_index in range(LAYERS):
        block = attn_pack[:, :, layer_index]
        part = block[..., : 3 * feature].reshape(slabs, cores, planes, sides, rows_of, 3 * feature)
        qkv_weights.append(part.transpose(0, 2, 1, 3, 4, 5).reshape(D, 3 * feature))
        part = block[..., 3 * feature :]
        out_weights.append(part.transpose(0, 2, 1, 3).reshape(feature, D))

    def gather_experts(halves):
        block = lax.all_gather(halves, LINE, axis=0)
        block = block.reshape(slabs, cores, planes, 2 * EXPERTS, depth, wide)
        if depth % 16 == 0:
            return block
        block = block.transpose(3, 0, 2, 1, 4, 5).reshape(2 * EXPERTS, D, wide)
        return block[None, None, None]

    expert_weights = [gather_experts(expert_packs[0])]
    ints = whole_f.reshape(sizes() + whole_f.shape[1:])
    whole = whole_f[:, : 2 + LAYERS].astype(jnp.int32)
    smalls = whole_f[:, 8:, :rows_of].transpose(1, 0, 2).reshape(16, D)
    router_all = smalls[: LAYERS * EXPERTS].reshape(LAYERS, EXPERTS, D).transpose(0, 2, 1)
    router_all = router_all.astype(jnp.bfloat16)
    gains_f = smalls[LAYERS * EXPERTS :]
    routes_lane = lax.dynamic_index_in_dim(
        whole.reshape(slabs, planes, cores, sides, 2 + LAYERS, own), z_at, 0, False
    )
    routes_lane = lax.dynamic_index_in_dim(routes_lane, core_at, 1, False)[:, :, 2:]
    routes_lane = routes_lane.transpose(2, 0, 1, 3)[..., None]
    routes_own = lax.dynamic_slice_in_dim(routes, side_at * own, own, axis=1)

    extent = -(-shard_rows // 256) * 256
    table = jnp.pad(vocab_table.astype(jnp.bfloat16), ((0, extent - shard_rows), (0, 0)))
    offsets = jnp.arange(chunk, dtype=jnp.int32)
    first_blk = z_at * planes * cores + core_at
    query_pos = jnp.concatenate([(first_blk + cores * part) * chunk + offsets for part in range(planes)])
    near_blks = [first_blk - 1 + part for part in range(2 * planes)]
    near_pos = jnp.concatenate([blk * chunk + offsets for blk in near_blks])
    query_seg = segment_of(query_pos, cont_ends)
    near_seg = segment_of(near_pos, cont_ends)
    places = (query_pos[None, :], query_seg[None, :], near_pos[:, None], near_seg[:, None])

    stream = embed(table, ints, own, shard_rows, 2)

    kept = []
    for layer_index in range(LAYERS):
        normed_lane, qkv = gather_project(
            rms_norm(stream, gains_f[2 * layer_index]).astype(jnp.bfloat16),
            qkv_weights[layer_index], False, 3,
        )
        qkv = qkv.reshape(lane, 3 * feature)
        queries = qkv[:, 2 * feature :]
        far, near = spread_keys(qkv[:, : 2 * feature], PROMPT, 10)
        if layer_index + 1 < LAYERS:
            far, halves = lax.optimization_barrier((far, expert_packs[layer_index + 1]))
            expert_weights.append(gather_experts(halves))
        mixed_t, mixed_low, log_total = attend(queries, far, near, places, chunk)
        middle = stream + project(
            mixed_low.reshape(planes, sides, own, feature), out_weights[layer_index], False, 15
        )
        normed_two = rms_norm(middle, gains_f[2 * layer_index + 1]).astype(jnp.bfloat16)
        chance = jax.nn.softmax(matmul(normed_two, router_all[layer_index]), axis=-1)
        output, wide_rows, before, hidden = experts(
            normed_two, routes_lane[layer_index], expert_weights[layer_index], 11
        )
        own_pick = (routes_own[layer_index][:, None] == expert_ids[None, :]).astype(jnp.float32)
        gate = jnp.sum(chance * own_pick, axis=1, keepdims=True)
        kept.append(
            (
                stream, normed_lane, queries, far, near, mixed_t, mixed_low, log_total, middle,
                normed_two, chance, wide_rows, before, hidden, output, own_pick, gate,
            )
        )
        stream = middle + gate * output

    final_gain = gains_f[2 * LAYERS]
    devices = tokens // own
    valid_rows = valid_f.reshape(sizes() + (1, own))
    final_all, row_logs, hits = gather_logits(
        rms_norm(stream, final_gain).astype(jnp.bfloat16), table, ints, valid_rows, shard_rows, 4
    )
    log_sums = merge_logs(row_logs.reshape(devices, 1, own), 5)
    log_sum = log_sums.reshape(tokens)
    own_log = lax.dynamic_slice_in_dim(log_sum, device_at * own, own)
    own_valid = lax.dynamic_slice_in_dim(valid_f, device_at * own, own)
    own_loss = jnp.sum(own_log * own_valid) - jnp.sum(hits)
    final_grad, table_grad = vocab_back(
        final_all, table, ints, log_sums.reshape(sizes() + (1, own)), valid_rows / token_count,
        shard_rows, 6,
    )
    stream_grad, final_gain_grad = jax.vjp(rms_norm, stream, final_gain)[1](final_grad)

    attn_packs = [None] * LAYERS
    router_list = [None] * LAYERS
    expert_sums = [None] * LAYERS
    gain_list = [None] * (2 * LAYERS + 1)
    gain_list[2 * LAYERS] = final_gain_grad
    for layer_index in reversed(range(LAYERS)):
        (
            stream, normed_lane, queries, far, near, mixed_t, mixed_low, log_total, middle,
            normed_two, chance, wide_rows, before, hidden, output, own_pick, gate,
        ) = kept[layer_index]
        out_grad = (gate * stream_grad).astype(jnp.bfloat16)
        chance_grad = jnp.sum(stream_grad * output, axis=1)[:, None] * own_pick
        choice_grad = chance * (chance_grad - jnp.sum(chance * chance_grad, axis=1, keepdims=True))
        router_list[layer_index] = jnp.dot(
            normed_two.astype(jnp.float32).T, choice_grad, precision=lax.Precision.HIGHEST
        )
        normed_grad = jnp.dot(
            choice_grad,
            router_all[layer_index].astype(jnp.float32).T,
            precision=lax.Precision.HIGHEST,
        )
        rows_grad, expert_grad = experts_back(
            out_grad, routes_lane[layer_index], expert_weights[layer_index], wide_rows, before,
            hidden, 12,
        )
        normed_grad = normed_grad + rows_grad
        middle_part, gain_list[2 * layer_index + 1] = jax.vjp(
            rms_norm, middle, gains_f[2 * layer_index + 1]
        )[1](normed_grad)
        middle_grad = stream_grad + middle_part
        branch_lane, answer = gather_project(
            middle_grad.astype(jnp.bfloat16), out_weights[layer_index], True, 16
        )
        answer = answer.reshape(lane, feature)
        out_proj = inner(mixed_low, branch_lane.reshape(lane, D)).astype(jnp.bfloat16)
        query_grad, far_grad, near_grad = attend_back(
            queries, far, near, places, log_total, mixed_t, answer, chunk
        )
        key_grad = collect_keys(far_grad, near_grad, 13)
        key_grad, expert_grad = lax.optimization_barrier((key_grad, expert_grad))
        expert_sums[layer_index] = lax.psum_scatter(
            expert_grad, LINE, scatter_dimension=0, tiled=True
        )[0]
        key_grad = key_grad.astype(jnp.bfloat16)
        qkv_grad = jnp.concatenate([key_grad, query_grad], axis=1)
        qkv_proj = inner(normed_lane.reshape(lane, D), qkv_grad).astype(jnp.bfloat16)
        qkv_proj = qkv_proj.reshape(slabs, planes, cores, sides, rows_of, 3 * feature)
        qkv_proj = qkv_proj.transpose(0, 2, 1, 3, 4, 5).reshape(
            slabs * cores, groups, rows_of, 3 * feature
        )
        out_proj = out_proj.reshape(slabs * cores, rows_of, groups, feature).transpose(0, 2, 1, 3)
        attn_packs[layer_index] = jnp.concatenate([qkv_proj, out_proj], axis=3)
        normed_att_grad = project(
            qkv_grad.reshape(planes, sides, own, 3 * feature), qkv_weights[layer_index], True, 14
        )
        stream_part, gain_list[2 * layer_index] = jax.vjp(
            rms_norm, stream, gains_f[2 * layer_index]
        )[1](normed_att_grad)
        stream_grad = middle_grad + stream_part

    small = jnp.concatenate(
        [jnp.stack(router_list).transpose(1, 0, 2).reshape(D, -1), jnp.stack(gain_list).T], axis=1
    )
    small = small.reshape(devices, rows_of, -1).transpose(0, 2, 1)
    small = jnp.pad(small, ((0, 0), (0, 16 - small.shape[1]), (0, 128 - rows_of)))
    attn_pack = jnp.stack(attn_packs, axis=2).reshape(slabs, cores, -1, D).transpose(1, 0, 2, 3)
    table_share, small, attn_pack = embed_back(
        stream_grad.astype(jnp.bfloat16), ints, table_grad, small, attn_pack, shard_rows, 7
    )
    squares = sum(
        jnp.sum(jnp.square(part.astype(jnp.float32)))
        for part in [table_share[:shard_rows], small[:, :rows_of], attn_pack] + expert_sums
    )
    sums = jnp.pad(jnp.stack([squares, own_loss])[:, None], ((0, 6), (0, 127)))
    sums = jnp.sum(swap(sums[None], True, 9)[:, :2, 0], axis=0)
    square_total, loss_sum = sums[0], sums[1]
    expert_shares = []
    for expert_grad in expert_sums:
        kept_half = lax.dynamic_index_in_dim(expert_grad, x_at, 0, False)
        sent_half = lax.dynamic_index_in_dim(expert_grad, 1 - x_at, 0, False)
        got_half = lax.ppermute(sent_half, "x", ((0, 1), (1, 0)))
        expert_grad = jnp.concatenate(
            [jnp.where(x_at == 0, kept_half, got_half), jnp.where(x_at == 0, got_half, kept_half)],
            axis=-1,
        )
        expert_shares.append(
            expert_grad.reshape(2, EXPERTS, depth, planes * wide).astype(jnp.float32)
        )
    attn_pack = attn_pack.reshape(groups, LAYERS, rows_of, D)
    table_share, small = table_share[:shard_rows], small[:, :rows_of]
    router_share = (
        small[: LAYERS * EXPERTS].reshape(LAYERS, EXPERTS, rows_of).transpose(0, 2, 1)
    )
    gain_share = small[LAYERS * EXPERTS : LAYERS * EXPERTS + 2 * LAYERS + 1]
    qkv_share = lax.all_to_all(
        attn_pack[..., : 3 * feature], PLANE, split_axis=0, concat_axis=0, tiled=True
    )
    qkv_share = qkv_share.reshape(groups, LAYERS, rows_of, 3, feature)
    qkv_share = jnp.concatenate([qkv_share[:, :, :, 2:], qkv_share[:, :, :, :2]], axis=3)
    qkv_share = qkv_share.transpose(1, 2, 3, 0, 4).reshape(LAYERS, rows_of, 3 * D)
    out_share = attn_pack[..., 3 * feature :].transpose(1, 2, 0, 3).reshape(LAYERS, rows_of, D)
    out_share = lax.ppermute(out_share, ALL, head_places(True))
    attn_share = jnp.concatenate([qkv_share, out_share], axis=2).astype(jnp.float32)
    up_share = jnp.stack([share[0] for share in expert_shares])
    down_share = jnp.stack([share[1] for share in expert_shares])
    shares = (table_share, attn_share, router_share, gain_share, up_share, down_share)
    grad_norm = jnp.sqrt(square_total)
    factor = CLIP_AT / jnp.maximum(grad_norm, CLIP_AT)
    weights = (vocab_table, attn_weights, router, norm_gains, expert_up, expert_down)
    firsts = (vocab_first, attn_first, router_first, gains_first, up_first, down_first)
    seconds = (vocab_second, attn_second, router_second, gains_second, up_second, down_second)
    results = [loss_sum, token_count, grad_norm]
    for number in range(6):
        results.extend(
            adam_update(
                weights[number],
                firsts[number],
                seconds[number],
                factor * shares[number],
                STEP_RATES[number],
                DECAY_RATES[number],
            )
        )
    return tuple(results)


def solution(mesh):
    blocks, sides = mesh.shape["blk"], mesh.shape["head"]
    fine = Mesh(mesh.devices.reshape(blocks // 4, 2, 2, sides), ALL)
    weight_specs = (
        (P(ALL, None),) * 3
        + (P(None, ALL, None),) * 3
        + (P(None, ALL, None),) * 3
        + (P(None, ALL),) * 3
        + (P(None, None, BLK, "head"),) * 6
    )
    return jax.shard_map(
        per_device,
        mesh=fine,
        in_specs=(P(BLK), P(BLK), P(), P(), P(None, BLK)) + weight_specs,
        out_specs=(P(), P(), P()) + weight_specs,
        check_vma=False,
    )
```

```python
import functools

import jax
import jax.numpy as jnp
from jax import lax
from jax.experimental import pallas as pl
from jax.experimental.pallas import tpu as pltpu
from jax.sharding import Mesh, PartitionSpec as P

D = 768
HEADS = 12
HEAD_DIM = 64
EXPERTS = 2
LAYERS = 2
PROMPT = 2048
STEP = 10

NORM_EPS = 1e-06
BETA_ONE = 0.9
BETA_TWO = 0.95
ADAM_EPS = 1e-08
CLIP_AT = 0.01
MASKED = -1e30
STEP_RATES = (2.0, 0.25, 0.04, 0.4, 0.04, 0.04)
DECAY_RATES = (0.01, 0.01, 0.01, 0.0, 0.01, 0.01)

ALL = ("z", "x", "core", "head")
BLK = ("z", "x", "core")
PLANE = ("x", "head")
LINE = ("z", "core")
MIB = 2**20
MESH = pl.DeviceIdType.MESH
ANY = pl.BlockSpec(memory_space=pl.ANY)
VMEM = pl.BlockSpec(memory_space=pltpu.VMEM)


def rms_norm(stream, gain):
    return stream * lax.rsqrt(jnp.mean(stream * stream, axis=-1, keepdims=True) + NORM_EPS) * gain


def segment_of(position, cont_ends):
    later = jnp.sum((cont_ends[None, :] <= (position - PROMPT)[:, None]).astype(jnp.int32), axis=1)
    return jnp.where(position < PROMPT, 0, 1 + later)


def place():
    return tuple(lax.axis_index(name) for name in ALL)


def sizes():
    return tuple(lax.axis_size(name) for name in ALL)


def remote(source, target, send, receive, device):
    return pltpu.make_async_remote_copy(
        src_ref=source, dst_ref=target, send_sem=send, recv_sem=receive,
        device_id=device, device_id_type=MESH,
    )


def greet(devices):
    barrier = pltpu.get_barrier_semaphore()
    for device in devices:
        pl.semaphore_signal(barrier, inc=1, device_id=device, device_id_type=MESH)
    pl.semaphore_wait(barrier, len(devices))


def around():
    z, x, c, y = place()
    return (z, x, c, y), (z, 1 - x, c, y), (z, x, c, 1 - y), (z, x, 1 - c, y)


def swap_kernel(broadcast, source, out, send_sem, receive_sem, own_sem):
    n_z, n_x, n_c, n_y = sizes()
    count = n_z * n_x * n_c * n_y
    z, x, c, y = place()
    me = ((z * n_x + x) * n_c + c) * n_y + y

    def device_of(index):
        return (
            index // (n_x * n_c * n_y), index // (n_c * n_y) % n_x, index // n_y % n_c, index % n_y
        )

    def taken(index):
        return source.at[0] if broadcast else source.at[index]

    barrier = pltpu.get_barrier_semaphore()

    def call(step, unused):
        other = lax.rem(me + step, count)
        pl.semaphore_signal(barrier, inc=1, device_id=device_of(other), device_id_type=MESH)
        return unused

    lax.fori_loop(1, count, call, 0)
    own = pltpu.make_async_copy(taken(me), out.at[me], own_sem)
    own.start()
    pl.semaphore_wait(barrier, count - 1)

    def copy(step):
        other = lax.rem(me + step, count)
        return remote(
            taken(other), out.at[me], send_sem.at[step], receive_sem.at[step], device_of(other)
        )

    def start(step, unused):
        copy(step).start()
        return unused

    def finish(step, unused):
        copy(step).wait()
        return unused

    lax.fori_loop(1, count, start, 0)
    lax.fori_loop(1, count, finish, 0)
    own.wait()


def swap(blocks, broadcast, collective_id):
    count = 1
    for size in sizes():
        count *= size
    return pl.pallas_call(
        functools.partial(swap_kernel, broadcast),
        out_shape=jax.ShapeDtypeStruct((count,) + blocks.shape[1:], blocks.dtype),
        in_specs=[VMEM],
        out_specs=VMEM,
        scratch_shapes=[
            pltpu.SemaphoreType.DMA((count,)),
            pltpu.SemaphoreType.DMA((count,)),
            pltpu.SemaphoreType.DMA,
        ],
        compiler_params=pltpu.CompilerParams(collective_id=collective_id, has_side_effects=True),
    )(blocks)


def total_of(*parts):
    total = parts[0].astype(jnp.float32)
    for part in parts[1:]:
        total = total + part.astype(jnp.float32)
    return total


PIECES = 4


def spread_kernel(
    prompt_slabs, own_rows, far, near, tail, z_send, z_recv, c_send, c_recv, n_send, n_recv, own_sem
):
    n_z = lax.axis_size("z")
    lane = own_rows.shape[0]
    chunk = lane // 2
    size = lane // PIECES
    (z, x, c, y), _, _, c_near = around()
    above, below = (z + 1, x, c, y), (z - 1, x, c, y)
    in_prompt = z < prompt_slabs
    takes_down = z < prompt_slabs - 1
    gives_down = (z > 0) & (z < prompt_slabs)

    barrier = pltpu.get_barrier_semaphore()
    pl.semaphore_signal(barrier, inc=1, device_id=c_near, device_id_type=MESH)

    @pl.when(z > 0)
    def _():
        pl.semaphore_signal(barrier, inc=1, device_id=below, device_id_type=MESH)

    @pl.when(takes_down)
    def _():
        pl.semaphore_signal(barrier, inc=1, device_id=above, device_id_type=MESH)

    first, second = pl.ds(0, chunk), pl.ds(chunk, chunk)
    own = [
        pltpu.make_async_copy(own_rows.at[first], near.at[1], own_sem.at[0]),
        pltpu.make_async_copy(own_rows.at[second], near.at[3], own_sem.at[1]),
    ]
    own_far = pltpu.make_async_copy(own_rows, far.at[jnp.minimum(z, prompt_slabs - 1), c], own_sem.at[2])
    own_edge = pltpu.make_async_copy(own_rows.at[first], near.at[0], own_sem.at[3])
    edge = (z == 0) & (c == 0)
    for copy in own:
        copy.start()

    @pl.when(in_prompt)
    def _():
        own_far.start()

    @pl.when(edge)
    def _():
        own_edge.start()

    pl.semaphore_wait(
        barrier, 1 + jnp.where(z < n_z - 1, 1, 0) + jnp.where(gives_down, 1, 0)
    )

    def part(index):
        return pl.ds(index * size, size)

    def z_copy(source, slab, index, up):
        return remote(
            source, far.at[slab, c, part(index)], z_send.at[slab, index, 1 if up else 0],
            z_recv.at[slab, index], above if up else below,
        )

    def c_copy(source, slab, index):
        return remote(
            source, far.at[slab, c, part(index)], c_send.at[slab, index], c_recv.at[slab, index], c_near
        )

    def t_copy():
        return remote(own_rows.at[second], tail, n_send.at[0], n_recv.at[0], above)

    def t_hand():
        return remote(tail, near.at[0], n_send.at[1], n_recv.at[1], c_near)

    def n_copy(half):
        slot = jnp.where(c == 0, 2 * half, 2)
        return remote(
            own_rows.at[pl.ds(half * chunk, chunk)], near.at[slot], n_send.at[2 + half], n_recv.at[2 + half],
            c_near,
        )

    @pl.when(in_prompt)
    def _():
        for index in range(PIECES):
            source = own_rows.at[part(index)]

            @pl.when(z < n_z - 1)
            def _():
                z_copy(source, z, index, True).start()

            @pl.when(z > 0)
            def _():
                z_copy(source, z, index, False).start()

            c_copy(source, z, index).start()

    @pl.when((c == 1) & (z < n_z - 1))
    def _():
        t_copy().start()

    n_copy(0).start()

    @pl.when(c == 0)
    def _():
        n_copy(1).start()

    for distance in range(1, n_z):
        low_slab, high_slab = z - distance, z + distance
        for index in range(PIECES):

            @pl.when((low_slab >= 0) & (low_slab < prompt_slabs))
            def _():
                source = far.at[low_slab, c, part(index)]
                z_copy(source, low_slab, index, True).wait_recv()

                @pl.when(z < n_z - 1)
                def _():
                    z_copy(source, low_slab, index, True).start()

                c_copy(source, low_slab, index).start()

            if distance < prompt_slabs:

                @pl.when(high_slab < prompt_slabs)
                def _():
                    source = far.at[high_slab, c, part(index)]
                    z_copy(source, high_slab, index, False).wait_recv()

                    @pl.when(z > 0)
                    def _():
                        z_copy(source, high_slab, index, False).start()

                    c_copy(source, high_slab, index).start()

    @pl.when((c == 1) & (z > 0))
    def _():
        t_copy().wait_recv()
        t_hand().start()
        t_hand().wait_send()

    @pl.when((c == 1) & (z < n_z - 1))
    def _():
        t_copy().wait_send()

    @pl.when((c == 0) & (z > 0))
    def _():
        t_hand().wait_recv()

    n_copy(0).wait_send()
    n_copy(0).wait_recv()

    @pl.when(c == 0)
    def _():
        n_copy(1).wait_send()

    @pl.when(c == 1)
    def _():
        n_copy(1).wait_recv()

    for slab in range(prompt_slabs):
        for index in range(PIECES):
            copy = c_copy(own_rows.at[part(index)], slab, index)
            copy.wait_send()
            copy.wait_recv()

            @pl.when((z < n_z - 1) & (slab <= z))
            def _():
                z_copy(own_rows.at[part(index)], slab, index, True).wait_send()

            @pl.when((z > 0) & (slab >= z))
            def _():
                z_copy(own_rows.at[part(index)], slab, index, False).wait_send()

    for copy in own:
        copy.wait()

    @pl.when(in_prompt)
    def _():
        own_far.wait()

    @pl.when(edge)
    def _():
        own_edge.wait()


def spread_keys(own_rows, prompt_rows, collective_id):
    lane, width = own_rows.shape
    slabs = prompt_rows // (2 * lane)
    dma = pltpu.SemaphoreType.DMA
    far, near, _ = pl.pallas_call(
        functools.partial(spread_kernel, slabs),
        out_shape=(
            jax.ShapeDtypeStruct((slabs, 2, lane, width), own_rows.dtype),
            jax.ShapeDtypeStruct((4, lane // 2, width), own_rows.dtype),
            jax.ShapeDtypeStruct((lane // 2, width), own_rows.dtype),
        ),
        in_specs=[VMEM],
        out_specs=(VMEM,) * 3,
        scratch_shapes=[
            dma((slabs, PIECES, 2)), dma((slabs, PIECES)), dma((slabs, PIECES)), dma((slabs, PIECES)),
            dma((4,)), dma((4,)), dma((4,)),
        ],
        compiler_params=pltpu.CompilerParams(collective_id=collective_id, has_side_effects=True),
    )(own_rows)
    return far.reshape(prompt_rows, width), near.reshape(2 * lane, width)


def collect_kernel(
    prompt_slabs, far, near, query_grad, whole, out, own, c_got, z_got, n_got, tail_pass, tail_got,
    c_send, c_recv, z_send, z_recv, n_send, n_recv,
):
    n_z = lax.axis_size("z")
    lane = out.shape[0]
    chunk = lane // 2
    size = lane // PIECES
    (z, x, c, y), _, _, c_near = around()
    above, below = (z + 1, x, c, y), (z - 1, x, c, y)

    barrier = pltpu.get_barrier_semaphore()
    pl.semaphore_signal(barrier, inc=1, device_id=c_near, device_id_type=MESH)

    @pl.when(z < n_z - 1)
    def _():
        pl.semaphore_signal(barrier, inc=1, device_id=above, device_id_type=MESH)

    pl.semaphore_wait(barrier, 1 + jnp.where(z > 0, 1, 0))

    def part(index):
        return pl.ds(index * size, size)

    def c_copy(slab, index):
        return remote(
            far.at[slab, 1 - c, part(index)], c_got.at[slab, part(index)], c_send.at[slab, index],
            c_recv.at[slab, index], c_near,
        )

    def z_copy(slab, index):
        return remote(
            own.at[slab, part(index)], z_got.at[slab, part(index)], z_send.at[slab, index],
            z_recv.at[slab, index], below,
        )

    def n_copy(half):
        slot = jnp.where(c == 0, 2, 2 * half)
        return remote(near.at[slot], n_got.at[half], n_send.at[half], n_recv.at[half], c_near)

    def t_hand():
        return remote(near.at[0], tail_pass, n_send.at[2], n_recv.at[2], c_near)

    def t_copy():
        return remote(tail_pass, tail_got, n_send.at[3], n_recv.at[3], below)

    for slab in range(prompt_slabs):
        for index in range(PIECES):
            c_copy(slab, index).start()
    n_copy(0).start()

    @pl.when(c == 1)
    def _():
        n_copy(1).start()

    @pl.when((c == 0) & (z > 0))
    def _():
        t_hand().start()

    for slab in range(prompt_slabs):
        for index in range(PIECES):
            c_copy(slab, index).wait_recv()
            rows = part(index)
            mine = total_of(far[slab, c, rows, :], c_got[slab, rows, :])

            @pl.when((z == n_z - 1) & (z > slab))
            def _():
                own[slab, rows, :] = mine.astype(jnp.bfloat16)
                z_copy(slab, index).start()

            @pl.when((z < n_z - 1) & (z > slab))
            def _():
                z_copy(slab, index).wait_recv()
                own[slab, rows, :] = total_of(mine, z_got[slab, rows, :]).astype(jnp.bfloat16)
                z_copy(slab, index).start()

            @pl.when((z < n_z - 1) & (z == slab))
            def _():
                z_copy(slab, index).wait_recv()
                out[rows, :] = total_of(mine, z_got[slab, rows, :])

            @pl.when((z == n_z - 1) & (z == slab))
            def _():
                out[rows, :] = mine

    @pl.when((c == 1) & (z > 0))
    def _():
        t_hand().wait_recv()
        t_copy().start()

    @pl.when(z >= prompt_slabs)
    def _():
        out[...] = jnp.zeros_like(out)

    n_copy(0).wait_recv()
    first, second = pl.ds(0, chunk), pl.ds(chunk, chunk)
    out[first, :] += total_of(near[1], n_got[0])
    out[second, :] += near[3].astype(jnp.float32)

    @pl.when(c == 0)
    def _():
        n_copy(1).wait_recv()
        out[second, :] += n_got[1].astype(jnp.float32)

    @pl.when((c == 1) & (z < n_z - 1))
    def _():
        t_copy().wait_recv()
        out[second, :] += tail_got[...].astype(jnp.float32)

    whole[...] = jnp.concatenate([out[...].astype(jnp.bfloat16), query_grad[...]], axis=1)

    @pl.when((c == 1) & (z > 0))
    def _():
        t_copy().wait_send()

    @pl.when((c == 0) & (z > 0))
    def _():
        t_hand().wait_send()

    n_copy(0).wait_send()

    @pl.when(c == 1)
    def _():
        n_copy(1).wait_send()

    for slab in range(prompt_slabs):
        for index in range(PIECES):
            c_copy(slab, index).wait_send()

            @pl.when(z > slab)
            def _():
                z_copy(slab, index).wait_send()


def collect_keys(far, near, query_grad, collective_id):
    prompt_rows, width = far.shape
    lane = near.shape[0] // 2
    slabs = prompt_rows // (2 * lane)
    dma = pltpu.SemaphoreType.DMA
    low = jnp.bfloat16
    return pl.pallas_call(
        functools.partial(collect_kernel, slabs),
        out_shape=jax.ShapeDtypeStruct((lane, width + query_grad.shape[1]), low),
        in_specs=[VMEM] * 3,
        out_specs=VMEM,
        scratch_shapes=[
            pltpu.VMEM((lane, width), jnp.float32),
            pltpu.VMEM((slabs, lane, width), low),
            pltpu.VMEM((slabs, lane, width), low),
            pltpu.VMEM((slabs, lane, width), low),
            pltpu.VMEM((2, lane // 2, width), low),
            pltpu.VMEM((lane // 2, width), low),
            pltpu.VMEM((lane // 2, width), low),
            dma((slabs, PIECES)), dma((slabs, PIECES)), dma((slabs, PIECES)), dma((slabs, PIECES)),
            dma((4,)), dma((4,)),
        ],
        compiler_params=pltpu.CompilerParams(
            collective_id=collective_id, has_side_effects=True, vmem_limit_bytes=20 * MIB
        ),
    )(far.astype(low).reshape(slabs, 2, lane, width), near.astype(low).reshape(4, lane // 2, width), query_grad)


def greet_all():
    n_z, n_x, n_c, n_y = sizes()
    count = n_z * n_x * n_c * n_y
    barrier = pltpu.get_barrier_semaphore()

    def call(step, unused):
        pl.semaphore_signal(barrier, inc=1, device_id=device_after(step), device_id_type=MESH)
        return unused

    lax.fori_loop(1, count, call, 0)
    pl.semaphore_wait(barrier, count - 1)


def index_after(step):
    n_z, n_x, n_c, n_y = sizes()
    z, x, c, y = place()
    me = ((z * n_x + x) * n_c + c) * n_y + y
    return lax.rem(me + step, n_z * n_x * n_c * n_y)


def device_after(step):
    _, n_x, n_c, n_y = sizes()
    index = index_after(step)
    return (
        index // (n_x * n_c * n_y), index // (n_c * n_y) % n_x, index // n_y % n_c, index % n_y
    )


def greet_near():
    n_z = lax.axis_size("z")
    (z, x, c, y), x_near, y_near, c_near = around()
    barrier = pltpu.get_barrier_semaphore()
    for device in (x_near, y_near, c_near):
        pl.semaphore_signal(barrier, inc=1, device_id=device, device_id_type=MESH)

    @pl.when(z > 0)
    def _():
        pl.semaphore_signal(barrier, inc=1, device_id=(z - 1, x, c, y), device_id_type=MESH)

    @pl.when(z < n_z - 1)
    def _():
        pl.semaphore_signal(barrier, inc=1, device_id=(z + 1, x, c, y), device_id_type=MESH)

    pl.semaphore_wait(barrier, 3 + jnp.where(z > 0, 1, 0) + jnp.where(z < n_z - 1, 1, 0))


Z_PIECES = 4


def gather_sems():
    n_z = lax.axis_size("z")
    dma = pltpu.SemaphoreType.DMA
    return [
        dma((n_z, Z_PIECES, 2)), dma((n_z, Z_PIECES)), dma((n_z, 2)), dma((n_z, 2)), dma((n_z, 2)),
        dma((n_z, 2)), dma((n_z, 4)), dma((n_z, 4)), dma,
    ]


def gather_slabs(rows_in, out, sems, work, beside=lambda step: None):
    z_send, z_recv, x_send, x_recv, y_send, y_recv, c_send, c_recv, own_sem = sems
    n_z = lax.axis_size("z")
    half = rows_in.shape[0] // 2
    size = rows_in.shape[0] // Z_PIECES
    (z, x, c, y), x_near, y_near, c_near = around()
    low, high = pl.ds(0, half), pl.ds(half, half)
    everything = pl.ds(0, 2 * half)
    own = pltpu.make_async_copy(rows_in, out.at[z, x, c, y], own_sem)
    own.start()

    def block(origin, px, py, rows):
        return out.at[origin, px, c, py, rows]

    def z_copy(source, origin, index, up):
        rows = pl.ds(index * size, size)
        other = (z + 1, x, c, y) if up else (z - 1, x, c, y)
        return remote(
            source.at[rows], block(origin, x, y, rows), z_send.at[origin, index, 1 if up else 0],
            z_recv.at[origin, index], other,
        )

    def x_copy(source, origin):
        return remote(source, out.at[origin, x, c, y], x_send.at[origin, 0], x_recv.at[origin, 0], x_near)

    def y_copy(source, origin):
        return remote(source, out.at[origin, x, c, y], y_send.at[origin, 0], y_recv.at[origin, 0], y_near)

    def x_relay(origin):
        part = block(origin, x, 1 - y, high)
        return remote(part, part, x_send.at[origin, 1], x_recv.at[origin, 1], x_near)

    def y_relay(origin):
        part = block(origin, 1 - x, y, low)
        return remote(part, part, y_send.at[origin, 1], y_recv.at[origin, 1], y_near)

    def c_copy(source, origin, px, py):
        slot = px * 2 + py
        return remote(
            source, out.at[origin, px, c, py], c_send.at[origin, slot], c_recv.at[origin, slot], c_near
        )

    def column(origin):
        return out.at[origin, x, c, y]

    def spread(source, origin):
        x_copy(source, origin).start()
        y_copy(source, origin).start()
        c_copy(source, origin, x, y).start()

    def relay(origin):
        x_copy(column(origin), origin).wait_recv()
        y_relay(origin).start()
        y_copy(column(origin), origin).wait_recv()
        x_relay(origin).start()
        c_copy(block(origin, 1 - x, y, everything), origin, 1 - x, y).start()
        c_copy(block(origin, x, 1 - y, everything), origin, x, 1 - y).start()

    def finish(origin):
        x_relay(origin).wait_recv()
        y_relay(origin).wait_recv()
        c_copy(block(origin, 1 - x, 1 - y, everything), origin, 1 - x, 1 - y).start()

    def use(origin):
        for px in range(2):
            for py in range(2):
                c_copy(out.at[origin, px, c, py], origin, px, py).wait_recv()
        work(origin)

    def arrive(step):
        below, above = z - step, z + step

        @pl.when(below >= 0)
        def _():
            for index in range(Z_PIECES):
                z_copy(rows_in, below, index, True).wait_recv()

                @pl.when(z < n_z - 1)
                def _():
                    z_copy(column(below), below, index, True).start()

            spread(column(below), below)

        @pl.when(above < n_z)
        def _():
            for index in range(Z_PIECES):
                z_copy(rows_in, above, index, False).wait_recv()

                @pl.when(z > 0)
                def _():
                    z_copy(column(above), above, index, False).start()

            spread(column(above), above)

    for index in range(Z_PIECES):

        @pl.when(z < n_z - 1)
        def _():
            z_copy(rows_in, z, index, True).start()

        @pl.when(z > 0)
        def _():
            z_copy(rows_in, z, index, False).start()

    spread(rows_in, z)
    for step in range(1, n_z + 3):
        if step < n_z:
            arrive(step)
        for action, back in ((relay, 1), (finish, 2), (use, 3)):
            late = step - back
            if late == 0:
                if action is use:
                    own.wait()
                action(z)
            elif 0 < late < n_z:
                for origin in (z - late, z + late):

                    @pl.when((origin >= 0) & (origin < n_z))
                    def _():
                        action(origin)

        beside(step)

    def close(origin, unused):
        x_copy(rows_in, origin).wait_send()
        y_copy(rows_in, origin).wait_send()
        x_relay(origin).wait_send()
        y_relay(origin).wait_send()
        for px in range(2):
            for py in range(2):
                c_copy(out.at[origin, px, c, py], origin, px, py).wait_send()
        for index in range(Z_PIECES):

            @pl.when((z < n_z - 1) & (origin <= z))
            def _():
                z_copy(rows_in, origin, index, True).wait_send()

            @pl.when((z > 0) & (origin >= z))
            def _():
                z_copy(rows_in, origin, index, False).wait_send()

        return unused

    lax.fori_loop(0, n_z, close, 0)


def line_gather_sems():
    n_z = lax.axis_size("z")
    dma = pltpu.SemaphoreType.DMA
    return [dma((n_z, 2, 2)), dma((n_z, 2)), dma((n_z, 2)), dma((n_z, 2)), dma((2,))]


def line_gather(own_parts, all_parts, sems):
    z_send, z_recv, c_send, c_recv, own_sem = sems
    n_z = lax.axis_size("z")
    (z, x, c, y), _, _, c_near = around()
    numbers = range(len(own_parts))

    def z_copy(source, number, origin, up):
        return remote(
            source, all_parts[number](origin, c), z_send.at[origin, number, 1 if up else 0],
            z_recv.at[origin, number], (z + 1, x, c, y) if up else (z - 1, x, c, y),
        )

    def c_copy(source, number, origin):
        return remote(
            source, all_parts[number](origin, c), c_send.at[origin, number], c_recv.at[origin, number], c_near
        )

    own = [
        pltpu.make_async_copy(own_parts[number], all_parts[number](z, c), own_sem.at[number])
        for number in numbers
    ]
    for copy in own:
        copy.start()
    for number in numbers:
        source = own_parts[number]

        @pl.when(z < n_z - 1)
        def _():
            z_copy(source, number, z, True).start()

        @pl.when(z > 0)
        def _():
            z_copy(source, number, z, False).start()

        c_copy(source, number, z).start()

    def beside(step):
        below, above = z - step, z + step

        @pl.when((step >= 1) & (below >= 0))
        def _():
            for number in numbers:
                source = all_parts[number](below, c)
                z_copy(source, number, below, True).wait_recv()

                @pl.when(z < n_z - 1)
                def _():
                    z_copy(source, number, below, True).start()

                c_copy(source, number, below).start()

        @pl.when((step >= 1) & (above < n_z))
        def _():
            for number in numbers:
                source = all_parts[number](above, c)
                z_copy(source, number, above, False).wait_recv()

                @pl.when(z > 0)
                def _():
                    z_copy(source, number, above, False).start()

                c_copy(source, number, above).start()

    def close():
        for copy in own:
            copy.wait()

        def one(origin, unused):
            for number in numbers:
                c_copy(own_parts[number], number, origin).wait()

                @pl.when((z < n_z - 1) & (origin <= z))
                def _():
                    z_copy(own_parts[number], number, origin, True).wait_send()

                @pl.when((z > 0) & (origin >= z))
                def _():
                    z_copy(own_parts[number], number, origin, False).wait_send()

            return unused

        lax.fori_loop(0, n_z, one, 0)

    return beside, close


def line_sems():
    n_z = lax.axis_size("z")
    dma = pltpu.SemaphoreType.DMA
    return [dma, dma, dma((n_z, 2)), dma((n_z, 2))]


def line_sum(pack, out, lanes, got, below, above, sems):
    c_send, c_recv, z_send, z_recv = sems
    n_z = lax.axis_size("z")
    (z, x, c, y), _, _, c_near = around()
    handed = remote(pack.at[1 - c], got, c_send, c_recv, c_near)

    def z_copy(slab, up):
        return remote(
            lanes.at[slab], below.at[slab] if up else above.at[slab], z_send.at[slab, 1 if up else 0],
            z_recv.at[slab, 1 if up else 0], (z + 1, x, c, y) if up else (z - 1, x, c, y),
        )

    handed.start()

    def merge():
        handed.wait()
        lanes[...] = total_of(pack[c], got[...]).astype(jnp.bfloat16)

    def hop(turn, step):
        high, low = n_z - 1 - turn, turn

        @pl.when((z == step - 1 - turn) & (z < high))
        def _():
            @pl.when(z > 0)
            def _():
                z_copy(high, True).wait_recv()
                lanes[high] = total_of(lanes[high], below[high]).astype(jnp.bfloat16)

            z_copy(high, True).start()

        @pl.when((n_z - 1 - z == step - 1 - turn) & (z > low))
        def _():
            @pl.when(z < n_z - 1)
            def _():
                z_copy(low, False).wait_recv()
                lanes[low] = total_of(lanes[low], above[low]).astype(jnp.bfloat16)

            z_copy(low, False).start()

    def beside(step):
        if step == 1:
            merge()
        if step < n_z:

            def body(turn, unused):
                hop(turn, step)
                return unused

            lax.fori_loop(0, n_z - 1, body, 0)

    def close():
        out[...] = lanes[z].astype(jnp.float32)

        @pl.when(z > 0)
        def _():
            z_copy(z, True).wait_recv()
            out[...] += below[z].astype(jnp.float32)

        @pl.when(z < n_z - 1)
        def _():
            z_copy(z, False).wait_recv()
            out[...] += above[z].astype(jnp.float32)

        def sent(slab, unused):
            @pl.when(slab > z)
            def _():
                z_copy(slab, True).wait_send()

            @pl.when(slab < z)
            def _():
                z_copy(slab, False).wait_send()

            return unused

        lax.fori_loop(0, n_z, sent, 0)

    return beside, close


def in_pairs(values, slab, px, pc, row):
    return jnp.concatenate([values[slab, px, pc, py, row : row + 1, :] for py in range(2)], axis=1)


def vocab_ids(extent, chunk, shard_rows):
    n_z, n_x, n_c, n_y = sizes()
    z, x, c, y = place()
    me = ((z * n_x + x) * n_c + c) * n_y + y
    rows = lax.broadcasted_iota(jnp.int32, (extent, chunk), 0)
    return rows + me * shard_rows


def logits_kernel(shard_rows, rows_in, table, ints, valid, out, logs, hits, *sems):
    extent = table.shape[0]
    chunk = 2 * rows_in.shape[0]
    scale = table.shape[1] ** (-0.5)
    greet_near()
    hits[...] = jnp.zeros_like(hits)

    def work(slab):
        def one(index, unused):
            px, pc = index // 2, index % 2
            rows = out[slab, px, pc].reshape(chunk, -1)
            value = outer(table[...], rows) * scale
            ids = vocab_ids(extent, chunk, shard_rows)
            inside = lax.broadcasted_iota(jnp.int32, (extent, chunk), 0) < shard_rows
            target = in_pairs(ints, slab, px, pc, 1).astype(jnp.int32)
            shown = in_pairs(valid, slab, px, pc, 0)
            hit = jnp.where(ids == target, value, 0.0)
            hits[...] += jnp.sum(hit, axis=0, keepdims=True) * shown
            value = jnp.where(inside, value, MASKED)
            peak = jnp.max(value, axis=0, keepdims=True)
            log = peak + jnp.log(jnp.sum(jnp.exp(value - peak), axis=0, keepdims=True))
            half = chunk // 2
            logs[slab, px, pc, 0] = log[:, :half]
            logs[slab, px, pc, 1] = log[:, half:]
            return unused

        lax.fori_loop(0, 4, one, 0)

    gather_slabs(rows_in, out, sems, work)


def gather_logits(rows, table, ints, valid, shard_rows, collective_id):
    own, width = rows.shape
    shape = sizes() + (own, width)
    return pl.pallas_call(
        functools.partial(logits_kernel, shard_rows),
        out_shape=(
            jax.ShapeDtypeStruct(shape, rows.dtype),
            jax.ShapeDtypeStruct(sizes() + (1, own), jnp.float32),
            jax.ShapeDtypeStruct((1, 2 * own), jnp.float32),
        ),
        in_specs=[VMEM] * 4,
        out_specs=(VMEM,) * 3,
        scratch_shapes=gather_sems(),
        compiler_params=pltpu.CompilerParams(
            collective_id=collective_id, has_side_effects=True,
            vmem_limit_bytes=lax.axis_size("z") * 2 * MIB + 20 * MIB,
        ),
    )(rows, table, ints, valid)


def embed_back_kernel(
    shard_rows, rows_in, ints, table_grad, smalls, pack, out, small_sum, pack_sum,
    slabs, small_got, lanes, got, below, above, *sems
):
    extent = out.shape[0]
    chunk = 2 * rows_in.shape[0]
    small_send, small_recv = sems[-6:-4]
    n_z, n_x, n_c, n_y = sizes()
    count = n_z * n_x * n_c * n_y
    me = index_after(0)
    greet_all()

    def small(step):
        return remote(
            smalls.at[index_after(step)], small_got.at[me], small_send.at[step], small_recv.at[step],
            device_after(step),
        )

    def each(action):
        def body(step, unused):
            action(step)
            return unused

        lax.fori_loop(1, count, body, 0)

    each(lambda step: small(step).start())
    beside, close_line = line_sum(pack, pack_sum, lanes, got, below, above, sems[-4:])
    small_got[me] = smalls[me]
    out[...] = table_grad[...]

    def work(slab):
        def one(index, unused):
            px, pc = index // 2, index % 2
            token = in_pairs(ints, slab, px, pc, 0).astype(jnp.int32)
            hot = vocab_ids(extent, chunk, shard_rows) == token
            hot = jnp.where(hot, 1.0, 0.0).astype(jnp.bfloat16)
            out[...] += matmul(hot, slabs[slab, px, pc].reshape(chunk, -1))
            return unused

        lax.fori_loop(0, 4, one, 0)

    gather_slabs(rows_in, slabs, sems[:-6], work, beside)
    close_line()
    each(lambda step: small(step).wait())
    small_sum[...] = jnp.sum(small_got[...], axis=0)


def embed_back(rows, ints, table_grad, smalls, pack, shard_rows, collective_id):
    own, width = rows.shape
    line = pack.shape[1:]
    count = smalls.shape[0]
    dma = pltpu.SemaphoreType.DMA
    return pl.pallas_call(
        functools.partial(embed_back_kernel, shard_rows),
        out_shape=(
            jax.ShapeDtypeStruct(table_grad.shape, jnp.float32),
            jax.ShapeDtypeStruct(smalls.shape[1:], jnp.float32),
            jax.ShapeDtypeStruct(line[1:], jnp.float32),
        ),
        in_specs=[VMEM] * 5,
        out_specs=(VMEM,) * 3,
        scratch_shapes=[
            pltpu.VMEM(sizes() + (own, width), rows.dtype), pltpu.VMEM(smalls.shape, jnp.float32),
            pltpu.VMEM(line, pack.dtype), pltpu.VMEM(line, pack.dtype),
            pltpu.VMEM(line, pack.dtype), pltpu.VMEM(line, pack.dtype),
        ] + gather_sems() + [dma((count,)), dma((count,))] + line_sems(),
        compiler_params=pltpu.CompilerParams(
            collective_id=collective_id, has_side_effects=True,
            vmem_limit_bytes=lax.axis_size("z") * 2 * MIB + 28 * MIB,
        ),
    )(rows, ints, table_grad, smalls, pack)


def slab_order():
    n_z = lax.axis_size("z")
    z = lax.axis_index("z")
    up, down = n_z - 1 - z, z
    longer, shorter = jnp.maximum(up, down), jnp.minimum(up, down)
    far_side = jnp.where(up >= down, 1, -1)

    def target(step):
        late = step - (longer - shorter)
        near_side = jnp.where(late % 2 == 0, far_side, -far_side)
        return jnp.where(
            late < 0, z + far_side * (longer - step), z + near_side * (shorter - late // 2)
        )

    return target


def scatter_scratch(rows, width):
    n_z, n_x, n_c, n_y = sizes()
    half = rows // 2
    low = jnp.bfloat16
    dma = pltpu.SemaphoreType.DMA
    return [
        pltpu.VMEM((n_z, n_x, n_y, rows, width), low),
        pltpu.VMEM((n_z, n_x, n_y, rows, width), low),
        pltpu.VMEM((n_z, n_x, n_y, rows, width), low),
        pltpu.VMEM((n_z, 2, half, width), low),
        pltpu.VMEM((n_z, 2, half, width), low),
        pltpu.VMEM((n_z, half, width), low),
        pltpu.VMEM((n_z, half, width), low),
        pltpu.VMEM((n_z, rows, width), low),
        pltpu.VMEM((n_z, rows, width), low),
        dma((n_z, 2)), dma((n_z, 2)), dma((n_z, 3)), dma((n_z, 3)), dma((n_z, 3)),
        dma((n_z, 3)), dma((n_z, 2)), dma((n_z, 2, 2)),
    ]


def scatter_slabs(out, scratch, before, make, after, beside=lambda step: None):
    (
        lanes, handed, c_got, x_got, y_got, x_last, y_last, below, above,
        c_send, c_recv, x_send, x_recv, y_send, y_recv, z_send, z_recv,
    ) = scratch
    n_z = lax.axis_size("z")
    rows = out.shape[0]
    half = rows // 2
    (z, x, c, y), x_near, y_near, c_near = around()
    halves = (pl.ds(0, half), pl.ds(half, half))
    low, high = halves
    target = slab_order()

    def c_copy(slab, px):
        return remote(
            handed.at[slab, px], c_got.at[slab, px], c_send.at[slab, px], c_recv.at[slab, px], c_near
        )

    def x_first(slab, part):
        block = lanes.at[slab, 1 - x, y if part == 0 else 1 - y, low]
        return remote(block, x_got.at[slab, part], x_send.at[slab, part], x_recv.at[slab, part], x_near)

    def y_first(slab, part):
        block = lanes.at[slab, x if part == 0 else 1 - x, 1 - y, high]
        return remote(block, y_got.at[slab, part], y_send.at[slab, part], y_recv.at[slab, part], y_near)

    def y_second(slab):
        block = lanes.at[slab, x, 1 - y, low]
        return remote(block, y_last.at[slab], y_send.at[slab, 2], y_recv.at[slab, 2], y_near)

    def x_second(slab):
        block = lanes.at[slab, 1 - x, y, high]
        return remote(block, x_last.at[slab], x_send.at[slab, 2], x_recv.at[slab, 2], x_near)

    def z_up(slab, part):
        return remote(
            lanes.at[slab, x, y, halves[part]], below.at[slab, halves[part]], z_send.at[slab, part],
            z_recv.at[slab, 0, part], (z + 1, x, c, y),
        )

    def z_down(slab, part):
        return remote(
            lanes.at[slab, x, y, halves[part]], above.at[slab, halves[part]], z_send.at[slab, part],
            z_recv.at[slab, 1, part], (z - 1, x, c, y),
        )

    def produce(step):
        slab = target(step)
        before(step)

        def hand(px, unused):
            handed[slab, px] = make(step, slab, px, 1 - c).reshape(2, rows, -1)
            c_copy(slab, px).start()
            return unused

        def keep(px, unused):
            lanes[slab, px] = make(step, slab, px, c).reshape(2, rows, -1)
            return unused

        lax.fori_loop(0, 2, hand, 0)
        lax.fori_loop(0, 2, keep, 0)

    def begin(step):
        slab = target(step)
        for px in range(2):
            c_copy(slab, px).wait_recv()

        def merge(px, py):
            lanes[slab, px, py] = total_of(lanes[slab, px, py], c_got[slab, px, py]).astype(jnp.bfloat16)

        merge(1 - x, 1 - y)
        x_first(slab, 1).start()
        y_first(slab, 1).start()
        merge(1 - x, y)
        x_first(slab, 0).start()
        merge(x, 1 - y)
        y_first(slab, 0).start()
        merge(x, y)
        after(step)

    def middle(step):
        slab = target(step)
        x_first(slab, 1).wait_recv()
        x_first(slab, 0).wait_send()
        y_first(slab, 0).wait_send()
        lanes[slab, x, 1 - y, low] = total_of(
            lanes[slab, x, 1 - y, low], x_got[slab, 1]
        ).astype(jnp.bfloat16)
        y_second(slab).start()
        y_first(slab, 1).wait_recv()
        lanes[slab, 1 - x, y, high] = total_of(
            lanes[slab, 1 - x, y, high], y_got[slab, 1]
        ).astype(jnp.bfloat16)
        x_second(slab).start()

    def finish(step):
        slab = target(step)
        for part in range(2):
            if part == 0:
                x_first(slab, 0).wait_recv()
                y_second(slab).wait_recv()
                value = total_of(lanes[slab, x, y, low], x_got[slab, 0], y_last[slab])
            else:
                y_first(slab, 0).wait_recv()
                x_second(slab).wait_recv()
                value = total_of(lanes[slab, x, y, high], y_got[slab, 0], x_last[slab])
            rows_of = halves[part]

            @pl.when(slab > z)
            def _():
                @pl.when(z == 0)
                def _():
                    lanes[slab, x, y, rows_of] = value.astype(jnp.bfloat16)

                @pl.when(z > 0)
                def _():
                    z_up(slab, part).wait_recv()
                    lanes[slab, x, y, rows_of] = total_of(value, below[slab, rows_of]).astype(jnp.bfloat16)

                z_up(slab, part).start()

            @pl.when(slab < z)
            def _():
                @pl.when(z == n_z - 1)
                def _():
                    lanes[slab, x, y, rows_of] = value.astype(jnp.bfloat16)

                @pl.when(z < n_z - 1)
                def _():
                    z_down(slab, part).wait_recv()
                    lanes[slab, x, y, rows_of] = total_of(value, above[slab, rows_of]).astype(jnp.bfloat16)

                z_down(slab, part).start()

            @pl.when(slab == z)
            def _():
                out[rows_of, :] = value

                @pl.when(z > 0)
                def _():
                    z_up(slab, part).wait_recv()
                    out[rows_of, :] += below[slab, rows_of].astype(jnp.float32)

                @pl.when(z < n_z - 1)
                def _():
                    z_down(slab, part).wait_recv()
                    out[rows_of, :] += above[slab, rows_of].astype(jnp.float32)

    def turn(step, unused):
        for action, back in ((produce, 0), (begin, 0), (middle, 1), (finish, 2)):

            @pl.when((step >= back) & (step < n_z + back))
            def _():
                action(step - back)

        beside(step)
        return unused

    lax.fori_loop(0, n_z + 2, turn, 0)

    def close(slab, unused):
        for px in range(2):
            c_copy(slab, px).wait_send()
        x_first(slab, 1).wait_send()
        y_first(slab, 1).wait_send()
        x_second(slab).wait_send()
        y_second(slab).wait_send()
        for part in range(2):

            @pl.when(slab > z)
            def _():
                z_up(slab, part).wait_send()

            @pl.when(slab < z)
            def _():
                z_down(slab, part).wait_send()

        return unused

    lax.fori_loop(0, n_z, close, 0)


def embed_kernel(shard_rows, table, ints, qkv_own, out_own, out, qkv_all, out_all, *scratch):
    extent = table.shape[0]
    chunk = 2 * out.shape[0]
    greet_near()
    beside, close = line_gather(
        (qkv_own, out_own),
        (lambda pz, pc: qkv_all.at[:, pz, :, pc], lambda pz, pc: out_all.at[:, pz, pc]),
        scratch[-5:],
    )

    def make(step, slab, px, pc):
        token = in_pairs(ints, slab, px, pc, 0).astype(jnp.int32)
        hot = vocab_ids(extent, chunk, shard_rows) == token
        hot = jnp.where(hot, 1.0, 0.0).astype(jnp.bfloat16)
        return inner(hot, table[...]).astype(jnp.bfloat16)

    scatter_slabs(out, scratch[:-5], lambda step: None, make, lambda step: None, beside)
    close()


def embed(table, ints, qkv_own, out_own, own, shard_rows, collective_id):
    width = table.shape[1]
    n_z, n_x, n_c, _ = sizes()
    layers = qkv_own.shape[0]
    return pl.pallas_call(
        functools.partial(embed_kernel, shard_rows),
        out_shape=(
            jax.ShapeDtypeStruct((own, width), jnp.float32),
            jax.ShapeDtypeStruct((layers, n_z, n_x, n_c) + qkv_own.shape[2:], qkv_own.dtype),
            jax.ShapeDtypeStruct((layers, n_z, n_c) + out_own.shape[1:], out_own.dtype),
        ),
        in_specs=[VMEM] * 4,
        out_specs=(VMEM,) * 3,
        scratch_shapes=scatter_scratch(own, width) + line_gather_sems(),
        compiler_params=pltpu.CompilerParams(
            collective_id=collective_id, has_side_effects=True,
            vmem_limit_bytes=lax.axis_size("z") * 3 * MIB + 12 * MIB,
        ),
    )(table, ints, qkv_own, out_own)


def vocab_back_kernel(
    shard_rows, held, rows_all, table, ints, logs, weights, out, table_grad, slab_rows, changes, slab_sem, *scratch
):
    extent, width = table.shape
    chunk = 2 * out.shape[0]
    scale = width ** (-0.5)
    n_z = lax.axis_size("z")
    target = slab_order()

    def load(step):
        return pltpu.make_async_copy(
            rows_all.at[target(step)], slab_rows.at[step % 2], slab_sem.at[step % 2]
        )

    if not held:
        load(0).start()
    greet_near()
    table_grad[...] = jnp.zeros_like(table_grad)

    def rows_of(step, px, pc):
        if held:
            return rows_all[target(step), px, pc].reshape(chunk, width)
        return slab_rows[step % 2, px, pc].reshape(chunk, width)

    def before(step):
        if held:
            return
        load(step).wait()

        @pl.when(step + 1 < n_z)
        def _():
            load(step + 1).start()

    def make(step, slab, px, pc):
        value = outer(table[...], rows_of(step, px, pc)) * scale
        aim = in_pairs(ints, slab, px, pc, 1).astype(jnp.int32)
        hot = jnp.where(vocab_ids(extent, chunk, shard_rows) == aim, 1.0, 0.0)
        change = jnp.exp(value - in_pairs(logs, slab, px, pc, 0)) - hot
        change = (change * in_pairs(weights, slab, px, pc, 0)).astype(jnp.bfloat16)
        changes[px, pc] = change
        return (inner(change, table[...]) * scale).astype(jnp.bfloat16)

    def after(step):
        def one(index, unused):
            px, pc = index // 2, index % 2
            table_grad[...] += matmul(changes[px, pc], rows_of(step, px, pc))
            return unused

        lax.fori_loop(0, 4, one, 0)

    scatter_slabs(out, scratch, before, make, after)
    table_grad[...] = table_grad[...] * scale


def vocab_back(rows_all, table, ints, logs, weights, shard_rows, collective_id):
    own, width = rows_all.shape[4:]
    extent = table.shape[0]
    n_z, n_x, n_c, n_y = sizes()
    held = n_z <= 4
    return pl.pallas_call(
        functools.partial(vocab_back_kernel, shard_rows, held),
        out_shape=(
            jax.ShapeDtypeStruct((own, width), jnp.float32),
            jax.ShapeDtypeStruct((extent, width), jnp.float32),
        ),
        in_specs=[VMEM if held else ANY] + [VMEM] * 4,
        out_specs=(VMEM,) * 2,
        scratch_shapes=[
            pltpu.VMEM((1,) * 6 if held else (2, n_x, n_c, n_y, own, width), rows_all.dtype),
            pltpu.VMEM((n_x, n_c, extent, 2 * own), jnp.bfloat16),
            pltpu.SemaphoreType.DMA((2,)),
        ] + scatter_scratch(own, width),
        compiler_params=pltpu.CompilerParams(
            collective_id=collective_id, has_side_effects=True,
            vmem_limit_bytes=n_z * 3 * MIB + 20 * MIB if n_z <= 8 else 62 * MIB,
        ),
    )(rows_all, table, ints, logs, weights)


SQRT_HALF = 0.5**0.5
DENSITY = 0.3989422804014327


def matmul(left, right):
    return jnp.dot(left, right, preferred_element_type=jnp.float32)


def inner(left, right):
    return lax.dot_general(
        left, right, (((0,), (0,)), ((), ())), preferred_element_type=jnp.float32
    )


def outer(left, right):
    return lax.dot_general(
        left, right, (((1,), (1,)), ((), ())), preferred_element_type=jnp.float32
    )


def plane_gather(own_rows, blocks, send_sem, recv_sem):
    half = own_rows.shape[0] // 2
    (z, x, c, y), x_near, y_near, _ = around()
    low, high = pl.ds(0, half), pl.ds(half, half)

    def copy(slot, px, py, rows, source, device):
        target = blocks.at[px, py, rows]
        return remote(target if source is None else source.at[rows], target, send_sem.at[slot], recv_sem.at[slot], device)

    first = [
        copy(0, x, y, low, own_rows, x_near),
        copy(1, x, y, high, own_rows, y_near),
        copy(2, x, y, high, own_rows, x_near),
        copy(3, x, y, low, own_rows, y_near),
    ]
    relays = [copy(4, 1 - x, y, low, None, y_near), copy(5, x, 1 - y, high, None, x_near)]
    for each in first:
        each.start()

    def wait_near():
        first[0].wait_recv()
        relays[0].start()
        first[1].wait_recv()
        relays[1].start()

    def wait_x():
        first[2].wait_recv()

    def wait_y():
        first[3].wait_recv()

    def wait_diagonal():
        for each in relays:
            each.wait_recv()

    def close():
        for each in first + relays:
            each.wait_send()

    return wait_near, wait_x, wait_y, wait_diagonal, close


def plane_sum(parts, got, out, send_sem, recv_sem):
    (z, x, c, y), x_near, y_near, _ = around()
    diagonal = (z, 1 - x, c, 1 - y)
    copies = [
        remote(parts.at[device[1], device[3]], got.at[slot], send_sem.at[slot], recv_sem.at[slot], device)
        for slot, device in enumerate((x_near, y_near, diagonal))
    ]

    def close():
        for each in copies:
            each.wait_recv()
        out[...] = total_of(parts[x, y], got[0], got[1], got[2])
        for each in copies:
            each.wait_send()

    return copies, close


def order_experts(weights, ordered, sems):
    n_z, n_c, n_x, _, depth, _ = weights.shape
    copies = []
    for pz in range(n_z):
        for pc in range(n_c):
            for px in range(n_x):
                at = (pz * n_x + px) * n_c + pc
                copies.append(
                    pltpu.make_async_copy(
                        weights.at[pz, pc, px], ordered.at[:, pl.ds(at * depth, depth)], sems.at[at]
                    )
                )
    for copy in copies:
        copy.start()
    return copies


def experts_kernel(
    own_rows, route, weights, out, wide, before, hidden, ordered, parts, got, w_sem, g_send, g_recv, s_send, s_recv
):
    (z, x, c, y), x_near, y_near, _ = around()
    diagonal = (z, 1 - x, c, 1 - y)
    loads = order_experts(weights, ordered, w_sem)
    up, down = ordered.at[pl.ds(0, 2)], ordered.at[pl.ds(2, 2)]
    greet((x_near, y_near, diagonal))
    wait_near, wait_x, wait_y, wait_diagonal, close = plane_gather(own_rows, wide, g_send, g_recv)
    copies, finish = plane_sum(parts, got, out, s_send, s_recv)
    wide[x, y] = own_rows[...]

    def work(px, py):
        rows = wide[px, py]
        first = route[px, py] == 0
        value = jnp.where(first, matmul(rows, up[0]), matmul(rows, up[1]))
        before[px, py] = value
        active = 0.5 * value * (1.0 + lax.erf(value * SQRT_HALF))
        hidden_first = jnp.where(first, active, 0.0).astype(jnp.bfloat16)
        hidden_second = jnp.where(first, 0.0, active).astype(jnp.bfloat16)
        hidden[px, py] = active.astype(jnp.bfloat16)
        total = outer(hidden_first, down[0]) + outer(hidden_second, down[1])
        parts[px, py] = total.astype(jnp.bfloat16)

    for load in loads:
        load.wait()
    work(x, y)
    wait_near()
    wait_x()
    work(1 - x, y)
    copies[0].start()
    wait_y()
    work(x, 1 - y)
    copies[1].start()
    wait_diagonal()
    work(1 - x, 1 - y)
    copies[2].start()
    finish()
    close()


def experts(own_rows, route, weights, collective_id):
    _, n_x, _, n_y = sizes()
    own, width = own_rows.shape
    wide = weights.shape[5]
    dma = pltpu.SemaphoreType.DMA
    low = jnp.bfloat16
    return pl.pallas_call(
        experts_kernel,
        out_shape=(
            jax.ShapeDtypeStruct((own, width), jnp.float32),
            jax.ShapeDtypeStruct((n_x, n_y, own, width), low),
            jax.ShapeDtypeStruct((n_x, n_y, own, wide), jnp.float32),
            jax.ShapeDtypeStruct((n_x, n_y, own, wide), low),
        ),
        in_specs=[VMEM, VMEM, ANY],
        out_specs=(VMEM,) * 4,
        scratch_shapes=[
            pltpu.VMEM((4, width, wide), low),
            pltpu.VMEM((n_x, n_y, own, width), low),
            pltpu.VMEM((3, own, width), low),
            dma((width // weights.shape[4],)), dma((6,)), dma((6,)), dma((3,)), dma((3,)),
        ],
        compiler_params=pltpu.CompilerParams(
            collective_id=collective_id, has_side_effects=True, vmem_limit_bytes=20 * MIB
        ),
        cost_estimate=pl.CostEstimate(
            flops=8 * own * 4 * width * wide, bytes_accessed=8 * MIB, transcendentals=4 * own * wide
        ),
    )(own_rows, route, weights)


def experts_back_kernel(
    own_rows, route, weights, wide, before, hidden, out, grads,
    ordered, wide_grad, before_grad, parts, got, w_sem, g_send, g_recv, s_send, s_recv,
):
    (z, x, c, y), x_near, y_near, _ = around()
    diagonal = (z, 1 - x, c, 1 - y)
    loads = order_experts(weights, ordered, w_sem)
    up, down = ordered.at[pl.ds(0, 2)], ordered.at[pl.ds(2, 2)]
    greet((x_near, y_near, diagonal))
    wait_near, wait_x, wait_y, wait_diagonal, close = plane_gather(own_rows, wide_grad, g_send, g_recv)
    copies, finish = plane_sum(parts, got, out, s_send, s_recv)
    wide_grad[x, y] = own_rows[...]

    def work(px, py):
        rows = wide_grad[px, py]
        first = route[px, py] == 0
        hidden_grad = jnp.where(first, matmul(rows, down[0]), matmul(rows, down[1]))
        value = before[px, py]
        slope = 0.5 * (1.0 + lax.erf(value * SQRT_HALF)) + value * (
            DENSITY * jnp.exp(-0.5 * value * value)
        )
        change = (hidden_grad * slope).astype(jnp.bfloat16)
        before_grad[px, py] = change
        change_first = jnp.where(first, change, 0)
        change_second = jnp.where(first, 0, change)
        total = outer(change_first, up[0]) + outer(change_second, up[1])
        parts[px, py] = total.astype(jnp.bfloat16)

    for load in loads:
        load.wait()
    work(x, y)
    wait_near()
    wait_x()
    work(1 - x, y)
    copies[0].start()
    wait_y()
    work(x, 1 - y)
    copies[1].start()
    wait_diagonal()
    work(1 - x, 1 - y)
    copies[2].start()
    close()

    lane = 4 * own_rows.shape[0]
    rows = wide[...].reshape(lane, -1)
    grad_rows = wide_grad[...].reshape(lane, -1)
    first = route[...].reshape(lane, 1) == 0
    change = before_grad[...].reshape(lane, -1)
    active = hidden[...].reshape(lane, -1)
    low = jnp.bfloat16
    n_z, n_x, n_c, _ = sizes()
    depth = grads.shape[3]

    def keep(slot, value):
        value = value.astype(low)
        for pz in range(n_z):
            for px in range(n_x):
                for pc in range(n_c):
                    start = ((pz * n_x + px) * n_c + pc) * depth
                    grads[pz * n_c + pc, px, slot] = value[start : start + depth]

    keep(0, inner(rows, jnp.where(first, change, 0)))
    keep(1, inner(rows, jnp.where(first, 0, change)))
    keep(2, inner(grad_rows, jnp.where(first, active, 0)))
    keep(3, inner(grad_rows, jnp.where(first, 0, active)))
    finish()


def experts_back(own_rows, route, weights, wide, before, hidden, collective_id):
    n_z, n_x, n_c, n_y = sizes()
    own, width = own_rows.shape
    units = weights.shape[5]
    dma = pltpu.SemaphoreType.DMA
    low = jnp.bfloat16
    return pl.pallas_call(
        experts_back_kernel,
        out_shape=(
            jax.ShapeDtypeStruct((own, width), jnp.float32),
            jax.ShapeDtypeStruct((n_z * n_c, n_x, 4, width // (n_z * n_x * n_c), units), low),
        ),
        in_specs=[VMEM, VMEM, ANY] + [VMEM] * 3,
        out_specs=(VMEM,) * 2,
        scratch_shapes=[
            pltpu.VMEM((4, width, units), low),
            pltpu.VMEM((n_x, n_y, own, width), low),
            pltpu.VMEM((n_x, n_y, own, units), low),
            pltpu.VMEM((n_x, n_y, own, width), low),
            pltpu.VMEM((3, own, width), low),
            dma((width // weights.shape[4],)), dma((6,)), dma((6,)), dma((3,)), dma((3,)),
        ],
        compiler_params=pltpu.CompilerParams(
            collective_id=collective_id, has_side_effects=True, vmem_limit_bytes=28 * MIB
        ),
        cost_estimate=pl.CostEstimate(
            flops=16 * own * 4 * width * units, bytes_accessed=12 * MIB, transcendentals=8 * own * units
        ),
    )(own_rows, route, weights, wide, before, hidden)


def project_kernel(transposed, rows, weight, out, parts, got, s_send, s_recv):
    (z, x, c, y), x_near, y_near, _ = around()
    diagonal = (z, 1 - x, c, 1 - y)
    barrier = pltpu.get_barrier_semaphore()
    for device in (x_near, y_near, diagonal):
        pl.semaphore_signal(barrier, inc=1, device_id=device, device_id_type=MESH)
    copies, finish = plane_sum(parts, got, out, s_send, s_recv)

    def work(px, py):
        times = outer if transposed else matmul
        parts[px, py] = times(rows[px, py], weight[...]).astype(jnp.bfloat16)

    work(1 - x, 1 - y)
    pl.semaphore_wait(barrier, 3)
    copies[2].start()
    work(1 - x, y)
    copies[0].start()
    work(x, 1 - y)
    copies[1].start()
    work(x, y)
    finish()


def project(rows, weight, transposed, collective_id):
    n_x, n_y, own, depth = rows.shape
    width = weight.shape[0] if transposed else weight.shape[1]
    low = jnp.bfloat16
    dma = pltpu.SemaphoreType.DMA
    return pl.pallas_call(
        functools.partial(project_kernel, transposed),
        out_shape=jax.ShapeDtypeStruct((own, width), jnp.float32),
        in_specs=[VMEM] * 2,
        out_specs=VMEM,
        scratch_shapes=[
            pltpu.VMEM((n_x, n_y, own, width), low), pltpu.VMEM((3, own, width), low), dma((3,)), dma((3,)),
        ],
        compiler_params=pltpu.CompilerParams(
            collective_id=collective_id, has_side_effects=True, vmem_limit_bytes=10 * MIB
        ),
        cost_estimate=pl.CostEstimate(
            flops=8 * own * width * depth, bytes_accessed=4 * MIB, transcendentals=0
        ),
    )(rows, weight)


def gather_project_kernel(transposed, split, own_rows, weight, wide, *rest):
    (z, x, c, y), x_near, y_near, _ = around()
    outs, (g_send, g_recv) = rest[:-2], rest[-2:]
    greet((x_near, y_near))
    wait_near, wait_x, wait_y, wait_diagonal, close = plane_gather(own_rows, wide, g_send, g_recv)
    wide[x, y] = own_rows[...]

    def work(px, py):
        times = outer if transposed else matmul
        value = times(wide[px, py], weight[...]).astype(jnp.bfloat16)
        start = 0
        for out, size in zip(outs, split):
            out[px, py] = value[:, start : start + size]
            start += size

    work(x, y)
    wait_near()
    wait_x()
    work(1 - x, y)
    wait_y()
    work(x, 1 - y)
    wait_diagonal()
    work(1 - x, 1 - y)
    close()


def gather_project(own_rows, weight, transposed, split, collective_id):
    _, n_x, _, n_y = sizes()
    own, width = own_rows.shape
    depth = weight.shape[0] if transposed else weight.shape[1]
    dma = pltpu.SemaphoreType.DMA
    low = jnp.bfloat16
    return pl.pallas_call(
        functools.partial(gather_project_kernel, transposed, split),
        out_shape=(
            jax.ShapeDtypeStruct((n_x, n_y, own, width), low),
        ) + tuple(jax.ShapeDtypeStruct((n_x, n_y, own, size), low) for size in split),
        in_specs=[VMEM] * 2,
        out_specs=(VMEM,) * (1 + len(split)),
        scratch_shapes=[dma((6,)), dma((6,))],
        compiler_params=pltpu.CompilerParams(
            collective_id=collective_id, has_side_effects=True, vmem_limit_bytes=12 * MIB
        ),
        cost_estimate=pl.CostEstimate(
            flops=8 * own * width * depth, bytes_accessed=4 * MIB, transcendentals=0
        ),
    )(own_rows, weight)


def merge_logs_kernel(source, out, got, mine, send_one, recv_one, send_two, recv_two):
    n_z, n_x, n_c, n_y = sizes()
    count = n_z * n_x * n_c * n_y
    z, x, c, y = place()
    me = ((z * n_x + x) * n_c + c) * n_y + y

    def device_of(index):
        return (
            index // (n_x * n_c * n_y), index // (n_c * n_y) % n_x, index // n_y % n_c, index % n_y
        )

    barrier = pltpu.get_barrier_semaphore()

    def call(step, unused):
        other = lax.rem(me + step, count)
        pl.semaphore_signal(barrier, inc=1, device_id=device_of(other), device_id_type=MESH)
        return unused

    lax.fori_loop(1, count, call, 0)
    got[me] = source[me]
    pl.semaphore_wait(barrier, count - 1)

    def first(step):
        other = lax.rem(me + step, count)
        return remote(
            source.at[other], got.at[me], send_one.at[step], recv_one.at[step], device_of(other)
        )

    def second(step):
        other = lax.rem(me + step, count)
        return remote(mine, out.at[me], send_two.at[step], recv_two.at[step], device_of(other))

    def each(action):
        def body(step, unused):
            action(step)
            return unused

        lax.fori_loop(1, count, body, 0)

    each(lambda step: first(step).start())
    each(lambda step: first(step).wait())
    values = got[...]
    peak = jnp.max(values, axis=0)
    mine[...] = peak + jnp.log(jnp.sum(jnp.exp(values - peak[None]), axis=0))
    out[me] = mine[...]
    each(lambda step: second(step).start())
    each(lambda step: second(step).wait())


def merge_logs(blocks, collective_id):
    count = blocks.shape[0]
    dma = pltpu.SemaphoreType.DMA
    return pl.pallas_call(
        merge_logs_kernel,
        out_shape=jax.ShapeDtypeStruct(blocks.shape, blocks.dtype),
        in_specs=[VMEM],
        out_specs=VMEM,
        scratch_shapes=[
            pltpu.VMEM(blocks.shape, blocks.dtype), pltpu.VMEM(blocks.shape[1:], blocks.dtype),
            dma((count,)), dma((count,)), dma((count,)), dma((count,)),
        ],
        compiler_params=pltpu.CompilerParams(collective_id=collective_id, has_side_effects=True),
    )(blocks)


def key_position(index, part, chunk):
    lane = 2 * chunk
    start = (part // 2) * (2 * lane) + (part % 2) * chunk
    return start + index + jnp.where(index >= chunk, chunk, 0)


def near_shown(side, chunk, query_pos, query_seg, near_pos, near_seg):
    columns = slice(side * chunk, (side + 1) * chunk)
    rows = slice(2 * side * chunk, 2 * (side + 1) * chunk)
    shown = (
        (near_seg[rows, :] == query_seg[:, columns])
        & (near_pos[rows, :] <= query_pos[:, columns])
        & (near_pos[rows, :] >= PROMPT)
    )
    return columns, rows, shown


def attend_kernel(
    chunk, query, far, near, query_pos, query_seg, near_pos, near_seg,
    out, out_low, log_total, scores, far_t, near_t,
):
    lane, feature = query.shape
    group = feature // HEAD_DIM
    prompt_rows = far.shape[0]
    parts = prompt_rows // lane
    query_t = (query[...].astype(jnp.float32) * HEAD_DIM ** (-0.5)).T.astype(jnp.bfloat16)
    far_t[...] = far[...].astype(jnp.float32).T.astype(jnp.bfloat16)
    near_t[...] = near[...].astype(jnp.float32).T.astype(jnp.bfloat16)
    row_of = lax.broadcasted_iota(jnp.int32, (feature, lane), 0)
    q_pos = query_pos[...]

    for head in range(group):
        low, high = head * HEAD_DIM, (head + 1) * HEAD_DIM
        query_h = jnp.where((row_of >= low) & (row_of < high), query_t, 0)

        def score_part(part, peak):
            block = far[pl.ds(pl.multiple_of(part * lane, lane), lane), :feature]
            value = matmul(block, query_h)
            index = lax.broadcasted_iota(jnp.int32, (lane, lane), 0)
            value = jnp.where(key_position(index, part, chunk) <= q_pos, value, MASKED)
            scores[pl.ds(pl.multiple_of(part * lane, lane), lane), :] = value
            return jnp.maximum(peak, jnp.max(value, axis=0, keepdims=True))

        peak = lax.fori_loop(0, parts, score_part, jnp.full((1, lane), MASKED, jnp.float32))
        near_peaks = []
        for side in range(2):
            columns, rows, shown = near_shown(side, chunk, query_pos, query_seg, near_pos, near_seg)
            value = matmul(near[rows, :feature], query_h[:, columns])
            value = jnp.where(shown, value, MASKED)
            scores[prompt_rows : prompt_rows + lane, columns] = value
            near_peaks.append(jnp.max(value, axis=0, keepdims=True))
        peak = jnp.maximum(peak, jnp.concatenate(near_peaks, axis=1))

        def weigh_part(part, state):
            total, mixed = state
            start = pl.multiple_of(part * lane, lane)
            chance = jnp.exp(scores[pl.ds(start, lane), :] - peak)
            total = total + jnp.sum(chance, axis=0, keepdims=True)
            mixed = mixed + matmul(
                far_t[feature + low : feature + high, pl.ds(start, lane)],
                chance.astype(jnp.bfloat16),
            )
            return total, mixed

        total, mixed = lax.fori_loop(
            0,
            parts,
            weigh_part,
            (jnp.zeros((1, lane), jnp.float32), jnp.zeros((HEAD_DIM, lane), jnp.float32)),
        )
        near_total, near_mixed = [], []
        for side in range(2):
            columns = slice(side * chunk, (side + 1) * chunk)
            rows = slice(side * lane, (side + 1) * lane)
            chance = jnp.exp(scores[prompt_rows : prompt_rows + lane, columns] - peak[:, columns])
            near_total.append(jnp.sum(chance, axis=0, keepdims=True))
            near_mixed.append(
                matmul(near_t[feature + low : feature + high, rows], chance.astype(jnp.bfloat16))
            )
        total = total + jnp.concatenate(near_total, axis=1)
        mixed = mixed + jnp.concatenate(near_mixed, axis=1)
        out[low:high, :] = mixed / total
        log_total[head : head + 1, :] = peak + jnp.log(total)
    out_low[...] = out[...].T.astype(jnp.bfloat16)


def attend(queries, far, near, places, chunk):
    lane, feature = queries.shape
    prompt_rows = far.shape[0]
    group = feature // HEAD_DIM
    total_rows = prompt_rows + lane
    return pl.pallas_call(
        functools.partial(attend_kernel, chunk),
        out_shape=(
            jax.ShapeDtypeStruct((feature, lane), jnp.float32),
            jax.ShapeDtypeStruct((lane, feature), jnp.bfloat16),
            jax.ShapeDtypeStruct((group, lane), jnp.float32),
        ),
        in_specs=[VMEM] * 7,
        out_specs=(VMEM,) * 3,
        scratch_shapes=[
            pltpu.VMEM((total_rows, lane), jnp.float32),
            pltpu.VMEM((2 * feature, prompt_rows), jnp.bfloat16),
            pltpu.VMEM((2 * feature, 2 * lane), jnp.bfloat16),
        ],
        compiler_params=pltpu.CompilerParams(vmem_limit_bytes=20 * MIB),
        cost_estimate=pl.CostEstimate(
            flops=8 * group * lane * total_rows * 128,
            bytes_accessed=8 * MIB,
            transcendentals=group * lane * total_rows,
        ),
    )(queries, far, near, *places)


def attend_back_kernel(
    chunk, query, far, near, query_pos, query_seg, near_pos, near_seg,
    log_total, mixed, answer, query_grad, far_grad, near_grad,
    far_t, near_t, far_values, near_values, far_sum, near_sum, query_sum,
):
    lane, feature = query.shape
    group = feature // HEAD_DIM
    prompt_rows = far.shape[0]
    parts = prompt_rows // lane
    scaled = (query[...].astype(jnp.float32) * HEAD_DIM ** (-0.5)).astype(jnp.bfloat16)
    query_t = scaled.astype(jnp.float32).T.astype(jnp.bfloat16)
    answers = answer[...]
    answer_t = answers.astype(jnp.float32).T.astype(jnp.bfloat16)
    far_t[...] = far[:, :feature].astype(jnp.float32).T.astype(jnp.bfloat16)
    near_t[...] = near[:, :feature].astype(jnp.float32).T.astype(jnp.bfloat16)
    far_values[...] = far[:, feature:]
    near_values[...] = near[:, feature:]
    row_of = lax.broadcasted_iota(jnp.int32, (feature, lane), 0)
    column_of = lax.broadcasted_iota(jnp.int32, (lane, feature), 1)
    q_pos = query_pos[...]

    for head in range(group):
        low, high = head * HEAD_DIM, (head + 1) * HEAD_DIM
        in_rows = (row_of >= low) & (row_of < high)
        in_columns = (column_of >= low) & (column_of < high)
        query_ht = jnp.where(in_rows, query_t, 0)
        answer_ht = jnp.where(in_rows, answer_t, 0)
        query_h = jnp.where(in_columns, scaled, 0)
        answer_h = jnp.where(in_columns, answers, 0)
        log_h = log_total[head : head + 1, :]
        delta_h = jnp.sum(
            answer_t[low:high, :].astype(jnp.float32) * mixed[low:high, :], axis=0, keepdims=True
        )

        def slopes(key_block, value_block, shown, columns):
            value = matmul(key_block, query_ht[:, columns])
            chance = jnp.exp(jnp.where(shown, value - log_h[:, columns], MASKED))
            slope = matmul(value_block, answer_ht[:, columns])
            change = (chance * (slope - delta_h[:, columns])).astype(jnp.bfloat16)
            chance = chance.astype(jnp.bfloat16)
            return change, matmul(change, query_h[columns]), matmul(chance, answer_h[columns])

        def add(sums, rows, key_part, value_part):
            if head == 0:
                sums[0, rows, :] = key_part
                sums[1, rows, :] = value_part
            else:
                sums[0, rows, :] += key_part
                sums[1, rows, :] += value_part

        def back_part(part, total):
            rows = pl.ds(pl.multiple_of(part * lane, lane), lane)
            index = lax.broadcasted_iota(jnp.int32, (lane, lane), 0)
            shown = key_position(index, part, chunk) <= q_pos
            change, key_part, value_part = slopes(
                far[rows, :feature], far_values[rows, :], shown, slice(0, lane)
            )
            add(far_sum, rows, key_part, value_part)
            return total + matmul(far_t[low:high, rows], change)

        total = lax.fori_loop(0, parts, back_part, jnp.zeros((HEAD_DIM, lane), jnp.float32))
        near_total = []
        for side in range(2):
            columns, rows, shown = near_shown(side, chunk, query_pos, query_seg, near_pos, near_seg)
            change, key_part, value_part = slopes(
                near[rows, :feature], near_values[rows, :], shown, columns
            )
            add(near_sum, rows, key_part, value_part)
            near_total.append(matmul(near_t[low:high, rows], change))
        query_sum[low:high, :] = (total + jnp.concatenate(near_total, axis=1)) * HEAD_DIM ** (-0.5)
    query_grad[...] = query_sum[...].T.astype(jnp.bfloat16)
    for sums, grad in ((far_sum, far_grad), (near_sum, near_grad)):
        grad[...] = jnp.concatenate(
            [sums[0].astype(jnp.bfloat16), sums[1].astype(jnp.bfloat16)], axis=1
        )


def attend_back(queries, far, near, places, log_total, mixed, answer, chunk):
    lane, feature = queries.shape
    prompt_rows = far.shape[0]
    group = feature // HEAD_DIM
    total_rows = prompt_rows + lane
    low = jnp.bfloat16
    return pl.pallas_call(
        functools.partial(attend_back_kernel, chunk),
        out_shape=(
            jax.ShapeDtypeStruct((lane, feature), low),
            jax.ShapeDtypeStruct((prompt_rows, 2 * feature), low),
            jax.ShapeDtypeStruct((2 * lane, 2 * feature), low),
        ),
        in_specs=[VMEM] * 10,
        out_specs=(VMEM,) * 3,
        scratch_shapes=[
            pltpu.VMEM((feature, prompt_rows), low),
            pltpu.VMEM((feature, 2 * lane), low),
            pltpu.VMEM((prompt_rows, feature), low),
            pltpu.VMEM((2 * lane, feature), low),
            pltpu.VMEM((2, prompt_rows, feature), jnp.float32),
            pltpu.VMEM((2, 2 * lane, feature), jnp.float32),
            pltpu.VMEM((feature, lane), jnp.float32),
        ],
        compiler_params=pltpu.CompilerParams(vmem_limit_bytes=28 * MIB),
        cost_estimate=pl.CostEstimate(
            flops=20 * group * lane * total_rows * 128,
            bytes_accessed=12 * MIB,
            transcendentals=group * lane * total_rows,
        ),
    )(queries, far, near, *places, log_total, mixed, answer)


def head_places(back):
    n_z, n_x, n_c, n_y = sizes()
    line = n_z * n_c
    pairs = []
    for device in range(line * n_x * n_y):
        group, at = device // line, device % line
        place_of = ((at // n_c * n_x + group // n_y) * n_c + at % n_c) * n_y + group % n_y
        pairs.append((place_of, device) if back else (device, place_of))
    return tuple(pairs)


def pad_rows(block):
    return jnp.pad(block, ((0, 8 - block.shape[0]), (0, 0)))


def adam_update(weight, moment_one, moment_two, gradient, step_rate, decay_rate):
    first_new = BETA_ONE * moment_one + (1.0 - BETA_ONE) * gradient
    second_new = BETA_TWO * moment_two + (1.0 - BETA_TWO) * gradient * gradient
    normalized = (
        first_new
        / (1.0 - BETA_ONE**STEP)
        / (jnp.sqrt(second_new / (1.0 - BETA_TWO**STEP)) + ADAM_EPS)
    )
    return (weight - step_rate * (normalized + decay_rate * weight), first_new, second_new)


def per_device(
    token_ids,
    targets,
    valid_mask,
    cont_lengths,
    routes,
    vocab_table,
    vocab_first,
    vocab_second,
    attn_weights,
    attn_first,
    attn_second,
    router,
    router_first,
    router_second,
    norm_gains,
    gains_first,
    gains_second,
    expert_up,
    up_first,
    up_second,
    expert_down,
    down_first,
    down_second,
):
    slabs = lax.axis_size("z")
    planes = lax.axis_size("x")
    cores = lax.axis_size("core")
    sides = lax.axis_size("head")
    groups = planes * sides
    z_at, x_at, core_at, side_at = (lax.axis_index(name) for name in ALL)
    blk_at = (z_at * planes + x_at) * cores + core_at
    device_at = blk_at * sides + side_at
    group_at = x_at * sides + side_at
    tokens = valid_mask.shape[0]
    chunk = token_ids.shape[0]
    own = chunk // sides
    lane = planes * chunk
    feature = D // groups
    wide = expert_up.shape[3] // planes
    shard_rows = vocab_table.shape[0]
    logit_scale = D ** (-0.5)

    cont_ends = jnp.cumsum(cont_lengths)
    valid_f = valid_mask.astype(jnp.float32)
    token_count = jnp.sum(valid_mask).astype(jnp.float32)
    expert_ids = jnp.arange(EXPERTS, dtype=jnp.int32)

    own_ints = jnp.concatenate([token_ids[None], targets[None], routes], axis=0)
    own_ints = lax.dynamic_slice_in_dim(own_ints, side_at * own, own, axis=1).astype(jnp.float32)
    rows_of = attn_weights.shape[1]
    smalls = jnp.concatenate(
        [router.transpose(0, 2, 1).reshape(LAYERS * EXPERTS, rows_of), norm_gains], axis=0
    )
    smalls = smalls.astype(jnp.bfloat16).astype(jnp.float32)
    smalls = jnp.pad(smalls, ((0, 16 - smalls.shape[0]), (0, own - rows_of)))
    whole_f = swap(jnp.concatenate([pad_rows(own_ints), smalls], axis=0)[None], True, 1)
    attn_low = attn_weights.astype(jnp.bfloat16)
    qkv_send = attn_low[:, :, : 3 * D].reshape(LAYERS, rows_of, 3, groups, feature)
    qkv_send = jnp.concatenate([qkv_send[:, :, 1:], qkv_send[:, :, :1]], axis=2)
    qkv_send = qkv_send.transpose(3, 0, 1, 2, 4).reshape(groups, LAYERS, rows_of, 3 * feature)
    qkv_got = lax.all_to_all(qkv_send, PLANE, split_axis=0, concat_axis=0, tiled=True)
    out_rows = lax.ppermute(attn_low[:, :, 3 * D :], ALL, head_places(False))
    expert_send = jnp.stack([expert_up, expert_down], axis=1).astype(jnp.bfloat16)
    depth = expert_send.shape[3]
    expert_send = expert_send.reshape(LAYERS, 2 * EXPERTS, depth, planes, wide)
    expert_send = expert_send.transpose(3, 0, 1, 2, 4)
    expert_halves = []
    for layer_index in range(LAYERS):
        kept_half = lax.dynamic_index_in_dim(expert_send[:, layer_index], x_at, 0, False)
        sent_half = lax.dynamic_index_in_dim(expert_send[:, layer_index], 1 - x_at, 0, False)
        got_half = lax.ppermute(sent_half, "x", ((0, 1), (1, 0)))
        expert_halves.append((kept_half, got_half))
    whole_f, qkv_got, out_rows, expert_halves = lax.optimization_barrier(
        (whole_f, qkv_got, out_rows, expert_halves)
    )
    qkv_own = qkv_got.reshape(planes, sides, LAYERS, rows_of, 3 * feature).transpose(2, 0, 1, 3, 4)
    qkv_own = qkv_own.reshape(LAYERS, planes, sides * rows_of, 3 * feature)
    expert_packs = []
    for kept_half, got_half in expert_halves:
        expert_packs.append(
            jnp.stack(
                [
                    jnp.where(x_at == 0, kept_half, got_half),
                    jnp.where(x_at == 0, got_half, kept_half),
                ]
            )
        )
    whole_f, expert_packs = lax.optimization_barrier((whole_f, expert_packs))

    def gather_experts(halves):
        block = lax.all_gather(halves, LINE, axis=0)
        block = block.reshape(slabs, cores, planes, 2 * EXPERTS, depth, wide)
        if depth % 16 == 0:
            return block
        block = block.transpose(3, 0, 2, 1, 4, 5).reshape(2 * EXPERTS, D, wide)
        return block[None, None, None]

    expert_weights = [gather_experts(expert_packs[0])]
    ints = whole_f.reshape(sizes() + whole_f.shape[1:])
    whole = whole_f[:, : 2 + LAYERS].astype(jnp.int32)
    smalls = whole_f[:, 8:, :rows_of].transpose(1, 0, 2).reshape(16, D)
    router_all = smalls[: LAYERS * EXPERTS].reshape(LAYERS, EXPERTS, D).transpose(0, 2, 1)
    router_all = router_all.astype(jnp.bfloat16)
    gains_f = smalls[LAYERS * EXPERTS :]
    routes_lane = lax.dynamic_index_in_dim(
        whole.reshape(slabs, planes, cores, sides, 2 + LAYERS, own), z_at, 0, False
    )
    routes_lane = lax.dynamic_index_in_dim(routes_lane, core_at, 1, False)[:, :, 2:]
    routes_lane = routes_lane.transpose(2, 0, 1, 3)[..., None]
    routes_own = lax.dynamic_slice_in_dim(routes, side_at * own, own, axis=1)

    extent = -(-shard_rows // 256) * 256
    table = jnp.pad(vocab_table.astype(jnp.bfloat16), ((0, extent - shard_rows), (0, 0)))
    offsets = jnp.arange(chunk, dtype=jnp.int32)
    first_blk = z_at * planes * cores + core_at
    query_pos = jnp.concatenate([(first_blk + cores * part) * chunk + offsets for part in range(planes)])
    near_blks = [first_blk - 1 + part for part in range(2 * planes)]
    near_pos = jnp.concatenate([blk * chunk + offsets for blk in near_blks])
    query_seg = segment_of(query_pos, cont_ends)
    near_seg = segment_of(near_pos, cont_ends)
    places = (query_pos[None, :], query_seg[None, :], near_pos[:, None], near_seg[:, None])

    stream, qkv_all, out_all = embed(table, ints, qkv_own, out_rows, own, shard_rows, 2)
    qkv_weights = [qkv_all[layer_index].reshape(D, 3 * feature) for layer_index in range(LAYERS)]
    out_weights = [out_all[layer_index].reshape(feature, D) for layer_index in range(LAYERS)]

    kept = []
    for layer_index in range(LAYERS):
        normed_lane, key_values, queries = gather_project(
            rms_norm(stream, gains_f[2 * layer_index]).astype(jnp.bfloat16),
            qkv_weights[layer_index], False, (2 * feature, feature), 3,
        )
        queries = queries.reshape(lane, feature)
        far, near = spread_keys(key_values.reshape(lane, 2 * feature), PROMPT, 10)
        if layer_index + 1 < LAYERS:
            far, halves = lax.optimization_barrier((far, expert_packs[layer_index + 1]))
            expert_weights.append(gather_experts(halves))
        mixed_t, mixed_low, log_total = attend(queries, far, near, places, chunk)
        middle = stream + project(
            mixed_low.reshape(planes, sides, own, feature), out_weights[layer_index], False, 15
        )
        normed_two = rms_norm(middle, gains_f[2 * layer_index + 1]).astype(jnp.bfloat16)
        chance = jax.nn.softmax(matmul(normed_two, router_all[layer_index]), axis=-1)
        output, wide_rows, before, hidden = experts(
            normed_two, routes_lane[layer_index], expert_weights[layer_index], 11
        )
        own_pick = (routes_own[layer_index][:, None] == expert_ids[None, :]).astype(jnp.float32)
        gate = jnp.sum(chance * own_pick, axis=1, keepdims=True)
        kept.append(
            (
                stream, normed_lane, queries, far, near, mixed_t, mixed_low, log_total, middle,
                normed_two, chance, wide_rows, before, hidden, output, own_pick, gate,
            )
        )
        stream = middle + gate * output

    final_gain = gains_f[2 * LAYERS]
    devices = tokens // own
    valid_rows = valid_f.reshape(sizes() + (1, own))
    final_all, row_logs, hits = gather_logits(
        rms_norm(stream, final_gain).astype(jnp.bfloat16), table, ints, valid_rows, shard_rows, 4
    )
    log_sums = merge_logs(row_logs.reshape(devices, 1, own), 5)
    log_sum = log_sums.reshape(tokens)
    own_log = lax.dynamic_slice_in_dim(log_sum, device_at * own, own)
    own_valid = lax.dynamic_slice_in_dim(valid_f, device_at * own, own)
    own_loss = jnp.sum(own_log * own_valid) - jnp.sum(hits)
    final_grad, table_grad = vocab_back(
        final_all, table, ints, log_sums.reshape(sizes() + (1, own)), valid_rows / token_count,
        shard_rows, 6,
    )
    stream_grad, final_gain_grad = jax.vjp(rms_norm, stream, final_gain)[1](final_grad)

    attn_packs = [None] * LAYERS
    router_list = [None] * LAYERS
    expert_sums = [None] * LAYERS
    gain_list = [None] * (2 * LAYERS + 1)
    gain_list[2 * LAYERS] = final_gain_grad
    for layer_index in reversed(range(LAYERS)):
        (
            stream, normed_lane, queries, far, near, mixed_t, mixed_low, log_total, middle,
            normed_two, chance, wide_rows, before, hidden, output, own_pick, gate,
        ) = kept[layer_index]
        out_grad = (gate * stream_grad).astype(jnp.bfloat16)
        chance_grad = jnp.sum(stream_grad * output, axis=1)[:, None] * own_pick
        choice_grad = chance * (chance_grad - jnp.sum(chance * chance_grad, axis=1, keepdims=True))
        router_list[layer_index] = jnp.dot(
            normed_two.astype(jnp.float32).T, choice_grad, precision=lax.Precision.HIGHEST
        )
        normed_grad = jnp.dot(
            choice_grad,
            router_all[layer_index].astype(jnp.float32).T,
            precision=lax.Precision.HIGHEST,
        )
        rows_grad, expert_grad = experts_back(
            out_grad, routes_lane[layer_index], expert_weights[layer_index], wide_rows, before,
            hidden, 12,
        )
        normed_grad = normed_grad + rows_grad
        middle_part, gain_list[2 * layer_index + 1] = jax.vjp(
            rms_norm, middle, gains_f[2 * layer_index + 1]
        )[1](normed_grad)
        middle_grad = stream_grad + middle_part
        branch_lane, answer = gather_project(
            middle_grad.astype(jnp.bfloat16), out_weights[layer_index], True, (feature,), 16
        )
        answer = answer.reshape(lane, feature)
        out_proj = inner(mixed_low, branch_lane.reshape(lane, D)).astype(jnp.bfloat16)
        query_grad, far_grad, near_grad = attend_back(
            queries, far, near, places, log_total, mixed_t, answer, chunk
        )
        qkv_grad = collect_keys(far_grad, near_grad, query_grad, 13)
        qkv_grad, expert_grad = lax.optimization_barrier((qkv_grad, expert_grad))
        expert_sums[layer_index] = lax.psum_scatter(
            expert_grad, LINE, scatter_dimension=0, tiled=True
        )[0]
        qkv_proj = inner(normed_lane.reshape(lane, D), qkv_grad).astype(jnp.bfloat16)
        qkv_proj = qkv_proj.reshape(slabs, planes, cores, sides, rows_of, 3 * feature)
        qkv_proj = qkv_proj.transpose(0, 2, 1, 3, 4, 5).reshape(
            slabs * cores, groups, rows_of, 3 * feature
        )
        out_proj = out_proj.reshape(slabs * cores, rows_of, groups, feature).transpose(0, 2, 1, 3)
        attn_packs[layer_index] = jnp.concatenate([qkv_proj, out_proj], axis=3)
        normed_att_grad = project(
            qkv_grad.reshape(planes, sides, own, 3 * feature), qkv_weights[layer_index], True, 14
        )
        stream_part, gain_list[2 * layer_index] = jax.vjp(
            rms_norm, stream, gains_f[2 * layer_index]
        )[1](normed_att_grad)
        stream_grad = middle_grad + stream_part

    small = jnp.concatenate(
        [jnp.stack(router_list).transpose(1, 0, 2).reshape(D, -1), jnp.stack(gain_list).T], axis=1
    )
    small = small.reshape(devices, rows_of, -1).transpose(0, 2, 1)
    small = jnp.pad(small, ((0, 0), (0, 16 - small.shape[1]), (0, 128 - rows_of)))
    attn_pack = jnp.stack(attn_packs, axis=2).reshape(slabs, cores, -1, D).transpose(1, 0, 2, 3)
    table_share, small, attn_pack = embed_back(
        stream_grad.astype(jnp.bfloat16), ints, table_grad, small, attn_pack, shard_rows, 7
    )
    squares = sum(
        jnp.sum(jnp.square(part.astype(jnp.float32)))
        for part in [table_share[:shard_rows], small[:, :rows_of], attn_pack] + expert_sums
    )
    sums = jnp.pad(jnp.stack([squares, own_loss])[:, None], ((0, 6), (0, 127)))
    sums = jnp.sum(swap(sums[None], True, 9)[:, :2, 0], axis=0)
    square_total, loss_sum = sums[0], sums[1]
    expert_shares = []
    for expert_grad in expert_sums:
        kept_half = lax.dynamic_index_in_dim(expert_grad, x_at, 0, False)
        sent_half = lax.dynamic_index_in_dim(expert_grad, 1 - x_at, 0, False)
        got_half = lax.ppermute(sent_half, "x", ((0, 1), (1, 0)))
        expert_grad = jnp.concatenate(
            [jnp.where(x_at == 0, kept_half, got_half), jnp.where(x_at == 0, got_half, kept_half)],
            axis=-1,
        )
        expert_shares.append(
            expert_grad.reshape(2, EXPERTS, depth, planes * wide).astype(jnp.float32)
        )
    attn_pack = attn_pack.reshape(groups, LAYERS, rows_of, D)
    table_share, small = table_share[:shard_rows], small[:, :rows_of]
    router_share = (
        small[: LAYERS * EXPERTS].reshape(LAYERS, EXPERTS, rows_of).transpose(0, 2, 1)
    )
    gain_share = small[LAYERS * EXPERTS : LAYERS * EXPERTS + 2 * LAYERS + 1]
    qkv_share = lax.all_to_all(
        attn_pack[..., : 3 * feature], PLANE, split_axis=0, concat_axis=0, tiled=True
    )
    qkv_share = qkv_share.reshape(groups, LAYERS, rows_of, 3, feature)
    qkv_share = jnp.concatenate([qkv_share[:, :, :, 2:], qkv_share[:, :, :, :2]], axis=3)
    qkv_share = qkv_share.transpose(1, 2, 3, 0, 4).reshape(LAYERS, rows_of, 3 * D)
    out_share = attn_pack[..., 3 * feature :].transpose(1, 2, 0, 3).reshape(LAYERS, rows_of, D)
    out_share = lax.ppermute(out_share, ALL, head_places(True))
    attn_share = jnp.concatenate([qkv_share, out_share], axis=2).astype(jnp.float32)
    up_share = jnp.stack([share[0] for share in expert_shares])
    down_share = jnp.stack([share[1] for share in expert_shares])
    shares = (table_share, attn_share, router_share, gain_share, up_share, down_share)
    grad_norm = jnp.sqrt(square_total)
    factor = CLIP_AT / jnp.maximum(grad_norm, CLIP_AT)
    weights = (vocab_table, attn_weights, router, norm_gains, expert_up, expert_down)
    firsts = (vocab_first, attn_first, router_first, gains_first, up_first, down_first)
    seconds = (vocab_second, attn_second, router_second, gains_second, up_second, down_second)
    results = [loss_sum, token_count, grad_norm]
    for number in range(6):
        results.extend(
            adam_update(
                weights[number],
                firsts[number],
                seconds[number],
                factor * shares[number],
                STEP_RATES[number],
                DECAY_RATES[number],
            )
        )
    return tuple(results)


def solution(mesh):
    blocks, sides = mesh.shape["blk"], mesh.shape["head"]
    fine = Mesh(mesh.devices.reshape(blocks // 4, 2, 2, sides), ALL)
    weight_specs = (
        (P(ALL, None),) * 3
        + (P(None, ALL, None),) * 3
        + (P(None, ALL, None),) * 3
        + (P(None, ALL),) * 3
        + (P(None, None, BLK, "head"),) * 6
    )
    return jax.shard_map(
        per_device,
        mesh=fine,
        in_specs=(P(BLK), P(BLK), P(), P(), P(None, BLK)) + weight_specs,
        out_specs=(P(), P(), P()) + weight_specs,
        check_vma=False,
    )
```

```python
import functools

import jax
import jax.numpy as jnp
from jax import lax
from jax.experimental import pallas as pl
from jax.experimental.pallas import tpu as pltpu
from jax.sharding import Mesh, PartitionSpec as P

D = 768
HEADS = 12
HEAD_DIM = 64
EXPERTS = 2
LAYERS = 2
PROMPT = 2048
STEP = 10

NORM_EPS = 1e-06
BETA_ONE = 0.9
BETA_TWO = 0.95
ADAM_EPS = 1e-08
CLIP_AT = 0.01
MASKED = -1e30
STEP_RATES = (2.0, 0.25, 0.04, 0.4, 0.04, 0.04)
DECAY_RATES = (0.01, 0.01, 0.01, 0.0, 0.01, 0.01)

ALL = ("z", "x", "core", "head")
BLK = ("z", "x", "core")
PLANE = ("x", "head")
LINE = ("z", "core")
MIB = 2**20
MESH = pl.DeviceIdType.MESH
ANY = pl.BlockSpec(memory_space=pl.ANY)
VMEM = pl.BlockSpec(memory_space=pltpu.VMEM)


def rms_norm(stream, gain):
    return stream * lax.rsqrt(jnp.mean(stream * stream, axis=-1, keepdims=True) + NORM_EPS) * gain


def segment_of(position, cont_ends):
    later = jnp.sum((cont_ends[None, :] <= (position - PROMPT)[:, None]).astype(jnp.int32), axis=1)
    return jnp.where(position < PROMPT, 0, 1 + later)


def place():
    return tuple(lax.axis_index(name) for name in ALL)


def sizes():
    return tuple(lax.axis_size(name) for name in ALL)


def remote(source, target, send, receive, device):
    return pltpu.make_async_remote_copy(
        src_ref=source, dst_ref=target, send_sem=send, recv_sem=receive,
        device_id=device, device_id_type=MESH,
    )


def greet(devices):
    barrier = pltpu.get_barrier_semaphore()
    for device in devices:
        pl.semaphore_signal(barrier, inc=1, device_id=device, device_id_type=MESH)
    pl.semaphore_wait(barrier, len(devices))


def around():
    z, x, c, y = place()
    return (z, x, c, y), (z, 1 - x, c, y), (z, x, c, 1 - y), (z, x, 1 - c, y)


def swap_kernel(broadcast, source, out, send_sem, receive_sem, own_sem):
    n_z, n_x, n_c, n_y = sizes()
    count = n_z * n_x * n_c * n_y
    z, x, c, y = place()
    me = ((z * n_x + x) * n_c + c) * n_y + y

    def device_of(index):
        return (
            index // (n_x * n_c * n_y), index // (n_c * n_y) % n_x, index // n_y % n_c, index % n_y
        )

    def taken(index):
        return source.at[0] if broadcast else source.at[index]

    barrier = pltpu.get_barrier_semaphore()

    def call(step, unused):
        other = lax.rem(me + step, count)
        pl.semaphore_signal(barrier, inc=1, device_id=device_of(other), device_id_type=MESH)
        return unused

    lax.fori_loop(1, count, call, 0)
    own = pltpu.make_async_copy(taken(me), out.at[me], own_sem)
    own.start()
    pl.semaphore_wait(barrier, count - 1)

    def copy(step):
        other = lax.rem(me + step, count)
        return remote(
            taken(other), out.at[me], send_sem.at[step], receive_sem.at[step], device_of(other)
        )

    def start(step, unused):
        copy(step).start()
        return unused

    def finish(step, unused):
        copy(step).wait()
        return unused

    lax.fori_loop(1, count, start, 0)
    lax.fori_loop(1, count, finish, 0)
    own.wait()


def swap(blocks, broadcast, collective_id):
    count = 1
    for size in sizes():
        count *= size
    return pl.pallas_call(
        functools.partial(swap_kernel, broadcast),
        out_shape=jax.ShapeDtypeStruct((count,) + blocks.shape[1:], blocks.dtype),
        in_specs=[VMEM],
        out_specs=VMEM,
        scratch_shapes=[
            pltpu.SemaphoreType.DMA((count,)),
            pltpu.SemaphoreType.DMA((count,)),
            pltpu.SemaphoreType.DMA,
        ],
        cost_estimate=pl.CostEstimate(
            flops=0, bytes_accessed=36 * MIB, transcendentals=0
        ),
        compiler_params=pltpu.CompilerParams(collective_id=collective_id, has_side_effects=True),
    )(blocks)


def total_of(*parts):
    total = parts[0].astype(jnp.float32)
    for part in parts[1:]:
        total = total + part.astype(jnp.float32)
    return total


PIECES = 4


def spread_kernel(
    prompt_slabs, own_rows, far, near, tail, z_send, z_recv, c_send, c_recv, n_send, n_recv, own_sem
):
    n_z = lax.axis_size("z")
    lane = own_rows.shape[0]
    chunk = lane // 2
    size = lane // PIECES
    (z, x, c, y), _, _, c_near = around()
    above, below = (z + 1, x, c, y), (z - 1, x, c, y)
    in_prompt = z < prompt_slabs
    takes_down = z < prompt_slabs - 1
    gives_down = (z > 0) & (z < prompt_slabs)

    barrier = pltpu.get_barrier_semaphore()
    pl.semaphore_signal(barrier, inc=1, device_id=c_near, device_id_type=MESH)

    @pl.when(z > 0)
    def _():
        pl.semaphore_signal(barrier, inc=1, device_id=below, device_id_type=MESH)

    @pl.when(takes_down)
    def _():
        pl.semaphore_signal(barrier, inc=1, device_id=above, device_id_type=MESH)

    first, second = pl.ds(0, chunk), pl.ds(chunk, chunk)
    own = [
        pltpu.make_async_copy(own_rows.at[first], near.at[1], own_sem.at[0]),
        pltpu.make_async_copy(own_rows.at[second], near.at[3], own_sem.at[1]),
    ]
    own_far = pltpu.make_async_copy(own_rows, far.at[jnp.minimum(z, prompt_slabs - 1), c], own_sem.at[2])
    own_edge = pltpu.make_async_copy(own_rows.at[first], near.at[0], own_sem.at[3])
    edge = (z == 0) & (c == 0)
    for copy in own:
        copy.start()

    @pl.when(in_prompt)
    def _():
        own_far.start()

    @pl.when(edge)
    def _():
        own_edge.start()

    pl.semaphore_wait(
        barrier, 1 + jnp.where(z < n_z - 1, 1, 0) + jnp.where(gives_down, 1, 0)
    )

    def part(index):
        return pl.ds(index * size, size)

    def z_copy(source, slab, index, up):
        return remote(
            source, far.at[slab, c, part(index)], z_send.at[slab, index, 1 if up else 0],
            z_recv.at[slab, index], above if up else below,
        )

    def c_copy(source, slab, index):
        return remote(
            source, far.at[slab, c, part(index)], c_send.at[slab, index], c_recv.at[slab, index], c_near
        )

    def t_copy():
        return remote(own_rows.at[second], tail, n_send.at[0], n_recv.at[0], above)

    def t_hand():
        return remote(tail, near.at[0], n_send.at[1], n_recv.at[1], c_near)

    def n_copy(half):
        slot = jnp.where(c == 0, 2 * half, 2)
        return remote(
            own_rows.at[pl.ds(half * chunk, chunk)], near.at[slot], n_send.at[2 + half], n_recv.at[2 + half],
            c_near,
        )

    @pl.when(in_prompt)
    def _():
        for index in range(PIECES):
            source = own_rows.at[part(index)]

            @pl.when(z < n_z - 1)
            def _():
                z_copy(source, z, index, True).start()

            @pl.when(z > 0)
            def _():
                z_copy(source, z, index, False).start()

            c_copy(source, z, index).start()

    @pl.when((c == 1) & (z < n_z - 1))
    def _():
        t_copy().start()

    n_copy(0).start()

    @pl.when(c == 0)
    def _():
        n_copy(1).start()

    for distance in range(1, n_z):
        low_slab, high_slab = z - distance, z + distance
        for index in range(PIECES):

            @pl.when((low_slab >= 0) & (low_slab < prompt_slabs))
            def _():
                source = far.at[low_slab, c, part(index)]
                z_copy(source, low_slab, index, True).wait_recv()

                @pl.when(z < n_z - 1)
                def _():
                    z_copy(source, low_slab, index, True).start()

                c_copy(source, low_slab, index).start()

            if distance < prompt_slabs:

                @pl.when(high_slab < prompt_slabs)
                def _():
                    source = far.at[high_slab, c, part(index)]
                    z_copy(source, high_slab, index, False).wait_recv()

                    @pl.when(z > 0)
                    def _():
                        z_copy(source, high_slab, index, False).start()

                    c_copy(source, high_slab, index).start()

    @pl.when((c == 1) & (z > 0))
    def _():
        t_copy().wait_recv()
        t_hand().start()
        t_hand().wait_send()

    @pl.when((c == 1) & (z < n_z - 1))
    def _():
        t_copy().wait_send()

    @pl.when((c == 0) & (z > 0))
    def _():
        t_hand().wait_recv()

    n_copy(0).wait_send()
    n_copy(0).wait_recv()

    @pl.when(c == 0)
    def _():
        n_copy(1).wait_send()

    @pl.when(c == 1)
    def _():
        n_copy(1).wait_recv()

    for slab in range(prompt_slabs):
        for index in range(PIECES):
            copy = c_copy(own_rows.at[part(index)], slab, index)
            copy.wait_send()
            copy.wait_recv()

            @pl.when((z < n_z - 1) & (slab <= z))
            def _():
                z_copy(own_rows.at[part(index)], slab, index, True).wait_send()

            @pl.when((z > 0) & (slab >= z))
            def _():
                z_copy(own_rows.at[part(index)], slab, index, False).wait_send()

    for copy in own:
        copy.wait()

    @pl.when(in_prompt)
    def _():
        own_far.wait()

    @pl.when(edge)
    def _():
        own_edge.wait()


def spread_keys(own_rows, prompt_rows, collective_id):
    lane, width = own_rows.shape
    slabs = prompt_rows // (2 * lane)
    dma = pltpu.SemaphoreType.DMA
    far, near, _ = pl.pallas_call(
        functools.partial(spread_kernel, slabs),
        out_shape=(
            jax.ShapeDtypeStruct((slabs, 2, lane, width), own_rows.dtype),
            jax.ShapeDtypeStruct((4, lane // 2, width), own_rows.dtype),
            jax.ShapeDtypeStruct((lane // 2, width), own_rows.dtype),
        ),
        in_specs=[VMEM],
        out_specs=(VMEM,) * 3,
        scratch_shapes=[
            dma((slabs, PIECES, 2)), dma((slabs, PIECES)), dma((slabs, PIECES)), dma((slabs, PIECES)),
            dma((4,)), dma((4,)), dma((4,)),
        ],
        cost_estimate=pl.CostEstimate(
            flops=0, bytes_accessed=60 * MIB, transcendentals=0
        ),
        compiler_params=pltpu.CompilerParams(collective_id=collective_id, has_side_effects=True),
    )(own_rows)
    return far.reshape(prompt_rows, width), near.reshape(2 * lane, width)


def collect_kernel(
    prompt_slabs, far, near, query_grad, whole, out, own, c_got, z_got, n_got, tail_pass, tail_got,
    c_send, c_recv, z_send, z_recv, n_send, n_recv,
):
    n_z = lax.axis_size("z")
    lane = out.shape[0]
    chunk = lane // 2
    size = lane // PIECES
    (z, x, c, y), _, _, c_near = around()
    above, below = (z + 1, x, c, y), (z - 1, x, c, y)

    barrier = pltpu.get_barrier_semaphore()
    pl.semaphore_signal(barrier, inc=1, device_id=c_near, device_id_type=MESH)

    @pl.when(z < n_z - 1)
    def _():
        pl.semaphore_signal(barrier, inc=1, device_id=above, device_id_type=MESH)

    pl.semaphore_wait(barrier, 1 + jnp.where(z > 0, 1, 0))

    def part(index):
        return pl.ds(index * size, size)

    def c_copy(slab, index):
        return remote(
            far.at[slab, 1 - c, part(index)], c_got.at[slab, part(index)], c_send.at[slab, index],
            c_recv.at[slab, index], c_near,
        )

    def z_copy(slab, index):
        return remote(
            own.at[slab, part(index)], z_got.at[slab, part(index)], z_send.at[slab, index],
            z_recv.at[slab, index], below,
        )

    def n_copy(half):
        slot = jnp.where(c == 0, 2, 2 * half)
        return remote(near.at[slot], n_got.at[half], n_send.at[half], n_recv.at[half], c_near)

    def t_hand():
        return remote(near.at[0], tail_pass, n_send.at[2], n_recv.at[2], c_near)

    def t_copy():
        return remote(tail_pass, tail_got, n_send.at[3], n_recv.at[3], below)

    for slab in range(prompt_slabs):
        for index in range(PIECES):
            c_copy(slab, index).start()
    n_copy(0).start()

    @pl.when(c == 1)
    def _():
        n_copy(1).start()

    @pl.when((c == 0) & (z > 0))
    def _():
        t_hand().start()

    for slab in range(prompt_slabs):
        for index in range(PIECES):
            c_copy(slab, index).wait_recv()
            rows = part(index)
            mine = total_of(far[slab, c, rows, :], c_got[slab, rows, :])

            @pl.when((z == n_z - 1) & (z > slab))
            def _():
                own[slab, rows, :] = mine.astype(jnp.bfloat16)
                z_copy(slab, index).start()

            @pl.when((z < n_z - 1) & (z > slab))
            def _():
                z_copy(slab, index).wait_recv()
                own[slab, rows, :] = total_of(mine, z_got[slab, rows, :]).astype(jnp.bfloat16)
                z_copy(slab, index).start()

            @pl.when((z < n_z - 1) & (z == slab))
            def _():
                z_copy(slab, index).wait_recv()
                out[rows, :] = total_of(mine, z_got[slab, rows, :])

            @pl.when((z == n_z - 1) & (z == slab))
            def _():
                out[rows, :] = mine

    @pl.when((c == 1) & (z > 0))
    def _():
        t_hand().wait_recv()
        t_copy().start()

    @pl.when(z >= prompt_slabs)
    def _():
        out[...] = jnp.zeros_like(out)

    n_copy(0).wait_recv()
    first, second = pl.ds(0, chunk), pl.ds(chunk, chunk)
    out[first, :] += total_of(near[1], n_got[0])
    out[second, :] += near[3].astype(jnp.float32)

    @pl.when(c == 0)
    def _():
        n_copy(1).wait_recv()
        out[second, :] += n_got[1].astype(jnp.float32)

    @pl.when((c == 1) & (z < n_z - 1))
    def _():
        t_copy().wait_recv()
        out[second, :] += tail_got[...].astype(jnp.float32)

    whole[...] = jnp.concatenate([out[...].astype(jnp.bfloat16), query_grad[...]], axis=1)

    @pl.when((c == 1) & (z > 0))
    def _():
        t_copy().wait_send()

    @pl.when((c == 0) & (z > 0))
    def _():
        t_hand().wait_send()

    n_copy(0).wait_send()

    @pl.when(c == 1)
    def _():
        n_copy(1).wait_send()

    for slab in range(prompt_slabs):
        for index in range(PIECES):
            c_copy(slab, index).wait_send()

            @pl.when(z > slab)
            def _():
                z_copy(slab, index).wait_send()


def collect_keys(far, near, query_grad, collective_id):
    prompt_rows, width = far.shape
    lane = near.shape[0] // 2
    slabs = prompt_rows // (2 * lane)
    dma = pltpu.SemaphoreType.DMA
    low = jnp.bfloat16
    return pl.pallas_call(
        functools.partial(collect_kernel, slabs),
        out_shape=jax.ShapeDtypeStruct((lane, width + query_grad.shape[1]), low),
        in_specs=[VMEM] * 3,
        out_specs=VMEM,
        scratch_shapes=[
            pltpu.VMEM((lane, width), jnp.float32),
            pltpu.VMEM((slabs, lane, width), low),
            pltpu.VMEM((slabs, lane, width), low),
            pltpu.VMEM((slabs, lane, width), low),
            pltpu.VMEM((2, lane // 2, width), low),
            pltpu.VMEM((lane // 2, width), low),
            pltpu.VMEM((lane // 2, width), low),
            dma((slabs, PIECES)), dma((slabs, PIECES)), dma((slabs, PIECES)), dma((slabs, PIECES)),
            dma((4,)), dma((4,)),
        ],
        cost_estimate=pl.CostEstimate(
            flops=0, bytes_accessed=60 * MIB, transcendentals=0
        ),
        compiler_params=pltpu.CompilerParams(
            collective_id=collective_id, has_side_effects=True, vmem_limit_bytes=20 * MIB
        ),
    )(far.astype(low).reshape(slabs, 2, lane, width), near.astype(low).reshape(4, lane // 2, width), query_grad)


def greet_all():
    n_z, n_x, n_c, n_y = sizes()
    count = n_z * n_x * n_c * n_y
    barrier = pltpu.get_barrier_semaphore()

    def call(step, unused):
        pl.semaphore_signal(barrier, inc=1, device_id=device_after(step), device_id_type=MESH)
        return unused

    lax.fori_loop(1, count, call, 0)
    pl.semaphore_wait(barrier, count - 1)


def index_after(step):
    n_z, n_x, n_c, n_y = sizes()
    z, x, c, y = place()
    me = ((z * n_x + x) * n_c + c) * n_y + y
    return lax.rem(me + step, n_z * n_x * n_c * n_y)


def device_after(step):
    _, n_x, n_c, n_y = sizes()
    index = index_after(step)
    return (
        index // (n_x * n_c * n_y), index // (n_c * n_y) % n_x, index // n_y % n_c, index % n_y
    )


def greet_near():
    n_z = lax.axis_size("z")
    (z, x, c, y), x_near, y_near, c_near = around()
    barrier = pltpu.get_barrier_semaphore()
    for device in (x_near, y_near, c_near):
        pl.semaphore_signal(barrier, inc=1, device_id=device, device_id_type=MESH)

    @pl.when(z > 0)
    def _():
        pl.semaphore_signal(barrier, inc=1, device_id=(z - 1, x, c, y), device_id_type=MESH)

    @pl.when(z < n_z - 1)
    def _():
        pl.semaphore_signal(barrier, inc=1, device_id=(z + 1, x, c, y), device_id_type=MESH)

    pl.semaphore_wait(barrier, 3 + jnp.where(z > 0, 1, 0) + jnp.where(z < n_z - 1, 1, 0))


Z_PIECES = 4


def gather_sems():
    n_z = lax.axis_size("z")
    dma = pltpu.SemaphoreType.DMA
    return [
        dma((n_z, Z_PIECES, 2)), dma((n_z, Z_PIECES)), dma((n_z, 2)), dma((n_z, 2)), dma((n_z, 2)),
        dma((n_z, 2)), dma((n_z, 4)), dma((n_z, 4)), dma,
    ]


def gather_slabs(rows_in, out, sems, work, beside=lambda step: None):
    z_send, z_recv, x_send, x_recv, y_send, y_recv, c_send, c_recv, own_sem = sems
    n_z = lax.axis_size("z")
    half = rows_in.shape[0] // 2
    size = rows_in.shape[0] // Z_PIECES
    (z, x, c, y), x_near, y_near, c_near = around()
    low, high = pl.ds(0, half), pl.ds(half, half)
    everything = pl.ds(0, 2 * half)
    own = pltpu.make_async_copy(rows_in, out.at[z, x, c, y], own_sem)
    own.start()

    def block(origin, px, py, rows):
        return out.at[origin, px, c, py, rows]

    def z_copy(source, origin, index, up):
        rows = pl.ds(index * size, size)
        other = (z + 1, x, c, y) if up else (z - 1, x, c, y)
        return remote(
            source.at[rows], block(origin, x, y, rows), z_send.at[origin, index, 1 if up else 0],
            z_recv.at[origin, index], other,
        )

    def x_copy(source, origin):
        return remote(source, out.at[origin, x, c, y], x_send.at[origin, 0], x_recv.at[origin, 0], x_near)

    def y_copy(source, origin):
        return remote(source, out.at[origin, x, c, y], y_send.at[origin, 0], y_recv.at[origin, 0], y_near)

    def x_relay(origin):
        part = block(origin, x, 1 - y, high)
        return remote(part, part, x_send.at[origin, 1], x_recv.at[origin, 1], x_near)

    def y_relay(origin):
        part = block(origin, 1 - x, y, low)
        return remote(part, part, y_send.at[origin, 1], y_recv.at[origin, 1], y_near)

    def c_copy(source, origin, px, py):
        slot = px * 2 + py
        return remote(
            source, out.at[origin, px, c, py], c_send.at[origin, slot], c_recv.at[origin, slot], c_near
        )

    def column(origin):
        return out.at[origin, x, c, y]

    def spread(source, origin):
        x_copy(source, origin).start()
        y_copy(source, origin).start()
        c_copy(source, origin, x, y).start()

    def relay(origin):
        x_copy(column(origin), origin).wait_recv()
        y_relay(origin).start()
        y_copy(column(origin), origin).wait_recv()
        x_relay(origin).start()
        c_copy(block(origin, 1 - x, y, everything), origin, 1 - x, y).start()
        c_copy(block(origin, x, 1 - y, everything), origin, x, 1 - y).start()

    def finish(origin):
        x_relay(origin).wait_recv()
        y_relay(origin).wait_recv()
        c_copy(block(origin, 1 - x, 1 - y, everything), origin, 1 - x, 1 - y).start()

    def use(origin):
        for px in range(2):
            for py in range(2):
                c_copy(out.at[origin, px, c, py], origin, px, py).wait_recv()
        work(origin)

    def arrive(step):
        below, above = z - step, z + step

        @pl.when(below >= 0)
        def _():
            for index in range(Z_PIECES):
                z_copy(rows_in, below, index, True).wait_recv()

                @pl.when(z < n_z - 1)
                def _():
                    z_copy(column(below), below, index, True).start()

            spread(column(below), below)

        @pl.when(above < n_z)
        def _():
            for index in range(Z_PIECES):
                z_copy(rows_in, above, index, False).wait_recv()

                @pl.when(z > 0)
                def _():
                    z_copy(column(above), above, index, False).start()

            spread(column(above), above)

    for index in range(Z_PIECES):

        @pl.when(z < n_z - 1)
        def _():
            z_copy(rows_in, z, index, True).start()

        @pl.when(z > 0)
        def _():
            z_copy(rows_in, z, index, False).start()

    spread(rows_in, z)
    for step in range(1, n_z + 3):
        if step < n_z:
            arrive(step)
        for action, back in ((relay, 1), (finish, 2), (use, 3)):
            late = step - back
            if late == 0:
                if action is use:
                    own.wait()
                action(z)
            elif 0 < late < n_z:
                for origin in (z - late, z + late):

                    @pl.when((origin >= 0) & (origin < n_z))
                    def _():
                        action(origin)

        beside(step)

    def close(origin, unused):
        x_copy(rows_in, origin).wait_send()
        y_copy(rows_in, origin).wait_send()
        x_relay(origin).wait_send()
        y_relay(origin).wait_send()
        for px in range(2):
            for py in range(2):
                c_copy(out.at[origin, px, c, py], origin, px, py).wait_send()
        for index in range(Z_PIECES):

            @pl.when((z < n_z - 1) & (origin <= z))
            def _():
                z_copy(rows_in, origin, index, True).wait_send()

            @pl.when((z > 0) & (origin >= z))
            def _():
                z_copy(rows_in, origin, index, False).wait_send()

        return unused

    lax.fori_loop(0, n_z, close, 0)


def line_gather_sems():
    n_z = lax.axis_size("z")
    dma = pltpu.SemaphoreType.DMA
    return [dma((n_z, 2, 2)), dma((n_z, 2)), dma((n_z, 2)), dma((n_z, 2)), dma((2,))]


def line_gather(own_parts, all_parts, sems):
    z_send, z_recv, c_send, c_recv, own_sem = sems
    n_z = lax.axis_size("z")
    (z, x, c, y), _, _, c_near = around()
    numbers = range(len(own_parts))

    def z_copy(source, number, origin, up):
        return remote(
            source, all_parts[number](origin, c), z_send.at[origin, number, 1 if up else 0],
            z_recv.at[origin, number], (z + 1, x, c, y) if up else (z - 1, x, c, y),
        )

    def c_copy(source, number, origin):
        return remote(
            source, all_parts[number](origin, c), c_send.at[origin, number], c_recv.at[origin, number], c_near
        )

    own = [
        pltpu.make_async_copy(own_parts[number], all_parts[number](z, c), own_sem.at[number])
        for number in numbers
    ]
    for copy in own:
        copy.start()
    for number in numbers:
        source = own_parts[number]

        @pl.when(z < n_z - 1)
        def _():
            z_copy(source, number, z, True).start()

        @pl.when(z > 0)
        def _():
            z_copy(source, number, z, False).start()

        c_copy(source, number, z).start()

    def beside(step):
        below, above = z - step, z + step

        @pl.when((step >= 1) & (below >= 0))
        def _():
            for number in numbers:
                source = all_parts[number](below, c)
                z_copy(source, number, below, True).wait_recv()

                @pl.when(z < n_z - 1)
                def _():
                    z_copy(source, number, below, True).start()

                c_copy(source, number, below).start()

        @pl.when((step >= 1) & (above < n_z))
        def _():
            for number in numbers:
                source = all_parts[number](above, c)
                z_copy(source, number, above, False).wait_recv()

                @pl.when(z > 0)
                def _():
                    z_copy(source, number, above, False).start()

                c_copy(source, number, above).start()

    def close():
        for copy in own:
            copy.wait()

        def one(origin, unused):
            for number in numbers:
                c_copy(own_parts[number], number, origin).wait()

                @pl.when((z < n_z - 1) & (origin <= z))
                def _():
                    z_copy(own_parts[number], number, origin, True).wait_send()

                @pl.when((z > 0) & (origin >= z))
                def _():
                    z_copy(own_parts[number], number, origin, False).wait_send()

            return unused

        lax.fori_loop(0, n_z, one, 0)

    return beside, close


def line_sems(parts):
    n_z = lax.axis_size("z")
    dma = pltpu.SemaphoreType.DMA
    return [dma((parts,)), dma((parts,)), dma((n_z, 2, parts)), dma((n_z, 2, parts))]


def line_sums(packs, outs, buffers, sems):
    c_send, c_recv, z_send, z_recv = sems
    n_z = lax.axis_size("z")
    (z, x, c, y), _, _, c_near = around()
    numbers = range(len(packs))
    lanes, got, below, above = (buffers[each :: 4] for each in range(4))
    handed = [
        remote(packs[each].at[1 - c], got[each], c_send.at[each], c_recv.at[each], c_near)
        for each in numbers
    ]

    def z_copy(slab, up, each):
        return remote(
            lanes[each].at[slab], (below if up else above)[each].at[slab],
            z_send.at[slab, 1 if up else 0, each], z_recv.at[slab, 1 if up else 0, each],
            (z + 1, x, c, y) if up else (z - 1, x, c, y),
        )

    for copy in handed:
        copy.start()

    def merge():
        for each in numbers:
            handed[each].wait()
            lanes[each][...] = total_of(packs[each][c], got[each][...]).astype(jnp.bfloat16)

    def hop(turn, step):
        high, low = n_z - 1 - turn, turn

        @pl.when((z == step - 1 - turn) & (z < high))
        def _():
            for each in numbers:

                @pl.when(z > 0)
                def _():
                    z_copy(high, True, each).wait_recv()
                    lanes[each][high] = total_of(lanes[each][high], below[each][high]).astype(jnp.bfloat16)

                z_copy(high, True, each).start()

        @pl.when((n_z - 1 - z == step - 1 - turn) & (z > low))
        def _():
            for each in numbers:

                @pl.when(z < n_z - 1)
                def _():
                    z_copy(low, False, each).wait_recv()
                    lanes[each][low] = total_of(lanes[each][low], above[each][low]).astype(jnp.bfloat16)

                z_copy(low, False, each).start()

    def beside(step):
        if step == 1:
            merge()
        if step < n_z:

            def body(turn, unused):
                hop(turn, step)
                return unused

            lax.fori_loop(0, n_z - 1, body, 0)

    def close():
        for each in numbers:
            out = outs[each]
            out[...] = lanes[each][z].astype(jnp.float32)

            @pl.when(z > 0)
            def _():
                z_copy(z, True, each).wait_recv()
                out[...] += below[each][z].astype(jnp.float32)

            @pl.when(z < n_z - 1)
            def _():
                z_copy(z, False, each).wait_recv()
                out[...] += above[each][z].astype(jnp.float32)

        def sent(slab, unused):
            for each in numbers:

                @pl.when(slab > z)
                def _():
                    z_copy(slab, True, each).wait_send()

                @pl.when(slab < z)
                def _():
                    z_copy(slab, False, each).wait_send()

            return unused

        lax.fori_loop(0, n_z, sent, 0)

    return beside, close


def in_pairs(values, slab, px, pc, row):
    return jnp.concatenate([values[slab, px, pc, py, row : row + 1, :] for py in range(2)], axis=1)


def vocab_ids(extent, chunk, shard_rows):
    n_z, n_x, n_c, n_y = sizes()
    z, x, c, y = place()
    me = ((z * n_x + x) * n_c + c) * n_y + y
    rows = lax.broadcasted_iota(jnp.int32, (extent, chunk), 0)
    return rows + me * shard_rows


def logits_kernel(shard_rows, rows_in, table, ints, valid, out, logs, hits, *sems):
    extent = table.shape[0]
    chunk = 2 * rows_in.shape[0]
    scale = table.shape[1] ** (-0.5)
    greet_near()
    hits[...] = jnp.zeros_like(hits)

    def work(slab):
        def one(index, unused):
            px, pc = index // 2, index % 2
            rows = out[slab, px, pc].reshape(chunk, -1)
            value = outer(table[...], rows) * scale
            ids = vocab_ids(extent, chunk, shard_rows)
            inside = lax.broadcasted_iota(jnp.int32, (extent, chunk), 0) < shard_rows
            target = in_pairs(ints, slab, px, pc, 1).astype(jnp.int32)
            shown = in_pairs(valid, slab, px, pc, 0)
            hit = jnp.where(ids == target, value, 0.0)
            hits[...] += jnp.sum(hit, axis=0, keepdims=True) * shown
            value = jnp.where(inside, value, MASKED)
            peak = jnp.max(value, axis=0, keepdims=True)
            log = peak + jnp.log(jnp.sum(jnp.exp(value - peak), axis=0, keepdims=True))
            half = chunk // 2
            logs[slab, px, pc, 0] = log[:, :half]
            logs[slab, px, pc, 1] = log[:, half:]
            return unused

        lax.fori_loop(0, 4, one, 0)

    gather_slabs(rows_in, out, sems, work)


def gather_logits(rows, table, ints, valid, shard_rows, collective_id):
    own, width = rows.shape
    shape = sizes() + (own, width)
    return pl.pallas_call(
        functools.partial(logits_kernel, shard_rows),
        out_shape=(
            jax.ShapeDtypeStruct(shape, rows.dtype),
            jax.ShapeDtypeStruct(sizes() + (1, own), jnp.float32),
            jax.ShapeDtypeStruct((1, 2 * own), jnp.float32),
        ),
        in_specs=[VMEM] * 4,
        out_specs=(VMEM,) * 3,
        scratch_shapes=gather_sems(),
        cost_estimate=pl.CostEstimate(
            flops=0, bytes_accessed=108 * MIB, transcendentals=0
        ),
        compiler_params=pltpu.CompilerParams(
            collective_id=collective_id, has_side_effects=True,
            vmem_limit_bytes=lax.axis_size("z") * 2 * MIB + 20 * MIB,
        ),
    )(rows, table, ints, valid)


def embed_back_kernel(shard_rows, parts, rows_in, ints, table_grad, smalls, *refs):
    packs, refs = refs[:parts], refs[parts:]
    out, small_sum, squares, refs = refs[0], refs[1], refs[2], refs[3:]
    pack_sums, refs = refs[:parts], refs[parts:]
    slabs, small_got, refs = refs[0], refs[1], refs[2:]
    buffers, sems = refs[: 4 * parts], refs[4 * parts :]
    extent = out.shape[0]
    chunk = 2 * rows_in.shape[0]
    small_send, small_recv = sems[-6:-4]
    n_z, n_x, n_c, n_y = sizes()
    count = n_z * n_x * n_c * n_y
    me = index_after(0)
    greet_all()

    def small(step):
        return remote(
            smalls.at[index_after(step)], small_got.at[me], small_send.at[step], small_recv.at[step],
            device_after(step),
        )

    def each(action):
        def body(step, unused):
            action(step)
            return unused

        lax.fori_loop(1, count, body, 0)

    each(lambda step: small(step).start())
    beside, close_line = line_sums(packs, pack_sums, buffers, sems[-4:])
    small_got[me] = smalls[me]
    out[...] = table_grad[...]

    def work(slab):
        def one(index, unused):
            px, pc = index // 2, index % 2
            token = in_pairs(ints, slab, px, pc, 0).astype(jnp.int32)
            hot = vocab_ids(extent, chunk, shard_rows) == token
            hot = jnp.where(hot, 1.0, 0.0).astype(jnp.bfloat16)
            out[...] += matmul(hot, slabs[slab, px, pc].reshape(chunk, -1))
            return unused

        lax.fori_loop(0, 4, one, 0)

    gather_slabs(rows_in, slabs, sems[:-6], work, beside)
    close_line()
    each(lambda step: small(step).wait())
    small_sum[...] = jnp.sum(small_got[...], axis=0)
    value = out[...]
    inside = lax.broadcasted_iota(jnp.int32, value.shape, 0) < shard_rows
    squares[...] = jnp.sum(jnp.where(inside, value * value, 0.0), axis=0, keepdims=True)


def embed_back(rows, ints, table_grad, smalls, packs, shard_rows, collective_id):
    own, width = rows.shape
    count = smalls.shape[0]
    dma = pltpu.SemaphoreType.DMA
    return pl.pallas_call(
        functools.partial(embed_back_kernel, shard_rows, len(packs)),
        out_shape=(
            jax.ShapeDtypeStruct(table_grad.shape, jnp.float32),
            jax.ShapeDtypeStruct(smalls.shape[1:], jnp.float32),
            jax.ShapeDtypeStruct((1, width), jnp.float32),
        )
        + tuple(jax.ShapeDtypeStruct(pack.shape[2:], jnp.float32) for pack in packs),
        in_specs=[VMEM] * (4 + len(packs)),
        out_specs=(VMEM,) * (3 + len(packs)),
        scratch_shapes=[
            pltpu.VMEM(sizes() + (own, width), rows.dtype), pltpu.VMEM(smalls.shape, jnp.float32),
        ]
        + [pltpu.VMEM(pack.shape[1:], pack.dtype) for pack in packs for _ in range(4)]
        + gather_sems() + [dma((count,)), dma((count,))] + line_sems(len(packs)),
        cost_estimate=pl.CostEstimate(
            flops=0, bytes_accessed=120 * MIB, transcendentals=0
        ),
        compiler_params=pltpu.CompilerParams(
            collective_id=collective_id, has_side_effects=True,
            vmem_limit_bytes=lax.axis_size("z") * 2 * MIB + 28 * MIB,
        ),
    )(rows, ints, table_grad, smalls, *packs)


def slab_order():
    n_z = lax.axis_size("z")
    z = lax.axis_index("z")
    up, down = n_z - 1 - z, z
    longer, shorter = jnp.maximum(up, down), jnp.minimum(up, down)
    far_side = jnp.where(up >= down, 1, -1)

    def target(step):
        late = step - (longer - shorter)
        near_side = jnp.where(late % 2 == 0, far_side, -far_side)
        return jnp.where(
            late < 0, z + far_side * (longer - step), z + near_side * (shorter - late // 2)
        )

    return target


def scatter_scratch(rows, width):
    n_z, n_x, n_c, n_y = sizes()
    half = rows // 2
    low = jnp.bfloat16
    dma = pltpu.SemaphoreType.DMA
    return [
        pltpu.VMEM((n_z, n_x, n_y, rows, width), low),
        pltpu.VMEM((n_z, n_x, n_y, rows, width), low),
        pltpu.VMEM((n_z, n_x, n_y, rows, width), low),
        pltpu.VMEM((n_z, 2, half, width), low),
        pltpu.VMEM((n_z, 2, half, width), low),
        pltpu.VMEM((n_z, half, width), low),
        pltpu.VMEM((n_z, half, width), low),
        pltpu.VMEM((n_z, rows, width), low),
        pltpu.VMEM((n_z, rows, width), low),
        dma((n_z, 2)), dma((n_z, 2)), dma((n_z, 3)), dma((n_z, 3)), dma((n_z, 3)),
        dma((n_z, 3)), dma((n_z, 2)), dma((n_z, 2, 2)),
    ]


def scatter_slabs(out, scratch, before, make, after, beside=lambda step: None):
    (
        lanes, handed, c_got, x_got, y_got, x_last, y_last, below, above,
        c_send, c_recv, x_send, x_recv, y_send, y_recv, z_send, z_recv,
    ) = scratch
    n_z = lax.axis_size("z")
    rows = out.shape[0]
    half = rows // 2
    (z, x, c, y), x_near, y_near, c_near = around()
    halves = (pl.ds(0, half), pl.ds(half, half))
    low, high = halves
    target = slab_order()

    def c_copy(slab, px):
        return remote(
            handed.at[slab, px], c_got.at[slab, px], c_send.at[slab, px], c_recv.at[slab, px], c_near
        )

    def x_first(slab, part):
        block = lanes.at[slab, 1 - x, y if part == 0 else 1 - y, low]
        return remote(block, x_got.at[slab, part], x_send.at[slab, part], x_recv.at[slab, part], x_near)

    def y_first(slab, part):
        block = lanes.at[slab, x if part == 0 else 1 - x, 1 - y, high]
        return remote(block, y_got.at[slab, part], y_send.at[slab, part], y_recv.at[slab, part], y_near)

    def y_second(slab):
        block = lanes.at[slab, x, 1 - y, low]
        return remote(block, y_last.at[slab], y_send.at[slab, 2], y_recv.at[slab, 2], y_near)

    def x_second(slab):
        block = lanes.at[slab, 1 - x, y, high]
        return remote(block, x_last.at[slab], x_send.at[slab, 2], x_recv.at[slab, 2], x_near)

    def z_up(slab, part):
        return remote(
            lanes.at[slab, x, y, halves[part]], below.at[slab, halves[part]], z_send.at[slab, part],
            z_recv.at[slab, 0, part], (z + 1, x, c, y),
        )

    def z_down(slab, part):
        return remote(
            lanes.at[slab, x, y, halves[part]], above.at[slab, halves[part]], z_send.at[slab, part],
            z_recv.at[slab, 1, part], (z - 1, x, c, y),
        )

    def produce(step):
        slab = target(step)
        before(step)

        def hand(px, unused):
            handed[slab, px] = make(step, slab, px, 1 - c).reshape(2, rows, -1)
            c_copy(slab, px).start()
            return unused

        def keep(px, unused):
            lanes[slab, px] = make(step, slab, px, c).reshape(2, rows, -1)
            return unused

        lax.fori_loop(0, 2, hand, 0)
        lax.fori_loop(0, 2, keep, 0)

    def begin(step):
        slab = target(step)
        for px in range(2):
            c_copy(slab, px).wait_recv()

        def merge(px, py):
            lanes[slab, px, py] = total_of(lanes[slab, px, py], c_got[slab, px, py]).astype(jnp.bfloat16)

        merge(1 - x, 1 - y)
        x_first(slab, 1).start()
        y_first(slab, 1).start()
        merge(1 - x, y)
        x_first(slab, 0).start()
        merge(x, 1 - y)
        y_first(slab, 0).start()
        merge(x, y)
        after(step)

    def middle(step):
        slab = target(step)
        x_first(slab, 1).wait_recv()
        x_first(slab, 0).wait_send()
        y_first(slab, 0).wait_send()
        lanes[slab, x, 1 - y, low] = total_of(
            lanes[slab, x, 1 - y, low], x_got[slab, 1]
        ).astype(jnp.bfloat16)
        y_second(slab).start()
        y_first(slab, 1).wait_recv()
        lanes[slab, 1 - x, y, high] = total_of(
            lanes[slab, 1 - x, y, high], y_got[slab, 1]
        ).astype(jnp.bfloat16)
        x_second(slab).start()

    def finish(step):
        slab = target(step)
        for part in range(2):
            if part == 0:
                x_first(slab, 0).wait_recv()
                y_second(slab).wait_recv()
                value = total_of(lanes[slab, x, y, low], x_got[slab, 0], y_last[slab])
            else:
                y_first(slab, 0).wait_recv()
                x_second(slab).wait_recv()
                value = total_of(lanes[slab, x, y, high], y_got[slab, 0], x_last[slab])
            rows_of = halves[part]

            @pl.when(slab > z)
            def _():
                @pl.when(z == 0)
                def _():
                    lanes[slab, x, y, rows_of] = value.astype(jnp.bfloat16)

                @pl.when(z > 0)
                def _():
                    z_up(slab, part).wait_recv()
                    lanes[slab, x, y, rows_of] = total_of(value, below[slab, rows_of]).astype(jnp.bfloat16)

                z_up(slab, part).start()

            @pl.when(slab < z)
            def _():
                @pl.when(z == n_z - 1)
                def _():
                    lanes[slab, x, y, rows_of] = value.astype(jnp.bfloat16)

                @pl.when(z < n_z - 1)
                def _():
                    z_down(slab, part).wait_recv()
                    lanes[slab, x, y, rows_of] = total_of(value, above[slab, rows_of]).astype(jnp.bfloat16)

                z_down(slab, part).start()

            @pl.when(slab == z)
            def _():
                out[rows_of, :] = value

                @pl.when(z > 0)
                def _():
                    z_up(slab, part).wait_recv()
                    out[rows_of, :] += below[slab, rows_of].astype(jnp.float32)

                @pl.when(z < n_z - 1)
                def _():
                    z_down(slab, part).wait_recv()
                    out[rows_of, :] += above[slab, rows_of].astype(jnp.float32)

    def turn(step, unused):
        for action, back in ((produce, 0), (begin, 0), (middle, 1), (finish, 2)):

            @pl.when((step >= back) & (step < n_z + back))
            def _():
                action(step - back)

        beside(step)
        return unused

    lax.fori_loop(0, n_z + 2, turn, 0)

    def close(slab, unused):
        for px in range(2):
            c_copy(slab, px).wait_send()
        x_first(slab, 1).wait_send()
        y_first(slab, 1).wait_send()
        x_second(slab).wait_send()
        y_second(slab).wait_send()
        for part in range(2):

            @pl.when(slab > z)
            def _():
                z_up(slab, part).wait_send()

            @pl.when(slab < z)
            def _():
                z_down(slab, part).wait_send()

        return unused

    lax.fori_loop(0, n_z, close, 0)


def embed_kernel(shard_rows, table, ints, qkv_own, out_own, out, qkv_all, out_all, *scratch):
    extent = table.shape[0]
    chunk = 2 * out.shape[0]
    greet_near()
    beside, close = line_gather(
        (qkv_own, out_own),
        (lambda pz, pc: qkv_all.at[:, pz, :, pc], lambda pz, pc: out_all.at[:, pz, pc]),
        scratch[-5:],
    )

    def make(step, slab, px, pc):
        token = in_pairs(ints, slab, px, pc, 0).astype(jnp.int32)
        hot = vocab_ids(extent, chunk, shard_rows) == token
        hot = jnp.where(hot, 1.0, 0.0).astype(jnp.bfloat16)
        return inner(hot, table[...]).astype(jnp.bfloat16)

    scatter_slabs(out, scratch[:-5], lambda step: None, make, lambda step: None, beside)
    close()


def embed(table, ints, qkv_own, out_own, own, shard_rows, collective_id):
    width = table.shape[1]
    n_z, n_x, n_c, _ = sizes()
    layers = qkv_own.shape[0]
    return pl.pallas_call(
        functools.partial(embed_kernel, shard_rows),
        out_shape=(
            jax.ShapeDtypeStruct((own, width), jnp.float32),
            jax.ShapeDtypeStruct((layers, n_z, n_x, n_c) + qkv_own.shape[2:], qkv_own.dtype),
            jax.ShapeDtypeStruct((layers, n_z, n_c) + out_own.shape[1:], out_own.dtype),
        ),
        in_specs=[VMEM] * 4,
        out_specs=(VMEM,) * 3,
        scratch_shapes=scatter_scratch(own, width) + line_gather_sems(),
        cost_estimate=pl.CostEstimate(
            flops=0, bytes_accessed=120 * MIB, transcendentals=0
        ),
        compiler_params=pltpu.CompilerParams(
            collective_id=collective_id, has_side_effects=True,
            vmem_limit_bytes=lax.axis_size("z") * 3 * MIB + 12 * MIB,
        ),
    )(table, ints, qkv_own, out_own)


def vocab_back_kernel(
    shard_rows, held, rows_all, table, ints, logs, weights, out, table_grad, slab_rows, changes, slab_sem, *scratch
):
    extent, width = table.shape
    chunk = 2 * out.shape[0]
    scale = width ** (-0.5)
    n_z = lax.axis_size("z")
    target = slab_order()

    def load(step):
        return pltpu.make_async_copy(
            rows_all.at[target(step)], slab_rows.at[step % 2], slab_sem.at[step % 2]
        )

    if not held:
        load(0).start()
    greet_near()
    table_grad[...] = jnp.zeros_like(table_grad)

    def rows_of(step, px, pc):
        if held:
            return rows_all[target(step), px, pc].reshape(chunk, width)
        return slab_rows[step % 2, px, pc].reshape(chunk, width)

    def before(step):
        if held:
            return
        load(step).wait()

        @pl.when(step + 1 < n_z)
        def _():
            load(step + 1).start()

    def make(step, slab, px, pc):
        value = outer(table[...], rows_of(step, px, pc)) * scale
        aim = in_pairs(ints, slab, px, pc, 1).astype(jnp.int32)
        hot = jnp.where(vocab_ids(extent, chunk, shard_rows) == aim, 1.0, 0.0)
        change = jnp.exp(value - in_pairs(logs, slab, px, pc, 0)) - hot
        change = (change * in_pairs(weights, slab, px, pc, 0)).astype(jnp.bfloat16)
        changes[px, pc] = change
        return (inner(change, table[...]) * scale).astype(jnp.bfloat16)

    def after(step):
        def one(index, unused):
            px, pc = index // 2, index % 2
            table_grad[...] += matmul(changes[px, pc], rows_of(step, px, pc))
            return unused

        lax.fori_loop(0, 4, one, 0)

    scatter_slabs(out, scratch, before, make, after)
    table_grad[...] = table_grad[...] * scale


def vocab_back(rows_all, table, ints, logs, weights, shard_rows, collective_id):
    own, width = rows_all.shape[4:]
    extent = table.shape[0]
    n_z, n_x, n_c, n_y = sizes()
    held = n_z <= 4
    return pl.pallas_call(
        functools.partial(vocab_back_kernel, shard_rows, held),
        out_shape=(
            jax.ShapeDtypeStruct((own, width), jnp.float32),
            jax.ShapeDtypeStruct((extent, width), jnp.float32),
        ),
        in_specs=[VMEM if held else ANY] + [VMEM] * 4,
        out_specs=(VMEM,) * 2,
        scratch_shapes=[
            pltpu.VMEM((1,) * 6 if held else (2, n_x, n_c, n_y, own, width), rows_all.dtype),
            pltpu.VMEM((n_x, n_c, extent, 2 * own), jnp.bfloat16),
            pltpu.SemaphoreType.DMA((2,)),
        ] + scatter_scratch(own, width),
        cost_estimate=pl.CostEstimate(
            flops=0, bytes_accessed=144 * MIB, transcendentals=0
        ),
        compiler_params=pltpu.CompilerParams(
            collective_id=collective_id, has_side_effects=True,
            vmem_limit_bytes=n_z * 3 * MIB + 20 * MIB if n_z <= 8 else 62 * MIB,
        ),
    )(rows_all, table, ints, logs, weights)


SQRT_HALF = 0.5**0.5
DENSITY = 0.3989422804014327


def matmul(left, right):
    return jnp.dot(left, right, preferred_element_type=jnp.float32)


def inner(left, right):
    return lax.dot_general(
        left, right, (((0,), (0,)), ((), ())), preferred_element_type=jnp.float32
    )


def outer(left, right):
    return lax.dot_general(
        left, right, (((1,), (1,)), ((), ())), preferred_element_type=jnp.float32
    )


def plane_gather(own_rows, blocks, send_sem, recv_sem):
    half = own_rows.shape[0] // 2
    (z, x, c, y), x_near, y_near, _ = around()
    low, high = pl.ds(0, half), pl.ds(half, half)

    def copy(slot, px, py, rows, source, device):
        target = blocks.at[px, py, rows]
        return remote(target if source is None else source.at[rows], target, send_sem.at[slot], recv_sem.at[slot], device)

    first = [
        copy(0, x, y, low, own_rows, x_near),
        copy(1, x, y, high, own_rows, y_near),
        copy(2, x, y, high, own_rows, x_near),
        copy(3, x, y, low, own_rows, y_near),
    ]
    relays = [copy(4, 1 - x, y, low, None, y_near), copy(5, x, 1 - y, high, None, x_near)]
    for each in first:
        each.start()

    def wait_near():
        first[0].wait_recv()
        relays[0].start()
        first[1].wait_recv()
        relays[1].start()

    def wait_x():
        first[2].wait_recv()

    def wait_y():
        first[3].wait_recv()

    def wait_diagonal():
        for each in relays:
            each.wait_recv()

    def close():
        for each in first + relays:
            each.wait_send()

    return wait_near, wait_x, wait_y, wait_diagonal, close


def plane_sum(parts, got, out, send_sem, recv_sem):
    (z, x, c, y), x_near, y_near, _ = around()
    diagonal = (z, 1 - x, c, 1 - y)
    copies = [
        remote(parts.at[device[1], device[3]], got.at[slot], send_sem.at[slot], recv_sem.at[slot], device)
        for slot, device in enumerate((x_near, y_near, diagonal))
    ]

    def close():
        for each in copies:
            each.wait_recv()
        out[...] = total_of(parts[x, y], got[0], got[1], got[2])
        for each in copies:
            each.wait_send()

    return copies, close


def order_experts(kept, got, ordered, sems):
    n_z, n_c, _, depth, _ = kept.shape
    x = lax.axis_index("x")
    copies = []
    for pz in range(n_z):
        for pc in range(n_c):
            for side, weights in enumerate((kept, got)):
                if depth == ordered.shape[1]:
                    rows, side = pl.ds(0, depth), 0
                else:
                    px = x if side == 0 else 1 - x
                    at = (pz * 2 + px) * n_c + pc
                    rows = pl.ds(pl.multiple_of(at * depth, 16), depth)
                slot = (pz * n_c + pc) * 2 + side
                if depth == ordered.shape[1] and weights is got:
                    continue
                copies.append(
                    pltpu.make_async_copy(weights.at[pz, pc], ordered.at[:, rows], sems.at[slot])
                )
    for copy in copies:
        copy.start()
    return copies


def experts_kernel(
    own_rows, route, w_kept, w_got, out, wide, before, hidden, ordered, parts, got, w_sem, g_send, g_recv, s_send, s_recv
):
    (z, x, c, y), x_near, y_near, _ = around()
    diagonal = (z, 1 - x, c, 1 - y)
    loads = order_experts(w_kept, w_got, ordered, w_sem)
    up, down = ordered.at[pl.ds(0, 2)], ordered.at[pl.ds(2, 2)]
    greet((x_near, y_near, diagonal))
    wait_near, wait_x, wait_y, wait_diagonal, close = plane_gather(own_rows, wide, g_send, g_recv)
    copies, finish = plane_sum(parts, got, out, s_send, s_recv)
    wide[x, y] = own_rows[...]

    def work(px, py):
        rows = wide[px, py]
        first = route[px, py] == 0
        value = jnp.where(first, matmul(rows, up[0]), matmul(rows, up[1]))
        before[px, py] = value
        active = 0.5 * value * (1.0 + lax.erf(value * SQRT_HALF))
        hidden_first = jnp.where(first, active, 0.0).astype(jnp.bfloat16)
        hidden_second = jnp.where(first, 0.0, active).astype(jnp.bfloat16)
        hidden[px, py] = active.astype(jnp.bfloat16)
        total = outer(hidden_first, down[0]) + outer(hidden_second, down[1])
        parts[px, py] = total.astype(jnp.bfloat16)

    for load in loads:
        load.wait()
    work(x, y)
    wait_near()
    wait_x()
    work(1 - x, y)
    copies[0].start()
    wait_y()
    work(x, 1 - y)
    copies[1].start()
    wait_diagonal()
    work(1 - x, 1 - y)
    copies[2].start()
    finish()
    close()


def experts(own_rows, route, weights, collective_id):
    _, n_x, _, n_y = sizes()
    own, width = own_rows.shape
    wide = weights[0].shape[4]
    dma = pltpu.SemaphoreType.DMA
    low = jnp.bfloat16
    return pl.pallas_call(
        experts_kernel,
        out_shape=(
            jax.ShapeDtypeStruct((own, width), jnp.float32),
            jax.ShapeDtypeStruct((n_x, n_y, own, width), low),
            jax.ShapeDtypeStruct((n_x, n_y, own, wide), jnp.float32),
            jax.ShapeDtypeStruct((n_x, n_y, own, wide), low),
        ),
        in_specs=[VMEM, VMEM, ANY, ANY],
        out_specs=(VMEM,) * 4,
        scratch_shapes=[
            pltpu.VMEM((4, width, wide), low),
            pltpu.VMEM((n_x, n_y, own, width), low),
            pltpu.VMEM((3, own, width), low),
            dma((width // weights[0].shape[3],)), dma((6,)), dma((6,)), dma((3,)), dma((3,)),
        ],
        compiler_params=pltpu.CompilerParams(
            collective_id=collective_id, has_side_effects=True, vmem_limit_bytes=20 * MIB
        ),
        cost_estimate=pl.CostEstimate(
            flops=8 * own * 4 * width * wide, bytes_accessed=54 * MIB, transcendentals=4 * own * wide
        ),
    )(own_rows, route, *weights)


def experts_back_kernel(
    own_rows, route, w_kept, w_got, wide, before, hidden, out, grads,
    ordered, wide_grad, before_grad, parts, got, w_sem, g_send, g_recv, s_send, s_recv,
):
    (z, x, c, y), x_near, y_near, _ = around()
    diagonal = (z, 1 - x, c, 1 - y)
    loads = order_experts(w_kept, w_got, ordered, w_sem)
    up, down = ordered.at[pl.ds(0, 2)], ordered.at[pl.ds(2, 2)]
    greet((x_near, y_near, diagonal))
    wait_near, wait_x, wait_y, wait_diagonal, close = plane_gather(own_rows, wide_grad, g_send, g_recv)
    copies, finish = plane_sum(parts, got, out, s_send, s_recv)
    wide_grad[x, y] = own_rows[...]

    def work(px, py):
        rows = wide_grad[px, py]
        first = route[px, py] == 0
        hidden_grad = jnp.where(first, matmul(rows, down[0]), matmul(rows, down[1]))
        value = before[px, py]
        slope = 0.5 * (1.0 + lax.erf(value * SQRT_HALF)) + value * (
            DENSITY * jnp.exp(-0.5 * value * value)
        )
        change = (hidden_grad * slope).astype(jnp.bfloat16)
        before_grad[px, py] = change
        change_first = jnp.where(first, change, 0)
        change_second = jnp.where(first, 0, change)
        total = outer(change_first, up[0]) + outer(change_second, up[1])
        parts[px, py] = total.astype(jnp.bfloat16)

    for load in loads:
        load.wait()
    work(x, y)
    wait_near()
    wait_x()
    work(1 - x, y)
    copies[0].start()
    wait_y()
    work(x, 1 - y)
    copies[1].start()
    wait_diagonal()
    work(1 - x, 1 - y)
    copies[2].start()
    close()

    lane = 4 * own_rows.shape[0]
    rows = wide[...].reshape(lane, -1)
    grad_rows = wide_grad[...].reshape(lane, -1)
    first = route[...].reshape(lane, 1) == 0
    change = before_grad[...].reshape(lane, -1)
    active = hidden[...].reshape(lane, -1)
    low = jnp.bfloat16
    n_z, n_x, n_c, _ = sizes()
    depth = grads.shape[3]

    def keep(slot, value):
        value = value.astype(low)
        for pz in range(n_z):
            for px in range(n_x):
                for pc in range(n_c):
                    start = ((pz * n_x + px) * n_c + pc) * depth
                    grads[pz * n_c + pc, px, slot] = value[start : start + depth]

    keep(0, inner(rows, jnp.where(first, change, 0)))
    keep(1, inner(rows, jnp.where(first, 0, change)))
    keep(2, inner(grad_rows, jnp.where(first, active, 0)))
    keep(3, inner(grad_rows, jnp.where(first, 0, active)))
    finish()


def experts_back(own_rows, route, weights, wide, before, hidden, collective_id):
    n_z, n_x, n_c, n_y = sizes()
    own, width = own_rows.shape
    units = weights[0].shape[4]
    dma = pltpu.SemaphoreType.DMA
    low = jnp.bfloat16
    return pl.pallas_call(
        experts_back_kernel,
        out_shape=(
            jax.ShapeDtypeStruct((own, width), jnp.float32),
            jax.ShapeDtypeStruct((n_z * n_c, n_x, 4, width // (n_z * n_x * n_c), units), low),
        ),
        in_specs=[VMEM, VMEM, ANY, ANY] + [VMEM] * 3,
        out_specs=(VMEM,) * 2,
        scratch_shapes=[
            pltpu.VMEM((4, width, units), low),
            pltpu.VMEM((n_x, n_y, own, width), low),
            pltpu.VMEM((n_x, n_y, own, units), low),
            pltpu.VMEM((n_x, n_y, own, width), low),
            pltpu.VMEM((3, own, width), low),
            dma((width // weights[0].shape[3],)), dma((6,)), dma((6,)), dma((3,)), dma((3,)),
        ],
        compiler_params=pltpu.CompilerParams(
            collective_id=collective_id, has_side_effects=True, vmem_limit_bytes=28 * MIB
        ),
        cost_estimate=pl.CostEstimate(
            flops=16 * own * 4 * width * units, bytes_accessed=54 * MIB, transcendentals=8 * own * units
        ),
    )(own_rows, route, *weights, wide, before, hidden)


def in_owner_order(value, target):
    value = value.astype(target.dtype)
    n_c, n_z = target.shape[:2]
    n_x = target.shape[2] if len(target.shape) == 5 else 1
    depth = target.shape[-2]
    for pz in range(n_z):
        for px in range(n_x):
            for pc in range(n_c):
                start = ((pz * n_x + px) * n_c + pc) * depth
                if len(target.shape) == 5:
                    target[pc, pz, px] = value[start : start + depth]
                else:
                    target[pc, pz] = value[start : start + depth]


def project_kernel(transposed, with_grad, *refs):
    if with_grad:
        rows, weight, left, out, grad, parts, got, s_send, s_recv = refs
    else:
        rows, weight, out, parts, got, s_send, s_recv = refs
    (z, x, c, y), x_near, y_near, _ = around()
    diagonal = (z, 1 - x, c, 1 - y)
    barrier = pltpu.get_barrier_semaphore()
    for device in (x_near, y_near, diagonal):
        pl.semaphore_signal(barrier, inc=1, device_id=device, device_id_type=MESH)
    copies, finish = plane_sum(parts, got, out, s_send, s_recv)

    def work(px, py):
        times = outer if transposed else matmul
        parts[px, py] = times(rows[px, py], weight[...]).astype(jnp.bfloat16)

    work(1 - x, 1 - y)
    pl.semaphore_wait(barrier, 3)
    copies[2].start()
    work(1 - x, y)
    copies[0].start()
    work(x, 1 - y)
    copies[1].start()
    work(x, y)
    if with_grad:
        lane = 4 * out.shape[0]
        in_owner_order(inner(left[...].reshape(lane, -1), rows[...].reshape(lane, -1)), grad)
    finish()


def project(rows, weight, transposed, left, collective_id):
    n_x, n_y, own, depth = rows.shape
    n_z, _, n_c, _ = sizes()
    width = weight.shape[0] if transposed else weight.shape[1]
    low = jnp.bfloat16
    dma = pltpu.SemaphoreType.DMA
    return pl.pallas_call(
        functools.partial(project_kernel, transposed, left is not None),
        out_shape=(jax.ShapeDtypeStruct((own, width), jnp.float32),)
        + (
            ()
            if left is None
            else (
                jax.ShapeDtypeStruct(
                    (n_c, n_z, n_x, left.shape[3] // (n_z * n_x * n_c), depth), low
                ),
            )
        ),
        in_specs=[VMEM] * (2 if left is None else 3),
        out_specs=(VMEM,) * (1 if left is None else 2),
        scratch_shapes=[
            pltpu.VMEM((n_x, n_y, own, width), low), pltpu.VMEM((3, own, width), low), dma((3,)), dma((3,)),
        ],
        compiler_params=pltpu.CompilerParams(
            collective_id=collective_id, has_side_effects=True, vmem_limit_bytes=16 * MIB
        ),
        cost_estimate=pl.CostEstimate(
            flops=8 * own * width * depth, bytes_accessed=24 * MIB, transcendentals=0
        ),
    )(rows, weight, *(() if left is None else (left,)))


def gather_project_kernel(transposed, split, with_grad, own_rows, weight, *rest):
    if with_grad:
        left, wide, rest = rest[0], rest[1], (rest[0],) + rest[2:]
    else:
        wide, rest = rest[0], rest[1:]

    (z, x, c, y), x_near, y_near, _ = around()
    rest, (g_send, g_recv) = rest[:-2], rest[-2:]
    left, outs = (rest[0], rest[1:]) if with_grad else (None, rest)
    greet((x_near, y_near))
    wait_near, wait_x, wait_y, wait_diagonal, close = plane_gather(own_rows, wide, g_send, g_recv)
    wide[x, y] = own_rows[...]

    def work(px, py):
        times = outer if transposed else matmul
        value = times(wide[px, py], weight[...]).astype(jnp.bfloat16)
        start = 0
        for out, size in zip(outs, split):
            out[px, py] = value[:, start : start + size]
            start += size

    work(x, y)
    wait_near()
    wait_x()
    work(1 - x, y)
    wait_y()
    work(x, 1 - y)
    wait_diagonal()
    work(1 - x, 1 - y)
    if with_grad:
        lane = 4 * own_rows.shape[0]
        in_owner_order(inner(left[...], wide[...].reshape(lane, -1)), outs[-1])
    close()


def gather_project(own_rows, weight, transposed, split, left, collective_id):
    n_z, n_x, n_c, n_y = sizes()
    own, width = own_rows.shape
    depth = weight.shape[0] if transposed else weight.shape[1]
    dma = pltpu.SemaphoreType.DMA
    low = jnp.bfloat16
    return pl.pallas_call(
        functools.partial(gather_project_kernel, transposed, split, left is not None),
        out_shape=(
            jax.ShapeDtypeStruct((n_x, n_y, own, width), low),
        ) + tuple(jax.ShapeDtypeStruct((n_x, n_y, own, size), low) for size in split)
        + (
            ()
            if left is None
            else (jax.ShapeDtypeStruct((n_c, n_z, left.shape[1] // (n_z * n_c), width), low),)
        ),
        in_specs=[VMEM] * (2 if left is None else 3),
        out_specs=(VMEM,) * (1 + len(split) + (0 if left is None else 1)),
        scratch_shapes=[dma((6,)), dma((6,))],
        compiler_params=pltpu.CompilerParams(
            collective_id=collective_id, has_side_effects=True, vmem_limit_bytes=12 * MIB
        ),
        cost_estimate=pl.CostEstimate(
            flops=8 * own * width * depth, bytes_accessed=24 * MIB, transcendentals=0
        ),
    )(own_rows, weight, *(() if left is None else (left,)))


def merge_logs_kernel(source, out, got, mine, send_one, recv_one, send_two, recv_two):
    n_z, n_x, n_c, n_y = sizes()
    count = n_z * n_x * n_c * n_y
    z, x, c, y = place()
    me = ((z * n_x + x) * n_c + c) * n_y + y

    def device_of(index):
        return (
            index // (n_x * n_c * n_y), index // (n_c * n_y) % n_x, index // n_y % n_c, index % n_y
        )

    barrier = pltpu.get_barrier_semaphore()

    def call(step, unused):
        other = lax.rem(me + step, count)
        pl.semaphore_signal(barrier, inc=1, device_id=device_of(other), device_id_type=MESH)
        return unused

    lax.fori_loop(1, count, call, 0)
    got[me] = source[me]
    pl.semaphore_wait(barrier, count - 1)

    def first(step):
        other = lax.rem(me + step, count)
        return remote(
            source.at[other], got.at[me], send_one.at[step], recv_one.at[step], device_of(other)
        )

    def second(step):
        other = lax.rem(me + step, count)
        return remote(mine, out.at[me], send_two.at[step], recv_two.at[step], device_of(other))

    def each(action):
        def body(step, unused):
            action(step)
            return unused

        lax.fori_loop(1, count, body, 0)

    each(lambda step: first(step).start())
    each(lambda step: first(step).wait())
    values = got[...]
    peak = jnp.max(values, axis=0)
    mine[...] = peak + jnp.log(jnp.sum(jnp.exp(values - peak[None]), axis=0))
    out[me] = mine[...]
    each(lambda step: second(step).start())
    each(lambda step: second(step).wait())


def merge_logs(blocks, collective_id):
    count = blocks.shape[0]
    dma = pltpu.SemaphoreType.DMA
    return pl.pallas_call(
        merge_logs_kernel,
        out_shape=jax.ShapeDtypeStruct(blocks.shape, blocks.dtype),
        in_specs=[VMEM],
        out_specs=VMEM,
        scratch_shapes=[
            pltpu.VMEM(blocks.shape, blocks.dtype), pltpu.VMEM(blocks.shape[1:], blocks.dtype),
            dma((count,)), dma((count,)), dma((count,)), dma((count,)),
        ],
        cost_estimate=pl.CostEstimate(
            flops=0, bytes_accessed=42 * MIB, transcendentals=0
        ),
        compiler_params=pltpu.CompilerParams(collective_id=collective_id, has_side_effects=True),
    )(blocks)


def key_position(index, part, chunk):
    lane = 2 * chunk
    start = (part // 2) * (2 * lane) + (part % 2) * chunk
    return start + index + jnp.where(index >= chunk, chunk, 0)


def near_shown(side, chunk, query_pos, query_seg, near_pos, near_seg):
    columns = slice(side * chunk, (side + 1) * chunk)
    rows = slice(2 * side * chunk, 2 * (side + 1) * chunk)
    shown = (
        (near_seg[rows, :] == query_seg[:, columns])
        & (near_pos[rows, :] <= query_pos[:, columns])
        & (near_pos[rows, :] >= PROMPT)
    )
    return columns, rows, shown


def attend_kernel(
    chunk, query, far, near, query_pos, query_seg, near_pos, near_seg,
    out, out_low, log_total, scores, far_t, near_t,
):
    lane, feature = query.shape
    group = feature // HEAD_DIM
    prompt_rows = far.shape[0]
    parts = prompt_rows // lane
    query_t = (query[...].astype(jnp.float32) * HEAD_DIM ** (-0.5)).T.astype(jnp.bfloat16)
    far_t[...] = far[...].astype(jnp.float32).T.astype(jnp.bfloat16)
    near_t[...] = near[...].astype(jnp.float32).T.astype(jnp.bfloat16)
    row_of = lax.broadcasted_iota(jnp.int32, (feature, lane), 0)
    q_pos = query_pos[...]

    for head in range(group):
        low, high = head * HEAD_DIM, (head + 1) * HEAD_DIM
        query_h = jnp.where((row_of >= low) & (row_of < high), query_t, 0)

        def score_part(part, peak):
            block = far[pl.ds(pl.multiple_of(part * lane, lane), lane), :feature]
            value = matmul(block, query_h)
            index = lax.broadcasted_iota(jnp.int32, (lane, lane), 0)
            value = jnp.where(key_position(index, part, chunk) <= q_pos, value, MASKED)
            scores[pl.ds(pl.multiple_of(part * lane, lane), lane), :] = value
            return jnp.maximum(peak, jnp.max(value, axis=0, keepdims=True))

        peak = lax.fori_loop(0, parts, score_part, jnp.full((1, lane), MASKED, jnp.float32))
        near_peaks = []
        for side in range(2):
            columns, rows, shown = near_shown(side, chunk, query_pos, query_seg, near_pos, near_seg)
            value = matmul(near[rows, :feature], query_h[:, columns])
            value = jnp.where(shown, value, MASKED)
            scores[prompt_rows : prompt_rows + lane, columns] = value
            near_peaks.append(jnp.max(value, axis=0, keepdims=True))
        peak = jnp.maximum(peak, jnp.concatenate(near_peaks, axis=1))

        def weigh_part(part, state):
            total, mixed = state
            start = pl.multiple_of(part * lane, lane)
            chance = jnp.exp(scores[pl.ds(start, lane), :] - peak)
            total = total + jnp.sum(chance, axis=0, keepdims=True)
            mixed = mixed + matmul(
                far_t[feature + low : feature + high, pl.ds(start, lane)],
                chance.astype(jnp.bfloat16),
            )
            return total, mixed

        total, mixed = lax.fori_loop(
            0,
            parts,
            weigh_part,
            (jnp.zeros((1, lane), jnp.float32), jnp.zeros((HEAD_DIM, lane), jnp.float32)),
        )
        near_total, near_mixed = [], []
        for side in range(2):
            columns = slice(side * chunk, (side + 1) * chunk)
            rows = slice(side * lane, (side + 1) * lane)
            chance = jnp.exp(scores[prompt_rows : prompt_rows + lane, columns] - peak[:, columns])
            near_total.append(jnp.sum(chance, axis=0, keepdims=True))
            near_mixed.append(
                matmul(near_t[feature + low : feature + high, rows], chance.astype(jnp.bfloat16))
            )
        total = total + jnp.concatenate(near_total, axis=1)
        mixed = mixed + jnp.concatenate(near_mixed, axis=1)
        out[low:high, :] = mixed / total
        log_total[head : head + 1, :] = peak + jnp.log(total)
    out_low[...] = out[...].T.astype(jnp.bfloat16)


def attend(queries, far, near, places, chunk):
    lane, feature = queries.shape
    prompt_rows = far.shape[0]
    group = feature // HEAD_DIM
    total_rows = prompt_rows + lane
    return pl.pallas_call(
        functools.partial(attend_kernel, chunk),
        out_shape=(
            jax.ShapeDtypeStruct((feature, lane), jnp.float32),
            jax.ShapeDtypeStruct((lane, feature), jnp.bfloat16),
            jax.ShapeDtypeStruct((group, lane), jnp.float32),
        ),
        in_specs=[VMEM] * 7,
        out_specs=(VMEM,) * 3,
        scratch_shapes=[
            pltpu.VMEM((total_rows, lane), jnp.float32),
            pltpu.VMEM((2 * feature, prompt_rows), jnp.bfloat16),
            pltpu.VMEM((2 * feature, 2 * lane), jnp.bfloat16),
        ],
        compiler_params=pltpu.CompilerParams(vmem_limit_bytes=20 * MIB),
        cost_estimate=pl.CostEstimate(
            flops=8 * group * lane * total_rows * 128,
            bytes_accessed=8 * MIB,
            transcendentals=group * lane * total_rows,
        ),
    )(queries, far, near, *places)


def attend_back_kernel(
    chunk, query, far, near, query_pos, query_seg, near_pos, near_seg,
    log_total, mixed, answer, query_grad, far_grad, near_grad,
    far_t, near_t, far_values, near_values, far_sum, near_sum, query_sum,
):
    lane, feature = query.shape
    group = feature // HEAD_DIM
    prompt_rows = far.shape[0]
    parts = prompt_rows // lane
    scaled = (query[...].astype(jnp.float32) * HEAD_DIM ** (-0.5)).astype(jnp.bfloat16)
    query_t = scaled.astype(jnp.float32).T.astype(jnp.bfloat16)
    answers = answer[...]
    answer_t = answers.astype(jnp.float32).T.astype(jnp.bfloat16)
    far_t[...] = far[:, :feature].astype(jnp.float32).T.astype(jnp.bfloat16)
    near_t[...] = near[:, :feature].astype(jnp.float32).T.astype(jnp.bfloat16)
    far_values[...] = far[:, feature:]
    near_values[...] = near[:, feature:]
    row_of = lax.broadcasted_iota(jnp.int32, (feature, lane), 0)
    column_of = lax.broadcasted_iota(jnp.int32, (lane, feature), 1)
    q_pos = query_pos[...]

    for head in range(group):
        low, high = head * HEAD_DIM, (head + 1) * HEAD_DIM
        in_rows = (row_of >= low) & (row_of < high)
        in_columns = (column_of >= low) & (column_of < high)
        query_ht = jnp.where(in_rows, query_t, 0)
        answer_ht = jnp.where(in_rows, answer_t, 0)
        query_h = jnp.where(in_columns, scaled, 0)
        answer_h = jnp.where(in_columns, answers, 0)
        log_h = log_total[head : head + 1, :]
        delta_h = jnp.sum(
            answer_t[low:high, :].astype(jnp.float32) * mixed[low:high, :], axis=0, keepdims=True
        )

        def slopes(key_block, value_block, shown, columns):
            value = matmul(key_block, query_ht[:, columns])
            chance = jnp.exp(jnp.where(shown, value - log_h[:, columns], MASKED))
            slope = matmul(value_block, answer_ht[:, columns])
            change = (chance * (slope - delta_h[:, columns])).astype(jnp.bfloat16)
            chance = chance.astype(jnp.bfloat16)
            return change, matmul(change, query_h[columns]), matmul(chance, answer_h[columns])

        def add(sums, rows, key_part, value_part):
            if head == 0:
                sums[0, rows, :] = key_part
                sums[1, rows, :] = value_part
            else:
                sums[0, rows, :] += key_part
                sums[1, rows, :] += value_part

        def back_part(part, total):
            rows = pl.ds(pl.multiple_of(part * lane, lane), lane)
            index = lax.broadcasted_iota(jnp.int32, (lane, lane), 0)
            shown = key_position(index, part, chunk) <= q_pos
            change, key_part, value_part = slopes(
                far[rows, :feature], far_values[rows, :], shown, slice(0, lane)
            )
            add(far_sum, rows, key_part, value_part)
            return total + matmul(far_t[low:high, rows], change)

        total = lax.fori_loop(0, parts, back_part, jnp.zeros((HEAD_DIM, lane), jnp.float32))
        near_total = []
        for side in range(2):
            columns, rows, shown = near_shown(side, chunk, query_pos, query_seg, near_pos, near_seg)
            change, key_part, value_part = slopes(
                near[rows, :feature], near_values[rows, :], shown, columns
            )
            add(near_sum, rows, key_part, value_part)
            near_total.append(matmul(near_t[low:high, rows], change))
        query_sum[low:high, :] = (total + jnp.concatenate(near_total, axis=1)) * HEAD_DIM ** (-0.5)
    query_grad[...] = query_sum[...].T.astype(jnp.bfloat16)
    for sums, grad in ((far_sum, far_grad), (near_sum, near_grad)):
        grad[...] = jnp.concatenate(
            [sums[0].astype(jnp.bfloat16), sums[1].astype(jnp.bfloat16)], axis=1
        )


def attend_back(queries, far, near, places, log_total, mixed, answer, chunk):
    lane, feature = queries.shape
    prompt_rows = far.shape[0]
    group = feature // HEAD_DIM
    total_rows = prompt_rows + lane
    low = jnp.bfloat16
    return pl.pallas_call(
        functools.partial(attend_back_kernel, chunk),
        out_shape=(
            jax.ShapeDtypeStruct((lane, feature), low),
            jax.ShapeDtypeStruct((prompt_rows, 2 * feature), low),
            jax.ShapeDtypeStruct((2 * lane, 2 * feature), low),
        ),
        in_specs=[VMEM] * 10,
        out_specs=(VMEM,) * 3,
        scratch_shapes=[
            pltpu.VMEM((feature, prompt_rows), low),
            pltpu.VMEM((feature, 2 * lane), low),
            pltpu.VMEM((prompt_rows, feature), low),
            pltpu.VMEM((2 * lane, feature), low),
            pltpu.VMEM((2, prompt_rows, feature), jnp.float32),
            pltpu.VMEM((2, 2 * lane, feature), jnp.float32),
            pltpu.VMEM((feature, lane), jnp.float32),
        ],
        compiler_params=pltpu.CompilerParams(vmem_limit_bytes=28 * MIB),
        cost_estimate=pl.CostEstimate(
            flops=20 * group * lane * total_rows * 128,
            bytes_accessed=12 * MIB,
            transcendentals=group * lane * total_rows,
        ),
    )(queries, far, near, *places, log_total, mixed, answer)


def head_places(back):
    n_z, n_x, n_c, n_y = sizes()
    line = n_z * n_c
    pairs = []
    for device in range(line * n_x * n_y):
        group, at = device // line, device % line
        place_of = ((at // n_c * n_x + group // n_y) * n_c + at % n_c) * n_y + group % n_y
        pairs.append((place_of, device) if back else (device, place_of))
    return tuple(pairs)


def pad_rows(block):
    return jnp.pad(block, ((0, 8 - block.shape[0]), (0, 0)))


def adam_update(weight, moment_one, moment_two, gradient, step_rate, decay_rate):
    first_new = BETA_ONE * moment_one + (1.0 - BETA_ONE) * gradient
    second_new = BETA_TWO * moment_two + (1.0 - BETA_TWO) * gradient * gradient
    normalized = (
        first_new
        / (1.0 - BETA_ONE**STEP)
        / (jnp.sqrt(second_new / (1.0 - BETA_TWO**STEP)) + ADAM_EPS)
    )
    return (weight - step_rate * (normalized + decay_rate * weight), first_new, second_new)


def per_device(
    token_ids,
    targets,
    valid_mask,
    cont_lengths,
    routes,
    vocab_table,
    vocab_first,
    vocab_second,
    attn_weights,
    attn_first,
    attn_second,
    router,
    router_first,
    router_second,
    norm_gains,
    gains_first,
    gains_second,
    expert_up,
    up_first,
    up_second,
    expert_down,
    down_first,
    down_second,
):
    slabs = lax.axis_size("z")
    planes = lax.axis_size("x")
    cores = lax.axis_size("core")
    sides = lax.axis_size("head")
    groups = planes * sides
    z_at, x_at, core_at, side_at = (lax.axis_index(name) for name in ALL)
    blk_at = (z_at * planes + x_at) * cores + core_at
    device_at = blk_at * sides + side_at
    group_at = x_at * sides + side_at
    tokens = valid_mask.shape[0]
    chunk = token_ids.shape[0]
    own = chunk // sides
    lane = planes * chunk
    feature = D // groups
    wide = expert_up.shape[3] // planes
    shard_rows = vocab_table.shape[0]
    logit_scale = D ** (-0.5)

    cont_ends = jnp.cumsum(cont_lengths)
    valid_f = valid_mask.astype(jnp.float32)
    token_count = jnp.sum(valid_mask).astype(jnp.float32)
    expert_ids = jnp.arange(EXPERTS, dtype=jnp.int32)

    own_ints = jnp.concatenate([token_ids[None], targets[None], routes], axis=0)
    own_ints = lax.dynamic_slice_in_dim(own_ints, side_at * own, own, axis=1).astype(jnp.float32)
    rows_of = attn_weights.shape[1]
    smalls = jnp.concatenate(
        [router.transpose(0, 2, 1).reshape(LAYERS * EXPERTS, rows_of), norm_gains], axis=0
    )
    smalls = smalls.astype(jnp.bfloat16).astype(jnp.float32)
    smalls = jnp.pad(smalls, ((0, 16 - smalls.shape[0]), (0, own - rows_of)))
    whole_f = swap(jnp.concatenate([pad_rows(own_ints), smalls], axis=0)[None], True, 1)
    attn_low = attn_weights.astype(jnp.bfloat16)
    qkv_send = attn_low[:, :, : 3 * D].reshape(LAYERS, rows_of, 3, groups, feature)
    qkv_send = jnp.concatenate([qkv_send[:, :, 1:], qkv_send[:, :, :1]], axis=2)
    qkv_send = qkv_send.transpose(3, 0, 1, 2, 4).reshape(groups, LAYERS, rows_of, 3 * feature)
    qkv_got = lax.all_to_all(qkv_send, PLANE, split_axis=0, concat_axis=0, tiled=True)
    out_rows = lax.ppermute(attn_low[:, :, 3 * D :], ALL, head_places(False))
    expert_send = jnp.stack([expert_up, expert_down], axis=1).astype(jnp.bfloat16)
    depth = expert_send.shape[3]
    expert_send = expert_send.reshape(LAYERS, 2 * EXPERTS, depth, planes, wide)
    expert_send = expert_send.transpose(3, 0, 1, 2, 4)
    expert_halves = []
    for layer_index in range(LAYERS):
        kept_half = lax.dynamic_index_in_dim(expert_send[:, layer_index], x_at, 0, False)
        sent_half = lax.dynamic_index_in_dim(expert_send[:, layer_index], 1 - x_at, 0, False)
        got_half = lax.ppermute(sent_half, "x", ((0, 1), (1, 0)))
        expert_halves.append((kept_half, got_half))
    got_halves = [got_half for _, got_half in expert_halves]
    whole_f, qkv_got, out_rows, got_halves = lax.optimization_barrier(
        (whole_f, qkv_got, out_rows, got_halves)
    )
    expert_halves = [(kept_half, got) for (kept_half, _), got in zip(expert_halves, got_halves)]
    qkv_own = qkv_got.reshape(planes, sides, LAYERS, rows_of, 3 * feature).transpose(2, 0, 1, 3, 4)
    qkv_own = qkv_own.reshape(LAYERS, planes, sides * rows_of, 3 * feature)

    def gather_experts(kept_half, got_half):
        if depth % 16 == 0:
            return lax.all_gather(kept_half, LINE, axis=0).reshape(
                (slabs, cores) + kept_half.shape
            ), lax.all_gather(got_half, LINE, axis=0).reshape((slabs, cores) + kept_half.shape)
        halves = jnp.stack(
            [jnp.where(x_at == 0, kept_half, got_half), jnp.where(x_at == 0, got_half, kept_half)]
        )
        block = lax.all_gather(halves, LINE, axis=0)
        block = block.reshape(slabs, cores, planes, 2 * EXPERTS, depth, wide)
        block = block.transpose(3, 0, 2, 1, 4, 5).reshape(1, 1, 2 * EXPERTS, D, wide)
        return block, block

    expert_weights = [gather_experts(*expert_halves[0])]
    ints = whole_f.reshape(sizes() + whole_f.shape[1:])
    whole = whole_f[:, : 2 + LAYERS].astype(jnp.int32)
    smalls = whole_f[:, 8:, :rows_of].transpose(1, 0, 2).reshape(16, D)
    router_all = smalls[: LAYERS * EXPERTS].reshape(LAYERS, EXPERTS, D).transpose(0, 2, 1)
    router_all = router_all.astype(jnp.bfloat16)
    gains_f = smalls[LAYERS * EXPERTS :]
    routes_lane = lax.dynamic_index_in_dim(
        whole.reshape(slabs, planes, cores, sides, 2 + LAYERS, own), z_at, 0, False
    )
    routes_lane = lax.dynamic_index_in_dim(routes_lane, core_at, 1, False)[:, :, 2:]
    routes_lane = routes_lane.transpose(2, 0, 1, 3)[..., None]
    routes_own = lax.dynamic_slice_in_dim(routes, side_at * own, own, axis=1)

    extent = -(-shard_rows // 256) * 256
    table = jnp.pad(vocab_table.astype(jnp.bfloat16), ((0, extent - shard_rows), (0, 0)))
    offsets = jnp.arange(chunk, dtype=jnp.int32)
    first_blk = z_at * planes * cores + core_at
    query_pos = jnp.concatenate([(first_blk + cores * part) * chunk + offsets for part in range(planes)])
    near_blks = [first_blk - 1 + part for part in range(2 * planes)]
    near_pos = jnp.concatenate([blk * chunk + offsets for blk in near_blks])
    query_seg = segment_of(query_pos, cont_ends)
    near_seg = segment_of(near_pos, cont_ends)
    places = (query_pos[None, :], query_seg[None, :], near_pos[:, None], near_seg[:, None])

    stream, qkv_all, out_all = embed(table, ints, qkv_own, out_rows, own, shard_rows, 2)
    qkv_weights = [qkv_all[layer_index].reshape(D, 3 * feature) for layer_index in range(LAYERS)]
    out_weights = [out_all[layer_index].reshape(feature, D) for layer_index in range(LAYERS)]

    kept = []
    for layer_index in range(LAYERS):
        normed_lane, key_values, queries = gather_project(
            rms_norm(stream, gains_f[2 * layer_index]).astype(jnp.bfloat16),
            qkv_weights[layer_index], False, (2 * feature, feature), None, 3,
        )
        queries = queries.reshape(lane, feature)
        far, near = spread_keys(key_values.reshape(lane, 2 * feature), PROMPT, 10)
        if layer_index + 1 < LAYERS:
            far, halves = lax.optimization_barrier((far, expert_halves[layer_index + 1]))
            expert_weights.append(gather_experts(*halves))
        mixed_t, mixed_low, log_total = attend(queries, far, near, places, chunk)
        (attended,) = project(
            mixed_low.reshape(planes, sides, own, feature), out_weights[layer_index], False, None, 15
        )
        middle = stream + attended
        normed_two = rms_norm(middle, gains_f[2 * layer_index + 1]).astype(jnp.bfloat16)
        chance = jax.nn.softmax(matmul(normed_two, router_all[layer_index]), axis=-1)
        output, wide_rows, before, hidden = experts(
            normed_two, routes_lane[layer_index], expert_weights[layer_index], 11
        )
        own_pick = (routes_own[layer_index][:, None] == expert_ids[None, :]).astype(jnp.float32)
        gate = jnp.sum(chance * own_pick, axis=1, keepdims=True)
        kept.append(
            (
                stream, normed_lane, queries, far, near, mixed_t, mixed_low, log_total, middle,
                normed_two, chance, wide_rows, before, hidden, output, own_pick, gate,
            )
        )
        stream = middle + gate * output

    final_gain = gains_f[2 * LAYERS]
    devices = tokens // own
    valid_rows = valid_f.reshape(sizes() + (1, own))
    final_all, row_logs, hits = gather_logits(
        rms_norm(stream, final_gain).astype(jnp.bfloat16), table, ints, valid_rows, shard_rows, 4
    )
    log_sums = merge_logs(row_logs.reshape(devices, 1, own), 5)
    log_sum = log_sums.reshape(tokens)
    own_log = lax.dynamic_slice_in_dim(log_sum, device_at * own, own)
    own_valid = lax.dynamic_slice_in_dim(valid_f, device_at * own, own)
    own_loss = jnp.sum(own_log * own_valid) - jnp.sum(hits)
    final_grad, table_grad = vocab_back(
        final_all, table, ints, log_sums.reshape(sizes() + (1, own)), valid_rows / token_count,
        shard_rows, 6,
    )
    stream_grad, final_gain_grad = jax.vjp(rms_norm, stream, final_gain)[1](final_grad)

    qkv_packs = [None] * LAYERS
    out_packs = [None] * LAYERS
    router_list = [None] * LAYERS
    expert_sums = [None] * LAYERS
    gain_list = [None] * (2 * LAYERS + 1)
    gain_list[2 * LAYERS] = final_gain_grad
    for layer_index in reversed(range(LAYERS)):
        (
            stream, normed_lane, queries, far, near, mixed_t, mixed_low, log_total, middle,
            normed_two, chance, wide_rows, before, hidden, output, own_pick, gate,
        ) = kept[layer_index]
        out_grad = (gate * stream_grad).astype(jnp.bfloat16)
        chance_grad = jnp.sum(stream_grad * output, axis=1)[:, None] * own_pick
        choice_grad = chance * (chance_grad - jnp.sum(chance * chance_grad, axis=1, keepdims=True))
        router_list[layer_index] = jnp.dot(
            normed_two.astype(jnp.float32).T, choice_grad, precision=lax.Precision.HIGHEST
        )
        normed_grad = jnp.dot(
            choice_grad,
            router_all[layer_index].astype(jnp.float32).T,
            precision=lax.Precision.HIGHEST,
        )
        rows_grad, expert_grad = experts_back(
            out_grad, routes_lane[layer_index], expert_weights[layer_index], wide_rows, before,
            hidden, 12,
        )
        normed_grad = normed_grad + rows_grad
        middle_part, gain_list[2 * layer_index + 1] = jax.vjp(
            rms_norm, middle, gains_f[2 * layer_index + 1]
        )[1](normed_grad)
        middle_grad = stream_grad + middle_part
        _, answer, out_packs[layer_index] = gather_project(
            middle_grad.astype(jnp.bfloat16), out_weights[layer_index], True, (feature,), mixed_low, 16
        )
        answer = answer.reshape(lane, feature)
        query_grad, far_grad, near_grad = attend_back(
            queries, far, near, places, log_total, mixed_t, answer, chunk
        )
        qkv_grad = collect_keys(far_grad, near_grad, query_grad, 13)
        qkv_grad, expert_grad = lax.optimization_barrier((qkv_grad, expert_grad))
        expert_sums[layer_index] = lax.psum_scatter(
            expert_grad, LINE, scatter_dimension=0, tiled=True
        )[0]
        normed_att_grad, qkv_packs[layer_index] = project(
            qkv_grad.reshape(planes, sides, own, 3 * feature), qkv_weights[layer_index], True,
            normed_lane, 14,
        )
        stream_part, gain_list[2 * layer_index] = jax.vjp(
            rms_norm, stream, gains_f[2 * layer_index]
        )[1](normed_att_grad)
        stream_grad = middle_grad + stream_part

    small = jnp.concatenate(
        [jnp.stack(router_list).transpose(1, 0, 2).reshape(D, -1), jnp.stack(gain_list).T], axis=1
    )
    small = small.reshape(devices, rows_of, -1).transpose(0, 2, 1)
    small = jnp.pad(small, ((0, 0), (0, 16 - small.shape[1]), (0, 128 - rows_of)))
    table_share, small, table_squares, *attn_sums = embed_back(
        stream_grad.astype(jnp.bfloat16), ints, table_grad, small, qkv_packs + out_packs, shard_rows, 7
    )
    squares = sum(
        jnp.sum(jnp.square(part.astype(jnp.float32)))
        for part in [small[:, :rows_of]] + attn_sums + expert_sums
    ) + jnp.sum(table_squares)
    sums = jnp.pad(jnp.stack([squares, own_loss])[:, None], ((0, 6), (0, 127)))
    sums = jnp.sum(swap(sums[None], True, 9)[:, :2, 0], axis=0)
    square_total, loss_sum = sums[0], sums[1]
    expert_shares = []
    for expert_grad in expert_sums:
        kept_half = lax.dynamic_index_in_dim(expert_grad, x_at, 0, False)
        sent_half = lax.dynamic_index_in_dim(expert_grad, 1 - x_at, 0, False)
        got_half = lax.ppermute(sent_half, "x", ((0, 1), (1, 0)))
        expert_grad = jnp.concatenate(
            [jnp.where(x_at == 0, kept_half, got_half), jnp.where(x_at == 0, got_half, kept_half)],
            axis=-1,
        )
        expert_shares.append(
            expert_grad.reshape(2, EXPERTS, depth, planes * wide).astype(jnp.float32)
        )
    table_share, small = table_share[:shard_rows], small[:, :rows_of]
    router_share = (
        small[: LAYERS * EXPERTS].reshape(LAYERS, EXPERTS, rows_of).transpose(0, 2, 1)
    )
    gain_share = small[LAYERS * EXPERTS : LAYERS * EXPERTS + 2 * LAYERS + 1]
    qkv_share = jnp.stack(attn_sums[:LAYERS], axis=1).reshape(
        planes, LAYERS, sides, rows_of, 3 * feature
    )
    qkv_share = qkv_share.transpose(0, 2, 1, 3, 4).reshape(groups, LAYERS, rows_of, 3 * feature)
    qkv_share = lax.all_to_all(qkv_share, PLANE, split_axis=0, concat_axis=0, tiled=True)
    qkv_share = qkv_share.reshape(groups, LAYERS, rows_of, 3, feature)
    qkv_share = jnp.concatenate([qkv_share[:, :, :, 2:], qkv_share[:, :, :, :2]], axis=3)
    qkv_share = qkv_share.transpose(1, 2, 3, 0, 4).reshape(LAYERS, rows_of, 3 * D)
    out_share = lax.ppermute(jnp.stack(attn_sums[LAYERS:]), ALL, head_places(True))
    attn_share = jnp.concatenate([qkv_share, out_share], axis=2).astype(jnp.float32)
    up_share = jnp.stack([share[0] for share in expert_shares])
    down_share = jnp.stack([share[1] for share in expert_shares])
    shares = (table_share, attn_share, router_share, gain_share, up_share, down_share)
    grad_norm = jnp.sqrt(square_total)
    factor = CLIP_AT / jnp.maximum(grad_norm, CLIP_AT)
    weights = (vocab_table, attn_weights, router, norm_gains, expert_up, expert_down)
    firsts = (vocab_first, attn_first, router_first, gains_first, up_first, down_first)
    seconds = (vocab_second, attn_second, router_second, gains_second, up_second, down_second)
    results = [loss_sum, token_count, grad_norm]
    for number in range(6):
        results.extend(
            adam_update(
                weights[number],
                firsts[number],
                seconds[number],
                factor * shares[number],
                STEP_RATES[number],
                DECAY_RATES[number],
            )
        )
    return tuple(results)


def solution(mesh):
    blocks, sides = mesh.shape["blk"], mesh.shape["head"]
    fine = Mesh(mesh.devices.reshape(blocks // 4, 2, 2, sides), ALL)
    weight_specs = (
        (P(ALL, None),) * 3
        + (P(None, ALL, None),) * 3
        + (P(None, ALL, None),) * 3
        + (P(None, ALL),) * 3
        + (P(None, None, BLK, "head"),) * 6
    )
    return jax.shard_map(
        per_device,
        mesh=fine,
        in_specs=(P(BLK), P(BLK), P(), P(), P(None, BLK)) + weight_specs,
        out_specs=(P(), P(), P()) + weight_specs,
        check_vma=False,
    )
```

```python
import functools

import jax
import jax.numpy as jnp
from jax import lax
from jax.experimental import pallas as pl
from jax.experimental.pallas import tpu as pltpu
from jax.sharding import Mesh, PartitionSpec as P

D = 768
HEADS = 12
HEAD_DIM = 64
EXPERTS = 2
LAYERS = 2
PROMPT = 2048
STEP = 10

NORM_EPS = 1e-06
BETA_ONE = 0.9
BETA_TWO = 0.95
ADAM_EPS = 1e-08
CLIP_AT = 0.01
MASKED = -1e30
STEP_RATES = (2.0, 0.25, 0.04, 0.4, 0.04, 0.04)
DECAY_RATES = (0.01, 0.01, 0.01, 0.0, 0.01, 0.01)

ALL = ("z", "x", "core", "head")
BLK = ("z", "x", "core")
PLANE = ("x", "head")
LINE = ("z", "core")
MIB = 2**20
MESH = pl.DeviceIdType.MESH
ANY = pl.BlockSpec(memory_space=pl.ANY)
VMEM = pl.BlockSpec(memory_space=pltpu.VMEM)


def rms_norm(stream, gain):
    return stream * lax.rsqrt(jnp.mean(stream * stream, axis=-1, keepdims=True) + NORM_EPS) * gain


def segment_of(position, cont_ends):
    later = jnp.sum((cont_ends[None, :] <= (position - PROMPT)[:, None]).astype(jnp.int32), axis=1)
    return jnp.where(position < PROMPT, 0, 1 + later)


def place():
    return tuple(lax.axis_index(name) for name in ALL)


def sizes():
    return tuple(lax.axis_size(name) for name in ALL)


def remote(source, target, send, receive, device):
    return pltpu.make_async_remote_copy(
        src_ref=source, dst_ref=target, send_sem=send, recv_sem=receive,
        device_id=device, device_id_type=MESH,
    )


def greet(devices):
    barrier = pltpu.get_barrier_semaphore()
    for device in devices:
        pl.semaphore_signal(barrier, inc=1, device_id=device, device_id_type=MESH)
    pl.semaphore_wait(barrier, len(devices))


def around():
    z, x, c, y = place()
    return (z, x, c, y), (z, 1 - x, c, y), (z, x, c, 1 - y), (z, x, 1 - c, y)


def swap_kernel(broadcast, source, out, send_sem, receive_sem, own_sem):
    n_z, n_x, n_c, n_y = sizes()
    count = n_z * n_x * n_c * n_y
    z, x, c, y = place()
    me = ((z * n_x + x) * n_c + c) * n_y + y

    def device_of(index):
        return (
            index // (n_x * n_c * n_y), index // (n_c * n_y) % n_x, index // n_y % n_c, index % n_y
        )

    def taken(index):
        return source.at[0] if broadcast else source.at[index]

    barrier = pltpu.get_barrier_semaphore()

    def call(step, unused):
        other = lax.rem(me + step, count)
        pl.semaphore_signal(barrier, inc=1, device_id=device_of(other), device_id_type=MESH)
        return unused

    lax.fori_loop(1, count, call, 0)
    own = pltpu.make_async_copy(taken(me), out.at[me], own_sem)
    own.start()
    pl.semaphore_wait(barrier, count - 1)

    def copy(step):
        other = lax.rem(me + step, count)
        return remote(
            taken(other), out.at[me], send_sem.at[step], receive_sem.at[step], device_of(other)
        )

    def start(step, unused):
        copy(step).start()
        return unused

    def finish(step, unused):
        copy(step).wait()
        return unused

    lax.fori_loop(1, count, start, 0)
    lax.fori_loop(1, count, finish, 0)
    own.wait()


def swap(blocks, broadcast, collective_id):
    count = 1
    for size in sizes():
        count *= size
    return pl.pallas_call(
        functools.partial(swap_kernel, broadcast),
        out_shape=jax.ShapeDtypeStruct((count,) + blocks.shape[1:], blocks.dtype),
        in_specs=[VMEM],
        out_specs=VMEM,
        scratch_shapes=[
            pltpu.SemaphoreType.DMA((count,)),
            pltpu.SemaphoreType.DMA((count,)),
            pltpu.SemaphoreType.DMA,
        ],
        cost_estimate=pl.CostEstimate(
            flops=0, bytes_accessed=36 * MIB, transcendentals=0
        ),
        compiler_params=pltpu.CompilerParams(
            collective_id=collective_id, has_side_effects=True, vmem_limit_bytes=8 * MIB
        ),
    )(blocks)


def total_of(*parts):
    total = parts[0].astype(jnp.float32)
    for part in parts[1:]:
        total = total + part.astype(jnp.float32)
    return total


PIECES = 4


def spread_kernel(
    prompt_slabs, own_rows, far, near, tail, z_send, z_recv, c_send, c_recv, n_send, n_recv, own_sem
):
    n_z = lax.axis_size("z")
    lane = own_rows.shape[0]
    chunk = lane // 2
    size = lane // PIECES
    (z, x, c, y), _, _, c_near = around()
    above, below = (z + 1, x, c, y), (z - 1, x, c, y)
    in_prompt = z < prompt_slabs
    takes_down = z < prompt_slabs - 1
    gives_down = (z > 0) & (z < prompt_slabs)

    barrier = pltpu.get_barrier_semaphore()
    pl.semaphore_signal(barrier, inc=1, device_id=c_near, device_id_type=MESH)

    @pl.when(z > 0)
    def _():
        pl.semaphore_signal(barrier, inc=1, device_id=below, device_id_type=MESH)

    @pl.when(takes_down)
    def _():
        pl.semaphore_signal(barrier, inc=1, device_id=above, device_id_type=MESH)

    first, second = pl.ds(0, chunk), pl.ds(chunk, chunk)
    own = [
        pltpu.make_async_copy(own_rows.at[first], near.at[1], own_sem.at[0]),
        pltpu.make_async_copy(own_rows.at[second], near.at[3], own_sem.at[1]),
    ]
    own_far = pltpu.make_async_copy(own_rows, far.at[jnp.minimum(z, prompt_slabs - 1), c], own_sem.at[2])
    own_edge = pltpu.make_async_copy(own_rows.at[first], near.at[0], own_sem.at[3])
    edge = (z == 0) & (c == 0)
    for copy in own:
        copy.start()

    @pl.when(in_prompt)
    def _():
        own_far.start()

    @pl.when(edge)
    def _():
        own_edge.start()

    pl.semaphore_wait(
        barrier, 1 + jnp.where(z < n_z - 1, 1, 0) + jnp.where(gives_down, 1, 0)
    )

    def part(index):
        return pl.ds(index * size, size)

    def z_copy(source, slab, index, up):
        return remote(
            source, far.at[slab, c, part(index)], z_send.at[slab, index, 1 if up else 0],
            z_recv.at[slab, index], above if up else below,
        )

    def c_copy(source, slab, index):
        return remote(
            source, far.at[slab, c, part(index)], c_send.at[slab, index], c_recv.at[slab, index], c_near
        )

    def t_copy():
        return remote(own_rows.at[second], tail, n_send.at[0], n_recv.at[0], above)

    def t_hand():
        return remote(tail, near.at[0], n_send.at[1], n_recv.at[1], c_near)

    def n_copy(half):
        slot = jnp.where(c == 0, 2 * half, 2)
        return remote(
            own_rows.at[pl.ds(half * chunk, chunk)], near.at[slot], n_send.at[2 + half], n_recv.at[2 + half],
            c_near,
        )

    @pl.when(in_prompt)
    def _():
        for index in range(PIECES):
            source = own_rows.at[part(index)]

            @pl.when(z < n_z - 1)
            def _():
                z_copy(source, z, index, True).start()

            @pl.when(z > 0)
            def _():
                z_copy(source, z, index, False).start()

            c_copy(source, z, index).start()

    @pl.when((c == 1) & (z < n_z - 1))
    def _():
        t_copy().start()

    n_copy(0).start()

    @pl.when(c == 0)
    def _():
        n_copy(1).start()

    for distance in range(1, n_z):
        low_slab, high_slab = z - distance, z + distance
        for index in range(PIECES):

            @pl.when((low_slab >= 0) & (low_slab < prompt_slabs))
            def _():
                source = far.at[low_slab, c, part(index)]
                z_copy(source, low_slab, index, True).wait_recv()

                @pl.when(z < n_z - 1)
                def _():
                    z_copy(source, low_slab, index, True).start()

                c_copy(source, low_slab, index).start()

            if distance < prompt_slabs:

                @pl.when(high_slab < prompt_slabs)
                def _():
                    source = far.at[high_slab, c, part(index)]
                    z_copy(source, high_slab, index, False).wait_recv()

                    @pl.when(z > 0)
                    def _():
                        z_copy(source, high_slab, index, False).start()

                    c_copy(source, high_slab, index).start()

    @pl.when((c == 1) & (z > 0))
    def _():
        t_copy().wait_recv()
        t_hand().start()
        t_hand().wait_send()

    @pl.when((c == 1) & (z < n_z - 1))
    def _():
        t_copy().wait_send()

    @pl.when((c == 0) & (z > 0))
    def _():
        t_hand().wait_recv()

    n_copy(0).wait_send()
    n_copy(0).wait_recv()

    @pl.when(c == 0)
    def _():
        n_copy(1).wait_send()

    @pl.when(c == 1)
    def _():
        n_copy(1).wait_recv()

    for slab in range(prompt_slabs):
        for index in range(PIECES):
            copy = c_copy(own_rows.at[part(index)], slab, index)
            copy.wait_send()
            copy.wait_recv()

            @pl.when((z < n_z - 1) & (slab <= z))
            def _():
                z_copy(own_rows.at[part(index)], slab, index, True).wait_send()

            @pl.when((z > 0) & (slab >= z))
            def _():
                z_copy(own_rows.at[part(index)], slab, index, False).wait_send()

    for copy in own:
        copy.wait()

    @pl.when(in_prompt)
    def _():
        own_far.wait()

    @pl.when(edge)
    def _():
        own_edge.wait()


def spread_keys(own_rows, prompt_rows, collective_id):
    lane, width = own_rows.shape
    slabs = prompt_rows // (2 * lane)
    dma = pltpu.SemaphoreType.DMA
    far, near, _ = pl.pallas_call(
        functools.partial(spread_kernel, slabs),
        out_shape=(
            jax.ShapeDtypeStruct((slabs, 2, lane, width), own_rows.dtype),
            jax.ShapeDtypeStruct((4, lane // 2, width), own_rows.dtype),
            jax.ShapeDtypeStruct((lane // 2, width), own_rows.dtype),
        ),
        in_specs=[VMEM],
        out_specs=(VMEM,) * 3,
        scratch_shapes=[
            dma((slabs, PIECES, 2)), dma((slabs, PIECES)), dma((slabs, PIECES)), dma((slabs, PIECES)),
            dma((4,)), dma((4,)), dma((4,)),
        ],
        cost_estimate=pl.CostEstimate(
            flops=0, bytes_accessed=60 * MIB, transcendentals=0
        ),
        compiler_params=pltpu.CompilerParams(
            collective_id=collective_id, has_side_effects=True, vmem_limit_bytes=12 * MIB
        ),
    )(own_rows)
    return far.reshape(prompt_rows, width), near.reshape(2 * lane, width)


def collect_kernel(
    prompt_slabs, far, near, query_grad, whole, out, own, c_got, z_got, n_got, tail_pass, tail_got,
    c_send, c_recv, z_send, z_recv, n_send, n_recv,
):
    n_z = lax.axis_size("z")
    lane = out.shape[0]
    chunk = lane // 2
    size = lane // PIECES
    (z, x, c, y), _, _, c_near = around()
    above, below = (z + 1, x, c, y), (z - 1, x, c, y)

    barrier = pltpu.get_barrier_semaphore()
    pl.semaphore_signal(barrier, inc=1, device_id=c_near, device_id_type=MESH)

    @pl.when(z < n_z - 1)
    def _():
        pl.semaphore_signal(barrier, inc=1, device_id=above, device_id_type=MESH)

    pl.semaphore_wait(barrier, 1 + jnp.where(z > 0, 1, 0))

    def part(index):
        return pl.ds(index * size, size)

    def c_copy(slab, index):
        return remote(
            far.at[slab, 1 - c, part(index)], c_got.at[slab, part(index)], c_send.at[slab, index],
            c_recv.at[slab, index], c_near,
        )

    def z_copy(slab, index):
        return remote(
            own.at[slab, part(index)], z_got.at[slab, part(index)], z_send.at[slab, index],
            z_recv.at[slab, index], below,
        )

    def n_copy(half):
        slot = jnp.where(c == 0, 2, 2 * half)
        return remote(near.at[slot], n_got.at[half], n_send.at[half], n_recv.at[half], c_near)

    def t_hand():
        return remote(near.at[0], tail_pass, n_send.at[2], n_recv.at[2], c_near)

    def t_copy():
        return remote(tail_pass, tail_got, n_send.at[3], n_recv.at[3], below)

    for slab in range(prompt_slabs):
        for index in range(PIECES):
            c_copy(slab, index).start()
    n_copy(0).start()

    @pl.when(c == 1)
    def _():
        n_copy(1).start()

    @pl.when((c == 0) & (z > 0))
    def _():
        t_hand().start()

    for slab in range(prompt_slabs):
        for index in range(PIECES):
            c_copy(slab, index).wait_recv()
            rows = part(index)
            mine = total_of(far[slab, c, rows, :], c_got[slab, rows, :])

            @pl.when((z == n_z - 1) & (z > slab))
            def _():
                own[slab, rows, :] = mine.astype(jnp.bfloat16)
                z_copy(slab, index).start()

            @pl.when((z < n_z - 1) & (z > slab))
            def _():
                z_copy(slab, index).wait_recv()
                own[slab, rows, :] = total_of(mine, z_got[slab, rows, :]).astype(jnp.bfloat16)
                z_copy(slab, index).start()

            @pl.when((z < n_z - 1) & (z == slab))
            def _():
                z_copy(slab, index).wait_recv()
                out[rows, :] = total_of(mine, z_got[slab, rows, :])

            @pl.when((z == n_z - 1) & (z == slab))
            def _():
                out[rows, :] = mine

    @pl.when((c == 1) & (z > 0))
    def _():
        t_hand().wait_recv()
        t_copy().start()

    @pl.when(z >= prompt_slabs)
    def _():
        out[...] = jnp.zeros_like(out)

    n_copy(0).wait_recv()
    first, second = pl.ds(0, chunk), pl.ds(chunk, chunk)
    out[first, :] += total_of(near[1], n_got[0])
    out[second, :] += near[3].astype(jnp.float32)

    @pl.when(c == 0)
    def _():
        n_copy(1).wait_recv()
        out[second, :] += n_got[1].astype(jnp.float32)

    @pl.when((c == 1) & (z < n_z - 1))
    def _():
        t_copy().wait_recv()
        out[second, :] += tail_got[...].astype(jnp.float32)

    whole[...] = jnp.concatenate([out[...].astype(jnp.bfloat16), query_grad[...]], axis=1)

    @pl.when((c == 1) & (z > 0))
    def _():
        t_copy().wait_send()

    @pl.when((c == 0) & (z > 0))
    def _():
        t_hand().wait_send()

    n_copy(0).wait_send()

    @pl.when(c == 1)
    def _():
        n_copy(1).wait_send()

    for slab in range(prompt_slabs):
        for index in range(PIECES):
            c_copy(slab, index).wait_send()

            @pl.when(z > slab)
            def _():
                z_copy(slab, index).wait_send()


def collect_keys(far, near, query_grad, collective_id):
    prompt_rows, width = far.shape
    lane = near.shape[0] // 2
    slabs = prompt_rows // (2 * lane)
    dma = pltpu.SemaphoreType.DMA
    low = jnp.bfloat16
    return pl.pallas_call(
        functools.partial(collect_kernel, slabs),
        out_shape=jax.ShapeDtypeStruct((lane, width + query_grad.shape[1]), low),
        in_specs=[VMEM] * 3,
        out_specs=VMEM,
        scratch_shapes=[
            pltpu.VMEM((lane, width), jnp.float32),
            pltpu.VMEM((slabs, lane, width), low),
            pltpu.VMEM((slabs, lane, width), low),
            pltpu.VMEM((slabs, lane, width), low),
            pltpu.VMEM((2, lane // 2, width), low),
            pltpu.VMEM((lane // 2, width), low),
            pltpu.VMEM((lane // 2, width), low),
            dma((slabs, PIECES)), dma((slabs, PIECES)), dma((slabs, PIECES)), dma((slabs, PIECES)),
            dma((4,)), dma((4,)),
        ],
        cost_estimate=pl.CostEstimate(
            flops=0, bytes_accessed=60 * MIB, transcendentals=0
        ),
        compiler_params=pltpu.CompilerParams(
            collective_id=collective_id, has_side_effects=True, vmem_limit_bytes=20 * MIB
        ),
    )(far.astype(low).reshape(slabs, 2, lane, width), near.astype(low).reshape(4, lane // 2, width), query_grad)


def greet_all():
    n_z, n_x, n_c, n_y = sizes()
    count = n_z * n_x * n_c * n_y
    barrier = pltpu.get_barrier_semaphore()

    def call(step, unused):
        pl.semaphore_signal(barrier, inc=1, device_id=device_after(step), device_id_type=MESH)
        return unused

    lax.fori_loop(1, count, call, 0)
    pl.semaphore_wait(barrier, count - 1)


def index_after(step):
    n_z, n_x, n_c, n_y = sizes()
    z, x, c, y = place()
    me = ((z * n_x + x) * n_c + c) * n_y + y
    return lax.rem(me + step, n_z * n_x * n_c * n_y)


def device_after(step):
    _, n_x, n_c, n_y = sizes()
    index = index_after(step)
    return (
        index // (n_x * n_c * n_y), index // (n_c * n_y) % n_x, index // n_y % n_c, index % n_y
    )


def greet_near():
    n_z = lax.axis_size("z")
    (z, x, c, y), x_near, y_near, c_near = around()
    barrier = pltpu.get_barrier_semaphore()
    for device in (x_near, y_near, c_near):
        pl.semaphore_signal(barrier, inc=1, device_id=device, device_id_type=MESH)

    @pl.when(z > 0)
    def _():
        pl.semaphore_signal(barrier, inc=1, device_id=(z - 1, x, c, y), device_id_type=MESH)

    @pl.when(z < n_z - 1)
    def _():
        pl.semaphore_signal(barrier, inc=1, device_id=(z + 1, x, c, y), device_id_type=MESH)

    pl.semaphore_wait(barrier, 3 + jnp.where(z > 0, 1, 0) + jnp.where(z < n_z - 1, 1, 0))


Z_PIECES = 4


def gather_sems():
    n_z = lax.axis_size("z")
    dma = pltpu.SemaphoreType.DMA
    return [
        dma((n_z, Z_PIECES, 2)), dma((n_z, Z_PIECES)), dma((n_z, 2)), dma((n_z, 2)), dma((n_z, 2)),
        dma((n_z, 2)), dma((n_z, 4)), dma((n_z, 4)), dma,
    ]


def gather_slabs(rows_in, out, sems, work, beside=lambda step: None):
    z_send, z_recv, x_send, x_recv, y_send, y_recv, c_send, c_recv, own_sem = sems
    n_z = lax.axis_size("z")
    half = rows_in.shape[0] // 2
    size = rows_in.shape[0] // Z_PIECES
    (z, x, c, y), x_near, y_near, c_near = around()
    low, high = pl.ds(0, half), pl.ds(half, half)
    everything = pl.ds(0, 2 * half)
    own = pltpu.make_async_copy(rows_in, out.at[z, x, c, y], own_sem)
    own.start()

    def block(origin, px, py, rows):
        return out.at[origin, px, c, py, rows]

    def z_copy(source, origin, index, up):
        rows = pl.ds(index * size, size)
        other = (z + 1, x, c, y) if up else (z - 1, x, c, y)
        return remote(
            source.at[rows], block(origin, x, y, rows), z_send.at[origin, index, 1 if up else 0],
            z_recv.at[origin, index], other,
        )

    def x_copy(source, origin):
        return remote(source, out.at[origin, x, c, y], x_send.at[origin, 0], x_recv.at[origin, 0], x_near)

    def y_copy(source, origin):
        return remote(source, out.at[origin, x, c, y], y_send.at[origin, 0], y_recv.at[origin, 0], y_near)

    def x_relay(origin):
        part = block(origin, x, 1 - y, high)
        return remote(part, part, x_send.at[origin, 1], x_recv.at[origin, 1], x_near)

    def y_relay(origin):
        part = block(origin, 1 - x, y, low)
        return remote(part, part, y_send.at[origin, 1], y_recv.at[origin, 1], y_near)

    def c_copy(source, origin, px, py):
        slot = px * 2 + py
        return remote(
            source, out.at[origin, px, c, py], c_send.at[origin, slot], c_recv.at[origin, slot], c_near
        )

    def column(origin):
        return out.at[origin, x, c, y]

    def spread(source, origin):
        x_copy(source, origin).start()
        y_copy(source, origin).start()
        c_copy(source, origin, x, y).start()

    def relay(origin):
        x_copy(column(origin), origin).wait_recv()
        y_relay(origin).start()
        y_copy(column(origin), origin).wait_recv()
        x_relay(origin).start()
        c_copy(block(origin, 1 - x, y, everything), origin, 1 - x, y).start()
        c_copy(block(origin, x, 1 - y, everything), origin, x, 1 - y).start()

    def finish(origin):
        x_relay(origin).wait_recv()
        y_relay(origin).wait_recv()
        c_copy(block(origin, 1 - x, 1 - y, everything), origin, 1 - x, 1 - y).start()

    def use(origin):
        for px in range(2):
            for py in range(2):
                c_copy(out.at[origin, px, c, py], origin, px, py).wait_recv()
        work(origin)

    def arrive(step):
        below, above = z - step, z + step

        @pl.when(below >= 0)
        def _():
            for index in range(Z_PIECES):
                z_copy(rows_in, below, index, True).wait_recv()

                @pl.when(z < n_z - 1)
                def _():
                    z_copy(column(below), below, index, True).start()

            spread(column(below), below)

        @pl.when(above < n_z)
        def _():
            for index in range(Z_PIECES):
                z_copy(rows_in, above, index, False).wait_recv()

                @pl.when(z > 0)
                def _():
                    z_copy(column(above), above, index, False).start()

            spread(column(above), above)

    for index in range(Z_PIECES):

        @pl.when(z < n_z - 1)
        def _():
            z_copy(rows_in, z, index, True).start()

        @pl.when(z > 0)
        def _():
            z_copy(rows_in, z, index, False).start()

    spread(rows_in, z)
    for step in range(1, n_z + 3):
        if step < n_z:
            arrive(step)
        for action, back in ((relay, 1), (finish, 2), (use, 3)):
            late = step - back
            if late == 0:
                if action is use:
                    own.wait()
                action(z)
            elif 0 < late < n_z:
                for origin in (z - late, z + late):

                    @pl.when((origin >= 0) & (origin < n_z))
                    def _():
                        action(origin)

        beside(step)

    def close(origin, unused):
        x_copy(rows_in, origin).wait_send()
        y_copy(rows_in, origin).wait_send()
        x_relay(origin).wait_send()
        y_relay(origin).wait_send()
        for px in range(2):
            for py in range(2):
                c_copy(out.at[origin, px, c, py], origin, px, py).wait_send()
        for index in range(Z_PIECES):

            @pl.when((z < n_z - 1) & (origin <= z))
            def _():
                z_copy(rows_in, origin, index, True).wait_send()

            @pl.when((z > 0) & (origin >= z))
            def _():
                z_copy(rows_in, origin, index, False).wait_send()

        return unused

    lax.fori_loop(0, n_z, close, 0)


def line_gather_sems():
    n_z = lax.axis_size("z")
    dma = pltpu.SemaphoreType.DMA
    return [dma((n_z, 2, 2)), dma((n_z, 2)), dma((n_z, 2)), dma((n_z, 2)), dma((2,))]


def line_gather(own_parts, all_parts, sems):
    z_send, z_recv, c_send, c_recv, own_sem = sems
    n_z = lax.axis_size("z")
    (z, x, c, y), _, _, c_near = around()
    numbers = range(len(own_parts))

    def z_copy(source, number, origin, up):
        return remote(
            source, all_parts[number](origin, c), z_send.at[origin, number, 1 if up else 0],
            z_recv.at[origin, number], (z + 1, x, c, y) if up else (z - 1, x, c, y),
        )

    def c_copy(source, number, origin):
        return remote(
            source, all_parts[number](origin, c), c_send.at[origin, number], c_recv.at[origin, number], c_near
        )

    own = [
        pltpu.make_async_copy(own_parts[number], all_parts[number](z, c), own_sem.at[number])
        for number in numbers
    ]
    for copy in own:
        copy.start()
    for number in numbers:
        source = own_parts[number]

        @pl.when(z < n_z - 1)
        def _():
            z_copy(source, number, z, True).start()

        @pl.when(z > 0)
        def _():
            z_copy(source, number, z, False).start()

        c_copy(source, number, z).start()

    def beside(step):
        below, above = z - step, z + step

        @pl.when((step >= 1) & (below >= 0))
        def _():
            for number in numbers:
                source = all_parts[number](below, c)
                z_copy(source, number, below, True).wait_recv()

                @pl.when(z < n_z - 1)
                def _():
                    z_copy(source, number, below, True).start()

                c_copy(source, number, below).start()

        @pl.when((step >= 1) & (above < n_z))
        def _():
            for number in numbers:
                source = all_parts[number](above, c)
                z_copy(source, number, above, False).wait_recv()

                @pl.when(z > 0)
                def _():
                    z_copy(source, number, above, False).start()

                c_copy(source, number, above).start()

    def close():
        for copy in own:
            copy.wait()

        def one(origin, unused):
            for number in numbers:
                c_copy(own_parts[number], number, origin).wait()

                @pl.when((z < n_z - 1) & (origin <= z))
                def _():
                    z_copy(own_parts[number], number, origin, True).wait_send()

                @pl.when((z > 0) & (origin >= z))
                def _():
                    z_copy(own_parts[number], number, origin, False).wait_send()

            return unused

        lax.fori_loop(0, n_z, one, 0)

    return beside, close


def line_sems(parts):
    n_z = lax.axis_size("z")
    dma = pltpu.SemaphoreType.DMA
    return [dma((parts,)), dma((parts,)), dma((n_z, 2, parts)), dma((n_z, 2, parts))]


def line_sums(packs, outs, buffers, sems):
    c_send, c_recv, z_send, z_recv = sems
    n_z = lax.axis_size("z")
    (z, x, c, y), _, _, c_near = around()
    numbers = range(len(packs))
    lanes, got, below, above = (buffers[each :: 4] for each in range(4))
    handed = [
        remote(packs[each].at[1 - c], got[each], c_send.at[each], c_recv.at[each], c_near)
        for each in numbers
    ]

    def z_copy(slab, up, each):
        return remote(
            lanes[each].at[slab], (below if up else above)[each].at[slab],
            z_send.at[slab, 1 if up else 0, each], z_recv.at[slab, 1 if up else 0, each],
            (z + 1, x, c, y) if up else (z - 1, x, c, y),
        )

    for copy in handed:
        copy.start()

    def merge():
        for each in numbers:
            handed[each].wait()
            lanes[each][...] = total_of(packs[each][c], got[each][...]).astype(jnp.bfloat16)

    def hop(turn, step):
        high, low = n_z - 1 - turn, turn

        @pl.when((z == step - 1 - turn) & (z < high))
        def _():
            for each in numbers:

                @pl.when(z > 0)
                def _():
                    z_copy(high, True, each).wait_recv()
                    lanes[each][high] = total_of(lanes[each][high], below[each][high]).astype(jnp.bfloat16)

                z_copy(high, True, each).start()

        @pl.when((n_z - 1 - z == step - 1 - turn) & (z > low))
        def _():
            for each in numbers:

                @pl.when(z < n_z - 1)
                def _():
                    z_copy(low, False, each).wait_recv()
                    lanes[each][low] = total_of(lanes[each][low], above[each][low]).astype(jnp.bfloat16)

                z_copy(low, False, each).start()

    def beside(step):
        if step == 1:
            merge()
        if step < n_z:

            def body(turn, unused):
                hop(turn, step)
                return unused

            lax.fori_loop(0, n_z - 1, body, 0)

    def close():
        for each in numbers:
            out = outs[each]
            out[...] = lanes[each][z].astype(jnp.float32)

            @pl.when(z > 0)
            def _():
                z_copy(z, True, each).wait_recv()
                out[...] += below[each][z].astype(jnp.float32)

            @pl.when(z < n_z - 1)
            def _():
                z_copy(z, False, each).wait_recv()
                out[...] += above[each][z].astype(jnp.float32)

        def sent(slab, unused):
            for each in numbers:

                @pl.when(slab > z)
                def _():
                    z_copy(slab, True, each).wait_send()

                @pl.when(slab < z)
                def _():
                    z_copy(slab, False, each).wait_send()

            return unused

        lax.fori_loop(0, n_z, sent, 0)

    return beside, close


def in_pairs(values, slab, px, pc, row):
    return jnp.concatenate([values[slab, px, pc, py, row : row + 1, :] for py in range(2)], axis=1)


def vocab_ids(extent, chunk, shard_rows):
    n_z, n_x, n_c, n_y = sizes()
    z, x, c, y = place()
    me = ((z * n_x + x) * n_c + c) * n_y + y
    rows = lax.broadcasted_iota(jnp.int32, (extent, chunk), 0)
    return rows + me * shard_rows


def logits_kernel(shard_rows, rows_in, table, ints, valid, out, logs, hits, *sems):
    extent = table.shape[0]
    chunk = 2 * rows_in.shape[0]
    scale = table.shape[1] ** (-0.5)
    greet_near()
    hits[...] = jnp.zeros_like(hits)

    def work(slab):
        def one(index, unused):
            px, pc = index // 2, index % 2
            rows = out[slab, px, pc].reshape(chunk, -1)
            value = outer(table[...], rows) * scale
            ids = vocab_ids(extent, chunk, shard_rows)
            inside = lax.broadcasted_iota(jnp.int32, (extent, chunk), 0) < shard_rows
            target = in_pairs(ints, slab, px, pc, 1).astype(jnp.int32)
            shown = in_pairs(valid, slab, px, pc, 0)
            hit = jnp.where(ids == target, value, 0.0)
            hits[...] += jnp.sum(hit, axis=0, keepdims=True) * shown
            value = jnp.where(inside, value, MASKED)
            peak = jnp.max(value, axis=0, keepdims=True)
            log = peak + jnp.log(jnp.sum(jnp.exp(value - peak), axis=0, keepdims=True))
            half = chunk // 2
            logs[slab, px, pc, 0] = log[:, :half]
            logs[slab, px, pc, 1] = log[:, half:]
            return unused

        lax.fori_loop(0, 4, one, 0)

    gather_slabs(rows_in, out, sems, work)


def gather_logits(rows, table, ints, valid, shard_rows, collective_id):
    own, width = rows.shape
    shape = sizes() + (own, width)
    return pl.pallas_call(
        functools.partial(logits_kernel, shard_rows),
        out_shape=(
            jax.ShapeDtypeStruct(shape, rows.dtype),
            jax.ShapeDtypeStruct(sizes() + (1, own), jnp.float32),
            jax.ShapeDtypeStruct((1, 2 * own), jnp.float32),
        ),
        in_specs=[VMEM] * 4,
        out_specs=(VMEM,) * 3,
        scratch_shapes=gather_sems(),
        cost_estimate=pl.CostEstimate(
            flops=0, bytes_accessed=108 * MIB, transcendentals=0
        ),
        compiler_params=pltpu.CompilerParams(
            collective_id=collective_id, has_side_effects=True,
            vmem_limit_bytes=lax.axis_size("z") * 2 * MIB + 20 * MIB,
        ),
    )(rows, table, ints, valid)


def embed_back_kernel(shard_rows, parts, rows_in, ints, table_grad, smalls, *refs):
    packs, refs = refs[:parts], refs[parts:]
    out, small_sum, squares, refs = refs[0], refs[1], refs[2], refs[3:]
    pack_sums, refs = refs[:parts], refs[parts:]
    slabs, small_got, refs = refs[0], refs[1], refs[2:]
    buffers, sems = refs[: 4 * parts], refs[4 * parts :]
    extent = out.shape[0]
    chunk = 2 * rows_in.shape[0]
    small_send, small_recv = sems[-6:-4]
    n_z, n_x, n_c, n_y = sizes()
    count = n_z * n_x * n_c * n_y
    me = index_after(0)
    greet_all()

    def small(step):
        return remote(
            smalls.at[index_after(step)], small_got.at[me], small_send.at[step], small_recv.at[step],
            device_after(step),
        )

    def each(action):
        def body(step, unused):
            action(step)
            return unused

        lax.fori_loop(1, count, body, 0)

    each(lambda step: small(step).start())
    beside, close_line = line_sums(packs, pack_sums, buffers, sems[-4:])
    small_got[me] = smalls[me]
    out[...] = table_grad[...]

    def work(slab):
        def one(index, unused):
            px, pc = index // 2, index % 2
            token = in_pairs(ints, slab, px, pc, 0).astype(jnp.int32)
            hot = vocab_ids(extent, chunk, shard_rows) == token
            hot = jnp.where(hot, 1.0, 0.0).astype(jnp.bfloat16)
            out[...] += matmul(hot, slabs[slab, px, pc].reshape(chunk, -1))
            return unused

        lax.fori_loop(0, 4, one, 0)

    gather_slabs(rows_in, slabs, sems[:-6], work, beside)
    close_line()
    each(lambda step: small(step).wait())
    small_sum[...] = jnp.sum(small_got[...], axis=0)
    value = out[...]
    inside = lax.broadcasted_iota(jnp.int32, value.shape, 0) < shard_rows
    squares[...] = jnp.sum(jnp.where(inside, value * value, 0.0), axis=0, keepdims=True)
    for part in pack_sums:
        value = part[...].reshape(-1, part.shape[-1])
        squares[:, : part.shape[-1]] += jnp.sum(value * value, axis=0, keepdims=True)


def embed_back(rows, ints, table_grad, smalls, packs, shard_rows, collective_id):
    own, width = rows.shape
    count = smalls.shape[0]
    dma = pltpu.SemaphoreType.DMA
    return pl.pallas_call(
        functools.partial(embed_back_kernel, shard_rows, len(packs)),
        out_shape=(
            jax.ShapeDtypeStruct(table_grad.shape, jnp.float32),
            jax.ShapeDtypeStruct(smalls.shape[1:], jnp.float32),
            jax.ShapeDtypeStruct((1, width), jnp.float32),
        )
        + tuple(jax.ShapeDtypeStruct(pack.shape[2:], jnp.float32) for pack in packs),
        in_specs=[VMEM] * (4 + len(packs)),
        out_specs=(VMEM,) * (3 + len(packs)),
        scratch_shapes=[
            pltpu.VMEM(sizes() + (own, width), rows.dtype), pltpu.VMEM(smalls.shape, jnp.float32),
        ]
        + [pltpu.VMEM(pack.shape[1:], pack.dtype) for pack in packs for _ in range(4)]
        + gather_sems() + [dma((count,)), dma((count,))] + line_sems(len(packs)),
        cost_estimate=pl.CostEstimate(
            flops=0, bytes_accessed=120 * MIB, transcendentals=0
        ),
        compiler_params=pltpu.CompilerParams(
            collective_id=collective_id, has_side_effects=True,
            vmem_limit_bytes=lax.axis_size("z") * 2 * MIB + 28 * MIB,
        ),
    )(rows, ints, table_grad, smalls, *packs)


def slab_order():
    n_z = lax.axis_size("z")
    z = lax.axis_index("z")
    up, down = n_z - 1 - z, z
    longer, shorter = jnp.maximum(up, down), jnp.minimum(up, down)
    far_side = jnp.where(up >= down, 1, -1)

    def target(step):
        late = step - (longer - shorter)
        near_side = jnp.where(late % 2 == 0, far_side, -far_side)
        return jnp.where(
            late < 0, z + far_side * (longer - step), z + near_side * (shorter - late // 2)
        )

    return target


def scatter_scratch(rows, width):
    n_z, n_x, n_c, n_y = sizes()
    half = rows // 2
    low = jnp.bfloat16
    dma = pltpu.SemaphoreType.DMA
    return [
        pltpu.VMEM((n_z, n_x, n_y, rows, width), low),
        pltpu.VMEM((n_z, n_x, n_y, rows, width), low),
        pltpu.VMEM((n_z, n_x, n_y, rows, width), low),
        pltpu.VMEM((n_z, 2, half, width), low),
        pltpu.VMEM((n_z, 2, half, width), low),
        pltpu.VMEM((n_z, half, width), low),
        pltpu.VMEM((n_z, half, width), low),
        pltpu.VMEM((n_z, rows, width), low),
        pltpu.VMEM((n_z, rows, width), low),
        dma((n_z, 2)), dma((n_z, 2)), dma((n_z, 3)), dma((n_z, 3)), dma((n_z, 3)),
        dma((n_z, 3)), dma((n_z, 2)), dma((n_z, 2, 2)),
    ]


def scatter_slabs(out, scratch, before, make, after, beside=lambda step: None):
    (
        lanes, handed, c_got, x_got, y_got, x_last, y_last, below, above,
        c_send, c_recv, x_send, x_recv, y_send, y_recv, z_send, z_recv,
    ) = scratch
    n_z = lax.axis_size("z")
    rows = out.shape[0]
    half = rows // 2
    (z, x, c, y), x_near, y_near, c_near = around()
    halves = (pl.ds(0, half), pl.ds(half, half))
    low, high = halves
    target = slab_order()

    def c_copy(slab, px):
        return remote(
            handed.at[slab, px], c_got.at[slab, px], c_send.at[slab, px], c_recv.at[slab, px], c_near
        )

    def x_first(slab, part):
        block = lanes.at[slab, 1 - x, y if part == 0 else 1 - y, low]
        return remote(block, x_got.at[slab, part], x_send.at[slab, part], x_recv.at[slab, part], x_near)

    def y_first(slab, part):
        block = lanes.at[slab, x if part == 0 else 1 - x, 1 - y, high]
        return remote(block, y_got.at[slab, part], y_send.at[slab, part], y_recv.at[slab, part], y_near)

    def y_second(slab):
        block = lanes.at[slab, x, 1 - y, low]
        return remote(block, y_last.at[slab], y_send.at[slab, 2], y_recv.at[slab, 2], y_near)

    def x_second(slab):
        block = lanes.at[slab, 1 - x, y, high]
        return remote(block, x_last.at[slab], x_send.at[slab, 2], x_recv.at[slab, 2], x_near)

    def z_up(slab, part):
        return remote(
            lanes.at[slab, x, y, halves[part]], below.at[slab, halves[part]], z_send.at[slab, part],
            z_recv.at[slab, 0, part], (z + 1, x, c, y),
        )

    def z_down(slab, part):
        return remote(
            lanes.at[slab, x, y, halves[part]], above.at[slab, halves[part]], z_send.at[slab, part],
            z_recv.at[slab, 1, part], (z - 1, x, c, y),
        )

    def produce(step):
        slab = target(step)
        before(step)

        def hand(px, unused):
            handed[slab, px] = make(step, slab, px, 1 - c).reshape(2, rows, -1)
            c_copy(slab, px).start()
            return unused

        def keep(px, unused):
            lanes[slab, px] = make(step, slab, px, c).reshape(2, rows, -1)
            return unused

        lax.fori_loop(0, 2, hand, 0)
        lax.fori_loop(0, 2, keep, 0)

    def begin(step):
        slab = target(step)
        for px in range(2):
            c_copy(slab, px).wait_recv()

        def merge(px, py):
            lanes[slab, px, py] = total_of(lanes[slab, px, py], c_got[slab, px, py]).astype(jnp.bfloat16)

        merge(1 - x, 1 - y)
        x_first(slab, 1).start()
        y_first(slab, 1).start()
        merge(1 - x, y)
        x_first(slab, 0).start()
        merge(x, 1 - y)
        y_first(slab, 0).start()
        merge(x, y)
        after(step)

    def middle(step):
        slab = target(step)
        x_first(slab, 1).wait_recv()
        x_first(slab, 0).wait_send()
        y_first(slab, 0).wait_send()
        lanes[slab, x, 1 - y, low] = total_of(
            lanes[slab, x, 1 - y, low], x_got[slab, 1]
        ).astype(jnp.bfloat16)
        y_second(slab).start()
        y_first(slab, 1).wait_recv()
        lanes[slab, 1 - x, y, high] = total_of(
            lanes[slab, 1 - x, y, high], y_got[slab, 1]
        ).astype(jnp.bfloat16)
        x_second(slab).start()

    def finish(step):
        slab = target(step)
        for part in range(2):
            if part == 0:
                x_first(slab, 0).wait_recv()
                y_second(slab).wait_recv()
                value = total_of(lanes[slab, x, y, low], x_got[slab, 0], y_last[slab])
            else:
                y_first(slab, 0).wait_recv()
                x_second(slab).wait_recv()
                value = total_of(lanes[slab, x, y, high], y_got[slab, 0], x_last[slab])
            rows_of = halves[part]

            @pl.when(slab > z)
            def _():
                @pl.when(z == 0)
                def _():
                    lanes[slab, x, y, rows_of] = value.astype(jnp.bfloat16)

                @pl.when(z > 0)
                def _():
                    z_up(slab, part).wait_recv()
                    lanes[slab, x, y, rows_of] = total_of(value, below[slab, rows_of]).astype(jnp.bfloat16)

                z_up(slab, part).start()

            @pl.when(slab < z)
            def _():
                @pl.when(z == n_z - 1)
                def _():
                    lanes[slab, x, y, rows_of] = value.astype(jnp.bfloat16)

                @pl.when(z < n_z - 1)
                def _():
                    z_down(slab, part).wait_recv()
                    lanes[slab, x, y, rows_of] = total_of(value, above[slab, rows_of]).astype(jnp.bfloat16)

                z_down(slab, part).start()

            @pl.when(slab == z)
            def _():
                out[rows_of, :] = value

                @pl.when(z > 0)
                def _():
                    z_up(slab, part).wait_recv()
                    out[rows_of, :] += below[slab, rows_of].astype(jnp.float32)

                @pl.when(z < n_z - 1)
                def _():
                    z_down(slab, part).wait_recv()
                    out[rows_of, :] += above[slab, rows_of].astype(jnp.float32)

    def turn(step, unused):
        for action, back in ((produce, 0), (begin, 0), (middle, 1), (finish, 2)):

            @pl.when((step >= back) & (step < n_z + back))
            def _():
                action(step - back)

        beside(step)
        return unused

    lax.fori_loop(0, n_z + 2, turn, 0)

    def close(slab, unused):
        for px in range(2):
            c_copy(slab, px).wait_send()
        x_first(slab, 1).wait_send()
        y_first(slab, 1).wait_send()
        x_second(slab).wait_send()
        y_second(slab).wait_send()
        for part in range(2):

            @pl.when(slab > z)
            def _():
                z_up(slab, part).wait_send()

            @pl.when(slab < z)
            def _():
                z_down(slab, part).wait_send()

        return unused

    lax.fori_loop(0, n_z, close, 0)


def embed_kernel(shard_rows, table, ints, qkv_own, out_own, out, qkv_all, out_all, *scratch):
    extent = table.shape[0]
    chunk = 2 * out.shape[0]
    greet_near()
    beside, close = line_gather(
        (qkv_own, out_own),
        (lambda pz, pc: qkv_all.at[:, pz, :, pc], lambda pz, pc: out_all.at[:, pz, pc]),
        scratch[-5:],
    )

    def make(step, slab, px, pc):
        token = in_pairs(ints, slab, px, pc, 0).astype(jnp.int32)
        hot = vocab_ids(extent, chunk, shard_rows) == token
        hot = jnp.where(hot, 1.0, 0.0).astype(jnp.bfloat16)
        return inner(hot, table[...]).astype(jnp.bfloat16)

    scatter_slabs(out, scratch[:-5], lambda step: None, make, lambda step: None, beside)
    close()


def embed(table, ints, qkv_own, out_own, own, shard_rows, collective_id):
    width = table.shape[1]
    n_z, n_x, n_c, _ = sizes()
    layers = qkv_own.shape[0]
    return pl.pallas_call(
        functools.partial(embed_kernel, shard_rows),
        out_shape=(
            jax.ShapeDtypeStruct((own, width), jnp.float32),
            jax.ShapeDtypeStruct((layers, n_z, n_x, n_c) + qkv_own.shape[2:], qkv_own.dtype),
            jax.ShapeDtypeStruct((layers, n_z, n_c) + out_own.shape[1:], out_own.dtype),
        ),
        in_specs=[VMEM] * 4,
        out_specs=(VMEM,) * 3,
        scratch_shapes=scatter_scratch(own, width) + line_gather_sems(),
        cost_estimate=pl.CostEstimate(
            flops=0, bytes_accessed=120 * MIB, transcendentals=0
        ),
        compiler_params=pltpu.CompilerParams(
            collective_id=collective_id, has_side_effects=True,
            vmem_limit_bytes=lax.axis_size("z") * 3 * MIB + 12 * MIB,
        ),
    )(table, ints, qkv_own, out_own)


def vocab_back_kernel(
    shard_rows, held, rows_all, table, ints, logs, weights, out, table_grad, slab_rows, changes, slab_sem, *scratch
):
    extent, width = table.shape
    chunk = 2 * out.shape[0]
    scale = width ** (-0.5)
    n_z = lax.axis_size("z")
    target = slab_order()

    def load(step):
        return pltpu.make_async_copy(
            rows_all.at[target(step)], slab_rows.at[step % 2], slab_sem.at[step % 2]
        )

    if not held:
        load(0).start()
    greet_near()
    table_grad[...] = jnp.zeros_like(table_grad)

    def rows_of(step, px, pc):
        if held:
            return rows_all[target(step), px, pc].reshape(chunk, width)
        return slab_rows[step % 2, px, pc].reshape(chunk, width)

    def before(step):
        if held:
            return
        load(step).wait()

        @pl.when(step + 1 < n_z)
        def _():
            load(step + 1).start()

    def make(step, slab, px, pc):
        value = outer(table[...], rows_of(step, px, pc)) * scale
        aim = in_pairs(ints, slab, px, pc, 1).astype(jnp.int32)
        hot = jnp.where(vocab_ids(extent, chunk, shard_rows) == aim, 1.0, 0.0)
        change = jnp.exp(value - in_pairs(logs, slab, px, pc, 0)) - hot
        change = (change * in_pairs(weights, slab, px, pc, 0)).astype(jnp.bfloat16)
        changes[px, pc] = change
        return (inner(change, table[...]) * scale).astype(jnp.bfloat16)

    def after(step):
        def one(index, unused):
            px, pc = index // 2, index % 2
            table_grad[...] += matmul(changes[px, pc], rows_of(step, px, pc))
            return unused

        lax.fori_loop(0, 4, one, 0)

    scatter_slabs(out, scratch, before, make, after)
    table_grad[...] = table_grad[...] * scale


def vocab_back(rows_all, table, ints, logs, weights, shard_rows, collective_id):
    own, width = rows_all.shape[4:]
    extent = table.shape[0]
    n_z, n_x, n_c, n_y = sizes()
    held = n_z <= 4
    return pl.pallas_call(
        functools.partial(vocab_back_kernel, shard_rows, held),
        out_shape=(
            jax.ShapeDtypeStruct((own, width), jnp.float32),
            jax.ShapeDtypeStruct((extent, width), jnp.float32),
        ),
        in_specs=[VMEM if held else ANY] + [VMEM] * 4,
        out_specs=(VMEM,) * 2,
        scratch_shapes=[
            pltpu.VMEM((1,) * 6 if held else (2, n_x, n_c, n_y, own, width), rows_all.dtype),
            pltpu.VMEM((n_x, n_c, extent, 2 * own), jnp.bfloat16),
            pltpu.SemaphoreType.DMA((2,)),
        ] + scatter_scratch(own, width),
        cost_estimate=pl.CostEstimate(
            flops=0, bytes_accessed=144 * MIB, transcendentals=0
        ),
        compiler_params=pltpu.CompilerParams(
            collective_id=collective_id, has_side_effects=True,
            vmem_limit_bytes=n_z * 3 * MIB + 20 * MIB if n_z <= 8 else 62 * MIB,
        ),
    )(rows_all, table, ints, logs, weights)


SQRT_HALF = 0.5**0.5
DENSITY = 0.3989422804014327


def matmul(left, right):
    return jnp.dot(left, right, preferred_element_type=jnp.float32)


def inner(left, right):
    return lax.dot_general(
        left, right, (((0,), (0,)), ((), ())), preferred_element_type=jnp.float32
    )


def outer(left, right):
    return lax.dot_general(
        left, right, (((1,), (1,)), ((), ())), preferred_element_type=jnp.float32
    )


def plane_gather(own_rows, blocks, send_sem, recv_sem):
    half = own_rows.shape[0] // 2
    (z, x, c, y), x_near, y_near, _ = around()
    low, high = pl.ds(0, half), pl.ds(half, half)

    def copy(slot, px, py, rows, source, device):
        target = blocks.at[px, py, rows]
        return remote(target if source is None else source.at[rows], target, send_sem.at[slot], recv_sem.at[slot], device)

    first = [
        copy(0, x, y, low, own_rows, x_near),
        copy(1, x, y, high, own_rows, y_near),
        copy(2, x, y, high, own_rows, x_near),
        copy(3, x, y, low, own_rows, y_near),
    ]
    relays = [copy(4, 1 - x, y, low, None, y_near), copy(5, x, 1 - y, high, None, x_near)]
    for each in first:
        each.start()

    def wait_near():
        first[0].wait_recv()
        relays[0].start()
        first[1].wait_recv()
        relays[1].start()

    def wait_x():
        first[2].wait_recv()

    def wait_y():
        first[3].wait_recv()

    def wait_diagonal():
        for each in relays:
            each.wait_recv()

    def close():
        for each in first + relays:
            each.wait_send()

    return wait_near, wait_x, wait_y, wait_diagonal, close


def plane_sum(parts, got, out, send_sem, recv_sem):
    (z, x, c, y), x_near, y_near, _ = around()
    diagonal = (z, 1 - x, c, 1 - y)
    copies = [
        remote(parts.at[device[1], device[3]], got.at[slot], send_sem.at[slot], recv_sem.at[slot], device)
        for slot, device in enumerate((x_near, y_near, diagonal))
    ]

    def close():
        for each in copies:
            each.wait_recv()
        out[...] = total_of(parts[x, y], got[0], got[1], got[2])
        for each in copies:
            each.wait_send()

    return copies, close


def order_experts(kept, got, ordered, sems):
    n_z, n_c, _, depth, _ = kept.shape
    x = lax.axis_index("x")
    copies = []
    for pz in range(n_z):
        for pc in range(n_c):
            for side, weights in enumerate((kept, got)):
                if depth == ordered.shape[1]:
                    rows, side = pl.ds(0, depth), 0
                else:
                    px = x if side == 0 else 1 - x
                    at = (pz * 2 + px) * n_c + pc
                    rows = pl.ds(pl.multiple_of(at * depth, 16), depth)
                slot = (pz * n_c + pc) * 2 + side
                if depth == ordered.shape[1] and weights is got:
                    continue
                copies.append(
                    pltpu.make_async_copy(weights.at[pz, pc], ordered.at[:, rows], sems.at[slot])
                )
    for copy in copies:
        copy.start()
    return copies


def experts_kernel(
    own_rows, route, w_kept, w_got, out, wide, before, hidden, ordered, parts, got, w_sem, g_send, g_recv, s_send, s_recv
):
    (z, x, c, y), x_near, y_near, _ = around()
    diagonal = (z, 1 - x, c, 1 - y)
    loads = order_experts(w_kept, w_got, ordered, w_sem)
    up, down = ordered.at[pl.ds(0, 2)], ordered.at[pl.ds(2, 2)]
    greet((x_near, y_near, diagonal))
    wait_near, wait_x, wait_y, wait_diagonal, close = plane_gather(own_rows, wide, g_send, g_recv)
    copies, finish = plane_sum(parts, got, out, s_send, s_recv)
    wide[x, y] = own_rows[...]

    def work(px, py):
        rows = wide[px, py]
        first = route[px, py] == 0
        value = jnp.where(first, matmul(rows, up[0]), matmul(rows, up[1]))
        before[px, py] = value
        active = 0.5 * value * (1.0 + lax.erf(value * SQRT_HALF))
        hidden_first = jnp.where(first, active, 0.0).astype(jnp.bfloat16)
        hidden_second = jnp.where(first, 0.0, active).astype(jnp.bfloat16)
        hidden[px, py] = active.astype(jnp.bfloat16)
        total = outer(hidden_first, down[0]) + outer(hidden_second, down[1])
        parts[px, py] = total.astype(jnp.bfloat16)

    for load in loads:
        load.wait()
    work(x, y)
    wait_near()
    wait_x()
    work(1 - x, y)
    copies[0].start()
    wait_y()
    work(x, 1 - y)
    copies[1].start()
    wait_diagonal()
    work(1 - x, 1 - y)
    copies[2].start()
    finish()
    close()


def experts(own_rows, route, weights, collective_id):
    _, n_x, _, n_y = sizes()
    own, width = own_rows.shape
    wide = weights[0].shape[4]
    dma = pltpu.SemaphoreType.DMA
    low = jnp.bfloat16
    return pl.pallas_call(
        experts_kernel,
        out_shape=(
            jax.ShapeDtypeStruct((own, width), jnp.float32),
            jax.ShapeDtypeStruct((n_x, n_y, own, width), low),
            jax.ShapeDtypeStruct((n_x, n_y, own, wide), jnp.float32),
            jax.ShapeDtypeStruct((n_x, n_y, own, wide), low),
        ),
        in_specs=[VMEM, VMEM, ANY, ANY],
        out_specs=(VMEM,) * 4,
        scratch_shapes=[
            pltpu.VMEM((4, width, wide), low),
            pltpu.VMEM((n_x, n_y, own, width), low),
            pltpu.VMEM((3, own, width), low),
            dma((width // weights[0].shape[3],)), dma((6,)), dma((6,)), dma((3,)), dma((3,)),
        ],
        compiler_params=pltpu.CompilerParams(
            collective_id=collective_id, has_side_effects=True, vmem_limit_bytes=20 * MIB
        ),
        cost_estimate=pl.CostEstimate(
            flops=8 * own * 4 * width * wide, bytes_accessed=54 * MIB, transcendentals=4 * own * wide
        ),
    )(own_rows, route, *weights)


def experts_back_kernel(
    own_rows, route, w_kept, w_got, wide, before, hidden, out, grads,
    ordered, wide_grad, before_grad, parts, got, w_sem, g_send, g_recv, s_send, s_recv,
):
    (z, x, c, y), x_near, y_near, _ = around()
    diagonal = (z, 1 - x, c, 1 - y)
    loads = order_experts(w_kept, w_got, ordered, w_sem)
    up, down = ordered.at[pl.ds(0, 2)], ordered.at[pl.ds(2, 2)]
    greet((x_near, y_near, diagonal))
    wait_near, wait_x, wait_y, wait_diagonal, close = plane_gather(own_rows, wide_grad, g_send, g_recv)
    copies, finish = plane_sum(parts, got, out, s_send, s_recv)
    wide_grad[x, y] = own_rows[...]

    def work(px, py):
        rows = wide_grad[px, py]
        first = route[px, py] == 0
        hidden_grad = jnp.where(first, matmul(rows, down[0]), matmul(rows, down[1]))
        value = before[px, py]
        slope = 0.5 * (1.0 + lax.erf(value * SQRT_HALF)) + value * (
            DENSITY * jnp.exp(-0.5 * value * value)
        )
        change = (hidden_grad * slope).astype(jnp.bfloat16)
        before_grad[px, py] = change
        change_first = jnp.where(first, change, 0)
        change_second = jnp.where(first, 0, change)
        total = outer(change_first, up[0]) + outer(change_second, up[1])
        parts[px, py] = total.astype(jnp.bfloat16)

    for load in loads:
        load.wait()
    work(x, y)
    wait_near()
    wait_x()
    work(1 - x, y)
    copies[0].start()
    wait_y()
    work(x, 1 - y)
    copies[1].start()
    wait_diagonal()
    work(1 - x, 1 - y)
    copies[2].start()
    close()

    lane = 4 * own_rows.shape[0]
    rows = wide[...].reshape(lane, -1)
    grad_rows = wide_grad[...].reshape(lane, -1)
    first = route[...].reshape(lane, 1) == 0
    change = before_grad[...].reshape(lane, -1)
    active = hidden[...].reshape(lane, -1)
    low = jnp.bfloat16
    n_z, n_x, n_c, _ = sizes()
    depth = grads.shape[3]

    def keep(slot, value):
        value = value.astype(low)
        for pz in range(n_z):
            for px in range(n_x):
                for pc in range(n_c):
                    start = ((pz * n_x + px) * n_c + pc) * depth
                    grads[pz * n_c + pc, px, slot] = value[start : start + depth]

    keep(0, inner(rows, jnp.where(first, change, 0)))
    keep(1, inner(rows, jnp.where(first, 0, change)))
    keep(2, inner(grad_rows, jnp.where(first, active, 0)))
    keep(3, inner(grad_rows, jnp.where(first, 0, active)))
    finish()


def experts_back(own_rows, route, weights, wide, before, hidden, collective_id):
    n_z, n_x, n_c, n_y = sizes()
    own, width = own_rows.shape
    units = weights[0].shape[4]
    dma = pltpu.SemaphoreType.DMA
    low = jnp.bfloat16
    return pl.pallas_call(
        experts_back_kernel,
        out_shape=(
            jax.ShapeDtypeStruct((own, width), jnp.float32),
            jax.ShapeDtypeStruct((n_z * n_c, n_x, 4, width // (n_z * n_x * n_c), units), low),
        ),
        in_specs=[VMEM, VMEM, ANY, ANY] + [VMEM] * 3,
        out_specs=(VMEM,) * 2,
        scratch_shapes=[
            pltpu.VMEM((4, width, units), low),
            pltpu.VMEM((n_x, n_y, own, width), low),
            pltpu.VMEM((n_x, n_y, own, units), low),
            pltpu.VMEM((n_x, n_y, own, width), low),
            pltpu.VMEM((3, own, width), low),
            dma((width // weights[0].shape[3],)), dma((6,)), dma((6,)), dma((3,)), dma((3,)),
        ],
        compiler_params=pltpu.CompilerParams(
            collective_id=collective_id, has_side_effects=True, vmem_limit_bytes=28 * MIB
        ),
        cost_estimate=pl.CostEstimate(
            flops=16 * own * 4 * width * units, bytes_accessed=54 * MIB, transcendentals=8 * own * units
        ),
    )(own_rows, route, *weights, wide, before, hidden)


def in_owner_order(value, target):
    value = value.astype(target.dtype)
    n_c, n_z = target.shape[:2]
    n_x = target.shape[2] if len(target.shape) == 5 else 1
    depth = target.shape[-2]
    for pz in range(n_z):
        for px in range(n_x):
            for pc in range(n_c):
                start = ((pz * n_x + px) * n_c + pc) * depth
                if len(target.shape) == 5:
                    target[pc, pz, px] = value[start : start + depth]
                else:
                    target[pc, pz] = value[start : start + depth]


def project_kernel(transposed, with_grad, *refs):
    if with_grad:
        rows, weight, left, out, grad, parts, got, s_send, s_recv = refs
    else:
        rows, weight, out, parts, got, s_send, s_recv = refs
    (z, x, c, y), x_near, y_near, _ = around()
    diagonal = (z, 1 - x, c, 1 - y)
    barrier = pltpu.get_barrier_semaphore()
    for device in (x_near, y_near, diagonal):
        pl.semaphore_signal(barrier, inc=1, device_id=device, device_id_type=MESH)
    copies, finish = plane_sum(parts, got, out, s_send, s_recv)

    def work(px, py):
        times = outer if transposed else matmul
        parts[px, py] = times(rows[px, py], weight[...]).astype(jnp.bfloat16)

    work(1 - x, 1 - y)
    pl.semaphore_wait(barrier, 3)
    copies[2].start()
    work(1 - x, y)
    copies[0].start()
    work(x, 1 - y)
    copies[1].start()
    work(x, y)
    if with_grad:
        lane = 4 * out.shape[0]
        in_owner_order(inner(left[...].reshape(lane, -1), rows[...].reshape(lane, -1)), grad)
    finish()


def project(rows, weight, transposed, left, collective_id):
    n_x, n_y, own, depth = rows.shape
    n_z, _, n_c, _ = sizes()
    width = weight.shape[0] if transposed else weight.shape[1]
    low = jnp.bfloat16
    dma = pltpu.SemaphoreType.DMA
    return pl.pallas_call(
        functools.partial(project_kernel, transposed, left is not None),
        out_shape=(jax.ShapeDtypeStruct((own, width), jnp.float32),)
        + (
            ()
            if left is None
            else (
                jax.ShapeDtypeStruct(
                    (n_c, n_z, n_x, left.shape[3] // (n_z * n_x * n_c), depth), low
                ),
            )
        ),
        in_specs=[VMEM] * (2 if left is None else 3),
        out_specs=(VMEM,) * (1 if left is None else 2),
        scratch_shapes=[
            pltpu.VMEM((n_x, n_y, own, width), low), pltpu.VMEM((3, own, width), low), dma((3,)), dma((3,)),
        ],
        compiler_params=pltpu.CompilerParams(
            collective_id=collective_id, has_side_effects=True, vmem_limit_bytes=16 * MIB
        ),
        cost_estimate=pl.CostEstimate(
            flops=8 * own * width * depth, bytes_accessed=24 * MIB, transcendentals=0
        ),
    )(rows, weight, *(() if left is None else (left,)))


def gather_project_kernel(transposed, split, with_grad, own_rows, weight, *rest):
    if with_grad:
        left, wide, rest = rest[0], rest[1], (rest[0],) + rest[2:]
    else:
        wide, rest = rest[0], rest[1:]

    (z, x, c, y), x_near, y_near, _ = around()
    rest, (g_send, g_recv) = rest[:-2], rest[-2:]
    left, outs = (rest[0], rest[1:]) if with_grad else (None, rest)
    greet((x_near, y_near))
    wait_near, wait_x, wait_y, wait_diagonal, close = plane_gather(own_rows, wide, g_send, g_recv)
    wide[x, y] = own_rows[...]

    def work(px, py):
        times = outer if transposed else matmul
        value = times(wide[px, py], weight[...]).astype(jnp.bfloat16)
        start = 0
        for out, size in zip(outs, split):
            out[px, py] = value[:, start : start + size]
            start += size

    work(x, y)
    wait_near()
    wait_x()
    work(1 - x, y)
    wait_y()
    work(x, 1 - y)
    wait_diagonal()
    work(1 - x, 1 - y)
    if with_grad:
        lane = 4 * own_rows.shape[0]
        in_owner_order(inner(left[...], wide[...].reshape(lane, -1)), outs[-1])
    close()


def gather_project(own_rows, weight, transposed, split, left, collective_id):
    n_z, n_x, n_c, n_y = sizes()
    own, width = own_rows.shape
    depth = weight.shape[0] if transposed else weight.shape[1]
    dma = pltpu.SemaphoreType.DMA
    low = jnp.bfloat16
    return pl.pallas_call(
        functools.partial(gather_project_kernel, transposed, split, left is not None),
        out_shape=(
            jax.ShapeDtypeStruct((n_x, n_y, own, width), low),
        ) + tuple(jax.ShapeDtypeStruct((n_x, n_y, own, size), low) for size in split)
        + (
            ()
            if left is None
            else (jax.ShapeDtypeStruct((n_c, n_z, left.shape[1] // (n_z * n_c), width), low),)
        ),
        in_specs=[VMEM] * (2 if left is None else 3),
        out_specs=(VMEM,) * (1 + len(split) + (0 if left is None else 1)),
        scratch_shapes=[dma((6,)), dma((6,))],
        compiler_params=pltpu.CompilerParams(
            collective_id=collective_id, has_side_effects=True, vmem_limit_bytes=12 * MIB
        ),
        cost_estimate=pl.CostEstimate(
            flops=8 * own * width * depth, bytes_accessed=24 * MIB, transcendentals=0
        ),
    )(own_rows, weight, *(() if left is None else (left,)))


def merge_logs_kernel(source, out, got, mine, send_one, recv_one, send_two, recv_two):
    n_z, n_x, n_c, n_y = sizes()
    count = n_z * n_x * n_c * n_y
    z, x, c, y = place()
    me = ((z * n_x + x) * n_c + c) * n_y + y

    def device_of(index):
        return (
            index // (n_x * n_c * n_y), index // (n_c * n_y) % n_x, index // n_y % n_c, index % n_y
        )

    barrier = pltpu.get_barrier_semaphore()

    def call(step, unused):
        other = lax.rem(me + step, count)
        pl.semaphore_signal(barrier, inc=1, device_id=device_of(other), device_id_type=MESH)
        return unused

    lax.fori_loop(1, count, call, 0)
    got[me] = source[me]
    pl.semaphore_wait(barrier, count - 1)

    def first(step):
        other = lax.rem(me + step, count)
        return remote(
            source.at[other], got.at[me], send_one.at[step], recv_one.at[step], device_of(other)
        )

    def second(step):
        other = lax.rem(me + step, count)
        return remote(mine, out.at[me], send_two.at[step], recv_two.at[step], device_of(other))

    def each(action):
        def body(step, unused):
            action(step)
            return unused

        lax.fori_loop(1, count, body, 0)

    each(lambda step: first(step).start())
    each(lambda step: first(step).wait())
    values = got[...]
    peak = jnp.max(values, axis=0)
    mine[...] = peak + jnp.log(jnp.sum(jnp.exp(values - peak[None]), axis=0))
    out[me] = mine[...]
    each(lambda step: second(step).start())
    each(lambda step: second(step).wait())


def merge_logs(blocks, collective_id):
    count = blocks.shape[0]
    dma = pltpu.SemaphoreType.DMA
    return pl.pallas_call(
        merge_logs_kernel,
        out_shape=jax.ShapeDtypeStruct(blocks.shape, blocks.dtype),
        in_specs=[VMEM],
        out_specs=VMEM,
        scratch_shapes=[
            pltpu.VMEM(blocks.shape, blocks.dtype), pltpu.VMEM(blocks.shape[1:], blocks.dtype),
            dma((count,)), dma((count,)), dma((count,)), dma((count,)),
        ],
        cost_estimate=pl.CostEstimate(
            flops=0, bytes_accessed=42 * MIB, transcendentals=0
        ),
        compiler_params=pltpu.CompilerParams(
            collective_id=collective_id, has_side_effects=True, vmem_limit_bytes=8 * MIB
        ),
    )(blocks)


def key_position(index, part, chunk):
    lane = 2 * chunk
    start = (part // 2) * (2 * lane) + (part % 2) * chunk
    return start + index + jnp.where(index >= chunk, chunk, 0)


def near_shown(side, chunk, query_pos, query_seg, near_pos, near_seg):
    columns = slice(side * chunk, (side + 1) * chunk)
    rows = slice(2 * side * chunk, 2 * (side + 1) * chunk)
    shown = (
        (near_seg[rows, :] == query_seg[:, columns])
        & (near_pos[rows, :] <= query_pos[:, columns])
        & (near_pos[rows, :] >= PROMPT)
    )
    return columns, rows, shown


def attend_kernel(
    chunk, query, far, near, query_pos, query_seg, near_pos, near_seg,
    out, out_low, log_total, scores, far_t, near_t,
):
    lane, feature = query.shape
    group = feature // HEAD_DIM
    prompt_rows = far.shape[0]
    parts = prompt_rows // lane
    query_t = (query[...].astype(jnp.float32) * HEAD_DIM ** (-0.5)).T.astype(jnp.bfloat16)
    far_t[...] = far[...].astype(jnp.float32).T.astype(jnp.bfloat16)
    near_t[...] = near[...].astype(jnp.float32).T.astype(jnp.bfloat16)
    row_of = lax.broadcasted_iota(jnp.int32, (feature, lane), 0)
    q_pos = query_pos[...]

    for head in range(group):
        low, high = head * HEAD_DIM, (head + 1) * HEAD_DIM
        query_h = jnp.where((row_of >= low) & (row_of < high), query_t, 0)

        def score_part(part, peak):
            block = far[pl.ds(pl.multiple_of(part * lane, lane), lane), :feature]
            value = matmul(block, query_h)
            index = lax.broadcasted_iota(jnp.int32, (lane, lane), 0)
            value = jnp.where(key_position(index, part, chunk) <= q_pos, value, MASKED)
            scores[pl.ds(pl.multiple_of(part * lane, lane), lane), :] = value
            return jnp.maximum(peak, jnp.max(value, axis=0, keepdims=True))

        peak = lax.fori_loop(0, parts, score_part, jnp.full((1, lane), MASKED, jnp.float32))
        near_peaks = []
        for side in range(2):
            columns, rows, shown = near_shown(side, chunk, query_pos, query_seg, near_pos, near_seg)
            value = matmul(near[rows, :feature], query_h[:, columns])
            value = jnp.where(shown, value, MASKED)
            scores[prompt_rows : prompt_rows + lane, columns] = value
            near_peaks.append(jnp.max(value, axis=0, keepdims=True))
        peak = jnp.maximum(peak, jnp.concatenate(near_peaks, axis=1))

        def weigh_part(part, state):
            total, mixed = state
            start = pl.multiple_of(part * lane, lane)
            chance = jnp.exp(scores[pl.ds(start, lane), :] - peak)
            total = total + jnp.sum(chance, axis=0, keepdims=True)
            mixed = mixed + matmul(
                far_t[feature + low : feature + high, pl.ds(start, lane)],
                chance.astype(jnp.bfloat16),
            )
            return total, mixed

        total, mixed = lax.fori_loop(
            0,
            parts,
            weigh_part,
            (jnp.zeros((1, lane), jnp.float32), jnp.zeros((HEAD_DIM, lane), jnp.float32)),
        )
        near_total, near_mixed = [], []
        for side in range(2):
            columns = slice(side * chunk, (side + 1) * chunk)
            rows = slice(side * lane, (side + 1) * lane)
            chance = jnp.exp(scores[prompt_rows : prompt_rows + lane, columns] - peak[:, columns])
            near_total.append(jnp.sum(chance, axis=0, keepdims=True))
            near_mixed.append(
                matmul(near_t[feature + low : feature + high, rows], chance.astype(jnp.bfloat16))
            )
        total = total + jnp.concatenate(near_total, axis=1)
        mixed = mixed + jnp.concatenate(near_mixed, axis=1)
        out[low:high, :] = mixed / total
        log_total[head : head + 1, :] = peak + jnp.log(total)
    out_low[...] = out[...].T.astype(jnp.bfloat16)


def attend(queries, far, near, places, chunk):
    lane, feature = queries.shape
    prompt_rows = far.shape[0]
    group = feature // HEAD_DIM
    total_rows = prompt_rows + lane
    return pl.pallas_call(
        functools.partial(attend_kernel, chunk),
        out_shape=(
            jax.ShapeDtypeStruct((feature, lane), jnp.float32),
            jax.ShapeDtypeStruct((lane, feature), jnp.bfloat16),
            jax.ShapeDtypeStruct((group, lane), jnp.float32),
        ),
        in_specs=[VMEM] * 7,
        out_specs=(VMEM,) * 3,
        scratch_shapes=[
            pltpu.VMEM((total_rows, lane), jnp.float32),
            pltpu.VMEM((2 * feature, prompt_rows), jnp.bfloat16),
            pltpu.VMEM((2 * feature, 2 * lane), jnp.bfloat16),
        ],
        compiler_params=pltpu.CompilerParams(vmem_limit_bytes=20 * MIB),
        cost_estimate=pl.CostEstimate(
            flops=8 * group * lane * total_rows * 128,
            bytes_accessed=8 * MIB,
            transcendentals=group * lane * total_rows,
        ),
    )(queries, far, near, *places)


def attend_back_kernel(
    chunk, query, far, near, query_pos, query_seg, near_pos, near_seg,
    log_total, mixed, answer, query_grad, far_grad, near_grad,
    far_t, near_t, far_values, near_values, far_sum, near_sum, query_sum,
):
    lane, feature = query.shape
    group = feature // HEAD_DIM
    prompt_rows = far.shape[0]
    parts = prompt_rows // lane
    scaled = (query[...].astype(jnp.float32) * HEAD_DIM ** (-0.5)).astype(jnp.bfloat16)
    query_t = scaled.astype(jnp.float32).T.astype(jnp.bfloat16)
    answers = answer[...]
    answer_t = answers.astype(jnp.float32).T.astype(jnp.bfloat16)
    far_t[...] = far[:, :feature].astype(jnp.float32).T.astype(jnp.bfloat16)
    near_t[...] = near[:, :feature].astype(jnp.float32).T.astype(jnp.bfloat16)
    far_values[...] = far[:, feature:]
    near_values[...] = near[:, feature:]
    row_of = lax.broadcasted_iota(jnp.int32, (feature, lane), 0)
    column_of = lax.broadcasted_iota(jnp.int32, (lane, feature), 1)
    q_pos = query_pos[...]

    for head in range(group):
        low, high = head * HEAD_DIM, (head + 1) * HEAD_DIM
        in_rows = (row_of >= low) & (row_of < high)
        in_columns = (column_of >= low) & (column_of < high)
        query_ht = jnp.where(in_rows, query_t, 0)
        answer_ht = jnp.where(in_rows, answer_t, 0)
        query_h = jnp.where(in_columns, scaled, 0)
        answer_h = jnp.where(in_columns, answers, 0)
        log_h = log_total[head : head + 1, :]
        delta_h = jnp.sum(
            answer_t[low:high, :].astype(jnp.float32) * mixed[low:high, :], axis=0, keepdims=True
        )

        def slopes(key_block, value_block, shown, columns):
            value = matmul(key_block, query_ht[:, columns])
            chance = jnp.exp(jnp.where(shown, value - log_h[:, columns], MASKED))
            slope = matmul(value_block, answer_ht[:, columns])
            change = (chance * (slope - delta_h[:, columns])).astype(jnp.bfloat16)
            chance = chance.astype(jnp.bfloat16)
            return change, matmul(change, query_h[columns]), matmul(chance, answer_h[columns])

        def add(sums, rows, key_part, value_part):
            if head == 0:
                sums[0, rows, :] = key_part
                sums[1, rows, :] = value_part
            else:
                sums[0, rows, :] += key_part
                sums[1, rows, :] += value_part

        def back_part(part, total):
            rows = pl.ds(pl.multiple_of(part * lane, lane), lane)
            index = lax.broadcasted_iota(jnp.int32, (lane, lane), 0)
            shown = key_position(index, part, chunk) <= q_pos
            change, key_part, value_part = slopes(
                far[rows, :feature], far_values[rows, :], shown, slice(0, lane)
            )
            add(far_sum, rows, key_part, value_part)
            return total + matmul(far_t[low:high, rows], change)

        total = lax.fori_loop(0, parts, back_part, jnp.zeros((HEAD_DIM, lane), jnp.float32))
        near_total = []
        for side in range(2):
            columns, rows, shown = near_shown(side, chunk, query_pos, query_seg, near_pos, near_seg)
            change, key_part, value_part = slopes(
                near[rows, :feature], near_values[rows, :], shown, columns
            )
            add(near_sum, rows, key_part, value_part)
            near_total.append(matmul(near_t[low:high, rows], change))
        query_sum[low:high, :] = (total + jnp.concatenate(near_total, axis=1)) * HEAD_DIM ** (-0.5)
    query_grad[...] = query_sum[...].T.astype(jnp.bfloat16)
    for sums, grad in ((far_sum, far_grad), (near_sum, near_grad)):
        grad[...] = jnp.concatenate(
            [sums[0].astype(jnp.bfloat16), sums[1].astype(jnp.bfloat16)], axis=1
        )


def attend_back(queries, far, near, places, log_total, mixed, answer, chunk):
    lane, feature = queries.shape
    prompt_rows = far.shape[0]
    group = feature // HEAD_DIM
    total_rows = prompt_rows + lane
    low = jnp.bfloat16
    return pl.pallas_call(
        functools.partial(attend_back_kernel, chunk),
        out_shape=(
            jax.ShapeDtypeStruct((lane, feature), low),
            jax.ShapeDtypeStruct((prompt_rows, 2 * feature), low),
            jax.ShapeDtypeStruct((2 * lane, 2 * feature), low),
        ),
        in_specs=[VMEM] * 10,
        out_specs=(VMEM,) * 3,
        scratch_shapes=[
            pltpu.VMEM((feature, prompt_rows), low),
            pltpu.VMEM((feature, 2 * lane), low),
            pltpu.VMEM((prompt_rows, feature), low),
            pltpu.VMEM((2 * lane, feature), low),
            pltpu.VMEM((2, prompt_rows, feature), jnp.float32),
            pltpu.VMEM((2, 2 * lane, feature), jnp.float32),
            pltpu.VMEM((feature, lane), jnp.float32),
        ],
        compiler_params=pltpu.CompilerParams(vmem_limit_bytes=28 * MIB),
        cost_estimate=pl.CostEstimate(
            flops=20 * group * lane * total_rows * 128,
            bytes_accessed=12 * MIB,
            transcendentals=group * lane * total_rows,
        ),
    )(queries, far, near, *places, log_total, mixed, answer)


def head_places(back):
    n_z, n_x, n_c, n_y = sizes()
    line = n_z * n_c
    pairs = []
    for device in range(line * n_x * n_y):
        group, at = device // line, device % line
        place_of = ((at // n_c * n_x + group // n_y) * n_c + at % n_c) * n_y + group % n_y
        pairs.append((place_of, device) if back else (device, place_of))
    return tuple(pairs)


def pad_rows(block):
    return jnp.pad(block, ((0, 8 - block.shape[0]), (0, 0)))


def adam_update(weight, moment_one, moment_two, gradient, step_rate, decay_rate):
    first_new = BETA_ONE * moment_one + (1.0 - BETA_ONE) * gradient
    second_new = BETA_TWO * moment_two + (1.0 - BETA_TWO) * gradient * gradient
    normalized = (
        first_new
        / (1.0 - BETA_ONE**STEP)
        / (jnp.sqrt(second_new / (1.0 - BETA_TWO**STEP)) + ADAM_EPS)
    )
    return (weight - step_rate * (normalized + decay_rate * weight), first_new, second_new)


def per_device(
    token_ids,
    targets,
    valid_mask,
    cont_lengths,
    routes,
    vocab_table,
    vocab_first,
    vocab_second,
    attn_weights,
    attn_first,
    attn_second,
    router,
    router_first,
    router_second,
    norm_gains,
    gains_first,
    gains_second,
    expert_up,
    up_first,
    up_second,
    expert_down,
    down_first,
    down_second,
):
    slabs = lax.axis_size("z")
    planes = lax.axis_size("x")
    cores = lax.axis_size("core")
    sides = lax.axis_size("head")
    groups = planes * sides
    z_at, x_at, core_at, side_at = (lax.axis_index(name) for name in ALL)
    blk_at = (z_at * planes + x_at) * cores + core_at
    device_at = blk_at * sides + side_at
    group_at = x_at * sides + side_at
    tokens = valid_mask.shape[0]
    chunk = token_ids.shape[0]
    own = chunk // sides
    lane = planes * chunk
    feature = D // groups
    wide = expert_up.shape[3] // planes
    shard_rows = vocab_table.shape[0]
    logit_scale = D ** (-0.5)

    cont_ends = jnp.cumsum(cont_lengths)
    valid_f = valid_mask.astype(jnp.float32)
    token_count = jnp.sum(valid_mask).astype(jnp.float32)
    expert_ids = jnp.arange(EXPERTS, dtype=jnp.int32)

    own_ints = jnp.concatenate([token_ids[None], targets[None], routes], axis=0)
    own_ints = lax.dynamic_slice_in_dim(own_ints, side_at * own, own, axis=1).astype(jnp.float32)
    rows_of = attn_weights.shape[1]
    smalls = jnp.concatenate(
        [router.transpose(0, 2, 1).reshape(LAYERS * EXPERTS, rows_of), norm_gains], axis=0
    )
    smalls = smalls.astype(jnp.bfloat16).astype(jnp.float32)
    smalls = jnp.pad(smalls, ((0, 16 - smalls.shape[0]), (0, own - rows_of)))
    whole_f = swap(jnp.concatenate([pad_rows(own_ints), smalls], axis=0)[None], True, 1)
    attn_low = attn_weights.astype(jnp.bfloat16)
    qkv_send = attn_low[:, :, : 3 * D].reshape(LAYERS, rows_of, 3, groups, feature)
    qkv_send = jnp.concatenate([qkv_send[:, :, 1:], qkv_send[:, :, :1]], axis=2)
    qkv_send = qkv_send.transpose(3, 0, 1, 2, 4).reshape(groups, LAYERS, rows_of, 3 * feature)
    qkv_got = lax.all_to_all(qkv_send, PLANE, split_axis=0, concat_axis=0, tiled=True)
    out_rows = lax.ppermute(attn_low[:, :, 3 * D :], ALL, head_places(False))
    expert_send = jnp.stack([expert_up, expert_down], axis=1).astype(jnp.bfloat16)
    depth = expert_send.shape[3]
    expert_send = expert_send.reshape(LAYERS, 2 * EXPERTS, depth, planes, wide)
    expert_send = expert_send.transpose(3, 0, 1, 2, 4)
    expert_halves = []
    for layer_index in range(LAYERS):
        kept_half = lax.dynamic_index_in_dim(expert_send[:, layer_index], x_at, 0, False)
        sent_half = lax.dynamic_index_in_dim(expert_send[:, layer_index], 1 - x_at, 0, False)
        got_half = lax.ppermute(sent_half, "x", ((0, 1), (1, 0)))
        expert_halves.append((kept_half, got_half))
    got_halves = [got_half for _, got_half in expert_halves]
    whole_f, qkv_got, out_rows, got_halves = lax.optimization_barrier(
        (whole_f, qkv_got, out_rows, got_halves)
    )
    expert_halves = [(kept_half, got) for (kept_half, _), got in zip(expert_halves, got_halves)]
    qkv_own = qkv_got.reshape(planes, sides, LAYERS, rows_of, 3 * feature).transpose(2, 0, 1, 3, 4)
    qkv_own = qkv_own.reshape(LAYERS, planes, sides * rows_of, 3 * feature)

    def gather_experts(kept_half, got_half):
        if depth % 16 == 0:
            return lax.all_gather(kept_half, LINE, axis=0).reshape(
                (slabs, cores) + kept_half.shape
            ), lax.all_gather(got_half, LINE, axis=0).reshape((slabs, cores) + kept_half.shape)
        halves = jnp.stack(
            [jnp.where(x_at == 0, kept_half, got_half), jnp.where(x_at == 0, got_half, kept_half)]
        )
        block = lax.all_gather(halves, LINE, axis=0)
        block = block.reshape(slabs, cores, planes, 2 * EXPERTS, depth, wide)
        block = block.transpose(3, 0, 2, 1, 4, 5).reshape(1, 1, 2 * EXPERTS, D, wide)
        return block, block

    expert_weights = [gather_experts(*expert_halves[0])]
    ints = whole_f.reshape(sizes() + whole_f.shape[1:])
    whole = whole_f[:, : 2 + LAYERS].astype(jnp.int32)
    smalls = whole_f[:, 8:, :rows_of].transpose(1, 0, 2).reshape(16, D)
    router_all = smalls[: LAYERS * EXPERTS].reshape(LAYERS, EXPERTS, D).transpose(0, 2, 1)
    router_all = router_all.astype(jnp.bfloat16)
    gains_f = smalls[LAYERS * EXPERTS :]
    routes_lane = lax.dynamic_index_in_dim(
        whole.reshape(slabs, planes, cores, sides, 2 + LAYERS, own), z_at, 0, False
    )
    routes_lane = lax.dynamic_index_in_dim(routes_lane, core_at, 1, False)[:, :, 2:]
    routes_lane = routes_lane.transpose(2, 0, 1, 3)[..., None]
    routes_own = lax.dynamic_slice_in_dim(routes, side_at * own, own, axis=1)

    extent = -(-shard_rows // 256) * 256
    table = jnp.pad(vocab_table.astype(jnp.bfloat16), ((0, extent - shard_rows), (0, 0)))
    offsets = jnp.arange(chunk, dtype=jnp.int32)
    first_blk = z_at * planes * cores + core_at
    query_pos = jnp.concatenate([(first_blk + cores * part) * chunk + offsets for part in range(planes)])
    near_blks = [first_blk - 1 + part for part in range(2 * planes)]
    near_pos = jnp.concatenate([blk * chunk + offsets for blk in near_blks])
    query_seg = segment_of(query_pos, cont_ends)
    near_seg = segment_of(near_pos, cont_ends)
    places = (query_pos[None, :], query_seg[None, :], near_pos[:, None], near_seg[:, None])

    stream, qkv_all, out_all = embed(table, ints, qkv_own, out_rows, own, shard_rows, 2)
    qkv_weights = [qkv_all[layer_index].reshape(D, 3 * feature) for layer_index in range(LAYERS)]
    out_weights = [out_all[layer_index].reshape(feature, D) for layer_index in range(LAYERS)]

    kept = []
    for layer_index in range(LAYERS):
        normed_lane, key_values, queries = gather_project(
            rms_norm(stream, gains_f[2 * layer_index]).astype(jnp.bfloat16),
            qkv_weights[layer_index], False, (2 * feature, feature), None, 3,
        )
        queries = queries.reshape(lane, feature)
        far, near = spread_keys(key_values.reshape(lane, 2 * feature), PROMPT, 10)
        if layer_index + 1 < LAYERS:
            far, halves = lax.optimization_barrier((far, expert_halves[layer_index + 1]))
            expert_weights.append(gather_experts(*halves))
        mixed_t, mixed_low, log_total = attend(queries, far, near, places, chunk)
        (attended,) = project(
            mixed_low.reshape(planes, sides, own, feature), out_weights[layer_index], False, None, 15
        )
        middle = stream + attended
        normed_two = rms_norm(middle, gains_f[2 * layer_index + 1]).astype(jnp.bfloat16)
        chance = jax.nn.softmax(matmul(normed_two, router_all[layer_index]), axis=-1)
        output, wide_rows, before, hidden = experts(
            normed_two, routes_lane[layer_index], expert_weights[layer_index], 11
        )
        own_pick = (routes_own[layer_index][:, None] == expert_ids[None, :]).astype(jnp.float32)
        gate = jnp.sum(chance * own_pick, axis=1, keepdims=True)
        kept.append(
            (
                stream, normed_lane, queries, far, near, mixed_t, mixed_low, log_total, middle,
                normed_two, chance, wide_rows, before, hidden, output, own_pick, gate,
            )
        )
        stream = middle + gate * output

    final_gain = gains_f[2 * LAYERS]
    devices = tokens // own
    valid_rows = valid_f.reshape(sizes() + (1, own))
    final_all, row_logs, hits = gather_logits(
        rms_norm(stream, final_gain).astype(jnp.bfloat16), table, ints, valid_rows, shard_rows, 4
    )
    log_sums = merge_logs(row_logs.reshape(devices, 1, own), 5)
    log_sum = log_sums.reshape(tokens)
    own_log = lax.dynamic_slice_in_dim(log_sum, device_at * own, own)
    own_valid = lax.dynamic_slice_in_dim(valid_f, device_at * own, own)
    own_loss = jnp.sum(own_log * own_valid) - jnp.sum(hits)
    final_grad, table_grad = vocab_back(
        final_all, table, ints, log_sums.reshape(sizes() + (1, own)), valid_rows / token_count,
        shard_rows, 6,
    )
    stream_grad, final_gain_grad = jax.vjp(rms_norm, stream, final_gain)[1](final_grad)

    qkv_packs = [None] * LAYERS
    out_packs = [None] * LAYERS
    router_list = [None] * LAYERS
    expert_sums = [None] * LAYERS
    gain_list = [None] * (2 * LAYERS + 1)
    gain_list[2 * LAYERS] = final_gain_grad
    for layer_index in reversed(range(LAYERS)):
        (
            stream, normed_lane, queries, far, near, mixed_t, mixed_low, log_total, middle,
            normed_two, chance, wide_rows, before, hidden, output, own_pick, gate,
        ) = kept[layer_index]
        out_grad = (gate * stream_grad).astype(jnp.bfloat16)
        chance_grad = jnp.sum(stream_grad * output, axis=1)[:, None] * own_pick
        choice_grad = chance * (chance_grad - jnp.sum(chance * chance_grad, axis=1, keepdims=True))
        router_list[layer_index] = jnp.dot(
            normed_two.astype(jnp.float32).T, choice_grad, precision=lax.Precision.HIGHEST
        )
        normed_grad = jnp.dot(
            choice_grad,
            router_all[layer_index].astype(jnp.float32).T,
            precision=lax.Precision.HIGHEST,
        )
        rows_grad, expert_grad = experts_back(
            out_grad, routes_lane[layer_index], expert_weights[layer_index], wide_rows, before,
            hidden, 12,
        )
        normed_grad = normed_grad + rows_grad
        middle_part, gain_list[2 * layer_index + 1] = jax.vjp(
            rms_norm, middle, gains_f[2 * layer_index + 1]
        )[1](normed_grad)
        middle_grad = stream_grad + middle_part
        _, answer, out_packs[layer_index] = gather_project(
            middle_grad.astype(jnp.bfloat16), out_weights[layer_index], True, (feature,), mixed_low, 16
        )
        answer = answer.reshape(lane, feature)
        query_grad, far_grad, near_grad = attend_back(
            queries, far, near, places, log_total, mixed_t, answer, chunk
        )
        qkv_grad = collect_keys(far_grad, near_grad, query_grad, 13)
        qkv_grad, expert_grad = lax.optimization_barrier((qkv_grad, expert_grad))
        expert_sums[layer_index] = lax.psum_scatter(
            expert_grad, LINE, scatter_dimension=0, tiled=True
        )[0]
        normed_att_grad, qkv_packs[layer_index] = project(
            qkv_grad.reshape(planes, sides, own, 3 * feature), qkv_weights[layer_index], True,
            normed_lane, 14,
        )
        stream_part, gain_list[2 * layer_index] = jax.vjp(
            rms_norm, stream, gains_f[2 * layer_index]
        )[1](normed_att_grad)
        stream_grad = middle_grad + stream_part

    small = jnp.concatenate(
        [jnp.stack(router_list).transpose(1, 0, 2).reshape(D, -1), jnp.stack(gain_list).T], axis=1
    )
    small = small.reshape(devices, rows_of, -1).transpose(0, 2, 1)
    small = jnp.pad(small, ((0, 0), (0, 16 - small.shape[1]), (0, 128 - rows_of)))
    table_share, small, near_squares, *attn_sums = embed_back(
        stream_grad.astype(jnp.bfloat16), ints, table_grad, small, qkv_packs + out_packs, shard_rows, 7
    )
    squares = sum(
        jnp.sum(jnp.square(part.astype(jnp.float32)))
        for part in [small[:, :rows_of]] + expert_sums
    ) + jnp.sum(near_squares)
    sums = jnp.pad(jnp.stack([squares, own_loss])[:, None], ((0, 6), (0, 127)))
    sums = jnp.sum(swap(sums[None], True, 9)[:, :2, 0], axis=0)
    square_total, loss_sum = sums[0], sums[1]
    expert_shares = []
    for expert_grad in expert_sums:
        kept_half = lax.dynamic_index_in_dim(expert_grad, x_at, 0, False)
        sent_half = lax.dynamic_index_in_dim(expert_grad, 1 - x_at, 0, False)
        got_half = lax.ppermute(sent_half, "x", ((0, 1), (1, 0)))
        expert_grad = jnp.concatenate(
            [jnp.where(x_at == 0, kept_half, got_half), jnp.where(x_at == 0, got_half, kept_half)],
            axis=-1,
        )
        expert_shares.append(
            expert_grad.reshape(2, EXPERTS, depth, planes * wide).astype(jnp.float32)
        )
    table_share, small = table_share[:shard_rows], small[:, :rows_of]
    router_share = (
        small[: LAYERS * EXPERTS].reshape(LAYERS, EXPERTS, rows_of).transpose(0, 2, 1)
    )
    gain_share = small[LAYERS * EXPERTS : LAYERS * EXPERTS + 2 * LAYERS + 1]
    qkv_share = jnp.stack(attn_sums[:LAYERS], axis=1).reshape(
        planes, LAYERS, sides, rows_of, 3 * feature
    )
    qkv_share = qkv_share.transpose(0, 2, 1, 3, 4).reshape(groups, LAYERS, rows_of, 3 * feature)
    qkv_share = lax.all_to_all(qkv_share, PLANE, split_axis=0, concat_axis=0, tiled=True)
    qkv_share = qkv_share.reshape(groups, LAYERS, rows_of, 3, feature)
    qkv_share = jnp.concatenate([qkv_share[:, :, :, 2:], qkv_share[:, :, :, :2]], axis=3)
    qkv_share = qkv_share.transpose(1, 2, 3, 0, 4).reshape(LAYERS, rows_of, 3 * D)
    out_share = lax.ppermute(jnp.stack(attn_sums[LAYERS:]), ALL, head_places(True))
    attn_share = jnp.concatenate([qkv_share, out_share], axis=2).astype(jnp.float32)
    up_share = jnp.stack([share[0] for share in expert_shares])
    down_share = jnp.stack([share[1] for share in expert_shares])
    shares = (table_share, attn_share, router_share, gain_share, up_share, down_share)
    grad_norm = jnp.sqrt(square_total)
    factor = CLIP_AT / jnp.maximum(grad_norm, CLIP_AT)
    weights = (vocab_table, attn_weights, router, norm_gains, expert_up, expert_down)
    firsts = (vocab_first, attn_first, router_first, gains_first, up_first, down_first)
    seconds = (vocab_second, attn_second, router_second, gains_second, up_second, down_second)
    results = [loss_sum, token_count, grad_norm]
    for number in range(6):
        results.extend(
            adam_update(
                weights[number],
                firsts[number],
                seconds[number],
                factor * shares[number],
                STEP_RATES[number],
                DECAY_RATES[number],
            )
        )
    return tuple(results)


def solution(mesh):
    blocks, sides = mesh.shape["blk"], mesh.shape["head"]
    fine = Mesh(mesh.devices.reshape(blocks // 4, 2, 2, sides), ALL)
    weight_specs = (
        (P(ALL, None),) * 3
        + (P(None, ALL, None),) * 3
        + (P(None, ALL, None),) * 3
        + (P(None, ALL),) * 3
        + (P(None, None, BLK, "head"),) * 6
    )
    return jax.shard_map(
        per_device,
        mesh=fine,
        in_specs=(P(BLK), P(BLK), P(), P(), P(None, BLK)) + weight_specs,
        out_specs=(P(), P(), P()) + weight_specs,
        check_vma=False,
    )
```

```python
import functools

import jax
import jax.numpy as jnp
from jax import lax
from jax.experimental import pallas as pl
from jax.experimental.pallas import tpu as pltpu
from jax.sharding import Mesh, PartitionSpec as P

D = 768
HEADS = 12
HEAD_DIM = 64
EXPERTS = 2
LAYERS = 2
PROMPT = 2048
STEP = 10

NORM_EPS = 1e-06
BETA_ONE = 0.9
BETA_TWO = 0.95
ADAM_EPS = 1e-08
CLIP_AT = 0.01
MASKED = -1e30
STEP_RATES = (2.0, 0.25, 0.04, 0.4, 0.04, 0.04)
DECAY_RATES = (0.01, 0.01, 0.01, 0.0, 0.01, 0.01)

ALL = ("z", "x", "core", "head")
BLK = ("z", "x", "core")
PLANE = ("x", "head")
LINE = ("z", "core")
MIB = 2**20
MESH = pl.DeviceIdType.MESH
ANY = pl.BlockSpec(memory_space=pl.ANY)
VMEM = pl.BlockSpec(memory_space=pltpu.VMEM)
HBM = pl.BlockSpec(memory_space=pltpu.HBM)


def rms_norm(stream, gain):
    return stream * lax.rsqrt(jnp.mean(stream * stream, axis=-1, keepdims=True) + NORM_EPS) * gain


def segment_of(position, cont_ends):
    later = jnp.sum((cont_ends[None, :] <= (position - PROMPT)[:, None]).astype(jnp.int32), axis=1)
    return jnp.where(position < PROMPT, 0, 1 + later)


def place():
    return tuple(lax.axis_index(name) for name in ALL)


def sizes():
    return tuple(lax.axis_size(name) for name in ALL)


def remote(source, target, send, receive, device):
    return pltpu.make_async_remote_copy(
        src_ref=source, dst_ref=target, send_sem=send, recv_sem=receive,
        device_id=device, device_id_type=MESH,
    )


def greet(devices):
    barrier = pltpu.get_barrier_semaphore()
    for device in devices:
        pl.semaphore_signal(barrier, inc=1, device_id=device, device_id_type=MESH)
    pl.semaphore_wait(barrier, len(devices))


def around():
    z, x, c, y = place()
    return (z, x, c, y), (z, 1 - x, c, y), (z, x, c, 1 - y), (z, x, 1 - c, y)


def swap_kernel(broadcast, source, out, send_sem, receive_sem, own_sem):
    n_z, n_x, n_c, n_y = sizes()
    count = n_z * n_x * n_c * n_y
    z, x, c, y = place()
    me = ((z * n_x + x) * n_c + c) * n_y + y

    def device_of(index):
        return (
            index // (n_x * n_c * n_y), index // (n_c * n_y) % n_x, index // n_y % n_c, index % n_y
        )

    def taken(index):
        return source.at[0] if broadcast else source.at[index]

    barrier = pltpu.get_barrier_semaphore()

    def call(step, unused):
        other = lax.rem(me + step, count)
        pl.semaphore_signal(barrier, inc=1, device_id=device_of(other), device_id_type=MESH)
        return unused

    lax.fori_loop(1, count, call, 0)
    own = pltpu.make_async_copy(taken(me), out.at[me], own_sem)
    own.start()
    pl.semaphore_wait(barrier, count - 1)

    def copy(step):
        other = lax.rem(me + step, count)
        return remote(
            taken(other), out.at[me], send_sem.at[step], receive_sem.at[step], device_of(other)
        )

    def start(step, unused):
        copy(step).start()
        return unused

    def finish(step, unused):
        copy(step).wait()
        return unused

    lax.fori_loop(1, count, start, 0)
    lax.fori_loop(1, count, finish, 0)
    own.wait()


def swap(blocks, broadcast, collective_id):
    count = 1
    for size in sizes():
        count *= size
    return pl.pallas_call(
        functools.partial(swap_kernel, broadcast),
        out_shape=jax.ShapeDtypeStruct((count,) + blocks.shape[1:], blocks.dtype),
        in_specs=[VMEM],
        out_specs=VMEM,
        scratch_shapes=[
            pltpu.SemaphoreType.DMA((count,)),
            pltpu.SemaphoreType.DMA((count,)),
            pltpu.SemaphoreType.DMA,
        ],
        cost_estimate=pl.CostEstimate(
            flops=0, bytes_accessed=36 * MIB, transcendentals=0
        ),
        compiler_params=pltpu.CompilerParams(
            collective_id=collective_id, has_side_effects=True, vmem_limit_bytes=8 * MIB
        ),
    )(blocks)


def total_of(*parts):
    total = parts[0].astype(jnp.float32)
    for part in parts[1:]:
        total = total + part.astype(jnp.float32)
    return total


PIECES = 4


def spread_kernel(
    prompt_slabs, own_rows, far, near, tail, z_send, z_recv, c_send, c_recv, n_send, n_recv, own_sem
):
    n_z = lax.axis_size("z")
    lane = own_rows.shape[0]
    chunk = lane // 2
    size = lane // PIECES
    (z, x, c, y), _, _, c_near = around()
    above, below = (z + 1, x, c, y), (z - 1, x, c, y)
    in_prompt = z < prompt_slabs
    takes_down = z < prompt_slabs - 1
    gives_down = (z > 0) & (z < prompt_slabs)

    barrier = pltpu.get_barrier_semaphore()
    pl.semaphore_signal(barrier, inc=1, device_id=c_near, device_id_type=MESH)

    @pl.when(z > 0)
    def _():
        pl.semaphore_signal(barrier, inc=1, device_id=below, device_id_type=MESH)

    @pl.when(takes_down)
    def _():
        pl.semaphore_signal(barrier, inc=1, device_id=above, device_id_type=MESH)

    first, second = pl.ds(0, chunk), pl.ds(chunk, chunk)
    own = [
        pltpu.make_async_copy(own_rows.at[first], near.at[1], own_sem.at[0]),
        pltpu.make_async_copy(own_rows.at[second], near.at[3], own_sem.at[1]),
    ]
    own_far = pltpu.make_async_copy(own_rows, far.at[jnp.minimum(z, prompt_slabs - 1), c], own_sem.at[2])
    own_edge = pltpu.make_async_copy(own_rows.at[first], near.at[0], own_sem.at[3])
    edge = (z == 0) & (c == 0)
    for copy in own:
        copy.start()

    @pl.when(in_prompt)
    def _():
        own_far.start()

    @pl.when(edge)
    def _():
        own_edge.start()

    pl.semaphore_wait(
        barrier, 1 + jnp.where(z < n_z - 1, 1, 0) + jnp.where(gives_down, 1, 0)
    )

    def part(index):
        return pl.ds(index * size, size)

    def z_copy(source, slab, index, up):
        return remote(
            source, far.at[slab, c, part(index)], z_send.at[slab, index, 1 if up else 0],
            z_recv.at[slab, index], above if up else below,
        )

    def c_copy(source, slab, index):
        return remote(
            source, far.at[slab, c, part(index)], c_send.at[slab, index], c_recv.at[slab, index], c_near
        )

    def t_copy():
        return remote(own_rows.at[second], tail, n_send.at[0], n_recv.at[0], above)

    def t_hand():
        return remote(tail, near.at[0], n_send.at[1], n_recv.at[1], c_near)

    def n_copy(half):
        slot = jnp.where(c == 0, 2 * half, 2)
        return remote(
            own_rows.at[pl.ds(half * chunk, chunk)], near.at[slot], n_send.at[2 + half], n_recv.at[2 + half],
            c_near,
        )

    @pl.when(in_prompt)
    def _():
        for index in range(PIECES):
            source = own_rows.at[part(index)]

            @pl.when(z < n_z - 1)
            def _():
                z_copy(source, z, index, True).start()

            @pl.when(z > 0)
            def _():
                z_copy(source, z, index, False).start()

            c_copy(source, z, index).start()

    @pl.when((c == 1) & (z < n_z - 1))
    def _():
        t_copy().start()

    n_copy(0).start()

    @pl.when(c == 0)
    def _():
        n_copy(1).start()

    for distance in range(1, n_z):
        low_slab, high_slab = z - distance, z + distance
        for index in range(PIECES):

            @pl.when((low_slab >= 0) & (low_slab < prompt_slabs))
            def _():
                source = far.at[low_slab, c, part(index)]
                z_copy(source, low_slab, index, True).wait_recv()

                @pl.when(z < n_z - 1)
                def _():
                    z_copy(source, low_slab, index, True).start()

                c_copy(source, low_slab, index).start()

            if distance < prompt_slabs:

                @pl.when(high_slab < prompt_slabs)
                def _():
                    source = far.at[high_slab, c, part(index)]
                    z_copy(source, high_slab, index, False).wait_recv()

                    @pl.when(z > 0)
                    def _():
                        z_copy(source, high_slab, index, False).start()

                    c_copy(source, high_slab, index).start()

    @pl.when((c == 1) & (z > 0))
    def _():
        t_copy().wait_recv()
        t_hand().start()
        t_hand().wait_send()

    @pl.when((c == 1) & (z < n_z - 1))
    def _():
        t_copy().wait_send()

    @pl.when((c == 0) & (z > 0))
    def _():
        t_hand().wait_recv()

    n_copy(0).wait_send()
    n_copy(0).wait_recv()

    @pl.when(c == 0)
    def _():
        n_copy(1).wait_send()

    @pl.when(c == 1)
    def _():
        n_copy(1).wait_recv()

    for slab in range(prompt_slabs):
        for index in range(PIECES):
            copy = c_copy(own_rows.at[part(index)], slab, index)
            copy.wait_send()
            copy.wait_recv()

            @pl.when((z < n_z - 1) & (slab <= z))
            def _():
                z_copy(own_rows.at[part(index)], slab, index, True).wait_send()

            @pl.when((z > 0) & (slab >= z))
            def _():
                z_copy(own_rows.at[part(index)], slab, index, False).wait_send()

    for copy in own:
        copy.wait()

    @pl.when(in_prompt)
    def _():
        own_far.wait()

    @pl.when(edge)
    def _():
        own_edge.wait()


def spread_keys(own_rows, prompt_rows, collective_id):
    lane, width = own_rows.shape
    slabs = prompt_rows // (2 * lane)
    dma = pltpu.SemaphoreType.DMA
    far, near, _ = pl.pallas_call(
        functools.partial(spread_kernel, slabs),
        out_shape=(
            jax.ShapeDtypeStruct((slabs, 2, lane, width), own_rows.dtype),
            jax.ShapeDtypeStruct((4, lane // 2, width), own_rows.dtype),
            jax.ShapeDtypeStruct((lane // 2, width), own_rows.dtype),
        ),
        in_specs=[VMEM],
        out_specs=(VMEM,) * 3,
        scratch_shapes=[
            dma((slabs, PIECES, 2)), dma((slabs, PIECES)), dma((slabs, PIECES)), dma((slabs, PIECES)),
            dma((4,)), dma((4,)), dma((4,)),
        ],
        cost_estimate=pl.CostEstimate(
            flops=0, bytes_accessed=60 * MIB, transcendentals=0
        ),
        compiler_params=pltpu.CompilerParams(
            collective_id=collective_id, has_side_effects=True, vmem_limit_bytes=12 * MIB
        ),
    )(own_rows)
    return far.reshape(prompt_rows, width), near.reshape(2 * lane, width)


def collect_kernel(
    prompt_slabs, far, near, query_grad, whole, out, own, c_got, z_got, n_got, tail_pass, tail_got,
    c_send, c_recv, z_send, z_recv, n_send, n_recv,
):
    n_z = lax.axis_size("z")
    lane = out.shape[0]
    chunk = lane // 2
    size = lane // PIECES
    (z, x, c, y), _, _, c_near = around()
    above, below = (z + 1, x, c, y), (z - 1, x, c, y)

    barrier = pltpu.get_barrier_semaphore()
    pl.semaphore_signal(barrier, inc=1, device_id=c_near, device_id_type=MESH)

    @pl.when(z < n_z - 1)
    def _():
        pl.semaphore_signal(barrier, inc=1, device_id=above, device_id_type=MESH)

    pl.semaphore_wait(barrier, 1 + jnp.where(z > 0, 1, 0))

    def part(index):
        return pl.ds(index * size, size)

    def c_copy(slab, index):
        return remote(
            far.at[slab, 1 - c, part(index)], c_got.at[slab, part(index)], c_send.at[slab, index],
            c_recv.at[slab, index], c_near,
        )

    def z_copy(slab, index):
        return remote(
            own.at[slab, part(index)], z_got.at[slab, part(index)], z_send.at[slab, index],
            z_recv.at[slab, index], below,
        )

    def n_copy(half):
        slot = jnp.where(c == 0, 2, 2 * half)
        return remote(near.at[slot], n_got.at[half], n_send.at[half], n_recv.at[half], c_near)

    def t_hand():
        return remote(near.at[0], tail_pass, n_send.at[2], n_recv.at[2], c_near)

    def t_copy():
        return remote(tail_pass, tail_got, n_send.at[3], n_recv.at[3], below)

    for slab in range(prompt_slabs):
        for index in range(PIECES):
            c_copy(slab, index).start()
    n_copy(0).start()

    @pl.when(c == 1)
    def _():
        n_copy(1).start()

    @pl.when((c == 0) & (z > 0))
    def _():
        t_hand().start()

    for slab in range(prompt_slabs):
        for index in range(PIECES):
            c_copy(slab, index).wait_recv()
            rows = part(index)
            mine = total_of(far[slab, c, rows, :], c_got[slab, rows, :])

            @pl.when((z == n_z - 1) & (z > slab))
            def _():
                own[slab, rows, :] = mine.astype(jnp.bfloat16)
                z_copy(slab, index).start()

            @pl.when((z < n_z - 1) & (z > slab))
            def _():
                z_copy(slab, index).wait_recv()
                own[slab, rows, :] = total_of(mine, z_got[slab, rows, :]).astype(jnp.bfloat16)
                z_copy(slab, index).start()

            @pl.when((z < n_z - 1) & (z == slab))
            def _():
                z_copy(slab, index).wait_recv()
                out[rows, :] = total_of(mine, z_got[slab, rows, :])

            @pl.when((z == n_z - 1) & (z == slab))
            def _():
                out[rows, :] = mine

    @pl.when((c == 1) & (z > 0))
    def _():
        t_hand().wait_recv()
        t_copy().start()

    @pl.when(z >= prompt_slabs)
    def _():
        out[...] = jnp.zeros_like(out)

    n_copy(0).wait_recv()
    first, second = pl.ds(0, chunk), pl.ds(chunk, chunk)
    out[first, :] += total_of(near[1], n_got[0])
    out[second, :] += near[3].astype(jnp.float32)

    @pl.when(c == 0)
    def _():
        n_copy(1).wait_recv()
        out[second, :] += n_got[1].astype(jnp.float32)

    @pl.when((c == 1) & (z < n_z - 1))
    def _():
        t_copy().wait_recv()
        out[second, :] += tail_got[...].astype(jnp.float32)

    whole[...] = jnp.concatenate([out[...].astype(jnp.bfloat16), query_grad[...]], axis=1)

    @pl.when((c == 1) & (z > 0))
    def _():
        t_copy().wait_send()

    @pl.when((c == 0) & (z > 0))
    def _():
        t_hand().wait_send()

    n_copy(0).wait_send()

    @pl.when(c == 1)
    def _():
        n_copy(1).wait_send()

    for slab in range(prompt_slabs):
        for index in range(PIECES):
            c_copy(slab, index).wait_send()

            @pl.when(z > slab)
            def _():
                z_copy(slab, index).wait_send()


def collect_keys(far, near, query_grad, collective_id):
    prompt_rows, width = far.shape
    lane = near.shape[0] // 2
    slabs = prompt_rows // (2 * lane)
    dma = pltpu.SemaphoreType.DMA
    low = jnp.bfloat16
    return pl.pallas_call(
        functools.partial(collect_kernel, slabs),
        out_shape=jax.ShapeDtypeStruct((lane, width + query_grad.shape[1]), low),
        in_specs=[VMEM] * 3,
        out_specs=VMEM,
        scratch_shapes=[
            pltpu.VMEM((lane, width), jnp.float32),
            pltpu.VMEM((slabs, lane, width), low),
            pltpu.VMEM((slabs, lane, width), low),
            pltpu.VMEM((slabs, lane, width), low),
            pltpu.VMEM((2, lane // 2, width), low),
            pltpu.VMEM((lane // 2, width), low),
            pltpu.VMEM((lane // 2, width), low),
            dma((slabs, PIECES)), dma((slabs, PIECES)), dma((slabs, PIECES)), dma((slabs, PIECES)),
            dma((4,)), dma((4,)),
        ],
        cost_estimate=pl.CostEstimate(
            flops=0, bytes_accessed=60 * MIB, transcendentals=0
        ),
        compiler_params=pltpu.CompilerParams(
            collective_id=collective_id, has_side_effects=True, vmem_limit_bytes=20 * MIB
        ),
    )(far.astype(low).reshape(slabs, 2, lane, width), near.astype(low).reshape(4, lane // 2, width), query_grad)


def greet_all():
    n_z, n_x, n_c, n_y = sizes()
    count = n_z * n_x * n_c * n_y
    barrier = pltpu.get_barrier_semaphore()

    def call(step, unused):
        pl.semaphore_signal(barrier, inc=1, device_id=device_after(step), device_id_type=MESH)
        return unused

    lax.fori_loop(1, count, call, 0)
    pl.semaphore_wait(barrier, count - 1)


def index_after(step):
    n_z, n_x, n_c, n_y = sizes()
    z, x, c, y = place()
    me = ((z * n_x + x) * n_c + c) * n_y + y
    return lax.rem(me + step, n_z * n_x * n_c * n_y)


def device_after(step):
    _, n_x, n_c, n_y = sizes()
    index = index_after(step)
    return (
        index // (n_x * n_c * n_y), index // (n_c * n_y) % n_x, index // n_y % n_c, index % n_y
    )


def greet_near():
    n_z = lax.axis_size("z")
    (z, x, c, y), x_near, y_near, c_near = around()
    barrier = pltpu.get_barrier_semaphore()
    for device in (x_near, y_near, c_near):
        pl.semaphore_signal(barrier, inc=1, device_id=device, device_id_type=MESH)

    @pl.when(z > 0)
    def _():
        pl.semaphore_signal(barrier, inc=1, device_id=(z - 1, x, c, y), device_id_type=MESH)

    @pl.when(z < n_z - 1)
    def _():
        pl.semaphore_signal(barrier, inc=1, device_id=(z + 1, x, c, y), device_id_type=MESH)

    pl.semaphore_wait(barrier, 3 + jnp.where(z > 0, 1, 0) + jnp.where(z < n_z - 1, 1, 0))


Z_PIECES = 4


def gather_sems():
    n_z = lax.axis_size("z")
    dma = pltpu.SemaphoreType.DMA
    return [
        dma((n_z, Z_PIECES, 2)), dma((n_z, Z_PIECES)), dma((n_z, 2)), dma((n_z, 2)), dma((n_z, 2)),
        dma((n_z, 2)), dma((n_z, 4)), dma((n_z, 4)), dma,
    ]


def gather_slabs(rows_in, out, sems, work, beside=lambda step: None):
    z_send, z_recv, x_send, x_recv, y_send, y_recv, c_send, c_recv, own_sem = sems
    n_z = lax.axis_size("z")
    half = rows_in.shape[0] // 2
    size = rows_in.shape[0] // Z_PIECES
    (z, x, c, y), x_near, y_near, c_near = around()
    low, high = pl.ds(0, half), pl.ds(half, half)
    everything = pl.ds(0, 2 * half)
    own = pltpu.make_async_copy(rows_in, out.at[z, x, c, y], own_sem)
    own.start()

    def block(origin, px, py, rows):
        return out.at[origin, px, c, py, rows]

    def z_copy(source, origin, index, up):
        rows = pl.ds(index * size, size)
        other = (z + 1, x, c, y) if up else (z - 1, x, c, y)
        return remote(
            source.at[rows], block(origin, x, y, rows), z_send.at[origin, index, 1 if up else 0],
            z_recv.at[origin, index], other,
        )

    def x_copy(source, origin):
        return remote(source, out.at[origin, x, c, y], x_send.at[origin, 0], x_recv.at[origin, 0], x_near)

    def y_copy(source, origin):
        return remote(source, out.at[origin, x, c, y], y_send.at[origin, 0], y_recv.at[origin, 0], y_near)

    def x_relay(origin):
        part = block(origin, x, 1 - y, high)
        return remote(part, part, x_send.at[origin, 1], x_recv.at[origin, 1], x_near)

    def y_relay(origin):
        part = block(origin, 1 - x, y, low)
        return remote(part, part, y_send.at[origin, 1], y_recv.at[origin, 1], y_near)

    def c_copy(source, origin, px, py):
        slot = px * 2 + py
        return remote(
            source, out.at[origin, px, c, py], c_send.at[origin, slot], c_recv.at[origin, slot], c_near
        )

    def column(origin):
        return out.at[origin, x, c, y]

    def spread(source, origin):
        x_copy(source, origin).start()
        y_copy(source, origin).start()
        c_copy(source, origin, x, y).start()

    def relay(origin):
        x_copy(column(origin), origin).wait_recv()
        y_relay(origin).start()
        y_copy(column(origin), origin).wait_recv()
        x_relay(origin).start()
        c_copy(block(origin, 1 - x, y, everything), origin, 1 - x, y).start()
        c_copy(block(origin, x, 1 - y, everything), origin, x, 1 - y).start()

    def finish(origin):
        x_relay(origin).wait_recv()
        y_relay(origin).wait_recv()
        c_copy(block(origin, 1 - x, 1 - y, everything), origin, 1 - x, 1 - y).start()

    def use(origin):
        for px in range(2):
            for py in range(2):
                c_copy(out.at[origin, px, c, py], origin, px, py).wait_recv()
        work(origin)

    def arrive(step):
        below, above = z - step, z + step

        @pl.when(below >= 0)
        def _():
            for index in range(Z_PIECES):
                z_copy(rows_in, below, index, True).wait_recv()

                @pl.when(z < n_z - 1)
                def _():
                    z_copy(column(below), below, index, True).start()

            spread(column(below), below)

        @pl.when(above < n_z)
        def _():
            for index in range(Z_PIECES):
                z_copy(rows_in, above, index, False).wait_recv()

                @pl.when(z > 0)
                def _():
                    z_copy(column(above), above, index, False).start()

            spread(column(above), above)

    for index in range(Z_PIECES):

        @pl.when(z < n_z - 1)
        def _():
            z_copy(rows_in, z, index, True).start()

        @pl.when(z > 0)
        def _():
            z_copy(rows_in, z, index, False).start()

    spread(rows_in, z)
    for step in range(1, n_z + 3):
        if step < n_z:
            arrive(step)
        for action, back in ((relay, 1), (finish, 2), (use, 3)):
            late = step - back
            if late == 0:
                if action is use:
                    own.wait()
                action(z)
            elif 0 < late < n_z:
                for origin in (z - late, z + late):

                    @pl.when((origin >= 0) & (origin < n_z))
                    def _():
                        action(origin)

        beside(step)

    def close(origin, unused):
        x_copy(rows_in, origin).wait_send()
        y_copy(rows_in, origin).wait_send()
        x_relay(origin).wait_send()
        y_relay(origin).wait_send()
        for px in range(2):
            for py in range(2):
                c_copy(out.at[origin, px, c, py], origin, px, py).wait_send()
        for index in range(Z_PIECES):

            @pl.when((z < n_z - 1) & (origin <= z))
            def _():
                z_copy(rows_in, origin, index, True).wait_send()

            @pl.when((z > 0) & (origin >= z))
            def _():
                z_copy(rows_in, origin, index, False).wait_send()

        return unused

    lax.fori_loop(0, n_z, close, 0)


def line_gather_sems():
    n_z = lax.axis_size("z")
    dma = pltpu.SemaphoreType.DMA
    return [dma((n_z, 2, 2)), dma((n_z, 2)), dma((n_z, 2)), dma((n_z, 2)), dma((2,))]


def line_gather(own_parts, all_parts, sems):
    z_send, z_recv, c_send, c_recv, own_sem = sems
    n_z = lax.axis_size("z")
    (z, x, c, y), _, _, c_near = around()
    numbers = range(len(own_parts))

    def z_copy(source, number, origin, up):
        return remote(
            source, all_parts[number](origin, c), z_send.at[origin, number, 1 if up else 0],
            z_recv.at[origin, number], (z + 1, x, c, y) if up else (z - 1, x, c, y),
        )

    def c_copy(source, number, origin):
        return remote(
            source, all_parts[number](origin, c), c_send.at[origin, number], c_recv.at[origin, number], c_near
        )

    own = [
        pltpu.make_async_copy(own_parts[number], all_parts[number](z, c), own_sem.at[number])
        for number in numbers
    ]
    for copy in own:
        copy.start()
    for number in numbers:
        source = own_parts[number]

        @pl.when(z < n_z - 1)
        def _():
            z_copy(source, number, z, True).start()

        @pl.when(z > 0)
        def _():
            z_copy(source, number, z, False).start()

        c_copy(source, number, z).start()

    def beside(step):
        below, above = z - step, z + step

        @pl.when((step >= 1) & (below >= 0))
        def _():
            for number in numbers:
                source = all_parts[number](below, c)
                z_copy(source, number, below, True).wait_recv()

                @pl.when(z < n_z - 1)
                def _():
                    z_copy(source, number, below, True).start()

                c_copy(source, number, below).start()

        @pl.when((step >= 1) & (above < n_z))
        def _():
            for number in numbers:
                source = all_parts[number](above, c)
                z_copy(source, number, above, False).wait_recv()

                @pl.when(z > 0)
                def _():
                    z_copy(source, number, above, False).start()

                c_copy(source, number, above).start()

    def close():
        for copy in own:
            copy.wait()

        def one(origin, unused):
            for number in numbers:
                c_copy(own_parts[number], number, origin).wait()

                @pl.when((z < n_z - 1) & (origin <= z))
                def _():
                    z_copy(own_parts[number], number, origin, True).wait_send()

                @pl.when((z > 0) & (origin >= z))
                def _():
                    z_copy(own_parts[number], number, origin, False).wait_send()

            return unused

        lax.fori_loop(0, n_z, one, 0)

    return beside, close


def line_sems(parts):
    n_z = lax.axis_size("z")
    dma = pltpu.SemaphoreType.DMA
    return [dma((parts,)), dma((parts,)), dma((n_z, 2, parts)), dma((n_z, 2, parts))]


def line_sums(packs, outs, buffers, sems):
    c_send, c_recv, z_send, z_recv = sems
    n_z = lax.axis_size("z")
    (z, x, c, y), _, _, c_near = around()
    numbers = range(len(packs))
    lanes, got, below, above = (buffers[each :: 4] for each in range(4))
    handed = [
        remote(packs[each].at[1 - c], got[each], c_send.at[each], c_recv.at[each], c_near)
        for each in numbers
    ]

    def z_copy(slab, up, each):
        return remote(
            lanes[each].at[slab], (below if up else above)[each].at[slab],
            z_send.at[slab, 1 if up else 0, each], z_recv.at[slab, 1 if up else 0, each],
            (z + 1, x, c, y) if up else (z - 1, x, c, y),
        )

    for copy in handed:
        copy.start()

    def merge():
        for each in numbers:
            handed[each].wait()
            lanes[each][...] = total_of(packs[each][c], got[each][...]).astype(jnp.bfloat16)

    def hop(turn, step):
        high, low = n_z - 1 - turn, turn

        @pl.when((z == step - 1 - turn) & (z < high))
        def _():
            for each in numbers:

                @pl.when(z > 0)
                def _():
                    z_copy(high, True, each).wait_recv()
                    lanes[each][high] = total_of(lanes[each][high], below[each][high]).astype(jnp.bfloat16)

                z_copy(high, True, each).start()

        @pl.when((n_z - 1 - z == step - 1 - turn) & (z > low))
        def _():
            for each in numbers:

                @pl.when(z < n_z - 1)
                def _():
                    z_copy(low, False, each).wait_recv()
                    lanes[each][low] = total_of(lanes[each][low], above[each][low]).astype(jnp.bfloat16)

                z_copy(low, False, each).start()

    def beside(step):
        if step == 1:
            merge()
        if step < n_z:

            def body(turn, unused):
                hop(turn, step)
                return unused

            lax.fori_loop(0, n_z - 1, body, 0)

    def close():
        for each in numbers:
            out = outs[each]
            out[...] = lanes[each][z].astype(jnp.float32)

            @pl.when(z > 0)
            def _():
                z_copy(z, True, each).wait_recv()
                out[...] += below[each][z].astype(jnp.float32)

            @pl.when(z < n_z - 1)
            def _():
                z_copy(z, False, each).wait_recv()
                out[...] += above[each][z].astype(jnp.float32)

        def sent(slab, unused):
            for each in numbers:

                @pl.when(slab > z)
                def _():
                    z_copy(slab, True, each).wait_send()

                @pl.when(slab < z)
                def _():
                    z_copy(slab, False, each).wait_send()

            return unused

        lax.fori_loop(0, n_z, sent, 0)

    return beside, close


def in_pairs(values, slab, px, pc, row):
    return jnp.concatenate([values[slab, px, pc, py, row : row + 1, :] for py in range(2)], axis=1)


def in_lane(values, slab, pc, row):
    return jnp.concatenate([in_pairs(values, slab, px, pc, row) for px in range(2)], axis=1)


def vocab_ids(extent, chunk, shard_rows):
    n_z, n_x, n_c, n_y = sizes()
    z, x, c, y = place()
    me = ((z * n_x + x) * n_c + c) * n_y + y
    rows = lax.broadcasted_iota(jnp.int32, (extent, chunk), 0)
    return rows + me * shard_rows


def logits_kernel(shard_rows, rows_in, table, ints, valid, out, logs, hits, *sems):
    extent = table.shape[0]
    chunk = 2 * rows_in.shape[0]
    scale = table.shape[1] ** (-0.5)
    greet_near()
    hits[...] = jnp.zeros_like(hits)

    def work(slab):
        def one(index, unused):
            px, pc = index // 2, index % 2
            rows = out[slab, px, pc].reshape(chunk, -1)
            value = outer(table[...], rows) * scale
            ids = vocab_ids(extent, chunk, shard_rows)
            inside = lax.broadcasted_iota(jnp.int32, (extent, chunk), 0) < shard_rows
            target = in_pairs(ints, slab, px, pc, 1).astype(jnp.int32)
            shown = in_pairs(valid, slab, px, pc, 0)
            hit = jnp.where(ids == target, value, 0.0)
            hits[...] += jnp.sum(hit, axis=0, keepdims=True) * shown
            value = jnp.where(inside, value, MASKED)
            peak = jnp.max(value, axis=0, keepdims=True)
            log = peak + jnp.log(jnp.sum(jnp.exp(value - peak), axis=0, keepdims=True))
            half = chunk // 2
            logs[slab, px, pc, 0] = log[:, :half]
            logs[slab, px, pc, 1] = log[:, half:]
            return unused

        lax.fori_loop(0, 4, one, 0)

    gather_slabs(rows_in, out, sems, work)


def gather_logits(rows, table, ints, valid, shard_rows, collective_id):
    own, width = rows.shape
    shape = sizes() + (own, width)
    return pl.pallas_call(
        functools.partial(logits_kernel, shard_rows),
        out_shape=(
            jax.ShapeDtypeStruct(shape, rows.dtype),
            jax.ShapeDtypeStruct(sizes() + (1, own), jnp.float32),
            jax.ShapeDtypeStruct((1, 2 * own), jnp.float32),
        ),
        in_specs=[VMEM] * 4,
        out_specs=(VMEM,) * 3,
        scratch_shapes=gather_sems(),
        cost_estimate=pl.CostEstimate(
            flops=0, bytes_accessed=108 * MIB, transcendentals=0
        ),
        compiler_params=pltpu.CompilerParams(
            collective_id=collective_id, has_side_effects=True,
            vmem_limit_bytes=lax.axis_size("z") * 2 * MIB + 20 * MIB,
        ),
    )(rows, table, ints, valid)


def embed_back_kernel(shard_rows, parts, rows_in, ints, table_grad, smalls, *refs):
    packs, refs = refs[:parts], refs[parts:]
    out, small_sum, squares, refs = refs[0], refs[1], refs[2], refs[3:]
    pack_sums, refs = refs[:parts], refs[parts:]
    slabs, small_got, refs = refs[0], refs[1], refs[2:]
    buffers, sems = refs[: 4 * parts], refs[4 * parts :]
    extent = out.shape[0]
    chunk = 2 * rows_in.shape[0]
    small_send, small_recv = sems[-6:-4]
    n_z, n_x, n_c, n_y = sizes()
    count = n_z * n_x * n_c * n_y
    me = index_after(0)
    greet_all()

    def small(step):
        return remote(
            smalls.at[index_after(step)], small_got.at[me], small_send.at[step], small_recv.at[step],
            device_after(step),
        )

    def each(action):
        def body(step, unused):
            action(step)
            return unused

        lax.fori_loop(1, count, body, 0)

    each(lambda step: small(step).start())
    beside, close_line = line_sums(packs, pack_sums, buffers, sems[-4:])
    small_got[me] = smalls[me]
    out[...] = table_grad[...]

    def work(slab):
        for pc in range(2):
            token = in_lane(ints, slab, pc, 0).astype(jnp.int32)
            hot = vocab_ids(extent, 2 * chunk, shard_rows) == token
            hot = jnp.where(hot, 1.0, 0.0).astype(jnp.bfloat16)
            out[...] += matmul(hot, slabs[slab, :, pc].reshape(2 * chunk, -1))

    gather_slabs(rows_in, slabs, sems[:-6], work, beside)
    close_line()
    each(lambda step: small(step).wait())
    small_sum[...] = jnp.sum(small_got[...], axis=0)
    value = out[...]
    inside = lax.broadcasted_iota(jnp.int32, value.shape, 0) < shard_rows
    squares[...] = jnp.sum(jnp.where(inside, value * value, 0.0), axis=0, keepdims=True)
    for part in pack_sums:
        value = part[...].reshape(-1, part.shape[-1])
        squares[:, : part.shape[-1]] += jnp.sum(value * value, axis=0, keepdims=True)


def embed_back(rows, ints, table_grad, smalls, packs, shard_rows, collective_id):
    own, width = rows.shape
    count = smalls.shape[0]
    dma = pltpu.SemaphoreType.DMA
    return pl.pallas_call(
        functools.partial(embed_back_kernel, shard_rows, len(packs)),
        out_shape=(
            jax.ShapeDtypeStruct(table_grad.shape, jnp.float32),
            jax.ShapeDtypeStruct(smalls.shape[1:], jnp.float32),
            jax.ShapeDtypeStruct((1, width), jnp.float32),
        )
        + tuple(jax.ShapeDtypeStruct(pack.shape[2:], jnp.float32) for pack in packs),
        in_specs=[VMEM] * (4 + len(packs)),
        out_specs=(VMEM,) * (3 + len(packs)),
        scratch_shapes=[
            pltpu.VMEM(sizes() + (own, width), rows.dtype), pltpu.VMEM(smalls.shape, jnp.float32),
        ]
        + [pltpu.VMEM(pack.shape[1:], pack.dtype) for pack in packs for _ in range(4)]
        + gather_sems() + [dma((count,)), dma((count,))] + line_sems(len(packs)),
        cost_estimate=pl.CostEstimate(
            flops=0, bytes_accessed=120 * MIB, transcendentals=0
        ),
        compiler_params=pltpu.CompilerParams(
            collective_id=collective_id, has_side_effects=True,
            vmem_limit_bytes=lax.axis_size("z") * 2 * MIB + 28 * MIB,
        ),
    )(rows, ints, table_grad, smalls, *packs)


def slab_order():
    n_z = lax.axis_size("z")
    z = lax.axis_index("z")
    up, down = n_z - 1 - z, z
    longer, shorter = jnp.maximum(up, down), jnp.minimum(up, down)
    far_side = jnp.where(up >= down, 1, -1)

    def target(step):
        late = step - (longer - shorter)
        near_side = jnp.where(late % 2 == 0, far_side, -far_side)
        return jnp.where(
            late < 0, z + far_side * (longer - step), z + near_side * (shorter - late // 2)
        )

    return target


def scatter_scratch(rows, width):
    n_z, n_x, n_c, n_y = sizes()
    half = rows // 2
    low = jnp.bfloat16
    dma = pltpu.SemaphoreType.DMA
    return [
        pltpu.VMEM((n_z, n_x, n_y, rows, width), low),
        pltpu.VMEM((n_z, n_x, n_y, rows, width), low),
        pltpu.VMEM((n_z, n_x, n_y, rows, width), low),
        pltpu.VMEM((n_z, 2, half, width), low),
        pltpu.VMEM((n_z, 2, half, width), low),
        pltpu.VMEM((n_z, half, width), low),
        pltpu.VMEM((n_z, half, width), low),
        pltpu.VMEM((n_z, rows, width), low),
        pltpu.VMEM((n_z, rows, width), low),
        dma((n_z, 2)), dma((n_z, 2)), dma((n_z, 3)), dma((n_z, 3)), dma((n_z, 3)),
        dma((n_z, 3)), dma((n_z, 2)), dma((n_z, 2, 2)),
    ]


def scatter_slabs(out, scratch, before, make, after, beside=lambda step: None):
    (
        lanes, handed, c_got, x_got, y_got, x_last, y_last, below, above,
        c_send, c_recv, x_send, x_recv, y_send, y_recv, z_send, z_recv,
    ) = scratch
    n_z = lax.axis_size("z")
    rows = out.shape[0]
    half = rows // 2
    (z, x, c, y), x_near, y_near, c_near = around()
    halves = (pl.ds(0, half), pl.ds(half, half))
    low, high = halves
    target = slab_order()

    def c_copy(slab, px):
        return remote(
            handed.at[slab, px], c_got.at[slab, px], c_send.at[slab, px], c_recv.at[slab, px], c_near
        )

    def x_first(slab, part):
        block = lanes.at[slab, 1 - x, y if part == 0 else 1 - y, low]
        return remote(block, x_got.at[slab, part], x_send.at[slab, part], x_recv.at[slab, part], x_near)

    def y_first(slab, part):
        block = lanes.at[slab, x if part == 0 else 1 - x, 1 - y, high]
        return remote(block, y_got.at[slab, part], y_send.at[slab, part], y_recv.at[slab, part], y_near)

    def y_second(slab):
        block = lanes.at[slab, x, 1 - y, low]
        return remote(block, y_last.at[slab], y_send.at[slab, 2], y_recv.at[slab, 2], y_near)

    def x_second(slab):
        block = lanes.at[slab, 1 - x, y, high]
        return remote(block, x_last.at[slab], x_send.at[slab, 2], x_recv.at[slab, 2], x_near)

    def z_up(slab, part):
        return remote(
            lanes.at[slab, x, y, halves[part]], below.at[slab, halves[part]], z_send.at[slab, part],
            z_recv.at[slab, 0, part], (z + 1, x, c, y),
        )

    def z_down(slab, part):
        return remote(
            lanes.at[slab, x, y, halves[part]], above.at[slab, halves[part]], z_send.at[slab, part],
            z_recv.at[slab, 1, part], (z - 1, x, c, y),
        )

    def produce(step):
        slab = target(step)
        before(step)

        mine = make(step, slab, 1 - c)
        for px in range(2):
            handed[slab, px] = mine[px]
            c_copy(slab, px).start()
        mine = make(step, slab, c)
        for px in range(2):
            lanes[slab, px] = mine[px]

    def begin(step):
        slab = target(step)
        for px in range(2):
            c_copy(slab, px).wait_recv()

        def merge(px, py):
            lanes[slab, px, py] = total_of(lanes[slab, px, py], c_got[slab, px, py]).astype(jnp.bfloat16)

        merge(1 - x, 1 - y)
        x_first(slab, 1).start()
        y_first(slab, 1).start()
        merge(1 - x, y)
        x_first(slab, 0).start()
        merge(x, 1 - y)
        y_first(slab, 0).start()
        merge(x, y)
        after(step)

    def middle(step):
        slab = target(step)
        x_first(slab, 1).wait_recv()
        x_first(slab, 0).wait_send()
        y_first(slab, 0).wait_send()
        lanes[slab, x, 1 - y, low] = total_of(
            lanes[slab, x, 1 - y, low], x_got[slab, 1]
        ).astype(jnp.bfloat16)
        y_second(slab).start()
        y_first(slab, 1).wait_recv()
        lanes[slab, 1 - x, y, high] = total_of(
            lanes[slab, 1 - x, y, high], y_got[slab, 1]
        ).astype(jnp.bfloat16)
        x_second(slab).start()

    def finish(step):
        slab = target(step)
        for part in range(2):
            if part == 0:
                x_first(slab, 0).wait_recv()
                y_second(slab).wait_recv()
                value = total_of(lanes[slab, x, y, low], x_got[slab, 0], y_last[slab])
            else:
                y_first(slab, 0).wait_recv()
                x_second(slab).wait_recv()
                value = total_of(lanes[slab, x, y, high], y_got[slab, 0], x_last[slab])
            rows_of = halves[part]

            @pl.when(slab > z)
            def _():
                @pl.when(z == 0)
                def _():
                    lanes[slab, x, y, rows_of] = value.astype(jnp.bfloat16)

                @pl.when(z > 0)
                def _():
                    z_up(slab, part).wait_recv()
                    lanes[slab, x, y, rows_of] = total_of(value, below[slab, rows_of]).astype(jnp.bfloat16)

                z_up(slab, part).start()

            @pl.when(slab < z)
            def _():
                @pl.when(z == n_z - 1)
                def _():
                    lanes[slab, x, y, rows_of] = value.astype(jnp.bfloat16)

                @pl.when(z < n_z - 1)
                def _():
                    z_down(slab, part).wait_recv()
                    lanes[slab, x, y, rows_of] = total_of(value, above[slab, rows_of]).astype(jnp.bfloat16)

                z_down(slab, part).start()

            @pl.when(slab == z)
            def _():
                out[rows_of, :] = value

                @pl.when(z > 0)
                def _():
                    z_up(slab, part).wait_recv()
                    out[rows_of, :] += below[slab, rows_of].astype(jnp.float32)

                @pl.when(z < n_z - 1)
                def _():
                    z_down(slab, part).wait_recv()
                    out[rows_of, :] += above[slab, rows_of].astype(jnp.float32)

    def turn(step, unused):
        for action, back in ((produce, 0), (begin, 0), (middle, 1), (finish, 2)):

            @pl.when((step >= back) & (step < n_z + back))
            def _():
                action(step - back)

        beside(step)
        return unused

    lax.fori_loop(0, n_z + 2, turn, 0)

    def close(slab, unused):
        for px in range(2):
            c_copy(slab, px).wait_send()
        x_first(slab, 1).wait_send()
        y_first(slab, 1).wait_send()
        x_second(slab).wait_send()
        y_second(slab).wait_send()
        for part in range(2):

            @pl.when(slab > z)
            def _():
                z_up(slab, part).wait_send()

            @pl.when(slab < z)
            def _():
                z_down(slab, part).wait_send()

        return unused

    lax.fori_loop(0, n_z, close, 0)


def embed_kernel(shard_rows, table, ints, qkv_own, out_own, out, qkv_all, out_all, *scratch):
    extent = table.shape[0]
    chunk = 2 * out.shape[0]
    greet_near()
    beside, close = line_gather(
        (qkv_own, out_own),
        (lambda pz, pc: qkv_all.at[:, pz, :, pc], lambda pz, pc: out_all.at[:, pz, pc]),
        scratch[-5:],
    )

    def make(step, slab, pc):
        token = in_lane(ints, slab, pc, 0).astype(jnp.int32)
        hot = vocab_ids(extent, 2 * chunk, shard_rows) == token
        hot = jnp.where(hot, 1.0, 0.0).astype(jnp.bfloat16)
        return inner(hot, table[...]).astype(jnp.bfloat16).reshape(2, 2, chunk // 2, -1)

    scatter_slabs(out, scratch[:-5], lambda step: None, make, lambda step: None, beside)
    close()


def embed(table, ints, qkv_own, out_own, own, shard_rows, collective_id):
    width = table.shape[1]
    n_z, n_x, n_c, _ = sizes()
    layers = qkv_own.shape[0]
    return pl.pallas_call(
        functools.partial(embed_kernel, shard_rows),
        out_shape=(
            jax.ShapeDtypeStruct((own, width), jnp.float32),
            jax.ShapeDtypeStruct((layers, n_z, n_x, n_c) + qkv_own.shape[2:], qkv_own.dtype),
            jax.ShapeDtypeStruct((layers, n_z, n_c) + out_own.shape[1:], out_own.dtype),
        ),
        in_specs=[VMEM] * 4,
        out_specs=(VMEM,) * 3,
        scratch_shapes=scatter_scratch(own, width) + line_gather_sems(),
        cost_estimate=pl.CostEstimate(
            flops=0, bytes_accessed=120 * MIB, transcendentals=0
        ),
        compiler_params=pltpu.CompilerParams(
            collective_id=collective_id, has_side_effects=True,
            vmem_limit_bytes=lax.axis_size("z") * 3 * MIB + 12 * MIB,
        ),
    )(table, ints, qkv_own, out_own)


def vocab_back_kernel(
    shard_rows, held, rows_all, table, ints, logs, weights, out, table_grad, slab_rows, changes, slab_sem, *scratch
):
    extent, width = table.shape
    chunk = 2 * out.shape[0]
    scale = width ** (-0.5)
    n_z = lax.axis_size("z")
    target = slab_order()

    def load(step):
        return pltpu.make_async_copy(
            rows_all.at[target(step)], slab_rows.at[step % 2], slab_sem.at[step % 2]
        )

    if not held:
        load(0).start()
    greet_near()
    table_grad[...] = jnp.zeros_like(table_grad)

    def rows_of(step, pc):
        if held:
            return rows_all[target(step), :, pc].reshape(2 * chunk, width)
        return slab_rows[step % 2, :, pc].reshape(2 * chunk, width)

    def before(step):
        if held:
            return
        load(step).wait()

        @pl.when(step + 1 < n_z)
        def _():
            load(step + 1).start()

    def make(step, slab, pc):
        value = outer(table[...], rows_of(step, pc)) * scale
        aim = in_lane(ints, slab, pc, 1).astype(jnp.int32)
        hot = jnp.where(vocab_ids(extent, 2 * chunk, shard_rows) == aim, 1.0, 0.0)
        change = jnp.exp(value - in_lane(logs, slab, pc, 0)) - hot
        change = (change * in_lane(weights, slab, pc, 0)).astype(jnp.bfloat16)
        changes[pc] = change
        return (inner(change, table[...]) * scale).astype(jnp.bfloat16).reshape(2, 2, chunk // 2, width)

    def after(step):
        for pc in range(2):
            table_grad[...] += matmul(changes[pc], rows_of(step, pc))

    scatter_slabs(out, scratch, before, make, after)
    table_grad[...] = table_grad[...] * scale


def vocab_back(rows_all, table, ints, logs, weights, shard_rows, collective_id):
    own, width = rows_all.shape[4:]
    extent = table.shape[0]
    n_z, n_x, n_c, n_y = sizes()
    held = n_z <= 4
    return pl.pallas_call(
        functools.partial(vocab_back_kernel, shard_rows, held),
        out_shape=(
            jax.ShapeDtypeStruct((own, width), jnp.float32),
            jax.ShapeDtypeStruct((extent, width), jnp.float32),
        ),
        in_specs=[VMEM if held else ANY] + [VMEM] * 4,
        out_specs=(VMEM,) * 2,
        scratch_shapes=[
            pltpu.VMEM((1,) * 6 if held else (2, n_x, n_c, n_y, own, width), rows_all.dtype),
            pltpu.VMEM((n_c, extent, 4 * own), jnp.bfloat16),
            pltpu.SemaphoreType.DMA((2,)),
        ] + scatter_scratch(own, width),
        cost_estimate=pl.CostEstimate(
            flops=0, bytes_accessed=144 * MIB, transcendentals=0
        ),
        compiler_params=pltpu.CompilerParams(
            collective_id=collective_id, has_side_effects=True,
            vmem_limit_bytes=n_z * 3 * MIB + 24 * MIB if n_z <= 8 else 62 * MIB,
        ),
    )(rows_all, table, ints, logs, weights)


SQRT_HALF = 0.5**0.5
DENSITY = 0.3989422804014327


def matmul(left, right):
    return jnp.dot(left, right, preferred_element_type=jnp.float32)


def inner(left, right):
    return lax.dot_general(
        left, right, (((0,), (0,)), ((), ())), preferred_element_type=jnp.float32
    )


def outer(left, right):
    return lax.dot_general(
        left, right, (((1,), (1,)), ((), ())), preferred_element_type=jnp.float32
    )


def plane_gather(own_rows, blocks, send_sem, recv_sem):
    half = own_rows.shape[0] // 2
    (z, x, c, y), x_near, y_near, _ = around()
    low, high = pl.ds(0, half), pl.ds(half, half)

    def copy(slot, px, py, rows, source, device):
        target = blocks.at[px, py, rows]
        return remote(target if source is None else source.at[rows], target, send_sem.at[slot], recv_sem.at[slot], device)

    first = [
        copy(0, x, y, low, own_rows, x_near),
        copy(1, x, y, high, own_rows, y_near),
        copy(2, x, y, high, own_rows, x_near),
        copy(3, x, y, low, own_rows, y_near),
    ]
    relays = [copy(4, 1 - x, y, low, None, y_near), copy(5, x, 1 - y, high, None, x_near)]
    for each in first:
        each.start()

    def wait_near():
        first[0].wait_recv()
        relays[0].start()
        first[1].wait_recv()
        relays[1].start()

    def wait_x():
        first[2].wait_recv()

    def wait_y():
        first[3].wait_recv()

    def wait_diagonal():
        for each in relays:
            each.wait_recv()

    def close():
        for each in first + relays:
            each.wait_send()

    return wait_near, wait_x, wait_y, wait_diagonal, close


def plane_sum(parts, got, out, send_sem, recv_sem):
    (z, x, c, y), x_near, y_near, _ = around()
    diagonal = (z, 1 - x, c, 1 - y)
    copies = [
        remote(parts.at[device[1], device[3]], got.at[slot], send_sem.at[slot], recv_sem.at[slot], device)
        for slot, device in enumerate((x_near, y_near, diagonal))
    ]

    def close():
        for each in copies:
            each.wait_recv()
        out[...] = total_of(parts[x, y], got[0], got[1], got[2])
        for each in copies:
            each.wait_send()

    return copies, close


def order_experts(kept, got, ordered, sems):
    n_z, n_c, _, depth, _ = kept.shape
    x = lax.axis_index("x")
    copies = []
    for pz in range(n_z):
        for pc in range(n_c):
            for side, weights in enumerate((kept, got)):
                if depth == ordered.shape[1]:
                    rows, side = pl.ds(0, depth), 0
                else:
                    px = x if side == 0 else 1 - x
                    at = (pz * 2 + px) * n_c + pc
                    rows = pl.ds(pl.multiple_of(at * depth, 16), depth)
                slot = (pz * n_c + pc) * 2 + side
                if depth == ordered.shape[1] and weights is got:
                    continue
                copies.append(
                    pltpu.make_async_copy(weights.at[pz, pc], ordered.at[:, rows], sems.at[slot])
                )
    for copy in copies:
        copy.start()
    return copies


def experts_kernel(
    own_rows, route, w_kept, w_got, out, wide, before, hidden, ordered, parts, got, w_sem, g_send, g_recv, s_send, s_recv
):
    (z, x, c, y), x_near, y_near, _ = around()
    diagonal = (z, 1 - x, c, 1 - y)
    loads = order_experts(w_kept, w_got, ordered, w_sem)
    up, down = ordered.at[pl.ds(0, 2)], ordered.at[pl.ds(2, 2)]
    greet((x_near, y_near, diagonal))
    wait_near, wait_x, wait_y, wait_diagonal, close = plane_gather(own_rows, wide, g_send, g_recv)
    copies, finish = plane_sum(parts, got, out, s_send, s_recv)
    wide[x, y] = own_rows[...]

    def work(px, py):
        rows = wide[px, py]
        first = route[px, py] == 0
        value = jnp.where(first, matmul(rows, up[0]), matmul(rows, up[1]))
        before[px, py] = value
        active = 0.5 * value * (1.0 + lax.erf(value * SQRT_HALF))
        hidden_first = jnp.where(first, active, 0.0).astype(jnp.bfloat16)
        hidden_second = jnp.where(first, 0.0, active).astype(jnp.bfloat16)
        hidden[px, py] = active.astype(jnp.bfloat16)
        total = outer(hidden_first, down[0]) + outer(hidden_second, down[1])
        parts[px, py] = total.astype(jnp.bfloat16)

    for load in loads:
        load.wait()
    work(x, y)
    wait_near()
    wait_x()
    work(1 - x, y)
    copies[0].start()
    wait_y()
    work(x, 1 - y)
    copies[1].start()
    wait_diagonal()
    work(1 - x, 1 - y)
    copies[2].start()
    finish()
    close()


def experts(own_rows, route, weights, collective_id):
    _, n_x, _, n_y = sizes()
    own, width = own_rows.shape
    wide = weights[0].shape[4]
    dma = pltpu.SemaphoreType.DMA
    low = jnp.bfloat16
    return pl.pallas_call(
        experts_kernel,
        out_shape=(
            jax.ShapeDtypeStruct((own, width), jnp.float32),
            jax.ShapeDtypeStruct((n_x, n_y, own, width), low),
            jax.ShapeDtypeStruct((n_x, n_y, own, wide), jnp.float32),
            jax.ShapeDtypeStruct((n_x, n_y, own, wide), low),
        ),
        in_specs=[VMEM, VMEM, HBM, HBM],
        out_specs=(VMEM,) * 4,
        scratch_shapes=[
            pltpu.VMEM((4, width, wide), low),
            pltpu.VMEM((n_x, n_y, own, width), low),
            pltpu.VMEM((3, own, width), low),
            dma((width // weights[0].shape[3],)), dma((6,)), dma((6,)), dma((3,)), dma((3,)),
        ],
        compiler_params=pltpu.CompilerParams(
            collective_id=collective_id, has_side_effects=True, vmem_limit_bytes=20 * MIB
        ),
        cost_estimate=pl.CostEstimate(
            flops=8 * own * 4 * width * wide, bytes_accessed=54 * MIB, transcendentals=4 * own * wide
        ),
    )(own_rows, route, *weights)


def experts_back_kernel(
    own_rows, route, w_kept, w_got, wide_kept, before_kept, hidden_kept, out, grads,
    ordered, wide, before, hidden, made, wide_grad, before_grad, parts, got,
    w_sem, k_sem, o_sem, g_send, g_recv, s_send, s_recv,
):
    (z, x, c, y), x_near, y_near, _ = around()
    diagonal = (z, 1 - x, c, 1 - y)
    loads = order_experts(w_kept, w_got, ordered, w_sem)
    for slot, (source, target) in enumerate(
        ((before_kept, before), (wide_kept, wide), (hidden_kept, hidden))
    ):
        load = pltpu.make_async_copy(source, target, k_sem.at[slot])
        load.start()
        loads.append(load)
    up, down = ordered.at[pl.ds(0, 2)], ordered.at[pl.ds(2, 2)]
    greet((x_near, y_near, diagonal))
    wait_near, wait_x, wait_y, wait_diagonal, close = plane_gather(own_rows, wide_grad, g_send, g_recv)
    copies, finish = plane_sum(parts, got, out, s_send, s_recv)
    wide_grad[x, y] = own_rows[...]

    def work(px, py):
        rows = wide_grad[px, py]
        first = route[px, py] == 0
        hidden_grad = jnp.where(first, matmul(rows, down[0]), matmul(rows, down[1]))
        value = before[px, py]
        slope = 0.5 * (1.0 + lax.erf(value * SQRT_HALF)) + value * (
            DENSITY * jnp.exp(-0.5 * value * value)
        )
        change = (hidden_grad * slope).astype(jnp.bfloat16)
        before_grad[px, py] = change
        change_first = jnp.where(first, change, 0)
        change_second = jnp.where(first, 0, change)
        total = outer(change_first, up[0]) + outer(change_second, up[1])
        parts[px, py] = total.astype(jnp.bfloat16)

    for load in loads:
        load.wait()
    work(x, y)
    wait_near()
    wait_x()
    work(1 - x, y)
    copies[0].start()
    wait_y()
    work(x, 1 - y)
    copies[1].start()
    wait_diagonal()
    work(1 - x, 1 - y)
    copies[2].start()
    close()

    lane = 4 * own_rows.shape[0]
    rows = wide[...].reshape(lane, -1)
    grad_rows = wide_grad[...].reshape(lane, -1)
    first = route[...].reshape(lane, 1) == 0
    change = before_grad[...].reshape(lane, -1)
    active = hidden[...].reshape(lane, -1)
    low = jnp.bfloat16
    n_z, n_x, n_c, _ = sizes()
    depth = grads.shape[3]
    saves = []

    def keep(slot, value):
        value = value.astype(low)
        for pz in range(n_z):
            for px in range(n_x):
                for pc in range(n_c):
                    start = ((pz * n_x + px) * n_c + pc) * depth
                    made[slot, pz * n_c + pc, px] = value[start : start + depth]
        save = pltpu.make_async_copy(made.at[slot], grads.at[:, :, slot], o_sem.at[slot])
        save.start()
        saves.append(save)

    keep(0, inner(rows, jnp.where(first, change, 0)))
    keep(1, inner(rows, jnp.where(first, 0, change)))
    keep(2, inner(grad_rows, jnp.where(first, active, 0)))
    keep(3, inner(grad_rows, jnp.where(first, 0, active)))
    finish()
    for save in saves:
        save.wait()


def experts_back(own_rows, route, weights, wide, before, hidden, collective_id):
    n_z, n_x, n_c, n_y = sizes()
    own, width = own_rows.shape
    units = weights[0].shape[4]
    dma = pltpu.SemaphoreType.DMA
    low = jnp.bfloat16
    return pl.pallas_call(
        experts_back_kernel,
        out_shape=(
            jax.ShapeDtypeStruct((own, width), jnp.float32),
            jax.ShapeDtypeStruct((n_z * n_c, n_x, 4, width // (n_z * n_x * n_c), units), low),
        ),
        in_specs=[VMEM, VMEM] + [HBM] * 5,
        out_specs=(VMEM, HBM),
        scratch_shapes=[
            pltpu.VMEM((4, width, units), low),
            pltpu.VMEM(wide.shape, wide.dtype), pltpu.VMEM(before.shape, before.dtype),
            pltpu.VMEM(hidden.shape, hidden.dtype),
            pltpu.VMEM((4, n_z * n_c, n_x, width // (n_z * n_x * n_c), units), low),
            pltpu.VMEM((n_x, n_y, own, width), low),
            pltpu.VMEM((n_x, n_y, own, units), low),
            pltpu.VMEM((n_x, n_y, own, width), low),
            pltpu.VMEM((3, own, width), low),
            dma((width // weights[0].shape[3],)), dma((3,)), dma((4,)), dma((6,)), dma((6,)), dma((3,)), dma((3,)),
        ],
        compiler_params=pltpu.CompilerParams(
            collective_id=collective_id, has_side_effects=True, vmem_limit_bytes=34 * MIB
        ),
        cost_estimate=pl.CostEstimate(
            flops=16 * own * 4 * width * units, bytes_accessed=54 * MIB, transcendentals=8 * own * units
        ),
    )(own_rows, route, *weights, wide, before, hidden)


def in_owner_order(value, target):
    value = value.astype(target.dtype)
    n_c, n_z = target.shape[:2]
    n_x = target.shape[2] if len(target.shape) == 5 else 1
    depth = target.shape[-2]
    for pz in range(n_z):
        for px in range(n_x):
            for pc in range(n_c):
                start = ((pz * n_x + px) * n_c + pc) * depth
                if len(target.shape) == 5:
                    target[pc, pz, px] = value[start : start + depth]
                else:
                    target[pc, pz] = value[start : start + depth]


def project_kernel(transposed, with_grad, *refs):
    if with_grad:
        rows, weight, left, out, grad, parts, got, s_send, s_recv = refs
    else:
        rows, weight, out, parts, got, s_send, s_recv = refs
    (z, x, c, y), x_near, y_near, _ = around()
    diagonal = (z, 1 - x, c, 1 - y)
    barrier = pltpu.get_barrier_semaphore()
    for device in (x_near, y_near, diagonal):
        pl.semaphore_signal(barrier, inc=1, device_id=device, device_id_type=MESH)
    copies, finish = plane_sum(parts, got, out, s_send, s_recv)

    def work(px, py):
        times = outer if transposed else matmul
        parts[px, py] = times(rows[px, py], weight[...]).astype(jnp.bfloat16)

    work(1 - x, 1 - y)
    pl.semaphore_wait(barrier, 3)
    copies[2].start()
    work(1 - x, y)
    copies[0].start()
    work(x, 1 - y)
    copies[1].start()
    work(x, y)
    if with_grad:
        lane = 4 * out.shape[0]
        in_owner_order(inner(left[...].reshape(lane, -1), rows[...].reshape(lane, -1)), grad)
    finish()


def project(rows, weight, transposed, left, collective_id):
    n_x, n_y, own, depth = rows.shape
    n_z, _, n_c, _ = sizes()
    width = weight.shape[0] if transposed else weight.shape[1]
    low = jnp.bfloat16
    dma = pltpu.SemaphoreType.DMA
    return pl.pallas_call(
        functools.partial(project_kernel, transposed, left is not None),
        out_shape=(jax.ShapeDtypeStruct((own, width), jnp.float32),)
        + (
            ()
            if left is None
            else (
                jax.ShapeDtypeStruct(
                    (n_c, n_z, n_x, left.shape[3] // (n_z * n_x * n_c), depth), low
                ),
            )
        ),
        in_specs=[VMEM] * (2 if left is None else 3),
        out_specs=(VMEM,) * (1 if left is None else 2),
        scratch_shapes=[
            pltpu.VMEM((n_x, n_y, own, width), low), pltpu.VMEM((3, own, width), low), dma((3,)), dma((3,)),
        ],
        compiler_params=pltpu.CompilerParams(
            collective_id=collective_id, has_side_effects=True, vmem_limit_bytes=16 * MIB
        ),
        cost_estimate=pl.CostEstimate(
            flops=8 * own * width * depth, bytes_accessed=24 * MIB, transcendentals=0
        ),
    )(rows, weight, *(() if left is None else (left,)))


def gather_project_kernel(transposed, split, with_grad, own_rows, weight, *rest):
    if with_grad:
        left, wide, rest = rest[0], rest[1], (rest[0],) + rest[2:]
    else:
        wide, rest = rest[0], rest[1:]

    (z, x, c, y), x_near, y_near, _ = around()
    rest, (g_send, g_recv) = rest[:-2], rest[-2:]
    left, outs = (rest[0], rest[1:]) if with_grad else (None, rest)
    greet((x_near, y_near))
    wait_near, wait_x, wait_y, wait_diagonal, close = plane_gather(own_rows, wide, g_send, g_recv)
    wide[x, y] = own_rows[...]

    def work(px, py):
        times = outer if transposed else matmul
        value = times(wide[px, py], weight[...]).astype(jnp.bfloat16)
        start = 0
        for out, size in zip(outs, split):
            out[px, py] = value[:, start : start + size]
            start += size

    work(x, y)
    wait_near()
    wait_x()
    work(1 - x, y)
    wait_y()
    work(x, 1 - y)
    wait_diagonal()
    work(1 - x, 1 - y)
    if with_grad:
        lane = 4 * own_rows.shape[0]
        in_owner_order(inner(left[...], wide[...].reshape(lane, -1)), outs[-1])
    close()


def gather_project(own_rows, weight, transposed, split, left, collective_id):
    n_z, n_x, n_c, n_y = sizes()
    own, width = own_rows.shape
    depth = weight.shape[0] if transposed else weight.shape[1]
    dma = pltpu.SemaphoreType.DMA
    low = jnp.bfloat16
    return pl.pallas_call(
        functools.partial(gather_project_kernel, transposed, split, left is not None),
        out_shape=(
            jax.ShapeDtypeStruct((n_x, n_y, own, width), low),
        ) + tuple(jax.ShapeDtypeStruct((n_x, n_y, own, size), low) for size in split)
        + (
            ()
            if left is None
            else (jax.ShapeDtypeStruct((n_c, n_z, left.shape[1] // (n_z * n_c), width), low),)
        ),
        in_specs=[VMEM] * (2 if left is None else 3),
        out_specs=(VMEM,) * (1 + len(split) + (0 if left is None else 1)),
        scratch_shapes=[dma((6,)), dma((6,))],
        compiler_params=pltpu.CompilerParams(
            collective_id=collective_id, has_side_effects=True, vmem_limit_bytes=12 * MIB
        ),
        cost_estimate=pl.CostEstimate(
            flops=8 * own * width * depth, bytes_accessed=24 * MIB, transcendentals=0
        ),
    )(own_rows, weight, *(() if left is None else (left,)))


def merge_logs_kernel(source, out, got, mine, send_one, recv_one, send_two, recv_two):
    n_z, n_x, n_c, n_y = sizes()
    count = n_z * n_x * n_c * n_y
    z, x, c, y = place()
    me = ((z * n_x + x) * n_c + c) * n_y + y

    def device_of(index):
        return (
            index // (n_x * n_c * n_y), index // (n_c * n_y) % n_x, index // n_y % n_c, index % n_y
        )

    barrier = pltpu.get_barrier_semaphore()

    def call(step, unused):
        other = lax.rem(me + step, count)
        pl.semaphore_signal(barrier, inc=1, device_id=device_of(other), device_id_type=MESH)
        return unused

    lax.fori_loop(1, count, call, 0)
    got[me] = source[me]
    pl.semaphore_wait(barrier, count - 1)

    def first(step):
        other = lax.rem(me + step, count)
        return remote(
            source.at[other], got.at[me], send_one.at[step], recv_one.at[step], device_of(other)
        )

    def second(step):
        other = lax.rem(me + step, count)
        return remote(mine, out.at[me], send_two.at[step], recv_two.at[step], device_of(other))

    def each(action):
        def body(step, unused):
            action(step)
            return unused

        lax.fori_loop(1, count, body, 0)

    each(lambda step: first(step).start())
    each(lambda step: first(step).wait())
    values = got[...]
    peak = jnp.max(values, axis=0)
    mine[...] = peak + jnp.log(jnp.sum(jnp.exp(values - peak[None]), axis=0))
    out[me] = mine[...]
    each(lambda step: second(step).start())
    each(lambda step: second(step).wait())


def merge_logs(blocks, collective_id):
    count = blocks.shape[0]
    dma = pltpu.SemaphoreType.DMA
    return pl.pallas_call(
        merge_logs_kernel,
        out_shape=jax.ShapeDtypeStruct(blocks.shape, blocks.dtype),
        in_specs=[VMEM],
        out_specs=VMEM,
        scratch_shapes=[
            pltpu.VMEM(blocks.shape, blocks.dtype), pltpu.VMEM(blocks.shape[1:], blocks.dtype),
            dma((count,)), dma((count,)), dma((count,)), dma((count,)),
        ],
        cost_estimate=pl.CostEstimate(
            flops=0, bytes_accessed=42 * MIB, transcendentals=0
        ),
        compiler_params=pltpu.CompilerParams(
            collective_id=collective_id, has_side_effects=True, vmem_limit_bytes=8 * MIB
        ),
    )(blocks)


def key_position(index, part, chunk):
    lane = 2 * chunk
    start = (part // 2) * (2 * lane) + (part % 2) * chunk
    return start + index + jnp.where(index >= chunk, chunk, 0)


def as_column(row):
    wide_row = jnp.broadcast_to(row.astype(jnp.float32), (8, row.shape[1]))
    return wide_row.T[:, :1].astype(jnp.int32)


def near_shown(side, chunk, query_pos, query_seg, near_pos, near_seg):
    columns = slice(side * chunk, (side + 1) * chunk)
    rows = slice(2 * side * chunk, 2 * (side + 1) * chunk)
    shown = (
        (near_seg[rows, :] == query_seg[:, columns])
        & (near_pos[rows, :] <= query_pos[:, columns])
        & (near_pos[rows, :] >= PROMPT)
    )
    return columns, rows, shown


def attend_kernel(
    chunk, query, far, near, query_pos, query_seg, near_pos, near_seg,
    out, out_low, log_total, scores, far_t, near_t,
):
    lane, feature = query.shape
    group = feature // HEAD_DIM
    prompt_rows = far.shape[0]
    parts = prompt_rows // lane
    query_t = (query[...].astype(jnp.float32) * HEAD_DIM ** (-0.5)).T.astype(jnp.bfloat16)
    far_t[...] = far[...].astype(jnp.float32).T.astype(jnp.bfloat16)
    near_t[...] = near[...].astype(jnp.float32).T.astype(jnp.bfloat16)
    row_of = lax.broadcasted_iota(jnp.int32, (feature, lane), 0)
    q_pos = query_pos[...]
    near_pos, near_seg = as_column(near_pos[...]), as_column(near_seg[...])

    for head in range(group):
        low, high = head * HEAD_DIM, (head + 1) * HEAD_DIM
        query_h = jnp.where((row_of >= low) & (row_of < high), query_t, 0)

        def score_part(part, peak):
            block = far[pl.ds(pl.multiple_of(part * lane, lane), lane), :feature]
            value = matmul(block, query_h)
            index = lax.broadcasted_iota(jnp.int32, (lane, lane), 0)
            value = jnp.where(key_position(index, part, chunk) <= q_pos, value, MASKED)
            scores[pl.ds(pl.multiple_of(part * lane, lane), lane), :] = value
            return jnp.maximum(peak, jnp.max(value, axis=0, keepdims=True))

        peak = lax.fori_loop(0, parts, score_part, jnp.full((1, lane), MASKED, jnp.float32))
        near_peaks = []
        for side in range(2):
            columns, rows, shown = near_shown(side, chunk, query_pos, query_seg, near_pos, near_seg)
            value = matmul(near[rows, :feature], query_h[:, columns])
            value = jnp.where(shown, value, MASKED)
            scores[prompt_rows : prompt_rows + lane, columns] = value
            near_peaks.append(jnp.max(value, axis=0, keepdims=True))
        peak = jnp.maximum(peak, jnp.concatenate(near_peaks, axis=1))

        def weigh_part(part, state):
            total, mixed = state
            start = pl.multiple_of(part * lane, lane)
            chance = jnp.exp(scores[pl.ds(start, lane), :] - peak)
            total = total + jnp.sum(chance, axis=0, keepdims=True)
            mixed = mixed + matmul(
                far_t[feature + low : feature + high, pl.ds(start, lane)],
                chance.astype(jnp.bfloat16),
            )
            return total, mixed

        total, mixed = lax.fori_loop(
            0,
            parts,
            weigh_part,
            (jnp.zeros((1, lane), jnp.float32), jnp.zeros((HEAD_DIM, lane), jnp.float32)),
        )
        near_total, near_mixed = [], []
        for side in range(2):
            columns = slice(side * chunk, (side + 1) * chunk)
            rows = slice(side * lane, (side + 1) * lane)
            chance = jnp.exp(scores[prompt_rows : prompt_rows + lane, columns] - peak[:, columns])
            near_total.append(jnp.sum(chance, axis=0, keepdims=True))
            near_mixed.append(
                matmul(near_t[feature + low : feature + high, rows], chance.astype(jnp.bfloat16))
            )
        total = total + jnp.concatenate(near_total, axis=1)
        mixed = mixed + jnp.concatenate(near_mixed, axis=1)
        out[low:high, :] = mixed / total
        log_total[head : head + 1, :] = peak + jnp.log(total)
    out_low[...] = out[...].T.astype(jnp.bfloat16)


def attend(queries, far, near, places, chunk):
    lane, feature = queries.shape
    prompt_rows = far.shape[0]
    group = feature // HEAD_DIM
    total_rows = prompt_rows + lane
    return pl.pallas_call(
        functools.partial(attend_kernel, chunk),
        out_shape=(
            jax.ShapeDtypeStruct((feature, lane), jnp.float32),
            jax.ShapeDtypeStruct((lane, feature), jnp.bfloat16),
            jax.ShapeDtypeStruct((group, lane), jnp.float32),
        ),
        in_specs=[VMEM] * 7,
        out_specs=(VMEM,) * 3,
        scratch_shapes=[
            pltpu.VMEM((total_rows, lane), jnp.float32),
            pltpu.VMEM((2 * feature, prompt_rows), jnp.bfloat16),
            pltpu.VMEM((2 * feature, 2 * lane), jnp.bfloat16),
        ],
        compiler_params=pltpu.CompilerParams(vmem_limit_bytes=20 * MIB),
        cost_estimate=pl.CostEstimate(
            flops=8 * group * lane * total_rows * 128,
            bytes_accessed=8 * MIB,
            transcendentals=group * lane * total_rows,
        ),
    )(queries, far, near, *places)


def attend_back_kernel(
    chunk, query, far, near, query_pos, query_seg, near_pos, near_seg,
    log_total, mixed, answer, query_grad, far_grad, near_grad,
    far_t, near_t, far_values, near_values, far_sum, near_sum, query_sum,
):
    lane, feature = query.shape
    group = feature // HEAD_DIM
    prompt_rows = far.shape[0]
    parts = prompt_rows // lane
    scaled = (query[...].astype(jnp.float32) * HEAD_DIM ** (-0.5)).astype(jnp.bfloat16)
    query_t = scaled.astype(jnp.float32).T.astype(jnp.bfloat16)
    answers = answer[...]
    answer_t = answers.astype(jnp.float32).T.astype(jnp.bfloat16)
    far_t[...] = far[:, :feature].astype(jnp.float32).T.astype(jnp.bfloat16)
    near_t[...] = near[:, :feature].astype(jnp.float32).T.astype(jnp.bfloat16)
    far_values[...] = far[:, feature:]
    near_values[...] = near[:, feature:]
    row_of = lax.broadcasted_iota(jnp.int32, (feature, lane), 0)
    column_of = lax.broadcasted_iota(jnp.int32, (lane, feature), 1)
    q_pos = query_pos[...]
    near_pos, near_seg = as_column(near_pos[...]), as_column(near_seg[...])

    for head in range(group):
        low, high = head * HEAD_DIM, (head + 1) * HEAD_DIM
        in_rows = (row_of >= low) & (row_of < high)
        in_columns = (column_of >= low) & (column_of < high)
        query_ht = jnp.where(in_rows, query_t, 0)
        answer_ht = jnp.where(in_rows, answer_t, 0)
        query_h = jnp.where(in_columns, scaled, 0)
        answer_h = jnp.where(in_columns, answers, 0)
        log_h = log_total[head : head + 1, :]
        delta_h = jnp.sum(
            answer_t[low:high, :].astype(jnp.float32) * mixed[low:high, :], axis=0, keepdims=True
        )

        def slopes(key_block, value_block, shown, columns):
            value = matmul(key_block, query_ht[:, columns])
            chance = jnp.exp(jnp.where(shown, value - log_h[:, columns], MASKED))
            slope = matmul(value_block, answer_ht[:, columns])
            change = (chance * (slope - delta_h[:, columns])).astype(jnp.bfloat16)
            chance = chance.astype(jnp.bfloat16)
            return change, matmul(change, query_h[columns]), matmul(chance, answer_h[columns])

        def add(sums, rows, key_part, value_part):
            if head == 0:
                sums[0, rows, :] = key_part
                sums[1, rows, :] = value_part
            else:
                sums[0, rows, :] += key_part
                sums[1, rows, :] += value_part

        def back_part(part, total):
            rows = pl.ds(pl.multiple_of(part * lane, lane), lane)
            index = lax.broadcasted_iota(jnp.int32, (lane, lane), 0)
            shown = key_position(index, part, chunk) <= q_pos
            change, key_part, value_part = slopes(
                far[rows, :feature], far_values[rows, :], shown, slice(0, lane)
            )
            add(far_sum, rows, key_part, value_part)
            return total + matmul(far_t[low:high, rows], change)

        total = lax.fori_loop(0, parts, back_part, jnp.zeros((HEAD_DIM, lane), jnp.float32))
        near_total = []
        for side in range(2):
            columns, rows, shown = near_shown(side, chunk, query_pos, query_seg, near_pos, near_seg)
            change, key_part, value_part = slopes(
                near[rows, :feature], near_values[rows, :], shown, columns
            )
            add(near_sum, rows, key_part, value_part)
            near_total.append(matmul(near_t[low:high, rows], change))
        query_sum[low:high, :] = (total + jnp.concatenate(near_total, axis=1)) * HEAD_DIM ** (-0.5)
    query_grad[...] = query_sum[...].T.astype(jnp.bfloat16)
    for sums, grad in ((far_sum, far_grad), (near_sum, near_grad)):
        grad[...] = jnp.concatenate(
            [sums[0].astype(jnp.bfloat16), sums[1].astype(jnp.bfloat16)], axis=1
        )


def attend_back(queries, far, near, places, log_total, mixed, answer, chunk):
    lane, feature = queries.shape
    prompt_rows = far.shape[0]
    group = feature // HEAD_DIM
    total_rows = prompt_rows + lane
    low = jnp.bfloat16
    return pl.pallas_call(
        functools.partial(attend_back_kernel, chunk),
        out_shape=(
            jax.ShapeDtypeStruct((lane, feature), low),
            jax.ShapeDtypeStruct((prompt_rows, 2 * feature), low),
            jax.ShapeDtypeStruct((2 * lane, 2 * feature), low),
        ),
        in_specs=[VMEM] * 10,
        out_specs=(VMEM,) * 3,
        scratch_shapes=[
            pltpu.VMEM((feature, prompt_rows), low),
            pltpu.VMEM((feature, 2 * lane), low),
            pltpu.VMEM((prompt_rows, feature), low),
            pltpu.VMEM((2 * lane, feature), low),
            pltpu.VMEM((2, prompt_rows, feature), jnp.float32),
            pltpu.VMEM((2, 2 * lane, feature), jnp.float32),
            pltpu.VMEM((feature, lane), jnp.float32),
        ],
        compiler_params=pltpu.CompilerParams(vmem_limit_bytes=28 * MIB),
        cost_estimate=pl.CostEstimate(
            flops=20 * group * lane * total_rows * 128,
            bytes_accessed=12 * MIB,
            transcendentals=group * lane * total_rows,
        ),
    )(queries, far, near, *places, log_total, mixed, answer)


def head_places(back):
    n_z, n_x, n_c, n_y = sizes()
    line = n_z * n_c
    pairs = []
    for device in range(line * n_x * n_y):
        group, at = device // line, device % line
        place_of = ((at // n_c * n_x + group // n_y) * n_c + at % n_c) * n_y + group % n_y
        pairs.append((place_of, device) if back else (device, place_of))
    return tuple(pairs)


def pad_rows(block):
    return jnp.pad(block, ((0, 8 - block.shape[0]), (0, 0)))


def adam_update(weight, moment_one, moment_two, gradient, step_rate, decay_rate):
    first_new = BETA_ONE * moment_one + (1.0 - BETA_ONE) * gradient
    second_new = BETA_TWO * moment_two + (1.0 - BETA_TWO) * gradient * gradient
    normalized = (
        first_new
        / (1.0 - BETA_ONE**STEP)
        / (jnp.sqrt(second_new / (1.0 - BETA_TWO**STEP)) + ADAM_EPS)
    )
    return (weight - step_rate * (normalized + decay_rate * weight), first_new, second_new)


def per_device(
    token_ids,
    targets,
    valid_mask,
    cont_lengths,
    routes,
    vocab_table,
    vocab_first,
    vocab_second,
    attn_weights,
    attn_first,
    attn_second,
    router,
    router_first,
    router_second,
    norm_gains,
    gains_first,
    gains_second,
    expert_up,
    up_first,
    up_second,
    expert_down,
    down_first,
    down_second,
):
    slabs = lax.axis_size("z")
    planes = lax.axis_size("x")
    cores = lax.axis_size("core")
    sides = lax.axis_size("head")
    groups = planes * sides
    z_at, x_at, core_at, side_at = (lax.axis_index(name) for name in ALL)
    blk_at = (z_at * planes + x_at) * cores + core_at
    device_at = blk_at * sides + side_at
    group_at = x_at * sides + side_at
    tokens = valid_mask.shape[0]
    chunk = token_ids.shape[0]
    own = chunk // sides
    lane = planes * chunk
    feature = D // groups
    wide = expert_up.shape[3] // planes
    shard_rows = vocab_table.shape[0]
    logit_scale = D ** (-0.5)

    cont_ends = jnp.cumsum(cont_lengths)
    valid_f = valid_mask.astype(jnp.float32)
    token_count = jnp.sum(valid_mask).astype(jnp.float32)
    expert_ids = jnp.arange(EXPERTS, dtype=jnp.int32)

    own_ints = jnp.concatenate([token_ids[None], targets[None], routes], axis=0)
    own_ints = lax.dynamic_slice_in_dim(own_ints, side_at * own, own, axis=1).astype(jnp.float32)
    rows_of = attn_weights.shape[1]
    smalls = jnp.concatenate(
        [router.transpose(0, 2, 1).reshape(LAYERS * EXPERTS, rows_of), norm_gains], axis=0
    )
    smalls = smalls.astype(jnp.bfloat16).astype(jnp.float32)
    smalls = jnp.pad(smalls, ((0, 16 - smalls.shape[0]), (0, own - rows_of)))
    whole_f = swap(jnp.concatenate([pad_rows(own_ints), smalls], axis=0)[None], True, 1)
    attn_low = attn_weights.astype(jnp.bfloat16)
    qkv_send = attn_low[:, :, : 3 * D].reshape(LAYERS, rows_of, 3, groups, feature)
    qkv_send = jnp.concatenate([qkv_send[:, :, 1:], qkv_send[:, :, :1]], axis=2)
    qkv_send = qkv_send.transpose(3, 0, 1, 2, 4).reshape(groups, LAYERS, rows_of, 3 * feature)
    qkv_got = lax.all_to_all(qkv_send, PLANE, split_axis=0, concat_axis=0, tiled=True)
    out_rows = lax.ppermute(attn_low[:, :, 3 * D :], ALL, head_places(False))
    expert_send = jnp.stack([expert_up, expert_down], axis=1).astype(jnp.bfloat16)
    depth = expert_send.shape[3]
    expert_send = expert_send.reshape(LAYERS, 2 * EXPERTS, depth, planes, wide)
    expert_send = expert_send.transpose(3, 0, 1, 2, 4)
    expert_halves = []
    for layer_index in range(LAYERS):
        kept_half = lax.dynamic_index_in_dim(expert_send[:, layer_index], x_at, 0, False)
        sent_half = lax.dynamic_index_in_dim(expert_send[:, layer_index], 1 - x_at, 0, False)
        got_half = lax.ppermute(sent_half, "x", ((0, 1), (1, 0)))
        expert_halves.append((kept_half, got_half))
    got_halves = [got_half for _, got_half in expert_halves]
    whole_f, qkv_got, out_rows, got_halves = lax.optimization_barrier(
        (whole_f, qkv_got, out_rows, got_halves)
    )
    expert_halves = [(kept_half, got) for (kept_half, _), got in zip(expert_halves, got_halves)]
    qkv_own = qkv_got.reshape(planes, sides, LAYERS, rows_of, 3 * feature).transpose(2, 0, 1, 3, 4)
    qkv_own = qkv_own.reshape(LAYERS, planes, sides * rows_of, 3 * feature)

    def gather_experts(kept_half, got_half):
        if depth % 16 == 0:
            return lax.all_gather(kept_half, LINE, axis=0).reshape(
                (slabs, cores) + kept_half.shape
            ), lax.all_gather(got_half, LINE, axis=0).reshape((slabs, cores) + kept_half.shape)
        halves = jnp.stack(
            [jnp.where(x_at == 0, kept_half, got_half), jnp.where(x_at == 0, got_half, kept_half)]
        )
        block = lax.all_gather(halves, LINE, axis=0)
        block = block.reshape(slabs, cores, planes, 2 * EXPERTS, depth, wide)
        block = block.transpose(3, 0, 2, 1, 4, 5).reshape(1, 1, 2 * EXPERTS, D, wide)
        return block, block

    expert_weights = [gather_experts(*expert_halves[0])]
    ints = whole_f.reshape(sizes() + whole_f.shape[1:])
    whole = whole_f[:, : 2 + LAYERS].astype(jnp.int32)
    smalls = whole_f[:, 8:, :rows_of].transpose(1, 0, 2).reshape(16, D)
    router_all = smalls[: LAYERS * EXPERTS].reshape(LAYERS, EXPERTS, D).transpose(0, 2, 1)
    router_all = router_all.astype(jnp.bfloat16)
    gains_f = smalls[LAYERS * EXPERTS :]
    routes_lane = lax.dynamic_index_in_dim(
        whole.reshape(slabs, planes, cores, sides, 2 + LAYERS, own), z_at, 0, False
    )
    routes_lane = lax.dynamic_index_in_dim(routes_lane, core_at, 1, False)[:, :, 2:]
    routes_lane = routes_lane.transpose(2, 0, 1, 3)[..., None]
    routes_own = lax.dynamic_slice_in_dim(routes, side_at * own, own, axis=1)

    extent = -(-shard_rows // 256) * 256
    table = jnp.pad(vocab_table.astype(jnp.bfloat16), ((0, extent - shard_rows), (0, 0)))
    offsets = jnp.arange(chunk, dtype=jnp.int32)
    first_blk = z_at * planes * cores + core_at
    query_pos = jnp.concatenate([(first_blk + cores * part) * chunk + offsets for part in range(planes)])
    near_blks = [first_blk - 1 + part for part in range(2 * planes)]
    near_pos = jnp.concatenate([blk * chunk + offsets for blk in near_blks])
    query_seg = segment_of(query_pos, cont_ends)
    near_seg = segment_of(near_pos, cont_ends)
    places = (query_pos[None, :], query_seg[None, :], near_pos[None, :], near_seg[None, :])

    stream, qkv_all, out_all = embed(table, ints, qkv_own, out_rows, own, shard_rows, 2)
    qkv_weights = [qkv_all[layer_index].reshape(D, 3 * feature) for layer_index in range(LAYERS)]
    out_weights = [out_all[layer_index].reshape(feature, D) for layer_index in range(LAYERS)]

    kept = []
    for layer_index in range(LAYERS):
        normed_lane, key_values, queries = gather_project(
            rms_norm(stream, gains_f[2 * layer_index : 2 * layer_index + 1]).astype(jnp.bfloat16),
            qkv_weights[layer_index], False, (2 * feature, feature), None, 3,
        )
        queries = queries.reshape(lane, feature)
        far, near = spread_keys(key_values.reshape(lane, 2 * feature), PROMPT, 10)
        if layer_index + 1 < LAYERS:
            far, halves = lax.optimization_barrier((far, expert_halves[layer_index + 1]))
            expert_weights.append(gather_experts(*halves))
        mixed_t, mixed_low, log_total = attend(queries, far, near, places, chunk)
        (attended,) = project(
            mixed_low.reshape(planes, sides, own, feature), out_weights[layer_index], False, None, 15
        )
        middle = stream + attended
        normed_two = rms_norm(middle, gains_f[2 * layer_index + 1 : 2 * layer_index + 2]).astype(jnp.bfloat16)
        chance = jax.nn.softmax(matmul(normed_two, router_all[layer_index]), axis=-1)
        output, wide_rows, before, hidden = experts(
            normed_two, routes_lane[layer_index], expert_weights[layer_index], 11
        )
        own_pick = (routes_own[layer_index][:, None] == expert_ids[None, :]).astype(jnp.float32)
        gate = jnp.sum(chance * own_pick, axis=1, keepdims=True)
        kept.append(
            (
                stream, normed_lane, queries, far, near, mixed_t, mixed_low, log_total, middle,
                normed_two, chance, wide_rows, before, hidden, output, own_pick, gate,
            )
        )
        stream = middle + gate * output

    final_gain = gains_f[2 * LAYERS : 2 * LAYERS + 1]
    devices = tokens // own
    valid_rows = valid_f.reshape(sizes() + (1, own))
    final_all, row_logs, hits = gather_logits(
        rms_norm(stream, final_gain).astype(jnp.bfloat16), table, ints, valid_rows, shard_rows, 4
    )
    log_sums = merge_logs(row_logs.reshape(devices, 1, own), 5)
    log_sum = log_sums.reshape(tokens)
    own_log = lax.dynamic_slice_in_dim(log_sum, device_at * own, own)
    own_valid = lax.dynamic_slice_in_dim(valid_f, device_at * own, own)
    own_loss = jnp.sum(own_log * own_valid) - jnp.sum(hits)
    final_grad, table_grad = vocab_back(
        final_all, table, ints, log_sums.reshape(sizes() + (1, own)), valid_rows / token_count,
        shard_rows, 6,
    )
    stream_grad, final_gain_grad = jax.vjp(rms_norm, stream, final_gain)[1](final_grad)

    qkv_packs = [None] * LAYERS
    out_packs = [None] * LAYERS
    router_list = [None] * LAYERS
    expert_sums = [None] * LAYERS
    gain_list = [None] * (2 * LAYERS + 1)
    gain_list[2 * LAYERS] = final_gain_grad
    for layer_index in reversed(range(LAYERS)):
        (
            stream, normed_lane, queries, far, near, mixed_t, mixed_low, log_total, middle,
            normed_two, chance, wide_rows, before, hidden, output, own_pick, gate,
        ) = kept[layer_index]
        out_grad = (gate * stream_grad).astype(jnp.bfloat16)
        chance_grad = jnp.sum(stream_grad * output, axis=1)[:, None] * own_pick
        choice_grad = chance * (chance_grad - jnp.sum(chance * chance_grad, axis=1, keepdims=True))
        router_list[layer_index] = jnp.dot(
            normed_two.astype(jnp.float32).T, choice_grad, precision=lax.Precision.HIGHEST
        )
        normed_grad = jnp.dot(
            choice_grad,
            router_all[layer_index].astype(jnp.float32).T,
            precision=lax.Precision.HIGHEST,
        )
        rows_grad, expert_grad = experts_back(
            out_grad, routes_lane[layer_index], expert_weights[layer_index], wide_rows, before,
            hidden, 12,
        )
        normed_grad = normed_grad + rows_grad
        middle_part, gain_list[2 * layer_index + 1] = jax.vjp(
            rms_norm, middle, gains_f[2 * layer_index + 1 : 2 * layer_index + 2]
        )[1](normed_grad)
        middle_grad = stream_grad + middle_part
        _, answer, out_packs[layer_index] = gather_project(
            middle_grad.astype(jnp.bfloat16), out_weights[layer_index], True, (feature,), mixed_low, 16
        )
        answer = answer.reshape(lane, feature)
        query_grad, far_grad, near_grad = attend_back(
            queries, far, near, places, log_total, mixed_t, answer, chunk
        )
        qkv_grad = collect_keys(far_grad, near_grad, query_grad, 13)
        qkv_grad, expert_grad = lax.optimization_barrier((qkv_grad, expert_grad))
        expert_sums[layer_index] = lax.psum_scatter(
            expert_grad, LINE, scatter_dimension=0, tiled=True
        )[0]
        normed_att_grad, qkv_packs[layer_index] = project(
            qkv_grad.reshape(planes, sides, own, 3 * feature), qkv_weights[layer_index], True,
            normed_lane, 14,
        )
        stream_part, gain_list[2 * layer_index] = jax.vjp(
            rms_norm, stream, gains_f[2 * layer_index : 2 * layer_index + 1]
        )[1](normed_att_grad)
        stream_grad = middle_grad + stream_part

    small = jnp.concatenate(
        [jnp.stack(router_list).transpose(1, 0, 2).reshape(D, -1), jnp.concatenate(gain_list, axis=0).T], axis=1
    )
    small = small.reshape(devices, rows_of, -1).transpose(0, 2, 1)
    small = jnp.pad(small, ((0, 0), (0, 16 - small.shape[1]), (0, 128 - rows_of)))
    table_share, small, near_squares, *attn_sums = embed_back(
        stream_grad.astype(jnp.bfloat16), ints, table_grad, small, qkv_packs + out_packs, shard_rows, 7
    )
    squares = sum(
        jnp.sum(jnp.square(part.astype(jnp.float32)))
        for part in [small[:, :rows_of]] + expert_sums
    ) + jnp.sum(near_squares)
    sums = jnp.pad(jnp.stack([squares, own_loss])[:, None], ((0, 6), (0, 127)))
    sums = jnp.sum(swap(sums[None], True, 9)[:, :2, 0], axis=0)
    square_total, loss_sum = sums[0], sums[1]
    expert_shares = []
    for expert_grad in expert_sums:
        kept_half = lax.dynamic_index_in_dim(expert_grad, x_at, 0, False)
        sent_half = lax.dynamic_index_in_dim(expert_grad, 1 - x_at, 0, False)
        got_half = lax.ppermute(sent_half, "x", ((0, 1), (1, 0)))
        expert_grad = jnp.concatenate(
            [jnp.where(x_at == 0, kept_half, got_half), jnp.where(x_at == 0, got_half, kept_half)],
            axis=-1,
        )
        expert_shares.append(
            expert_grad.reshape(2, EXPERTS, depth, planes * wide).astype(jnp.float32)
        )
    table_share, small = table_share[:shard_rows], small[:, :rows_of]
    router_share = (
        small[: LAYERS * EXPERTS].reshape(LAYERS, EXPERTS, rows_of).transpose(0, 2, 1)
    )
    gain_share = small[LAYERS * EXPERTS : LAYERS * EXPERTS + 2 * LAYERS + 1]
    qkv_share = jnp.stack(attn_sums[:LAYERS], axis=1).reshape(
        planes, LAYERS, sides, rows_of, 3 * feature
    )
    qkv_share = qkv_share.transpose(0, 2, 1, 3, 4).reshape(groups, LAYERS, rows_of, 3 * feature)
    qkv_share = lax.all_to_all(qkv_share, PLANE, split_axis=0, concat_axis=0, tiled=True)
    qkv_share = qkv_share.reshape(groups, LAYERS, rows_of, 3, feature)
    qkv_share = jnp.concatenate([qkv_share[:, :, :, 2:], qkv_share[:, :, :, :2]], axis=3)
    qkv_share = qkv_share.transpose(1, 2, 3, 0, 4).reshape(LAYERS, rows_of, 3 * D)
    out_share = lax.ppermute(jnp.stack(attn_sums[LAYERS:]), ALL, head_places(True))
    attn_share = jnp.concatenate([qkv_share, out_share], axis=2).astype(jnp.float32)
    up_share = jnp.stack([share[0] for share in expert_shares])
    down_share = jnp.stack([share[1] for share in expert_shares])
    shares = (table_share, attn_share, router_share, gain_share, up_share, down_share)
    grad_norm = jnp.sqrt(square_total)
    factor = CLIP_AT / jnp.maximum(grad_norm, CLIP_AT)
    weights = (vocab_table, attn_weights, router, norm_gains, expert_up, expert_down)
    firsts = (vocab_first, attn_first, router_first, gains_first, up_first, down_first)
    seconds = (vocab_second, attn_second, router_second, gains_second, up_second, down_second)
    results = [loss_sum, token_count, grad_norm]
    for number in range(6):
        results.extend(
            adam_update(
                weights[number],
                firsts[number],
                seconds[number],
                factor * shares[number],
                STEP_RATES[number],
                DECAY_RATES[number],
            )
        )
    return tuple(results)


def solution(mesh):
    blocks, sides = mesh.shape["blk"], mesh.shape["head"]
    fine = Mesh(mesh.devices.reshape(blocks // 4, 2, 2, sides), ALL)
    weight_specs = (
        (P(ALL, None),) * 3
        + (P(None, ALL, None),) * 3
        + (P(None, ALL, None),) * 3
        + (P(None, ALL),) * 3
        + (P(None, None, BLK, "head"),) * 6
    )
    return jax.shard_map(
        per_device,
        mesh=fine,
        in_specs=(P(BLK), P(BLK), P(), P(), P(None, BLK)) + weight_specs,
        out_specs=(P(), P(), P()) + weight_specs,
        check_vma=False,
    )
```

```python
import functools

import jax
import jax.numpy as jnp
from jax import lax
from jax.experimental import pallas as pl
from jax.experimental.pallas import tpu as pltpu
from jax.sharding import Mesh, PartitionSpec as P

D = 768
HEADS = 12
HEAD_DIM = 64
EXPERTS = 2
LAYERS = 2
PROMPT = 2048
STEP = 10

NORM_EPS = 1e-06
BETA_ONE = 0.9
BETA_TWO = 0.95
ADAM_EPS = 1e-08
CLIP_AT = 0.01
MASKED = -1e30
STEP_RATES = (2.0, 0.25, 0.04, 0.4, 0.04, 0.04)
DECAY_RATES = (0.01, 0.01, 0.01, 0.0, 0.01, 0.01)

ALL = ("z", "x", "core", "head")
BLK = ("z", "x", "core")
PLANE = ("x", "head")
LINE = ("z", "core")
MIB = 2**20
MESH = pl.DeviceIdType.MESH
ANY = pl.BlockSpec(memory_space=pl.ANY)
VMEM = pl.BlockSpec(memory_space=pltpu.VMEM)
HBM = pl.BlockSpec(memory_space=pltpu.HBM)


def rms_norm(stream, gain):
    return stream * lax.rsqrt(jnp.mean(stream * stream, axis=-1, keepdims=True) + NORM_EPS) * gain


def segment_of(position, cont_ends):
    later = jnp.sum((cont_ends[None, :] <= (position - PROMPT)[:, None]).astype(jnp.int32), axis=1)
    return jnp.where(position < PROMPT, 0, 1 + later)


def place():
    return tuple(lax.axis_index(name) for name in ALL)


def sizes():
    return tuple(lax.axis_size(name) for name in ALL)


def remote(source, target, send, receive, device):
    return pltpu.make_async_remote_copy(
        src_ref=source, dst_ref=target, send_sem=send, recv_sem=receive,
        device_id=device, device_id_type=MESH,
    )


def greet(devices):
    barrier = pltpu.get_barrier_semaphore()
    for device in devices:
        pl.semaphore_signal(barrier, inc=1, device_id=device, device_id_type=MESH)
    pl.semaphore_wait(barrier, len(devices))


def around():
    z, x, c, y = place()
    return (z, x, c, y), (z, 1 - x, c, y), (z, x, c, 1 - y), (z, x, 1 - c, y)


def swap_kernel(broadcast, source, out, send_sem, receive_sem, own_sem):
    n_z, n_x, n_c, n_y = sizes()
    count = n_z * n_x * n_c * n_y
    z, x, c, y = place()
    me = ((z * n_x + x) * n_c + c) * n_y + y

    def device_of(index):
        return (
            index // (n_x * n_c * n_y), index // (n_c * n_y) % n_x, index // n_y % n_c, index % n_y
        )

    def taken(index):
        return source.at[0] if broadcast else source.at[index]

    barrier = pltpu.get_barrier_semaphore()

    def call(step, unused):
        other = lax.rem(me + step, count)
        pl.semaphore_signal(barrier, inc=1, device_id=device_of(other), device_id_type=MESH)
        return unused

    lax.fori_loop(1, count, call, 0)
    own = pltpu.make_async_copy(taken(me), out.at[me], own_sem)
    own.start()
    pl.semaphore_wait(barrier, count - 1)

    def copy(step):
        other = lax.rem(me + step, count)
        return remote(
            taken(other), out.at[me], send_sem.at[step], receive_sem.at[step], device_of(other)
        )

    def start(step, unused):
        copy(step).start()
        return unused

    def finish(step, unused):
        copy(step).wait()
        return unused

    lax.fori_loop(1, count, start, 0)
    lax.fori_loop(1, count, finish, 0)
    own.wait()


def swap(blocks, broadcast, collective_id):
    count = 1
    for size in sizes():
        count *= size
    return pl.pallas_call(
        functools.partial(swap_kernel, broadcast),
        out_shape=jax.ShapeDtypeStruct((count,) + blocks.shape[1:], blocks.dtype),
        in_specs=[VMEM],
        out_specs=VMEM,
        scratch_shapes=[
            pltpu.SemaphoreType.DMA((count,)),
            pltpu.SemaphoreType.DMA((count,)),
            pltpu.SemaphoreType.DMA,
        ],
        cost_estimate=pl.CostEstimate(
            flops=0, bytes_accessed=36 * MIB, transcendentals=0
        ),
        compiler_params=pltpu.CompilerParams(
            collective_id=collective_id, has_side_effects=True, vmem_limit_bytes=8 * MIB
        ),
    )(blocks)


def total_of(*parts):
    total = parts[0].astype(jnp.float32)
    for part in parts[1:]:
        total = total + part.astype(jnp.float32)
    return total


PIECES = 4


def spread_kernel(
    prompt_slabs, own_rows, far, near, tail, z_send, z_recv, c_send, c_recv, n_send, n_recv, own_sem
):
    n_z = lax.axis_size("z")
    lane = own_rows.shape[0]
    chunk = lane // 2
    size = lane // PIECES
    (z, x, c, y), _, _, c_near = around()
    above, below = (z + 1, x, c, y), (z - 1, x, c, y)
    in_prompt = z < prompt_slabs
    takes_down = z < prompt_slabs - 1
    gives_down = (z > 0) & (z < prompt_slabs)

    barrier = pltpu.get_barrier_semaphore()
    pl.semaphore_signal(barrier, inc=1, device_id=c_near, device_id_type=MESH)

    @pl.when(z > 0)
    def _():
        pl.semaphore_signal(barrier, inc=1, device_id=below, device_id_type=MESH)

    @pl.when(takes_down)
    def _():
        pl.semaphore_signal(barrier, inc=1, device_id=above, device_id_type=MESH)

    first, second = pl.ds(0, chunk), pl.ds(chunk, chunk)
    own = [
        pltpu.make_async_copy(own_rows.at[first], near.at[1], own_sem.at[0]),
        pltpu.make_async_copy(own_rows.at[second], near.at[3], own_sem.at[1]),
    ]
    own_far = pltpu.make_async_copy(own_rows, far.at[jnp.minimum(z, prompt_slabs - 1), c], own_sem.at[2])
    own_edge = pltpu.make_async_copy(own_rows.at[first], near.at[0], own_sem.at[3])
    edge = (z == 0) & (c == 0)
    for copy in own:
        copy.start()

    @pl.when(in_prompt)
    def _():
        own_far.start()

    @pl.when(edge)
    def _():
        own_edge.start()

    pl.semaphore_wait(
        barrier, 1 + jnp.where(z < n_z - 1, 1, 0) + jnp.where(gives_down, 1, 0)
    )

    def part(index):
        return pl.ds(index * size, size)

    def z_copy(source, slab, index, up):
        return remote(
            source, far.at[slab, c, part(index)], z_send.at[slab, index, 1 if up else 0],
            z_recv.at[slab, index], above if up else below,
        )

    def c_copy(source, slab, index):
        return remote(
            source, far.at[slab, c, part(index)], c_send.at[slab, index], c_recv.at[slab, index], c_near
        )

    def t_copy():
        return remote(own_rows.at[second], tail, n_send.at[0], n_recv.at[0], above)

    def t_hand():
        return remote(tail, near.at[0], n_send.at[1], n_recv.at[1], c_near)

    def n_copy(half):
        slot = jnp.where(c == 0, 2 * half, 2)
        return remote(
            own_rows.at[pl.ds(half * chunk, chunk)], near.at[slot], n_send.at[2 + half], n_recv.at[2 + half],
            c_near,
        )

    @pl.when(in_prompt)
    def _():
        for index in range(PIECES):
            source = own_rows.at[part(index)]

            @pl.when(z < n_z - 1)
            def _():
                z_copy(source, z, index, True).start()

            @pl.when(z > 0)
            def _():
                z_copy(source, z, index, False).start()

            c_copy(source, z, index).start()

    @pl.when((c == 1) & (z < n_z - 1))
    def _():
        t_copy().start()

    n_copy(0).start()

    @pl.when(c == 0)
    def _():
        n_copy(1).start()

    for distance in range(1, n_z):
        low_slab, high_slab = z - distance, z + distance
        for index in range(PIECES):

            @pl.when((low_slab >= 0) & (low_slab < prompt_slabs))
            def _():
                source = far.at[low_slab, c, part(index)]
                z_copy(source, low_slab, index, True).wait_recv()

                @pl.when(z < n_z - 1)
                def _():
                    z_copy(source, low_slab, index, True).start()

                c_copy(source, low_slab, index).start()

            if distance < prompt_slabs:

                @pl.when(high_slab < prompt_slabs)
                def _():
                    source = far.at[high_slab, c, part(index)]
                    z_copy(source, high_slab, index, False).wait_recv()

                    @pl.when(z > 0)
                    def _():
                        z_copy(source, high_slab, index, False).start()

                    c_copy(source, high_slab, index).start()

    @pl.when((c == 1) & (z > 0))
    def _():
        t_copy().wait_recv()
        t_hand().start()
        t_hand().wait_send()

    @pl.when((c == 1) & (z < n_z - 1))
    def _():
        t_copy().wait_send()

    @pl.when((c == 0) & (z > 0))
    def _():
        t_hand().wait_recv()

    n_copy(0).wait_send()
    n_copy(0).wait_recv()

    @pl.when(c == 0)
    def _():
        n_copy(1).wait_send()

    @pl.when(c == 1)
    def _():
        n_copy(1).wait_recv()

    for slab in range(prompt_slabs):
        for index in range(PIECES):
            copy = c_copy(own_rows.at[part(index)], slab, index)
            copy.wait_send()
            copy.wait_recv()

            @pl.when((z < n_z - 1) & (slab <= z))
            def _():
                z_copy(own_rows.at[part(index)], slab, index, True).wait_send()

            @pl.when((z > 0) & (slab >= z))
            def _():
                z_copy(own_rows.at[part(index)], slab, index, False).wait_send()

    for copy in own:
        copy.wait()

    @pl.when(in_prompt)
    def _():
        own_far.wait()

    @pl.when(edge)
    def _():
        own_edge.wait()


def spread_keys(own_rows, prompt_rows, collective_id):
    lane, width = own_rows.shape
    slabs = prompt_rows // (2 * lane)
    dma = pltpu.SemaphoreType.DMA
    far, near, _ = pl.pallas_call(
        functools.partial(spread_kernel, slabs),
        out_shape=(
            jax.ShapeDtypeStruct((slabs, 2, lane, width), own_rows.dtype),
            jax.ShapeDtypeStruct((4, lane // 2, width), own_rows.dtype),
            jax.ShapeDtypeStruct((lane // 2, width), own_rows.dtype),
        ),
        in_specs=[VMEM],
        out_specs=(VMEM,) * 3,
        scratch_shapes=[
            dma((slabs, PIECES, 2)), dma((slabs, PIECES)), dma((slabs, PIECES)), dma((slabs, PIECES)),
            dma((4,)), dma((4,)), dma((4,)),
        ],
        cost_estimate=pl.CostEstimate(
            flops=0, bytes_accessed=60 * MIB, transcendentals=0
        ),
        compiler_params=pltpu.CompilerParams(
            collective_id=collective_id, has_side_effects=True, vmem_limit_bytes=12 * MIB
        ),
    )(own_rows)
    return far.reshape(prompt_rows, width), near.reshape(2 * lane, width)


def collect_kernel(
    prompt_slabs, far, near, query_grad, whole, out, own, c_got, z_got, n_got, tail_pass, tail_got,
    c_send, c_recv, z_send, z_recv, n_send, n_recv,
):
    n_z = lax.axis_size("z")
    lane = out.shape[0]
    chunk = lane // 2
    size = lane // PIECES
    (z, x, c, y), _, _, c_near = around()
    above, below = (z + 1, x, c, y), (z - 1, x, c, y)

    barrier = pltpu.get_barrier_semaphore()
    pl.semaphore_signal(barrier, inc=1, device_id=c_near, device_id_type=MESH)

    @pl.when(z < n_z - 1)
    def _():
        pl.semaphore_signal(barrier, inc=1, device_id=above, device_id_type=MESH)

    pl.semaphore_wait(barrier, 1 + jnp.where(z > 0, 1, 0))

    def part(index):
        return pl.ds(index * size, size)

    def c_copy(slab, index):
        return remote(
            far.at[slab, 1 - c, part(index)], c_got.at[slab, part(index)], c_send.at[slab, index],
            c_recv.at[slab, index], c_near,
        )

    def z_copy(slab, index):
        return remote(
            own.at[slab, part(index)], z_got.at[slab, part(index)], z_send.at[slab, index],
            z_recv.at[slab, index], below,
        )

    def n_copy(half):
        slot = jnp.where(c == 0, 2, 2 * half)
        return remote(near.at[slot], n_got.at[half], n_send.at[half], n_recv.at[half], c_near)

    def t_hand():
        return remote(near.at[0], tail_pass, n_send.at[2], n_recv.at[2], c_near)

    def t_copy():
        return remote(tail_pass, tail_got, n_send.at[3], n_recv.at[3], below)

    for slab in range(prompt_slabs):
        for index in range(PIECES):
            c_copy(slab, index).start()
    n_copy(0).start()

    @pl.when(c == 1)
    def _():
        n_copy(1).start()

    @pl.when((c == 0) & (z > 0))
    def _():
        t_hand().start()

    for slab in range(prompt_slabs):
        for index in range(PIECES):
            c_copy(slab, index).wait_recv()
            rows = part(index)
            mine = total_of(far[slab, c, rows, :], c_got[slab, rows, :])

            @pl.when((z == n_z - 1) & (z > slab))
            def _():
                own[slab, rows, :] = mine.astype(jnp.bfloat16)
                z_copy(slab, index).start()

            @pl.when((z < n_z - 1) & (z > slab))
            def _():
                z_copy(slab, index).wait_recv()
                own[slab, rows, :] = total_of(mine, z_got[slab, rows, :]).astype(jnp.bfloat16)
                z_copy(slab, index).start()

            @pl.when((z < n_z - 1) & (z == slab))
            def _():
                z_copy(slab, index).wait_recv()
                out[rows, :] = total_of(mine, z_got[slab, rows, :])

            @pl.when((z == n_z - 1) & (z == slab))
            def _():
                out[rows, :] = mine

    @pl.when((c == 1) & (z > 0))
    def _():
        t_hand().wait_recv()
        t_copy().start()

    @pl.when(z >= prompt_slabs)
    def _():
        out[...] = jnp.zeros_like(out)

    n_copy(0).wait_recv()
    first, second = pl.ds(0, chunk), pl.ds(chunk, chunk)
    out[first, :] += total_of(near[1], n_got[0])
    out[second, :] += near[3].astype(jnp.float32)

    @pl.when(c == 0)
    def _():
        n_copy(1).wait_recv()
        out[second, :] += n_got[1].astype(jnp.float32)

    @pl.when((c == 1) & (z < n_z - 1))
    def _():
        t_copy().wait_recv()
        out[second, :] += tail_got[...].astype(jnp.float32)

    whole[...] = jnp.concatenate([out[...].astype(jnp.bfloat16), query_grad[...]], axis=1)

    @pl.when((c == 1) & (z > 0))
    def _():
        t_copy().wait_send()

    @pl.when((c == 0) & (z > 0))
    def _():
        t_hand().wait_send()

    n_copy(0).wait_send()

    @pl.when(c == 1)
    def _():
        n_copy(1).wait_send()

    for slab in range(prompt_slabs):
        for index in range(PIECES):
            c_copy(slab, index).wait_send()

            @pl.when(z > slab)
            def _():
                z_copy(slab, index).wait_send()


def collect_keys(far, near, query_grad, collective_id):
    prompt_rows, width = far.shape
    lane = near.shape[0] // 2
    slabs = prompt_rows // (2 * lane)
    dma = pltpu.SemaphoreType.DMA
    low = jnp.bfloat16
    return pl.pallas_call(
        functools.partial(collect_kernel, slabs),
        out_shape=jax.ShapeDtypeStruct((lane, width + query_grad.shape[1]), low),
        in_specs=[VMEM] * 3,
        out_specs=VMEM,
        scratch_shapes=[
            pltpu.VMEM((lane, width), jnp.float32),
            pltpu.VMEM((slabs, lane, width), low),
            pltpu.VMEM((slabs, lane, width), low),
            pltpu.VMEM((slabs, lane, width), low),
            pltpu.VMEM((2, lane // 2, width), low),
            pltpu.VMEM((lane // 2, width), low),
            pltpu.VMEM((lane // 2, width), low),
            dma((slabs, PIECES)), dma((slabs, PIECES)), dma((slabs, PIECES)), dma((slabs, PIECES)),
            dma((4,)), dma((4,)),
        ],
        cost_estimate=pl.CostEstimate(
            flops=0, bytes_accessed=60 * MIB, transcendentals=0
        ),
        compiler_params=pltpu.CompilerParams(
            collective_id=collective_id, has_side_effects=True, vmem_limit_bytes=20 * MIB
        ),
    )(far.astype(low).reshape(slabs, 2, lane, width), near.astype(low).reshape(4, lane // 2, width), query_grad)


def greet_all():
    n_z, n_x, n_c, n_y = sizes()
    count = n_z * n_x * n_c * n_y
    barrier = pltpu.get_barrier_semaphore()

    def call(step, unused):
        pl.semaphore_signal(barrier, inc=1, device_id=device_after(step), device_id_type=MESH)
        return unused

    lax.fori_loop(1, count, call, 0)
    pl.semaphore_wait(barrier, count - 1)


def index_after(step):
    n_z, n_x, n_c, n_y = sizes()
    z, x, c, y = place()
    me = ((z * n_x + x) * n_c + c) * n_y + y
    return lax.rem(me + step, n_z * n_x * n_c * n_y)


def device_after(step):
    _, n_x, n_c, n_y = sizes()
    index = index_after(step)
    return (
        index // (n_x * n_c * n_y), index // (n_c * n_y) % n_x, index // n_y % n_c, index % n_y
    )


def greet_near():
    n_z = lax.axis_size("z")
    (z, x, c, y), x_near, y_near, c_near = around()
    barrier = pltpu.get_barrier_semaphore()
    for device in (x_near, y_near, c_near):
        pl.semaphore_signal(barrier, inc=1, device_id=device, device_id_type=MESH)

    @pl.when(z > 0)
    def _():
        pl.semaphore_signal(barrier, inc=1, device_id=(z - 1, x, c, y), device_id_type=MESH)

    @pl.when(z < n_z - 1)
    def _():
        pl.semaphore_signal(barrier, inc=1, device_id=(z + 1, x, c, y), device_id_type=MESH)

    pl.semaphore_wait(barrier, 3 + jnp.where(z > 0, 1, 0) + jnp.where(z < n_z - 1, 1, 0))


Z_PIECES = 4


def gather_sems():
    n_z = lax.axis_size("z")
    dma = pltpu.SemaphoreType.DMA
    return [
        dma((n_z, Z_PIECES, 2)), dma((n_z, Z_PIECES)), dma((n_z, 2)), dma((n_z, 2)), dma((n_z, 2)),
        dma((n_z, 2)), dma((n_z, 4)), dma((n_z, 4)), dma,
    ]


def gather_slabs(rows_in, out, sems, work, beside=lambda step: None):
    z_send, z_recv, x_send, x_recv, y_send, y_recv, c_send, c_recv, own_sem = sems
    n_z = lax.axis_size("z")
    half = rows_in.shape[0] // 2
    size = rows_in.shape[0] // Z_PIECES
    (z, x, c, y), x_near, y_near, c_near = around()
    low, high = pl.ds(0, half), pl.ds(half, half)
    everything = pl.ds(0, 2 * half)
    own = pltpu.make_async_copy(rows_in, out.at[z, x, c, y], own_sem)
    own.start()

    def block(origin, px, py, rows):
        return out.at[origin, px, c, py, rows]

    def z_copy(source, origin, index, up):
        rows = pl.ds(index * size, size)
        other = (z + 1, x, c, y) if up else (z - 1, x, c, y)
        return remote(
            source.at[rows], block(origin, x, y, rows), z_send.at[origin, index, 1 if up else 0],
            z_recv.at[origin, index], other,
        )

    def x_copy(source, origin):
        return remote(source, out.at[origin, x, c, y], x_send.at[origin, 0], x_recv.at[origin, 0], x_near)

    def y_copy(source, origin):
        return remote(source, out.at[origin, x, c, y], y_send.at[origin, 0], y_recv.at[origin, 0], y_near)

    def x_relay(origin):
        part = block(origin, x, 1 - y, high)
        return remote(part, part, x_send.at[origin, 1], x_recv.at[origin, 1], x_near)

    def y_relay(origin):
        part = block(origin, 1 - x, y, low)
        return remote(part, part, y_send.at[origin, 1], y_recv.at[origin, 1], y_near)

    def c_copy(source, origin, px, py):
        slot = px * 2 + py
        return remote(
            source, out.at[origin, px, c, py], c_send.at[origin, slot], c_recv.at[origin, slot], c_near
        )

    def column(origin):
        return out.at[origin, x, c, y]

    def spread(source, origin):
        x_copy(source, origin).start()
        y_copy(source, origin).start()
        c_copy(source, origin, x, y).start()

    def relay(origin):
        x_copy(column(origin), origin).wait_recv()
        y_relay(origin).start()
        y_copy(column(origin), origin).wait_recv()
        x_relay(origin).start()
        c_copy(block(origin, 1 - x, y, everything), origin, 1 - x, y).start()
        c_copy(block(origin, x, 1 - y, everything), origin, x, 1 - y).start()

    def finish(origin):
        x_relay(origin).wait_recv()
        y_relay(origin).wait_recv()
        c_copy(block(origin, 1 - x, 1 - y, everything), origin, 1 - x, 1 - y).start()

    def use(origin):
        for px in range(2):
            for py in range(2):
                c_copy(out.at[origin, px, c, py], origin, px, py).wait_recv()
        work(origin)

    def arrive(step):
        below, above = z - step, z + step

        @pl.when(below >= 0)
        def _():
            for index in range(Z_PIECES):
                z_copy(rows_in, below, index, True).wait_recv()

                @pl.when(z < n_z - 1)
                def _():
                    z_copy(column(below), below, index, True).start()

            spread(column(below), below)

        @pl.when(above < n_z)
        def _():
            for index in range(Z_PIECES):
                z_copy(rows_in, above, index, False).wait_recv()

                @pl.when(z > 0)
                def _():
                    z_copy(column(above), above, index, False).start()

            spread(column(above), above)

    for index in range(Z_PIECES):

        @pl.when(z < n_z - 1)
        def _():
            z_copy(rows_in, z, index, True).start()

        @pl.when(z > 0)
        def _():
            z_copy(rows_in, z, index, False).start()

    spread(rows_in, z)
    for step in range(1, n_z + 3):
        if step < n_z:
            arrive(step)
        for action, back in ((relay, 1), (finish, 2), (use, 3)):
            late = step - back
            if late == 0:
                if action is use:
                    own.wait()
                action(z)
            elif 0 < late < n_z:
                for origin in (z - late, z + late):

                    @pl.when((origin >= 0) & (origin < n_z))
                    def _():
                        action(origin)

        beside(step)

    def close(origin, unused):
        x_copy(rows_in, origin).wait_send()
        y_copy(rows_in, origin).wait_send()
        x_relay(origin).wait_send()
        y_relay(origin).wait_send()
        for px in range(2):
            for py in range(2):
                c_copy(out.at[origin, px, c, py], origin, px, py).wait_send()
        for index in range(Z_PIECES):

            @pl.when((z < n_z - 1) & (origin <= z))
            def _():
                z_copy(rows_in, origin, index, True).wait_send()

            @pl.when((z > 0) & (origin >= z))
            def _():
                z_copy(rows_in, origin, index, False).wait_send()

        return unused

    lax.fori_loop(0, n_z, close, 0)


def line_gather_sems():
    n_z = lax.axis_size("z")
    dma = pltpu.SemaphoreType.DMA
    return [dma((n_z, 2, 2)), dma((n_z, 2)), dma((n_z, 2)), dma((n_z, 2)), dma((2,))]


def line_gather(own_parts, all_parts, sems):
    z_send, z_recv, c_send, c_recv, own_sem = sems
    n_z = lax.axis_size("z")
    (z, x, c, y), _, _, c_near = around()
    numbers = range(len(own_parts))

    def z_copy(source, number, origin, up):
        return remote(
            source, all_parts[number](origin, c), z_send.at[origin, number, 1 if up else 0],
            z_recv.at[origin, number], (z + 1, x, c, y) if up else (z - 1, x, c, y),
        )

    def c_copy(source, number, origin):
        return remote(
            source, all_parts[number](origin, c), c_send.at[origin, number], c_recv.at[origin, number], c_near
        )

    own = [
        pltpu.make_async_copy(own_parts[number], all_parts[number](z, c), own_sem.at[number])
        for number in numbers
    ]
    for copy in own:
        copy.start()
    for number in numbers:
        source = own_parts[number]

        @pl.when(z < n_z - 1)
        def _():
            z_copy(source, number, z, True).start()

        @pl.when(z > 0)
        def _():
            z_copy(source, number, z, False).start()

        c_copy(source, number, z).start()

    def beside(step):
        below, above = z - step, z + step

        @pl.when((step >= 1) & (below >= 0))
        def _():
            for number in numbers:
                source = all_parts[number](below, c)
                z_copy(source, number, below, True).wait_recv()

                @pl.when(z < n_z - 1)
                def _():
                    z_copy(source, number, below, True).start()

                c_copy(source, number, below).start()

        @pl.when((step >= 1) & (above < n_z))
        def _():
            for number in numbers:
                source = all_parts[number](above, c)
                z_copy(source, number, above, False).wait_recv()

                @pl.when(z > 0)
                def _():
                    z_copy(source, number, above, False).start()

                c_copy(source, number, above).start()

    def close():
        for copy in own:
            copy.wait()

        def one(origin, unused):
            for number in numbers:
                c_copy(own_parts[number], number, origin).wait()

                @pl.when((z < n_z - 1) & (origin <= z))
                def _():
                    z_copy(own_parts[number], number, origin, True).wait_send()

                @pl.when((z > 0) & (origin >= z))
                def _():
                    z_copy(own_parts[number], number, origin, False).wait_send()

            return unused

        lax.fori_loop(0, n_z, one, 0)

    return beside, close


def line_sems(parts):
    n_z = lax.axis_size("z")
    dma = pltpu.SemaphoreType.DMA
    return [dma((parts,)), dma((parts,)), dma((n_z, 2, parts)), dma((n_z, 2, parts))]


def line_sums(packs, outs, buffers, sems):
    c_send, c_recv, z_send, z_recv = sems
    n_z = lax.axis_size("z")
    (z, x, c, y), _, _, c_near = around()
    numbers = range(len(packs))
    lanes, got, below, above = (buffers[each :: 4] for each in range(4))
    handed = [
        remote(packs[each].at[1 - c], got[each], c_send.at[each], c_recv.at[each], c_near)
        for each in numbers
    ]

    def z_copy(slab, up, each):
        return remote(
            lanes[each].at[slab], (below if up else above)[each].at[slab],
            z_send.at[slab, 1 if up else 0, each], z_recv.at[slab, 1 if up else 0, each],
            (z + 1, x, c, y) if up else (z - 1, x, c, y),
        )

    for copy in handed:
        copy.start()

    def merge():
        for each in numbers:
            handed[each].wait()
            lanes[each][...] = total_of(packs[each][c], got[each][...]).astype(jnp.bfloat16)

    def hop(turn, step):
        high, low = n_z - 1 - turn, turn

        @pl.when((z == step - 1 - turn) & (z < high))
        def _():
            for each in numbers:

                @pl.when(z > 0)
                def _():
                    z_copy(high, True, each).wait_recv()
                    lanes[each][high] = total_of(lanes[each][high], below[each][high]).astype(jnp.bfloat16)

                z_copy(high, True, each).start()

        @pl.when((n_z - 1 - z == step - 1 - turn) & (z > low))
        def _():
            for each in numbers:

                @pl.when(z < n_z - 1)
                def _():
                    z_copy(low, False, each).wait_recv()
                    lanes[each][low] = total_of(lanes[each][low], above[each][low]).astype(jnp.bfloat16)

                z_copy(low, False, each).start()

    def beside(step):
        if step == 1:
            merge()
        if step < n_z:

            def body(turn, unused):
                hop(turn, step)
                return unused

            lax.fori_loop(0, n_z - 1, body, 0)

    def close():
        for each in numbers:
            out = outs[each]
            out[...] = lanes[each][z].astype(jnp.float32)

            @pl.when(z > 0)
            def _():
                z_copy(z, True, each).wait_recv()
                out[...] += below[each][z].astype(jnp.float32)

            @pl.when(z < n_z - 1)
            def _():
                z_copy(z, False, each).wait_recv()
                out[...] += above[each][z].astype(jnp.float32)

        def sent(slab, unused):
            for each in numbers:

                @pl.when(slab > z)
                def _():
                    z_copy(slab, True, each).wait_send()

                @pl.when(slab < z)
                def _():
                    z_copy(slab, False, each).wait_send()

            return unused

        lax.fori_loop(0, n_z, sent, 0)

    return beside, close


def in_pairs(values, slab, px, pc, row):
    return jnp.concatenate([values[slab, px, pc, py, row : row + 1, :] for py in range(2)], axis=1)


def in_lane(values, slab, pc, row):
    return jnp.concatenate([in_pairs(values, slab, px, pc, row) for px in range(2)], axis=1)


def vocab_ids(extent, chunk, shard_rows):
    n_z, n_x, n_c, n_y = sizes()
    z, x, c, y = place()
    me = ((z * n_x + x) * n_c + c) * n_y + y
    rows = lax.broadcasted_iota(jnp.int32, (extent, chunk), 0)
    return rows + me * shard_rows


def logits_kernel(shard_rows, rows_in, table, ints, valid, out, logs, hits, *sems):
    extent = table.shape[0]
    chunk = 2 * rows_in.shape[0]
    scale = table.shape[1] ** (-0.5)
    greet_near()
    hits[...] = jnp.zeros_like(hits)

    def work(slab):
        def one(index, unused):
            px, pc = index // 2, index % 2
            rows = out[slab, px, pc].reshape(chunk, -1)
            value = outer(table[...], rows) * scale
            ids = vocab_ids(extent, chunk, shard_rows)
            inside = lax.broadcasted_iota(jnp.int32, (extent, chunk), 0) < shard_rows
            target = in_pairs(ints, slab, px, pc, 1).astype(jnp.int32)
            shown = in_pairs(valid, slab, px, pc, 0)
            hit = jnp.where(ids == target, value, 0.0)
            hits[...] += jnp.sum(hit, axis=0, keepdims=True) * shown
            value = jnp.where(inside, value, MASKED)
            peak = jnp.max(value, axis=0, keepdims=True)
            log = peak + jnp.log(jnp.sum(jnp.exp(value - peak), axis=0, keepdims=True))
            half = chunk // 2
            logs[slab, px, pc, 0] = log[:, :half]
            logs[slab, px, pc, 1] = log[:, half:]
            return unused

        lax.fori_loop(0, 4, one, 0)

    gather_slabs(rows_in, out, sems, work)


def gather_logits(rows, table, ints, valid, shard_rows, collective_id):
    own, width = rows.shape
    shape = sizes() + (own, width)
    return pl.pallas_call(
        functools.partial(logits_kernel, shard_rows),
        out_shape=(
            jax.ShapeDtypeStruct(shape, rows.dtype),
            jax.ShapeDtypeStruct(sizes() + (1, own), jnp.float32),
            jax.ShapeDtypeStruct((1, 2 * own), jnp.float32),
        ),
        in_specs=[VMEM] * 4,
        out_specs=(VMEM,) * 3,
        scratch_shapes=gather_sems(),
        cost_estimate=pl.CostEstimate(
            flops=0, bytes_accessed=108 * MIB, transcendentals=0
        ),
        compiler_params=pltpu.CompilerParams(
            collective_id=collective_id, has_side_effects=True,
            vmem_limit_bytes=lax.axis_size("z") * 2 * MIB + 20 * MIB,
        ),
    )(rows, table, ints, valid)


def embed_back_kernel(shard_rows, parts, rows_in, ints, table_grad, smalls, *refs):
    packs, refs = refs[:parts], refs[parts:]
    out, small_sum, squares, refs = refs[0], refs[1], refs[2], refs[3:]
    pack_sums, refs = refs[:parts], refs[parts:]
    slabs, small_got, refs = refs[0], refs[1], refs[2:]
    buffers, sems = refs[: 4 * parts], refs[4 * parts :]
    extent = out.shape[0]
    chunk = 2 * rows_in.shape[0]
    small_send, small_recv = sems[-6:-4]
    n_z, n_x, n_c, n_y = sizes()
    count = n_z * n_x * n_c * n_y
    me = index_after(0)
    greet_all()

    def small(step):
        return remote(
            smalls.at[index_after(step)], small_got.at[me], small_send.at[step], small_recv.at[step],
            device_after(step),
        )

    def each(action):
        def body(step, unused):
            action(step)
            return unused

        lax.fori_loop(1, count, body, 0)

    each(lambda step: small(step).start())
    beside, close_line = line_sums(packs, pack_sums, buffers, sems[-4:])
    small_got[me] = smalls[me]
    out[...] = table_grad[...]

    def work(slab):
        for pc in range(2):
            token = in_lane(ints, slab, pc, 0).astype(jnp.int32)
            hot = vocab_ids(extent, 2 * chunk, shard_rows) == token
            hot = jnp.where(hot, 1.0, 0.0).astype(jnp.bfloat16)
            out[...] += matmul(hot, slabs[slab, :, pc].reshape(2 * chunk, -1))

    gather_slabs(rows_in, slabs, sems[:-6], work, beside)
    close_line()
    each(lambda step: small(step).wait())
    small_sum[...] = jnp.sum(small_got[...], axis=0)
    value = out[...]
    inside = lax.broadcasted_iota(jnp.int32, value.shape, 0) < shard_rows
    squares[...] = jnp.sum(jnp.where(inside, value * value, 0.0), axis=0, keepdims=True)
    for part in pack_sums:
        value = part[...].reshape(-1, part.shape[-1])
        squares[:, : part.shape[-1]] += jnp.sum(value * value, axis=0, keepdims=True)


def embed_back(rows, ints, table_grad, smalls, packs, shard_rows, collective_id):
    own, width = rows.shape
    count = smalls.shape[0]
    dma = pltpu.SemaphoreType.DMA
    return pl.pallas_call(
        functools.partial(embed_back_kernel, shard_rows, len(packs)),
        out_shape=(
            jax.ShapeDtypeStruct(table_grad.shape, jnp.float32),
            jax.ShapeDtypeStruct(smalls.shape[1:], jnp.float32),
            jax.ShapeDtypeStruct((1, width), jnp.float32),
        )
        + tuple(jax.ShapeDtypeStruct(pack.shape[2:], jnp.float32) for pack in packs),
        in_specs=[VMEM] * (4 + len(packs)),
        out_specs=(VMEM,) * (3 + len(packs)),
        scratch_shapes=[
            pltpu.VMEM(sizes() + (own, width), rows.dtype), pltpu.VMEM(smalls.shape, jnp.float32),
        ]
        + [pltpu.VMEM(pack.shape[1:], pack.dtype) for pack in packs for _ in range(4)]
        + gather_sems() + [dma((count,)), dma((count,))] + line_sems(len(packs)),
        cost_estimate=pl.CostEstimate(
            flops=0, bytes_accessed=120 * MIB, transcendentals=0
        ),
        compiler_params=pltpu.CompilerParams(
            collective_id=collective_id, has_side_effects=True,
            vmem_limit_bytes=lax.axis_size("z") * 2 * MIB + 28 * MIB,
        ),
    )(rows, ints, table_grad, smalls, *packs)


def slab_order():
    n_z = lax.axis_size("z")
    z = lax.axis_index("z")
    up, down = n_z - 1 - z, z
    longer, shorter = jnp.maximum(up, down), jnp.minimum(up, down)
    far_side = jnp.where(up >= down, 1, -1)

    def target(step):
        late = step - (longer - shorter)
        near_side = jnp.where(late % 2 == 0, far_side, -far_side)
        return jnp.where(
            late < 0, z + far_side * (longer - step), z + near_side * (shorter - late // 2)
        )

    return target


def scatter_scratch(rows, width):
    n_z, n_x, n_c, n_y = sizes()
    half = rows // 2
    low = jnp.bfloat16
    dma = pltpu.SemaphoreType.DMA
    return [
        pltpu.VMEM((n_z, n_x, n_y, rows, width), low),
        pltpu.VMEM((n_z, n_x, n_y, rows, width), low),
        pltpu.VMEM((n_z, n_x, n_y, rows, width), low),
        pltpu.VMEM((n_z, 2, half, width), low),
        pltpu.VMEM((n_z, 2, half, width), low),
        pltpu.VMEM((n_z, half, width), low),
        pltpu.VMEM((n_z, half, width), low),
        pltpu.VMEM((n_z, rows, width), low),
        pltpu.VMEM((n_z, rows, width), low),
        dma((n_z, 2)), dma((n_z, 2)), dma((n_z, 3)), dma((n_z, 3)), dma((n_z, 3)),
        dma((n_z, 3)), dma((n_z, 2)), dma((n_z, 2, 2)),
    ]


def scatter_slabs(out, scratch, before, make, after, beside=lambda step: None):
    (
        lanes, handed, c_got, x_got, y_got, x_last, y_last, below, above,
        c_send, c_recv, x_send, x_recv, y_send, y_recv, z_send, z_recv,
    ) = scratch
    n_z = lax.axis_size("z")
    rows = out.shape[0]
    half = rows // 2
    (z, x, c, y), x_near, y_near, c_near = around()
    halves = (pl.ds(0, half), pl.ds(half, half))
    low, high = halves
    target = slab_order()

    def c_copy(slab, px):
        return remote(
            handed.at[slab, px], c_got.at[slab, px], c_send.at[slab, px], c_recv.at[slab, px], c_near
        )

    def x_first(slab, part):
        block = lanes.at[slab, 1 - x, y if part == 0 else 1 - y, low]
        return remote(block, x_got.at[slab, part], x_send.at[slab, part], x_recv.at[slab, part], x_near)

    def y_first(slab, part):
        block = lanes.at[slab, x if part == 0 else 1 - x, 1 - y, high]
        return remote(block, y_got.at[slab, part], y_send.at[slab, part], y_recv.at[slab, part], y_near)

    def y_second(slab):
        block = lanes.at[slab, x, 1 - y, low]
        return remote(block, y_last.at[slab], y_send.at[slab, 2], y_recv.at[slab, 2], y_near)

    def x_second(slab):
        block = lanes.at[slab, 1 - x, y, high]
        return remote(block, x_last.at[slab], x_send.at[slab, 2], x_recv.at[slab, 2], x_near)

    def z_up(slab, part):
        return remote(
            lanes.at[slab, x, y, halves[part]], below.at[slab, halves[part]], z_send.at[slab, part],
            z_recv.at[slab, 0, part], (z + 1, x, c, y),
        )

    def z_down(slab, part):
        return remote(
            lanes.at[slab, x, y, halves[part]], above.at[slab, halves[part]], z_send.at[slab, part],
            z_recv.at[slab, 1, part], (z - 1, x, c, y),
        )

    def produce(step):
        slab = target(step)
        before(step)

        mine = make(step, slab, 1 - c)
        for px in range(2):
            handed[slab, px] = mine[px]
            c_copy(slab, px).start()
        mine = make(step, slab, c)
        for px in range(2):
            lanes[slab, px] = mine[px]

    def begin(step):
        slab = target(step)
        for px in range(2):
            c_copy(slab, px).wait_recv()

        def merge(px, py):
            lanes[slab, px, py] = total_of(lanes[slab, px, py], c_got[slab, px, py]).astype(jnp.bfloat16)

        merge(1 - x, 1 - y)
        x_first(slab, 1).start()
        y_first(slab, 1).start()
        merge(1 - x, y)
        x_first(slab, 0).start()
        merge(x, 1 - y)
        y_first(slab, 0).start()
        merge(x, y)
        after(step)

    def middle(step):
        slab = target(step)
        x_first(slab, 1).wait_recv()
        x_first(slab, 0).wait_send()
        y_first(slab, 0).wait_send()
        lanes[slab, x, 1 - y, low] = total_of(
            lanes[slab, x, 1 - y, low], x_got[slab, 1]
        ).astype(jnp.bfloat16)
        y_second(slab).start()
        y_first(slab, 1).wait_recv()
        lanes[slab, 1 - x, y, high] = total_of(
            lanes[slab, 1 - x, y, high], y_got[slab, 1]
        ).astype(jnp.bfloat16)
        x_second(slab).start()

    def finish(step):
        slab = target(step)
        for part in range(2):
            if part == 0:
                x_first(slab, 0).wait_recv()
                y_second(slab).wait_recv()
                value = total_of(lanes[slab, x, y, low], x_got[slab, 0], y_last[slab])
            else:
                y_first(slab, 0).wait_recv()
                x_second(slab).wait_recv()
                value = total_of(lanes[slab, x, y, high], y_got[slab, 0], x_last[slab])
            rows_of = halves[part]

            @pl.when(slab > z)
            def _():
                @pl.when(z == 0)
                def _():
                    lanes[slab, x, y, rows_of] = value.astype(jnp.bfloat16)

                @pl.when(z > 0)
                def _():
                    z_up(slab, part).wait_recv()
                    lanes[slab, x, y, rows_of] = total_of(value, below[slab, rows_of]).astype(jnp.bfloat16)

                z_up(slab, part).start()

            @pl.when(slab < z)
            def _():
                @pl.when(z == n_z - 1)
                def _():
                    lanes[slab, x, y, rows_of] = value.astype(jnp.bfloat16)

                @pl.when(z < n_z - 1)
                def _():
                    z_down(slab, part).wait_recv()
                    lanes[slab, x, y, rows_of] = total_of(value, above[slab, rows_of]).astype(jnp.bfloat16)

                z_down(slab, part).start()

            @pl.when(slab == z)
            def _():
                out[rows_of, :] = value

                @pl.when(z > 0)
                def _():
                    z_up(slab, part).wait_recv()
                    out[rows_of, :] += below[slab, rows_of].astype(jnp.float32)

                @pl.when(z < n_z - 1)
                def _():
                    z_down(slab, part).wait_recv()
                    out[rows_of, :] += above[slab, rows_of].astype(jnp.float32)

    def turn(step, unused):
        for action, back in ((produce, 0), (begin, 0), (middle, 1), (finish, 2)):

            @pl.when((step >= back) & (step < n_z + back))
            def _():
                action(step - back)

        beside(step)
        return unused

    lax.fori_loop(0, n_z + 2, turn, 0)

    def close(slab, unused):
        for px in range(2):
            c_copy(slab, px).wait_send()
        x_first(slab, 1).wait_send()
        y_first(slab, 1).wait_send()
        x_second(slab).wait_send()
        y_second(slab).wait_send()
        for part in range(2):

            @pl.when(slab > z)
            def _():
                z_up(slab, part).wait_send()

            @pl.when(slab < z)
            def _():
                z_down(slab, part).wait_send()

        return unused

    lax.fori_loop(0, n_z, close, 0)


def embed_kernel(shard_rows, table, ints, qkv_own, out_own, out, qkv_all, out_all, *scratch):
    extent = table.shape[0]
    chunk = 2 * out.shape[0]
    greet_near()
    beside, close = line_gather(
        (qkv_own, out_own),
        (lambda pz, pc: qkv_all.at[:, pz, :, pc], lambda pz, pc: out_all.at[:, pz, pc]),
        scratch[-5:],
    )

    def make(step, slab, pc):
        token = in_lane(ints, slab, pc, 0).astype(jnp.int32)
        hot = vocab_ids(extent, 2 * chunk, shard_rows) == token
        hot = jnp.where(hot, 1.0, 0.0).astype(jnp.bfloat16)
        return inner(hot, table[...]).astype(jnp.bfloat16).reshape(2, 2, chunk // 2, -1)

    scatter_slabs(out, scratch[:-5], lambda step: None, make, lambda step: None, beside)
    close()


def embed(table, ints, qkv_own, out_own, own, shard_rows, collective_id):
    width = table.shape[1]
    n_z, n_x, n_c, _ = sizes()
    layers = qkv_own.shape[0]
    return pl.pallas_call(
        functools.partial(embed_kernel, shard_rows),
        out_shape=(
            jax.ShapeDtypeStruct((own, width), jnp.float32),
            jax.ShapeDtypeStruct((layers, n_z, n_x, n_c) + qkv_own.shape[2:], qkv_own.dtype),
            jax.ShapeDtypeStruct((layers, n_z, n_c) + out_own.shape[1:], out_own.dtype),
        ),
        in_specs=[VMEM] * 4,
        out_specs=(VMEM,) * 3,
        scratch_shapes=scatter_scratch(own, width) + line_gather_sems(),
        cost_estimate=pl.CostEstimate(
            flops=0, bytes_accessed=120 * MIB, transcendentals=0
        ),
        compiler_params=pltpu.CompilerParams(
            collective_id=collective_id, has_side_effects=True,
            vmem_limit_bytes=lax.axis_size("z") * 3 * MIB + 12 * MIB,
        ),
    )(table, ints, qkv_own, out_own)


def vocab_back_kernel(
    shard_rows, held, rows_all, table, ints, logs, weights, out, table_grad, slab_rows, changes, slab_sem, *scratch
):
    extent, width = table.shape
    chunk = 2 * out.shape[0]
    scale = width ** (-0.5)
    n_z = lax.axis_size("z")
    target = slab_order()

    def load(step):
        return pltpu.make_async_copy(
            rows_all.at[target(step)], slab_rows.at[step % 2], slab_sem.at[step % 2]
        )

    if not held:
        load(0).start()
    greet_near()
    table_grad[...] = jnp.zeros_like(table_grad)

    def rows_of(step, pc):
        if held:
            return rows_all[target(step), :, pc].reshape(2 * chunk, width)
        return slab_rows[step % 2, :, pc].reshape(2 * chunk, width)

    def before(step):
        if held:
            return
        load(step).wait()

        @pl.when(step + 1 < n_z)
        def _():
            load(step + 1).start()

    def make(step, slab, pc):
        value = outer(table[...], rows_of(step, pc)) * scale
        aim = in_lane(ints, slab, pc, 1).astype(jnp.int32)
        hot = jnp.where(vocab_ids(extent, 2 * chunk, shard_rows) == aim, 1.0, 0.0)
        change = jnp.exp(value - in_lane(logs, slab, pc, 0)) - hot
        change = (change * in_lane(weights, slab, pc, 0)).astype(jnp.bfloat16)
        changes[pc] = change
        return (inner(change, table[...]) * scale).astype(jnp.bfloat16).reshape(2, 2, chunk // 2, width)

    def after(step):
        for pc in range(2):
            table_grad[...] += matmul(changes[pc], rows_of(step, pc))

    scatter_slabs(out, scratch, before, make, after)
    table_grad[...] = table_grad[...] * scale


def vocab_back(rows_all, table, ints, logs, weights, shard_rows, collective_id):
    own, width = rows_all.shape[4:]
    extent = table.shape[0]
    n_z, n_x, n_c, n_y = sizes()
    held = n_z <= 4
    return pl.pallas_call(
        functools.partial(vocab_back_kernel, shard_rows, held),
        out_shape=(
            jax.ShapeDtypeStruct((own, width), jnp.float32),
            jax.ShapeDtypeStruct((extent, width), jnp.float32),
        ),
        in_specs=[VMEM if held else ANY] + [VMEM] * 4,
        out_specs=(VMEM,) * 2,
        scratch_shapes=[
            pltpu.VMEM((1,) * 6 if held else (2, n_x, n_c, n_y, own, width), rows_all.dtype),
            pltpu.VMEM((n_c, extent, 4 * own), jnp.bfloat16),
            pltpu.SemaphoreType.DMA((2,)),
        ] + scatter_scratch(own, width),
        cost_estimate=pl.CostEstimate(
            flops=0, bytes_accessed=144 * MIB, transcendentals=0
        ),
        compiler_params=pltpu.CompilerParams(
            collective_id=collective_id, has_side_effects=True,
            vmem_limit_bytes=n_z * 3 * MIB + 24 * MIB if n_z <= 8 else 62 * MIB,
        ),
    )(rows_all, table, ints, logs, weights)


SQRT_HALF = 0.5**0.5
DENSITY = 0.3989422804014327


def matmul(left, right):
    return jnp.dot(left, right, preferred_element_type=jnp.float32)


def inner(left, right):
    return lax.dot_general(
        left, right, (((0,), (0,)), ((), ())), preferred_element_type=jnp.float32
    )


def outer(left, right):
    return lax.dot_general(
        left, right, (((1,), (1,)), ((), ())), preferred_element_type=jnp.float32
    )


def plane_gather(own_rows, blocks, send_sem, recv_sem):
    half = own_rows.shape[0] // 2
    (z, x, c, y), x_near, y_near, _ = around()
    low, high = pl.ds(0, half), pl.ds(half, half)

    def copy(slot, px, py, rows, source, device):
        target = blocks.at[px, py, rows]
        return remote(target if source is None else source.at[rows], target, send_sem.at[slot], recv_sem.at[slot], device)

    first = [
        copy(0, x, y, low, own_rows, x_near),
        copy(1, x, y, high, own_rows, y_near),
        copy(2, x, y, high, own_rows, x_near),
        copy(3, x, y, low, own_rows, y_near),
    ]
    relays = [copy(4, 1 - x, y, low, None, y_near), copy(5, x, 1 - y, high, None, x_near)]
    for each in first:
        each.start()

    def wait_near():
        first[0].wait_recv()
        relays[0].start()
        first[1].wait_recv()
        relays[1].start()

    def wait_x():
        first[2].wait_recv()

    def wait_y():
        first[3].wait_recv()

    def wait_diagonal():
        for each in relays:
            each.wait_recv()

    def close():
        for each in first + relays:
            each.wait_send()

    return wait_near, wait_x, wait_y, wait_diagonal, close


def plane_sum(parts, got, out, send_sem, recv_sem):
    (z, x, c, y), x_near, y_near, _ = around()
    diagonal = (z, 1 - x, c, 1 - y)
    copies = [
        remote(parts.at[device[1], device[3]], got.at[slot], send_sem.at[slot], recv_sem.at[slot], device)
        for slot, device in enumerate((x_near, y_near, diagonal))
    ]

    def close():
        for each in copies:
            each.wait_recv()
        out[...] = total_of(parts[x, y], got[0], got[1], got[2])
        for each in copies:
            each.wait_send()

    return copies, close


def order_experts(kept, got, ordered, sems):
    n_z, n_c, _, depth, _ = kept.shape
    x = lax.axis_index("x")
    copies = []
    for pz in range(n_z):
        for pc in range(n_c):
            for side, weights in enumerate((kept, got)):
                if depth == ordered.shape[1]:
                    rows, side = pl.ds(0, depth), 0
                else:
                    px = x if side == 0 else 1 - x
                    at = (pz * 2 + px) * n_c + pc
                    rows = pl.ds(pl.multiple_of(at * depth, 16), depth)
                slot = (pz * n_c + pc) * 2 + side
                if depth == ordered.shape[1] and weights is got:
                    continue
                copies.append(
                    pltpu.make_async_copy(weights.at[pz, pc], ordered.at[:, rows], sems.at[slot])
                )
    for copy in copies:
        copy.start()
    return copies


def experts_kernel(
    own_rows, route, w_kept, w_got, out, wide, before, hidden, ordered, parts, got, w_sem, g_send, g_recv, s_send, s_recv
):
    (z, x, c, y), x_near, y_near, _ = around()
    diagonal = (z, 1 - x, c, 1 - y)
    loads = order_experts(w_kept, w_got, ordered, w_sem)
    up, down = ordered.at[pl.ds(0, 2)], ordered.at[pl.ds(2, 2)]
    greet((x_near, y_near, diagonal))
    wait_near, wait_x, wait_y, wait_diagonal, close = plane_gather(own_rows, wide, g_send, g_recv)
    copies, finish = plane_sum(parts, got, out, s_send, s_recv)
    wide[x, y] = own_rows[...]

    def work(px, py):
        rows = wide[px, py]
        first = route[px, py] == 0
        value = jnp.where(first, matmul(rows, up[0]), matmul(rows, up[1]))
        before[px, py] = value
        active = 0.5 * value * (1.0 + lax.erf(value * SQRT_HALF))
        hidden_first = jnp.where(first, active, 0.0).astype(jnp.bfloat16)
        hidden_second = jnp.where(first, 0.0, active).astype(jnp.bfloat16)
        hidden[px, py] = active.astype(jnp.bfloat16)
        total = outer(hidden_first, down[0]) + outer(hidden_second, down[1])
        parts[px, py] = total.astype(jnp.bfloat16)

    for load in loads:
        load.wait()
    work(x, y)
    wait_near()
    wait_x()
    work(1 - x, y)
    copies[0].start()
    wait_y()
    work(x, 1 - y)
    copies[1].start()
    wait_diagonal()
    work(1 - x, 1 - y)
    copies[2].start()
    finish()
    close()


def experts(own_rows, route, weights, collective_id):
    _, n_x, _, n_y = sizes()
    own, width = own_rows.shape
    wide = weights[0].shape[4]
    dma = pltpu.SemaphoreType.DMA
    low = jnp.bfloat16
    return pl.pallas_call(
        experts_kernel,
        out_shape=(
            jax.ShapeDtypeStruct((own, width), jnp.float32),
            jax.ShapeDtypeStruct((n_x, n_y, own, width), low),
            jax.ShapeDtypeStruct((n_x, n_y, own, wide), jnp.float32),
            jax.ShapeDtypeStruct((n_x, n_y, own, wide), low),
        ),
        in_specs=[VMEM, VMEM, HBM, HBM],
        out_specs=(VMEM,) * 4,
        scratch_shapes=[
            pltpu.VMEM((4, width, wide), low),
            pltpu.VMEM((n_x, n_y, own, width), low),
            pltpu.VMEM((3, own, width), low),
            dma((width // weights[0].shape[3],)), dma((6,)), dma((6,)), dma((3,)), dma((3,)),
        ],
        compiler_params=pltpu.CompilerParams(
            collective_id=collective_id, has_side_effects=True, vmem_limit_bytes=56 * MIB
        ),
        cost_estimate=pl.CostEstimate(
            flops=8 * own * 4 * width * wide, bytes_accessed=54 * MIB, transcendentals=4 * own * wide
        ),
    )(own_rows, route, *weights)


def experts_back_kernel(
    own_rows, route, w_kept, w_got, wide_kept, before_kept, hidden_kept, out, grads,
    ordered, wide, before, hidden, made, wide_grad, before_grad, parts, got,
    w_sem, k_sem, o_sem, g_send, g_recv, s_send, s_recv,
):
    (z, x, c, y), x_near, y_near, _ = around()
    diagonal = (z, 1 - x, c, 1 - y)
    loads = order_experts(w_kept, w_got, ordered, w_sem)
    for slot, (source, target) in enumerate(
        ((before_kept, before), (wide_kept, wide), (hidden_kept, hidden))
    ):
        load = pltpu.make_async_copy(source, target, k_sem.at[slot])
        load.start()
        loads.append(load)
    up, down = ordered.at[pl.ds(0, 2)], ordered.at[pl.ds(2, 2)]
    greet((x_near, y_near, diagonal))
    wait_near, wait_x, wait_y, wait_diagonal, close = plane_gather(own_rows, wide_grad, g_send, g_recv)
    copies, finish = plane_sum(parts, got, out, s_send, s_recv)
    wide_grad[x, y] = own_rows[...]

    def work(px, py):
        rows = wide_grad[px, py]
        first = route[px, py] == 0
        hidden_grad = jnp.where(first, matmul(rows, down[0]), matmul(rows, down[1]))
        value = before[px, py]
        slope = 0.5 * (1.0 + lax.erf(value * SQRT_HALF)) + value * (
            DENSITY * jnp.exp(-0.5 * value * value)
        )
        change = (hidden_grad * slope).astype(jnp.bfloat16)
        before_grad[px, py] = change
        change_first = jnp.where(first, change, 0)
        change_second = jnp.where(first, 0, change)
        total = outer(change_first, up[0]) + outer(change_second, up[1])
        parts[px, py] = total.astype(jnp.bfloat16)

    for load in loads:
        load.wait()
    work(x, y)
    wait_near()
    wait_x()
    work(1 - x, y)
    copies[0].start()
    wait_y()
    work(x, 1 - y)
    copies[1].start()
    wait_diagonal()
    work(1 - x, 1 - y)
    copies[2].start()
    close()

    lane = 4 * own_rows.shape[0]
    rows = wide[...].reshape(lane, -1)
    grad_rows = wide_grad[...].reshape(lane, -1)
    first = route[...].reshape(lane, 1) == 0
    change = before_grad[...].reshape(lane, -1)
    active = hidden[...].reshape(lane, -1)
    low = jnp.bfloat16
    n_z, n_x, n_c, _ = sizes()
    depth = grads.shape[3]
    saves = []

    def keep(slot, value):
        value = value.astype(low)
        for pz in range(n_z):
            for px in range(n_x):
                for pc in range(n_c):
                    start = ((pz * n_x + px) * n_c + pc) * depth
                    made[slot, pz * n_c + pc, px] = value[start : start + depth]
        save = pltpu.make_async_copy(made.at[slot], grads.at[:, :, slot], o_sem.at[slot])
        save.start()
        saves.append(save)

    keep(0, inner(rows, jnp.where(first, change, 0)))
    keep(1, inner(rows, jnp.where(first, 0, change)))
    keep(2, inner(grad_rows, jnp.where(first, active, 0)))
    keep(3, inner(grad_rows, jnp.where(first, 0, active)))
    finish()
    for save in saves:
        save.wait()


def experts_back(own_rows, route, weights, wide, before, hidden, collective_id):
    n_z, n_x, n_c, n_y = sizes()
    own, width = own_rows.shape
    units = weights[0].shape[4]
    dma = pltpu.SemaphoreType.DMA
    low = jnp.bfloat16
    return pl.pallas_call(
        experts_back_kernel,
        out_shape=(
            jax.ShapeDtypeStruct((own, width), jnp.float32),
            jax.ShapeDtypeStruct((n_z * n_c, n_x, 4, width // (n_z * n_x * n_c), units), low),
        ),
        in_specs=[VMEM, VMEM] + [HBM] * 5,
        out_specs=(VMEM, HBM),
        scratch_shapes=[
            pltpu.VMEM((4, width, units), low),
            pltpu.VMEM(wide.shape, wide.dtype), pltpu.VMEM(before.shape, before.dtype),
            pltpu.VMEM(hidden.shape, hidden.dtype),
            pltpu.VMEM((4, n_z * n_c, n_x, width // (n_z * n_x * n_c), units), low),
            pltpu.VMEM((n_x, n_y, own, width), low),
            pltpu.VMEM((n_x, n_y, own, units), low),
            pltpu.VMEM((n_x, n_y, own, width), low),
            pltpu.VMEM((3, own, width), low),
            dma((width // weights[0].shape[3],)), dma((3,)), dma((4,)), dma((6,)), dma((6,)), dma((3,)), dma((3,)),
        ],
        compiler_params=pltpu.CompilerParams(
            collective_id=collective_id, has_side_effects=True, vmem_limit_bytes=56 * MIB
        ),
        cost_estimate=pl.CostEstimate(
            flops=16 * own * 4 * width * units, bytes_accessed=54 * MIB, transcendentals=8 * own * units
        ),
    )(own_rows, route, *weights, wide, before, hidden)


def in_owner_order(value, target):
    value = value.astype(target.dtype)
    n_c, n_z = target.shape[:2]
    n_x = target.shape[2] if len(target.shape) == 5 else 1
    depth = target.shape[-2]
    for pz in range(n_z):
        for px in range(n_x):
            for pc in range(n_c):
                start = ((pz * n_x + px) * n_c + pc) * depth
                if len(target.shape) == 5:
                    target[pc, pz, px] = value[start : start + depth]
                else:
                    target[pc, pz] = value[start : start + depth]


def project_kernel(transposed, with_grad, *refs):
    if with_grad:
        rows, weight, left, out, grad, parts, got, s_send, s_recv = refs
    else:
        rows, weight, out, parts, got, s_send, s_recv = refs
    (z, x, c, y), x_near, y_near, _ = around()
    diagonal = (z, 1 - x, c, 1 - y)
    barrier = pltpu.get_barrier_semaphore()
    for device in (x_near, y_near, diagonal):
        pl.semaphore_signal(barrier, inc=1, device_id=device, device_id_type=MESH)
    copies, finish = plane_sum(parts, got, out, s_send, s_recv)

    def work(px, py):
        times = outer if transposed else matmul
        parts[px, py] = times(rows[px, py], weight[...]).astype(jnp.bfloat16)

    work(1 - x, 1 - y)
    pl.semaphore_wait(barrier, 3)
    copies[2].start()
    work(1 - x, y)
    copies[0].start()
    work(x, 1 - y)
    copies[1].start()
    work(x, y)
    if with_grad:
        lane = 4 * out.shape[0]
        in_owner_order(inner(left[...].reshape(lane, -1), rows[...].reshape(lane, -1)), grad)
    finish()


def project(rows, weight, transposed, left, collective_id):
    n_x, n_y, own, depth = rows.shape
    n_z, _, n_c, _ = sizes()
    width = weight.shape[0] if transposed else weight.shape[1]
    low = jnp.bfloat16
    dma = pltpu.SemaphoreType.DMA
    return pl.pallas_call(
        functools.partial(project_kernel, transposed, left is not None),
        out_shape=(jax.ShapeDtypeStruct((own, width), jnp.float32),)
        + (
            ()
            if left is None
            else (
                jax.ShapeDtypeStruct(
                    (n_c, n_z, n_x, left.shape[3] // (n_z * n_x * n_c), depth), low
                ),
            )
        ),
        in_specs=[VMEM] * (2 if left is None else 3),
        out_specs=(VMEM,) * (1 if left is None else 2),
        scratch_shapes=[
            pltpu.VMEM((n_x, n_y, own, width), low), pltpu.VMEM((3, own, width), low), dma((3,)), dma((3,)),
        ],
        compiler_params=pltpu.CompilerParams(
            collective_id=collective_id, has_side_effects=True, vmem_limit_bytes=16 * MIB
        ),
        cost_estimate=pl.CostEstimate(
            flops=8 * own * width * depth, bytes_accessed=24 * MIB, transcendentals=0
        ),
    )(rows, weight, *(() if left is None else (left,)))


def gather_project_kernel(transposed, split, with_grad, own_rows, weight, *rest):
    if with_grad:
        left, wide, rest = rest[0], rest[1], (rest[0],) + rest[2:]
    else:
        wide, rest = rest[0], rest[1:]

    (z, x, c, y), x_near, y_near, _ = around()
    rest, (g_send, g_recv) = rest[:-2], rest[-2:]
    left, outs = (rest[0], rest[1:]) if with_grad else (None, rest)
    greet((x_near, y_near))
    wait_near, wait_x, wait_y, wait_diagonal, close = plane_gather(own_rows, wide, g_send, g_recv)
    wide[x, y] = own_rows[...]

    def work(px, py):
        times = outer if transposed else matmul
        value = times(wide[px, py], weight[...]).astype(jnp.bfloat16)
        start = 0
        for out, size in zip(outs, split):
            out[px, py] = value[:, start : start + size]
            start += size

    work(x, y)
    wait_near()
    wait_x()
    work(1 - x, y)
    wait_y()
    work(x, 1 - y)
    wait_diagonal()
    work(1 - x, 1 - y)
    if with_grad:
        lane = 4 * own_rows.shape[0]
        in_owner_order(inner(left[...], wide[...].reshape(lane, -1)), outs[-1])
    close()


def gather_project(own_rows, weight, transposed, split, left, collective_id):
    n_z, n_x, n_c, n_y = sizes()
    own, width = own_rows.shape
    depth = weight.shape[0] if transposed else weight.shape[1]
    dma = pltpu.SemaphoreType.DMA
    low = jnp.bfloat16
    return pl.pallas_call(
        functools.partial(gather_project_kernel, transposed, split, left is not None),
        out_shape=(
            jax.ShapeDtypeStruct((n_x, n_y, own, width), low),
        ) + tuple(jax.ShapeDtypeStruct((n_x, n_y, own, size), low) for size in split)
        + (
            ()
            if left is None
            else (jax.ShapeDtypeStruct((n_c, n_z, left.shape[1] // (n_z * n_c), width), low),)
        ),
        in_specs=[VMEM] * (2 if left is None else 3),
        out_specs=(VMEM,) * (1 + len(split) + (0 if left is None else 1)),
        scratch_shapes=[dma((6,)), dma((6,))],
        compiler_params=pltpu.CompilerParams(
            collective_id=collective_id, has_side_effects=True, vmem_limit_bytes=12 * MIB
        ),
        cost_estimate=pl.CostEstimate(
            flops=8 * own * width * depth, bytes_accessed=24 * MIB, transcendentals=0
        ),
    )(own_rows, weight, *(() if left is None else (left,)))


def merge_logs_kernel(source, out, got, mine, send_one, recv_one, send_two, recv_two):
    n_z, n_x, n_c, n_y = sizes()
    count = n_z * n_x * n_c * n_y
    z, x, c, y = place()
    me = ((z * n_x + x) * n_c + c) * n_y + y

    def device_of(index):
        return (
            index // (n_x * n_c * n_y), index // (n_c * n_y) % n_x, index // n_y % n_c, index % n_y
        )

    barrier = pltpu.get_barrier_semaphore()

    def call(step, unused):
        other = lax.rem(me + step, count)
        pl.semaphore_signal(barrier, inc=1, device_id=device_of(other), device_id_type=MESH)
        return unused

    lax.fori_loop(1, count, call, 0)
    got[me] = source[me]
    pl.semaphore_wait(barrier, count - 1)

    def first(step):
        other = lax.rem(me + step, count)
        return remote(
            source.at[other], got.at[me], send_one.at[step], recv_one.at[step], device_of(other)
        )

    def second(step):
        other = lax.rem(me + step, count)
        return remote(mine, out.at[me], send_two.at[step], recv_two.at[step], device_of(other))

    def each(action):
        def body(step, unused):
            action(step)
            return unused

        lax.fori_loop(1, count, body, 0)

    each(lambda step: first(step).start())
    each(lambda step: first(step).wait())
    values = got[...]
    peak = jnp.max(values, axis=0)
    mine[...] = peak + jnp.log(jnp.sum(jnp.exp(values - peak[None]), axis=0))
    out[me] = mine[...]
    each(lambda step: second(step).start())
    each(lambda step: second(step).wait())


def merge_logs(blocks, collective_id):
    count = blocks.shape[0]
    dma = pltpu.SemaphoreType.DMA
    return pl.pallas_call(
        merge_logs_kernel,
        out_shape=jax.ShapeDtypeStruct(blocks.shape, blocks.dtype),
        in_specs=[VMEM],
        out_specs=VMEM,
        scratch_shapes=[
            pltpu.VMEM(blocks.shape, blocks.dtype), pltpu.VMEM(blocks.shape[1:], blocks.dtype),
            dma((count,)), dma((count,)), dma((count,)), dma((count,)),
        ],
        cost_estimate=pl.CostEstimate(
            flops=0, bytes_accessed=42 * MIB, transcendentals=0
        ),
        compiler_params=pltpu.CompilerParams(
            collective_id=collective_id, has_side_effects=True, vmem_limit_bytes=8 * MIB
        ),
    )(blocks)


def key_position(index, part, chunk):
    lane = 2 * chunk
    start = (part // 2) * (2 * lane) + (part % 2) * chunk
    return start + index + jnp.where(index >= chunk, chunk, 0)


def as_column(row):
    wide_row = jnp.broadcast_to(row.astype(jnp.float32), (8, row.shape[1]))
    return wide_row.T[:, :1].astype(jnp.int32)


def near_shown(side, chunk, query_pos, query_seg, near_pos, near_seg):
    columns = slice(side * chunk, (side + 1) * chunk)
    rows = slice(2 * side * chunk, 2 * (side + 1) * chunk)
    shown = (
        (near_seg[rows, :] == query_seg[:, columns])
        & (near_pos[rows, :] <= query_pos[:, columns])
        & (near_pos[rows, :] >= PROMPT)
    )
    return columns, rows, shown


def attend_kernel(
    chunk, query, far, near, query_pos, query_seg, near_pos, near_seg,
    out, out_low, log_total, scores, far_t, near_t,
):
    lane, feature = query.shape
    group = feature // HEAD_DIM
    prompt_rows = far.shape[0]
    parts = prompt_rows // lane
    query_t = (query[...].astype(jnp.float32) * HEAD_DIM ** (-0.5)).T.astype(jnp.bfloat16)
    far_t[...] = far[...].astype(jnp.float32).T.astype(jnp.bfloat16)
    near_t[...] = near[...].astype(jnp.float32).T.astype(jnp.bfloat16)
    row_of = lax.broadcasted_iota(jnp.int32, (feature, lane), 0)
    q_pos = query_pos[...]
    near_pos, near_seg = as_column(near_pos[...]), as_column(near_seg[...])

    for head in range(group):
        low, high = head * HEAD_DIM, (head + 1) * HEAD_DIM
        query_h = jnp.where((row_of >= low) & (row_of < high), query_t, 0)

        def score_part(part, peak):
            block = far[pl.ds(pl.multiple_of(part * lane, lane), lane), :feature]
            value = matmul(block, query_h)
            index = lax.broadcasted_iota(jnp.int32, (lane, lane), 0)
            value = jnp.where(key_position(index, part, chunk) <= q_pos, value, MASKED)
            scores[pl.ds(pl.multiple_of(part * lane, lane), lane), :] = value
            return jnp.maximum(peak, jnp.max(value, axis=0, keepdims=True))

        peak = lax.fori_loop(0, parts, score_part, jnp.full((1, lane), MASKED, jnp.float32))
        near_peaks = []
        for side in range(2):
            columns, rows, shown = near_shown(side, chunk, query_pos, query_seg, near_pos, near_seg)
            value = matmul(near[rows, :feature], query_h[:, columns])
            value = jnp.where(shown, value, MASKED)
            scores[prompt_rows : prompt_rows + lane, columns] = value
            near_peaks.append(jnp.max(value, axis=0, keepdims=True))
        peak = jnp.maximum(peak, jnp.concatenate(near_peaks, axis=1))

        def weigh_part(part, state):
            total, mixed = state
            start = pl.multiple_of(part * lane, lane)
            chance = jnp.exp(scores[pl.ds(start, lane), :] - peak)
            total = total + jnp.sum(chance, axis=0, keepdims=True)
            mixed = mixed + matmul(
                far_t[feature + low : feature + high, pl.ds(start, lane)],
                chance.astype(jnp.bfloat16),
            )
            return total, mixed

        total, mixed = lax.fori_loop(
            0,
            parts,
            weigh_part,
            (jnp.zeros((1, lane), jnp.float32), jnp.zeros((HEAD_DIM, lane), jnp.float32)),
        )
        near_total, near_mixed = [], []
        for side in range(2):
            columns = slice(side * chunk, (side + 1) * chunk)
            rows = slice(side * lane, (side + 1) * lane)
            chance = jnp.exp(scores[prompt_rows : prompt_rows + lane, columns] - peak[:, columns])
            near_total.append(jnp.sum(chance, axis=0, keepdims=True))
            near_mixed.append(
                matmul(near_t[feature + low : feature + high, rows], chance.astype(jnp.bfloat16))
            )
        total = total + jnp.concatenate(near_total, axis=1)
        mixed = mixed + jnp.concatenate(near_mixed, axis=1)
        out[low:high, :] = mixed / total
        log_total[head : head + 1, :] = peak + jnp.log(total)
    out_low[...] = out[...].T.astype(jnp.bfloat16)


def attend(queries, far, near, places, chunk):
    lane, feature = queries.shape
    prompt_rows = far.shape[0]
    group = feature // HEAD_DIM
    total_rows = prompt_rows + lane
    return pl.pallas_call(
        functools.partial(attend_kernel, chunk),
        out_shape=(
            jax.ShapeDtypeStruct((feature, lane), jnp.float32),
            jax.ShapeDtypeStruct((lane, feature), jnp.bfloat16),
            jax.ShapeDtypeStruct((group, lane), jnp.float32),
        ),
        in_specs=[VMEM] * 7,
        out_specs=(VMEM,) * 3,
        scratch_shapes=[
            pltpu.VMEM((total_rows, lane), jnp.float32),
            pltpu.VMEM((2 * feature, prompt_rows), jnp.bfloat16),
            pltpu.VMEM((2 * feature, 2 * lane), jnp.bfloat16),
        ],
        compiler_params=pltpu.CompilerParams(vmem_limit_bytes=20 * MIB),
        cost_estimate=pl.CostEstimate(
            flops=8 * group * lane * total_rows * 128,
            bytes_accessed=8 * MIB,
            transcendentals=group * lane * total_rows,
        ),
    )(queries, far, near, *places)


def attend_back_kernel(
    chunk, query, far, near, query_pos, query_seg, near_pos, near_seg,
    log_total, mixed, answer, query_grad, far_grad, near_grad,
    far_t, near_t, far_values, near_values, far_sum, near_sum, query_sum,
):
    lane, feature = query.shape
    group = feature // HEAD_DIM
    prompt_rows = far.shape[0]
    parts = prompt_rows // lane
    scaled = (query[...].astype(jnp.float32) * HEAD_DIM ** (-0.5)).astype(jnp.bfloat16)
    query_t = scaled.astype(jnp.float32).T.astype(jnp.bfloat16)
    answers = answer[...]
    answer_t = answers.astype(jnp.float32).T.astype(jnp.bfloat16)
    far_t[...] = far[:, :feature].astype(jnp.float32).T.astype(jnp.bfloat16)
    near_t[...] = near[:, :feature].astype(jnp.float32).T.astype(jnp.bfloat16)
    far_values[...] = far[:, feature:]
    near_values[...] = near[:, feature:]
    row_of = lax.broadcasted_iota(jnp.int32, (feature, lane), 0)
    column_of = lax.broadcasted_iota(jnp.int32, (lane, feature), 1)
    q_pos = query_pos[...]
    near_pos, near_seg = as_column(near_pos[...]), as_column(near_seg[...])

    for head in range(group):
        low, high = head * HEAD_DIM, (head + 1) * HEAD_DIM
        in_rows = (row_of >= low) & (row_of < high)
        in_columns = (column_of >= low) & (column_of < high)
        query_ht = jnp.where(in_rows, query_t, 0)
        answer_ht = jnp.where(in_rows, answer_t, 0)
        query_h = jnp.where(in_columns, scaled, 0)
        answer_h = jnp.where(in_columns, answers, 0)
        log_h = log_total[head : head + 1, :]
        delta_h = jnp.sum(
            answer_t[low:high, :].astype(jnp.float32) * mixed[low:high, :], axis=0, keepdims=True
        )

        def slopes(key_block, value_block, shown, columns):
            value = matmul(key_block, query_ht[:, columns])
            chance = jnp.exp(jnp.where(shown, value - log_h[:, columns], MASKED))
            slope = matmul(value_block, answer_ht[:, columns])
            change = (chance * (slope - delta_h[:, columns])).astype(jnp.bfloat16)
            chance = chance.astype(jnp.bfloat16)
            return change, matmul(change, query_h[columns]), matmul(chance, answer_h[columns])

        def add(sums, rows, key_part, value_part):
            if head == 0:
                sums[0, rows, :] = key_part
                sums[1, rows, :] = value_part
            else:
                sums[0, rows, :] += key_part
                sums[1, rows, :] += value_part

        def back_part(part, total):
            rows = pl.ds(pl.multiple_of(part * lane, lane), lane)
            index = lax.broadcasted_iota(jnp.int32, (lane, lane), 0)
            shown = key_position(index, part, chunk) <= q_pos
            change, key_part, value_part = slopes(
                far[rows, :feature], far_values[rows, :], shown, slice(0, lane)
            )
            add(far_sum, rows, key_part, value_part)
            return total + matmul(far_t[low:high, rows], change)

        total = lax.fori_loop(0, parts, back_part, jnp.zeros((HEAD_DIM, lane), jnp.float32))
        near_total = []
        for side in range(2):
            columns, rows, shown = near_shown(side, chunk, query_pos, query_seg, near_pos, near_seg)
            change, key_part, value_part = slopes(
                near[rows, :feature], near_values[rows, :], shown, columns
            )
            add(near_sum, rows, key_part, value_part)
            near_total.append(matmul(near_t[low:high, rows], change))
        query_sum[low:high, :] = (total + jnp.concatenate(near_total, axis=1)) * HEAD_DIM ** (-0.5)
    query_grad[...] = query_sum[...].T.astype(jnp.bfloat16)
    for sums, grad in ((far_sum, far_grad), (near_sum, near_grad)):
        grad[...] = jnp.concatenate(
            [sums[0].astype(jnp.bfloat16), sums[1].astype(jnp.bfloat16)], axis=1
        )


def attend_back(queries, far, near, places, log_total, mixed, answer, chunk):
    lane, feature = queries.shape
    prompt_rows = far.shape[0]
    group = feature // HEAD_DIM
    total_rows = prompt_rows + lane
    low = jnp.bfloat16
    return pl.pallas_call(
        functools.partial(attend_back_kernel, chunk),
        out_shape=(
            jax.ShapeDtypeStruct((lane, feature), low),
            jax.ShapeDtypeStruct((prompt_rows, 2 * feature), low),
            jax.ShapeDtypeStruct((2 * lane, 2 * feature), low),
        ),
        in_specs=[VMEM] * 10,
        out_specs=(VMEM,) * 3,
        scratch_shapes=[
            pltpu.VMEM((feature, prompt_rows), low),
            pltpu.VMEM((feature, 2 * lane), low),
            pltpu.VMEM((prompt_rows, feature), low),
            pltpu.VMEM((2 * lane, feature), low),
            pltpu.VMEM((2, prompt_rows, feature), jnp.float32),
            pltpu.VMEM((2, 2 * lane, feature), jnp.float32),
            pltpu.VMEM((feature, lane), jnp.float32),
        ],
        compiler_params=pltpu.CompilerParams(vmem_limit_bytes=28 * MIB),
        cost_estimate=pl.CostEstimate(
            flops=20 * group * lane * total_rows * 128,
            bytes_accessed=12 * MIB,
            transcendentals=group * lane * total_rows,
        ),
    )(queries, far, near, *places, log_total, mixed, answer)


def head_places(back):
    n_z, n_x, n_c, n_y = sizes()
    line = n_z * n_c
    pairs = []
    for device in range(line * n_x * n_y):
        group, at = device // line, device % line
        place_of = ((at // n_c * n_x + group // n_y) * n_c + at % n_c) * n_y + group % n_y
        pairs.append((place_of, device) if back else (device, place_of))
    return tuple(pairs)


def pad_rows(block):
    return jnp.pad(block, ((0, 8 - block.shape[0]), (0, 0)))


def adam_update(weight, moment_one, moment_two, gradient, step_rate, decay_rate):
    first_new = BETA_ONE * moment_one + (1.0 - BETA_ONE) * gradient
    second_new = BETA_TWO * moment_two + (1.0 - BETA_TWO) * gradient * gradient
    normalized = (
        first_new
        / (1.0 - BETA_ONE**STEP)
        / (jnp.sqrt(second_new / (1.0 - BETA_TWO**STEP)) + ADAM_EPS)
    )
    return (weight - step_rate * (normalized + decay_rate * weight), first_new, second_new)


def per_device(
    token_ids,
    targets,
    valid_mask,
    cont_lengths,
    routes,
    vocab_table,
    vocab_first,
    vocab_second,
    attn_weights,
    attn_first,
    attn_second,
    router,
    router_first,
    router_second,
    norm_gains,
    gains_first,
    gains_second,
    expert_up,
    up_first,
    up_second,
    expert_down,
    down_first,
    down_second,
):
    slabs = lax.axis_size("z")
    planes = lax.axis_size("x")
    cores = lax.axis_size("core")
    sides = lax.axis_size("head")
    groups = planes * sides
    z_at, x_at, core_at, side_at = (lax.axis_index(name) for name in ALL)
    blk_at = (z_at * planes + x_at) * cores + core_at
    device_at = blk_at * sides + side_at
    group_at = x_at * sides + side_at
    tokens = valid_mask.shape[0]
    chunk = token_ids.shape[0]
    own = chunk // sides
    lane = planes * chunk
    feature = D // groups
    wide = expert_up.shape[3] // planes
    shard_rows = vocab_table.shape[0]
    logit_scale = D ** (-0.5)

    cont_ends = jnp.cumsum(cont_lengths)
    valid_f = valid_mask.astype(jnp.float32)
    token_count = jnp.sum(valid_mask).astype(jnp.float32)
    expert_ids = jnp.arange(EXPERTS, dtype=jnp.int32)

    own_ints = jnp.concatenate([token_ids[None], targets[None], routes], axis=0)
    own_ints = lax.dynamic_slice_in_dim(own_ints, side_at * own, own, axis=1).astype(jnp.float32)
    rows_of = attn_weights.shape[1]
    smalls = jnp.concatenate(
        [router.transpose(0, 2, 1).reshape(LAYERS * EXPERTS, rows_of), norm_gains], axis=0
    )
    smalls = smalls.astype(jnp.bfloat16).astype(jnp.float32)
    smalls = jnp.pad(smalls, ((0, 16 - smalls.shape[0]), (0, own - rows_of)))
    whole_f = swap(jnp.concatenate([pad_rows(own_ints), smalls], axis=0)[None], True, 1)
    attn_low = attn_weights.astype(jnp.bfloat16)
    qkv_send = attn_low[:, :, : 3 * D].reshape(LAYERS, rows_of, 3, groups, feature)
    qkv_send = jnp.concatenate([qkv_send[:, :, 1:], qkv_send[:, :, :1]], axis=2)
    qkv_send = qkv_send.transpose(3, 0, 1, 2, 4).reshape(groups, LAYERS, rows_of, 3 * feature)
    qkv_got = lax.all_to_all(qkv_send, PLANE, split_axis=0, concat_axis=0, tiled=True)
    out_rows = lax.ppermute(attn_low[:, :, 3 * D :], ALL, head_places(False))
    expert_send = jnp.stack([expert_up, expert_down], axis=1).astype(jnp.bfloat16)
    depth = expert_send.shape[3]
    expert_send = expert_send.reshape(LAYERS, 2 * EXPERTS, depth, planes, wide)
    expert_send = expert_send.transpose(3, 0, 1, 2, 4)
    expert_halves = []
    for layer_index in range(LAYERS):
        kept_half = lax.dynamic_index_in_dim(expert_send[:, layer_index], x_at, 0, False)
        sent_half = lax.dynamic_index_in_dim(expert_send[:, layer_index], 1 - x_at, 0, False)
        expert_halves.append((kept_half, sent_half))

    def across(half):
        return lax.ppermute(half, "x", ((0, 1), (1, 0)))

    got_half = across(expert_halves[0][1])
    whole_f, qkv_got, out_rows, got_half = lax.optimization_barrier(
        (whole_f, qkv_got, out_rows, got_half)
    )
    qkv_own = qkv_got.reshape(planes, sides, LAYERS, rows_of, 3 * feature).transpose(2, 0, 1, 3, 4)
    qkv_own = qkv_own.reshape(LAYERS, planes, sides * rows_of, 3 * feature)

    def gather_experts(kept_half, got_half):
        if depth % 16 == 0:
            return lax.all_gather(kept_half, LINE, axis=0).reshape(
                (slabs, cores) + kept_half.shape
            ), lax.all_gather(got_half, LINE, axis=0).reshape((slabs, cores) + kept_half.shape)
        halves = jnp.stack(
            [jnp.where(x_at == 0, kept_half, got_half), jnp.where(x_at == 0, got_half, kept_half)]
        )
        block = lax.all_gather(halves, LINE, axis=0)
        block = block.reshape(slabs, cores, planes, 2 * EXPERTS, depth, wide)
        block = block.transpose(3, 0, 2, 1, 4, 5).reshape(1, 1, 2 * EXPERTS, D, wide)
        return block, block

    expert_weights = [gather_experts(expert_halves[0][0], got_half)]
    ints = whole_f.reshape(sizes() + whole_f.shape[1:])
    whole = whole_f[:, : 2 + LAYERS].astype(jnp.int32)
    smalls = whole_f[:, 8:, :rows_of].transpose(1, 0, 2).reshape(16, D)
    router_all = smalls[: LAYERS * EXPERTS].reshape(LAYERS, EXPERTS, D).transpose(0, 2, 1)
    router_all = router_all.astype(jnp.bfloat16)
    gains_f = smalls[LAYERS * EXPERTS :]
    routes_lane = lax.dynamic_index_in_dim(
        whole.reshape(slabs, planes, cores, sides, 2 + LAYERS, own), z_at, 0, False
    )
    routes_lane = lax.dynamic_index_in_dim(routes_lane, core_at, 1, False)[:, :, 2:]
    routes_lane = routes_lane.transpose(2, 0, 1, 3)[..., None]
    routes_own = lax.dynamic_slice_in_dim(routes, side_at * own, own, axis=1)

    extent = -(-shard_rows // 256) * 256
    table = jnp.pad(vocab_table.astype(jnp.bfloat16), ((0, extent - shard_rows), (0, 0)))
    offsets = jnp.arange(chunk, dtype=jnp.int32)
    first_blk = z_at * planes * cores + core_at
    query_pos = jnp.concatenate([(first_blk + cores * part) * chunk + offsets for part in range(planes)])
    near_blks = [first_blk - 1 + part for part in range(2 * planes)]
    near_pos = jnp.concatenate([blk * chunk + offsets for blk in near_blks])
    query_seg = segment_of(query_pos, cont_ends)
    near_seg = segment_of(near_pos, cont_ends)
    places = (query_pos[None, :], query_seg[None, :], near_pos[None, :], near_seg[None, :])

    stream, qkv_all, out_all = embed(table, ints, qkv_own, out_rows, own, shard_rows, 2)
    qkv_weights = [qkv_all[layer_index].reshape(D, 3 * feature) for layer_index in range(LAYERS)]
    out_weights = [out_all[layer_index].reshape(feature, D) for layer_index in range(LAYERS)]

    kept = []
    for layer_index in range(LAYERS):
        normed_lane, key_values, queries = gather_project(
            rms_norm(stream, gains_f[2 * layer_index : 2 * layer_index + 1]).astype(jnp.bfloat16),
            qkv_weights[layer_index], False, (2 * feature, feature), None, 3,
        )
        if layer_index + 1 < LAYERS:
            kept_half, sent_half = expert_halves[layer_index + 1]
            key_values, sent_half = lax.optimization_barrier((key_values, sent_half))
            got_half = across(sent_half)
        queries = queries.reshape(lane, feature)
        far, near = spread_keys(key_values.reshape(lane, 2 * feature), PROMPT, 10)
        if layer_index + 1 < LAYERS:
            far, kept_half, got_half = lax.optimization_barrier((far, kept_half, got_half))
            expert_weights.append(gather_experts(kept_half, got_half))
        mixed_t, mixed_low, log_total = attend(queries, far, near, places, chunk)
        (attended,) = project(
            mixed_low.reshape(planes, sides, own, feature), out_weights[layer_index], False, None, 15
        )
        middle = stream + attended
        normed_two = rms_norm(middle, gains_f[2 * layer_index + 1 : 2 * layer_index + 2]).astype(jnp.bfloat16)
        chance = jax.nn.softmax(matmul(normed_two, router_all[layer_index]), axis=-1)
        output, wide_rows, before, hidden = experts(
            normed_two, routes_lane[layer_index], expert_weights[layer_index], 11
        )
        own_pick = (routes_own[layer_index][:, None] == expert_ids[None, :]).astype(jnp.float32)
        gate = jnp.sum(chance * own_pick, axis=1, keepdims=True)
        kept.append(
            (
                stream, normed_lane, queries, far, near, mixed_t, mixed_low, log_total, middle,
                normed_two, chance, wide_rows, before, hidden, output, own_pick, gate,
            )
        )
        stream = middle + gate * output

    final_gain = gains_f[2 * LAYERS : 2 * LAYERS + 1]
    devices = tokens // own
    valid_rows = valid_f.reshape(sizes() + (1, own))
    final_all, row_logs, hits = gather_logits(
        rms_norm(stream, final_gain).astype(jnp.bfloat16), table, ints, valid_rows, shard_rows, 4
    )
    log_sums = merge_logs(row_logs.reshape(devices, 1, own), 5)
    log_sum = log_sums.reshape(tokens)
    own_log = lax.dynamic_slice_in_dim(log_sum, device_at * own, own)
    own_valid = lax.dynamic_slice_in_dim(valid_f, device_at * own, own)
    own_loss = jnp.sum(own_log * own_valid) - jnp.sum(hits)
    final_grad, table_grad = vocab_back(
        final_all, table, ints, log_sums.reshape(sizes() + (1, own)), valid_rows / token_count,
        shard_rows, 6,
    )
    stream_grad, final_gain_grad = jax.vjp(rms_norm, stream, final_gain)[1](final_grad)

    qkv_packs = [None] * LAYERS
    out_packs = [None] * LAYERS
    router_list = [None] * LAYERS
    expert_sums = [None] * LAYERS
    gain_list = [None] * (2 * LAYERS + 1)
    gain_list[2 * LAYERS] = final_gain_grad
    for layer_index in reversed(range(LAYERS)):
        (
            stream, normed_lane, queries, far, near, mixed_t, mixed_low, log_total, middle,
            normed_two, chance, wide_rows, before, hidden, output, own_pick, gate,
        ) = kept[layer_index]
        out_grad = (gate * stream_grad).astype(jnp.bfloat16)
        chance_grad = jnp.sum(stream_grad * output, axis=1)[:, None] * own_pick
        choice_grad = chance * (chance_grad - jnp.sum(chance * chance_grad, axis=1, keepdims=True))
        router_list[layer_index] = jnp.dot(
            normed_two.astype(jnp.float32).T, choice_grad, precision=lax.Precision.HIGHEST
        )
        normed_grad = jnp.dot(
            choice_grad,
            router_all[layer_index].astype(jnp.float32).T,
            precision=lax.Precision.HIGHEST,
        )
        rows_grad, expert_grad = experts_back(
            out_grad, routes_lane[layer_index], expert_weights[layer_index], wide_rows, before,
            hidden, 12,
        )
        normed_grad = normed_grad + rows_grad
        middle_part, gain_list[2 * layer_index + 1] = jax.vjp(
            rms_norm, middle, gains_f[2 * layer_index + 1 : 2 * layer_index + 2]
        )[1](normed_grad)
        middle_grad = stream_grad + middle_part
        _, answer, out_packs[layer_index] = gather_project(
            middle_grad.astype(jnp.bfloat16), out_weights[layer_index], True, (feature,), mixed_low, 16
        )
        answer = answer.reshape(lane, feature)
        query_grad, far_grad, near_grad = attend_back(
            queries, far, near, places, log_total, mixed_t, answer, chunk
        )
        qkv_grad = collect_keys(far_grad, near_grad, query_grad, 13)
        qkv_grad, expert_grad = lax.optimization_barrier((qkv_grad, expert_grad))
        expert_sums[layer_index] = lax.psum_scatter(
            expert_grad, LINE, scatter_dimension=0, tiled=True
        )[0]
        normed_att_grad, qkv_packs[layer_index] = project(
            qkv_grad.reshape(planes, sides, own, 3 * feature), qkv_weights[layer_index], True,
            normed_lane, 14,
        )
        stream_part, gain_list[2 * layer_index] = jax.vjp(
            rms_norm, stream, gains_f[2 * layer_index : 2 * layer_index + 1]
        )[1](normed_att_grad)
        stream_grad = middle_grad + stream_part

    small = jnp.concatenate(
        [jnp.stack(router_list).transpose(1, 0, 2).reshape(D, -1), jnp.concatenate(gain_list, axis=0).T], axis=1
    )
    small = small.reshape(devices, rows_of, -1).transpose(0, 2, 1)
    small = jnp.pad(small, ((0, 0), (0, 16 - small.shape[1]), (0, 128 - rows_of)))
    table_share, small, near_squares, *attn_sums = embed_back(
        stream_grad.astype(jnp.bfloat16), ints, table_grad, small, qkv_packs + out_packs, shard_rows, 7
    )
    squares = sum(
        jnp.sum(jnp.square(part.astype(jnp.float32)))
        for part in [small[:, :rows_of]] + expert_sums
    ) + jnp.sum(near_squares)
    sums = jnp.pad(jnp.stack([squares, own_loss])[:, None], ((0, 6), (0, 127)))
    sums = jnp.sum(swap(sums[None], True, 9)[:, :2, 0], axis=0)
    square_total, loss_sum = sums[0], sums[1]
    expert_shares = []
    for expert_grad in expert_sums:
        kept_half = lax.dynamic_index_in_dim(expert_grad, x_at, 0, False)
        sent_half = lax.dynamic_index_in_dim(expert_grad, 1 - x_at, 0, False)
        got_half = lax.ppermute(sent_half, "x", ((0, 1), (1, 0)))
        expert_grad = jnp.concatenate(
            [jnp.where(x_at == 0, kept_half, got_half), jnp.where(x_at == 0, got_half, kept_half)],
            axis=-1,
        )
        expert_shares.append(
            expert_grad.reshape(2, EXPERTS, depth, planes * wide).astype(jnp.float32)
        )
    table_share, small = table_share[:shard_rows], small[:, :rows_of]
    router_share = (
        small[: LAYERS * EXPERTS].reshape(LAYERS, EXPERTS, rows_of).transpose(0, 2, 1)
    )
    gain_share = small[LAYERS * EXPERTS : LAYERS * EXPERTS + 2 * LAYERS + 1]
    qkv_share = jnp.stack(attn_sums[:LAYERS], axis=1).reshape(
        planes, LAYERS, sides, rows_of, 3 * feature
    )
    qkv_share = qkv_share.transpose(0, 2, 1, 3, 4).reshape(groups, LAYERS, rows_of, 3 * feature)
    qkv_share = lax.all_to_all(qkv_share, PLANE, split_axis=0, concat_axis=0, tiled=True)
    qkv_share = qkv_share.reshape(groups, LAYERS, rows_of, 3, feature)
    qkv_share = jnp.concatenate([qkv_share[:, :, :, 2:], qkv_share[:, :, :, :2]], axis=3)
    qkv_share = qkv_share.transpose(1, 2, 3, 0, 4).reshape(LAYERS, rows_of, 3 * D)
    out_share = lax.ppermute(jnp.stack(attn_sums[LAYERS:]), ALL, head_places(True))
    attn_share = jnp.concatenate([qkv_share, out_share], axis=2).astype(jnp.float32)
    up_share = jnp.stack([share[0] for share in expert_shares])
    down_share = jnp.stack([share[1] for share in expert_shares])
    shares = (table_share, attn_share, router_share, gain_share, up_share, down_share)
    grad_norm = jnp.sqrt(square_total)
    factor = CLIP_AT / jnp.maximum(grad_norm, CLIP_AT)
    weights = (vocab_table, attn_weights, router, norm_gains, expert_up, expert_down)
    firsts = (vocab_first, attn_first, router_first, gains_first, up_first, down_first)
    seconds = (vocab_second, attn_second, router_second, gains_second, up_second, down_second)
    results = [loss_sum, token_count, grad_norm]
    for number in range(6):
        results.extend(
            adam_update(
                weights[number],
                firsts[number],
                seconds[number],
                factor * shares[number],
                STEP_RATES[number],
                DECAY_RATES[number],
            )
        )
    return tuple(results)


def solution(mesh):
    blocks, sides = mesh.shape["blk"], mesh.shape["head"]
    fine = Mesh(mesh.devices.reshape(blocks // 4, 2, 2, sides), ALL)
    weight_specs = (
        (P(ALL, None),) * 3
        + (P(None, ALL, None),) * 3
        + (P(None, ALL, None),) * 3
        + (P(None, ALL),) * 3
        + (P(None, None, BLK, "head"),) * 6
    )
    return jax.shard_map(
        per_device,
        mesh=fine,
        in_specs=(P(BLK), P(BLK), P(), P(), P(None, BLK)) + weight_specs,
        out_specs=(P(), P(), P()) + weight_specs,
        check_vma=False,
    )
```
